32 devices in a mesh: seq: 8 (over y, x, core), batch: 4 (over z).
Axes of the slice: x: 2, y: 2, z: 4, core: 2. Of those that a mesh axis runs over, the one named last changes fastest.
Arguments:
- inputs: bfloat16 [4, 1024, 1024], P('batch', 'seq'), may hold values from -6 to 6
- teacher: bfloat16 [4, 1024, 1024], P('batch', 'seq'), may hold values from -6 to 6
- lengths: int32 [4], P('batch'), may hold values from 960 to 1023
- variate_ids: int32 [4, 1024], P('batch', 'seq'), may hold values from 0 to 15, as said below
- time_ids: int32 [4, 1024], P('batch', 'seq'), may hold values from 0 to 1008, as said below
- observed: int32 [4, 1024], P('batch', 'seq'), may hold values from 0 to 1, as said below
- attend_weight: float32 [3, 1024, 1024], P(None, ('seq', 'batch')), may hold values from -0.1875 to 0.1875
- output_weight: float32 [1024, 1024], P(('seq', 'batch')), may hold values from -5 to 5
- expand_weight: float32 [2, 1024, 4096], P(None, ('seq', 'batch')), may hold values from -0.1875 to 0.1875
- reduce_weight: float32 [4096, 1024], P(('seq', 'batch')), may hold values from -0.09375 to 0.09375
- norm_gains: float32 [2, 1024], replicated, may hold values from 0.25 to 2.8
- variate_bias: float32 [2, 16], replicated, may hold values from -4 to 4
- attend_first: float32 [3, 1024, 1024], P(None, ('seq', 'batch')), may hold values from -0.00015258789 to 0.00015258789
- output_first: float32 [1024, 1024], P(('seq', 'batch')), may hold values from -0.00015258789 to 0.00015258789
- expand_first: float32 [2, 1024, 4096], P(None, ('seq', 'batch')), may hold values from -0.00015258789 to 0.00015258789
- reduce_first: float32 [4096, 1024], P(('seq', 'batch')), may hold values from -0.00015258789 to 0.00015258789
- gains_first: float32 [2, 1024], replicated, may hold values from -0.00048828125 to 0.00048828125
- bias_first: float32 [2, 16], replicated, may hold values from -0.0017089844 to 0.0017089844
- attend_second: float32 [3, 1024, 1024], P(None, ('seq', 'batch')), may hold values from 1.2159348e-09 to 4.863739e-09
- output_second: float32 [1024, 1024], P(('seq', 'batch')), may hold values from 1.2159347e-11 to 4.863739e-11
- expand_second: float32 [2, 1024, 4096], P(None, ('seq', 'batch')), may hold values from 1.2159347e-10 to 4.863739e-10
- reduce_second: float32 [4096, 1024], P(('seq', 'batch')), may hold values from 1.2159348e-09 to 4.863739e-09
- gains_second: float32 [2, 1024], replicated, may hold values from 1.07288365e-08 to 4.3511392e-08
- bias_second: float32 [2, 16], replicated, may hold values from 1.2159347e-07 to 4.863739e-07
Outputs:
- layer_output: float32 [4, 1024, 1024], P('batch', 'seq')
- loss: float32 [], replicated
- input_gradient: float32 [4, 1024, 1024], P('batch', 'seq')
- grad_norm: float32 [], replicated
- attend_new: float32 [3, 1024, 1024], P(None, ('seq', 'batch'))
- attend_copy: bfloat16 [3, 1024, 1024], P(None, ('seq', 'batch'))
- attend_first_new: float32 [3, 1024, 1024], P(None, ('seq', 'batch'))
- attend_second_new: float32 [3, 1024, 1024], P(None, ('seq', 'batch'))
- output_new: float32 [1024, 1024], P(('seq', 'batch'))
- output_copy: bfloat16 [1024, 1024], P(('seq', 'batch'))
- output_first_new: float32 [1024, 1024], P(('seq', 'batch'))
- output_second_new: float32 [1024, 1024], P(('seq', 'batch'))
- expand_new: float32 [2, 1024, 4096], P(None, ('seq', 'batch'))
- expand_copy: bfloat16 [2, 1024, 4096], P(None, ('seq', 'batch'))
- expand_first_new: float32 [2, 1024, 4096], P(None, ('seq', 'batch'))
- expand_second_new: float32 [2, 1024, 4096], P(None, ('seq', 'batch'))
- reduce_new: float32 [4096, 1024], P(('seq', 'batch'))
- reduce_copy: bfloat16 [4096, 1024], P(('seq', 'batch'))
- reduce_first_new: float32 [4096, 1024], P(('seq', 'batch'))
- reduce_second_new: float32 [4096, 1024], P(('seq', 'batch'))
- gains_new: float32 [2, 1024], replicated
- gains_first_new: float32 [2, 1024], replicated
- gains_second_new: float32 [2, 1024], replicated
- bias_new: float32 [2, 16], replicated
- bias_first_new: float32 [2, 16], replicated
- bias_second_new: float32 [2, 16], replicated
The draws below stay inside these ranges and needn't reach their ends.
Inputs may be any that keep to these rules, and one draw needn't show every extreme that they name: `variate_ids`: non-decreasing along each sequence; each of the 16 variates has one or more positions. `time_ids`: the position counted from the first position of its variate. `observed`: the first position of each sequence is 1.
All inputs are finite; a program needn't handle non-finite values.
Results may differ from the reference program's by a relative error of at most 0.012.
The reference program's roundings to bfloat16 on the way count: a program that leaves them out, or rounds other values in their place, can miss the bound.
Values may be sent and summed in bfloat16 or wider, within the bound.
A program may use at most 384 MiB of HBM per device.

```python
import math
import jax
import jax.numpy as jnp
from jax import lax

D = 1024
HEADS = 16
HEAD_DIM = 64
FF = 4096
TOK_DEV = 128
VARIATES = 16
STEP = 10
SEQS = 4
LENGTH = 1024


def variate_layout(key):
    row_keys = jax.random.split(key, SEQS)
    chosen = jax.random.randint(jax.random.fold_in(key, 5), (), 0, SEQS)
    row_numbers = jnp.arange(SEQS, dtype=jnp.int32)

    def one_row(row_key, row_number):
        drawn = jax.random.permutation(row_key, LENGTH - 1)[:VARIATES - 1].astype(jnp.int32) + 1
        packed = jnp.arange(1, VARIATES, dtype=jnp.int32)
        borders = jnp.where(row_number == chosen, packed, drawn)
        borders = jnp.sort(borders)
        positions = jnp.arange(LENGTH, dtype=jnp.int32)
        passed = positions[:, None] >= borders[None, :]
        variate = jnp.sum(passed.astype(jnp.int32), axis=1)
        begins = jnp.max(jnp.where(passed, borders[None, :], 0), axis=1)
        return (variate.astype(jnp.int32), (positions - begins).astype(jnp.int32))
    return jax.vmap(one_row)(row_keys, row_numbers)


def draw_variate_ids(key, part):
    return variate_layout(key)[0]


def draw_time_ids(key, part):
    return variate_layout(key)[1]


def draw_lengths(key, part):
    key = jax.random.fold_in(key, 3)
    widest = TOK_DEV // 2
    padding = jax.random.randint(jax.random.fold_in(key, 1), (SEQS,), 1, widest + 1)
    ranking = jax.random.permutation(jax.random.fold_in(key, 2), SEQS)
    padding = jnp.where(ranking == 0, 1, jnp.where(ranking == 1, widest, padding))
    return (LENGTH - padding).astype(jnp.int32)


def draw_observed(key, part):
    key = jax.random.fold_in(key, 7)
    spread = max(SEQS - 1, 1)
    positions = jnp.arange(LENGTH, dtype=jnp.int32)[None, :]
    sequence = jnp.arange(SEQS, dtype=jnp.int32)[:, None]
    rolled = jax.random.randint(key, (SEQS, LENGTH), 0, 30 * LENGTH * spread)
    bound_row = (3 * LENGTH + 6 * positions) * (spread + 2 * sequence)
    marks = (rolled < bound_row).astype(jnp.int32)
    return marks.at[:, 0].set(1)


def draw_norm_gains(key, part):
    key = jax.random.fold_in(key, 11)
    ramped = jnp.arange(D, dtype=jnp.float32) / (D - 1)
    lowest = 0.5
    factors = jax.random.uniform(key, (2, D), jnp.float32, 0.65, 1.35)
    return (lowest + ramped)[None, :] * factors


def steps_of(stream_key, dims, shards, least, largest):
    gain = 1.0
    for dim, parts in shards:
        draws = jax.random.uniform(jax.random.fold_in(jax.random.fold_in(stream_key, 6), dim), (parts,), jnp.float32, least / len(shards), largest / len(shards))
        gain = gain * jnp.repeat(jnp.exp(draws), dims[dim] // parts).reshape((-1,) + (1,) * (len(dims) - 1 - dim))
    return gain


def bell_draw(key, extent, scale, most, shards=(), held_as=jnp.bfloat16):
    result = scale * jax.random.normal(key, extent, jnp.float32)
    if shards:
        result = result * steps_of(key, extent, shards, -0.22, 0.18)
    return jnp.clip(result, -most, most).astype(held_as)


def setup_inputs(seed: int = 0) -> dict:
    streams_of = jax.random.split(jax.random.key(seed), 25)
    inputs = bell_draw(streams_of[0], (SEQS, LENGTH, D), 1.0, 6.0, ((0, 4), (1, 8)))
    teacher = bell_draw(streams_of[1], (SEQS, LENGTH, D), 1.0, 6.0, ((0, 4), (1, 8)))
    lengths = draw_lengths(jax.random.fold_in(streams_of[24], 71), 0)
    variate_ids = draw_variate_ids(jax.random.fold_in(streams_of[24], 71), 0)
    time_ids = draw_time_ids(jax.random.fold_in(streams_of[24], 71), 0)
    observed = draw_observed(jax.random.fold_in(streams_of[24], 71), 0)
    attend_weight = bell_draw(streams_of[6], (3, D, D), D ** -0.5, 0.1875, ((1, 32),), jnp.float32)
    output_weight = bell_draw(streams_of[7], (D, D), ((LENGTH // 8) ** 0.5 * D ** -0.5), 5.0, ((0, 32),), jnp.float32)
    expand_weight = bell_draw(streams_of[8], (2, D, FF), D ** -0.5, 0.1875, ((1, 32),), jnp.float32)
    reduce_weight = bell_draw(streams_of[9], (FF, D), FF ** -0.5, 0.09375, ((0, 32),), jnp.float32)
    norm_gains = draw_norm_gains(jax.random.fold_in(streams_of[24], 71), 0)
    variate_bias = bell_draw(streams_of[11], (2, HEADS), 1.0, 4.0, (), jnp.float32)
    attend_first = bell_draw(streams_of[12], (3, D, D), (0.11 * (4 * D * D + 3 * D * FF) ** -0.5), 0.00015258789, ((1, 32),), jnp.float32)
    output_first = bell_draw(streams_of[13], (D, D), (0.11 * (4 * D * D + 3 * D * FF) ** -0.5), 0.00015258789, ((0, 32),), jnp.float32)
    expand_first = bell_draw(streams_of[14], (2, D, FF), (0.11 * (4 * D * D + 3 * D * FF) ** -0.5), 0.00015258789, ((1, 32),), jnp.float32)
    reduce_first = bell_draw(streams_of[15], (FF, D), (0.11 * (4 * D * D + 3 * D * FF) ** -0.5), 0.00015258789, ((0, 32),), jnp.float32)
    gains_first = bell_draw(streams_of[16], (2, D), (0.33 * (4 * D * D + 3 * D * FF) ** -0.5), 0.00048828125, (), jnp.float32)
    bias_first = bell_draw(streams_of[17], (2, HEADS), (1.1 * (4 * D * D + 3 * D * FF) ** -0.5), 0.0017089844, (), jnp.float32)
    attend_second = jnp.clip(jnp.exp(math.log(4.863739189175931e-09) - 1.3862944 * jax.random.uniform(streams_of[18], (3, D, D), jnp.float32) ** steps_of(streams_of[18], (3, D, D), ((1, 32),), -0.2, 0.2)), 1.2159347972939827e-09, 4.863739189175931e-09)
    output_second = jnp.clip(jnp.exp(math.log(4.8637389254979624e-11) - 1.3862944 * jax.random.uniform(streams_of[19], (D, D), jnp.float32) ** steps_of(streams_of[19], (D, D), ((0, 32),), -0.2, 0.2)), 1.2159347313744906e-11, 4.8637389254979624e-11)
    expand_second = jnp.clip(jnp.exp(math.log(4.863738856109023e-10) - 1.3862944 * jax.random.uniform(streams_of[20], (2, D, FF), jnp.float32) ** steps_of(streams_of[20], (2, D, FF), ((1, 32),), -0.2, 0.2)), 1.2159347140272558e-10, 4.863738856109023e-10)
    reduce_second = jnp.clip(jnp.exp(math.log(4.863739189175931e-09) - 1.3862944 * jax.random.uniform(streams_of[21], (FF, D), jnp.float32) ** steps_of(streams_of[21], (FF, D), ((0, 32),), -0.2, 0.2)), 1.2159347972939827e-09, 4.863739189175931e-09)
    gains_second = jnp.clip(jnp.exp(jax.random.uniform(streams_of[22], (2, D), jnp.float32, math.log(1.0728836485895954e-08), math.log(4.3511391822903533e-08))), 1.0728836485895954e-08, 4.3511391822903533e-08)
    bias_second = jnp.clip(jnp.exp(jax.random.uniform(streams_of[23], (2, HEADS), jnp.float32, math.log(1.2159347306806012e-07), math.log(4.863738922722405e-07))), 1.2159347306806012e-07, 4.863738922722405e-07)
    return {"inputs": inputs, "teacher": teacher, "lengths": lengths, "variate_ids": variate_ids, "time_ids": time_ids, "observed": observed, "attend_weight": attend_weight, "output_weight": output_weight, "expand_weight": expand_weight, "reduce_weight": reduce_weight, "norm_gains": norm_gains, "variate_bias": variate_bias, "attend_first": attend_first, "output_first": output_first, "expand_first": expand_first, "reduce_first": reduce_first, "gains_first": gains_first, "bias_first": bias_first, "attend_second": attend_second, "output_second": output_second, "expand_second": expand_second, "reduce_second": reduce_second, "gains_second": gains_second, "bias_second": bias_second}


NORM_EPS = 1e-05
ROPE_BASE = 10000.0
MASKED = -1e+30
CLIP_NORM = 1.0
BETA_ONE = 0.9
BETA_TWO = 0.98
ADAM_EPS = 1e-08
WEIGHT_DECAY = 0.1
RATE_ATTEND = 0.03
RATE_OUTPUT = 0.5
RATE_EXPAND = 0.03
RATE_REDUCE = 0.015
RATE_GAINS = 1.0
RATE_BIAS = 0.5
HIGHEST = lax.Precision.HIGHEST

@jax.custom_vjp
def low(v):
    return lax.optimization_barrier(v.astype(jnp.bfloat16)).astype(jnp.float32)

@jax.custom_vjp
def low_back(v):
    return v

def low_keep(v):
    return (low(v), None)

def low_pass(kept, grad):
    return (grad,)

def back_keep(v):
    return (v, None)

def back_low(kept, grad):
    return (low(grad),)
low.defvjp(low_keep, low_pass)
low_back.defvjp(back_keep, back_low)

def angles(times):
    half_dim = HEAD_DIM // 2
    frequency = jnp.exp(-math.log(ROPE_BASE) * jnp.arange(half_dim).astype(jnp.float32) / half_dim)
    angle_table = times.astype(jnp.float32)[..., None] * frequency
    return (jnp.cos(angle_table)[..., None, :], jnp.sin(angle_table)[..., None, :])

def rotate(values, cos_table, sin_table):
    half_dim = values.shape[-1] // 2
    first_half = values[..., :half_dim]
    second_half = values[..., half_dim:]
    return jnp.concatenate([first_half * cos_table - second_half * sin_table, second_half * cos_table + first_half * sin_table], axis=-1)

def attend_rows(query_rows, query_labels, key_rows, value_rows, key_labels, bias_table):
    scores = jnp.einsum('ihe,jhe->hij', query_rows, key_rows, precision=HIGHEST) * HEAD_DIM ** (-0.5)
    same_var = query_labels[:, None] == key_labels[None, :]
    scores = scores + jnp.where(same_var[None], bias_table[0][:, None, None], bias_table[1][:, None, None])
    scores = low_back(scores)
    scores = jnp.where(key_labels[None, None, :] >= 0, scores, MASKED)
    row_top = jnp.floor(lax.optimization_barrier(jnp.max(scores, axis=-1, keepdims=True)))
    log_total = row_top + jnp.log(lax.optimization_barrier(jnp.sum(jnp.exp(scores - row_top), axis=-1, keepdims=True)))
    weights = low(jnp.exp(scores - log_total))
    return jnp.einsum('hij,jhe->ihe', weights, value_rows, precision=HIGHEST)

def adam_step(weight, first_moment, second_moment, gradient, step_rate, decay_rate):
    first_moment = BETA_ONE * first_moment + (1.0 - BETA_ONE) * gradient
    second_moment = BETA_TWO * second_moment + (1.0 - BETA_TWO) * gradient * gradient
    direction = first_moment / (1.0 - BETA_ONE ** STEP) / (jnp.sqrt(second_moment / (1.0 - BETA_TWO ** STEP)) + ADAM_EPS)
    return (weight - step_rate * (direction + decay_rate * weight), first_moment, second_moment)

def reference(inputs, teacher, lengths, variate_ids, time_ids, observed, attend_weight, output_weight, expand_weight, reduce_weight, norm_gains, variate_bias, attend_first, output_first, expand_first, reduce_first, gains_first, bias_first, attend_second, output_second, expand_second, reduce_second, gains_second, bias_second):
    length = inputs.shape[1]
    positions = jnp.arange(length, dtype=jnp.int32)
    inside = positions[None, :] < lengths[:, None]
    scored = jnp.logical_and(inside, observed == 1)
    count_all = jnp.sum(scored.astype(jnp.int32)).astype(jnp.float32)
    key_labels = jnp.where(inside, variate_ids, -1)
    cos_table, sin_table = angles(time_ids)
    block_rows = math.gcd(length, 512)
    blocks = length // block_rows
    targets = teacher.astype(jnp.float32)
    checked = jax.checkpoint(attend_rows)

    def forward(states, attend_full, output_full, expand_full, reduce_full, gain_rows, bias_table):
        attend_low = low(attend_full)
        output_low = low(output_full)
        expand_low = low(expand_full)
        reduce_low = low(reduce_full)

        def one_sequence(running, pieces):
            state_row, target_row, cos_row, sin_row, query_lab, key_lab, scored_row = pieces
            unit_one = state_row * lax.rsqrt(lax.optimization_barrier(jnp.mean(state_row * state_row, axis=-1, keepdims=True)) + NORM_EPS)
            act_one = low(unit_one * gain_rows[0])
            project = jnp.einsum('td,cde->cte', act_one, attend_low, precision=HIGHEST)
            query = low(rotate(low_back(project[0]).reshape(length, HEADS, HEAD_DIM), cos_row, sin_row))
            keys = low(rotate(low_back(project[1]).reshape(length, HEADS, HEAD_DIM), cos_row, sin_row))
            values = low(low_back(project[2])).reshape(length, HEADS, HEAD_DIM)

            def one_block(pair):
                return checked(pair[0], pair[1], keys, values, key_lab, bias_table)
            mixed = lax.map(one_block, (query.reshape(blocks, block_rows, HEADS, HEAD_DIM), query_lab.reshape(blocks, block_rows)))
            mixed = low(low_back(mixed.reshape(length, D)))
            middle = state_row + low_back(jnp.dot(mixed, output_low, precision=HIGHEST))
            unit_two = middle * lax.rsqrt(lax.optimization_barrier(jnp.mean(middle * middle, axis=-1, keepdims=True)) + NORM_EPS)
            act_two = low(unit_two * gain_rows[1])
            gate_up = low_back(jnp.einsum('td,cdf->ctf', act_two, expand_low, precision=HIGHEST))
            hidden = low(jax.nn.silu(gate_up[0]) * gate_up[1])
            output = middle + low_back(jnp.dot(hidden, reduce_low, precision=HIGHEST))
            error = output - target_row
            return (running + jnp.sum(jnp.where(scored_row[:, None], error * error, 0.0)), output)
        squared, outputs = lax.scan(one_sequence, jnp.zeros((), jnp.float32), (states, targets, cos_table, sin_table, variate_ids, key_labels, scored))
        return (outputs, squared / (count_all * D))
    states = inputs.astype(jnp.float32)
    (outputs, loss), pullback = jax.vjp(forward, states, attend_weight, output_weight, expand_weight, reduce_weight, norm_gains, variate_bias)
    gradients = pullback((jnp.zeros_like(outputs), jnp.ones_like(loss)))
    squares = jnp.zeros((), jnp.float32)
    for piece in gradients[1:]:
        squares = squares + jnp.sum(piece * piece)
    grad_norm = jnp.sqrt(squares)
    clip_scale = jnp.minimum(1.0, CLIP_NORM / grad_norm)
    attend_new, attend_first_new, attend_second_new = adam_step(attend_weight, attend_first, attend_second, gradients[1] * clip_scale, RATE_ATTEND, WEIGHT_DECAY)
    output_new, output_first_new, output_second_new = adam_step(output_weight, output_first, output_second, gradients[2] * clip_scale, RATE_OUTPUT, WEIGHT_DECAY)
    expand_new, expand_first_new, expand_second_new = adam_step(expand_weight, expand_first, expand_second, gradients[3] * clip_scale, RATE_EXPAND, WEIGHT_DECAY)
    reduce_new, reduce_first_new, reduce_second_new = adam_step(reduce_weight, reduce_first, reduce_second, gradients[4] * clip_scale, RATE_REDUCE, WEIGHT_DECAY)
    gains_new, gains_first_new, gains_second_new = adam_step(norm_gains, gains_first, gains_second, gradients[5] * clip_scale, RATE_GAINS, 0.0)
    bias_new, bias_first_new, bias_second_new = adam_step(variate_bias, bias_first, bias_second, gradients[6] * clip_scale, RATE_BIAS, 0.0)
    input_gradient = gradients[0] * count_all * D
    return (outputs, loss, input_gradient, grad_norm, attend_new, attend_new.astype(jnp.bfloat16), attend_first_new, attend_second_new, output_new, output_new.astype(jnp.bfloat16), output_first_new, output_second_new, expand_new, expand_new.astype(jnp.bfloat16), expand_first_new, expand_second_new, reduce_new, reduce_new.astype(jnp.bfloat16), reduce_first_new, reduce_second_new, gains_new, gains_first_new, gains_second_new, bias_new, bias_first_new, bias_second_new)
```

```python
import functools
import math

import jax
import jax.numpy as jnp
from jax import lax
from jax.experimental import pallas as pl
from jax.experimental.pallas import tpu as pltpu
from jax.sharding import PartitionSpec as P

D = 1024
HEADS = 16
HEAD_DIM = 64
STEP = 10


NORM_EPS = 1e-05
ROPE_BASE = 10000.0
MASKED = -1e30
CLIP_NORM = 1.0
BETA_ONE = 0.9
BETA_TWO = 0.98
ADAM_EPS = 1e-08
WEIGHT_DECAY = 0.1
RATE_ATTEND = 0.03
RATE_OUTPUT = 0.5
RATE_EXPAND = 0.03
RATE_REDUCE = 0.015
RATE_GAINS = 1.0
RATE_BIAS = 0.5


def angles(times):
    half_dim = HEAD_DIM // 2
    frequency = jnp.exp(-math.log(ROPE_BASE) * jnp.arange(half_dim).astype(jnp.float32) / half_dim)
    angle_table = times.astype(jnp.float32)[..., None] * frequency
    return (jnp.cos(angle_table)[..., None, :], jnp.sin(angle_table)[..., None, :])


def rotate(values, cos_table, sin_table):
    half_dim = values.shape[-1] // 2
    first_half = values[..., :half_dim]
    second_half = values[..., half_dim:]
    return jnp.concatenate(
        [
            first_half * cos_table - second_half * sin_table,
            second_half * cos_table + first_half * sin_table,
        ],
        axis=-1,
    )


def unrotate(values, cos_table, sin_table):
    half_dim = values.shape[-1] // 2
    first_half = values[..., :half_dim]
    second_half = values[..., half_dim:]
    return jnp.concatenate(
        [
            first_half * cos_table + second_half * sin_table,
            second_half * cos_table - first_half * sin_table,
        ],
        axis=-1,
    )


def normalize(values):
    inv_scale = lax.rsqrt(jnp.mean(values * values, axis=-1, keepdims=True) + NORM_EPS)
    return (values * inv_scale, inv_scale)


def norm_back(grad_act, unit_rows, inv_scale, gain_row):
    grad_unit = grad_act * gain_row
    return inv_scale * (
        grad_unit - unit_rows * jnp.mean(grad_unit * unit_rows, axis=-1, keepdims=True)
    )


def score_block(query_rows, query_labels, key_rows, key_labels, bias_table):
    scores = jnp.einsum(
        "ihe,jhe->hij", query_rows, key_rows, preferred_element_type=jnp.float32
    ) * HEAD_DIM ** (-0.5)
    same_var = query_labels[:, None] == key_labels[None, :]
    scores = scores + jnp.where(
        same_var[None], bias_table[0][:, None, None], bias_table[1][:, None, None]
    )
    scores = jnp.where(key_labels[None, None, :] >= 0, scores, MASKED)
    return (scores, same_var)


def block_grads(
    query_rows,
    query_labels,
    grad_rows,
    lse_rows,
    delta_rows,
    key_rows,
    value_rows,
    key_labels,
    bias_table,
    need_query,
    need_keys,
):
    scores, same_var = score_block(query_rows, query_labels, key_rows, key_labels, bias_table)
    weights = jnp.exp(scores - lse_rows.T[:, :, None])
    grad_weights = jnp.einsum(
        "ihe,jhe->hij", grad_rows, value_rows, preferred_element_type=jnp.float32
    )
    grad_scores = (weights * (grad_weights - delta_rows.T[:, :, None])).astype(jnp.bfloat16)
    result = ()
    if need_query:
        grad_query = jnp.einsum(
            "hij,jhe->ihe", grad_scores, key_rows, preferred_element_type=jnp.float32
        ) * HEAD_DIM ** (-0.5)
        widened = grad_scores.astype(jnp.float32)
        bias_same = jnp.sum(jnp.where(same_var[None], widened, 0.0), axis=(1, 2))
        bias_other = jnp.sum(jnp.where(same_var[None], 0.0, widened), axis=(1, 2))
        result = result + (grad_query, jnp.stack([bias_same, bias_other]))
    if need_keys:
        grad_key = jnp.einsum(
            "hij,ihe->jhe", grad_scores, query_rows, preferred_element_type=jnp.float32
        ) * HEAD_DIM ** (-0.5)
        grad_value = jnp.einsum(
            "hij,ihe->jhe",
            weights.astype(jnp.bfloat16),
            grad_rows,
            preferred_element_type=jnp.float32,
        )
        result = result + (grad_key, grad_value)
    return result


def adam_step(weight, first_moment, second_moment, gradient, step_rate, decay_rate):
    first_moment = BETA_ONE * first_moment + (1.0 - BETA_ONE) * gradient
    second_moment = BETA_TWO * second_moment + (1.0 - BETA_TWO) * gradient * gradient
    direction = (
        first_moment
        / (1.0 - BETA_ONE**STEP)
        / (jnp.sqrt(second_moment / (1.0 - BETA_TWO**STEP)) + ADAM_EPS)
    )
    return (weight - step_rate * (direction + decay_rate * weight), first_moment, second_moment)


def general_body(
    inputs,
    teacher,
    lengths,
    variate_ids,
    time_ids,
    observed,
    attend_weight,
    output_weight,
    expand_weight,
    reduce_weight,
    norm_gains,
    variate_bias,
    attend_first,
    output_first,
    expand_first,
    reduce_first,
    gains_first,
    bias_first,
    attend_second,
    output_second,
    expand_second,
    reduce_second,
    gains_second,
    bias_second,
):
    row_count = inputs.shape[1]
    length = row_count * lax.axis_size("seq")
    block_rows = math.gcd(length, 1024)
    blocks = length // block_rows
    states = inputs[0].astype(jnp.float32)
    positions = lax.axis_index("seq") * row_count + jnp.arange(row_count, dtype=jnp.int32)
    inside = positions < lengths[0]
    scored = jnp.logical_and(inside, observed[0] == 1)
    local_count = jnp.sum(scored.astype(jnp.int32))
    count_early = lax.psum(local_count, ("seq", "batch"))
    full_attend, full_output, full_expand, full_reduce = (
        lax.all_gather(attend_weight.astype(jnp.bfloat16), ("seq", "batch"), axis=1, tiled=True),
        lax.all_gather(output_weight.astype(jnp.bfloat16), ("seq", "batch"), axis=0, tiled=True),
        lax.all_gather(expand_weight.astype(jnp.bfloat16), ("seq", "batch"), axis=1, tiled=True),
        lax.all_gather(reduce_weight.astype(jnp.bfloat16), ("seq", "batch"), axis=0, tiled=True),
    )
    unit_one, scale_one = normalize(states)
    act_one = (unit_one * norm_gains[0]).astype(jnp.bfloat16)
    project = jnp.einsum("td,cde->cte", act_one, full_attend, preferred_element_type=jnp.float32)
    cos_table, sin_table = angles(time_ids[0])
    query = rotate(project[0].reshape(row_count, HEADS, HEAD_DIM), cos_table, sin_table).astype(
        jnp.bfloat16
    )
    key_rows = (
        rotate(project[1].reshape(row_count, HEADS, HEAD_DIM), cos_table, sin_table)
        .astype(jnp.bfloat16)
        .reshape(row_count, D)
    )
    value_rows = project[2].astype(jnp.bfloat16)
    own_labels = jnp.where(inside, variate_ids[0], -1).astype(jnp.bfloat16)
    all_keys, all_values, all_labels = (
        lax.all_gather(key_rows, "seq", axis=0, tiled=True),
        lax.all_gather(value_rows, "seq", axis=0, tiled=True),
        lax.all_gather(own_labels, "seq", axis=0, tiled=True),
    )
    key_blocks = all_keys.reshape(blocks, block_rows, HEADS, HEAD_DIM)
    value_blocks = all_values.reshape(blocks, block_rows, HEADS, HEAD_DIM)
    label_blocks = all_labels.astype(jnp.float32).reshape(blocks, block_rows)
    query_labels = variate_ids[0].astype(jnp.float32)

    def sweep_top(carry, pieces):
        running, sum_exp = carry
        scores, same_var = score_block(query, query_labels, pieces[0], pieces[1], variate_bias)
        raised = jnp.maximum(running, jnp.floor(jnp.max(scores, axis=-1)))
        sum_exp = sum_exp * jnp.exp(running - raised) + jnp.sum(
            jnp.exp(scores - raised[..., None]), axis=-1
        )
        return ((raised, sum_exp), None)

    start_top = jnp.full((HEADS, row_count), MASKED, jnp.float32)
    (row_top, sum_exp), unused = lax.scan(
        sweep_top,
        (start_top, jnp.zeros((HEADS, row_count), jnp.float32)),
        (key_blocks, label_blocks),
    )
    log_total = row_top + jnp.log(sum_exp)

    def sweep_out(carry, pieces):
        coarse, finest = carry
        scores, same_var = score_block(query, query_labels, pieces[0], pieces[2], variate_bias)
        weights = jnp.exp(scores - log_total[..., None])
        rounded = weights.astype(jnp.bfloat16)
        residue = (weights - rounded.astype(jnp.float32)).astype(jnp.bfloat16)
        coarse = coarse + jnp.einsum(
            "hij,jhe->ihe", rounded, pieces[1], preferred_element_type=jnp.float32
        )
        finest = finest + jnp.einsum(
            "hij,jhe->ihe", residue, pieces[1], preferred_element_type=jnp.float32
        )
        return ((coarse, finest), None)

    zero_heads = jnp.zeros((row_count, HEADS, HEAD_DIM), jnp.float32)
    (coarse, finest), unused = lax.scan(
        sweep_out, (zero_heads, zero_heads), (key_blocks, value_blocks, label_blocks)
    )
    exact_heads = coarse + finest
    mixed = coarse.reshape(row_count, D).astype(jnp.bfloat16)
    middle = states + jnp.dot(mixed, full_output, preferred_element_type=jnp.float32)
    unit_two, scale_two = normalize(middle)
    act_two = (unit_two * norm_gains[1]).astype(jnp.bfloat16)
    gate_up = jnp.einsum("td,cdf->ctf", act_two, full_expand, preferred_element_type=jnp.float32)
    sigmoid = jax.nn.sigmoid(gate_up[0])
    hidden = (gate_up[0] * sigmoid * gate_up[1]).astype(jnp.bfloat16)
    output = middle + jnp.dot(hidden, full_reduce, preferred_element_type=jnp.float32)
    error = output - teacher[0].astype(jnp.float32)
    local_square = jnp.sum(jnp.where(scored[:, None], error * error, 0.0))
    square_total = lax.psum(local_square, ("seq", "batch"))
    count_all = count_early.astype(jnp.float32)
    loss = square_total / (count_all * D)
    grad_out = jnp.where(scored[:, None], error * (2.0 / (count_all * D)), 0.0)
    back_attend, back_output, back_expand, back_reduce = (
        lax.all_gather(attend_weight.astype(jnp.bfloat16), ("seq", "batch"), axis=1, tiled=True),
        lax.all_gather(output_weight.astype(jnp.bfloat16), ("seq", "batch"), axis=0, tiled=True),
        lax.all_gather(expand_weight.astype(jnp.bfloat16), ("seq", "batch"), axis=1, tiled=True),
        lax.all_gather(reduce_weight.astype(jnp.bfloat16), ("seq", "batch"), axis=0, tiled=True),
    )
    grad_branch = grad_out.astype(jnp.bfloat16)
    reduce_grad = jnp.einsum("tf,td->fd", hidden, grad_branch, preferred_element_type=jnp.float32)
    grad_hidden = jnp.einsum(
        "td,fd->tf", grad_branch, back_reduce, preferred_element_type=jnp.float32
    )
    grad_gate = grad_hidden * gate_up[1] * sigmoid * (1.0 + gate_up[0] * (1.0 - sigmoid))
    grad_up = grad_hidden * gate_up[0] * sigmoid
    grad_expand = jnp.stack([grad_gate, grad_up]).astype(jnp.bfloat16)
    expand_grad = jnp.einsum(
        "td,ctf->cdf", act_two, grad_expand, preferred_element_type=jnp.float32
    )
    grad_act_two = jnp.einsum(
        "ctf,cdf->td", grad_expand, back_expand, preferred_element_type=jnp.float32
    )
    expand_share, reduce_share = (
        lax.psum_scatter(expand_grad, ("seq", "batch"), scatter_dimension=1, tiled=True),
        lax.psum_scatter(reduce_grad, ("seq", "batch"), scatter_dimension=0, tiled=True),
    )
    grad_middle = grad_out + norm_back(grad_act_two, unit_two, scale_two, norm_gains[1])
    grad_attn = grad_middle.astype(jnp.bfloat16)
    output_grad = jnp.einsum("td,te->de", mixed, grad_attn, preferred_element_type=jnp.float32)
    grad_mixed = jnp.einsum(
        "te,de->td", grad_attn, back_output, preferred_element_type=jnp.float32
    ).astype(jnp.bfloat16)
    grad_heads = grad_mixed.reshape(row_count, HEADS, HEAD_DIM)
    row_delta = jnp.sum(grad_heads.astype(jnp.float32) * exact_heads, axis=-1)
    lse_rows = log_total.T
    zero_bias = jnp.zeros((2, HEADS), jnp.float32)

    def sweep_query(carry, pieces):
        part_query, part_bias = block_grads(
            query,
            query_labels,
            grad_heads,
            lse_rows,
            row_delta,
            pieces[0],
            pieces[1],
            pieces[2],
            variate_bias,
            True,
            False,
        )
        return ((carry[0] + part_query, carry[1] + part_bias), None)

    (query_total, bias_grad), unused = lax.scan(
        sweep_query, (zero_heads, zero_bias), (key_blocks, value_blocks, label_blocks)
    )
    all_query, all_grad = (
        lax.all_gather(query.reshape(row_count, D), "seq", axis=0, tiled=True),
        lax.all_gather(grad_mixed, "seq", axis=0, tiled=True),
    )
    all_lse, all_delta = (
        lax.all_gather(lse_rows, "seq", axis=0, tiled=True),
        lax.all_gather(row_delta, "seq", axis=0, tiled=True),
    )
    key_heads = key_rows.reshape(row_count, HEADS, HEAD_DIM)
    value_heads = value_rows.reshape(row_count, HEADS, HEAD_DIM)
    own_float = own_labels.astype(jnp.float32)

    def sweep_keys(carry, pieces):
        part_key, part_value = block_grads(
            pieces[0],
            pieces[1],
            pieces[2],
            pieces[3],
            pieces[4],
            key_heads,
            value_heads,
            own_float,
            variate_bias,
            False,
            True,
        )
        return ((carry[0] + part_key, carry[1] + part_value), None)

    (key_total, value_heads_total), unused = lax.scan(
        sweep_keys,
        (zero_heads, zero_heads),
        (
            all_query.reshape(blocks, block_rows, HEADS, HEAD_DIM),
            label_blocks,
            all_grad.reshape(blocks, block_rows, HEADS, HEAD_DIM),
            all_lse.reshape(blocks, block_rows, HEADS),
            all_delta.reshape(blocks, block_rows, HEADS),
        ),
    )
    value_total = value_heads_total.reshape(row_count, D)
    grad_query = unrotate(query_total, cos_table, sin_table).reshape(row_count, D)
    grad_key = unrotate(key_total, cos_table, sin_table).reshape(row_count, D)
    grad_project = jnp.stack([grad_query, grad_key, value_total]).astype(jnp.bfloat16)
    attend_grad = jnp.einsum(
        "td,cte->cde", act_one, grad_project, preferred_element_type=jnp.float32
    )
    grad_act_one = jnp.einsum(
        "cte,cde->td", grad_project, back_attend, preferred_element_type=jnp.float32
    )
    attend_share, output_share = (
        lax.psum_scatter(attend_grad, ("seq", "batch"), scatter_dimension=1, tiled=True),
        lax.psum_scatter(output_grad, ("seq", "batch"), scatter_dimension=0, tiled=True),
    )
    grad_input = grad_middle + norm_back(grad_act_one, unit_one, scale_one, norm_gains[0])
    gains_grad = jnp.stack(
        [jnp.sum(grad_act_one * unit_one, axis=0), jnp.sum(grad_act_two * unit_two, axis=0)]
    )
    local_squares = (
        jnp.sum(attend_share * attend_share)
        + jnp.sum(output_share * output_share)
        + jnp.sum(expand_share * expand_share)
        + jnp.sum(reduce_share * reduce_share)
    )
    gains_total, bias_total, square_sum = lax.psum(
        (gains_grad, bias_grad, local_squares), ("seq", "batch")
    )
    grad_norm = jnp.sqrt(
        square_sum + jnp.sum(gains_total * gains_total) + jnp.sum(bias_total * bias_total)
    )
    clip_scale = jnp.minimum(1.0, CLIP_NORM / grad_norm)
    attend_new, attend_first_new, attend_second_new = adam_step(
        attend_weight,
        attend_first,
        attend_second,
        attend_share * clip_scale,
        RATE_ATTEND,
        WEIGHT_DECAY,
    )
    output_new, output_first_new, output_second_new = adam_step(
        output_weight,
        output_first,
        output_second,
        output_share * clip_scale,
        RATE_OUTPUT,
        WEIGHT_DECAY,
    )
    expand_new, expand_first_new, expand_second_new = adam_step(
        expand_weight,
        expand_first,
        expand_second,
        expand_share * clip_scale,
        RATE_EXPAND,
        WEIGHT_DECAY,
    )
    reduce_new, reduce_first_new, reduce_second_new = adam_step(
        reduce_weight,
        reduce_first,
        reduce_second,
        reduce_share * clip_scale,
        RATE_REDUCE,
        WEIGHT_DECAY,
    )
    gains_new, gains_first_new, gains_second_new = adam_step(
        norm_gains, gains_first, gains_second, gains_total * clip_scale, RATE_GAINS, 0.0
    )
    bias_new, bias_first_new, bias_second_new = adam_step(
        variate_bias, bias_first, bias_second, bias_total * clip_scale, RATE_BIAS, 0.0
    )
    input_gradient = (grad_input * count_all * D)[None]
    return (
        output[None],
        loss,
        input_gradient,
        grad_norm,
        attend_new,
        attend_new.astype(jnp.bfloat16),
        attend_first_new,
        attend_second_new,
        output_new,
        output_new.astype(jnp.bfloat16),
        output_first_new,
        output_second_new,
        expand_new,
        expand_new.astype(jnp.bfloat16),
        expand_first_new,
        expand_second_new,
        reduce_new,
        reduce_new.astype(jnp.bfloat16),
        reduce_first_new,
        reduce_second_new,
        gains_new,
        gains_first_new,
        gains_second_new,
        bias_new,
        bias_first_new,
        bias_second_new,
    )


MESH = pl.DeviceIdType.MESH
IN_VMEM = pl.BlockSpec(memory_space=pltpu.VMEM)
IN_SMEM = pl.BlockSpec(memory_space=pltpu.SMEM)
LANES = 128
QUERY_BLOCK = 256
MIB = 1 << 20


def fast_fits(seq, batch):
    power = seq & (seq - 1) == 0
    return power and seq >= 2 and seq * LANES == D and D % (16 * seq * batch) == 0


def flip(index, mask):
    result, bit = index, 1
    while bit <= mask:
        if mask & bit:
            result = result + bit - 2 * bit * lax.rem(lax.div(index, bit), 2)
        bit *= 2
    return result


def push(source, target, sends, recvs, slot, device):
    return pltpu.make_async_remote_copy(
        src_ref=source,
        dst_ref=target,
        send_sem=sends.at[slot],
        recv_sem=recvs.at[slot],
        device_id=device,
        device_id_type=MESH,
    )


def chip_masks(seq):
    return sorted(range(2, seq, 2), key=lambda mask: -bin(mask).count("1"))


def greet_sequence(seq):
    me, group = lax.axis_index("seq"), lax.axis_index("batch")
    barrier = pltpu.get_barrier_semaphore()
    masks = [1] + chip_masks(seq)
    for mask in masks:
        pl.semaphore_signal(barrier, inc=1, device_id=(flip(me, mask), group), device_id_type=MESH)
    pl.semaphore_wait(barrier, len(masks))


def greet_all(seq, batch):
    me = lax.axis_index("seq") * batch + lax.axis_index("batch")
    barrier = pltpu.get_barrier_semaphore()

    def greet(step, unused):
        other = lax.rem(me + step, seq * batch)
        pl.semaphore_signal(
            barrier,
            inc=1,
            device_id=(lax.div(other, batch), lax.rem(other, batch)),
            device_id_type=MESH,
        )
        return unused

    lax.fori_loop(1, seq * batch, greet, 0)
    pl.semaphore_wait(barrier, seq * batch - 1)


def spread_tile(seq, batch, tile, tiles, sends, recvs):
    me = lax.axis_index("seq") * batch + lax.axis_index("batch")

    def copy_of(step):
        other = lax.rem(me + step, seq * batch)
        return push(
            tile,
            tiles.at[me],
            sends,
            recvs,
            step,
            (lax.div(other, batch), lax.rem(other, batch)),
        )

    def begin(step, unused):
        copy_of(step).start()
        return unused

    def finish(step, unused):
        copy_of(step).wait()
        return unused

    lax.fori_loop(1, seq * batch, begin, 0)
    return lambda: lax.fori_loop(1, seq * batch, finish, 0)


def begin_gather_rows(seq, rows, all_rows, sends, recvs):
    me, group = lax.axis_index("seq"), lax.axis_index("batch")
    first = {
        mask: push(rows, all_rows.at[me], sends, recvs, mask, (flip(me, mask), group))
        for mask in chip_masks(seq) + [1]
    }
    for copy in first.values():
        copy.start()

    def finish():
        all_rows[me] = rows[...]
        second = []
        for mask in reversed(chip_masks(seq)):
            first[mask].wait_recv()
            slot = flip(me, mask)
            copy = push(
                all_rows.at[slot],
                all_rows.at[slot],
                sends,
                recvs,
                mask + 1,
                (flip(me, 1), group),
            )
            copy.start()
            second.append(copy)
        first[1].wait_recv()
        for copy in second:
            copy.wait_recv()
        for copy in list(first.values()) + second:
            copy.wait_send()

    return finish


def weights_kernel(
    seq,
    batch,
    attend,
    output,
    expand,
    reduce,
    act,
    tile,
    attend_all,
    output_all,
    expand_all,
    reduce_all,
    act_all,
    tiles,
    plane_send,
    plane_recv,
    line_send,
    line_recv,
    act_send,
    act_recv,
    tile_send,
    tile_recv,
):
    me, group = lax.axis_index("seq"), lax.axis_index("batch")
    greet_all(seq, batch)
    end_tiles = spread_tile(seq, batch, tile, tiles, tile_send, tile_recv)
    tiles[me * batch + group] = tile[...]
    masks = sorted(range(1, seq), key=lambda mask: -bin(mask).count("1"))
    planes = []
    for row, (source, target) in enumerate(((attend, attend_all), (expand, expand_all))):
        width = target.shape[-1]
        copies = []
        for mask in masks:
            other = flip(me, mask)
            copy = push(
                source.at[:, :, pl.ds(pl.multiple_of(other * width, LANES), width)],
                target.at[:, me, group],
                plane_send.at[row],
                plane_recv.at[row],
                mask,
                (other, group),
            )
            copy.start()
            copies.append(copy)
        planes.append(copies)
    end_act = begin_gather_rows(seq, act, act_all, act_send, act_recv)
    output_all[group] = output[...]
    reduce_all[group] = reduce[...]
    for source, target in ((attend, attend_all), (expand, expand_all)):
        width = target.shape[-1]
        target[:, me, group] = source[:, :, pl.ds(pl.multiple_of(me * width, LANES), width)]
    lines = []

    def send_line(row, part):
        for step in range(1, batch):
            copy = push(
                part,
                part,
                line_send.at[row],
                line_recv.at[row],
                step,
                (me, lax.rem(group + step, batch)),
            )
            copy.start()
            lines.append(copy)

    for copy in planes[0]:
        copy.wait_recv()
    send_line(0, attend_all.at[:, :, group])
    send_line(1, output_all.at[group])
    for copy in planes[1]:
        copy.wait_recv()
    send_line(2, expand_all.at[:, :, group])
    send_line(3, reduce_all.at[group])
    end_act()
    end_tiles()
    for copies in planes:
        for copy in copies:
            copy.wait_send()
    for copy in lines:
        copy.wait()


def call_weights(seq, batch, attend, output, expand, reduce, act, tile):
    rows = attend.shape[1]
    dtype = jnp.bfloat16
    return pl.pallas_call(
        functools.partial(weights_kernel, seq, batch),
        out_shape=[
            jax.ShapeDtypeStruct((3, seq, batch, rows, D // seq), dtype),
            jax.ShapeDtypeStruct((batch,) + output.shape, dtype),
            jax.ShapeDtypeStruct((2, seq, batch, rows, expand.shape[2] // seq), dtype),
            jax.ShapeDtypeStruct((batch,) + reduce.shape, dtype),
            jax.ShapeDtypeStruct((seq,) + act.shape, dtype),
            jax.ShapeDtypeStruct((seq * batch,) + tile.shape, jnp.float32),
        ],
        in_specs=[IN_VMEM] * 6,
        out_specs=[IN_VMEM] * 6,
        scratch_shapes=[
            pltpu.SemaphoreType.DMA((2, seq)),
            pltpu.SemaphoreType.DMA((2, seq)),
            pltpu.SemaphoreType.DMA((4, batch)),
            pltpu.SemaphoreType.DMA((4, batch)),
            pltpu.SemaphoreType.DMA((seq,)),
            pltpu.SemaphoreType.DMA((seq,)),
            pltpu.SemaphoreType.DMA((seq * batch,)),
            pltpu.SemaphoreType.DMA((seq * batch,)),
        ],
        compiler_params=pltpu.CompilerParams(
            collective_id=0, has_side_effects=True, vmem_limit_bytes=40 * MIB
        ),
    )(attend, output, expand, reduce, act, tile)


def gather_kernel(seq, rows, all_rows, sends, recvs):
    greet_sequence(seq)
    begin_gather_rows(seq, rows, all_rows, sends, recvs)()


def gather_rows(seq, rows):
    gathered = pl.pallas_call(
        functools.partial(gather_kernel, seq),
        out_shape=jax.ShapeDtypeStruct((seq,) + rows.shape, rows.dtype),
        in_specs=[IN_VMEM],
        out_specs=IN_VMEM,
        scratch_shapes=[pltpu.SemaphoreType.DMA((seq,)), pltpu.SemaphoreType.DMA((seq,))],
        compiler_params=pltpu.CompilerParams(
            collective_id=1, has_side_effects=True, vmem_limit_bytes=32 * MIB
        ),
    )(rows)
    return gathered.reshape(seq * rows.shape[0], rows.shape[1])


def scatter_kernel(seq, parts, total, near, chip, far, near_send, near_recv, far_send, far_recv):
    me, group = lax.axis_index("seq"), lax.axis_index("batch")
    greet_sequence(seq)
    masks = chip_masks(seq) + [0]
    first = {}
    for mask in masks:
        first[mask] = push(
            parts.at[flip(me, mask + 1)],
            near.at[mask // 2],
            near_send,
            near_recv,
            mask // 2,
            (flip(me, 1), group),
        )
        first[mask].start()
    second = {}
    for mask in masks[:-1]:
        first[mask].wait_recv()
        both = parts[flip(me, mask)].astype(jnp.float32) + near[mask // 2].astype(jnp.float32)
        chip[mask // 2] = both.astype(jnp.bfloat16)
        second[mask] = push(
            chip.at[mask // 2],
            far.at[mask // 2],
            far_send,
            far_recv,
            mask // 2,
            (flip(me, mask), group),
        )
        second[mask].start()
    first[0].wait_recv()
    total[...] = parts[me].astype(jnp.float32) + near[0].astype(jnp.float32)
    for mask in reversed(masks[:-1]):
        second[mask].wait_recv()
        total[...] += far[mask // 2].astype(jnp.float32)
    for copy in list(first.values()) + list(second.values()):
        copy.wait_send()


def scatter_rows(seq, parts):
    rows = parts.shape[0] // seq
    chips = seq // 2
    block = pltpu.VMEM((chips, rows, parts.shape[1]), jnp.bfloat16)
    sems = pltpu.SemaphoreType.DMA((chips,))
    return pl.pallas_call(
        functools.partial(scatter_kernel, seq),
        out_shape=jax.ShapeDtypeStruct((rows, parts.shape[1]), jnp.float32),
        in_specs=[IN_VMEM],
        out_specs=IN_VMEM,
        scratch_shapes=[block, block, block, sems, sems, sems, sems],
        compiler_params=pltpu.CompilerParams(
            collective_id=2, has_side_effects=True, vmem_limit_bytes=32 * MIB
        ),
    )(parts.reshape(seq, rows, parts.shape[1]))


def grads_kernel(
    seq,
    batch,
    attend,
    output,
    expand,
    reduce,
    attend_sum,
    output_sum,
    expand_sum,
    reduce_sum,
    attend_line,
    output_line,
    expand_line,
    reduce_line,
    attend_part,
    expand_part,
    line_send,
    line_recv,
    plane_send,
    plane_recv,
):
    me, group = lax.axis_index("seq"), lax.axis_index("batch")
    greet_all(seq, batch)
    sources = (expand, reduce, attend, output)
    landed = (expand_line, reduce_line, attend_line, output_line)
    lines = []
    for row, (source, target) in enumerate(zip(sources, landed)):
        copies = []
        for step in range(1, batch):
            other = lax.rem(group + step, batch)
            part = source.at[:, :, other] if len(source.shape) == 5 else source.at[other]
            copy = push(
                part,
                target.at[step - 1],
                line_send.at[row],
                line_recv.at[row],
                step,
                (me, other),
            )
            copy.start()
            copies.append(copy)
        lines.append(copies)
    masks = sorted(range(1, seq), key=lambda mask: -bin(mask).count("1"))
    planes = []
    for row in (0, 2, 1, 3):
        for copy in lines[row]:
            copy.wait_recv()
        source, target = sources[row], landed[row]
        if row % 2:
            total = source[group].astype(jnp.float32)
            for step in range(1, batch):
                total += target[step - 1].astype(jnp.float32)
            (reduce_sum if row == 1 else output_sum)[...] = total
            continue
        part = expand_part if row == 0 else attend_part
        whole = expand_sum if row == 0 else attend_sum
        width = source.shape[-1]

        def add_block(block, unused):
            total = source[:, block, group].astype(jnp.float32)
            for step in range(1, batch):
                total += target[step - 1, :, block].astype(jnp.float32)
            part[:, block] = total.astype(jnp.bfloat16)
            return unused

        lax.fori_loop(0, seq, add_block, 0)
        columns = pl.ds(pl.multiple_of(me * width, LANES), width)
        for mask in masks:
            other = flip(me, mask)
            copy = push(
                part.at[:, other],
                whole.at[:, :, columns],
                plane_send.at[row // 2],
                plane_recv.at[row // 2],
                mask,
                (other, group),
            )
            copy.start()
            planes.append(copy)
        whole[:, :, columns] = part[:, me]
    for copies in lines:
        for copy in copies:
            copy.wait_send()
    for copy in planes:
        copy.wait()


def call_grads(seq, batch, attend, output, expand, reduce):
    rows, width, hidden = attend.shape[3], attend.shape[4], expand.shape[4]
    dtype = jnp.bfloat16
    return pl.pallas_call(
        functools.partial(grads_kernel, seq, batch),
        out_shape=[
            jax.ShapeDtypeStruct((3, rows, width * seq), dtype),
            jax.ShapeDtypeStruct(output.shape[1:], jnp.float32),
            jax.ShapeDtypeStruct((2, rows, hidden * seq), dtype),
            jax.ShapeDtypeStruct(reduce.shape[1:], jnp.float32),
        ],
        in_specs=[IN_VMEM] * 4,
        out_specs=[IN_VMEM] * 4,
        scratch_shapes=[
            pltpu.VMEM((batch - 1, 3, seq, rows, width), dtype),
            pltpu.VMEM((batch - 1,) + output.shape[1:], dtype),
            pltpu.VMEM((batch - 1, 2, seq, rows, hidden), dtype),
            pltpu.VMEM((batch - 1,) + reduce.shape[1:], dtype),
            pltpu.VMEM((3, seq, rows, width), dtype),
            pltpu.VMEM((2, seq, rows, hidden), dtype),
            pltpu.SemaphoreType.DMA((4, batch)),
            pltpu.SemaphoreType.DMA((4, batch)),
            pltpu.SemaphoreType.DMA((2, seq)),
            pltpu.SemaphoreType.DMA((2, seq)),
        ],
        compiler_params=pltpu.CompilerParams(
            collective_id=3, has_side_effects=True, vmem_limit_bytes=40 * MIB
        ),
    )(attend, output, expand, reduce)


def total_kernel(seq, batch, tile, total, tiles, sends, recvs):
    greet_all(seq, batch)
    finish = spread_tile(seq, batch, tile, tiles, sends, recvs)
    tiles[lax.axis_index("seq") * batch + lax.axis_index("batch")] = tile[...]
    finish()
    total[...] = jnp.sum(tiles[...], axis=0)


def sum_tile(seq, batch, tile):
    sems = pltpu.SemaphoreType.DMA((seq * batch,))
    return pl.pallas_call(
        functools.partial(total_kernel, seq, batch),
        out_shape=jax.ShapeDtypeStruct(tile.shape, jnp.float32),
        in_specs=[IN_VMEM],
        out_specs=IN_VMEM,
        scratch_shapes=[pltpu.VMEM((seq * batch,) + tile.shape, jnp.float32), sems, sems],
        compiler_params=pltpu.CompilerParams(
            collective_id=4, has_side_effects=True, vmem_limit_bytes=16 * MIB
        ),
    )(tile)


def turn(values, cos_lanes, sin_lanes):
    half = HEAD_DIM // 2
    lane = lax.broadcasted_iota(jnp.int32, values.shape, 1)
    swapped = jnp.where(
        lax.rem(lane, HEAD_DIM) < half,
        pltpu.roll(values, values.shape[1] - half, 1),
        pltpu.roll(values, half, 1),
    )
    return values * cos_lanes + swapped * sin_lanes


def head_only(values, head):
    lane = lax.broadcasted_iota(jnp.int32, values.shape, 1)
    inside = jnp.logical_and(lane >= head * HEAD_DIM, lane < (head + 1) * HEAD_DIM)
    return jnp.where(inside, values, jnp.zeros_like(values))


def bias_columns(key_label, query_label, bias, head):
    same = key_label == query_label
    return jnp.where(key_label >= 0.0, jnp.where(same, bias[0, head], bias[1, head]), MASKED), same


def attention_kernel(
    project,
    cos_lanes,
    sin_lanes,
    key_label,
    query_label,
    bias,
    query_out,
    key_out,
    value_out,
    mixed,
    exact,
    lse,
    query_turned,
    value_turned,
    key_heads,
    mixed_turned,
):
    heads = LANES // HEAD_DIM
    query = turn(project[0], cos_lanes[...], sin_lanes[...]).astype(jnp.bfloat16)
    key = turn(project[1], cos_lanes[...], sin_lanes[...]).astype(jnp.bfloat16)
    value = project[2].astype(jnp.bfloat16)
    query_out[...] = query
    key_out[...] = key
    value_out[...] = value
    query_turned[...] = (query.astype(jnp.float32) * HEAD_DIM ** (-0.5)).T.astype(jnp.bfloat16)
    value_turned[...] = value.astype(jnp.float32).T.astype(jnp.bfloat16)
    for head in range(heads):
        key_heads[head] = head_only(key, head)

    def one_block(block, unused):
        columns = pl.ds(pl.multiple_of(block * QUERY_BLOCK, QUERY_BLOCK), QUERY_BLOCK)
        for head in range(heads):
            rows = pl.ds(head * HEAD_DIM, HEAD_DIM)
            offset, same = bias_columns(key_label[...], query_label[0:1, columns], bias, head)
            scores = (
                jnp.dot(key_heads[head], query_turned[:, columns], preferred_element_type=jnp.float32)
                + offset
            )
            top = jnp.floor(jnp.max(scores, axis=0, keepdims=True))
            powers = jnp.exp(scores - top)
            total = jnp.sum(powers, axis=0, keepdims=True)
            lse[head : head + 1, columns] = top + jnp.log(total)
            probs = powers * (1.0 / total)
            rounded = probs.astype(jnp.bfloat16)
            residue = (probs - rounded.astype(jnp.float32)).astype(jnp.bfloat16)
            coarse = jnp.dot(value_turned[rows, :], rounded, preferred_element_type=jnp.float32)
            finest = jnp.dot(value_turned[rows, :], residue, preferred_element_type=jnp.float32)
            mixed_turned[rows, columns] = coarse
            exact[rows, columns] = coarse + finest
        return unused

    lax.fori_loop(0, project.shape[1] // QUERY_BLOCK, one_block, 0)
    mixed[...] = mixed_turned[...].T.astype(jnp.bfloat16)


def attention(project, cos_lanes, sin_lanes, key_label, query_label, bias):
    length = project.shape[1]
    low = jax.ShapeDtypeStruct((length, LANES), jnp.bfloat16)
    return pl.pallas_call(
        attention_kernel,
        out_shape=[
            low,
            low,
            low,
            low,
            jax.ShapeDtypeStruct((LANES, length), jnp.float32),
            jax.ShapeDtypeStruct((8, length), jnp.float32),
        ],
        in_specs=[IN_VMEM] * 5 + [IN_SMEM],
        out_specs=[IN_VMEM] * 6,
        scratch_shapes=[
            pltpu.VMEM((LANES, length), jnp.bfloat16),
            pltpu.VMEM((LANES, length), jnp.bfloat16),
            pltpu.VMEM((LANES // HEAD_DIM, length, LANES), jnp.bfloat16),
            pltpu.VMEM((LANES, length), jnp.float32),
        ],
        compiler_params=pltpu.CompilerParams(vmem_limit_bytes=48 * MIB),
    )(project, cos_lanes, sin_lanes, key_label, query_label, bias)


def attention_back_kernel(
    query,
    key,
    value,
    grad,
    exact,
    lse,
    cos_lanes,
    sin_lanes,
    key_label,
    query_label,
    bias,
    grad_project,
    bias_sums,
    query_turned,
    grad_turned,
    key_turned,
    key_heads,
    value_heads,
    query_heads,
    grad_heads,
    delta,
    query_total,
    key_total,
    value_total,
):
    heads = LANES // HEAD_DIM
    scale = HEAD_DIM ** (-0.5)
    scaled = query[...].astype(jnp.float32) * scale
    query_turned[...] = scaled.T.astype(jnp.bfloat16)
    key_turned[...] = key[...].astype(jnp.float32).T.astype(jnp.bfloat16)
    grad_wide = grad[...].astype(jnp.float32).T
    grad_turned[...] = grad_wide.astype(jnp.bfloat16)
    product = grad_wide * exact[...]
    for head in range(heads):
        rows = slice(head * HEAD_DIM, (head + 1) * HEAD_DIM)
        delta[head : head + 1, :] = jnp.sum(product[rows], axis=0, keepdims=True)
        key_heads[head] = head_only(key[...], head)
        value_heads[head] = head_only(value[...], head)
        query_heads[head] = head_only(scaled.astype(jnp.bfloat16), head)
        grad_heads[head] = head_only(grad[...], head)
    key_total[...] = jnp.zeros_like(key_total)
    value_total[...] = jnp.zeros_like(value_total)
    bias_sums[...] = jnp.zeros_like(bias_sums)

    def one_block(block, unused):
        columns = pl.ds(pl.multiple_of(block * QUERY_BLOCK, QUERY_BLOCK), QUERY_BLOCK)
        for head in range(heads):
            rows = pl.ds(head * HEAD_DIM, HEAD_DIM)
            offset, same = bias_columns(key_label[...], query_label[0:1, columns], bias, head)
            scores = (
                jnp.dot(key_heads[head], query_turned[:, columns], preferred_element_type=jnp.float32)
                + offset
            )
            probs = jnp.exp(scores - lse[head : head + 1, columns])
            grad_probs = jnp.dot(
                value_heads[head], grad_turned[:, columns], preferred_element_type=jnp.float32
            )
            grad_scores = (probs * (grad_probs - delta[head : head + 1, columns])).astype(jnp.bfloat16)
            value_total[...] += jnp.dot(
                probs.astype(jnp.bfloat16),
                grad_heads[head, columns],
                preferred_element_type=jnp.float32,
            )
            key_total[...] += jnp.dot(
                grad_scores, query_heads[head, columns], preferred_element_type=jnp.float32
            )
            query_total[rows, columns] = jnp.dot(
                key_turned[rows, :], grad_scores, preferred_element_type=jnp.float32
            )
            wide = grad_scores.astype(jnp.float32)
            for row, kept in ((head, same), (heads + head, jnp.logical_not(same))):
                bias_sums[row : row + 1, :] += jnp.sum(
                    jnp.where(kept, wide, 0.0), axis=0, keepdims=True
                )
        return unused

    lax.fori_loop(0, query.shape[0] // QUERY_BLOCK, one_block, 0)
    cosines, sines = cos_lanes[...], -sin_lanes[...]
    grad_project[0] = turn(query_total[...].T * scale, cosines, sines).astype(jnp.bfloat16)
    grad_project[1] = turn(key_total[...], cosines, sines).astype(jnp.bfloat16)
    grad_project[2] = value_total[...].astype(jnp.bfloat16)


def attention_back(query, key, value, grad, exact, lse, cos_lanes, sin_lanes, key_label, query_label, bias):
    length = query.shape[0]
    heads = LANES // HEAD_DIM
    turned = pltpu.VMEM((LANES, length), jnp.bfloat16)
    split = pltpu.VMEM((heads, length, LANES), jnp.bfloat16)
    return pl.pallas_call(
        attention_back_kernel,
        out_shape=[
            jax.ShapeDtypeStruct((3, length, LANES), jnp.bfloat16),
            jax.ShapeDtypeStruct((8, QUERY_BLOCK), jnp.float32),
        ],
        in_specs=[IN_VMEM] * 10 + [IN_SMEM],
        out_specs=[IN_VMEM] * 2,
        scratch_shapes=[
            turned,
            turned,
            turned,
            split,
            split,
            split,
            split,
            pltpu.VMEM((8, length), jnp.float32),
            pltpu.VMEM((LANES, length), jnp.float32),
            pltpu.VMEM((length, LANES), jnp.float32),
            pltpu.VMEM((length, LANES), jnp.float32),
        ],
        compiler_params=pltpu.CompilerParams(vmem_limit_bytes=48 * MIB),
    )(query, key, value, grad, exact, lse, cos_lanes, sin_lanes, key_label, query_label, bias)


def wide_dot(spec, left, right):
    return jnp.einsum(spec, left, right, preferred_element_type=jnp.float32)


def fast_body(
    seq,
    batch,
    inputs,
    teacher,
    lengths,
    variate_ids,
    time_ids,
    observed,
    attend_weight,
    output_weight,
    expand_weight,
    reduce_weight,
    norm_gains,
    variate_bias,
    attend_first,
    output_first,
    expand_first,
    reduce_first,
    gains_first,
    bias_first,
    attend_second,
    output_second,
    expand_second,
    reduce_second,
    gains_second,
    bias_second,
):
    low = jnp.bfloat16
    me, group = lax.axis_index("seq"), lax.axis_index("batch")
    rows = inputs.shape[1]
    length = rows * seq
    heads = HEADS // seq
    hidden_width = expand_weight.shape[2] // seq
    share = attend_weight.shape[1]
    states = inputs[0].astype(jnp.float32)
    positions = me * rows + jnp.arange(rows, dtype=jnp.int32)
    inside = positions < lengths[0]
    scored = jnp.logical_and(inside, observed[0] == 1)
    facts = [
        jnp.where(inside, variate_ids[0], -1).astype(jnp.float32),
        variate_ids[0].astype(jnp.float32),
        time_ids[0].astype(jnp.float32),
        scored.astype(jnp.float32),
    ]
    tile = jnp.concatenate([jnp.stack(facts), jnp.zeros((4, rows), jnp.float32)])
    unit_one, scale_one = normalize(states)
    act_one = (unit_one * norm_gains[0]).astype(low)
    attend_all, output_all, expand_all, reduce_all, act_all, tiles = call_weights(
        seq,
        batch,
        attend_weight.astype(low),
        output_weight.astype(low),
        expand_weight.astype(low),
        reduce_weight.astype(low),
        act_one,
        tile,
    )
    attend_all = attend_all.reshape(3, D, D // seq)
    output_all = output_all.reshape(D // seq, D)
    expand_all = expand_all.reshape(2, D, hidden_width)
    reduce_all = reduce_all.reshape(hidden_width, D)
    act_all = act_all.reshape(length, D)
    tiles = tiles.reshape(seq, batch, 8, rows)
    count_all = jnp.sum(tiles[:, :, 3])
    own = lax.dynamic_index_in_dim(tiles, group, 1, keepdims=False)
    key_label = own[:, 0].reshape(length, 1)
    query_label = jnp.broadcast_to(own[:, 1].reshape(1, length), (8, length))
    half_dim = HEAD_DIM // 2
    frequency = jnp.exp(-math.log(ROPE_BASE) * jnp.arange(half_dim).astype(jnp.float32) / half_dim)
    angle = own[:, 2].reshape(length, 1) * frequency
    cosine, sine = jnp.cos(angle), jnp.sin(angle)
    cos_lanes = jnp.tile(cosine, (1, 2 * heads))
    sin_lanes = jnp.tile(jnp.concatenate([-sine, sine], axis=1), (1, heads))
    bias = lax.dynamic_slice_in_dim(variate_bias, me * heads, heads, 1)

    project = wide_dot("td,cde->cte", act_all, attend_all)
    query, key, value, mixed, exact, lse = attention(
        project, cos_lanes, sin_lanes, key_label, query_label, bias
    )
    middle = states + scatter_rows(seq, wide_dot("td,de->te", mixed, output_all).astype(low))
    unit_two, scale_two = normalize(middle)
    act_two = (unit_two * norm_gains[1]).astype(low)
    act_two_all = gather_rows(seq, act_two)
    gate_up = wide_dot("td,cdf->ctf", act_two_all, expand_all)
    sigmoid = jax.nn.sigmoid(gate_up[0])
    hidden = (gate_up[0] * sigmoid * gate_up[1]).astype(low)
    output = middle + scatter_rows(seq, wide_dot("tf,fd->td", hidden, reduce_all).astype(low))
    error = output - teacher[0].astype(jnp.float32)
    local_square = jnp.sum(jnp.where(scored[:, None], error * error, 0.0))
    grad_out = jnp.where(scored[:, None], error * (2.0 / (count_all * D)), 0.0)
    branch_all = gather_rows(seq, grad_out.astype(low))
    reduce_grad = wide_dot("tf,td->fd", hidden, branch_all)
    grad_hidden = wide_dot("td,fd->tf", branch_all, reduce_all)
    grad_gate = grad_hidden * gate_up[1] * sigmoid * (1.0 + gate_up[0] * (1.0 - sigmoid))
    grad_up = grad_hidden * gate_up[0] * sigmoid
    grad_expand = jnp.stack([grad_gate, grad_up]).astype(low)
    expand_grad = wide_dot("td,ctf->cdf", act_two_all, grad_expand)
    grad_act_two = scatter_rows(seq, wide_dot("ctf,cdf->td", grad_expand, expand_all).astype(low))
    grad_middle = grad_out + norm_back(grad_act_two, unit_two, scale_two, norm_gains[1])
    grad_attn_all = gather_rows(seq, grad_middle.astype(low))
    output_grad = wide_dot("td,te->de", mixed, grad_attn_all)
    grad_mixed = wide_dot("te,de->td", grad_attn_all, output_all).astype(low)
    grad_project, bias_sums = attention_back(
        query,
        key,
        value,
        grad_mixed,
        exact,
        lse,
        cos_lanes,
        sin_lanes,
        key_label,
        query_label,
        bias,
    )
    attend_grad = wide_dot("td,cte->cde", act_all, grad_project)
    grad_act_one = scatter_rows(seq, wide_dot("cte,cde->td", grad_project, attend_all).astype(low))
    attend_share, output_share, expand_share, reduce_share = call_grads(
        seq,
        batch,
        attend_grad.astype(low).reshape(3, seq, batch, share, D // seq),
        output_grad.astype(low).reshape(batch, -1, D),
        expand_grad.astype(low).reshape(2, seq, batch, share, hidden_width),
        reduce_grad.astype(low).reshape(batch, -1, D),
    )
    attend_share, expand_share = attend_share.astype(jnp.float32), expand_share.astype(jnp.float32)
    grad_input = grad_middle + norm_back(grad_act_one, unit_one, scale_one, norm_gains[0])
    gains_grad = jnp.stack(
        [jnp.sum(grad_act_one * unit_one, axis=0), jnp.sum(grad_act_two * unit_two, axis=0)]
    )
    bias_grad = jnp.sum(bias_sums[: 2 * heads], axis=1).reshape(2, heads)
    bias_grad = lax.dynamic_update_slice_in_dim(
        jnp.zeros((2, HEADS), jnp.float32), bias_grad, me * heads, 1
    )
    local_squares = (
        jnp.sum(attend_share * attend_share)
        + jnp.sum(output_share * output_share)
        + jnp.sum(expand_share * expand_share)
        + jnp.sum(reduce_share * reduce_share)
    )
    small = jnp.concatenate([bias_grad.reshape(2 * HEADS), jnp.stack([local_squares, local_square])])
    small = jnp.pad(small, (0, 8 * LANES - small.shape[0])).reshape(8, LANES)
    totals = sum_tile(seq, batch, jnp.concatenate([gains_grad.reshape(-1, LANES), small]))
    gains_total = totals[:-8].reshape(2, D)
    bias_total = totals[-8, : 2 * HEADS].reshape(2, HEADS)
    square_sum, square_total = totals[-8, 2 * HEADS], totals[-8, 2 * HEADS + 1]
    loss = square_total / (count_all * D)
    grad_norm = jnp.sqrt(
        square_sum + jnp.sum(gains_total * gains_total) + jnp.sum(bias_total * bias_total)
    )
    clip_scale = jnp.minimum(1.0, CLIP_NORM / grad_norm)
    result = [output[None], loss, (grad_input * count_all * D)[None], grad_norm]
    for weight, first, second, gradient, rate in (
        (attend_weight, attend_first, attend_second, attend_share, RATE_ATTEND),
        (output_weight, output_first, output_second, output_share, RATE_OUTPUT),
        (expand_weight, expand_first, expand_second, expand_share, RATE_EXPAND),
        (reduce_weight, reduce_first, reduce_second, reduce_share, RATE_REDUCE),
    ):
        new, first_new, second_new = adam_step(
            weight, first, second, gradient * clip_scale, rate, WEIGHT_DECAY
        )
        result += [new, new.astype(low), first_new, second_new]
    for weight, first, second, gradient, rate in (
        (norm_gains, gains_first, gains_second, gains_total, RATE_GAINS),
        (variate_bias, bias_first, bias_second, bias_total, RATE_BIAS),
    ):
        result += adam_step(weight, first, second, gradient * clip_scale, rate, 0.0)
    return tuple(result)


def solution(mesh):
    seq, batch = mesh.shape["seq"], mesh.shape["batch"]
    body = functools.partial(fast_body, seq, batch) if fast_fits(seq, batch) else general_body
    in_specs = (
        P("batch", "seq", None),
        P("batch", "seq", None),
        P("batch"),
        P("batch", "seq"),
        P("batch", "seq"),
        P("batch", "seq"),
        P(None, ("seq", "batch"), None),
        P(("seq", "batch"), None),
        P(None, ("seq", "batch"), None),
        P(("seq", "batch"), None),
        P(),
        P(),
        P(None, ("seq", "batch"), None),
        P(("seq", "batch"), None),
        P(None, ("seq", "batch"), None),
        P(("seq", "batch"), None),
        P(),
        P(),
        P(None, ("seq", "batch"), None),
        P(("seq", "batch"), None),
        P(None, ("seq", "batch"), None),
        P(("seq", "batch"), None),
        P(),
        P(),
    )
    out_specs = (
        P("batch", "seq", None),
        P(),
        P("batch", "seq", None),
        P(),
        P(None, ("seq", "batch"), None),
        P(None, ("seq", "batch"), None),
        P(None, ("seq", "batch"), None),
        P(None, ("seq", "batch"), None),
        P(("seq", "batch"), None),
        P(("seq", "batch"), None),
        P(("seq", "batch"), None),
        P(("seq", "batch"), None),
        P(None, ("seq", "batch"), None),
        P(None, ("seq", "batch"), None),
        P(None, ("seq", "batch"), None),
        P(None, ("seq", "batch"), None),
        P(("seq", "batch"), None),
        P(("seq", "batch"), None),
        P(("seq", "batch"), None),
        P(("seq", "batch"), None),
        P(),
        P(),
        P(),
        P(),
        P(),
        P(),
    )
    return jax.shard_map(body, mesh=mesh, in_specs=in_specs, out_specs=out_specs, check_vma=False)
```

```python
import functools
import math
import types

import jax
import jax.numpy as jnp
from jax import lax
from jax.experimental import pallas as pl
from jax.experimental.pallas import tpu as pltpu
from jax.sharding import PartitionSpec as P

D = 1024
HEADS = 16
HEAD_DIM = 64
STEP = 10


NORM_EPS = 1e-05
ROPE_BASE = 10000.0
MASKED = -1e30
CLIP_NORM = 1.0
BETA_ONE = 0.9
BETA_TWO = 0.98
ADAM_EPS = 1e-08
WEIGHT_DECAY = 0.1
RATE_ATTEND = 0.03
RATE_OUTPUT = 0.5
RATE_EXPAND = 0.03
RATE_REDUCE = 0.015
RATE_GAINS = 1.0
RATE_BIAS = 0.5


def angles(times):
    half_dim = HEAD_DIM // 2
    frequency = jnp.exp(-math.log(ROPE_BASE) * jnp.arange(half_dim).astype(jnp.float32) / half_dim)
    angle_table = times.astype(jnp.float32)[..., None] * frequency
    return (jnp.cos(angle_table)[..., None, :], jnp.sin(angle_table)[..., None, :])


def rotate(values, cos_table, sin_table):
    half_dim = values.shape[-1] // 2
    first_half = values[..., :half_dim]
    second_half = values[..., half_dim:]
    return jnp.concatenate(
        [
            first_half * cos_table - second_half * sin_table,
            second_half * cos_table + first_half * sin_table,
        ],
        axis=-1,
    )


def unrotate(values, cos_table, sin_table):
    half_dim = values.shape[-1] // 2
    first_half = values[..., :half_dim]
    second_half = values[..., half_dim:]
    return jnp.concatenate(
        [
            first_half * cos_table + second_half * sin_table,
            second_half * cos_table - first_half * sin_table,
        ],
        axis=-1,
    )


def normalize(values):
    inv_scale = lax.rsqrt(jnp.mean(values * values, axis=-1, keepdims=True) + NORM_EPS)
    return (values * inv_scale, inv_scale)


def norm_back(grad_act, unit_rows, inv_scale, gain_row):
    grad_unit = grad_act * gain_row
    return inv_scale * (
        grad_unit - unit_rows * jnp.mean(grad_unit * unit_rows, axis=-1, keepdims=True)
    )


def score_block(query_rows, query_labels, key_rows, key_labels, bias_table):
    scores = jnp.einsum(
        "ihe,jhe->hij", query_rows, key_rows, preferred_element_type=jnp.float32
    ) * HEAD_DIM ** (-0.5)
    same_var = query_labels[:, None] == key_labels[None, :]
    scores = scores + jnp.where(
        same_var[None], bias_table[0][:, None, None], bias_table[1][:, None, None]
    )
    scores = jnp.where(key_labels[None, None, :] >= 0, scores, MASKED)
    return (scores, same_var)


def block_grads(
    query_rows,
    query_labels,
    grad_rows,
    lse_rows,
    delta_rows,
    key_rows,
    value_rows,
    key_labels,
    bias_table,
    need_query,
    need_keys,
):
    scores, same_var = score_block(query_rows, query_labels, key_rows, key_labels, bias_table)
    weights = jnp.exp(scores - lse_rows.T[:, :, None])
    grad_weights = jnp.einsum(
        "ihe,jhe->hij", grad_rows, value_rows, preferred_element_type=jnp.float32
    )
    grad_scores = (weights * (grad_weights - delta_rows.T[:, :, None])).astype(jnp.bfloat16)
    result = ()
    if need_query:
        grad_query = jnp.einsum(
            "hij,jhe->ihe", grad_scores, key_rows, preferred_element_type=jnp.float32
        ) * HEAD_DIM ** (-0.5)
        widened = grad_scores.astype(jnp.float32)
        bias_same = jnp.sum(jnp.where(same_var[None], widened, 0.0), axis=(1, 2))
        bias_other = jnp.sum(jnp.where(same_var[None], 0.0, widened), axis=(1, 2))
        result = result + (grad_query, jnp.stack([bias_same, bias_other]))
    if need_keys:
        grad_key = jnp.einsum(
            "hij,ihe->jhe", grad_scores, query_rows, preferred_element_type=jnp.float32
        ) * HEAD_DIM ** (-0.5)
        grad_value = jnp.einsum(
            "hij,ihe->jhe",
            weights.astype(jnp.bfloat16),
            grad_rows,
            preferred_element_type=jnp.float32,
        )
        result = result + (grad_key, grad_value)
    return result


def adam_step(weight, first_moment, second_moment, gradient, step_rate, decay_rate):
    first_moment = BETA_ONE * first_moment + (1.0 - BETA_ONE) * gradient
    second_moment = BETA_TWO * second_moment + (1.0 - BETA_TWO) * gradient * gradient
    direction = (
        first_moment
        / (1.0 - BETA_ONE**STEP)
        / (jnp.sqrt(second_moment / (1.0 - BETA_TWO**STEP)) + ADAM_EPS)
    )
    return (weight - step_rate * (direction + decay_rate * weight), first_moment, second_moment)


def general_body(
    inputs,
    teacher,
    lengths,
    variate_ids,
    time_ids,
    observed,
    attend_weight,
    output_weight,
    expand_weight,
    reduce_weight,
    norm_gains,
    variate_bias,
    attend_first,
    output_first,
    expand_first,
    reduce_first,
    gains_first,
    bias_first,
    attend_second,
    output_second,
    expand_second,
    reduce_second,
    gains_second,
    bias_second,
):
    row_count = inputs.shape[1]
    length = row_count * lax.axis_size("seq")
    block_rows = math.gcd(length, 1024)
    blocks = length // block_rows
    states = inputs[0].astype(jnp.float32)
    positions = lax.axis_index("seq") * row_count + jnp.arange(row_count, dtype=jnp.int32)
    inside = positions < lengths[0]
    scored = jnp.logical_and(inside, observed[0] == 1)
    local_count = jnp.sum(scored.astype(jnp.int32))
    count_early = lax.psum(local_count, ("seq", "batch"))
    full_attend, full_output, full_expand, full_reduce = (
        lax.all_gather(attend_weight.astype(jnp.bfloat16), ("seq", "batch"), axis=1, tiled=True),
        lax.all_gather(output_weight.astype(jnp.bfloat16), ("seq", "batch"), axis=0, tiled=True),
        lax.all_gather(expand_weight.astype(jnp.bfloat16), ("seq", "batch"), axis=1, tiled=True),
        lax.all_gather(reduce_weight.astype(jnp.bfloat16), ("seq", "batch"), axis=0, tiled=True),
    )
    unit_one, scale_one = normalize(states)
    act_one = (unit_one * norm_gains[0]).astype(jnp.bfloat16)
    project = jnp.einsum("td,cde->cte", act_one, full_attend, preferred_element_type=jnp.float32)
    cos_table, sin_table = angles(time_ids[0])
    query = rotate(project[0].reshape(row_count, HEADS, HEAD_DIM), cos_table, sin_table).astype(
        jnp.bfloat16
    )
    key_rows = (
        rotate(project[1].reshape(row_count, HEADS, HEAD_DIM), cos_table, sin_table)
        .astype(jnp.bfloat16)
        .reshape(row_count, D)
    )
    value_rows = project[2].astype(jnp.bfloat16)
    own_labels = jnp.where(inside, variate_ids[0], -1).astype(jnp.bfloat16)
    all_keys, all_values, all_labels = (
        lax.all_gather(key_rows, "seq", axis=0, tiled=True),
        lax.all_gather(value_rows, "seq", axis=0, tiled=True),
        lax.all_gather(own_labels, "seq", axis=0, tiled=True),
    )
    key_blocks = all_keys.reshape(blocks, block_rows, HEADS, HEAD_DIM)
    value_blocks = all_values.reshape(blocks, block_rows, HEADS, HEAD_DIM)
    label_blocks = all_labels.astype(jnp.float32).reshape(blocks, block_rows)
    query_labels = variate_ids[0].astype(jnp.float32)

    def sweep_top(carry, pieces):
        running, sum_exp = carry
        scores, same_var = score_block(query, query_labels, pieces[0], pieces[1], variate_bias)
        raised = jnp.maximum(running, jnp.floor(jnp.max(scores, axis=-1)))
        sum_exp = sum_exp * jnp.exp(running - raised) + jnp.sum(
            jnp.exp(scores - raised[..., None]), axis=-1
        )
        return ((raised, sum_exp), None)

    start_top = jnp.full((HEADS, row_count), MASKED, jnp.float32)
    (row_top, sum_exp), unused = lax.scan(
        sweep_top,
        (start_top, jnp.zeros((HEADS, row_count), jnp.float32)),
        (key_blocks, label_blocks),
    )
    log_total = row_top + jnp.log(sum_exp)

    def sweep_out(carry, pieces):
        coarse, finest = carry
        scores, same_var = score_block(query, query_labels, pieces[0], pieces[2], variate_bias)
        weights = jnp.exp(scores - log_total[..., None])
        rounded = weights.astype(jnp.bfloat16)
        residue = (weights - rounded.astype(jnp.float32)).astype(jnp.bfloat16)
        coarse = coarse + jnp.einsum(
            "hij,jhe->ihe", rounded, pieces[1], preferred_element_type=jnp.float32
        )
        finest = finest + jnp.einsum(
            "hij,jhe->ihe", residue, pieces[1], preferred_element_type=jnp.float32
        )
        return ((coarse, finest), None)

    zero_heads = jnp.zeros((row_count, HEADS, HEAD_DIM), jnp.float32)
    (coarse, finest), unused = lax.scan(
        sweep_out, (zero_heads, zero_heads), (key_blocks, value_blocks, label_blocks)
    )
    exact_heads = coarse + finest
    mixed = coarse.reshape(row_count, D).astype(jnp.bfloat16)
    middle = states + jnp.dot(mixed, full_output, preferred_element_type=jnp.float32)
    unit_two, scale_two = normalize(middle)
    act_two = (unit_two * norm_gains[1]).astype(jnp.bfloat16)
    gate_up = jnp.einsum("td,cdf->ctf", act_two, full_expand, preferred_element_type=jnp.float32)
    sigmoid = jax.nn.sigmoid(gate_up[0])
    hidden = (gate_up[0] * sigmoid * gate_up[1]).astype(jnp.bfloat16)
    output = middle + jnp.dot(hidden, full_reduce, preferred_element_type=jnp.float32)
    error = output - teacher[0].astype(jnp.float32)
    local_square = jnp.sum(jnp.where(scored[:, None], error * error, 0.0))
    square_total = lax.psum(local_square, ("seq", "batch"))
    count_all = count_early.astype(jnp.float32)
    loss = square_total / (count_all * D)
    grad_out = jnp.where(scored[:, None], error * (2.0 / (count_all * D)), 0.0)
    back_attend, back_output, back_expand, back_reduce = (
        lax.all_gather(attend_weight.astype(jnp.bfloat16), ("seq", "batch"), axis=1, tiled=True),
        lax.all_gather(output_weight.astype(jnp.bfloat16), ("seq", "batch"), axis=0, tiled=True),
        lax.all_gather(expand_weight.astype(jnp.bfloat16), ("seq", "batch"), axis=1, tiled=True),
        lax.all_gather(reduce_weight.astype(jnp.bfloat16), ("seq", "batch"), axis=0, tiled=True),
    )
    grad_branch = grad_out.astype(jnp.bfloat16)
    reduce_grad = jnp.einsum("tf,td->fd", hidden, grad_branch, preferred_element_type=jnp.float32)
    grad_hidden = jnp.einsum(
        "td,fd->tf", grad_branch, back_reduce, preferred_element_type=jnp.float32
    )
    grad_gate = grad_hidden * gate_up[1] * sigmoid * (1.0 + gate_up[0] * (1.0 - sigmoid))
    grad_up = grad_hidden * gate_up[0] * sigmoid
    grad_expand = jnp.stack([grad_gate, grad_up]).astype(jnp.bfloat16)
    expand_grad = jnp.einsum(
        "td,ctf->cdf", act_two, grad_expand, preferred_element_type=jnp.float32
    )
    grad_act_two = jnp.einsum(
        "ctf,cdf->td", grad_expand, back_expand, preferred_element_type=jnp.float32
    )
    expand_share, reduce_share = (
        lax.psum_scatter(expand_grad, ("seq", "batch"), scatter_dimension=1, tiled=True),
        lax.psum_scatter(reduce_grad, ("seq", "batch"), scatter_dimension=0, tiled=True),
    )
    grad_middle = grad_out + norm_back(grad_act_two, unit_two, scale_two, norm_gains[1])
    grad_attn = grad_middle.astype(jnp.bfloat16)
    output_grad = jnp.einsum("td,te->de", mixed, grad_attn, preferred_element_type=jnp.float32)
    grad_mixed = jnp.einsum(
        "te,de->td", grad_attn, back_output, preferred_element_type=jnp.float32
    ).astype(jnp.bfloat16)
    grad_heads = grad_mixed.reshape(row_count, HEADS, HEAD_DIM)
    row_delta = jnp.sum(grad_heads.astype(jnp.float32) * exact_heads, axis=-1)
    lse_rows = log_total.T
    zero_bias = jnp.zeros((2, HEADS), jnp.float32)

    def sweep_query(carry, pieces):
        part_query, part_bias = block_grads(
            query,
            query_labels,
            grad_heads,
            lse_rows,
            row_delta,
            pieces[0],
            pieces[1],
            pieces[2],
            variate_bias,
            True,
            False,
        )
        return ((carry[0] + part_query, carry[1] + part_bias), None)

    (query_total, bias_grad), unused = lax.scan(
        sweep_query, (zero_heads, zero_bias), (key_blocks, value_blocks, label_blocks)
    )
    all_query, all_grad = (
        lax.all_gather(query.reshape(row_count, D), "seq", axis=0, tiled=True),
        lax.all_gather(grad_mixed, "seq", axis=0, tiled=True),
    )
    all_lse, all_delta = (
        lax.all_gather(lse_rows, "seq", axis=0, tiled=True),
        lax.all_gather(row_delta, "seq", axis=0, tiled=True),
    )
    key_heads = key_rows.reshape(row_count, HEADS, HEAD_DIM)
    value_heads = value_rows.reshape(row_count, HEADS, HEAD_DIM)
    own_float = own_labels.astype(jnp.float32)

    def sweep_keys(carry, pieces):
        part_key, part_value = block_grads(
            pieces[0],
            pieces[1],
            pieces[2],
            pieces[3],
            pieces[4],
            key_heads,
            value_heads,
            own_float,
            variate_bias,
            False,
            True,
        )
        return ((carry[0] + part_key, carry[1] + part_value), None)

    (key_total, value_heads_total), unused = lax.scan(
        sweep_keys,
        (zero_heads, zero_heads),
        (
            all_query.reshape(blocks, block_rows, HEADS, HEAD_DIM),
            label_blocks,
            all_grad.reshape(blocks, block_rows, HEADS, HEAD_DIM),
            all_lse.reshape(blocks, block_rows, HEADS),
            all_delta.reshape(blocks, block_rows, HEADS),
        ),
    )
    value_total = value_heads_total.reshape(row_count, D)
    grad_query = unrotate(query_total, cos_table, sin_table).reshape(row_count, D)
    grad_key = unrotate(key_total, cos_table, sin_table).reshape(row_count, D)
    grad_project = jnp.stack([grad_query, grad_key, value_total]).astype(jnp.bfloat16)
    attend_grad = jnp.einsum(
        "td,cte->cde", act_one, grad_project, preferred_element_type=jnp.float32
    )
    grad_act_one = jnp.einsum(
        "cte,cde->td", grad_project, back_attend, preferred_element_type=jnp.float32
    )
    attend_share, output_share = (
        lax.psum_scatter(attend_grad, ("seq", "batch"), scatter_dimension=1, tiled=True),
        lax.psum_scatter(output_grad, ("seq", "batch"), scatter_dimension=0, tiled=True),
    )
    grad_input = grad_middle + norm_back(grad_act_one, unit_one, scale_one, norm_gains[0])
    gains_grad = jnp.stack(
        [jnp.sum(grad_act_one * unit_one, axis=0), jnp.sum(grad_act_two * unit_two, axis=0)]
    )
    local_squares = (
        jnp.sum(attend_share * attend_share)
        + jnp.sum(output_share * output_share)
        + jnp.sum(expand_share * expand_share)
        + jnp.sum(reduce_share * reduce_share)
    )
    gains_total, bias_total, square_sum = lax.psum(
        (gains_grad, bias_grad, local_squares), ("seq", "batch")
    )
    grad_norm = jnp.sqrt(
        square_sum + jnp.sum(gains_total * gains_total) + jnp.sum(bias_total * bias_total)
    )
    clip_scale = jnp.minimum(1.0, CLIP_NORM / grad_norm)
    attend_new, attend_first_new, attend_second_new = adam_step(
        attend_weight,
        attend_first,
        attend_second,
        attend_share * clip_scale,
        RATE_ATTEND,
        WEIGHT_DECAY,
    )
    output_new, output_first_new, output_second_new = adam_step(
        output_weight,
        output_first,
        output_second,
        output_share * clip_scale,
        RATE_OUTPUT,
        WEIGHT_DECAY,
    )
    expand_new, expand_first_new, expand_second_new = adam_step(
        expand_weight,
        expand_first,
        expand_second,
        expand_share * clip_scale,
        RATE_EXPAND,
        WEIGHT_DECAY,
    )
    reduce_new, reduce_first_new, reduce_second_new = adam_step(
        reduce_weight,
        reduce_first,
        reduce_second,
        reduce_share * clip_scale,
        RATE_REDUCE,
        WEIGHT_DECAY,
    )
    gains_new, gains_first_new, gains_second_new = adam_step(
        norm_gains, gains_first, gains_second, gains_total * clip_scale, RATE_GAINS, 0.0
    )
    bias_new, bias_first_new, bias_second_new = adam_step(
        variate_bias, bias_first, bias_second, bias_total * clip_scale, RATE_BIAS, 0.0
    )
    input_gradient = (grad_input * count_all * D)[None]
    return (
        output[None],
        loss,
        input_gradient,
        grad_norm,
        attend_new,
        attend_new.astype(jnp.bfloat16),
        attend_first_new,
        attend_second_new,
        output_new,
        output_new.astype(jnp.bfloat16),
        output_first_new,
        output_second_new,
        expand_new,
        expand_new.astype(jnp.bfloat16),
        expand_first_new,
        expand_second_new,
        reduce_new,
        reduce_new.astype(jnp.bfloat16),
        reduce_first_new,
        reduce_second_new,
        gains_new,
        gains_first_new,
        gains_second_new,
        bias_new,
        bias_first_new,
        bias_second_new,
    )


MESH = pl.DeviceIdType.MESH
IN_VMEM = pl.BlockSpec(memory_space=pltpu.VMEM)
IN_SMEM = pl.BlockSpec(memory_space=pltpu.SMEM)
LANES = 128
HEADS_HERE = LANES // HEAD_DIM
MIB = 1 << 20
LOW = jnp.bfloat16
WIDE = jnp.float32
TOTAL_ROWS = 24


def fast_fits(seq, batch):
    return seq == 8 and batch == 4 and seq * LANES == D


def flip(index, mask):
    result, bit = index, 1
    while bit <= mask:
        if mask & bit:
            result = result + bit - 2 * bit * lax.rem(lax.div(index, bit), 2)
        bit *= 2
    return result


def push(source, target, send_sem, recv_sem, device):
    return pltpu.make_async_remote_copy(
        src_ref=source,
        dst_ref=target,
        send_sem=send_sem,
        recv_sem=recv_sem,
        device_id=device,
        device_id_type=MESH,
    )


def block_of(index, size):
    return pl.ds(pl.multiple_of(index * size, size), size)


def dot(left, right):
    return jnp.dot(left, right, preferred_element_type=WIDE)


def dot_turned(left, right):
    return lax.dot_general(left, right, (((1,), (1,)), ((), ())), preferred_element_type=WIDE)


def turned_dot(left, right):
    return lax.dot_general(left, right, (((0,), (0,)), ((), ())), preferred_element_type=WIDE)


class Team:
    def __init__(self, index, place):
        self.index, self.place = index, place

    def at(self, mask):
        return flip(self.index, mask)


def head_team(me, group):
    return Team(me, lambda mask: (flip(me, mask), group))


def feed_team(me, group):
    return Team(
        4 * lax.rem(group, 2) + lax.rem(me, 4),
        lambda mask: (flip(me, mask % 4), flip(group, mask // 4)),
    )


class Gather:
    def __init__(self, team, rows, all_rows, sends, recvs):
        self.team, self.rows, self.all_rows, self.sends, self.recvs = team, rows, all_rows, sends, recvs
        self.size = rows.shape[0]

    def copy(self, mask, passing):
        source = self.all_rows.at[block_of(self.team.at(mask - 1 if passing else 0), self.size)]
        return push(
            source if passing else self.rows,
            source,
            self.sends.at[mask],
            self.recvs.at[mask],
            self.team.place(1 if passing else mask),
        )

    def start(self):
        for mask in (6, 2, 4, 1):
            self.copy(mask, False).start()
        self.all_rows[block_of(self.team.index, self.size)] = self.rows[...]

    def pass_on(self, chip):
        self.copy(2 * chip, False).wait_recv()
        self.copy(2 * chip + 1, True).start()

    def complete(self, chip):
        self.copy(2 * chip + 1, chip > 0).wait_recv()

    def finish(self):
        for mask in (6, 2, 4, 1):
            self.copy(mask, False).wait_send()
        for mask in (3, 5, 7):
            self.copy(mask, True).wait_send()


def at_step(step, number, *works):
    @pl.when(step == number)
    def _():
        for work in works:
            work()


def each_chip(gather, work, after):
    def one_chip(chip, unused):
        @pl.when(chip == 0)
        def _():
            gather.complete(0)

        @pl.when(chip == 1)
        def _():
            gather.pass_on(1)
            gather.pass_on(2)
            gather.complete(1)

        @pl.when(chip == 2)
        def _():
            gather.pass_on(3)
            gather.complete(2)

        @pl.when(chip == 3)
        def _():
            gather.complete(3)

        work(chip)
        for number, works in after.items():
            at_step(chip, number, *works)
        return unused

    lax.fori_loop(0, 4, one_chip, 0)
    gather.finish()


class Scatter:
    def __init__(self, team, buffers, near_sends, near_recvs, far_sends, far_recvs):
        self.whole, self.keep, self.near_from, self.near, self.far_from, self.far = buffers
        self.sems = near_sends, near_recvs, far_sends, far_recvs
        self.team = team
        self.size = self.keep.shape[1]

    def near_copy(self, chip):
        return push(
            self.near_from.at[chip],
            self.near.at[chip],
            self.sems[0].at[chip],
            self.sems[1].at[chip],
            self.team.place(1),
        )

    def far_copy(self, chip):
        return push(
            self.far_from.at[chip],
            self.far.at[chip],
            self.sems[2].at[chip],
            self.sems[3].at[chip],
            self.team.place(2 * chip),
        )

    def put(self, chip, rows):
        core = lax.rem(self.team.index, 2)
        self.whole[...] = rows
        self.near_from[chip] = self.whole[block_of(1 - core, self.size)].astype(LOW)
        self.near_copy(chip).start()
        self.keep[chip] = self.whole[block_of(core, self.size)]

    def combine(self, chip):
        self.near_copy(chip).wait_recv()
        self.far_from[chip] = (self.keep[chip] + self.near[chip].astype(WIDE)).astype(LOW)
        self.far_copy(chip).start()

    def total(self):
        self.near_copy(0).wait_recv()
        total = self.keep[0] + self.near[0].astype(WIDE)
        for chip in (1, 2, 3):
            self.far_copy(chip).wait_recv()
            total = total + self.far[chip].astype(WIDE)
        for chip in (0, 1, 2, 3):
            self.near_copy(chip).wait_send()
            if chip:
                self.far_copy(chip).wait_send()
        return total


class LineGather:
    def __init__(self, part_of, sends, recvs, me, group):
        self.part_of, self.sends, self.recvs, self.me, self.group = part_of, sends, recvs, me, group
        self.middle = jnp.logical_and(group >= 1, group <= 2)

    def copy(self, part, target, slot):
        return push(
            self.part_of(part),
            self.part_of(part),
            self.sends.at[slot],
            self.recvs.at[part],
            (self.me, target),
        )

    def start(self):
        group = self.group

        @pl.when(self.middle)
        def _():
            self.copy(group, 3 - group, 3 - group).start()
            self.copy(group, 3 * (group - 1), 3 * (group - 1)).start()

        @pl.when(jnp.logical_not(self.middle))
        def _():
            for step in (2, 1, 3):
                other = lax.rem(group + step, 4)
                self.copy(group, other, other).start()

    def pass_on(self):
        group = self.group

        @pl.when(self.middle)
        def _():
            self.copy(3 - group, 3 * (group - 1), group).wait_recv()
            self.copy(3 - group, 3 * (group - 1), group).start()

    def land(self):
        group = self.group

        @pl.when(self.middle)
        def _():
            for part in (0, 3):
                self.copy(part, 3 - group, group).wait_recv()

        @pl.when(jnp.logical_not(self.middle))
        def _():
            for step in (1, 2, 3):
                other = lax.rem(group + step, 4)
                self.copy(other, other, other).wait_recv()

    def finish(self):
        group = self.group

        @pl.when(self.middle)
        def _():
            for other in (3 - group, 3 * (group - 1), group):
                self.copy(group, 3 - group, other).wait_send()

        @pl.when(jnp.logical_not(self.middle))
        def _():
            for step in (1, 2, 3):
                other = lax.rem(group + step, 4)
                self.copy(group, other, other).wait_send()


class LineScatter:
    def __init__(self, part_of, landing, sends, recvs, me, group):
        self.part_of, self.landing, self.sends, self.recvs = part_of, landing, sends, recvs
        self.me, self.group = me, group
        self.middle = jnp.logical_and(group >= 1, group <= 2)
        self.opposite = 3 - 3 * lax.div(group, 2)

    def copy(self, part, slot, target, sem):
        return push(
            self.part_of(part),
            self.landing.at[slot],
            self.sends.at[sem],
            self.recvs.at[slot],
            (self.me, target),
        )

    def start(self):
        group = self.group

        @pl.when(self.middle)
        def _():
            for other in (3 - group, 3 * (group - 1)):
                self.copy(other, group, other, other).start()

        @pl.when(jnp.logical_not(self.middle))
        def _():
            beside = 1 + lax.div(group, 3)
            self.copy(3 - group, beside, beside, 3 - group).start()
            for other in (3 - beside, beside):
                self.copy(other, group, other, other).start()

    def pass_on(self):
        group, opposite = self.group, self.opposite

        @pl.when(self.middle)
        def _():
            self.copy(opposite, group, opposite, group).wait_recv()
            part = self.part_of(opposite)
            part[...] = (part[...].astype(WIDE) + self.landing[group].astype(WIDE)).astype(LOW)
            self.copy(opposite, group, opposite, group).start()

    def land(self):
        group = self.group

        @pl.when(self.middle)
        def _():
            for slot in (0, 3 - group, 3):
                self.copy(group, slot, 3 - group, group).wait_recv()

        @pl.when(jnp.logical_not(self.middle))
        def _():
            for slot in (1, 2):
                self.copy(group, slot, slot, group).wait_recv()

    def add(self, own, landed, store):
        group = self.group

        @pl.when(self.middle)
        def _():
            store(own() + landed(0) + landed(3 - group) + landed(3))

        @pl.when(jnp.logical_not(self.middle))
        def _():
            store(own() + landed(1) + landed(2))

    def finish(self):
        group = self.group

        @pl.when(self.middle)
        def _():
            for sem in (3 - group, 3 * (group - 1), group):
                self.copy(group, group, 3 - group, sem).wait_send()

        @pl.when(jnp.logical_not(self.middle))
        def _():
            for sem in (3 - group, 1, 2):
                self.copy(group, group, 1, sem).wait_send()


class QuadGather:
    def __init__(self, part_of, sends, recvs, me, group):
        self.part_of, self.sends, self.recvs = part_of, sends, recvs
        self.part = 2 * lax.div(me, 4) + lax.div(group, 2)
        self.along_y, self.along_z = (flip(me, 4), group), (me, flip(group, 2))

    def copy(self, way):
        part = self.part_of(flip(self.part, 1) if way == 3 else self.part)
        device = self.along_z if way == 1 else self.along_y
        return push(part, part, self.sends.at[way], self.recvs.at[way], device)

    def start_y(self):
        self.copy(2).start()

    def start_z(self):
        self.copy(1).start()

    def pass_on(self):
        self.copy(1).wait_recv()
        self.copy(3).start()

    def land(self):
        self.copy(2).wait_recv()
        self.copy(3).wait_recv()

    def finish(self):
        for way in (1, 2, 3):
            self.copy(way).wait_send()


class QuadScatter:
    def __init__(self, part_of, landing, sends, recvs, me, group):
        self.part_of, self.landing, self.sends, self.recvs = part_of, landing, sends, recvs
        self.part = 2 * lax.div(me, 4) + lax.div(group, 2)
        self.along_y, self.along_z = (flip(me, 4), group), (me, flip(group, 2))

    def copy(self, slot):
        return push(
            self.part_of(flip(self.part, (2, 3, 1)[slot])),
            self.landing.at[slot],
            self.sends.at[slot],
            self.recvs.at[slot],
            self.along_z if slot == 2 else self.along_y,
        )

    def start(self):
        self.copy(1).start()
        self.copy(0).start()

    def pass_on(self):
        self.copy(1).wait_recv()
        part = self.part_of(flip(self.part, 1))
        part[...] = (part[...].astype(WIDE) + self.landing[1].astype(WIDE)).astype(LOW)
        self.copy(2).start()

    def land(self):
        self.copy(0).wait_recv()
        self.copy(2).wait_recv()

    def finish(self):
        for slot in (0, 1, 2):
            self.copy(slot).wait_send()


def chip_of(team, chip):
    here = lax.div(team.index, 2)
    if isinstance(chip, int):
        return flip(here, chip)
    column = lax.rem(lax.rem(here, 2) + lax.rem(chip, 2), 2)
    row = lax.rem(lax.div(here, 2) + lax.div(chip, 2), 2)
    return 2 * row + column


def turn_rows(values, cosine, sine):
    half = HEAD_DIM // 2
    pieces = []
    for start in range(0, values.shape[0], HEAD_DIM):
        first, second = values[start : start + half], values[start + half : start + HEAD_DIM]
        pieces += [first * cosine - second * sine, second * cosine + first * sine]
    return jnp.concatenate(pieces, axis=0)


def head_only(values, head):
    lane = lax.broadcasted_iota(jnp.int32, values.shape, 1)
    inside = jnp.logical_and(lane >= head * HEAD_DIM, lane < (head + 1) * HEAD_DIM)
    return jnp.where(inside, values, jnp.zeros_like(values))


def norm_rows(values):
    scale = lax.rsqrt(jnp.mean(values * values, axis=-1, keepdims=True) + NORM_EPS)
    return values * scale, scale


def feed_block(block):
    y, x, core, far_z, near_z = (block // 16, block // 8 % 2, block // 4 % 2, block // 2 % 2, block % 2)
    return 4 * near_z + 2 * x + core, 2 * y + far_z


def layer_kernel(seq, batch, ins, outs, mem):
    me, group = lax.axis_index("seq"), lax.axis_index("batch")
    rows = ins.inputs.shape[0]
    length = rows * seq
    pair = 2 * rows
    share = ins.attend.shape[1]
    wide_columns = ins.expand.shape[2] // D
    hidden_width = mem.reduce_all.shape[0] * mem.reduce_all.shape[1]
    blocks = ins.expand.shape[2] // LANES
    heads, feeds = head_team(me, group), feed_team(me, group)
    quad = 2 * lax.div(me, 4) + lax.div(group, 2)

    staged = [(ins.attend.at[which], mem.keep.at[0, block_of(which, share)]) for which in range(3)]
    staged.append((ins.output, mem.keep.at[0, block_of(3, share)]))
    staged.append((ins.reduce, mem.keep.at[1]))
    for which in range(2):
        for block in range(wide_columns):
            columns = slice(block * D, (block + 1) * D)
            staged.append(
                (ins.expand.at[which, :, columns], mem.keep.at[2 + which, block_of(block, share)])
            )
    staged = [
        pltpu.make_async_copy(source, target, mem.stage_sem.at[number])
        for number, (source, target) in enumerate(staged)
    ]
    for copy in staged:
        copy.start()
    barrier = pltpu.get_barrier_semaphore()
    for mask in range(1, seq):
        pl.semaphore_signal(barrier, inc=1, device_id=(flip(me, mask), group), device_id_type=MESH)
    for step in range(1, batch):
        pl.semaphore_signal(
            barrier, inc=1, device_id=(me, lax.rem(group + step, batch)), device_id_type=MESH
        )
    for mask in (5, 6, 7):
        pl.semaphore_signal(barrier, inc=1, device_id=feeds.place(mask), device_id_type=MESH)

    unit_one, scale_one = norm_rows(ins.inputs[...].astype(WIDE))
    mem.own_rows[0] = (unit_one * ins.gains[0:1, :]).astype(LOW)
    for copy in staged:
        copy.wait()
    for which in range(3):
        mem.attend_low[which] = mem.keep[0, block_of(which, share)].astype(LOW)
    mem.output_all[group] = mem.keep[0, block_of(3, share)].astype(LOW)
    mem.reduce_all[quad] = mem.keep[1].astype(LOW)
    for which in range(2):
        for block in range(blocks):
            owner, part = feed_block(block)
            row, lane = divmod(block * LANES, D)
            mem.expand_low[which, owner, :, part * LANES : (part + 1) * LANES] = mem.keep[
                2 + which, block_of(row, share), lane : lane + LANES
            ].astype(LOW)
    pl.semaphore_wait(barrier, seq + batch + 1)

    masks = (6, 7, 4, 5, 2, 3, 1)

    def start_attend_columns():
        copies = []
        for mask in masks:
            copy = push(
                mem.attend_low.at[:, :, block_of(heads.at(mask), LANES)],
                mem.attend_all.at[:, me, group],
                mem.column_send.at[0, mask],
                mem.column_recv.at[0, mask],
                heads.place(mask),
            )
            copy.start()
            copies.append(copy)
        mem.attend_all[:, me, group] = mem.attend_low[:, :, block_of(me, LANES)]
        return copies

    def start_expand_columns():
        copies = []
        for mask in masks:
            copy = push(
                mem.expand_low.at[:, feeds.at(mask)],
                mem.expand_all.at[:, me, group],
                mem.column_send.at[1, mask],
                mem.column_recv.at[1, mask],
                feeds.place(mask),
            )
            copy.start()
            copies.append(copy)
        mem.expand_all[:, me, group] = mem.expand_low[:, feeds.index]
        return copies

    def expand_part_of(array, which):
        def part_of(part):
            return array.at[which, pl.ds(4 * lax.div(part, 2), 4), pl.ds(2 * lax.rem(part, 2), 2)]

        return part_of

    def line_gather(row, part_of):
        return LineGather(part_of, mem.line_send.at[row], mem.line_recv.at[row], me, group)

    def quad_gather(row, part_of):
        return QuadGather(part_of, mem.line_send.at[row], mem.line_recv.at[row], me, group)

    def gather(team, phase, all_rows):
        return Gather(
            team,
            mem.own_rows.at[phase],
            all_rows,
            mem.gather_send.at[phase],
            mem.gather_recv.at[phase],
        )

    def scatter(team, phase):
        return Scatter(
            team,
            (mem.whole, mem.keep, mem.near_from, mem.near, mem.far_from, mem.far),
            mem.near_send.at[phase],
            mem.near_recv.at[phase],
            mem.far_send.at[phase],
            mem.far_recv.at[phase],
        )

    attend_columns = start_attend_columns()
    line_output = line_gather(1, lambda part: mem.output_all.at[part])
    line_output.start()
    facts = Gather(heads, ins.facts, mem.facts_all, mem.facts_send, mem.facts_recv)
    facts.start()
    acts = gather(heads, 0, mem.act_one)
    acts.start()
    for copy in attend_columns:
        copy.wait_recv()
    line_attend = line_gather(0, lambda part: mem.attend_all.at[:, :, part])
    line_attend.start()
    expand_columns = start_expand_columns()
    line_reduce = quad_gather(4, lambda part: mem.reduce_all.at[part])
    line_reduce.start_y()
    for chip in (1, 2, 3):
        facts.pass_on(chip)
    for chip in (0, 1, 2, 3):
        facts.complete(chip)
    facts.finish()
    step_rows = ins.facts.shape[0]
    half = HEAD_DIM // 2
    count = jnp.zeros((8, LANES), WIDE)
    for slot in range(seq):
        columns = slice(slot * rows, (slot + 1) * rows)
        start = slot * step_rows
        mem.cosine[:, columns] = mem.facts_all[start : start + half]
        mem.sine[:, columns] = mem.facts_all[start + half : start + 2 * half]
        labels = mem.facts_all[start + 2 * half : start + 2 * half + 8]
        mem.labels[:, columns] = labels
        count = count + labels
    mem.count[group] = count
    mem.key_label[...] = jnp.broadcast_to(mem.labels[0:1, :], (LANES, length)).T
    count_copies = []
    for step in range(1, batch):
        copy = push(
            mem.count.at[group],
            mem.count.at[group],
            mem.count_send.at[step],
            mem.count_recv.at[step],
            (me, lax.rem(group + step, batch)),
        )
        copy.start()
        count_copies.append(copy)
    acts.pass_on(1)
    acts.pass_on(2)
    line_output.pass_on()
    line_attend.pass_on()
    acts.pass_on(3)
    for chip in range(4):
        acts.complete(chip)
    acts.finish()
    for copy in expand_columns:
        copy.wait_recv()
    line_expand = [
        quad_gather(2 + which, expand_part_of(mem.expand_all, which)) for which in range(2)
    ]
    for line in line_expand:
        line.start_y()
    line_output.land()
    line_attend.land()
    for line in line_expand:
        line.start_z()
    line_reduce.start_z()

    def attend_matrix(which):
        return mem.attend_all[which].reshape(D, LANES)

    def project(block, unused):
        span = block_of(block, pair)
        act = mem.act_one[span, :]
        cosine, sine = mem.cosine[:, span], mem.sine[:, span]
        query = turn_rows(dot(act, attend_matrix(0)).T, cosine, sine).astype(LOW)
        mem.query_turned[:, span] = (query.astype(WIDE) * HEAD_DIM ** (-0.5)).astype(LOW)
        key = turn_rows(dot(act, attend_matrix(1)).T, cosine, sine).astype(LOW)
        mem.key_turned[:, span] = key
        key = key.astype(WIDE).T.astype(LOW)
        value = dot(act, attend_matrix(2)).astype(LOW)
        mem.value_turned[:, span] = value.astype(WIDE).T.astype(LOW)
        for head in range(HEADS_HERE):
            mem.key_heads[head, span, :] = head_only(key, head)
            mem.value_heads[head, span, :] = head_only(value, head)
        return unused

    lax.fori_loop(0, length // pair, project, 0)

    def masked_bias(columns, head):
        label = jnp.concatenate([mem.key_label[...]] * (pair // LANES), axis=1)
        same = label == mem.labels[1:2, columns]
        number = me * HEADS_HERE + head
        chosen = jnp.where(same, ins.bias[0, number], ins.bias[1, number])
        return jnp.where(label >= 0.0, chosen, MASKED), same

    def attend_block(chip):
        columns = block_of(chip_of(heads, chip), pair)
        for head in range(HEADS_HERE):
            span = slice(head * HEAD_DIM, (head + 1) * HEAD_DIM)
            offset, same = masked_bias(columns, head)
            scores = dot(mem.key_heads[head], mem.query_turned[:, columns]) + offset
            top = jnp.floor(jnp.max(scores, axis=0, keepdims=True))
            powers = jnp.exp(scores - top)
            total = jnp.sum(powers, axis=0, keepdims=True)
            mem.lse[head : head + 1, columns] = top + jnp.log(total)
            probs = powers * (1.0 / total)
            rounded = probs.astype(LOW)
            residue = (probs - rounded.astype(WIDE)).astype(LOW)
            coarse = dot(mem.value_turned[span, :], rounded)
            mem.exact[span, columns] = coarse + dot(mem.value_turned[span, :], residue)
            mem.mixed_wide[span, :] = coarse
        mem.mixed_turned[:, columns] = mem.mixed_wide[...].astype(LOW)
        return mem.mixed_wide[...].T.astype(LOW)

    sums = scatter(heads, 0)

    def attend_step(step, unused):
        chip = lax.rem(step + 1, 4)
        mixed = attend_block(chip)
        sums.put(chip, dot(mixed, mem.output_all[...].reshape(LANES, D)))
        at_step(step, 1, lambda: sums.combine(1))
        at_step(step, 2, lambda: sums.combine(2))
        return unused

    lax.fori_loop(0, 4, attend_step, 0)
    sums.combine(3)
    line_expand[0].pass_on()
    middle = ins.inputs[...].astype(WIDE) + sums.total()
    mem.middle[...] = middle
    unit_two, scale_two = norm_rows(middle)
    mem.own_rows[1] = (unit_two * ins.gains[1:2, :]).astype(LOW)
    acts = gather(feeds, 1, mem.act_two)
    acts.start()
    line_expand[1].pass_on()
    for line in line_expand:
        line.land()

    def expand_matrix(which):
        return mem.expand_all[which].reshape(D, hidden_width)

    def reduce_matrix():
        return mem.reduce_all[...].reshape(hidden_width, D)

    def feed(chip):
        span = block_of(chip_of(feeds, chip), pair)
        act = mem.act_two[span, :]
        gate = dot(act, expand_matrix(0))
        up = dot(act, expand_matrix(1))
        sigmoid = 1.0 / (1.0 + jnp.exp(-gate))
        swish = gate * sigmoid
        mem.by_up[span, :] = swish
        mem.by_gate[span, :] = up * sigmoid * (1.0 + gate * (1.0 - sigmoid))
        hidden = (swish * up).astype(LOW)
        mem.hidden[span, :] = hidden


    each_chip(acts, feed, {1: [line_reduce.pass_on]})
    line_reduce.land()
    sums = scatter(feeds, 1)

    def feed_down(step, unused):
        chip = lax.rem(step + 1, 4)
        span = block_of(chip_of(feeds, chip), pair)
        sums.put(chip, dot(mem.hidden[span, :], reduce_matrix()))
        at_step(step, 1, lambda: sums.combine(1))
        at_step(step, 2, lambda: sums.combine(2))
        return unused

    lax.fori_loop(0, 4, feed_down, 0)
    sums.combine(3)
    output = mem.middle[...] + sums.total()
    outs.layer_output[...] = output
    for copy in count_copies:
        copy.wait()
    count_all = jnp.sum(
        mem.count[0, 2:3] + mem.count[1, 2:3] + mem.count[2, 2:3] + mem.count[3, 2:3],
        axis=1,
        keepdims=True,
    )
    error = jnp.where(ins.scored[...] > 0.0, output - ins.teacher[...].astype(WIDE), 0.0)
    mem.squares[1:2, :] = jnp.sum(error * error, axis=0, keepdims=True)
    grad_out = error * (2.0 / (count_all * D))
    mem.grad_own[...] = grad_out
    mem.own_rows[2] = grad_out.astype(LOW)
    acts = gather(feeds, 2, mem.branch)
    acts.start()

    sums = scatter(feeds, 2)

    def feed_back(chip):
        span = block_of(chip_of(feeds, chip), pair)
        grad_hidden = dot_turned(mem.branch[span, :], reduce_matrix())
        grad_gate = (grad_hidden * mem.by_gate[span, :]).astype(LOW)
        grad_up = (grad_hidden * mem.by_up[span, :]).astype(LOW)
        mem.grad_gate[span, :] = grad_gate
        mem.grad_up[span, :] = grad_up
        sums.put(
            chip, dot_turned(grad_gate, expand_matrix(0)) + dot_turned(grad_up, expand_matrix(1))
        )

    each_chip(
        acts, feed_back, {2: [lambda: sums.combine(1)], 3: [lambda: sums.combine(2)]}
    )
    sums.combine(3)

    def line_scatter(row, part_of, landing):
        return LineScatter(
            part_of, landing, mem.back_send.at[row], mem.back_recv.at[row], me, group
        )

    def quad_scatter(row, part_of, landing):
        return QuadScatter(
            part_of, landing, mem.back_send.at[row], mem.back_recv.at[row], me, group
        )

    def reduce_grad(part, unused):
        mem.reduce_grad[part] = turned_dot(
            mem.hidden[:, block_of(part, rows)], mem.branch[...]
        ).astype(LOW)
        return unused

    lax.fori_loop(0, batch, reduce_grad, 0)
    back_reduce = quad_scatter(0, lambda part: mem.reduce_grad.at[part], mem.reduce_land)
    back_reduce.start()

    def expand_grad(which):
        grads = (mem.grad_gate, mem.grad_up)[which]

        def one_block(block, unused):
            products = turned_dot(mem.act_two[:, block_of(block, pair)], grads[...]).astype(LOW)
            mem.expand_grad[which, pl.ds(2 * block, 2)] = products.reshape(
                2, batch, share, hidden_width
            )
            return unused

        lax.fori_loop(0, seq // 2, one_block, 0)
        line = quad_scatter(
            1 + which, expand_part_of(mem.expand_grad, which), mem.expand_land.at[which]
        )
        line.start()
        return line

    back_expand = [expand_grad(0)]
    grad_act = sums.total()
    unit_two, scale_two = norm_rows(mem.middle[...])
    gain = ins.gains[1:2, :]
    grad_unit = grad_act * gain
    mem.gains[1:2, :] = jnp.sum(grad_act * unit_two, axis=0, keepdims=True)
    grad_middle = mem.grad_own[...] + scale_two * (
        grad_unit - unit_two * jnp.mean(grad_unit * unit_two, axis=-1, keepdims=True)
    )
    mem.grad_own[...] = grad_middle
    mem.own_rows[3] = grad_middle.astype(LOW)
    acts = gather(heads, 3, mem.grad_attn)
    acts.start()

    back_reduce.pass_on()
    back_expand.append(expand_grad(1))

    mem.query_total[...] = jnp.zeros_like(mem.query_total)
    mem.key_total[...] = jnp.zeros_like(mem.key_total)
    mem.value_total[...] = jnp.zeros_like(mem.value_total)
    mem.bias_sums[...] = jnp.zeros_like(mem.bias_sums)

    def attend_back(chip):
        columns = block_of(chip_of(heads, chip), pair)
        output_matrix = mem.output_all[...].reshape(LANES, D)
        grad_mixed = dot_turned(output_matrix, mem.grad_attn[columns, :]).astype(LOW)
        delta = grad_mixed.astype(WIDE) * mem.exact[:, columns]
        for head in range(HEADS_HERE):
            span = slice(head * HEAD_DIM, (head + 1) * HEAD_DIM)
            offset, same = masked_bias(columns, head)
            scores = dot(mem.key_heads[head], mem.query_turned[:, columns]) + offset
            probs = jnp.exp(scores - mem.lse[head : head + 1, columns])
            grad_probs = dot(mem.value_heads[head], grad_mixed)
            change = grad_probs - jnp.sum(delta[span], axis=0, keepdims=True)
            grad_scores = (probs * change).astype(LOW)
            mem.value_total[span, :] += dot_turned(grad_mixed[span], probs.astype(LOW))
            mem.key_total[span, :] += dot_turned(mem.query_turned[span, columns], grad_scores)
            mem.query_total[span, columns] = dot(mem.key_turned[span, :], grad_scores)
            wide = grad_scores.astype(WIDE)
            for row, kept in ((head, same), (HEADS_HERE + head, jnp.logical_not(same))):
                mem.bias_sums[row : row + 1, :] += jnp.sum(
                    jnp.where(kept, wide, 0.0), axis=0, keepdims=True
                )

    each_chip(acts, attend_back, {2: [back_expand[0].pass_on]})
    mem.output_grad[...] = (
        dot(mem.mixed_turned[...], mem.grad_attn[...]).astype(LOW).reshape(mem.output_grad.shape)
    )
    back_output = line_scatter(3, lambda part: mem.output_grad.at[part], mem.output_land)
    back_output.start()
    cosine, sine = mem.cosine[...], -mem.sine[...]
    scale = HEAD_DIM ** (-0.5)
    mem.grad_project[0] = turn_rows(mem.query_total[...] * scale, cosine, sine).astype(LOW)
    mem.grad_project[1] = turn_rows(mem.key_total[...], cosine, sine).astype(LOW)
    mem.grad_project[2] = mem.value_total[...].astype(LOW)

    def attend_grad(which, unused):
        grads = dot(mem.grad_project[which], mem.act_one[...])
        mem.attend_grad[which] = grads.T.astype(LOW).reshape(seq, batch, share, LANES)
        return unused

    lax.fori_loop(0, 3, attend_grad, 0)
    back_attend = line_scatter(4, lambda part: mem.attend_grad.at[:, :, part], mem.attend_land)
    back_attend.start()

    sums = scatter(heads, 3)

    def project_back(step, unused):
        chip = lax.rem(step + 1, 4)
        span = block_of(chip_of(heads, chip), pair)
        total = jnp.zeros((pair, D), WIDE)
        for which in range(3):
            grads = mem.grad_project[which, :, span].astype(WIDE).T.astype(LOW)
            total = total + dot_turned(grads, attend_matrix(which))
        sums.put(chip, total)
        at_step(step, 1, lambda: sums.combine(1))
        at_step(step, 2, lambda: sums.combine(2))
        return unused

    lax.fori_loop(0, 4, project_back, 0)
    sums.combine(3)

    back_expand[1].pass_on()
    back_output.pass_on()

    column_copies = []
    mem.squares[0:1, :] = jnp.zeros((1, D), WIDE)

    def add_squares(total):
        flat = total.reshape(-1, total.shape[-1])
        width = flat.shape[1]
        mem.squares[0:1, :width] += jnp.sum(flat * flat, axis=0, keepdims=True)

    def store_whole(total, out):
        out[...] = total
        add_squares(total)

    back_reduce.land()
    store_whole(
        mem.reduce_grad[quad].astype(WIDE)
        + mem.reduce_land[0].astype(WIDE)
        + mem.reduce_land[2].astype(WIDE),
        outs.reduce_share,
    )
    grad_act = sums.total()
    unit_one, scale_one = norm_rows(ins.inputs[...].astype(WIDE))
    gain = ins.gains[0:1, :]
    grad_unit = grad_act * gain
    mem.gains[0:1, :] = jnp.sum(grad_act * unit_one, axis=0, keepdims=True)
    grad_input = mem.grad_own[...] + scale_one * (
        grad_unit - unit_one * jnp.mean(grad_unit * unit_one, axis=-1, keepdims=True)
    )
    outs.input_gradient[...] = grad_input * (count_all * D)
    outs.count[...] = jnp.broadcast_to(count_all, (8, LANES))
    back_attend.pass_on()

    def expand_shares(which):
        back_expand[which].land()
        own = expand_part_of(mem.expand_grad, which)(quad)

        def one_block(block, unused):
            total = (
                own[block].astype(WIDE)
                + mem.expand_land[which, 0, block].astype(WIDE)
                + mem.expand_land[which, 2, block].astype(WIDE)
            )
            mem.expand_part[which, block] = total.astype(LOW)
            add_squares(total)
            return unused

        lax.fori_loop(0, 4, one_block, 0)
        for mask in masks:
            other = feeds.at(mask)
            copy = push(
                mem.expand_part.at[which, lax.rem(other, 4), lax.div(other, 4)],
                mem.expand_share.at[which, feeds.index],
                mem.share_send.at[which, mask],
                mem.share_recv.at[which, mask],
                feeds.place(mask),
            )
            copy.start()
            column_copies.append(copy)
        mem.expand_share[which, feeds.index] = mem.expand_part[
            which, lax.rem(feeds.index, 4), lax.div(feeds.index, 4)
        ]

    for which in range(2):
        expand_shares(which)
    back_output.land()
    back_output.add(
        lambda: mem.output_grad[group].astype(WIDE),
        lambda slot: mem.output_land[slot].astype(WIDE),
        lambda total: store_whole(total, outs.output_share),
    )
    back_attend.land()

    def attend_shares(block, unused):
        def store(total):
            mem.attend_part[:, block] = total.astype(LOW)
            add_squares(total)

        back_attend.add(
            lambda: mem.attend_grad[:, block, group].astype(WIDE),
            lambda slot: mem.attend_land[slot, :, block].astype(WIDE),
            store,
        )
        return unused

    lax.fori_loop(0, seq, attend_shares, 0)
    for mask in masks:
        copy = push(
            mem.attend_part.at[:, heads.at(mask)],
            outs.attend_share.at[:, :, block_of(me, LANES)],
            mem.share_send.at[2, mask],
            mem.share_recv.at[2, mask],
            heads.place(mask),
        )
        copy.start()
        column_copies.append(copy)
    outs.attend_share[:, :, block_of(me, LANES)] = mem.attend_part[:, me]

    lane = lax.broadcasted_iota(jnp.int32, (1, LANES), 1)
    lines = [
        mem.gains[which : which + 1, start : start + LANES]
        for which in range(2)
        for start in range(0, D, LANES)
    ]
    bias_line = jnp.zeros((1, LANES), WIDE)
    for row in range(2 * HEADS_HERE):
        place = row // HEADS_HERE * HEADS + me * HEADS_HERE + row % HEADS_HERE
        amount = jnp.sum(mem.bias_sums[row : row + 1, :], axis=1, keepdims=True)
        bias_line = bias_line + jnp.where(lane == place, amount, 0.0)
    amounts = jnp.sum(mem.squares[0:2, :], axis=1, keepdims=True)
    amount_line = jnp.where(lane == 0, amounts[0:1], 0.0) + jnp.where(lane == 1, amounts[1:2], 0.0)
    lines += [bias_line, amount_line, jnp.zeros((6, LANES), WIDE)]
    mem.plane_totals[me] = jnp.concatenate(lines, axis=0)
    plane_copies = []
    for mask in masks:
        copy = push(
            mem.plane_totals.at[me],
            mem.plane_totals.at[me],
            mem.total_send.at[0, mask],
            mem.total_recv.at[0, mask],
            (flip(me, mask), group),
        )
        copy.start()
        plane_copies.append(copy)
    for copy in plane_copies:
        copy.wait()
    mem.line_totals[group] = jnp.sum(mem.plane_totals[...], axis=0)
    total_copies = []
    for step in range(1, batch):
        copy = push(
            mem.line_totals.at[group],
            mem.line_totals.at[group],
            mem.total_send.at[1, step],
            mem.total_recv.at[1, step],
            (me, lax.rem(group + step, batch)),
        )
        copy.start()
        total_copies.append(copy)
    for copy in total_copies:
        copy.wait()
    outs.totals[...] = jnp.sum(mem.line_totals[...], axis=0)
    for copy in column_copies:
        copy.wait()
    for which in range(2):
        for block in range(blocks):
            owner, part = feed_block(block)
            outs.expand_share[which, :, block * LANES : (block + 1) * LANES] = mem.expand_share[
                which, owner, :, part * LANES : (part + 1) * LANES
            ]
    for copies in (attend_columns, expand_columns):
        for copy in copies:
            copy.wait_send()
    for line in [line_attend, line_output, line_reduce] + line_expand:
        line.finish()
    for line in [back_attend, back_output, back_reduce] + back_expand:
        line.finish()


def call_layer(seq, batch, inputs, teacher, facts, scored, bias, gains, attend, output, expand, reduce):
    rows, share, hidden = inputs.shape[0], attend.shape[1], expand.shape[2] // seq
    length, pair, chips = rows * seq, 2 * rows, seq // 2
    low = lambda *shape: pltpu.VMEM(shape, LOW)
    wide = lambda *shape: pltpu.VMEM(shape, WIDE)
    sems = lambda *shape: pltpu.SemaphoreType.DMA(shape)
    in_names = ["inputs", "teacher", "facts", "scored", "bias", "gains"]
    in_names += ["attend", "output", "expand", "reduce"]
    outs = dict(
        layer_output=((rows, D), WIDE),
        input_gradient=((rows, D), WIDE),
        totals=((TOTAL_ROWS, LANES), WIDE),
        count=((8, LANES), WIDE),
        attend_share=((3, share, D), LOW),
        output_share=((output.shape[0], D), WIDE),
        expand_share=((2, share, hidden * seq), LOW),
        reduce_share=((reduce.shape[0], D), WIDE),
    )
    scratch = dict(
        gains=wide(2, D),
        squares=wide(8, D),
        plane_totals=wide(seq, TOTAL_ROWS, LANES),
        line_totals=wide(batch, TOTAL_ROWS, LANES),
        attend_low=low(3, share, D),
        expand_low=low(2, seq, share, hidden),
        attend_all=low(3, seq, batch, share, LANES),
        output_all=low(batch, output.shape[0], D),
        expand_all=low(2, seq, batch, share, hidden),
        reduce_all=low(batch, reduce.shape[0], D),
        own_rows=low(4, rows, D),
        act_one=low(length, D),
        act_two=low(length, D),
        branch=low(length, D),
        grad_attn=low(length, D),
        facts_all=wide(seq * facts.shape[0], LANES),
        cosine=wide(HEAD_DIM // 2, length),
        sine=wide(HEAD_DIM // 2, length),
        labels=wide(8, length),
        key_label=wide(length, LANES),
        count=wide(batch, 8, LANES),
        query_turned=low(LANES, length),
        key_turned=low(LANES, length),
        value_turned=low(LANES, length),
        key_heads=low(HEADS_HERE, length, LANES),
        value_heads=low(HEADS_HERE, length, LANES),
        lse=wide(8, length),
        exact=wide(LANES, length),
        mixed_wide=wide(LANES, pair),
        mixed_turned=low(LANES, length),
        whole=wide(pair, D),
        keep=wide(chips, rows, D),
        near_from=low(chips, rows, D),
        near=low(chips, rows, D),
        far_from=low(chips, rows, D),
        far=low(chips, rows, D),
        middle=wide(rows, D),
        grad_own=wide(rows, D),
        by_up=wide(length, hidden),
        by_gate=wide(length, hidden),
        hidden=low(length, hidden),
        grad_gate=low(length, hidden),
        grad_up=low(length, hidden),
        query_total=wide(LANES, length),
        key_total=wide(LANES, length),
        value_total=wide(LANES, length),
        bias_sums=wide(8, pair),
        grad_project=low(3, LANES, length),
        reduce_grad=low(batch, reduce.shape[0], D),
        expand_grad=low(2, seq, batch, share, hidden),
        output_grad=low(batch, output.shape[0], D),
        attend_grad=low(3, seq, batch, share, LANES),
        reduce_land=low(3, reduce.shape[0], D),
        expand_land=low(2, 3, 4, 2, share, hidden),
        output_land=low(batch, output.shape[0], D),
        attend_land=low(batch, 3, seq, share, LANES),
        expand_part=low(2, 4, 2, share, hidden),
        expand_share=low(2, seq, share, hidden),
        attend_part=low(3, seq, share, LANES),
        stage_sem=sems(5 + 2 * (expand.shape[2] // D)),
        total_send=sems(2, seq),
        total_recv=sems(2, seq),
        column_send=sems(2, seq),
        column_recv=sems(2, seq),
        line_send=sems(5, batch),
        line_recv=sems(5, batch),
        facts_send=sems(seq),
        facts_recv=sems(seq),
        gather_send=sems(4, seq),
        gather_recv=sems(4, seq),
        count_send=sems(batch),
        count_recv=sems(batch),
        near_send=sems(4, chips),
        near_recv=sems(4, chips),
        far_send=sems(4, chips),
        far_recv=sems(4, chips),
        back_send=sems(5, batch),
        back_recv=sems(5, batch),
        share_send=sems(3, seq),
        share_recv=sems(3, seq),
    )

    places = dict.fromkeys(("attend", "output", "expand", "reduce"), pl.BlockSpec(memory_space=pl.ANY))
    places["bias"] = IN_SMEM

    def kernel(*refs):
        groups, start = [], 0
        for names in (in_names, outs, scratch):
            names = list(names)
            groups.append(types.SimpleNamespace(**dict(zip(names, refs[start : start + len(names)]))))
            start += len(names)
        layer_kernel(seq, batch, *groups)

    results = pl.pallas_call(
        kernel,
        out_shape=[jax.ShapeDtypeStruct(*out) for out in outs.values()],
        in_specs=[places.get(name, IN_VMEM) for name in in_names],
        out_specs=[IN_VMEM] * len(outs),
        scratch_shapes=list(scratch.values()),
        compiler_params=pltpu.CompilerParams(
            collective_id=0, has_side_effects=True, vmem_limit_bytes=63 * MIB
        ),
        name="layer",
    )(inputs, teacher, facts, scored, bias, gains, attend, output, expand, reduce)
    return types.SimpleNamespace(**dict(zip(outs, results)))


def update_kernel(
    totals,
    count,
    layer_output,
    input_gradient,
    attend_share,
    output_share,
    expand_share,
    reduce_share,
    gains,
    gains_first,
    gains_second,
    bias,
    bias_first,
    bias_second,
    *refs,
):
    olds, news = refs[:12], refs[12:]
    news[0][...] = layer_output[...]
    news[1][...] = input_gradient[...]
    gains_total = jnp.concatenate(
        [
            jnp.concatenate([totals[row + i : row + i + 1, :] for i in range(D // LANES)], axis=1)
            for row in (0, D // LANES)
        ],
        axis=0,
    )
    row = 2 * D // LANES
    bias_total = jnp.concatenate(
        [totals[row : row + 1, :HEADS], totals[row : row + 1, HEADS : 2 * HEADS]], axis=0
    )
    row += 1

    def sum_all(values):
        return jnp.sum(jnp.sum(values, axis=0, keepdims=True), axis=1, keepdims=True)

    squares = (
        totals[row : row + 1, 0:1] + sum_all(gains_total * gains_total) + sum_all(bias_total * bias_total)
    )
    grad_norm = jnp.sqrt(squares)
    clip = jnp.minimum(1.0, CLIP_NORM / grad_norm)
    news[2][...] = totals[row : row + 1, 1:2] / (count[0:1, 0:1] * D)
    news[3][...] = grad_norm
    shares = (attend_share, output_share, expand_share, reduce_share)
    rates = (RATE_ATTEND, RATE_OUTPUT, RATE_EXPAND, RATE_REDUCE)
    for number, (share, rate) in enumerate(zip(shares, rates)):
        weight, first, second = olds[3 * number : 3 * number + 3]
        new, copy, first_new, second_new = news[4 + 4 * number : 8 + 4 * number]
        scale = clip.reshape((1,) * share.ndim)
        new[...], first_new[...], second_new[...] = adam_step(
            weight[...], first[...], second[...], share[...].astype(WIDE) * scale, rate, WEIGHT_DECAY
        )
        copy[...] = new[...].astype(LOW)
    for number, (old, total, rate) in enumerate(
        (
            ((gains, gains_first, gains_second), gains_total, RATE_GAINS),
            ((bias, bias_first, bias_second), bias_total, RATE_BIAS),
        )
    ):
        new, first_new, second_new = news[20 + 3 * number : 23 + 3 * number]
        new[...], first_new[...], second_new[...] = adam_step(
            old[0][...], old[1][...], old[2][...], total * clip, rate, 0.0
        )


UPDATE_STEPS = 2


def cut_spec(shape):
    rows = shape[-2] // UPDATE_STEPS
    if len(shape) == 3:
        return pl.BlockSpec((shape[0], rows, shape[2]), lambda step: (0, step, 0))
    return pl.BlockSpec((rows, shape[1]), lambda step: (step, 0))


def whole_spec(shape):
    return pl.BlockSpec(shape, lambda step: (0,) * len(shape))


def call_update(done, shares, smalls, olds):
    whole = [done.totals, done.count]
    cut = [done.layer_output, done.input_gradient] + shares
    outs = [(done.layer_output, WIDE, cut_spec), (done.input_gradient, WIDE, cut_spec)]
    one = jax.ShapeDtypeStruct((1, 1), WIDE)
    outs += [(one, WIDE, whole_spec)] * 2
    for weight in olds[::3]:
        outs += [(weight, dtype, cut_spec) for dtype in (WIDE, LOW, WIDE, WIDE)]
    outs += [(small, WIDE, whole_spec) for small in smalls]
    return pl.pallas_call(
        update_kernel,
        grid=(UPDATE_STEPS,),
        out_shape=[jax.ShapeDtypeStruct(array.shape, dtype) for array, dtype, spec in outs],
        in_specs=[whole_spec(array.shape) for array in whole]
        + [cut_spec(array.shape) for array in cut]
        + [whole_spec(array.shape) for array in smalls]
        + [cut_spec(array.shape) for array in olds],
        out_specs=[spec(array.shape) for array, dtype, spec in outs],
        compiler_params=pltpu.CompilerParams(vmem_limit_bytes=63 * MIB),
        name="update",
    )(*whole, *cut, *smalls, *olds)


def fast_body(
    seq,
    batch,
    inputs,
    teacher,
    lengths,
    variate_ids,
    time_ids,
    observed,
    attend_weight,
    output_weight,
    expand_weight,
    reduce_weight,
    norm_gains,
    variate_bias,
    attend_first,
    output_first,
    expand_first,
    reduce_first,
    gains_first,
    bias_first,
    attend_second,
    output_second,
    expand_second,
    reduce_second,
    gains_second,
    bias_second,
):
    me = lax.axis_index("seq")
    rows = inputs.shape[1]
    positions = me * rows + jnp.arange(rows, dtype=jnp.int32)
    inside = positions < lengths[0]
    scored = jnp.logical_and(inside, observed[0] == 1)
    half_dim = HEAD_DIM // 2
    frequency = jnp.exp(-math.log(ROPE_BASE) * jnp.arange(half_dim).astype(WIDE) / half_dim)
    angle = frequency[:, None] * time_ids[0].astype(WIDE)[None, :]
    labels = jnp.stack(
        [
            jnp.where(inside, variate_ids[0], -1).astype(WIDE),
            variate_ids[0].astype(WIDE),
            scored.astype(WIDE),
        ]
    )
    facts = jnp.concatenate([jnp.cos(angle), jnp.sin(angle), jnp.pad(labels, ((0, 5), (0, 0)))])
    done = call_layer(
        seq,
        batch,
        inputs[0],
        teacher[0],
        facts,
        scored.astype(WIDE)[:, None],
        variate_bias,
        norm_gains,
        attend_weight,
        output_weight,
        expand_weight,
        reduce_weight,
    )
    results = call_update(
        done,
        [done.attend_share, done.output_share, done.expand_share, done.reduce_share],
        [norm_gains, gains_first, gains_second, variate_bias, bias_first, bias_second],
        [attend_weight, attend_first, attend_second]
        + [output_weight, output_first, output_second]
        + [expand_weight, expand_first, expand_second]
        + [reduce_weight, reduce_first, reduce_second],
    )
    output, input_gradient, loss, grad_norm = results[:4]
    return (
        output[None],
        loss.reshape(()),
        input_gradient[None],
        grad_norm.reshape(()),
    ) + tuple(results[4:])


def solution(mesh):
    seq, batch = mesh.shape["seq"], mesh.shape["batch"]
    body = functools.partial(fast_body, seq, batch) if fast_fits(seq, batch) else general_body
    in_specs = (
        P("batch", "seq", None),
        P("batch", "seq", None),
        P("batch"),
        P("batch", "seq"),
        P("batch", "seq"),
        P("batch", "seq"),
        P(None, ("seq", "batch"), None),
        P(("seq", "batch"), None),
        P(None, ("seq", "batch"), None),
        P(("seq", "batch"), None),
        P(),
        P(),
        P(None, ("seq", "batch"), None),
        P(("seq", "batch"), None),
        P(None, ("seq", "batch"), None),
        P(("seq", "batch"), None),
        P(),
        P(),
        P(None, ("seq", "batch"), None),
        P(("seq", "batch"), None),
        P(None, ("seq", "batch"), None),
        P(("seq", "batch"), None),
        P(),
        P(),
    )
    out_specs = (
        P("batch", "seq", None),
        P(),
        P("batch", "seq", None),
        P(),
        P(None, ("seq", "batch"), None),
        P(None, ("seq", "batch"), None),
        P(None, ("seq", "batch"), None),
        P(None, ("seq", "batch"), None),
        P(("seq", "batch"), None),
        P(("seq", "batch"), None),
        P(("seq", "batch"), None),
        P(("seq", "batch"), None),
        P(None, ("seq", "batch"), None),
        P(None, ("seq", "batch"), None),
        P(None, ("seq", "batch"), None),
        P(None, ("seq", "batch"), None),
        P(("seq", "batch"), None),
        P(("seq", "batch"), None),
        P(("seq", "batch"), None),
        P(("seq", "batch"), None),
        P(),
        P(),
        P(),
        P(),
        P(),
        P(),
    )
    return jax.shard_map(body, mesh=mesh, in_specs=in_specs, out_specs=out_specs, check_vma=False)
```

```python
import functools
import math
import types

import jax
import jax.numpy as jnp
from jax import lax
from jax.experimental import pallas as pl
from jax.experimental.pallas import tpu as pltpu
from jax.sharding import PartitionSpec as P

D = 1024
HEADS = 16
HEAD_DIM = 64
STEP = 10


NORM_EPS = 1e-05
ROPE_BASE = 10000.0
MASKED = -1e30
CLIP_NORM = 1.0
BETA_ONE = 0.9
BETA_TWO = 0.98
ADAM_EPS = 1e-08
WEIGHT_DECAY = 0.1
RATE_ATTEND = 0.03
RATE_OUTPUT = 0.5
RATE_EXPAND = 0.03
RATE_REDUCE = 0.015
RATE_GAINS = 1.0
RATE_BIAS = 0.5


def angles(times):
    half_dim = HEAD_DIM // 2
    frequency = jnp.exp(-math.log(ROPE_BASE) * jnp.arange(half_dim).astype(jnp.float32) / half_dim)
    angle_table = times.astype(jnp.float32)[..., None] * frequency
    return (jnp.cos(angle_table)[..., None, :], jnp.sin(angle_table)[..., None, :])


def rotate(values, cos_table, sin_table):
    half_dim = values.shape[-1] // 2
    first_half = values[..., :half_dim]
    second_half = values[..., half_dim:]
    return jnp.concatenate(
        [
            first_half * cos_table - second_half * sin_table,
            second_half * cos_table + first_half * sin_table,
        ],
        axis=-1,
    )


def unrotate(values, cos_table, sin_table):
    half_dim = values.shape[-1] // 2
    first_half = values[..., :half_dim]
    second_half = values[..., half_dim:]
    return jnp.concatenate(
        [
            first_half * cos_table + second_half * sin_table,
            second_half * cos_table - first_half * sin_table,
        ],
        axis=-1,
    )


def normalize(values):
    inv_scale = lax.rsqrt(jnp.mean(values * values, axis=-1, keepdims=True) + NORM_EPS)
    return (values * inv_scale, inv_scale)


def norm_back(grad_act, unit_rows, inv_scale, gain_row):
    grad_unit = grad_act * gain_row
    return inv_scale * (
        grad_unit - unit_rows * jnp.mean(grad_unit * unit_rows, axis=-1, keepdims=True)
    )


def score_block(query_rows, query_labels, key_rows, key_labels, bias_table):
    scores = jnp.einsum(
        "ihe,jhe->hij", query_rows, key_rows, preferred_element_type=jnp.float32
    ) * HEAD_DIM ** (-0.5)
    same_var = query_labels[:, None] == key_labels[None, :]
    scores = scores + jnp.where(
        same_var[None], bias_table[0][:, None, None], bias_table[1][:, None, None]
    )
    scores = jnp.where(key_labels[None, None, :] >= 0, scores, MASKED)
    return (scores, same_var)


def block_grads(
    query_rows,
    query_labels,
    grad_rows,
    lse_rows,
    delta_rows,
    key_rows,
    value_rows,
    key_labels,
    bias_table,
    need_query,
    need_keys,
):
    scores, same_var = score_block(query_rows, query_labels, key_rows, key_labels, bias_table)
    weights = jnp.exp(scores - lse_rows.T[:, :, None])
    grad_weights = jnp.einsum(
        "ihe,jhe->hij", grad_rows, value_rows, preferred_element_type=jnp.float32
    )
    grad_scores = (weights * (grad_weights - delta_rows.T[:, :, None])).astype(jnp.bfloat16)
    result = ()
    if need_query:
        grad_query = jnp.einsum(
            "hij,jhe->ihe", grad_scores, key_rows, preferred_element_type=jnp.float32
        ) * HEAD_DIM ** (-0.5)
        widened = grad_scores.astype(jnp.float32)
        bias_same = jnp.sum(jnp.where(same_var[None], widened, 0.0), axis=(1, 2))
        bias_other = jnp.sum(jnp.where(same_var[None], 0.0, widened), axis=(1, 2))
        result = result + (grad_query, jnp.stack([bias_same, bias_other]))
    if need_keys:
        grad_key = jnp.einsum(
            "hij,ihe->jhe", grad_scores, query_rows, preferred_element_type=jnp.float32
        ) * HEAD_DIM ** (-0.5)
        grad_value = jnp.einsum(
            "hij,ihe->jhe",
            weights.astype(jnp.bfloat16),
            grad_rows,
            preferred_element_type=jnp.float32,
        )
        result = result + (grad_key, grad_value)
    return result


def adam_step(weight, first_moment, second_moment, gradient, step_rate, decay_rate):
    first_moment = BETA_ONE * first_moment + (1.0 - BETA_ONE) * gradient
    second_moment = BETA_TWO * second_moment + (1.0 - BETA_TWO) * gradient * gradient
    direction = (
        first_moment
        / (1.0 - BETA_ONE**STEP)
        / (jnp.sqrt(second_moment / (1.0 - BETA_TWO**STEP)) + ADAM_EPS)
    )
    return (weight - step_rate * (direction + decay_rate * weight), first_moment, second_moment)


def general_body(
    inputs,
    teacher,
    lengths,
    variate_ids,
    time_ids,
    observed,
    attend_weight,
    output_weight,
    expand_weight,
    reduce_weight,
    norm_gains,
    variate_bias,
    attend_first,
    output_first,
    expand_first,
    reduce_first,
    gains_first,
    bias_first,
    attend_second,
    output_second,
    expand_second,
    reduce_second,
    gains_second,
    bias_second,
):
    row_count = inputs.shape[1]
    length = row_count * lax.axis_size("seq")
    block_rows = math.gcd(length, 1024)
    blocks = length // block_rows
    states = inputs[0].astype(jnp.float32)
    positions = lax.axis_index("seq") * row_count + jnp.arange(row_count, dtype=jnp.int32)
    inside = positions < lengths[0]
    scored = jnp.logical_and(inside, observed[0] == 1)
    local_count = jnp.sum(scored.astype(jnp.int32))
    count_early = lax.psum(local_count, ("seq", "batch"))
    full_attend, full_output, full_expand, full_reduce = (
        lax.all_gather(attend_weight.astype(jnp.bfloat16), ("seq", "batch"), axis=1, tiled=True),
        lax.all_gather(output_weight.astype(jnp.bfloat16), ("seq", "batch"), axis=0, tiled=True),
        lax.all_gather(expand_weight.astype(jnp.bfloat16), ("seq", "batch"), axis=1, tiled=True),
        lax.all_gather(reduce_weight.astype(jnp.bfloat16), ("seq", "batch"), axis=0, tiled=True),
    )
    unit_one, scale_one = normalize(states)
    act_one = (unit_one * norm_gains[0]).astype(jnp.bfloat16)
    project = jnp.einsum("td,cde->cte", act_one, full_attend, preferred_element_type=jnp.float32)
    cos_table, sin_table = angles(time_ids[0])
    query = rotate(project[0].reshape(row_count, HEADS, HEAD_DIM), cos_table, sin_table).astype(
        jnp.bfloat16
    )
    key_rows = (
        rotate(project[1].reshape(row_count, HEADS, HEAD_DIM), cos_table, sin_table)
        .astype(jnp.bfloat16)
        .reshape(row_count, D)
    )
    value_rows = project[2].astype(jnp.bfloat16)
    own_labels = jnp.where(inside, variate_ids[0], -1).astype(jnp.bfloat16)
    all_keys, all_values, all_labels = (
        lax.all_gather(key_rows, "seq", axis=0, tiled=True),
        lax.all_gather(value_rows, "seq", axis=0, tiled=True),
        lax.all_gather(own_labels, "seq", axis=0, tiled=True),
    )
    key_blocks = all_keys.reshape(blocks, block_rows, HEADS, HEAD_DIM)
    value_blocks = all_values.reshape(blocks, block_rows, HEADS, HEAD_DIM)
    label_blocks = all_labels.astype(jnp.float32).reshape(blocks, block_rows)
    query_labels = variate_ids[0].astype(jnp.float32)

    def sweep_top(carry, pieces):
        running, sum_exp = carry
        scores, same_var = score_block(query, query_labels, pieces[0], pieces[1], variate_bias)
        raised = jnp.maximum(running, jnp.floor(jnp.max(scores, axis=-1)))
        sum_exp = sum_exp * jnp.exp(running - raised) + jnp.sum(
            jnp.exp(scores - raised[..., None]), axis=-1
        )
        return ((raised, sum_exp), None)

    start_top = jnp.full((HEADS, row_count), MASKED, jnp.float32)
    (row_top, sum_exp), unused = lax.scan(
        sweep_top,
        (start_top, jnp.zeros((HEADS, row_count), jnp.float32)),
        (key_blocks, label_blocks),
    )
    log_total = row_top + jnp.log(sum_exp)

    def sweep_out(carry, pieces):
        coarse, finest = carry
        scores, same_var = score_block(query, query_labels, pieces[0], pieces[2], variate_bias)
        weights = jnp.exp(scores - log_total[..., None])
        rounded = weights.astype(jnp.bfloat16)
        residue = (weights - rounded.astype(jnp.float32)).astype(jnp.bfloat16)
        coarse = coarse + jnp.einsum(
            "hij,jhe->ihe", rounded, pieces[1], preferred_element_type=jnp.float32
        )
        finest = finest + jnp.einsum(
            "hij,jhe->ihe", residue, pieces[1], preferred_element_type=jnp.float32
        )
        return ((coarse, finest), None)

    zero_heads = jnp.zeros((row_count, HEADS, HEAD_DIM), jnp.float32)
    (coarse, finest), unused = lax.scan(
        sweep_out, (zero_heads, zero_heads), (key_blocks, value_blocks, label_blocks)
    )
    exact_heads = coarse + finest
    mixed = coarse.reshape(row_count, D).astype(jnp.bfloat16)
    middle = states + jnp.dot(mixed, full_output, preferred_element_type=jnp.float32)
    unit_two, scale_two = normalize(middle)
    act_two = (unit_two * norm_gains[1]).astype(jnp.bfloat16)
    gate_up = jnp.einsum("td,cdf->ctf", act_two, full_expand, preferred_element_type=jnp.float32)
    sigmoid = jax.nn.sigmoid(gate_up[0])
    hidden = (gate_up[0] * sigmoid * gate_up[1]).astype(jnp.bfloat16)
    output = middle + jnp.dot(hidden, full_reduce, preferred_element_type=jnp.float32)
    error = output - teacher[0].astype(jnp.float32)
    local_square = jnp.sum(jnp.where(scored[:, None], error * error, 0.0))
    square_total = lax.psum(local_square, ("seq", "batch"))
    count_all = count_early.astype(jnp.float32)
    loss = square_total / (count_all * D)
    grad_out = jnp.where(scored[:, None], error * (2.0 / (count_all * D)), 0.0)
    back_attend, back_output, back_expand, back_reduce = (
        lax.all_gather(attend_weight.astype(jnp.bfloat16), ("seq", "batch"), axis=1, tiled=True),
        lax.all_gather(output_weight.astype(jnp.bfloat16), ("seq", "batch"), axis=0, tiled=True),
        lax.all_gather(expand_weight.astype(jnp.bfloat16), ("seq", "batch"), axis=1, tiled=True),
        lax.all_gather(reduce_weight.astype(jnp.bfloat16), ("seq", "batch"), axis=0, tiled=True),
    )
    grad_branch = grad_out.astype(jnp.bfloat16)
    reduce_grad = jnp.einsum("tf,td->fd", hidden, grad_branch, preferred_element_type=jnp.float32)
    grad_hidden = jnp.einsum(
        "td,fd->tf", grad_branch, back_reduce, preferred_element_type=jnp.float32
    )
    grad_gate = grad_hidden * gate_up[1] * sigmoid * (1.0 + gate_up[0] * (1.0 - sigmoid))
    grad_up = grad_hidden * gate_up[0] * sigmoid
    grad_expand = jnp.stack([grad_gate, grad_up]).astype(jnp.bfloat16)
    expand_grad = jnp.einsum(
        "td,ctf->cdf", act_two, grad_expand, preferred_element_type=jnp.float32
    )
    grad_act_two = jnp.einsum(
        "ctf,cdf->td", grad_expand, back_expand, preferred_element_type=jnp.float32
    )
    expand_share, reduce_share = (
        lax.psum_scatter(expand_grad, ("seq", "batch"), scatter_dimension=1, tiled=True),
        lax.psum_scatter(reduce_grad, ("seq", "batch"), scatter_dimension=0, tiled=True),
    )
    grad_middle = grad_out + norm_back(grad_act_two, unit_two, scale_two, norm_gains[1])
    grad_attn = grad_middle.astype(jnp.bfloat16)
    output_grad = jnp.einsum("td,te->de", mixed, grad_attn, preferred_element_type=jnp.float32)
    grad_mixed = jnp.einsum(
        "te,de->td", grad_attn, back_output, preferred_element_type=jnp.float32
    ).astype(jnp.bfloat16)
    grad_heads = grad_mixed.reshape(row_count, HEADS, HEAD_DIM)
    row_delta = jnp.sum(grad_heads.astype(jnp.float32) * exact_heads, axis=-1)
    lse_rows = log_total.T
    zero_bias = jnp.zeros((2, HEADS), jnp.float32)

    def sweep_query(carry, pieces):
        part_query, part_bias = block_grads(
            query,
            query_labels,
            grad_heads,
            lse_rows,
            row_delta,
            pieces[0],
            pieces[1],
            pieces[2],
            variate_bias,
            True,
            False,
        )
        return ((carry[0] + part_query, carry[1] + part_bias), None)

    (query_total, bias_grad), unused = lax.scan(
        sweep_query, (zero_heads, zero_bias), (key_blocks, value_blocks, label_blocks)
    )
    all_query, all_grad = (
        lax.all_gather(query.reshape(row_count, D), "seq", axis=0, tiled=True),
        lax.all_gather(grad_mixed, "seq", axis=0, tiled=True),
    )
    all_lse, all_delta = (
        lax.all_gather(lse_rows, "seq", axis=0, tiled=True),
        lax.all_gather(row_delta, "seq", axis=0, tiled=True),
    )
    key_heads = key_rows.reshape(row_count, HEADS, HEAD_DIM)
    value_heads = value_rows.reshape(row_count, HEADS, HEAD_DIM)
    own_float = own_labels.astype(jnp.float32)

    def sweep_keys(carry, pieces):
        part_key, part_value = block_grads(
            pieces[0],
            pieces[1],
            pieces[2],
            pieces[3],
            pieces[4],
            key_heads,
            value_heads,
            own_float,
            variate_bias,
            False,
            True,
        )
        return ((carry[0] + part_key, carry[1] + part_value), None)

    (key_total, value_heads_total), unused = lax.scan(
        sweep_keys,
        (zero_heads, zero_heads),
        (
            all_query.reshape(blocks, block_rows, HEADS, HEAD_DIM),
            label_blocks,
            all_grad.reshape(blocks, block_rows, HEADS, HEAD_DIM),
            all_lse.reshape(blocks, block_rows, HEADS),
            all_delta.reshape(blocks, block_rows, HEADS),
        ),
    )
    value_total = value_heads_total.reshape(row_count, D)
    grad_query = unrotate(query_total, cos_table, sin_table).reshape(row_count, D)
    grad_key = unrotate(key_total, cos_table, sin_table).reshape(row_count, D)
    grad_project = jnp.stack([grad_query, grad_key, value_total]).astype(jnp.bfloat16)
    attend_grad = jnp.einsum(
        "td,cte->cde", act_one, grad_project, preferred_element_type=jnp.float32
    )
    grad_act_one = jnp.einsum(
        "cte,cde->td", grad_project, back_attend, preferred_element_type=jnp.float32
    )
    attend_share, output_share = (
        lax.psum_scatter(attend_grad, ("seq", "batch"), scatter_dimension=1, tiled=True),
        lax.psum_scatter(output_grad, ("seq", "batch"), scatter_dimension=0, tiled=True),
    )
    grad_input = grad_middle + norm_back(grad_act_one, unit_one, scale_one, norm_gains[0])
    gains_grad = jnp.stack(
        [jnp.sum(grad_act_one * unit_one, axis=0), jnp.sum(grad_act_two * unit_two, axis=0)]
    )
    local_squares = (
        jnp.sum(attend_share * attend_share)
        + jnp.sum(output_share * output_share)
        + jnp.sum(expand_share * expand_share)
        + jnp.sum(reduce_share * reduce_share)
    )
    gains_total, bias_total, square_sum = lax.psum(
        (gains_grad, bias_grad, local_squares), ("seq", "batch")
    )
    grad_norm = jnp.sqrt(
        square_sum + jnp.sum(gains_total * gains_total) + jnp.sum(bias_total * bias_total)
    )
    clip_scale = jnp.minimum(1.0, CLIP_NORM / grad_norm)
    attend_new, attend_first_new, attend_second_new = adam_step(
        attend_weight,
        attend_first,
        attend_second,
        attend_share * clip_scale,
        RATE_ATTEND,
        WEIGHT_DECAY,
    )
    output_new, output_first_new, output_second_new = adam_step(
        output_weight,
        output_first,
        output_second,
        output_share * clip_scale,
        RATE_OUTPUT,
        WEIGHT_DECAY,
    )
    expand_new, expand_first_new, expand_second_new = adam_step(
        expand_weight,
        expand_first,
        expand_second,
        expand_share * clip_scale,
        RATE_EXPAND,
        WEIGHT_DECAY,
    )
    reduce_new, reduce_first_new, reduce_second_new = adam_step(
        reduce_weight,
        reduce_first,
        reduce_second,
        reduce_share * clip_scale,
        RATE_REDUCE,
        WEIGHT_DECAY,
    )
    gains_new, gains_first_new, gains_second_new = adam_step(
        norm_gains, gains_first, gains_second, gains_total * clip_scale, RATE_GAINS, 0.0
    )
    bias_new, bias_first_new, bias_second_new = adam_step(
        variate_bias, bias_first, bias_second, bias_total * clip_scale, RATE_BIAS, 0.0
    )
    input_gradient = (grad_input * count_all * D)[None]
    return (
        output[None],
        loss,
        input_gradient,
        grad_norm,
        attend_new,
        attend_new.astype(jnp.bfloat16),
        attend_first_new,
        attend_second_new,
        output_new,
        output_new.astype(jnp.bfloat16),
        output_first_new,
        output_second_new,
        expand_new,
        expand_new.astype(jnp.bfloat16),
        expand_first_new,
        expand_second_new,
        reduce_new,
        reduce_new.astype(jnp.bfloat16),
        reduce_first_new,
        reduce_second_new,
        gains_new,
        gains_first_new,
        gains_second_new,
        bias_new,
        bias_first_new,
        bias_second_new,
    )


MESH = pl.DeviceIdType.MESH
IN_VMEM = pl.BlockSpec(memory_space=pltpu.VMEM)
IN_SMEM = pl.BlockSpec(memory_space=pltpu.SMEM)
LANES = 128
HEADS_HERE = LANES // HEAD_DIM
MIB = 1 << 20
LOW = jnp.bfloat16
WIDE = jnp.float32
TOTAL_ROWS = 24


def fast_fits(seq, batch):
    return seq == 8 and batch == 4 and seq * LANES == D


def flip(index, mask):
    result, bit = index, 1
    while bit <= mask:
        if mask & bit:
            result = result + bit - 2 * bit * lax.rem(lax.div(index, bit), 2)
        bit *= 2
    return result


def push(source, target, send_sem, recv_sem, device):
    return pltpu.make_async_remote_copy(
        src_ref=source,
        dst_ref=target,
        send_sem=send_sem,
        recv_sem=recv_sem,
        device_id=device,
        device_id_type=MESH,
    )


def block_of(index, size):
    return pl.ds(pl.multiple_of(index * size, size), size)


def dot(left, right):
    return jnp.dot(left, right, preferred_element_type=WIDE)


def dot_turned(left, right):
    return lax.dot_general(left, right, (((1,), (1,)), ((), ())), preferred_element_type=WIDE)


def turned_dot(left, right):
    return lax.dot_general(left, right, (((0,), (0,)), ((), ())), preferred_element_type=WIDE)


class Team:
    def __init__(self, index, place):
        self.index, self.place = index, place

    def at(self, mask):
        return flip(self.index, mask)


def head_team(me, group):
    return Team(me, lambda mask: (flip(me, mask), group))


def feed_team(me, group):
    return Team(
        4 * lax.rem(group, 2) + lax.rem(me, 4),
        lambda mask: (flip(me, mask % 4), flip(group, mask // 4)),
    )


class Gather:
    def __init__(self, team, rows, all_rows, sends, recvs):
        self.team, self.rows, self.all_rows, self.sends, self.recvs = team, rows, all_rows, sends, recvs
        self.size = rows.shape[0]

    def copy(self, mask, passing):
        source = self.all_rows.at[block_of(self.team.at(mask - 1 if passing else 0), self.size)]
        return push(
            source if passing else self.rows,
            source,
            self.sends.at[mask],
            self.recvs.at[mask],
            self.team.place(1 if passing else mask),
        )

    def start(self):
        for mask in (6, 2, 4, 1):
            self.copy(mask, False).start()
        self.all_rows[block_of(self.team.index, self.size)] = self.rows[...]

    def pass_on(self, chip):
        self.copy(2 * chip, False).wait_recv()
        self.copy(2 * chip + 1, True).start()

    def complete(self, chip):
        self.copy(2 * chip + 1, chip > 0).wait_recv()

    def finish(self):
        for mask in (6, 2, 4, 1):
            self.copy(mask, False).wait_send()
        for mask in (3, 5, 7):
            self.copy(mask, True).wait_send()


def at_step(step, number, *works):
    @pl.when(step == number)
    def _():
        for work in works:
            work()


def each_chip(gather, work, after):
    def one_chip(chip, unused):
        @pl.when(chip == 0)
        def _():
            gather.complete(0)

        @pl.when(chip == 1)
        def _():
            gather.pass_on(1)
            gather.pass_on(2)
            gather.complete(1)

        @pl.when(chip == 2)
        def _():
            gather.pass_on(3)
            gather.complete(2)

        @pl.when(chip == 3)
        def _():
            gather.complete(3)

        work(chip)
        for number, works in after.items():
            at_step(chip, number, *works)
        return unused

    lax.fori_loop(0, 4, one_chip, 0)
    gather.finish()


class Scatter:
    def __init__(self, team, buffers, near_sends, near_recvs, far_sends, far_recvs):
        self.whole, self.keep, self.near_from, self.near, self.far_from, self.far = buffers
        self.sems = near_sends, near_recvs, far_sends, far_recvs
        self.team = team
        self.size = self.keep.shape[1]

    def near_copy(self, chip):
        return push(
            self.near_from.at[chip],
            self.near.at[chip],
            self.sems[0].at[chip],
            self.sems[1].at[chip],
            self.team.place(1),
        )

    def far_copy(self, chip):
        return push(
            self.far_from.at[chip],
            self.far.at[chip],
            self.sems[2].at[chip],
            self.sems[3].at[chip],
            self.team.place(2 * chip),
        )

    def put(self, chip, rows):
        core = lax.rem(self.team.index, 2)
        self.whole[...] = rows
        self.near_from[chip] = self.whole[block_of(1 - core, self.size)].astype(LOW)
        self.near_copy(chip).start()
        self.keep[chip] = self.whole[block_of(core, self.size)]

    def combine(self, chip):
        self.near_copy(chip).wait_recv()
        self.far_from[chip] = (self.keep[chip] + self.near[chip].astype(WIDE)).astype(LOW)
        self.far_copy(chip).start()

    def total(self):
        self.near_copy(0).wait_recv()
        total = self.keep[0] + self.near[0].astype(WIDE)
        for chip in (1, 2, 3):
            self.far_copy(chip).wait_recv()
            total = total + self.far[chip].astype(WIDE)
        for chip in (0, 1, 2, 3):
            self.near_copy(chip).wait_send()
            if chip:
                self.far_copy(chip).wait_send()
        return total


class LineGather:
    def __init__(self, part_of, sends, recvs, me, group):
        self.part_of, self.sends, self.recvs, self.me, self.group = part_of, sends, recvs, me, group
        self.middle = jnp.logical_and(group >= 1, group <= 2)

    def copy(self, part, target, slot):
        return push(
            self.part_of(part),
            self.part_of(part),
            self.sends.at[slot],
            self.recvs.at[part],
            (self.me, target),
        )

    def start(self):
        group = self.group

        @pl.when(self.middle)
        def _():
            self.copy(group, 3 - group, 3 - group).start()
            self.copy(group, 3 * (group - 1), 3 * (group - 1)).start()

        @pl.when(jnp.logical_not(self.middle))
        def _():
            for step in (2, 1, 3):
                other = lax.rem(group + step, 4)
                self.copy(group, other, other).start()

    def pass_on(self):
        group = self.group

        @pl.when(self.middle)
        def _():
            self.copy(3 - group, 3 * (group - 1), group).wait_recv()
            self.copy(3 - group, 3 * (group - 1), group).start()

    def land(self):
        group = self.group

        @pl.when(self.middle)
        def _():
            for part in (0, 3):
                self.copy(part, 3 - group, group).wait_recv()

        @pl.when(jnp.logical_not(self.middle))
        def _():
            for step in (1, 2, 3):
                other = lax.rem(group + step, 4)
                self.copy(other, other, other).wait_recv()

    def finish(self):
        group = self.group

        @pl.when(self.middle)
        def _():
            for other in (3 - group, 3 * (group - 1), group):
                self.copy(group, 3 - group, other).wait_send()

        @pl.when(jnp.logical_not(self.middle))
        def _():
            for step in (1, 2, 3):
                other = lax.rem(group + step, 4)
                self.copy(group, other, other).wait_send()


class LineScatter:
    def __init__(self, part_of, landing, sends, recvs, me, group):
        self.part_of, self.landing, self.sends, self.recvs = part_of, landing, sends, recvs
        self.me, self.group = me, group
        self.middle = jnp.logical_and(group >= 1, group <= 2)
        self.opposite = 3 - 3 * lax.div(group, 2)

    def copy(self, part, slot, target, sem):
        return push(
            self.part_of(part),
            self.landing.at[slot],
            self.sends.at[sem],
            self.recvs.at[slot],
            (self.me, target),
        )

    def start(self):
        group = self.group

        @pl.when(self.middle)
        def _():
            for other in (3 - group, 3 * (group - 1)):
                self.copy(other, group, other, other).start()

        @pl.when(jnp.logical_not(self.middle))
        def _():
            beside = 1 + lax.div(group, 3)
            self.copy(3 - group, beside, beside, 3 - group).start()
            for other in (3 - beside, beside):
                self.copy(other, group, other, other).start()

    def pass_on(self):
        group, opposite = self.group, self.opposite

        @pl.when(self.middle)
        def _():
            self.copy(opposite, group, opposite, group).wait_recv()
            part = self.part_of(opposite)
            part[...] = (part[...].astype(WIDE) + self.landing[group].astype(WIDE)).astype(LOW)
            self.copy(opposite, group, opposite, group).start()

    def land(self):
        group = self.group

        @pl.when(self.middle)
        def _():
            for slot in (0, 3 - group, 3):
                self.copy(group, slot, 3 - group, group).wait_recv()

        @pl.when(jnp.logical_not(self.middle))
        def _():
            for slot in (1, 2):
                self.copy(group, slot, slot, group).wait_recv()

    def add(self, own, landed, store):
        group = self.group

        @pl.when(self.middle)
        def _():
            store(own() + landed(0) + landed(3 - group) + landed(3))

        @pl.when(jnp.logical_not(self.middle))
        def _():
            store(own() + landed(1) + landed(2))

    def finish(self):
        group = self.group

        @pl.when(self.middle)
        def _():
            for sem in (3 - group, 3 * (group - 1), group):
                self.copy(group, group, 3 - group, sem).wait_send()

        @pl.when(jnp.logical_not(self.middle))
        def _():
            for sem in (3 - group, 1, 2):
                self.copy(group, group, 1, sem).wait_send()


class QuadGather:
    def __init__(self, part_of, sends, recvs, me, group):
        self.part_of, self.sends, self.recvs = part_of, sends, recvs
        self.part = 2 * lax.div(me, 4) + lax.div(group, 2)
        self.along_y, self.along_z = (flip(me, 4), group), (me, flip(group, 2))

    def copy(self, way):
        part = self.part_of(flip(self.part, 1) if way == 3 else self.part)
        device = self.along_z if way == 1 else self.along_y
        return push(part, part, self.sends.at[way], self.recvs.at[way], device)

    def start_y(self):
        self.copy(2).start()

    def start_z(self):
        self.copy(1).start()

    def pass_on(self):
        self.copy(1).wait_recv()
        self.copy(3).start()

    def land(self):
        self.copy(2).wait_recv()
        self.copy(3).wait_recv()

    def finish(self):
        for way in (1, 2, 3):
            self.copy(way).wait_send()


class QuadScatter:
    def __init__(self, part_of, landing, sends, recvs, me, group):
        self.part_of, self.landing, self.sends, self.recvs = part_of, landing, sends, recvs
        self.part = 2 * lax.div(me, 4) + lax.div(group, 2)
        self.along_y, self.along_z = (flip(me, 4), group), (me, flip(group, 2))

    def copy(self, slot):
        return push(
            self.part_of(flip(self.part, (2, 3, 1)[slot])),
            self.landing.at[slot],
            self.sends.at[slot],
            self.recvs.at[slot],
            self.along_z if slot == 2 else self.along_y,
        )

    def start_far(self):
        self.copy(1).start()

    def start_near(self):
        self.copy(0).start()

    def pass_on(self):
        self.copy(1).wait_recv()
        part = self.part_of(flip(self.part, 1))
        part[...] = (part[...].astype(WIDE) + self.landing[1].astype(WIDE)).astype(LOW)
        self.copy(2).start()

    def land(self):
        self.copy(0).wait_recv()
        self.copy(2).wait_recv()

    def finish(self):
        for slot in (0, 1, 2):
            self.copy(slot).wait_send()


def chip_of(team, chip):
    here = lax.div(team.index, 2)
    if isinstance(chip, int):
        return flip(here, chip)
    column = lax.rem(lax.rem(here, 2) + lax.rem(chip, 2), 2)
    row = lax.rem(lax.div(here, 2) + lax.div(chip, 2), 2)
    return 2 * row + column


def turn_rows(values, cosine, sine):
    half = HEAD_DIM // 2
    pieces = []
    for start in range(0, values.shape[0], HEAD_DIM):
        first, second = values[start : start + half], values[start + half : start + HEAD_DIM]
        pieces += [first * cosine - second * sine, second * cosine + first * sine]
    return jnp.concatenate(pieces, axis=0)


def head_only(values, head):
    lane = lax.broadcasted_iota(jnp.int32, values.shape, 1)
    inside = jnp.logical_and(lane >= head * HEAD_DIM, lane < (head + 1) * HEAD_DIM)
    return jnp.where(inside, values, jnp.zeros_like(values))


def norm_rows(values):
    scale = lax.rsqrt(jnp.mean(values * values, axis=-1, keepdims=True) + NORM_EPS)
    return values * scale, scale


def feed_block(block):
    y, x, core, far_z, near_z = (block // 16, block // 8 % 2, block // 4 % 2, block // 2 % 2, block % 2)
    return 4 * near_z + 2 * x + core, 2 * y + far_z


def layer_kernel(seq, batch, ins, outs, mem):
    me, group = lax.axis_index("seq"), lax.axis_index("batch")
    rows = ins.inputs.shape[0]
    length = rows * seq
    pair = 2 * rows
    share = ins.attend.shape[1]
    wide_columns = ins.expand.shape[2] // D
    hidden_width = mem.reduce_all.shape[0] * mem.reduce_all.shape[1]
    blocks = ins.expand.shape[2] // LANES
    heads, feeds = head_team(me, group), feed_team(me, group)
    quad = 2 * lax.div(me, 4) + lax.div(group, 2)

    staged = [(ins.attend.at[which], mem.keep.at[0, block_of(which, share)]) for which in range(3)]
    staged.append((ins.output, mem.keep.at[0, block_of(3, share)]))
    staged.append((ins.reduce, mem.keep.at[1]))
    for which in range(2):
        for block in range(wide_columns):
            columns = slice(block * D, (block + 1) * D)
            staged.append(
                (ins.expand.at[which, :, columns], mem.keep.at[2 + which, block_of(block, share)])
            )
    staged = [
        pltpu.make_async_copy(source, target, mem.stage_sem.at[number])
        for number, (source, target) in enumerate(staged)
    ]
    for copy in staged:
        copy.start()
    barrier = pltpu.get_barrier_semaphore()
    for mask in range(1, seq):
        pl.semaphore_signal(barrier, inc=1, device_id=(flip(me, mask), group), device_id_type=MESH)
    for step in range(1, batch):
        pl.semaphore_signal(
            barrier, inc=1, device_id=(me, lax.rem(group + step, batch)), device_id_type=MESH
        )
    for mask in (5, 6, 7):
        pl.semaphore_signal(barrier, inc=1, device_id=feeds.place(mask), device_id_type=MESH)

    unit_one, scale_one = norm_rows(ins.inputs[...].astype(WIDE))
    mem.own_rows[0] = (unit_one * ins.gains[0:1, :]).astype(LOW)
    for copy in staged:
        copy.wait()
    for which in range(3):
        mem.attend_low[which] = mem.keep[0, block_of(which, share)].astype(LOW)
    mem.output_all[group] = mem.keep[0, block_of(3, share)].astype(LOW)
    mem.reduce_all[quad] = mem.keep[1].astype(LOW)
    for which in range(2):
        for block in range(blocks):
            owner, part = feed_block(block)
            row, lane = divmod(block * LANES, D)
            mem.expand_low[which, owner, :, part * LANES : (part + 1) * LANES] = mem.keep[
                2 + which, block_of(row, share), lane : lane + LANES
            ].astype(LOW)
    pl.semaphore_wait(barrier, seq + batch + 1)

    masks = (6, 7, 4, 5, 2, 3, 1)

    def start_attend_columns():
        copies = []
        for mask in masks:
            copy = push(
                mem.attend_low.at[:, :, block_of(heads.at(mask), LANES)],
                mem.attend_all.at[:, me, group],
                mem.column_send.at[0, mask],
                mem.column_recv.at[0, mask],
                heads.place(mask),
            )
            copy.start()
            copies.append(copy)
        mem.attend_all[:, me, group] = mem.attend_low[:, :, block_of(me, LANES)]
        return copies

    def start_expand_columns():
        copies = []
        for mask in masks:
            copy = push(
                mem.expand_low.at[:, feeds.at(mask)],
                mem.expand_all.at[:, me, group],
                mem.column_send.at[1, mask],
                mem.column_recv.at[1, mask],
                feeds.place(mask),
            )
            copy.start()
            copies.append(copy)
        mem.expand_all[:, me, group] = mem.expand_low[:, feeds.index]
        return copies

    def expand_part_of(array, which):
        def part_of(part):
            return array.at[which, pl.ds(4 * lax.div(part, 2), 4), pl.ds(2 * lax.rem(part, 2), 2)]

        return part_of

    def line_gather(row, part_of):
        return LineGather(part_of, mem.line_send.at[row], mem.line_recv.at[row], me, group)

    def quad_gather(row, part_of):
        return QuadGather(part_of, mem.line_send.at[row], mem.line_recv.at[row], me, group)

    def gather(team, phase, all_rows):
        return Gather(
            team,
            mem.own_rows.at[phase],
            all_rows,
            mem.gather_send.at[phase],
            mem.gather_recv.at[phase],
        )

    def scatter(team, phase):
        return Scatter(
            team,
            (mem.whole, mem.keep, mem.near_from, mem.near, mem.far_from, mem.far),
            mem.near_send.at[phase],
            mem.near_recv.at[phase],
            mem.far_send.at[phase],
            mem.far_recv.at[phase],
        )

    attend_columns = start_attend_columns()
    line_output = line_gather(1, lambda part: mem.output_all.at[part])
    line_output.start()
    facts = Gather(heads, ins.facts, mem.facts_all, mem.facts_send, mem.facts_recv)
    facts.start()
    for copy in attend_columns:
        copy.wait_recv()
    line_attend = line_gather(0, lambda part: mem.attend_all.at[:, :, part])
    line_attend.start()
    acts = gather(heads, 0, mem.act_one)
    acts.start()
    for chip in (1, 2, 3):
        facts.pass_on(chip)
    for chip in (0, 1, 2, 3):
        facts.complete(chip)
    facts.finish()
    step_rows = ins.facts.shape[0]
    half = HEAD_DIM // 2
    count = jnp.zeros((8, LANES), WIDE)
    for slot in range(seq):
        columns = slice(slot * rows, (slot + 1) * rows)
        start = slot * step_rows
        mem.cosine[:, columns] = mem.facts_all[start : start + half]
        mem.sine[:, columns] = mem.facts_all[start + half : start + 2 * half]
        labels = mem.facts_all[start + 2 * half : start + 2 * half + 8]
        mem.labels[:, columns] = labels
        count = count + labels
    mem.count[group] = count
    mem.key_label[...] = jnp.broadcast_to(mem.labels[0:1, :], (LANES, length)).T
    count_copies = []
    for step in range(1, batch):
        copy = push(
            mem.count.at[group],
            mem.count.at[group],
            mem.count_send.at[step],
            mem.count_recv.at[step],
            (me, lax.rem(group + step, batch)),
        )
        copy.start()
        count_copies.append(copy)
    acts.pass_on(1)
    acts.pass_on(2)
    line_output.pass_on()
    line_attend.pass_on()
    acts.pass_on(3)
    for chip in range(4):
        acts.complete(chip)
    acts.finish()
    line_output.land()
    line_attend.land()

    expand_columns = start_expand_columns()
    line_reduce = quad_gather(4, lambda part: mem.reduce_all.at[part])
    line_reduce.start_z()
    line_reduce.start_y()
    line_expand = [
        quad_gather(2 + which, expand_part_of(mem.expand_all, which)) for which in range(2)
    ]

    def attend_matrix(which):
        return mem.attend_all[which].reshape(D, LANES)

    def project(block, unused):
        span = block_of(block, pair)
        act = mem.act_one[span, :]
        cosine, sine = mem.cosine[:, span], mem.sine[:, span]
        query = turn_rows(dot(act, attend_matrix(0)).T, cosine, sine).astype(LOW)
        mem.query_turned[:, span] = (query.astype(WIDE) * HEAD_DIM ** (-0.5)).astype(LOW)
        key = turn_rows(dot(act, attend_matrix(1)).T, cosine, sine).astype(LOW)
        mem.key_turned[:, span] = key
        key = key.astype(WIDE).T.astype(LOW)
        value = dot(act, attend_matrix(2)).astype(LOW)
        mem.value_turned[:, span] = value.astype(WIDE).T.astype(LOW)
        for head in range(HEADS_HERE):
            mem.key_heads[head, span, :] = head_only(key, head)
            mem.value_heads[head, span, :] = head_only(value, head)
        return unused

    lax.fori_loop(0, length // pair, project, 0)
    for copy in expand_columns:
        copy.wait_recv()
    line_expand[0].start_y()

    def masked_bias(columns, head):
        label = jnp.concatenate([mem.key_label[...]] * (pair // LANES), axis=1)
        same = label == mem.labels[1:2, columns]
        number = me * HEADS_HERE + head
        chosen = jnp.where(same, ins.bias[0, number], ins.bias[1, number])
        return jnp.where(label >= 0.0, chosen, MASKED), same

    def attend_block(chip):
        columns = block_of(chip_of(heads, chip), pair)
        for head in range(HEADS_HERE):
            span = slice(head * HEAD_DIM, (head + 1) * HEAD_DIM)
            offset, same = masked_bias(columns, head)
            scores = dot(mem.key_heads[head], mem.query_turned[:, columns]) + offset
            top = jnp.floor(jnp.max(scores, axis=0, keepdims=True))
            powers = jnp.exp(scores - top)
            total = jnp.sum(powers, axis=0, keepdims=True)
            mem.lse[head : head + 1, columns] = top + jnp.log(total)
            probs = powers * (1.0 / total)
            rounded = probs.astype(LOW)
            residue = (probs - rounded.astype(WIDE)).astype(LOW)
            coarse = dot(mem.value_turned[span, :], rounded)
            mem.exact[span, columns] = coarse + dot(mem.value_turned[span, :], residue)
            mem.mixed_wide[span, :] = coarse
        mem.mixed_turned[:, columns] = mem.mixed_wide[...].astype(LOW)
        return mem.mixed_wide[...].T.astype(LOW)

    sums = scatter(heads, 0)

    def attend_step(step, unused):
        chip = lax.rem(step + 1, 4)
        mixed = attend_block(chip)
        sums.put(chip, dot(mixed, mem.output_all[...].reshape(LANES, D)))
        at_step(step, 1, lambda: sums.combine(1))
        at_step(step, 2, lambda: sums.combine(2), line_expand[0].start_z)
        return unused

    lax.fori_loop(0, 4, attend_step, 0)
    sums.combine(3)
    middle = ins.inputs[...].astype(WIDE) + sums.total()
    mem.middle[...] = middle
    unit_two, scale_two = norm_rows(middle)
    mem.own_rows[1] = (unit_two * ins.gains[1:2, :]).astype(LOW)
    acts = gather(feeds, 1, mem.act_two)
    acts.start()
    line_expand[1].start_z()
    line_expand[0].pass_on()
    line_reduce.pass_on()
    line_expand[1].start_y()
    line_expand[0].land()

    def expand_matrix(which):
        return mem.expand_all[which].reshape(D, hidden_width)

    def reduce_matrix():
        return mem.reduce_all[...].reshape(hidden_width, D)

    def feed_gate(chip):
        span = block_of(chip_of(feeds, chip), pair)
        mem.by_gate[span, :] = dot(mem.act_two[span, :], expand_matrix(0))

    each_chip(acts, feed_gate, {2: [line_expand[1].pass_on]})
    line_expand[1].land()
    line_reduce.land()
    sums = scatter(feeds, 1)

    def feed_down(step, unused):
        chip = lax.rem(step + 1, 4)
        span = block_of(chip_of(feeds, chip), pair)
        gate = mem.by_gate[span, :]
        up = dot(mem.act_two[span, :], expand_matrix(1))
        sigmoid = 1.0 / (1.0 + jnp.exp(-gate))
        swish = gate * sigmoid
        mem.by_up[span, :] = swish
        mem.by_gate[span, :] = up * sigmoid * (1.0 + gate * (1.0 - sigmoid))
        hidden = (swish * up).astype(LOW)
        mem.hidden[span, :] = hidden
        sums.put(chip, dot(hidden, reduce_matrix()))
        at_step(step, 1, lambda: sums.combine(1))
        at_step(step, 2, lambda: sums.combine(2))
        return unused

    lax.fori_loop(0, 4, feed_down, 0)
    sums.combine(3)
    output = mem.middle[...] + sums.total()
    outs.layer_output[...] = output
    for copy in count_copies:
        copy.wait()
    count_all = jnp.sum(
        mem.count[0, 2:3] + mem.count[1, 2:3] + mem.count[2, 2:3] + mem.count[3, 2:3],
        axis=1,
        keepdims=True,
    )
    error = jnp.where(ins.scored[...] > 0.0, output - ins.teacher[...].astype(WIDE), 0.0)
    mem.squares[1:2, :] = jnp.sum(error * error, axis=0, keepdims=True)
    grad_out = error * (2.0 / (count_all * D))
    mem.grad_own[...] = grad_out
    mem.own_rows[2] = grad_out.astype(LOW)
    acts = gather(feeds, 2, mem.branch)
    acts.start()

    sums = scatter(feeds, 2)

    def feed_back(chip):
        span = block_of(chip_of(feeds, chip), pair)
        grad_hidden = dot_turned(mem.branch[span, :], reduce_matrix())
        grad_gate = (grad_hidden * mem.by_gate[span, :]).astype(LOW)
        grad_up = (grad_hidden * mem.by_up[span, :]).astype(LOW)
        mem.grad_gate[span, :] = grad_gate
        mem.grad_up[span, :] = grad_up
        sums.put(
            chip, dot_turned(grad_gate, expand_matrix(0)) + dot_turned(grad_up, expand_matrix(1))
        )

    each_chip(
        acts, feed_back, {2: [lambda: sums.combine(1)], 3: [lambda: sums.combine(2)]}
    )
    sums.combine(3)

    def line_scatter(row, part_of, landing):
        return LineScatter(
            part_of, landing, mem.back_send.at[row], mem.back_recv.at[row], me, group
        )

    def quad_scatter(row, part_of, landing):
        return QuadScatter(
            part_of, landing, mem.back_send.at[row], mem.back_recv.at[row], me, group
        )

    def reduce_grad(part, unused):
        mem.reduce_grad[part] = turned_dot(
            mem.hidden[:, block_of(part, rows)], mem.branch[...]
        ).astype(LOW)
        return unused

    lax.fori_loop(0, batch, reduce_grad, 0)
    back_reduce = quad_scatter(0, lambda part: mem.reduce_grad.at[part], mem.reduce_land)
    back_reduce.start_far()

    def expand_grad(which):
        grads = (mem.grad_gate, mem.grad_up)[which]

        def one_block(block, unused):
            products = turned_dot(mem.act_two[:, block_of(block, pair)], grads[...]).astype(LOW)
            mem.expand_grad[which, pl.ds(2 * block, 2)] = products.reshape(
                2, batch, share, hidden_width
            )
            return unused

        lax.fori_loop(0, seq // 2, one_block, 0)
        line = quad_scatter(
            1 + which, expand_part_of(mem.expand_grad, which), mem.expand_land.at[which]
        )
        return line

    back_expand = [expand_grad(0)]
    back_expand[0].start_far()
    grad_act = sums.total()
    unit_two, scale_two = norm_rows(mem.middle[...])
    gain = ins.gains[1:2, :]
    grad_unit = grad_act * gain
    mem.gains[1:2, :] = jnp.sum(grad_act * unit_two, axis=0, keepdims=True)
    grad_middle = mem.grad_own[...] + scale_two * (
        grad_unit - unit_two * jnp.mean(grad_unit * unit_two, axis=-1, keepdims=True)
    )
    mem.grad_own[...] = grad_middle
    mem.own_rows[3] = grad_middle.astype(LOW)
    acts = gather(heads, 3, mem.grad_attn)
    acts.start()

    back_reduce.pass_on()
    back_expand.append(expand_grad(1))

    mem.query_total[...] = jnp.zeros_like(mem.query_total)
    mem.key_total[...] = jnp.zeros_like(mem.key_total)
    mem.value_total[...] = jnp.zeros_like(mem.value_total)
    mem.bias_sums[...] = jnp.zeros_like(mem.bias_sums)

    def attend_back(chip):
        columns = block_of(chip_of(heads, chip), pair)
        output_matrix = mem.output_all[...].reshape(LANES, D)
        grad_mixed = dot_turned(output_matrix, mem.grad_attn[columns, :]).astype(LOW)
        delta = grad_mixed.astype(WIDE) * mem.exact[:, columns]
        for head in range(HEADS_HERE):
            span = slice(head * HEAD_DIM, (head + 1) * HEAD_DIM)
            offset, same = masked_bias(columns, head)
            scores = dot(mem.key_heads[head], mem.query_turned[:, columns]) + offset
            probs = jnp.exp(scores - mem.lse[head : head + 1, columns])
            grad_probs = dot(mem.value_heads[head], grad_mixed)
            change = grad_probs - jnp.sum(delta[span], axis=0, keepdims=True)
            grad_scores = (probs * change).astype(LOW)
            mem.value_total[span, :] += dot_turned(grad_mixed[span], probs.astype(LOW))
            mem.key_total[span, :] += dot_turned(mem.query_turned[span, columns], grad_scores)
            mem.query_total[span, columns] = dot(mem.key_turned[span, :], grad_scores)
            wide = grad_scores.astype(WIDE)
            for row, kept in ((head, same), (HEADS_HERE + head, jnp.logical_not(same))):
                mem.bias_sums[row : row + 1, :] += jnp.sum(
                    jnp.where(kept, wide, 0.0), axis=0, keepdims=True
                )

    each_chip(
        acts,
        attend_back,
        {
            1: [back_expand[0].pass_on],
            2: [back_expand[1].start_far, back_reduce.start_near],
            3: [back_expand[0].start_near, back_expand[1].start_near],
        },
    )
    mem.output_grad[...] = (
        dot(mem.mixed_turned[...], mem.grad_attn[...]).astype(LOW).reshape(mem.output_grad.shape)
    )
    back_output = line_scatter(3, lambda part: mem.output_grad.at[part], mem.output_land)
    back_output.start()
    cosine, sine = mem.cosine[...], -mem.sine[...]
    scale = HEAD_DIM ** (-0.5)
    mem.grad_project[0] = turn_rows(mem.query_total[...] * scale, cosine, sine).astype(LOW)
    mem.grad_project[1] = turn_rows(mem.key_total[...], cosine, sine).astype(LOW)
    mem.grad_project[2] = mem.value_total[...].astype(LOW)

    def attend_grad(which, unused):
        grads = dot(mem.grad_project[which], mem.act_one[...])
        mem.attend_grad[which] = grads.T.astype(LOW).reshape(seq, batch, share, LANES)
        return unused

    lax.fori_loop(0, 3, attend_grad, 0)
    back_attend = line_scatter(4, lambda part: mem.attend_grad.at[:, :, part], mem.attend_land)
    back_attend.start()
    back_expand[1].pass_on()

    sums = scatter(heads, 3)

    def project_back(step, unused):
        chip = lax.rem(step + 1, 4)
        span = block_of(chip_of(heads, chip), pair)
        total = jnp.zeros((pair, D), WIDE)
        for which in range(3):
            grads = mem.grad_project[which, :, span].astype(WIDE).T.astype(LOW)
            total = total + dot_turned(grads, attend_matrix(which))
        sums.put(chip, total)
        at_step(step, 1, lambda: sums.combine(1))
        at_step(step, 2, lambda: sums.combine(2))
        return unused

    lax.fori_loop(0, 4, project_back, 0)
    sums.combine(3)

    back_output.pass_on()

    column_copies = []
    mem.squares[0:1, :] = jnp.zeros((1, D), WIDE)

    def add_squares(total):
        flat = total.reshape(-1, total.shape[-1])
        width = flat.shape[1]
        mem.squares[0:1, :width] += jnp.sum(flat * flat, axis=0, keepdims=True)

    def store_whole(total, out):
        out[...] = total
        add_squares(total)

    back_reduce.land()
    store_whole(
        mem.reduce_grad[quad].astype(WIDE)
        + mem.reduce_land[0].astype(WIDE)
        + mem.reduce_land[2].astype(WIDE),
        outs.reduce_share,
    )
    grad_act = sums.total()
    unit_one, scale_one = norm_rows(ins.inputs[...].astype(WIDE))
    gain = ins.gains[0:1, :]
    grad_unit = grad_act * gain
    mem.gains[0:1, :] = jnp.sum(grad_act * unit_one, axis=0, keepdims=True)
    grad_input = mem.grad_own[...] + scale_one * (
        grad_unit - unit_one * jnp.mean(grad_unit * unit_one, axis=-1, keepdims=True)
    )
    outs.input_gradient[...] = grad_input * (count_all * D)
    outs.count[...] = jnp.broadcast_to(count_all, (8, LANES))
    back_attend.pass_on()

    def expand_shares(which):
        back_expand[which].land()
        own = expand_part_of(mem.expand_grad, which)(quad)

        def one_block(block, unused):
            total = (
                own[block].astype(WIDE)
                + mem.expand_land[which, 0, block].astype(WIDE)
                + mem.expand_land[which, 2, block].astype(WIDE)
            )
            mem.expand_part[which, block] = total.astype(LOW)
            add_squares(total)
            return unused

        lax.fori_loop(0, 4, one_block, 0)
        for mask in masks:
            other = feeds.at(mask)
            copy = push(
                mem.expand_part.at[which, lax.rem(other, 4), lax.div(other, 4)],
                mem.expand_share.at[which, feeds.index],
                mem.share_send.at[which, mask],
                mem.share_recv.at[which, mask],
                feeds.place(mask),
            )
            copy.start()
            column_copies.append(copy)
        mem.expand_share[which, feeds.index] = mem.expand_part[
            which, lax.rem(feeds.index, 4), lax.div(feeds.index, 4)
        ]

    for which in range(2):
        expand_shares(which)
    back_output.land()
    back_output.add(
        lambda: mem.output_grad[group].astype(WIDE),
        lambda slot: mem.output_land[slot].astype(WIDE),
        lambda total: store_whole(total, outs.output_share),
    )
    back_attend.land()

    def attend_shares(block, unused):
        def store(total):
            mem.attend_part[:, block] = total.astype(LOW)
            add_squares(total)

        back_attend.add(
            lambda: mem.attend_grad[:, block, group].astype(WIDE),
            lambda slot: mem.attend_land[slot, :, block].astype(WIDE),
            store,
        )
        return unused

    lax.fori_loop(0, seq, attend_shares, 0)
    for mask in masks:
        copy = push(
            mem.attend_part.at[:, heads.at(mask)],
            outs.attend_share.at[:, :, block_of(me, LANES)],
            mem.share_send.at[2, mask],
            mem.share_recv.at[2, mask],
            heads.place(mask),
        )
        copy.start()
        column_copies.append(copy)
    outs.attend_share[:, :, block_of(me, LANES)] = mem.attend_part[:, me]

    lane = lax.broadcasted_iota(jnp.int32, (1, LANES), 1)
    lines = [
        mem.gains[which : which + 1, start : start + LANES]
        for which in range(2)
        for start in range(0, D, LANES)
    ]
    bias_line = jnp.zeros((1, LANES), WIDE)
    for row in range(2 * HEADS_HERE):
        place = row // HEADS_HERE * HEADS + me * HEADS_HERE + row % HEADS_HERE
        amount = jnp.sum(mem.bias_sums[row : row + 1, :], axis=1, keepdims=True)
        bias_line = bias_line + jnp.where(lane == place, amount, 0.0)
    amounts = jnp.sum(mem.squares[0:2, :], axis=1, keepdims=True)
    amount_line = jnp.where(lane == 0, amounts[0:1], 0.0) + jnp.where(lane == 1, amounts[1:2], 0.0)
    lines += [bias_line, amount_line, jnp.zeros((6, LANES), WIDE)]
    mem.plane_totals[me] = jnp.concatenate(lines, axis=0)
    plane_copies = []
    for mask in masks:
        copy = push(
            mem.plane_totals.at[me],
            mem.plane_totals.at[me],
            mem.total_send.at[0, mask],
            mem.total_recv.at[0, mask],
            (flip(me, mask), group),
        )
        copy.start()
        plane_copies.append(copy)
    for copy in plane_copies:
        copy.wait()
    mem.line_totals[group] = jnp.sum(mem.plane_totals[...], axis=0)
    total_copies = []
    for step in range(1, batch):
        copy = push(
            mem.line_totals.at[group],
            mem.line_totals.at[group],
            mem.total_send.at[1, step],
            mem.total_recv.at[1, step],
            (me, lax.rem(group + step, batch)),
        )
        copy.start()
        total_copies.append(copy)
    for copy in total_copies:
        copy.wait()
    outs.totals[...] = jnp.sum(mem.line_totals[...], axis=0)
    for copy in column_copies:
        copy.wait()
    for which in range(2):
        for block in range(blocks):
            owner, part = feed_block(block)
            outs.expand_share[which, :, block * LANES : (block + 1) * LANES] = mem.expand_share[
                which, owner, :, part * LANES : (part + 1) * LANES
            ]
    for copies in (attend_columns, expand_columns):
        for copy in copies:
            copy.wait_send()
    for line in [line_attend, line_output, line_reduce] + line_expand:
        line.finish()
    for line in [back_attend, back_output, back_reduce] + back_expand:
        line.finish()


def call_layer(seq, batch, inputs, teacher, facts, scored, bias, gains, attend, output, expand, reduce):
    rows, share, hidden = inputs.shape[0], attend.shape[1], expand.shape[2] // seq
    length, pair, chips = rows * seq, 2 * rows, seq // 2
    low = lambda *shape: pltpu.VMEM(shape, LOW)
    wide = lambda *shape: pltpu.VMEM(shape, WIDE)
    sems = lambda *shape: pltpu.SemaphoreType.DMA(shape)
    in_names = ["inputs", "teacher", "facts", "scored", "bias", "gains"]
    in_names += ["attend", "output", "expand", "reduce"]
    outs = dict(
        layer_output=((rows, D), WIDE),
        input_gradient=((rows, D), WIDE),
        totals=((TOTAL_ROWS, LANES), WIDE),
        count=((8, LANES), WIDE),
        attend_share=((3, share, D), LOW),
        output_share=((output.shape[0], D), WIDE),
        expand_share=((2, share, hidden * seq), LOW),
        reduce_share=((reduce.shape[0], D), WIDE),
    )
    scratch = dict(
        gains=wide(2, D),
        squares=wide(8, D),
        plane_totals=wide(seq, TOTAL_ROWS, LANES),
        line_totals=wide(batch, TOTAL_ROWS, LANES),
        attend_low=low(3, share, D),
        expand_low=low(2, seq, share, hidden),
        attend_all=low(3, seq, batch, share, LANES),
        output_all=low(batch, output.shape[0], D),
        expand_all=low(2, seq, batch, share, hidden),
        reduce_all=low(batch, reduce.shape[0], D),
        own_rows=low(4, rows, D),
        act_one=low(length, D),
        act_two=low(length, D),
        branch=low(length, D),
        grad_attn=low(length, D),
        facts_all=wide(seq * facts.shape[0], LANES),
        cosine=wide(HEAD_DIM // 2, length),
        sine=wide(HEAD_DIM // 2, length),
        labels=wide(8, length),
        key_label=wide(length, LANES),
        count=wide(batch, 8, LANES),
        query_turned=low(LANES, length),
        key_turned=low(LANES, length),
        value_turned=low(LANES, length),
        key_heads=low(HEADS_HERE, length, LANES),
        value_heads=low(HEADS_HERE, length, LANES),
        lse=wide(8, length),
        exact=wide(LANES, length),
        mixed_wide=wide(LANES, pair),
        mixed_turned=low(LANES, length),
        whole=wide(pair, D),
        keep=wide(chips, rows, D),
        near_from=low(chips, rows, D),
        near=low(chips, rows, D),
        far_from=low(chips, rows, D),
        far=low(chips, rows, D),
        middle=wide(rows, D),
        grad_own=wide(rows, D),
        by_up=wide(length, hidden),
        by_gate=wide(length, hidden),
        hidden=low(length, hidden),
        grad_gate=low(length, hidden),
        grad_up=low(length, hidden),
        query_total=wide(LANES, length),
        key_total=wide(LANES, length),
        value_total=wide(LANES, length),
        bias_sums=wide(8, pair),
        grad_project=low(3, LANES, length),
        reduce_grad=low(batch, reduce.shape[0], D),
        expand_grad=low(2, seq, batch, share, hidden),
        output_grad=low(batch, output.shape[0], D),
        attend_grad=low(3, seq, batch, share, LANES),
        reduce_land=low(3, reduce.shape[0], D),
        expand_land=low(2, 3, 4, 2, share, hidden),
        output_land=low(batch, output.shape[0], D),
        attend_land=low(batch, 3, seq, share, LANES),
        expand_part=low(2, 4, 2, share, hidden),
        expand_share=low(2, seq, share, hidden),
        attend_part=low(3, seq, share, LANES),
        stage_sem=sems(5 + 2 * (expand.shape[2] // D)),
        total_send=sems(2, seq),
        total_recv=sems(2, seq),
        column_send=sems(2, seq),
        column_recv=sems(2, seq),
        line_send=sems(5, batch),
        line_recv=sems(5, batch),
        facts_send=sems(seq),
        facts_recv=sems(seq),
        gather_send=sems(4, seq),
        gather_recv=sems(4, seq),
        count_send=sems(batch),
        count_recv=sems(batch),
        near_send=sems(4, chips),
        near_recv=sems(4, chips),
        far_send=sems(4, chips),
        far_recv=sems(4, chips),
        back_send=sems(5, batch),
        back_recv=sems(5, batch),
        share_send=sems(3, seq),
        share_recv=sems(3, seq),
    )

    places = dict.fromkeys(("attend", "output", "expand", "reduce"), pl.BlockSpec(memory_space=pl.ANY))
    places["bias"] = IN_SMEM

    def kernel(*refs):
        groups, start = [], 0
        for names in (in_names, outs, scratch):
            names = list(names)
            groups.append(types.SimpleNamespace(**dict(zip(names, refs[start : start + len(names)]))))
            start += len(names)
        layer_kernel(seq, batch, *groups)

    results = pl.pallas_call(
        kernel,
        out_shape=[jax.ShapeDtypeStruct(*out) for out in outs.values()],
        in_specs=[places.get(name, IN_VMEM) for name in in_names],
        out_specs=[IN_VMEM] * len(outs),
        scratch_shapes=list(scratch.values()),
        compiler_params=pltpu.CompilerParams(
            collective_id=0, has_side_effects=True, vmem_limit_bytes=63 * MIB
        ),
        name="layer",
    )(inputs, teacher, facts, scored, bias, gains, attend, output, expand, reduce)
    return types.SimpleNamespace(**dict(zip(outs, results)))


def update_kernel(
    totals,
    count,
    layer_output,
    input_gradient,
    attend_share,
    output_share,
    expand_share,
    reduce_share,
    gains,
    gains_first,
    gains_second,
    bias,
    bias_first,
    bias_second,
    *refs,
):
    olds, news = refs[:12], refs[12:]
    news[0][...] = layer_output[...]
    news[1][...] = input_gradient[...]
    gains_total = jnp.concatenate(
        [
            jnp.concatenate([totals[row + i : row + i + 1, :] for i in range(D // LANES)], axis=1)
            for row in (0, D // LANES)
        ],
        axis=0,
    )
    row = 2 * D // LANES
    bias_total = jnp.concatenate(
        [totals[row : row + 1, :HEADS], totals[row : row + 1, HEADS : 2 * HEADS]], axis=0
    )
    row += 1

    def sum_all(values):
        return jnp.sum(jnp.sum(values, axis=0, keepdims=True), axis=1, keepdims=True)

    squares = (
        totals[row : row + 1, 0:1] + sum_all(gains_total * gains_total) + sum_all(bias_total * bias_total)
    )
    grad_norm = jnp.sqrt(squares)
    clip = jnp.minimum(1.0, CLIP_NORM / grad_norm)
    news[2][...] = totals[row : row + 1, 1:2] / (count[0:1, 0:1] * D)
    news[3][...] = grad_norm
    shares = (attend_share, output_share, expand_share, reduce_share)
    rates = (RATE_ATTEND, RATE_OUTPUT, RATE_EXPAND, RATE_REDUCE)
    for number, (share, rate) in enumerate(zip(shares, rates)):
        weight, first, second = olds[3 * number : 3 * number + 3]
        new, copy, first_new, second_new = news[4 + 4 * number : 8 + 4 * number]
        scale = clip.reshape((1,) * share.ndim)
        new[...], first_new[...], second_new[...] = adam_step(
            weight[...], first[...], second[...], share[...].astype(WIDE) * scale, rate, WEIGHT_DECAY
        )
        copy[...] = new[...].astype(LOW)
    for number, (old, total, rate) in enumerate(
        (
            ((gains, gains_first, gains_second), gains_total, RATE_GAINS),
            ((bias, bias_first, bias_second), bias_total, RATE_BIAS),
        )
    ):
        new, first_new, second_new = news[20 + 3 * number : 23 + 3 * number]
        new[...], first_new[...], second_new[...] = adam_step(
            old[0][...], old[1][...], old[2][...], total * clip, rate, 0.0
        )


UPDATE_STEPS = 2


def cut_spec(shape):
    rows = shape[-2] // UPDATE_STEPS
    if len(shape) == 3:
        return pl.BlockSpec((shape[0], rows, shape[2]), lambda step: (0, step, 0))
    return pl.BlockSpec((rows, shape[1]), lambda step: (step, 0))


def whole_spec(shape):
    return pl.BlockSpec(shape, lambda step: (0,) * len(shape))


def call_update(done, shares, smalls, olds):
    whole = [done.totals, done.count]
    cut = [done.layer_output, done.input_gradient] + shares
    outs = [(done.layer_output, WIDE, cut_spec), (done.input_gradient, WIDE, cut_spec)]
    one = jax.ShapeDtypeStruct((1, 1), WIDE)
    outs += [(one, WIDE, whole_spec)] * 2
    for weight in olds[::3]:
        outs += [(weight, dtype, cut_spec) for dtype in (WIDE, LOW, WIDE, WIDE)]
    outs += [(small, WIDE, whole_spec) for small in smalls]
    return pl.pallas_call(
        update_kernel,
        grid=(UPDATE_STEPS,),
        out_shape=[jax.ShapeDtypeStruct(array.shape, dtype) for array, dtype, spec in outs],
        in_specs=[whole_spec(array.shape) for array in whole]
        + [cut_spec(array.shape) for array in cut]
        + [whole_spec(array.shape) for array in smalls]
        + [cut_spec(array.shape) for array in olds],
        out_specs=[spec(array.shape) for array, dtype, spec in outs],
        compiler_params=pltpu.CompilerParams(vmem_limit_bytes=63 * MIB),
        name="update",
    )(*whole, *cut, *smalls, *olds)


def fast_body(
    seq,
    batch,
    inputs,
    teacher,
    lengths,
    variate_ids,
    time_ids,
    observed,
    attend_weight,
    output_weight,
    expand_weight,
    reduce_weight,
    norm_gains,
    variate_bias,
    attend_first,
    output_first,
    expand_first,
    reduce_first,
    gains_first,
    bias_first,
    attend_second,
    output_second,
    expand_second,
    reduce_second,
    gains_second,
    bias_second,
):
    me = lax.axis_index("seq")
    rows = inputs.shape[1]
    positions = me * rows + jnp.arange(rows, dtype=jnp.int32)
    inside = positions < lengths[0]
    scored = jnp.logical_and(inside, observed[0] == 1)
    half_dim = HEAD_DIM // 2
    frequency = jnp.exp(-math.log(ROPE_BASE) * jnp.arange(half_dim).astype(WIDE) / half_dim)
    angle = frequency[:, None] * time_ids[0].astype(WIDE)[None, :]
    labels = jnp.stack(
        [
            jnp.where(inside, variate_ids[0], -1).astype(WIDE),
            variate_ids[0].astype(WIDE),
            scored.astype(WIDE),
        ]
    )
    facts = jnp.concatenate([jnp.cos(angle), jnp.sin(angle), jnp.pad(labels, ((0, 5), (0, 0)))])
    done = call_layer(
        seq,
        batch,
        inputs[0],
        teacher[0],
        facts,
        scored.astype(WIDE)[:, None],
        variate_bias,
        norm_gains,
        attend_weight,
        output_weight,
        expand_weight,
        reduce_weight,
    )
    results = call_update(
        done,
        [done.attend_share, done.output_share, done.expand_share, done.reduce_share],
        [norm_gains, gains_first, gains_second, variate_bias, bias_first, bias_second],
        [attend_weight, attend_first, attend_second]
        + [output_weight, output_first, output_second]
        + [expand_weight, expand_first, expand_second]
        + [reduce_weight, reduce_first, reduce_second],
    )
    output, input_gradient, loss, grad_norm = results[:4]
    return (
        output[None],
        loss.reshape(()),
        input_gradient[None],
        grad_norm.reshape(()),
    ) + tuple(results[4:])


def solution(mesh):
    seq, batch = mesh.shape["seq"], mesh.shape["batch"]
    body = functools.partial(fast_body, seq, batch) if fast_fits(seq, batch) else general_body
    in_specs = (
        P("batch", "seq", None),
        P("batch", "seq", None),
        P("batch"),
        P("batch", "seq"),
        P("batch", "seq"),
        P("batch", "seq"),
        P(None, ("seq", "batch"), None),
        P(("seq", "batch"), None),
        P(None, ("seq", "batch"), None),
        P(("seq", "batch"), None),
        P(),
        P(),
        P(None, ("seq", "batch"), None),
        P(("seq", "batch"), None),
        P(None, ("seq", "batch"), None),
        P(("seq", "batch"), None),
        P(),
        P(),
        P(None, ("seq", "batch"), None),
        P(("seq", "batch"), None),
        P(None, ("seq", "batch"), None),
        P(("seq", "batch"), None),
        P(),
        P(),
    )
    out_specs = (
        P("batch", "seq", None),
        P(),
        P("batch", "seq", None),
        P(),
        P(None, ("seq", "batch"), None),
        P(None, ("seq", "batch"), None),
        P(None, ("seq", "batch"), None),
        P(None, ("seq", "batch"), None),
        P(("seq", "batch"), None),
        P(("seq", "batch"), None),
        P(("seq", "batch"), None),
        P(("seq", "batch"), None),
        P(None, ("seq", "batch"), None),
        P(None, ("seq", "batch"), None),
        P(None, ("seq", "batch"), None),
        P(None, ("seq", "batch"), None),
        P(("seq", "batch"), None),
        P(("seq", "batch"), None),
        P(("seq", "batch"), None),
        P(("seq", "batch"), None),
        P(),
        P(),
        P(),
        P(),
        P(),
        P(),
    )
    return jax.shard_map(body, mesh=mesh, in_specs=in_specs, out_specs=out_specs, check_vma=False)
```

```python
import functools
import math
import types

import jax
import jax.numpy as jnp
from jax import lax
from jax.experimental import pallas as pl
from jax.experimental.pallas import tpu as pltpu
from jax.sharding import PartitionSpec as P

D = 1024
HEADS = 16
HEAD_DIM = 64
STEP = 10


NORM_EPS = 1e-05
ROPE_BASE = 10000.0
MASKED = -1e30
CLIP_NORM = 1.0
BETA_ONE = 0.9
BETA_TWO = 0.98
ADAM_EPS = 1e-08
WEIGHT_DECAY = 0.1
RATE_ATTEND = 0.03
RATE_OUTPUT = 0.5
RATE_EXPAND = 0.03
RATE_REDUCE = 0.015
RATE_GAINS = 1.0
RATE_BIAS = 0.5


def angles(times):
    half_dim = HEAD_DIM // 2
    frequency = jnp.exp(-math.log(ROPE_BASE) * jnp.arange(half_dim).astype(jnp.float32) / half_dim)
    angle_table = times.astype(jnp.float32)[..., None] * frequency
    return (jnp.cos(angle_table)[..., None, :], jnp.sin(angle_table)[..., None, :])


def rotate(values, cos_table, sin_table):
    half_dim = values.shape[-1] // 2
    first_half = values[..., :half_dim]
    second_half = values[..., half_dim:]
    return jnp.concatenate(
        [
            first_half * cos_table - second_half * sin_table,
            second_half * cos_table + first_half * sin_table,
        ],
        axis=-1,
    )


def unrotate(values, cos_table, sin_table):
    half_dim = values.shape[-1] // 2
    first_half = values[..., :half_dim]
    second_half = values[..., half_dim:]
    return jnp.concatenate(
        [
            first_half * cos_table + second_half * sin_table,
            second_half * cos_table - first_half * sin_table,
        ],
        axis=-1,
    )


def normalize(values):
    inv_scale = lax.rsqrt(jnp.mean(values * values, axis=-1, keepdims=True) + NORM_EPS)
    return (values * inv_scale, inv_scale)


def norm_back(grad_act, unit_rows, inv_scale, gain_row):
    grad_unit = grad_act * gain_row
    return inv_scale * (
        grad_unit - unit_rows * jnp.mean(grad_unit * unit_rows, axis=-1, keepdims=True)
    )


def score_block(query_rows, query_labels, key_rows, key_labels, bias_table):
    scores = jnp.einsum(
        "ihe,jhe->hij", query_rows, key_rows, preferred_element_type=jnp.float32
    ) * HEAD_DIM ** (-0.5)
    same_var = query_labels[:, None] == key_labels[None, :]
    scores = scores + jnp.where(
        same_var[None], bias_table[0][:, None, None], bias_table[1][:, None, None]
    )
    scores = jnp.where(key_labels[None, None, :] >= 0, scores, MASKED)
    return (scores, same_var)


def block_grads(
    query_rows,
    query_labels,
    grad_rows,
    lse_rows,
    delta_rows,
    key_rows,
    value_rows,
    key_labels,
    bias_table,
    need_query,
    need_keys,
):
    scores, same_var = score_block(query_rows, query_labels, key_rows, key_labels, bias_table)
    weights = jnp.exp(scores - lse_rows.T[:, :, None])
    grad_weights = jnp.einsum(
        "ihe,jhe->hij", grad_rows, value_rows, preferred_element_type=jnp.float32
    )
    grad_scores = (weights * (grad_weights - delta_rows.T[:, :, None])).astype(jnp.bfloat16)
    result = ()
    if need_query:
        grad_query = jnp.einsum(
            "hij,jhe->ihe", grad_scores, key_rows, preferred_element_type=jnp.float32
        ) * HEAD_DIM ** (-0.5)
        widened = grad_scores.astype(jnp.float32)
        bias_same = jnp.sum(jnp.where(same_var[None], widened, 0.0), axis=(1, 2))
        bias_other = jnp.sum(jnp.where(same_var[None], 0.0, widened), axis=(1, 2))
        result = result + (grad_query, jnp.stack([bias_same, bias_other]))
    if need_keys:
        grad_key = jnp.einsum(
            "hij,ihe->jhe", grad_scores, query_rows, preferred_element_type=jnp.float32
        ) * HEAD_DIM ** (-0.5)
        grad_value = jnp.einsum(
            "hij,ihe->jhe",
            weights.astype(jnp.bfloat16),
            grad_rows,
            preferred_element_type=jnp.float32,
        )
        result = result + (grad_key, grad_value)
    return result


def adam_step(weight, first_moment, second_moment, gradient, step_rate, decay_rate):
    first_moment = BETA_ONE * first_moment + (1.0 - BETA_ONE) * gradient
    second_moment = BETA_TWO * second_moment + (1.0 - BETA_TWO) * gradient * gradient
    direction = (
        first_moment
        / (1.0 - BETA_ONE**STEP)
        / (jnp.sqrt(second_moment / (1.0 - BETA_TWO**STEP)) + ADAM_EPS)
    )
    return (weight - step_rate * (direction + decay_rate * weight), first_moment, second_moment)


def general_body(
    inputs,
    teacher,
    lengths,
    variate_ids,
    time_ids,
    observed,
    attend_weight,
    output_weight,
    expand_weight,
    reduce_weight,
    norm_gains,
    variate_bias,
    attend_first,
    output_first,
    expand_first,
    reduce_first,
    gains_first,
    bias_first,
    attend_second,
    output_second,
    expand_second,
    reduce_second,
    gains_second,
    bias_second,
):
    row_count = inputs.shape[1]
    length = row_count * lax.axis_size("seq")
    block_rows = math.gcd(length, 1024)
    blocks = length // block_rows
    states = inputs[0].astype(jnp.float32)
    positions = lax.axis_index("seq") * row_count + jnp.arange(row_count, dtype=jnp.int32)
    inside = positions < lengths[0]
    scored = jnp.logical_and(inside, observed[0] == 1)
    local_count = jnp.sum(scored.astype(jnp.int32))
    count_early = lax.psum(local_count, ("seq", "batch"))
    full_attend, full_output, full_expand, full_reduce = (
        lax.all_gather(attend_weight.astype(jnp.bfloat16), ("seq", "batch"), axis=1, tiled=True),
        lax.all_gather(output_weight.astype(jnp.bfloat16), ("seq", "batch"), axis=0, tiled=True),
        lax.all_gather(expand_weight.astype(jnp.bfloat16), ("seq", "batch"), axis=1, tiled=True),
        lax.all_gather(reduce_weight.astype(jnp.bfloat16), ("seq", "batch"), axis=0, tiled=True),
    )
    unit_one, scale_one = normalize(states)
    act_one = (unit_one * norm_gains[0]).astype(jnp.bfloat16)
    project = jnp.einsum("td,cde->cte", act_one, full_attend, preferred_element_type=jnp.float32)
    cos_table, sin_table = angles(time_ids[0])
    query = rotate(project[0].reshape(row_count, HEADS, HEAD_DIM), cos_table, sin_table).astype(
        jnp.bfloat16
    )
    key_rows = (
        rotate(project[1].reshape(row_count, HEADS, HEAD_DIM), cos_table, sin_table)
        .astype(jnp.bfloat16)
        .reshape(row_count, D)
    )
    value_rows = project[2].astype(jnp.bfloat16)
    own_labels = jnp.where(inside, variate_ids[0], -1).astype(jnp.bfloat16)
    all_keys, all_values, all_labels = (
        lax.all_gather(key_rows, "seq", axis=0, tiled=True),
        lax.all_gather(value_rows, "seq", axis=0, tiled=True),
        lax.all_gather(own_labels, "seq", axis=0, tiled=True),
    )
    key_blocks = all_keys.reshape(blocks, block_rows, HEADS, HEAD_DIM)
    value_blocks = all_values.reshape(blocks, block_rows, HEADS, HEAD_DIM)
    label_blocks = all_labels.astype(jnp.float32).reshape(blocks, block_rows)
    query_labels = variate_ids[0].astype(jnp.float32)

    def sweep_top(carry, pieces):
        running, sum_exp = carry
        scores, same_var = score_block(query, query_labels, pieces[0], pieces[1], variate_bias)
        raised = jnp.maximum(running, jnp.floor(jnp.max(scores, axis=-1)))
        sum_exp = sum_exp * jnp.exp(running - raised) + jnp.sum(
            jnp.exp(scores - raised[..., None]), axis=-1
        )
        return ((raised, sum_exp), None)

    start_top = jnp.full((HEADS, row_count), MASKED, jnp.float32)
    (row_top, sum_exp), unused = lax.scan(
        sweep_top,
        (start_top, jnp.zeros((HEADS, row_count), jnp.float32)),
        (key_blocks, label_blocks),
    )
    log_total = row_top + jnp.log(sum_exp)

    def sweep_out(carry, pieces):
        coarse, finest = carry
        scores, same_var = score_block(query, query_labels, pieces[0], pieces[2], variate_bias)
        weights = jnp.exp(scores - log_total[..., None])
        rounded = weights.astype(jnp.bfloat16)
        residue = (weights - rounded.astype(jnp.float32)).astype(jnp.bfloat16)
        coarse = coarse + jnp.einsum(
            "hij,jhe->ihe", rounded, pieces[1], preferred_element_type=jnp.float32
        )
        finest = finest + jnp.einsum(
            "hij,jhe->ihe", residue, pieces[1], preferred_element_type=jnp.float32
        )
        return ((coarse, finest), None)

    zero_heads = jnp.zeros((row_count, HEADS, HEAD_DIM), jnp.float32)
    (coarse, finest), unused = lax.scan(
        sweep_out, (zero_heads, zero_heads), (key_blocks, value_blocks, label_blocks)
    )
    exact_heads = coarse + finest
    mixed = coarse.reshape(row_count, D).astype(jnp.bfloat16)
    middle = states + jnp.dot(mixed, full_output, preferred_element_type=jnp.float32)
    unit_two, scale_two = normalize(middle)
    act_two = (unit_two * norm_gains[1]).astype(jnp.bfloat16)
    gate_up = jnp.einsum("td,cdf->ctf", act_two, full_expand, preferred_element_type=jnp.float32)
    sigmoid = jax.nn.sigmoid(gate_up[0])
    hidden = (gate_up[0] * sigmoid * gate_up[1]).astype(jnp.bfloat16)
    output = middle + jnp.dot(hidden, full_reduce, preferred_element_type=jnp.float32)
    error = output - teacher[0].astype(jnp.float32)
    local_square = jnp.sum(jnp.where(scored[:, None], error * error, 0.0))
    square_total = lax.psum(local_square, ("seq", "batch"))
    count_all = count_early.astype(jnp.float32)
    loss = square_total / (count_all * D)
    grad_out = jnp.where(scored[:, None], error * (2.0 / (count_all * D)), 0.0)
    back_attend, back_output, back_expand, back_reduce = (
        lax.all_gather(attend_weight.astype(jnp.bfloat16), ("seq", "batch"), axis=1, tiled=True),
        lax.all_gather(output_weight.astype(jnp.bfloat16), ("seq", "batch"), axis=0, tiled=True),
        lax.all_gather(expand_weight.astype(jnp.bfloat16), ("seq", "batch"), axis=1, tiled=True),
        lax.all_gather(reduce_weight.astype(jnp.bfloat16), ("seq", "batch"), axis=0, tiled=True),
    )
    grad_branch = grad_out.astype(jnp.bfloat16)
    reduce_grad = jnp.einsum("tf,td->fd", hidden, grad_branch, preferred_element_type=jnp.float32)
    grad_hidden = jnp.einsum(
        "td,fd->tf", grad_branch, back_reduce, preferred_element_type=jnp.float32
    )
    grad_gate = grad_hidden * gate_up[1] * sigmoid * (1.0 + gate_up[0] * (1.0 - sigmoid))
    grad_up = grad_hidden * gate_up[0] * sigmoid
    grad_expand = jnp.stack([grad_gate, grad_up]).astype(jnp.bfloat16)
    expand_grad = jnp.einsum(
        "td,ctf->cdf", act_two, grad_expand, preferred_element_type=jnp.float32
    )
    grad_act_two = jnp.einsum(
        "ctf,cdf->td", grad_expand, back_expand, preferred_element_type=jnp.float32
    )
    expand_share, reduce_share = (
        lax.psum_scatter(expand_grad, ("seq", "batch"), scatter_dimension=1, tiled=True),
        lax.psum_scatter(reduce_grad, ("seq", "batch"), scatter_dimension=0, tiled=True),
    )
    grad_middle = grad_out + norm_back(grad_act_two, unit_two, scale_two, norm_gains[1])
    grad_attn = grad_middle.astype(jnp.bfloat16)
    output_grad = jnp.einsum("td,te->de", mixed, grad_attn, preferred_element_type=jnp.float32)
    grad_mixed = jnp.einsum(
        "te,de->td", grad_attn, back_output, preferred_element_type=jnp.float32
    ).astype(jnp.bfloat16)
    grad_heads = grad_mixed.reshape(row_count, HEADS, HEAD_DIM)
    row_delta = jnp.sum(grad_heads.astype(jnp.float32) * exact_heads, axis=-1)
    lse_rows = log_total.T
    zero_bias = jnp.zeros((2, HEADS), jnp.float32)

    def sweep_query(carry, pieces):
        part_query, part_bias = block_grads(
            query,
            query_labels,
            grad_heads,
            lse_rows,
            row_delta,
            pieces[0],
            pieces[1],
            pieces[2],
            variate_bias,
            True,
            False,
        )
        return ((carry[0] + part_query, carry[1] + part_bias), None)

    (query_total, bias_grad), unused = lax.scan(
        sweep_query, (zero_heads, zero_bias), (key_blocks, value_blocks, label_blocks)
    )
    all_query, all_grad = (
        lax.all_gather(query.reshape(row_count, D), "seq", axis=0, tiled=True),
        lax.all_gather(grad_mixed, "seq", axis=0, tiled=True),
    )
    all_lse, all_delta = (
        lax.all_gather(lse_rows, "seq", axis=0, tiled=True),
        lax.all_gather(row_delta, "seq", axis=0, tiled=True),
    )
    key_heads = key_rows.reshape(row_count, HEADS, HEAD_DIM)
    value_heads = value_rows.reshape(row_count, HEADS, HEAD_DIM)
    own_float = own_labels.astype(jnp.float32)

    def sweep_keys(carry, pieces):
        part_key, part_value = block_grads(
            pieces[0],
            pieces[1],
            pieces[2],
            pieces[3],
            pieces[4],
            key_heads,
            value_heads,
            own_float,
            variate_bias,
            False,
            True,
        )
        return ((carry[0] + part_key, carry[1] + part_value), None)

    (key_total, value_heads_total), unused = lax.scan(
        sweep_keys,
        (zero_heads, zero_heads),
        (
            all_query.reshape(blocks, block_rows, HEADS, HEAD_DIM),
            label_blocks,
            all_grad.reshape(blocks, block_rows, HEADS, HEAD_DIM),
            all_lse.reshape(blocks, block_rows, HEADS),
            all_delta.reshape(blocks, block_rows, HEADS),
        ),
    )
    value_total = value_heads_total.reshape(row_count, D)
    grad_query = unrotate(query_total, cos_table, sin_table).reshape(row_count, D)
    grad_key = unrotate(key_total, cos_table, sin_table).reshape(row_count, D)
    grad_project = jnp.stack([grad_query, grad_key, value_total]).astype(jnp.bfloat16)
    attend_grad = jnp.einsum(
        "td,cte->cde", act_one, grad_project, preferred_element_type=jnp.float32
    )
    grad_act_one = jnp.einsum(
        "cte,cde->td", grad_project, back_attend, preferred_element_type=jnp.float32
    )
    attend_share, output_share = (
        lax.psum_scatter(attend_grad, ("seq", "batch"), scatter_dimension=1, tiled=True),
        lax.psum_scatter(output_grad, ("seq", "batch"), scatter_dimension=0, tiled=True),
    )
    grad_input = grad_middle + norm_back(grad_act_one, unit_one, scale_one, norm_gains[0])
    gains_grad = jnp.stack(
        [jnp.sum(grad_act_one * unit_one, axis=0), jnp.sum(grad_act_two * unit_two, axis=0)]
    )
    local_squares = (
        jnp.sum(attend_share * attend_share)
        + jnp.sum(output_share * output_share)
        + jnp.sum(expand_share * expand_share)
        + jnp.sum(reduce_share * reduce_share)
    )
    gains_total, bias_total, square_sum = lax.psum(
        (gains_grad, bias_grad, local_squares), ("seq", "batch")
    )
    grad_norm = jnp.sqrt(
        square_sum + jnp.sum(gains_total * gains_total) + jnp.sum(bias_total * bias_total)
    )
    clip_scale = jnp.minimum(1.0, CLIP_NORM / grad_norm)
    attend_new, attend_first_new, attend_second_new = adam_step(
        attend_weight,
        attend_first,
        attend_second,
        attend_share * clip_scale,
        RATE_ATTEND,
        WEIGHT_DECAY,
    )
    output_new, output_first_new, output_second_new = adam_step(
        output_weight,
        output_first,
        output_second,
        output_share * clip_scale,
        RATE_OUTPUT,
        WEIGHT_DECAY,
    )
    expand_new, expand_first_new, expand_second_new = adam_step(
        expand_weight,
        expand_first,
        expand_second,
        expand_share * clip_scale,
        RATE_EXPAND,
        WEIGHT_DECAY,
    )
    reduce_new, reduce_first_new, reduce_second_new = adam_step(
        reduce_weight,
        reduce_first,
        reduce_second,
        reduce_share * clip_scale,
        RATE_REDUCE,
        WEIGHT_DECAY,
    )
    gains_new, gains_first_new, gains_second_new = adam_step(
        norm_gains, gains_first, gains_second, gains_total * clip_scale, RATE_GAINS, 0.0
    )
    bias_new, bias_first_new, bias_second_new = adam_step(
        variate_bias, bias_first, bias_second, bias_total * clip_scale, RATE_BIAS, 0.0
    )
    input_gradient = (grad_input * count_all * D)[None]
    return (
        output[None],
        loss,
        input_gradient,
        grad_norm,
        attend_new,
        attend_new.astype(jnp.bfloat16),
        attend_first_new,
        attend_second_new,
        output_new,
        output_new.astype(jnp.bfloat16),
        output_first_new,
        output_second_new,
        expand_new,
        expand_new.astype(jnp.bfloat16),
        expand_first_new,
        expand_second_new,
        reduce_new,
        reduce_new.astype(jnp.bfloat16),
        reduce_first_new,
        reduce_second_new,
        gains_new,
        gains_first_new,
        gains_second_new,
        bias_new,
        bias_first_new,
        bias_second_new,
    )


MESH = pl.DeviceIdType.MESH
IN_VMEM = pl.BlockSpec(memory_space=pltpu.VMEM)
IN_SMEM = pl.BlockSpec(memory_space=pltpu.SMEM)
LANES = 128
HEADS_HERE = LANES // HEAD_DIM
VARIATES = 16
MIB = 1 << 20
LOW = jnp.bfloat16
WIDE = jnp.float32
TOTAL_ROWS = 24


def fast_fits(seq, batch):
    return seq == 8 and batch == 4 and seq * LANES == D


def flip(index, mask):
    result, bit = index, 1
    while bit <= mask:
        if mask & bit:
            result = result + bit - 2 * bit * lax.rem(lax.div(index, bit), 2)
        bit *= 2
    return result


def push(source, target, send_sem, recv_sem, device):
    return pltpu.make_async_remote_copy(
        src_ref=source,
        dst_ref=target,
        send_sem=send_sem,
        recv_sem=recv_sem,
        device_id=device,
        device_id_type=MESH,
    )


def block_of(index, size):
    return pl.ds(pl.multiple_of(index * size, size), size)


def dot(left, right):
    return jnp.dot(left, right, preferred_element_type=WIDE)


def dot_turned(left, right):
    return lax.dot_general(left, right, (((1,), (1,)), ((), ())), preferred_element_type=WIDE)


def turned_dot(left, right):
    return lax.dot_general(left, right, (((0,), (0,)), ((), ())), preferred_element_type=WIDE)


class Team:
    def __init__(self, index, place):
        self.index, self.place = index, place

    def at(self, mask):
        return flip(self.index, mask)


def head_team(me, group):
    return Team(me, lambda mask: (flip(me, mask), group))


def feed_team(me, group):
    return Team(
        4 * lax.rem(group, 2) + lax.rem(me, 4),
        lambda mask: (flip(me, mask % 4), flip(group, mask // 4)),
    )


class Gather:
    def __init__(self, team, rows, all_rows, sends, recvs):
        self.team, self.all_rows, self.sends, self.recvs = team, all_rows, sends, recvs
        self.size = all_rows.shape[0] // 8
        self.given = rows
        self.rows = all_rows.at[block_of(team.index, self.size)] if rows is None else rows

    def copy(self, mask, passing):
        source = self.all_rows.at[block_of(self.team.at(mask - 1 if passing else 0), self.size)]
        return push(
            source if passing else self.rows,
            source,
            self.sends.at[mask],
            self.recvs.at[mask],
            self.team.place(1 if passing else mask),
        )

    def start(self):
        for mask in (6, 2, 4, 1):
            self.copy(mask, False).start()
        if self.given is not None:
            self.all_rows[block_of(self.team.index, self.size)] = self.given[...]

    def pass_on(self, chip):
        self.copy(2 * chip, False).wait_recv()
        self.copy(2 * chip + 1, True).start()

    def complete(self, chip):
        self.copy(2 * chip + 1, chip > 0).wait_recv()

    def finish(self):
        for mask in (6, 2, 4, 1):
            self.copy(mask, False).wait_send()
        for mask in (3, 5, 7):
            self.copy(mask, True).wait_send()


def at_step(step, number, *works):
    @pl.when(step == number)
    def _():
        for work in works:
            work()


def each_chip(gather, work, after):
    def one_chip(chip, unused):
        @pl.when(chip == 0)
        def _():
            gather.complete(0)

        @pl.when(chip == 1)
        def _():
            gather.pass_on(1)
            gather.pass_on(2)
            gather.complete(1)

        @pl.when(chip == 2)
        def _():
            gather.pass_on(3)
            gather.complete(2)

        @pl.when(chip == 3)
        def _():
            gather.complete(3)

        work(chip)
        for number, works in after.items():
            at_step(chip, number, *works)
        return unused

    lax.fori_loop(0, 4, one_chip, 0)
    gather.finish()


class Scatter:
    def __init__(self, team, buffers, near_sends, near_recvs, far_sends, far_recvs):
        self.whole, self.keep, self.near_from, self.near, self.far_from, self.far = buffers
        self.sems = near_sends, near_recvs, far_sends, far_recvs
        self.team = team
        self.size = self.keep.shape[1]

    def near_copy(self, chip):
        return push(
            self.near_from.at[chip],
            self.near.at[chip],
            self.sems[0].at[chip],
            self.sems[1].at[chip],
            self.team.place(1),
        )

    def far_copy(self, chip):
        return push(
            self.far_from.at[chip],
            self.far.at[chip],
            self.sems[2].at[chip],
            self.sems[3].at[chip],
            self.team.place(2 * chip),
        )

    def put(self, chip, rows):
        core = lax.rem(self.team.index, 2)
        self.whole[...] = rows
        self.near_from[chip] = self.whole[block_of(1 - core, self.size)].astype(LOW)
        self.near_copy(chip).start()
        self.keep[chip] = self.whole[block_of(core, self.size)]

    def combine(self, chip):
        self.near_copy(chip).wait_recv()
        self.far_from[chip] = (self.keep[chip] + self.near[chip].astype(WIDE)).astype(LOW)
        self.far_copy(chip).start()

    def total(self):
        self.near_copy(0).wait_recv()
        total = self.keep[0] + self.near[0].astype(WIDE)
        for chip in (1, 2, 3):
            self.far_copy(chip).wait_recv()
            total = total + self.far[chip].astype(WIDE)
        for chip in (0, 1, 2, 3):
            self.near_copy(chip).wait_send()
            if chip:
                self.far_copy(chip).wait_send()
        return total


class LineGather:
    def __init__(self, part_of, sends, recvs, me, group):
        self.part_of, self.sends, self.recvs, self.me, self.group = part_of, sends, recvs, me, group
        self.middle = jnp.logical_and(group >= 1, group <= 2)

    def copy(self, part, target, slot):
        return push(
            self.part_of(part),
            self.part_of(part),
            self.sends.at[slot],
            self.recvs.at[part],
            (self.me, target),
        )

    def start(self):
        group = self.group

        @pl.when(self.middle)
        def _():
            self.copy(group, 3 - group, 3 - group).start()
            self.copy(group, 3 * (group - 1), 3 * (group - 1)).start()

        @pl.when(jnp.logical_not(self.middle))
        def _():
            for step in (2, 1, 3):
                other = lax.rem(group + step, 4)
                self.copy(group, other, other).start()

    def pass_on(self):
        group = self.group

        @pl.when(self.middle)
        def _():
            self.copy(3 - group, 3 * (group - 1), group).wait_recv()
            self.copy(3 - group, 3 * (group - 1), group).start()

    def land(self):
        group = self.group

        @pl.when(self.middle)
        def _():
            for part in (0, 3):
                self.copy(part, 3 - group, group).wait_recv()

        @pl.when(jnp.logical_not(self.middle))
        def _():
            for step in (1, 2, 3):
                other = lax.rem(group + step, 4)
                self.copy(other, other, other).wait_recv()

    def finish(self):
        group = self.group

        @pl.when(self.middle)
        def _():
            for other in (3 - group, 3 * (group - 1), group):
                self.copy(group, 3 - group, other).wait_send()

        @pl.when(jnp.logical_not(self.middle))
        def _():
            for step in (1, 2, 3):
                other = lax.rem(group + step, 4)
                self.copy(group, other, other).wait_send()


class LineScatter:
    def __init__(self, part_of, landing, sends, recvs, me, group):
        self.part_of, self.landing, self.sends, self.recvs = part_of, landing, sends, recvs
        self.me, self.group = me, group
        self.middle = jnp.logical_and(group >= 1, group <= 2)
        self.opposite = 3 - 3 * lax.div(group, 2)

    def copy(self, part, slot, target, sem):
        return push(
            self.part_of(part),
            self.landing.at[slot],
            self.sends.at[sem],
            self.recvs.at[slot],
            (self.me, target),
        )

    def start(self):
        group = self.group

        @pl.when(self.middle)
        def _():
            for other in (3 - group, 3 * (group - 1)):
                self.copy(other, group, other, other).start()

        @pl.when(jnp.logical_not(self.middle))
        def _():
            beside = 1 + lax.div(group, 3)
            self.copy(3 - group, beside, beside, 3 - group).start()
            for other in (3 - beside, beside):
                self.copy(other, group, other, other).start()

    def pass_on(self):
        group, opposite = self.group, self.opposite

        @pl.when(self.middle)
        def _():
            self.copy(opposite, group, opposite, group).wait_recv()
            part = self.part_of(opposite)
            part[...] = (part[...].astype(WIDE) + self.landing[group].astype(WIDE)).astype(LOW)
            self.copy(opposite, group, opposite, group).start()

    def land(self):
        group = self.group

        @pl.when(self.middle)
        def _():
            for slot in (0, 3 - group, 3):
                self.copy(group, slot, 3 - group, group).wait_recv()

        @pl.when(jnp.logical_not(self.middle))
        def _():
            for slot in (1, 2):
                self.copy(group, slot, slot, group).wait_recv()

    def add(self, own, landed, store):
        group = self.group

        @pl.when(self.middle)
        def _():
            store(own() + landed(0) + landed(3 - group) + landed(3))

        @pl.when(jnp.logical_not(self.middle))
        def _():
            store(own() + landed(1) + landed(2))

    def finish(self):
        group = self.group

        @pl.when(self.middle)
        def _():
            for sem in (3 - group, 3 * (group - 1), group):
                self.copy(group, group, 3 - group, sem).wait_send()

        @pl.when(jnp.logical_not(self.middle))
        def _():
            for sem in (3 - group, 1, 2):
                self.copy(group, group, 1, sem).wait_send()


class QuadGather:
    def __init__(self, part_of, sends, recvs, me, group):
        self.part_of, self.sends, self.recvs = part_of, sends, recvs
        self.part = 2 * lax.div(me, 4) + lax.div(group, 2)
        self.along_y, self.along_z = (flip(me, 4), group), (me, flip(group, 2))

    def copy(self, way):
        part = self.part_of(flip(self.part, 1) if way == 3 else self.part)
        device = self.along_z if way == 1 else self.along_y
        return push(part, part, self.sends.at[way], self.recvs.at[way], device)

    def start_y(self):
        self.copy(2).start()

    def start_z(self):
        self.copy(1).start()

    def pass_on(self):
        self.copy(1).wait_recv()
        self.copy(3).start()

    def land(self):
        self.copy(2).wait_recv()
        self.copy(3).wait_recv()

    def finish(self):
        for way in (1, 2, 3):
            self.copy(way).wait_send()


class QuadScatter:
    def __init__(self, part_of, landing, sends, recvs, me, group):
        self.part_of, self.landing, self.sends, self.recvs = part_of, landing, sends, recvs
        self.part = 2 * lax.div(me, 4) + lax.div(group, 2)
        self.along_y, self.along_z = (flip(me, 4), group), (me, flip(group, 2))

    def copy(self, slot):
        return push(
            self.part_of(flip(self.part, (2, 3, 1)[slot])),
            self.landing.at[slot],
            self.sends.at[slot],
            self.recvs.at[slot],
            self.along_z if slot == 2 else self.along_y,
        )

    def start_far(self):
        self.copy(1).start()

    def start_near(self):
        self.copy(0).start()

    def pass_on(self):
        self.copy(1).wait_recv()
        part = self.part_of(flip(self.part, 1))
        part[...] = (part[...].astype(WIDE) + self.landing[1].astype(WIDE)).astype(LOW)
        self.copy(2).start()

    def land(self):
        self.copy(0).wait_recv()
        self.copy(2).wait_recv()

    def finish(self):
        for slot in (0, 1, 2):
            self.copy(slot).wait_send()


def chip_of(team, chip):
    here = lax.div(team.index, 2)
    if isinstance(chip, int):
        return flip(here, chip)
    column = lax.rem(lax.rem(here, 2) + lax.rem(chip, 2), 2)
    row = lax.rem(lax.div(here, 2) + lax.div(chip, 2), 2)
    return 2 * row + column


def turn_rows(values, cosine, sine):
    half = HEAD_DIM // 2
    pieces = []
    for start in range(0, values.shape[0], HEAD_DIM):
        first, second = values[start : start + half], values[start + half : start + HEAD_DIM]
        pieces += [first * cosine - second * sine, second * cosine + first * sine]
    return jnp.concatenate(pieces, axis=0)


def thirds(values):
    first = values.astype(LOW).astype(WIDE)
    second = (values - first).astype(LOW).astype(WIDE)
    return first, second, values - first - second


def pick(row, choices):
    result = jnp.zeros(row.shape, WIDE)
    for number, choice in choices.items():
        result = jnp.where(row == number, choice, result)
    return result


def norm_rows(values):
    scale = lax.rsqrt(jnp.mean(values * values, axis=-1, keepdims=True) + NORM_EPS)
    return values * scale, scale


def feed_block(block):
    y, x, core, far_z, near_z = (block // 16, block // 8 % 2, block // 4 % 2, block // 2 % 2, block % 2)
    return 4 * near_z + 2 * x + core, 2 * y + far_z


def layer_kernel(seq, batch, ins, outs, mem):
    me, group = lax.axis_index("seq"), lax.axis_index("batch")
    rows = ins.inputs.shape[0]
    length = rows * seq
    pair = 2 * rows
    share = ins.attend.shape[1]
    wide_columns = ins.expand.shape[2] // D
    hidden_width = mem.reduce_all.shape[0] * mem.reduce_all.shape[1]
    blocks = ins.expand.shape[2] // LANES
    heads, feeds = head_team(me, group), feed_team(me, group)
    quad = 2 * lax.div(me, 4) + lax.div(group, 2)

    staged = [(ins.attend.at[which], mem.keep.at[0, block_of(which, share)]) for which in range(3)]
    staged.append((ins.output, mem.keep.at[0, block_of(3, share)]))
    staged.append((ins.reduce, mem.keep.at[1]))
    for which in range(2):
        for block in range(wide_columns):
            columns = slice(block * D, (block + 1) * D)
            staged.append(
                (ins.expand.at[which, :, columns], mem.keep.at[2 + which, block_of(block, share)])
            )
    staged = [
        pltpu.make_async_copy(source, target, mem.stage_sem.at[number])
        for number, (source, target) in enumerate(staged)
    ]
    for copy in staged:
        copy.start()
    barrier = pltpu.get_barrier_semaphore()
    for mask in range(1, seq):
        pl.semaphore_signal(barrier, inc=1, device_id=(flip(me, mask), group), device_id_type=MESH)
    for step in range(1, batch):
        pl.semaphore_signal(
            barrier, inc=1, device_id=(me, lax.rem(group + step, batch)), device_id_type=MESH
        )
    for mask in (5, 6, 7):
        pl.semaphore_signal(barrier, inc=1, device_id=feeds.place(mask), device_id_type=MESH)

    unit_one, scale_one = norm_rows(ins.inputs[...].astype(WIDE))
    mem.own_rows[0] = (unit_one * ins.gains[0:1, :]).astype(LOW)
    for copy in staged:
        copy.wait()
    for which in range(3):
        mem.attend_low[which] = mem.keep[0, block_of(which, share)].astype(LOW)
    mem.output_full[block_of(batch * me + group, share)] = mem.keep[0, block_of(3, share)].astype(LOW)
    mem.reduce_all[quad] = mem.keep[1].astype(LOW)
    for which in range(2):
        for block in range(blocks):
            owner, part = feed_block(block)
            row, lane = divmod(block * LANES, D)
            mem.expand_low[which, owner, :, part * LANES : (part + 1) * LANES] = mem.keep[
                2 + which, block_of(row, share), lane : lane + LANES
            ].astype(LOW)
    pl.semaphore_wait(barrier, seq + batch + 1)

    masks = (6, 7, 4, 5, 2, 3, 1)

    def start_attend_columns():
        copies = []
        for mask in masks:
            copy = push(
                mem.attend_low.at[:, :, block_of(heads.at(mask), LANES)],
                mem.attend_all.at[:, me, group],
                mem.column_send.at[0, mask],
                mem.column_recv.at[0, mask],
                heads.place(mask),
            )
            copy.start()
            copies.append(copy)
        mem.attend_all[:, me, group] = mem.attend_low[:, :, block_of(me, LANES)]
        return copies

    def start_expand_columns():
        copies = []
        for mask in masks:
            copy = push(
                mem.expand_low.at[:, feeds.at(mask)],
                mem.expand_all.at[:, me, group],
                mem.column_send.at[1, mask],
                mem.column_recv.at[1, mask],
                feeds.place(mask),
            )
            copy.start()
            copies.append(copy)
        mem.expand_all[:, me, group] = mem.expand_low[:, feeds.index]
        return copies

    def expand_part_of(array, which):
        def part_of(part):
            return array.at[which, pl.ds(4 * lax.div(part, 2), 4), pl.ds(2 * lax.rem(part, 2), 2)]

        return part_of

    def line_gather(row, part_of):
        return LineGather(part_of, mem.line_send.at[row], mem.line_recv.at[row], me, group)

    def quad_gather(row, part_of):
        return QuadGather(part_of, mem.line_send.at[row], mem.line_recv.at[row], me, group)

    def gather(team, phase, all_rows):
        return Gather(
            team,
            mem.own_rows.at[phase],
            all_rows,
            mem.gather_send.at[phase],
            mem.gather_recv.at[phase],
        )

    def scatter(team, phase):
        return Scatter(
            team,
            (mem.whole, mem.keep, mem.near_from, mem.near, mem.far_from, mem.far),
            mem.near_send.at[phase],
            mem.near_recv.at[phase],
            mem.far_send.at[phase],
            mem.far_recv.at[phase],
        )

    attend_columns = start_attend_columns()
    line_output = line_gather(1, lambda part: mem.output_full.at[block_of(batch * me + part, share)])
    line_output.start()
    facts = Gather(heads, ins.facts, mem.facts_all, mem.facts_send, mem.facts_recv)
    facts.start()
    for copy in attend_columns:
        copy.wait_recv()
    line_attend = line_gather(0, lambda part: mem.attend_all.at[:, :, part])
    line_attend.start()
    acts = gather(heads, 0, mem.act_one)
    acts.start()
    for chip in (1, 2, 3):
        facts.pass_on(chip)
    for chip in (0, 1, 2, 3):
        facts.complete(chip)
    facts.finish()
    step_rows = ins.facts.shape[0]
    half = HEAD_DIM // 2
    count = jnp.zeros((8, LANES), WIDE)
    for slot in range(seq):
        columns = slice(slot * rows, (slot + 1) * rows)
        start = slot * step_rows
        mem.cosine[:, columns] = mem.facts_all[start : start + half]
        mem.sine[:, columns] = mem.facts_all[start + half : start + 2 * half]
        labels = mem.facts_all[start + 2 * half : start + 2 * half + 8]
        mem.labels[:, columns] = labels
        count = count + labels
    mem.count[group] = count
    count_copies = []
    for step in range(1, batch):
        copy = push(
            mem.count.at[group],
            mem.count.at[group],
            mem.count_send.at[step],
            mem.count_recv.at[step],
            (me, lax.rem(group + step, batch)),
        )
        copy.start()
        count_copies.append(copy)
    acts.pass_on(1)
    acts.pass_on(2)
    line_output.pass_on()
    line_attend.pass_on()
    acts.pass_on(3)
    for chip in range(4):
        acts.complete(chip)
    acts.finish()
    line_output.land()
    line_attend.land()

    outputs = Gather(heads, None, mem.output_full, mem.output_send, mem.output_recv)
    outputs.start()
    expand_columns = start_expand_columns()
    line_reduce = quad_gather(4, lambda part: mem.reduce_all.at[part])
    line_reduce.start_z()
    line_reduce.start_y()
    line_expand = [
        quad_gather(2 + which, expand_part_of(mem.expand_all, which)) for which in range(2)
    ]

    def attend_matrix(which):
        return mem.attend_all[which].reshape(D, LANES)

    def project(block, unused):
        span = block_of(block, pair)
        act = mem.act_one[span, :]
        cosine, sine = mem.cosine[:, span], mem.sine[:, span]
        query = turn_rows(dot(act, attend_matrix(0)).T, cosine, sine).astype(LOW)
        query = (query.astype(WIDE) * HEAD_DIM ** (-0.5)).astype(LOW)
        key = turn_rows(dot(act, attend_matrix(1)).T, cosine, sine).astype(LOW)
        value = dot(act, attend_matrix(2)).T.astype(LOW)
        mem.key_turned[:, span] = key
        mem.value_turned[:, span] = value

        row = lax.broadcasted_iota(jnp.int32, (HEAD_DIM, pair), 0)
        third = lax.div(row, VARIATES)
        variate = lax.rem(row, VARIATES).astype(WIDE)
        key_label, query_label = mem.labels[0:1, span], mem.labels[1:2, span]
        ones = jnp.ones((1, pair), WIDE)
        last = 3 * VARIATES
        key_marks = jnp.where(
            third < 3,
            (key_label == variate).astype(WIDE),
            pick(row, {last: ones, last + 1: ones, last + 2: ones, last + 3: (key_label < 0.0).astype(WIDE)}),
        ).astype(LOW)
        mem.key_marks[:, span] = key_marks
        query_marks = (query_label == variate).astype(WIDE)
        sum_marks = jnp.where(row < VARIATES, query_marks, pick(row, {VARIATES: ones})).astype(LOW)
        value_marks = pick(row, {0: ones, 1: ones, 2: ones}).astype(LOW)
        for head in range(HEADS_HERE):
            features = slice(head * HEAD_DIM, (head + 1) * HEAD_DIM)
            number = me * HEADS_HERE + head
            other = jnp.full((HEAD_DIM, pair), ins.bias[1, number], WIDE)
            more = thirds(jnp.full((HEAD_DIM, pair), ins.bias[0, number], WIDE) - other)
            other = thirds(other)
            bias_marks = jnp.where(
                third < 3,
                query_marks * jnp.where(third == 0, more[0], jnp.where(third == 1, more[1], more[2])),
                pick(row, {last: other[0], last + 1: other[1], last + 2: other[2], last + 3: MASKED}),
            ).astype(LOW)
            mem.query_turned[head, :, span] = jnp.concatenate([query[features], bias_marks], axis=0)
            mem.key_heads[head, span, :] = jnp.concatenate([key[features], key_marks], axis=0).T
            mem.value_heads[head, span, :] = jnp.concatenate([value[features], value_marks], axis=0).T
            mem.query_heads[head, span, :] = jnp.concatenate([query[features], sum_marks], axis=0).T
        return unused

    lax.fori_loop(0, length // pair, project, 0)
    for copy in expand_columns:
        copy.wait_recv()
    line_expand[0].start_y()

    core = lax.rem(me, 2)

    def mixed_copy(chip, which):
        other = 2 * chip_of(heads, chip) + which
        slot = 2 * chip + lax.rem(which + core, 2)
        return push(
            mem.mixed_out.at[block_of(other, rows)],
            mem.mixed_rows.at[:, block_of(me, LANES)],
            mem.mixed_send.at[slot],
            mem.mixed_recv.at[slot],
            (other, group),
        )

    def attend_block(chip):
        columns = block_of(chip_of(heads, chip), pair)
        for head in range(HEADS_HERE):
            span = slice(head * HEAD_DIM, (head + 1) * HEAD_DIM)
            scores = dot(mem.key_heads[head], mem.query_turned[head, :, columns])
            top = jnp.floor(jnp.max(scores, axis=0, keepdims=True))
            powers = jnp.exp(scores - top)
            probs = powers * (1.0 / jnp.sum(powers, axis=0, keepdims=True))
            rounded = probs.astype(LOW)
            mem.probs[head, :, columns] = rounded
            residue = (probs - rounded.astype(WIDE)).astype(LOW)
            coarse = dot(mem.value_turned[span, :], rounded)
            mem.exact[span, columns] = coarse + dot(mem.value_turned[span, :], residue)
            mem.mixed_wide[span, :] = coarse
        mixed = mem.mixed_wide[...].astype(LOW)
        mem.mixed_turned[:, columns] = mixed
        mem.mixed_out[columns, :] = mixed.T

    def attend_step(step, unused):
        chip = lax.rem(step + 1, 4)
        attend_block(chip)
        for which in range(2):

            @pl.when(jnp.logical_or(chip > 0, core != which))
            def _():
                mixed_copy(chip, which).start()

        at_step(step, 2, lambda: outputs.pass_on(1), lambda: outputs.pass_on(2), line_expand[0].start_z)
        return unused

    lax.fori_loop(0, 4, attend_step, 0)
    mem.mixed_rows[:, block_of(me, LANES)] = mem.mixed_out[block_of(me, rows), :]
    outputs.pass_on(3)
    for chip in range(4):
        outputs.complete(chip)
    outputs.finish()

    def wait_pieces(copy):
        for mask in range(1, seq):
            copy(mask).wait()

    def mixed_wait(mask):
        other = heads.at(mask)
        return push(
            mem.mixed_out.at[block_of(other, rows)],
            mem.mixed_rows.at[:, block_of(other, LANES)],
            mem.mixed_send.at[mask],
            mem.mixed_recv.at[mask],
            (other, group),
        )

    wait_pieces(mixed_wait)
    middle = ins.inputs[...].astype(WIDE) + dot(mem.mixed_rows[...], mem.output_full[...])
    mem.middle[...] = middle
    unit_two, scale_two = norm_rows(middle)
    mem.own_rows[1] = (unit_two * ins.gains[1:2, :]).astype(LOW)
    acts = gather(feeds, 1, mem.act_two)
    acts.start()
    line_expand[1].start_z()
    line_expand[0].pass_on()
    line_reduce.pass_on()
    line_expand[1].start_y()
    for which in range(3):
        mem.attend_back[block_of(which, LANES)] = attend_matrix(which).T
    line_expand[0].land()

    def expand_matrix(which):
        return mem.expand_all[which].reshape(D, hidden_width)

    def reduce_matrix():
        return mem.reduce_all[...].reshape(hidden_width, D)

    def feed_gate(chip):
        span = block_of(chip_of(feeds, chip), pair)
        mem.by_gate[span, :] = dot(mem.act_two[span, :], expand_matrix(0))

    each_chip(acts, feed_gate, {2: [line_expand[1].pass_on]})
    line_expand[1].land()
    line_reduce.land()
    sums = scatter(feeds, 1)

    def feed_down(step, unused):
        chip = lax.rem(step + 1, 4)
        span = block_of(chip_of(feeds, chip), pair)
        gate = mem.by_gate[span, :]
        up = dot(mem.act_two[span, :], expand_matrix(1))
        sigmoid = 1.0 / (1.0 + jnp.exp(-gate))
        swish = gate * sigmoid
        mem.by_up[span, :] = swish
        mem.by_gate[span, :] = up * sigmoid * (1.0 + gate * (1.0 - sigmoid))
        hidden = (swish * up).astype(LOW)
        mem.hidden[span, :] = hidden
        sums.put(chip, dot(hidden, reduce_matrix()))
        at_step(step, 1, lambda: sums.combine(1))
        at_step(step, 2, lambda: sums.combine(2))
        return unused

    lax.fori_loop(0, 4, feed_down, 0)
    sums.combine(3)

    for which in range(2):
        mem.expand_back[block_of(which, hidden_width)] = expand_matrix(which).T
    mem.reduce_back[...] = reduce_matrix().T
    for block in range(length // pair):
        span = block_of(block, pair)
        mem.hidden_turned[:, span] = mem.hidden[span, :].T
    output = mem.middle[...] + sums.total()
    outs.layer_output[...] = output
    for copy in count_copies:
        copy.wait()
    count_all = jnp.sum(
        mem.count[0, 2:3] + mem.count[1, 2:3] + mem.count[2, 2:3] + mem.count[3, 2:3],
        axis=1,
        keepdims=True,
    )
    error = jnp.where(ins.scored[...] > 0.0, output - ins.teacher[...].astype(WIDE), 0.0)
    mem.squares[1:2, :] = jnp.sum(error * error, axis=0, keepdims=True)
    grad_out = error * (2.0 / (count_all * D))
    mem.grad_own[...] = grad_out
    mem.own_rows[2] = grad_out.astype(LOW)
    acts = gather(feeds, 2, mem.branch)
    acts.start()

    sums = scatter(feeds, 2)
    for block in range(length // pair):
        span = block_of(block, pair)
        mem.act_two_turned[:, span] = mem.act_two[span, :].T

    def feed_back(chip):
        span = block_of(chip_of(feeds, chip), pair)
        grad_hidden = dot(mem.branch[span, :], mem.reduce_back[...])
        grad_gate = (grad_hidden * mem.by_gate[span, :]).astype(LOW)
        grad_up = (grad_hidden * mem.by_up[span, :]).astype(LOW)
        mem.grad_gate[span, :] = grad_gate
        mem.grad_up[span, :] = grad_up
        sums.put(
            chip,
            dot(grad_gate, mem.expand_back[:hidden_width])
            + dot(grad_up, mem.expand_back[hidden_width:]),
        )

    each_chip(
        acts, feed_back, {2: [lambda: sums.combine(1)], 3: [lambda: sums.combine(2)]}
    )
    sums.combine(3)

    def line_scatter(row, part_of, landing):
        return LineScatter(
            part_of, landing, mem.back_send.at[row], mem.back_recv.at[row], me, group
        )

    def quad_scatter(row, part_of, landing):
        return QuadScatter(
            part_of, landing, mem.back_send.at[row], mem.back_recv.at[row], me, group
        )

    def reduce_grad(part, unused):
        mem.reduce_grad[part] = dot(
            mem.hidden_turned[block_of(part, rows), :], mem.branch[...]
        ).astype(LOW)
        return unused

    lax.fori_loop(0, batch, reduce_grad, 0)
    back_reduce = quad_scatter(0, lambda part: mem.reduce_grad.at[part], mem.reduce_land)
    back_reduce.start_far()

    def expand_grad(which):
        grads = (mem.grad_gate, mem.grad_up)[which]

        def one_block(block, unused):
            products = dot(mem.act_two_turned[block_of(block, pair), :], grads[...]).astype(LOW)
            mem.expand_grad[which, pl.ds(2 * block, 2)] = products.reshape(
                2, batch, share, hidden_width
            )
            return unused

        lax.fori_loop(0, seq // 2, one_block, 0)
        line = quad_scatter(
            1 + which, expand_part_of(mem.expand_grad, which), mem.expand_land.at[which]
        )
        return line

    back_expand = [expand_grad(0)]
    back_expand[0].start_far()
    grad_act = sums.total()
    unit_two, scale_two = norm_rows(mem.middle[...])
    gain = ins.gains[1:2, :]
    grad_unit = grad_act * gain
    mem.gains[1:2, :] = jnp.sum(grad_act * unit_two, axis=0, keepdims=True)
    grad_middle = mem.grad_own[...] + scale_two * (
        grad_unit - unit_two * jnp.mean(grad_unit * unit_two, axis=-1, keepdims=True)
    )
    mem.grad_own[...] = grad_middle
    mem.own_rows[3] = grad_middle.astype(LOW)
    grad_mixed = dot(mem.output_full[...], grad_middle.T.astype(LOW)).astype(LOW)
    mem.grad_mixed_out[...] = grad_mixed.reshape(seq, LANES, rows)

    def grad_copy(mask, back=False):
        return push(
            mem.grad_mixed_out.at[heads.at(mask)],
            mem.grad_mixed.at[:, block_of(heads.at(mask) if back else me, rows)],
            mem.mixed_send.at[8 + mask],
            mem.mixed_recv.at[8 + mask],
            heads.place(mask),
        )

    for mask in masks:
        grad_copy(mask).start()
    mem.grad_mixed[:, block_of(me, rows)] = mem.grad_mixed_out[me]
    acts = gather(heads, 3, mem.grad_attn)
    acts.start()
    back_reduce.pass_on()
    back_expand.append(expand_grad(1))

    wait_pieces(lambda mask: grad_copy(mask, True))
    back_attend = [
        line_scatter(
            4 + which,
            lambda part, which=which: mem.attend_grad.at[which, :, part],
            mem.attend_land.at[which],
        )
        for which in range(3)
    ]

    def attend_grad(which):
        grads = dot(mem.grad_project[which], mem.act_one[...])
        mem.attend_grad[which] = grads.T.astype(LOW).reshape(seq, batch, share, LANES)
        back_attend[which].start()

    lane = lax.broadcasted_iota(jnp.int32, (pair, LANES), 1)

    def grad_rows(block, unused):
        span = block_of(block, pair)
        whole = mem.grad_mixed[:, span].astype(WIDE).T
        for head in range(HEADS_HERE):
            mem.grad_heads[head, span, :] = jnp.where(lax.div(lane, HEAD_DIM) == head, whole, 0.0).astype(LOW)
        return unused

    lax.fori_loop(0, length // pair, grad_rows, 0)

    def value_back(block, unused):
        span = block_of(block, pair)
        total = dot(mem.probs[0, span, :], mem.grad_heads[0])
        for head in range(1, HEADS_HERE):
            total = total + dot(mem.probs[head, span, :], mem.grad_heads[head])
        mem.grad_project[2, :, span] = total.T.astype(LOW)
        return unused

    lax.fori_loop(0, length // pair, value_back, 0)
    attend_grad(2)

    def score_back(block, unused):
        columns = block_of(block, pair)
        row = lax.broadcasted_iota(jnp.int32, (HEAD_DIM, pair), 0)
        grads = mem.grad_mixed[:, columns]
        delta = grads.astype(WIDE) * mem.exact[:, columns]
        for head in range(HEADS_HERE):
            span = slice(head * HEAD_DIM, (head + 1) * HEAD_DIM)
            pieces = thirds(-jnp.sum(delta[span], axis=0, keepdims=True))
            marks = pick(row, dict(enumerate(pieces))).astype(LOW)
            change = dot(mem.value_heads[head], jnp.concatenate([grads[span], marks], axis=0))
            mem.probs[head, :, columns] = (mem.probs[head, :, columns].astype(WIDE) * change).astype(LOW)
        at_step(block, 1, lambda: acts.pass_on(1), lambda: acts.pass_on(2), back_expand[0].pass_on)
        at_step(block, 2, lambda: acts.pass_on(3))
        return unused

    lax.fori_loop(0, length // pair, score_back, 0)
    back_expand[1].start_far()
    back_reduce.start_near()
    mem.bias_sums[...] = jnp.zeros_like(mem.bias_sums)
    scale = HEAD_DIM ** (-0.5)

    def project_grads(block, unused):
        span = block_of(block, pair)
        cosine, sine = mem.cosine[:, span], -mem.sine[:, span]
        queries, keys = [], []
        for head in range(HEADS_HERE):
            features = slice(head * HEAD_DIM, (head + 1) * HEAD_DIM)
            queries.append(dot(mem.key_turned[features, :], mem.probs[head, :, span]) * scale)
            sums = dot(mem.probs[head, span, :], mem.query_heads[head]).T
            keys.append(sums[:HEAD_DIM])
            by_variate = sums[HEAD_DIM : HEAD_DIM + VARIATES]
            same = by_variate * mem.key_marks[:VARIATES, span].astype(WIDE)
            mem.bias_sums[head : head + 1, :] += jnp.sum(same, axis=0, keepdims=True)
            total = sums[HEAD_DIM + VARIATES : HEAD_DIM + VARIATES + 1]
            mem.bias_sums[HEADS_HERE + head : HEADS_HERE + head + 1, :] += total
        mem.grad_project[0, :, span] = turn_rows(jnp.concatenate(queries, axis=0), cosine, sine).astype(LOW)
        mem.grad_project[1, :, span] = turn_rows(jnp.concatenate(keys, axis=0), cosine, sine).astype(LOW)
        return unused

    lax.fori_loop(0, length // pair, project_grads, 0)
    for which in range(2):
        attend_grad(which)
    back_expand[0].start_near()
    back_expand[1].start_near()
    sums = scatter(heads, 3)

    def project_back(step, unused):
        chip = lax.rem(step + 1, 4)
        span = block_of(chip_of(heads, chip), pair)
        grads = [mem.grad_project[which, :, span].astype(WIDE).T.astype(LOW) for which in range(3)]
        sums.put(chip, dot(jnp.concatenate(grads, axis=1), mem.attend_back[...]))
        at_step(step, 1, lambda: sums.combine(1))
        at_step(step, 2, lambda: sums.combine(2))
        return unused

    lax.fori_loop(0, 4, project_back, 0)
    sums.combine(3)
    for chip in range(4):
        acts.complete(chip)
    acts.finish()
    mem.output_grad[...] = (
        dot(mem.mixed_turned[...], mem.grad_attn[...]).astype(LOW).reshape(mem.output_grad.shape)
    )
    back_output = line_scatter(3, lambda part: mem.output_grad.at[part], mem.output_land)
    back_output.start()
    back_expand[1].pass_on()
    back_attend[2].pass_on()

    column_copies = []
    mem.squares[0:1, :] = jnp.zeros((1, D), WIDE)

    def add_squares(total):
        flat = total.reshape(-1, total.shape[-1])
        width = flat.shape[1]
        mem.squares[0:1, :width] += jnp.sum(flat * flat, axis=0, keepdims=True)

    def store_whole(total, out):
        out[...] = total
        add_squares(total)

    back_reduce.land()
    store_whole(
        mem.reduce_grad[quad].astype(WIDE)
        + mem.reduce_land[0].astype(WIDE)
        + mem.reduce_land[2].astype(WIDE),
        outs.reduce_share,
    )
    grad_act = sums.total()
    unit_one, scale_one = norm_rows(ins.inputs[...].astype(WIDE))
    gain = ins.gains[0:1, :]
    grad_unit = grad_act * gain
    mem.gains[0:1, :] = jnp.sum(grad_act * unit_one, axis=0, keepdims=True)
    grad_input = mem.grad_own[...] + scale_one * (
        grad_unit - unit_one * jnp.mean(grad_unit * unit_one, axis=-1, keepdims=True)
    )
    outs.input_gradient[...] = grad_input * (count_all * D)
    outs.count[...] = jnp.broadcast_to(count_all, (8, LANES))
    back_attend[0].pass_on()
    back_attend[1].pass_on()
    back_output.pass_on()

    def expand_shares(which):
        back_expand[which].land()
        own = expand_part_of(mem.expand_grad, which)(quad)

        def one_block(block, unused):
            total = (
                own[block].astype(WIDE)
                + mem.expand_land[which, 0, block].astype(WIDE)
                + mem.expand_land[which, 2, block].astype(WIDE)
            )
            mem.expand_part[which, block] = total.astype(LOW)
            add_squares(total)
            return unused

        lax.fori_loop(0, 4, one_block, 0)
        for mask in masks:
            other = feeds.at(mask)
            copy = push(
                mem.expand_part.at[which, lax.rem(other, 4), lax.div(other, 4)],
                mem.expand_share.at[which, feeds.index],
                mem.share_send.at[which, mask],
                mem.share_recv.at[which, mask],
                feeds.place(mask),
            )
            copy.start()
            column_copies.append(copy)
        mem.expand_share[which, feeds.index] = mem.expand_part[
            which, lax.rem(feeds.index, 4), lax.div(feeds.index, 4)
        ]

    for which in range(2):
        expand_shares(which)
    back_output.land()
    back_output.add(
        lambda: mem.output_grad[group].astype(WIDE),
        lambda slot: mem.output_land[slot].astype(WIDE),
        lambda total: store_whole(total, outs.output_share),
    )

    def attend_shares(which):
        def store(total):
            mem.attend_part[which] = total.astype(LOW)
            add_squares(total)

        back_attend[which].land()
        back_attend[which].add(
            lambda: mem.attend_grad[which, :, group].astype(WIDE),
            lambda slot: mem.attend_land[which, slot].astype(WIDE),
            store,
        )

    for which in (2, 0, 1):
        attend_shares(which)
    for mask in masks:
        copy = push(
            mem.attend_part.at[:, heads.at(mask)],
            outs.attend_share.at[:, :, block_of(me, LANES)],
            mem.share_send.at[2, mask],
            mem.share_recv.at[2, mask],
            heads.place(mask),
        )
        copy.start()
        column_copies.append(copy)
    outs.attend_share[:, :, block_of(me, LANES)] = mem.attend_part[:, me]

    lane = lax.broadcasted_iota(jnp.int32, (1, LANES), 1)
    lines = [
        mem.gains[which : which + 1, start : start + LANES]
        for which in range(2)
        for start in range(0, D, LANES)
    ]
    bias_line = jnp.zeros((1, LANES), WIDE)
    for row in range(2 * HEADS_HERE):
        place = row // HEADS_HERE * HEADS + me * HEADS_HERE + row % HEADS_HERE
        line = mem.bias_sums[row : row + 1, :]
        if row >= HEADS_HERE:
            line = line - mem.bias_sums[row - HEADS_HERE : row - HEADS_HERE + 1, :]
        amount = jnp.sum(line, axis=1, keepdims=True)
        bias_line = bias_line + jnp.where(lane == place, amount, 0.0)
    amounts = jnp.sum(mem.squares[0:2, :], axis=1, keepdims=True)
    amount_line = jnp.where(lane == 0, amounts[0:1], 0.0) + jnp.where(lane == 1, amounts[1:2], 0.0)
    lines += [bias_line, amount_line, jnp.zeros((6, LANES), WIDE)]
    mem.plane_totals[me] = jnp.concatenate(lines, axis=0)
    plane_copies = []
    for mask in masks:
        copy = push(
            mem.plane_totals.at[me],
            mem.plane_totals.at[me],
            mem.total_send.at[0, mask],
            mem.total_recv.at[0, mask],
            (flip(me, mask), group),
        )
        copy.start()
        plane_copies.append(copy)
    for copy in plane_copies:
        copy.wait()
    mem.line_totals[group] = jnp.sum(mem.plane_totals[...], axis=0)
    total_copies = []
    for step in range(1, batch):
        copy = push(
            mem.line_totals.at[group],
            mem.line_totals.at[group],
            mem.total_send.at[1, step],
            mem.total_recv.at[1, step],
            (me, lax.rem(group + step, batch)),
        )
        copy.start()
        total_copies.append(copy)
    for copy in total_copies:
        copy.wait()
    outs.totals[...] = jnp.sum(mem.line_totals[...], axis=0)
    for copy in column_copies:
        copy.wait()
    for which in range(2):
        for block in range(blocks):
            owner, part = feed_block(block)
            outs.expand_share[which, :, block * LANES : (block + 1) * LANES] = mem.expand_share[
                which, owner, :, part * LANES : (part + 1) * LANES
            ]
    for copies in (attend_columns, expand_columns):
        for copy in copies:
            copy.wait_send()
    for line in [line_attend, line_output, line_reduce] + line_expand:
        line.finish()
    for line in [back_output, back_reduce] + back_attend + back_expand:
        line.finish()


def call_layer(seq, batch, inputs, teacher, facts, scored, bias, gains, attend, output, expand, reduce):
    rows, share, hidden = inputs.shape[0], attend.shape[1], expand.shape[2] // seq
    length, pair, chips = rows * seq, 2 * rows, seq // 2
    low = lambda *shape: pltpu.VMEM(shape, LOW)
    wide = lambda *shape: pltpu.VMEM(shape, WIDE)
    sems = lambda *shape: pltpu.SemaphoreType.DMA(shape)
    in_names = ["inputs", "teacher", "facts", "scored", "bias", "gains"]
    in_names += ["attend", "output", "expand", "reduce"]
    outs = dict(
        layer_output=((rows, D), WIDE),
        input_gradient=((rows, D), WIDE),
        totals=((TOTAL_ROWS, LANES), WIDE),
        count=((8, LANES), WIDE),
        attend_share=((3, share, D), LOW),
        output_share=((output.shape[0], D), WIDE),
        expand_share=((2, share, hidden * seq), LOW),
        reduce_share=((reduce.shape[0], D), WIDE),
    )
    scratch = dict(
        gains=wide(2, D),
        squares=wide(8, D),
        plane_totals=wide(seq, TOTAL_ROWS, LANES),
        line_totals=wide(batch, TOTAL_ROWS, LANES),
        attend_low=low(3, share, D),
        expand_low=low(2, seq, share, hidden),
        attend_all=low(3, seq, batch, share, LANES),
        output_full=low(D, D),
        expand_all=low(2, seq, batch, share, hidden),
        reduce_all=low(batch, reduce.shape[0], D),
        own_rows=low(4, rows, D),
        act_one=low(length, D),
        act_two=low(length, D),
        branch=low(length, D),
        grad_attn=low(length, D),
        facts_all=wide(seq * facts.shape[0], LANES),
        cosine=wide(HEAD_DIM // 2, length),
        sine=wide(HEAD_DIM // 2, length),
        labels=wide(8, length),
        key_marks=low(HEAD_DIM, length),
        count=wide(batch, 8, LANES),
        query_turned=low(HEADS_HERE, LANES, length),
        key_turned=low(LANES, length),
        value_turned=low(LANES, length),
        key_heads=low(HEADS_HERE, length, LANES),
        value_heads=low(HEADS_HERE, length, LANES),
        query_heads=low(HEADS_HERE, length, LANES),
        grad_heads=low(HEADS_HERE, length, LANES),
        grad_mixed=low(LANES, length),
        grad_mixed_out=low(seq, LANES, rows),
        probs=low(HEADS_HERE, length, length),
        mixed_out=low(length, LANES),
        mixed_rows=low(rows, D),
        attend_back=low(3 * LANES, D),
        expand_back=low(2 * hidden, D),
        reduce_back=low(D, hidden),
        hidden_turned=low(hidden, length),
        act_two_turned=low(D, length),
        exact=wide(LANES, length),
        mixed_wide=wide(LANES, pair),
        mixed_turned=low(LANES, length),
        whole=wide(pair, D),
        keep=wide(chips, rows, D),
        near_from=low(chips, rows, D),
        near=low(chips, rows, D),
        far_from=low(chips, rows, D),
        far=low(chips, rows, D),
        middle=wide(rows, D),
        grad_own=wide(rows, D),
        by_up=wide(length, hidden),
        by_gate=wide(length, hidden),
        hidden=low(length, hidden),
        grad_gate=low(length, hidden),
        grad_up=low(length, hidden),
        bias_sums=wide(8, pair),
        grad_project=low(3, LANES, length),
        reduce_grad=low(batch, reduce.shape[0], D),
        expand_grad=low(2, seq, batch, share, hidden),
        output_grad=low(batch, output.shape[0], D),
        attend_grad=low(3, seq, batch, share, LANES),
        reduce_land=low(3, reduce.shape[0], D),
        expand_land=low(2, 3, 4, 2, share, hidden),
        output_land=low(batch, output.shape[0], D),
        attend_land=low(3, batch, seq, share, LANES),
        expand_part=low(2, 4, 2, share, hidden),
        expand_share=low(2, seq, share, hidden),
        attend_part=low(3, seq, share, LANES),
        stage_sem=sems(5 + 2 * (expand.shape[2] // D)),
        total_send=sems(2, seq),
        total_recv=sems(2, seq),
        column_send=sems(2, seq),
        column_recv=sems(2, seq),
        line_send=sems(5, batch),
        line_recv=sems(5, batch),
        facts_send=sems(seq),
        facts_recv=sems(seq),
        gather_send=sems(4, seq),
        gather_recv=sems(4, seq),
        count_send=sems(batch),
        count_recv=sems(batch),
        near_send=sems(4, chips),
        near_recv=sems(4, chips),
        far_send=sems(4, chips),
        far_recv=sems(4, chips),
        back_send=sems(7, batch),
        back_recv=sems(7, batch),
        output_send=sems(seq),
        output_recv=sems(seq),
        mixed_send=sems(2 * seq),
        mixed_recv=sems(2 * seq),
        share_send=sems(3, seq),
        share_recv=sems(3, seq),
    )

    places = dict.fromkeys(("attend", "output", "expand", "reduce"), pl.BlockSpec(memory_space=pl.ANY))
    places["bias"] = IN_SMEM

    def kernel(*refs):
        groups, start = [], 0
        for names in (in_names, outs, scratch):
            names = list(names)
            groups.append(types.SimpleNamespace(**dict(zip(names, refs[start : start + len(names)]))))
            start += len(names)
        layer_kernel(seq, batch, *groups)

    results = pl.pallas_call(
        kernel,
        out_shape=[jax.ShapeDtypeStruct(*out) for out in outs.values()],
        in_specs=[places.get(name, IN_VMEM) for name in in_names],
        out_specs=[IN_VMEM] * len(outs),
        scratch_shapes=list(scratch.values()),
        compiler_params=pltpu.CompilerParams(
            collective_id=0, has_side_effects=True, vmem_limit_bytes=63 * MIB
        ),
        name="layer",
    )(inputs, teacher, facts, scored, bias, gains, attend, output, expand, reduce)
    return types.SimpleNamespace(**dict(zip(outs, results)))


def update_kernel(
    totals,
    count,
    layer_output,
    input_gradient,
    attend_share,
    output_share,
    expand_share,
    reduce_share,
    gains,
    gains_first,
    gains_second,
    bias,
    bias_first,
    bias_second,
    *refs,
):
    olds, news = refs[:12], refs[12:]
    news[0][...] = layer_output[...]
    news[1][...] = input_gradient[...]
    gains_total = jnp.concatenate(
        [
            jnp.concatenate([totals[row + i : row + i + 1, :] for i in range(D // LANES)], axis=1)
            for row in (0, D // LANES)
        ],
        axis=0,
    )
    row = 2 * D // LANES
    bias_total = jnp.concatenate(
        [totals[row : row + 1, :HEADS], totals[row : row + 1, HEADS : 2 * HEADS]], axis=0
    )
    row += 1

    def sum_all(values):
        return jnp.sum(jnp.sum(values, axis=0, keepdims=True), axis=1, keepdims=True)

    squares = (
        totals[row : row + 1, 0:1] + sum_all(gains_total * gains_total) + sum_all(bias_total * bias_total)
    )
    grad_norm = jnp.sqrt(squares)
    clip = jnp.minimum(1.0, CLIP_NORM / grad_norm)
    news[2][...] = totals[row : row + 1, 1:2] / (count[0:1, 0:1] * D)
    news[3][...] = grad_norm
    shares = (attend_share, output_share, expand_share, reduce_share)
    rates = (RATE_ATTEND, RATE_OUTPUT, RATE_EXPAND, RATE_REDUCE)
    for number, (share, rate) in enumerate(zip(shares, rates)):
        weight, first, second = olds[3 * number : 3 * number + 3]
        new, copy, first_new, second_new = news[4 + 4 * number : 8 + 4 * number]
        scale = clip.reshape((1,) * share.ndim)
        new[...], first_new[...], second_new[...] = adam_step(
            weight[...], first[...], second[...], share[...].astype(WIDE) * scale, rate, WEIGHT_DECAY
        )
        copy[...] = new[...].astype(LOW)
    for number, (old, total, rate) in enumerate(
        (
            ((gains, gains_first, gains_second), gains_total, RATE_GAINS),
            ((bias, bias_first, bias_second), bias_total, RATE_BIAS),
        )
    ):
        new, first_new, second_new = news[20 + 3 * number : 23 + 3 * number]
        new[...], first_new[...], second_new[...] = adam_step(
            old[0][...], old[1][...], old[2][...], total * clip, rate, 0.0
        )


UPDATE_STEPS = 2


def cut_spec(shape):
    rows = shape[-2] // UPDATE_STEPS
    if len(shape) == 3:
        return pl.BlockSpec((shape[0], rows, shape[2]), lambda step: (0, step, 0))
    return pl.BlockSpec((rows, shape[1]), lambda step: (step, 0))


def whole_spec(shape):
    return pl.BlockSpec(shape, lambda step: (0,) * len(shape))


def call_update(done, shares, smalls, olds):
    whole = [done.totals, done.count]
    cut = [done.layer_output, done.input_gradient] + shares
    outs = [(done.layer_output, WIDE, cut_spec), (done.input_gradient, WIDE, cut_spec)]
    one = jax.ShapeDtypeStruct((1, 1), WIDE)
    outs += [(one, WIDE, whole_spec)] * 2
    for weight in olds[::3]:
        outs += [(weight, dtype, cut_spec) for dtype in (WIDE, LOW, WIDE, WIDE)]
    outs += [(small, WIDE, whole_spec) for small in smalls]
    return pl.pallas_call(
        update_kernel,
        grid=(UPDATE_STEPS,),
        out_shape=[jax.ShapeDtypeStruct(array.shape, dtype) for array, dtype, spec in outs],
        in_specs=[whole_spec(array.shape) for array in whole]
        + [cut_spec(array.shape) for array in cut]
        + [whole_spec(array.shape) for array in smalls]
        + [cut_spec(array.shape) for array in olds],
        out_specs=[spec(array.shape) for array, dtype, spec in outs],
        compiler_params=pltpu.CompilerParams(vmem_limit_bytes=63 * MIB),
        name="update",
    )(*whole, *cut, *smalls, *olds)


def fast_body(
    seq,
    batch,
    inputs,
    teacher,
    lengths,
    variate_ids,
    time_ids,
    observed,
    attend_weight,
    output_weight,
    expand_weight,
    reduce_weight,
    norm_gains,
    variate_bias,
    attend_first,
    output_first,
    expand_first,
    reduce_first,
    gains_first,
    bias_first,
    attend_second,
    output_second,
    expand_second,
    reduce_second,
    gains_second,
    bias_second,
):
    me = lax.axis_index("seq")
    rows = inputs.shape[1]
    positions = me * rows + jnp.arange(rows, dtype=jnp.int32)
    inside = positions < lengths[0]
    scored = jnp.logical_and(inside, observed[0] == 1)
    half_dim = HEAD_DIM // 2
    frequency = jnp.exp(-math.log(ROPE_BASE) * jnp.arange(half_dim).astype(WIDE) / half_dim)
    angle = frequency[:, None] * time_ids[0].astype(WIDE)[None, :]
    labels = jnp.stack(
        [
            jnp.where(inside, variate_ids[0], -1).astype(WIDE),
            variate_ids[0].astype(WIDE),
            scored.astype(WIDE),
        ]
    )
    facts = jnp.concatenate([jnp.cos(angle), jnp.sin(angle), jnp.pad(labels, ((0, 5), (0, 0)))])
    done = call_layer(
        seq,
        batch,
        inputs[0],
        teacher[0],
        facts,
        scored.astype(WIDE)[:, None],
        variate_bias,
        norm_gains,
        attend_weight,
        output_weight,
        expand_weight,
        reduce_weight,
    )
    results = call_update(
        done,
        [done.attend_share, done.output_share, done.expand_share, done.reduce_share],
        [norm_gains, gains_first, gains_second, variate_bias, bias_first, bias_second],
        [attend_weight, attend_first, attend_second]
        + [output_weight, output_first, output_second]
        + [expand_weight, expand_first, expand_second]
        + [reduce_weight, reduce_first, reduce_second],
    )
    output, input_gradient, loss, grad_norm = results[:4]
    return (
        output[None],
        loss.reshape(()),
        input_gradient[None],
        grad_norm.reshape(()),
    ) + tuple(results[4:])


def solution(mesh):
    seq, batch = mesh.shape["seq"], mesh.shape["batch"]
    body = functools.partial(fast_body, seq, batch) if fast_fits(seq, batch) else general_body
    in_specs = (
        P("batch", "seq", None),
        P("batch", "seq", None),
        P("batch"),
        P("batch", "seq"),
        P("batch", "seq"),
        P("batch", "seq"),
        P(None, ("seq", "batch"), None),
        P(("seq", "batch"), None),
        P(None, ("seq", "batch"), None),
        P(("seq", "batch"), None),
        P(),
        P(),
        P(None, ("seq", "batch"), None),
        P(("seq", "batch"), None),
        P(None, ("seq", "batch"), None),
        P(("seq", "batch"), None),
        P(),
        P(),
        P(None, ("seq", "batch"), None),
        P(("seq", "batch"), None),
        P(None, ("seq", "batch"), None),
        P(("seq", "batch"), None),
        P(),
        P(),
    )
    out_specs = (
        P("batch", "seq", None),
        P(),
        P("batch", "seq", None),
        P(),
        P(None, ("seq", "batch"), None),
        P(None, ("seq", "batch"), None),
        P(None, ("seq", "batch"), None),
        P(None, ("seq", "batch"), None),
        P(("seq", "batch"), None),
        P(("seq", "batch"), None),
        P(("seq", "batch"), None),
        P(("seq", "batch"), None),
        P(None, ("seq", "batch"), None),
        P(None, ("seq", "batch"), None),
        P(None, ("seq", "batch"), None),
        P(None, ("seq", "batch"), None),
        P(("seq", "batch"), None),
        P(("seq", "batch"), None),
        P(("seq", "batch"), None),
        P(("seq", "batch"), None),
        P(),
        P(),
        P(),
        P(),
        P(),
        P(),
    )
    return jax.shard_map(body, mesh=mesh, in_specs=in_specs, out_specs=out_specs, check_vma=False)
```

```python
import functools
import math
import types

import jax
import jax.numpy as jnp
from jax import lax
from jax.experimental import pallas as pl
from jax.experimental.pallas import tpu as pltpu
from jax.sharding import PartitionSpec as P

D = 1024
HEADS = 16
HEAD_DIM = 64
STEP = 10


NORM_EPS = 1e-05
ROPE_BASE = 10000.0
MASKED = -1e30
CLIP_NORM = 1.0
BETA_ONE = 0.9
BETA_TWO = 0.98
ADAM_EPS = 1e-08
WEIGHT_DECAY = 0.1
RATE_ATTEND = 0.03
RATE_OUTPUT = 0.5
RATE_EXPAND = 0.03
RATE_REDUCE = 0.015
RATE_GAINS = 1.0
RATE_BIAS = 0.5


def angles(times):
    half_dim = HEAD_DIM // 2
    frequency = jnp.exp(-math.log(ROPE_BASE) * jnp.arange(half_dim).astype(jnp.float32) / half_dim)
    angle_table = times.astype(jnp.float32)[..., None] * frequency
    return (jnp.cos(angle_table)[..., None, :], jnp.sin(angle_table)[..., None, :])


def rotate(values, cos_table, sin_table):
    half_dim = values.shape[-1] // 2
    first_half = values[..., :half_dim]
    second_half = values[..., half_dim:]
    return jnp.concatenate(
        [
            first_half * cos_table - second_half * sin_table,
            second_half * cos_table + first_half * sin_table,
        ],
        axis=-1,
    )


def unrotate(values, cos_table, sin_table):
    half_dim = values.shape[-1] // 2
    first_half = values[..., :half_dim]
    second_half = values[..., half_dim:]
    return jnp.concatenate(
        [
            first_half * cos_table + second_half * sin_table,
            second_half * cos_table - first_half * sin_table,
        ],
        axis=-1,
    )


def normalize(values):
    inv_scale = lax.rsqrt(jnp.mean(values * values, axis=-1, keepdims=True) + NORM_EPS)
    return (values * inv_scale, inv_scale)


def norm_back(grad_act, unit_rows, inv_scale, gain_row):
    grad_unit = grad_act * gain_row
    return inv_scale * (
        grad_unit - unit_rows * jnp.mean(grad_unit * unit_rows, axis=-1, keepdims=True)
    )


def score_block(query_rows, query_labels, key_rows, key_labels, bias_table):
    scores = jnp.einsum(
        "ihe,jhe->hij", query_rows, key_rows, preferred_element_type=jnp.float32
    ) * HEAD_DIM ** (-0.5)
    same_var = query_labels[:, None] == key_labels[None, :]
    scores = scores + jnp.where(
        same_var[None], bias_table[0][:, None, None], bias_table[1][:, None, None]
    )
    scores = jnp.where(key_labels[None, None, :] >= 0, scores, MASKED)
    return (scores, same_var)


def block_grads(
    query_rows,
    query_labels,
    grad_rows,
    lse_rows,
    delta_rows,
    key_rows,
    value_rows,
    key_labels,
    bias_table,
    need_query,
    need_keys,
):
    scores, same_var = score_block(query_rows, query_labels, key_rows, key_labels, bias_table)
    weights = jnp.exp(scores - lse_rows.T[:, :, None])
    grad_weights = jnp.einsum(
        "ihe,jhe->hij", grad_rows, value_rows, preferred_element_type=jnp.float32
    )
    grad_scores = (weights * (grad_weights - delta_rows.T[:, :, None])).astype(jnp.bfloat16)
    result = ()
    if need_query:
        grad_query = jnp.einsum(
            "hij,jhe->ihe", grad_scores, key_rows, preferred_element_type=jnp.float32
        ) * HEAD_DIM ** (-0.5)
        widened = grad_scores.astype(jnp.float32)
        bias_same = jnp.sum(jnp.where(same_var[None], widened, 0.0), axis=(1, 2))
        bias_other = jnp.sum(jnp.where(same_var[None], 0.0, widened), axis=(1, 2))
        result = result + (grad_query, jnp.stack([bias_same, bias_other]))
    if need_keys:
        grad_key = jnp.einsum(
            "hij,ihe->jhe", grad_scores, query_rows, preferred_element_type=jnp.float32
        ) * HEAD_DIM ** (-0.5)
        grad_value = jnp.einsum(
            "hij,ihe->jhe",
            weights.astype(jnp.bfloat16),
            grad_rows,
            preferred_element_type=jnp.float32,
        )
        result = result + (grad_key, grad_value)
    return result


def adam_step(weight, first_moment, second_moment, gradient, step_rate, decay_rate):
    first_moment = BETA_ONE * first_moment + (1.0 - BETA_ONE) * gradient
    second_moment = BETA_TWO * second_moment + (1.0 - BETA_TWO) * gradient * gradient
    direction = (
        first_moment
        / (1.0 - BETA_ONE**STEP)
        / (jnp.sqrt(second_moment / (1.0 - BETA_TWO**STEP)) + ADAM_EPS)
    )
    return (weight - step_rate * (direction + decay_rate * weight), first_moment, second_moment)


def general_body(
    inputs,
    teacher,
    lengths,
    variate_ids,
    time_ids,
    observed,
    attend_weight,
    output_weight,
    expand_weight,
    reduce_weight,
    norm_gains,
    variate_bias,
    attend_first,
    output_first,
    expand_first,
    reduce_first,
    gains_first,
    bias_first,
    attend_second,
    output_second,
    expand_second,
    reduce_second,
    gains_second,
    bias_second,
):
    row_count = inputs.shape[1]
    length = row_count * lax.axis_size("seq")
    block_rows = math.gcd(length, 1024)
    blocks = length // block_rows
    states = inputs[0].astype(jnp.float32)
    positions = lax.axis_index("seq") * row_count + jnp.arange(row_count, dtype=jnp.int32)
    inside = positions < lengths[0]
    scored = jnp.logical_and(inside, observed[0] == 1)
    local_count = jnp.sum(scored.astype(jnp.int32))
    count_early = lax.psum(local_count, ("seq", "batch"))
    full_attend, full_output, full_expand, full_reduce = (
        lax.all_gather(attend_weight.astype(jnp.bfloat16), ("seq", "batch"), axis=1, tiled=True),
        lax.all_gather(output_weight.astype(jnp.bfloat16), ("seq", "batch"), axis=0, tiled=True),
        lax.all_gather(expand_weight.astype(jnp.bfloat16), ("seq", "batch"), axis=1, tiled=True),
        lax.all_gather(reduce_weight.astype(jnp.bfloat16), ("seq", "batch"), axis=0, tiled=True),
    )
    unit_one, scale_one = normalize(states)
    act_one = (unit_one * norm_gains[0]).astype(jnp.bfloat16)
    project = jnp.einsum("td,cde->cte", act_one, full_attend, preferred_element_type=jnp.float32)
    cos_table, sin_table = angles(time_ids[0])
    query = rotate(project[0].reshape(row_count, HEADS, HEAD_DIM), cos_table, sin_table).astype(
        jnp.bfloat16
    )
    key_rows = (
        rotate(project[1].reshape(row_count, HEADS, HEAD_DIM), cos_table, sin_table)
        .astype(jnp.bfloat16)
        .reshape(row_count, D)
    )
    value_rows = project[2].astype(jnp.bfloat16)
    own_labels = jnp.where(inside, variate_ids[0], -1).astype(jnp.bfloat16)
    all_keys, all_values, all_labels = (
        lax.all_gather(key_rows, "seq", axis=0, tiled=True),
        lax.all_gather(value_rows, "seq", axis=0, tiled=True),
        lax.all_gather(own_labels, "seq", axis=0, tiled=True),
    )
    key_blocks = all_keys.reshape(blocks, block_rows, HEADS, HEAD_DIM)
    value_blocks = all_values.reshape(blocks, block_rows, HEADS, HEAD_DIM)
    label_blocks = all_labels.astype(jnp.float32).reshape(blocks, block_rows)
    query_labels = variate_ids[0].astype(jnp.float32)

    def sweep_top(carry, pieces):
        running, sum_exp = carry
        scores, same_var = score_block(query, query_labels, pieces[0], pieces[1], variate_bias)
        raised = jnp.maximum(running, jnp.floor(jnp.max(scores, axis=-1)))
        sum_exp = sum_exp * jnp.exp(running - raised) + jnp.sum(
            jnp.exp(scores - raised[..., None]), axis=-1
        )
        return ((raised, sum_exp), None)

    start_top = jnp.full((HEADS, row_count), MASKED, jnp.float32)
    (row_top, sum_exp), unused = lax.scan(
        sweep_top,
        (start_top, jnp.zeros((HEADS, row_count), jnp.float32)),
        (key_blocks, label_blocks),
    )
    log_total = row_top + jnp.log(sum_exp)

    def sweep_out(carry, pieces):
        coarse, finest = carry
        scores, same_var = score_block(query, query_labels, pieces[0], pieces[2], variate_bias)
        weights = jnp.exp(scores - log_total[..., None])
        rounded = weights.astype(jnp.bfloat16)
        residue = (weights - rounded.astype(jnp.float32)).astype(jnp.bfloat16)
        coarse = coarse + jnp.einsum(
            "hij,jhe->ihe", rounded, pieces[1], preferred_element_type=jnp.float32
        )
        finest = finest + jnp.einsum(
            "hij,jhe->ihe", residue, pieces[1], preferred_element_type=jnp.float32
        )
        return ((coarse, finest), None)

    zero_heads = jnp.zeros((row_count, HEADS, HEAD_DIM), jnp.float32)
    (coarse, finest), unused = lax.scan(
        sweep_out, (zero_heads, zero_heads), (key_blocks, value_blocks, label_blocks)
    )
    exact_heads = coarse + finest
    mixed = coarse.reshape(row_count, D).astype(jnp.bfloat16)
    middle = states + jnp.dot(mixed, full_output, preferred_element_type=jnp.float32)
    unit_two, scale_two = normalize(middle)
    act_two = (unit_two * norm_gains[1]).astype(jnp.bfloat16)
    gate_up = jnp.einsum("td,cdf->ctf", act_two, full_expand, preferred_element_type=jnp.float32)
    sigmoid = jax.nn.sigmoid(gate_up[0])
    hidden = (gate_up[0] * sigmoid * gate_up[1]).astype(jnp.bfloat16)
    output = middle + jnp.dot(hidden, full_reduce, preferred_element_type=jnp.float32)
    error = output - teacher[0].astype(jnp.float32)
    local_square = jnp.sum(jnp.where(scored[:, None], error * error, 0.0))
    square_total = lax.psum(local_square, ("seq", "batch"))
    count_all = count_early.astype(jnp.float32)
    loss = square_total / (count_all * D)
    grad_out = jnp.where(scored[:, None], error * (2.0 / (count_all * D)), 0.0)
    back_attend, back_output, back_expand, back_reduce = (
        lax.all_gather(attend_weight.astype(jnp.bfloat16), ("seq", "batch"), axis=1, tiled=True),
        lax.all_gather(output_weight.astype(jnp.bfloat16), ("seq", "batch"), axis=0, tiled=True),
        lax.all_gather(expand_weight.astype(jnp.bfloat16), ("seq", "batch"), axis=1, tiled=True),
        lax.all_gather(reduce_weight.astype(jnp.bfloat16), ("seq", "batch"), axis=0, tiled=True),
    )
    grad_branch = grad_out.astype(jnp.bfloat16)
    reduce_grad = jnp.einsum("tf,td->fd", hidden, grad_branch, preferred_element_type=jnp.float32)
    grad_hidden = jnp.einsum(
        "td,fd->tf", grad_branch, back_reduce, preferred_element_type=jnp.float32
    )
    grad_gate = grad_hidden * gate_up[1] * sigmoid * (1.0 + gate_up[0] * (1.0 - sigmoid))
    grad_up = grad_hidden * gate_up[0] * sigmoid
    grad_expand = jnp.stack([grad_gate, grad_up]).astype(jnp.bfloat16)
    expand_grad = jnp.einsum(
        "td,ctf->cdf", act_two, grad_expand, preferred_element_type=jnp.float32
    )
    grad_act_two = jnp.einsum(
        "ctf,cdf->td", grad_expand, back_expand, preferred_element_type=jnp.float32
    )
    expand_share, reduce_share = (
        lax.psum_scatter(expand_grad, ("seq", "batch"), scatter_dimension=1, tiled=True),
        lax.psum_scatter(reduce_grad, ("seq", "batch"), scatter_dimension=0, tiled=True),
    )
    grad_middle = grad_out + norm_back(grad_act_two, unit_two, scale_two, norm_gains[1])
    grad_attn = grad_middle.astype(jnp.bfloat16)
    output_grad = jnp.einsum("td,te->de", mixed, grad_attn, preferred_element_type=jnp.float32)
    grad_mixed = jnp.einsum(
        "te,de->td", grad_attn, back_output, preferred_element_type=jnp.float32
    ).astype(jnp.bfloat16)
    grad_heads = grad_mixed.reshape(row_count, HEADS, HEAD_DIM)
    row_delta = jnp.sum(grad_heads.astype(jnp.float32) * exact_heads, axis=-1)
    lse_rows = log_total.T
    zero_bias = jnp.zeros((2, HEADS), jnp.float32)

    def sweep_query(carry, pieces):
        part_query, part_bias = block_grads(
            query,
            query_labels,
            grad_heads,
            lse_rows,
            row_delta,
            pieces[0],
            pieces[1],
            pieces[2],
            variate_bias,
            True,
            False,
        )
        return ((carry[0] + part_query, carry[1] + part_bias), None)

    (query_total, bias_grad), unused = lax.scan(
        sweep_query, (zero_heads, zero_bias), (key_blocks, value_blocks, label_blocks)
    )
    all_query, all_grad = (
        lax.all_gather(query.reshape(row_count, D), "seq", axis=0, tiled=True),
        lax.all_gather(grad_mixed, "seq", axis=0, tiled=True),
    )
    all_lse, all_delta = (
        lax.all_gather(lse_rows, "seq", axis=0, tiled=True),
        lax.all_gather(row_delta, "seq", axis=0, tiled=True),
    )
    key_heads = key_rows.reshape(row_count, HEADS, HEAD_DIM)
    value_heads = value_rows.reshape(row_count, HEADS, HEAD_DIM)
    own_float = own_labels.astype(jnp.float32)

    def sweep_keys(carry, pieces):
        part_key, part_value = block_grads(
            pieces[0],
            pieces[1],
            pieces[2],
            pieces[3],
            pieces[4],
            key_heads,
            value_heads,
            own_float,
            variate_bias,
            False,
            True,
        )
        return ((carry[0] + part_key, carry[1] + part_value), None)

    (key_total, value_heads_total), unused = lax.scan(
        sweep_keys,
        (zero_heads, zero_heads),
        (
            all_query.reshape(blocks, block_rows, HEADS, HEAD_DIM),
            label_blocks,
            all_grad.reshape(blocks, block_rows, HEADS, HEAD_DIM),
            all_lse.reshape(blocks, block_rows, HEADS),
            all_delta.reshape(blocks, block_rows, HEADS),
        ),
    )
    value_total = value_heads_total.reshape(row_count, D)
    grad_query = unrotate(query_total, cos_table, sin_table).reshape(row_count, D)
    grad_key = unrotate(key_total, cos_table, sin_table).reshape(row_count, D)
    grad_project = jnp.stack([grad_query, grad_key, value_total]).astype(jnp.bfloat16)
    attend_grad = jnp.einsum(
        "td,cte->cde", act_one, grad_project, preferred_element_type=jnp.float32
    )
    grad_act_one = jnp.einsum(
        "cte,cde->td", grad_project, back_attend, preferred_element_type=jnp.float32
    )
    attend_share, output_share = (
        lax.psum_scatter(attend_grad, ("seq", "batch"), scatter_dimension=1, tiled=True),
        lax.psum_scatter(output_grad, ("seq", "batch"), scatter_dimension=0, tiled=True),
    )
    grad_input = grad_middle + norm_back(grad_act_one, unit_one, scale_one, norm_gains[0])
    gains_grad = jnp.stack(
        [jnp.sum(grad_act_one * unit_one, axis=0), jnp.sum(grad_act_two * unit_two, axis=0)]
    )
    local_squares = (
        jnp.sum(attend_share * attend_share)
        + jnp.sum(output_share * output_share)
        + jnp.sum(expand_share * expand_share)
        + jnp.sum(reduce_share * reduce_share)
    )
    gains_total, bias_total, square_sum = lax.psum(
        (gains_grad, bias_grad, local_squares), ("seq", "batch")
    )
    grad_norm = jnp.sqrt(
        square_sum + jnp.sum(gains_total * gains_total) + jnp.sum(bias_total * bias_total)
    )
    clip_scale = jnp.minimum(1.0, CLIP_NORM / grad_norm)
    attend_new, attend_first_new, attend_second_new = adam_step(
        attend_weight,
        attend_first,
        attend_second,
        attend_share * clip_scale,
        RATE_ATTEND,
        WEIGHT_DECAY,
    )
    output_new, output_first_new, output_second_new = adam_step(
        output_weight,
        output_first,
        output_second,
        output_share * clip_scale,
        RATE_OUTPUT,
        WEIGHT_DECAY,
    )
    expand_new, expand_first_new, expand_second_new = adam_step(
        expand_weight,
        expand_first,
        expand_second,
        expand_share * clip_scale,
        RATE_EXPAND,
        WEIGHT_DECAY,
    )
    reduce_new, reduce_first_new, reduce_second_new = adam_step(
        reduce_weight,
        reduce_first,
        reduce_second,
        reduce_share * clip_scale,
        RATE_REDUCE,
        WEIGHT_DECAY,
    )
    gains_new, gains_first_new, gains_second_new = adam_step(
        norm_gains, gains_first, gains_second, gains_total * clip_scale, RATE_GAINS, 0.0
    )
    bias_new, bias_first_new, bias_second_new = adam_step(
        variate_bias, bias_first, bias_second, bias_total * clip_scale, RATE_BIAS, 0.0
    )
    input_gradient = (grad_input * count_all * D)[None]
    return (
        output[None],
        loss,
        input_gradient,
        grad_norm,
        attend_new,
        attend_new.astype(jnp.bfloat16),
        attend_first_new,
        attend_second_new,
        output_new,
        output_new.astype(jnp.bfloat16),
        output_first_new,
        output_second_new,
        expand_new,
        expand_new.astype(jnp.bfloat16),
        expand_first_new,
        expand_second_new,
        reduce_new,
        reduce_new.astype(jnp.bfloat16),
        reduce_first_new,
        reduce_second_new,
        gains_new,
        gains_first_new,
        gains_second_new,
        bias_new,
        bias_first_new,
        bias_second_new,
    )


MESH = pl.DeviceIdType.MESH
IN_VMEM = pl.BlockSpec(memory_space=pltpu.VMEM)
IN_SMEM = pl.BlockSpec(memory_space=pltpu.SMEM)
LANES = 128
HEADS_HERE = LANES // HEAD_DIM
VARIATES = 16
MIB = 1 << 20
LOW = jnp.bfloat16
WIDE = jnp.float32
TOTAL_ROWS = 24


def fast_fits(seq, batch):
    return seq == 8 and batch == 4 and seq * LANES == D


def flip(index, mask):
    result, bit = index, 1
    while bit <= mask:
        if mask & bit:
            result = result + bit - 2 * bit * lax.rem(lax.div(index, bit), 2)
        bit *= 2
    return result


def push(source, target, send_sem, recv_sem, device):
    return pltpu.make_async_remote_copy(
        src_ref=source,
        dst_ref=target,
        send_sem=send_sem,
        recv_sem=recv_sem,
        device_id=device,
        device_id_type=MESH,
    )


def block_of(index, size):
    return pl.ds(pl.multiple_of(index * size, size), size)


def dot(left, right):
    return jnp.dot(left, right, preferred_element_type=WIDE)


def dot_turned(left, right):
    return lax.dot_general(left, right, (((1,), (1,)), ((), ())), preferred_element_type=WIDE)


def turned_dot(left, right):
    return lax.dot_general(left, right, (((0,), (0,)), ((), ())), preferred_element_type=WIDE)


class Team:
    def __init__(self, index, place):
        self.index, self.place = index, place

    def at(self, mask):
        return flip(self.index, mask)


def head_team(me, group):
    return Team(me, lambda mask: (flip(me, mask), group))


def feed_team(me, group):
    return Team(
        4 * lax.rem(group, 2) + lax.rem(me, 4),
        lambda mask: (flip(me, mask % 4), flip(group, mask // 4)),
    )


class Gather:
    def __init__(self, team, rows, all_rows, sends, recvs):
        self.team, self.all_rows, self.sends, self.recvs = team, all_rows, sends, recvs
        self.size = all_rows.shape[0] // 8
        self.given = rows
        self.rows = all_rows.at[block_of(team.index, self.size)] if rows is None else rows

    def copy(self, mask, passing):
        source = self.all_rows.at[block_of(self.team.at(mask - 1 if passing else 0), self.size)]
        return push(
            source if passing else self.rows,
            source,
            self.sends.at[mask],
            self.recvs.at[mask],
            self.team.place(1 if passing else mask),
        )

    def start(self):
        for mask in (6, 2, 4, 1):
            self.copy(mask, False).start()
        if self.given is not None:
            self.all_rows[block_of(self.team.index, self.size)] = self.given[...]

    def pass_on(self, chip):
        self.copy(2 * chip, False).wait_recv()
        self.copy(2 * chip + 1, True).start()

    def complete(self, chip):
        self.copy(2 * chip + 1, chip > 0).wait_recv()

    def finish(self):
        for mask in (6, 2, 4, 1):
            self.copy(mask, False).wait_send()
        for mask in (3, 5, 7):
            self.copy(mask, True).wait_send()


def at_step(step, number, *works):
    @pl.when(step == number)
    def _():
        for work in works:
            work()


def each_chip(gather, work, after):
    def one_chip(chip, unused):
        @pl.when(chip == 0)
        def _():
            gather.complete(0)

        @pl.when(chip == 1)
        def _():
            gather.pass_on(1)
            gather.pass_on(2)
            gather.complete(1)

        @pl.when(chip == 2)
        def _():
            gather.pass_on(3)
            gather.complete(2)

        @pl.when(chip == 3)
        def _():
            gather.complete(3)

        work(chip)
        for number, works in after.items():
            at_step(chip, number, *works)
        return unused

    lax.fori_loop(0, 4, one_chip, 0)
    gather.finish()


class Scatter:
    def __init__(self, team, buffers, near_sends, near_recvs, far_sends, far_recvs):
        self.whole, self.keep, self.near_from, self.near, self.far_from, self.far = buffers
        self.sems = near_sends, near_recvs, far_sends, far_recvs
        self.team = team
        self.size = self.keep.shape[1]

    def near_copy(self, chip):
        return push(
            self.near_from.at[chip],
            self.near.at[chip],
            self.sems[0].at[chip],
            self.sems[1].at[chip],
            self.team.place(1),
        )

    def far_copy(self, chip):
        return push(
            self.far_from.at[chip],
            self.far.at[chip],
            self.sems[2].at[chip],
            self.sems[3].at[chip],
            self.team.place(2 * chip),
        )

    def put(self, chip, rows):
        core = lax.rem(self.team.index, 2)
        self.whole[...] = rows
        self.near_from[chip] = self.whole[block_of(1 - core, self.size)].astype(LOW)
        self.near_copy(chip).start()
        self.keep[chip] = self.whole[block_of(core, self.size)]

    def combine(self, chip):
        self.near_copy(chip).wait_recv()
        self.far_from[chip] = (self.keep[chip] + self.near[chip].astype(WIDE)).astype(LOW)
        self.far_copy(chip).start()

    def total(self):
        self.near_copy(0).wait_recv()
        total = self.keep[0] + self.near[0].astype(WIDE)
        for chip in (1, 2, 3):
            self.far_copy(chip).wait_recv()
            total = total + self.far[chip].astype(WIDE)
        for chip in (0, 1, 2, 3):
            self.near_copy(chip).wait_send()
            if chip:
                self.far_copy(chip).wait_send()
        return total


class LineGather:
    def __init__(self, part_of, sends, recvs, me, group):
        self.part_of, self.sends, self.recvs, self.me, self.group = part_of, sends, recvs, me, group
        self.middle = jnp.logical_and(group >= 1, group <= 2)

    def copy(self, part, target, slot):
        return push(
            self.part_of(part),
            self.part_of(part),
            self.sends.at[slot],
            self.recvs.at[part],
            (self.me, target),
        )

    def start(self):
        group = self.group

        @pl.when(self.middle)
        def _():
            self.copy(group, 3 - group, 3 - group).start()
            self.copy(group, 3 * (group - 1), 3 * (group - 1)).start()

        @pl.when(jnp.logical_not(self.middle))
        def _():
            for step in (2, 1, 3):
                other = lax.rem(group + step, 4)
                self.copy(group, other, other).start()

    def pass_on(self):
        group = self.group

        @pl.when(self.middle)
        def _():
            self.copy(3 - group, 3 * (group - 1), group).wait_recv()
            self.copy(3 - group, 3 * (group - 1), group).start()

    def land(self):
        group = self.group

        @pl.when(self.middle)
        def _():
            for part in (0, 3):
                self.copy(part, 3 - group, group).wait_recv()

        @pl.when(jnp.logical_not(self.middle))
        def _():
            for step in (1, 2, 3):
                other = lax.rem(group + step, 4)
                self.copy(other, other, other).wait_recv()

    def finish(self):
        group = self.group

        @pl.when(self.middle)
        def _():
            for other in (3 - group, 3 * (group - 1), group):
                self.copy(group, 3 - group, other).wait_send()

        @pl.when(jnp.logical_not(self.middle))
        def _():
            for step in (1, 2, 3):
                other = lax.rem(group + step, 4)
                self.copy(group, other, other).wait_send()


class LineScatter:
    def __init__(self, part_of, landing, sends, recvs, me, group):
        self.part_of, self.landing, self.sends, self.recvs = part_of, landing, sends, recvs
        self.me, self.group = me, group
        self.middle = jnp.logical_and(group >= 1, group <= 2)
        self.opposite = 3 - 3 * lax.div(group, 2)

    def copy(self, part, slot, target, sem):
        return push(
            self.part_of(part),
            self.landing.at[slot],
            self.sends.at[sem],
            self.recvs.at[slot],
            (self.me, target),
        )

    def start(self):
        group = self.group

        @pl.when(self.middle)
        def _():
            for other in (3 - group, 3 * (group - 1)):
                self.copy(other, group, other, other).start()

        @pl.when(jnp.logical_not(self.middle))
        def _():
            beside = 1 + lax.div(group, 3)
            self.copy(3 - group, beside, beside, 3 - group).start()
            for other in (3 - beside, beside):
                self.copy(other, group, other, other).start()

    def pass_on(self):
        group, opposite = self.group, self.opposite

        @pl.when(self.middle)
        def _():
            self.copy(opposite, group, opposite, group).wait_recv()
            part = self.part_of(opposite)
            part[...] = (part[...].astype(WIDE) + self.landing[group].astype(WIDE)).astype(LOW)
            self.copy(opposite, group, opposite, group).start()

    def land(self):
        group = self.group

        @pl.when(self.middle)
        def _():
            for slot in (0, 3 - group, 3):
                self.copy(group, slot, 3 - group, group).wait_recv()

        @pl.when(jnp.logical_not(self.middle))
        def _():
            for slot in (1, 2):
                self.copy(group, slot, slot, group).wait_recv()

    def add(self, own, landed, store):
        group = self.group

        @pl.when(self.middle)
        def _():
            store(own() + landed(0) + landed(3 - group) + landed(3))

        @pl.when(jnp.logical_not(self.middle))
        def _():
            store(own() + landed(1) + landed(2))

    def finish(self):
        group = self.group

        @pl.when(self.middle)
        def _():
            for sem in (3 - group, 3 * (group - 1), group):
                self.copy(group, group, 3 - group, sem).wait_send()

        @pl.when(jnp.logical_not(self.middle))
        def _():
            for sem in (3 - group, 1, 2):
                self.copy(group, group, 1, sem).wait_send()


class QuadGather:
    def __init__(self, part_of, sends, recvs, me, group):
        self.part_of, self.sends, self.recvs = part_of, sends, recvs
        self.part = 2 * lax.div(me, 4) + lax.div(group, 2)
        self.along_y, self.along_z = (flip(me, 4), group), (me, flip(group, 2))

    def copy(self, way):
        part = self.part_of(flip(self.part, 1) if way == 3 else self.part)
        device = self.along_z if way == 1 else self.along_y
        return push(part, part, self.sends.at[way], self.recvs.at[way], device)

    def start_y(self):
        self.copy(2).start()

    def start_z(self):
        self.copy(1).start()

    def pass_on(self):
        self.copy(1).wait_recv()
        self.copy(3).start()

    def land(self):
        self.copy(2).wait_recv()
        self.copy(3).wait_recv()

    def finish(self):
        for way in (1, 2, 3):
            self.copy(way).wait_send()


class QuadScatter:
    def __init__(self, part_of, landing, sends, recvs, me, group):
        self.part_of, self.landing, self.sends, self.recvs = part_of, landing, sends, recvs
        self.part = 2 * lax.div(me, 4) + lax.div(group, 2)
        self.along_y, self.along_z = (flip(me, 4), group), (me, flip(group, 2))

    def copy(self, slot):
        return push(
            self.part_of(flip(self.part, (2, 3, 1)[slot])),
            self.landing.at[slot],
            self.sends.at[slot],
            self.recvs.at[slot],
            self.along_z if slot == 2 else self.along_y,
        )

    def start_far(self):
        self.copy(1).start()

    def start_near(self):
        self.copy(0).start()

    def pass_on(self):
        self.copy(1).wait_recv()
        part = self.part_of(flip(self.part, 1))
        part[...] = (part[...].astype(WIDE) + self.landing[1].astype(WIDE)).astype(LOW)
        self.copy(2).start()

    def land(self):
        self.copy(0).wait_recv()
        self.copy(2).wait_recv()

    def finish(self):
        for slot in (0, 1, 2):
            self.copy(slot).wait_send()


def chip_of(team, chip):
    here = lax.div(team.index, 2)
    if isinstance(chip, int):
        return flip(here, chip)
    column = lax.rem(lax.rem(here, 2) + lax.rem(chip, 2), 2)
    row = lax.rem(lax.div(here, 2) + lax.div(chip, 2), 2)
    return 2 * row + column


def turn_rows(values, cosine, sine):
    half = HEAD_DIM // 2
    pieces = []
    for start in range(0, values.shape[0], HEAD_DIM):
        first, second = values[start : start + half], values[start + half : start + HEAD_DIM]
        pieces += [first * cosine - second * sine, second * cosine + first * sine]
    return jnp.concatenate(pieces, axis=0)


def thirds(values):
    first = values.astype(LOW).astype(WIDE)
    second = (values - first).astype(LOW).astype(WIDE)
    return first, second, values - first - second


def pick(row, choices):
    result = jnp.zeros(row.shape, WIDE)
    for number, choice in choices.items():
        result = jnp.where(row == number, choice, result)
    return result


def norm_rows(values):
    scale = lax.rsqrt(jnp.mean(values * values, axis=-1, keepdims=True) + NORM_EPS)
    return values * scale, scale


def feed_block(block):
    y, x, core, far_z, near_z = (block // 16, block // 8 % 2, block // 4 % 2, block // 2 % 2, block % 2)
    return 4 * near_z + 2 * x + core, 2 * y + far_z


def layer_kernel(seq, batch, ins, outs, mem):
    me, group = lax.axis_index("seq"), lax.axis_index("batch")
    rows = ins.inputs.shape[0]
    length = rows * seq
    pair = 2 * rows
    share = ins.attend.shape[1]
    wide_columns = ins.expand.shape[2] // D
    hidden_width = mem.reduce_all.shape[0] * mem.reduce_all.shape[1]
    blocks = ins.expand.shape[2] // LANES
    heads, feeds = head_team(me, group), feed_team(me, group)
    quad = 2 * lax.div(me, 4) + lax.div(group, 2)

    staged = [(ins.attend.at[which], mem.keep.at[0, block_of(which, share)]) for which in range(3)]
    staged.append((ins.output, mem.keep.at[0, block_of(3, share)]))
    staged.append((ins.reduce, mem.keep.at[1]))
    for which in range(2):
        for block in range(wide_columns):
            columns = slice(block * D, (block + 1) * D)
            staged.append(
                (ins.expand.at[which, :, columns], mem.keep.at[2 + which, block_of(block, share)])
            )
    staged = [
        pltpu.make_async_copy(source, target, mem.stage_sem.at[number])
        for number, (source, target) in enumerate(staged)
    ]
    for copy in staged:
        copy.start()
    barrier = pltpu.get_barrier_semaphore()
    for mask in range(1, seq):
        pl.semaphore_signal(barrier, inc=1, device_id=(flip(me, mask), group), device_id_type=MESH)
    for step in range(1, batch):
        pl.semaphore_signal(
            barrier, inc=1, device_id=(me, lax.rem(group + step, batch)), device_id_type=MESH
        )
    for mask in (5, 6, 7):
        pl.semaphore_signal(barrier, inc=1, device_id=feeds.place(mask), device_id_type=MESH)

    unit_one, scale_one = norm_rows(ins.inputs[...].astype(WIDE))
    mem.own_rows[0] = (unit_one * ins.gains[0:1, :]).astype(LOW)
    for copy in staged:
        copy.wait()
    for which in range(3):
        mem.attend_low[which] = mem.keep[0, block_of(which, share)].astype(LOW)
    mem.output_full[block_of(batch * me + group, share)] = mem.keep[0, block_of(3, share)].astype(LOW)
    mem.reduce_all[quad] = mem.keep[1].astype(LOW)
    for which in range(2):
        for block in range(blocks):
            owner, part = feed_block(block)
            row, lane = divmod(block * LANES, D)
            mem.expand_low[which, owner, :, part * LANES : (part + 1) * LANES] = mem.keep[
                2 + which, block_of(row, share), lane : lane + LANES
            ].astype(LOW)
    pl.semaphore_wait(barrier, seq + batch + 1)

    masks = (6, 7, 4, 5, 2, 3, 1)

    def start_attend_columns():
        copies = []
        for mask in masks:
            copy = push(
                mem.attend_low.at[:, :, block_of(heads.at(mask), LANES)],
                mem.attend_all.at[:, me, group],
                mem.column_send.at[0, mask],
                mem.column_recv.at[0, mask],
                heads.place(mask),
            )
            copy.start()
            copies.append(copy)
        mem.attend_all[:, me, group] = mem.attend_low[:, :, block_of(me, LANES)]
        return copies

    def start_expand_columns():
        copies = []
        for mask in masks:
            copy = push(
                mem.expand_low.at[:, feeds.at(mask)],
                mem.expand_all.at[:, me, group],
                mem.column_send.at[1, mask],
                mem.column_recv.at[1, mask],
                feeds.place(mask),
            )
            copy.start()
            copies.append(copy)
        mem.expand_all[:, me, group] = mem.expand_low[:, feeds.index]
        return copies

    def expand_part_of(array, which):
        def part_of(part):
            return array.at[which, pl.ds(4 * lax.div(part, 2), 4), pl.ds(2 * lax.rem(part, 2), 2)]

        return part_of

    def line_gather(row, part_of):
        return LineGather(part_of, mem.line_send.at[row], mem.line_recv.at[row], me, group)

    def quad_gather(row, part_of):
        return QuadGather(part_of, mem.line_send.at[row], mem.line_recv.at[row], me, group)

    def gather(team, phase, all_rows):
        return Gather(
            team,
            mem.own_rows.at[phase],
            all_rows,
            mem.gather_send.at[phase],
            mem.gather_recv.at[phase],
        )

    def scatter(team, phase):
        return Scatter(
            team,
            (mem.whole, mem.keep, mem.near_from, mem.near, mem.far_from, mem.far),
            mem.near_send.at[phase],
            mem.near_recv.at[phase],
            mem.far_send.at[phase],
            mem.far_recv.at[phase],
        )

    attend_columns = start_attend_columns()
    line_output = line_gather(1, lambda part: mem.output_full.at[block_of(batch * me + part, share)])
    line_output.start()
    facts = Gather(heads, ins.facts, mem.facts_all, mem.facts_send, mem.facts_recv)
    facts.start()
    for copy in attend_columns:
        copy.wait_recv()
    line_attend = line_gather(0, lambda part: mem.attend_all.at[:, :, part])
    line_attend.start()
    acts = gather(heads, 0, mem.act_one)
    acts.start()
    for chip in (1, 2, 3):
        facts.pass_on(chip)
    for chip in (0, 1, 2, 3):
        facts.complete(chip)
    facts.finish()
    step_rows = ins.facts.shape[0]
    half = HEAD_DIM // 2
    count = jnp.zeros((8, LANES), WIDE)
    for slot in range(seq):
        columns = slice(slot * rows, (slot + 1) * rows)
        start = slot * step_rows
        mem.cosine[:, columns] = mem.facts_all[start : start + half]
        mem.sine[:, columns] = mem.facts_all[start + half : start + 2 * half]
        labels = mem.facts_all[start + 2 * half : start + 2 * half + 8]
        mem.labels[:, columns] = labels
        count = count + labels
    mem.count[group] = count
    count_copies = []
    for step in range(1, batch):
        copy = push(
            mem.count.at[group],
            mem.count.at[group],
            mem.count_send.at[step],
            mem.count_recv.at[step],
            (me, lax.rem(group + step, batch)),
        )
        copy.start()
        count_copies.append(copy)

    def mark(block, unused):
        span = block_of(block, pair)
        row = lax.broadcasted_iota(jnp.int32, (HEAD_DIM, pair), 0)
        third = lax.div(row, VARIATES)
        variate = lax.rem(row, VARIATES).astype(WIDE)
        key_label, query_label = mem.labels[0:1, span], mem.labels[1:2, span]
        ones = jnp.ones((1, pair), WIDE)
        last = 3 * VARIATES
        hidden_keys = (key_label < 0.0).astype(WIDE)
        mem.key_marks[:, span] = jnp.where(
            third < 3,
            (key_label == variate).astype(WIDE),
            pick(row, {last: ones, last + 1: ones, last + 2: ones, last + 3: hidden_keys}),
        ).astype(LOW)
        query_marks = (query_label == variate).astype(WIDE)
        mem.sum_marks[:, span] = jnp.where(
            row < VARIATES, query_marks, pick(row, {VARIATES: ones})
        ).astype(LOW)
        for head in range(HEADS_HERE):
            number = me * HEADS_HERE + head
            other = jnp.full((HEAD_DIM, pair), ins.bias[1, number], WIDE)
            more = thirds(jnp.full((HEAD_DIM, pair), ins.bias[0, number], WIDE) - other)
            other = thirds(other)
            mem.query_turned[head, HEAD_DIM:, span] = jnp.where(
                third < 3,
                query_marks * jnp.where(third == 0, more[0], jnp.where(third == 1, more[1], more[2])),
                pick(row, {last: other[0], last + 1: other[1], last + 2: other[2], last + 3: MASKED}),
            ).astype(LOW)
        return unused

    lax.fori_loop(0, length // pair, mark, 0)
    acts.pass_on(1)
    acts.pass_on(2)
    line_output.pass_on()
    line_output.land()
    outputs = Gather(heads, None, mem.output_full, mem.output_send, mem.output_recv)
    outputs.start()
    acts.pass_on(3)
    line_attend.pass_on()
    for chip in range(4):
        acts.complete(chip)
    acts.finish()
    line_attend.land()

    expand_columns = start_expand_columns()
    line_reduce = quad_gather(4, lambda part: mem.reduce_all.at[part])
    line_reduce.start_z()
    line_reduce.start_y()
    line_expand = [
        quad_gather(2 + which, expand_part_of(mem.expand_all, which)) for which in range(2)
    ]

    def attend_matrix(which):
        return mem.attend_all[which].reshape(D, LANES)

    def project(block, unused):
        span = block_of(block, pair)
        act = mem.act_one[span, :]
        cosine, sine = mem.cosine[:, span], mem.sine[:, span]
        query = turn_rows(dot(act, attend_matrix(0)).T, cosine, sine).astype(LOW)
        query = (query.astype(WIDE) * HEAD_DIM ** (-0.5)).astype(LOW)
        key = turn_rows(dot(act, attend_matrix(1)).T, cosine, sine).astype(LOW)
        value = dot(act, attend_matrix(2)).T.astype(LOW)
        mem.key_turned[:, span] = key
        mem.value_turned[:, span] = value

        for head in range(HEADS_HERE):
            features = slice(head * HEAD_DIM, (head + 1) * HEAD_DIM)
            mem.query_turned[head, :HEAD_DIM, span] = query[features]
            whole = jnp.concatenate([key[features], mem.key_marks[:, span]], axis=0)
            mem.key_heads[head, span, :] = whole.T
        return unused

    lax.fori_loop(0, length // pair, project, 0)
    outputs.pass_on(1)
    outputs.pass_on(2)
    for copy in expand_columns:
        copy.wait_recv()
    line_expand[0].start_z()
    line_expand[0].start_y()

    core = lax.rem(me, 2)

    def mixed_copy(chip, which):
        other = 2 * chip_of(heads, chip) + which
        slot = 2 * chip + lax.rem(which + core, 2)
        return push(
            mem.mixed_out.at[block_of(other, rows)],
            mem.mixed_rows.at[:, block_of(me, LANES)],
            mem.mixed_send.at[slot],
            mem.mixed_recv.at[slot],
            (other, group),
        )

    def attend_block(chip):
        columns = block_of(chip_of(heads, chip), pair)
        for head in range(HEADS_HERE):
            span = slice(head * HEAD_DIM, (head + 1) * HEAD_DIM)
            scores = dot(mem.key_heads[head], mem.query_turned[head, :, columns])
            top = jnp.floor(jnp.max(scores, axis=0, keepdims=True))
            powers = jnp.exp(scores - top)
            probs = powers * (1.0 / jnp.sum(powers, axis=0, keepdims=True))
            rounded = probs.astype(LOW)
            mem.probs[head, :, columns] = rounded
            residue = (probs - rounded.astype(WIDE)).astype(LOW)
            coarse = dot(mem.value_turned[span, :], rounded)
            mem.exact[span, columns] = coarse + dot(mem.value_turned[span, :], residue)
            mem.mixed_wide[span, :] = coarse
        mixed = mem.mixed_wide[...].astype(LOW)
        mem.mixed_turned[:, columns] = mixed
        mem.mixed_out[columns, :] = mixed.T

    def attend_step(step, unused):
        chip = lax.rem(step + 1, 4)
        attend_block(chip)
        for which in range(2):

            @pl.when(jnp.logical_or(chip > 0, core != which))
            def _():
                mixed_copy(chip, which).start()

        at_step(step, 1, lambda: outputs.pass_on(3))
        return unused

    lax.fori_loop(0, 4, attend_step, 0)
    line_expand[1].start_z()
    line_expand[1].start_y()
    mem.mixed_rows[:, block_of(me, LANES)] = mem.mixed_out[block_of(me, rows), :]
    for chip in range(4):
        outputs.complete(chip)
    outputs.finish()

    def wait_pieces(copy):
        for mask in range(1, seq):
            copy(mask).wait()

    def mixed_wait(mask):
        other = heads.at(mask)
        return push(
            mem.mixed_out.at[block_of(other, rows)],
            mem.mixed_rows.at[:, block_of(other, LANES)],
            mem.mixed_send.at[mask],
            mem.mixed_recv.at[mask],
            (other, group),
        )

    wait_pieces(mixed_wait)
    middle = ins.inputs[...].astype(WIDE) + dot(mem.mixed_rows[...], mem.output_full[...])
    mem.middle[...] = middle
    unit_two, scale_two = norm_rows(middle)
    mem.own_rows[1] = (unit_two * ins.gains[1:2, :]).astype(LOW)
    acts = gather(feeds, 1, mem.act_two)
    acts.start()
    line_reduce.pass_on()
    line_expand[0].pass_on()

    def split_heads(block, unused):
        span = block_of(block, pair)
        row = lax.broadcasted_iota(jnp.int32, (HEAD_DIM, pair), 0)
        value_marks = jnp.where(row < 3, 1.0, 0.0).astype(LOW)
        for head in range(HEADS_HERE):
            features = slice(head * HEAD_DIM, (head + 1) * HEAD_DIM)
            value = mem.value_turned[features, span]
            mem.value_heads[head, span, :] = jnp.concatenate([value, value_marks], axis=0).T
            query = mem.query_turned[head, :HEAD_DIM, span]
            whole = jnp.concatenate([query, mem.sum_marks[:, span]], axis=0)
            mem.query_heads[head, span, :] = whole.T
        return unused

    lax.fori_loop(0, length // pair, split_heads, 0)
    line_expand[0].land()

    def expand_matrix(which):
        return mem.expand_all[which].reshape(D, hidden_width)

    def reduce_matrix():
        return mem.reduce_all[...].reshape(hidden_width, D)

    def feed_gate(chip):
        span = block_of(chip_of(feeds, chip), pair)
        mem.by_gate[span, :] = dot(mem.act_two[span, :], expand_matrix(0))

    each_chip(acts, feed_gate, {2: [line_expand[1].pass_on]})
    line_expand[1].land()
    line_reduce.land()
    sums = scatter(feeds, 1)

    def feed_down(step, unused):
        chip = lax.rem(step + 1, 4)
        span = block_of(chip_of(feeds, chip), pair)
        gate = mem.by_gate[span, :]
        up = dot(mem.act_two[span, :], expand_matrix(1))
        sigmoid = 1.0 / (1.0 + jnp.exp(-gate))
        swish = gate * sigmoid
        mem.by_up[span, :] = swish
        mem.by_gate[span, :] = up * sigmoid * (1.0 + gate * (1.0 - sigmoid))
        hidden = (swish * up).astype(LOW)
        mem.hidden[span, :] = hidden
        sums.put(chip, dot(hidden, reduce_matrix()))
        at_step(step, 1, lambda: sums.combine(1))
        at_step(step, 2, lambda: sums.combine(2))
        return unused

    lax.fori_loop(0, 4, feed_down, 0)
    sums.combine(3)

    for block in range(length // pair):
        span = block_of(block, pair)
        mem.hidden_turned[:, span] = mem.hidden[span, :].T
        mem.act_two_turned[:, span] = mem.act_two[span, :].T
    output = mem.middle[...] + sums.total()
    outs.layer_output[...] = output
    for copy in count_copies:
        copy.wait()
    count_all = jnp.sum(
        mem.count[0, 2:3] + mem.count[1, 2:3] + mem.count[2, 2:3] + mem.count[3, 2:3],
        axis=1,
        keepdims=True,
    )
    error = jnp.where(ins.scored[...] > 0.0, output - ins.teacher[...].astype(WIDE), 0.0)
    mem.squares[1:2, :] = jnp.sum(error * error, axis=0, keepdims=True)
    grad_out = error * (2.0 / (count_all * D))
    mem.grad_own[...] = grad_out
    mem.own_rows[2] = grad_out.astype(LOW)
    acts = gather(feeds, 2, mem.branch)
    acts.start()

    sums = scatter(feeds, 2)

    def feed_back(chip):
        span = block_of(chip_of(feeds, chip), pair)
        grad_hidden = dot_turned(mem.branch[span, :], reduce_matrix())
        grad_gate = (grad_hidden * mem.by_gate[span, :]).astype(LOW)
        grad_up = (grad_hidden * mem.by_up[span, :]).astype(LOW)
        mem.grad_gate[span, :] = grad_gate
        mem.grad_up[span, :] = grad_up
        sums.put(
            chip,
            dot_turned(grad_gate, expand_matrix(0)) + dot_turned(grad_up, expand_matrix(1)),
        )

    each_chip(
        acts, feed_back, {2: [lambda: sums.combine(1)], 3: [lambda: sums.combine(2)]}
    )
    sums.combine(3)

    def line_scatter(row, part_of, landing):
        return LineScatter(
            part_of, landing, mem.back_send.at[row], mem.back_recv.at[row], me, group
        )

    def quad_scatter(row, part_of, landing):
        return QuadScatter(
            part_of, landing, mem.back_send.at[row], mem.back_recv.at[row], me, group
        )

    def reduce_grad(part, unused):
        mem.reduce_grad[part] = dot(
            mem.hidden_turned[block_of(part, rows), :], mem.branch[...]
        ).astype(LOW)
        return unused

    lax.fori_loop(0, batch, reduce_grad, 0)
    back_reduce = quad_scatter(0, lambda part: mem.reduce_grad.at[part], mem.reduce_land)
    back_reduce.start_far()

    def expand_grad(which):
        grads = (mem.grad_gate, mem.grad_up)[which]

        def one_block(block, unused):
            products = dot(mem.act_two_turned[block_of(block, pair), :], grads[...]).astype(LOW)
            mem.expand_grad[which, pl.ds(2 * block, 2)] = products.reshape(
                2, batch, share, hidden_width
            )
            return unused

        lax.fori_loop(0, seq // 2, one_block, 0)
        line = quad_scatter(
            1 + which, expand_part_of(mem.expand_grad, which), mem.expand_land.at[which]
        )
        return line

    back_expand = []
    for which in range(2):
        back_expand.append(expand_grad(which))
        back_expand[which].start_far()
    grad_act = sums.total()
    unit_two, scale_two = norm_rows(mem.middle[...])
    gain = ins.gains[1:2, :]
    grad_unit = grad_act * gain
    mem.gains[1:2, :] = jnp.sum(grad_act * unit_two, axis=0, keepdims=True)
    grad_middle = mem.grad_own[...] + scale_two * (
        grad_unit - unit_two * jnp.mean(grad_unit * unit_two, axis=-1, keepdims=True)
    )
    mem.grad_own[...] = grad_middle
    mem.own_rows[3] = grad_middle.astype(LOW)
    grad_mixed = dot(mem.output_full[...], grad_middle.T.astype(LOW)).astype(LOW)
    mem.grad_mixed_out[...] = grad_mixed.reshape(seq, LANES, rows)

    def grad_copy(mask, back=False):
        return push(
            mem.grad_mixed_out.at[heads.at(mask)],
            mem.grad_mixed.at[:, block_of(heads.at(mask) if back else me, rows)],
            mem.mixed_send.at[8 + mask],
            mem.mixed_recv.at[8 + mask],
            heads.place(mask),
        )

    for mask in masks:
        grad_copy(mask).start()
    mem.grad_mixed[:, block_of(me, rows)] = mem.grad_mixed_out[me]
    back_reduce.pass_on()

    wait_pieces(lambda mask: grad_copy(mask, True))
    acts = gather(heads, 3, mem.grad_attn)
    acts.start()
    back_reduce.start_near()
    back_expand[0].start_near()
    back_expand[0].pass_on()
    back_attend = [
        line_scatter(
            4 + which,
            lambda part, which=which: mem.attend_grad.at[which, :, part],
            mem.attend_land.at[which],
        )
        for which in range(3)
    ]

    def attend_grad(which):
        grads = dot(mem.grad_project[which], mem.act_one[...])
        mem.attend_grad[which] = grads.T.astype(LOW).reshape(seq, batch, share, LANES)
        back_attend[which].start()

    lane = lax.broadcasted_iota(jnp.int32, (pair, LANES), 1)

    def grad_rows(block, unused):
        span = block_of(block, pair)
        whole = mem.grad_mixed[:, span].astype(WIDE).T
        for head in range(HEADS_HERE):
            mem.grad_heads[head, span, :] = jnp.where(lax.div(lane, HEAD_DIM) == head, whole, 0.0).astype(LOW)
        return unused

    lax.fori_loop(0, length // pair, grad_rows, 0)

    def value_back(block, unused):
        span = block_of(block, pair)
        total = dot(mem.probs[0, span, :], mem.grad_heads[0])
        for head in range(1, HEADS_HERE):
            total = total + dot(mem.probs[head, span, :], mem.grad_heads[head])
        mem.grad_project[2, :, span] = total.T.astype(LOW)
        return unused

    lax.fori_loop(0, length // pair, value_back, 0)
    attend_grad(2)

    def score_back(block, unused):
        columns = block_of(block, pair)
        row = lax.broadcasted_iota(jnp.int32, (HEAD_DIM, pair), 0)
        grads = mem.grad_mixed[:, columns]
        delta = grads.astype(WIDE) * mem.exact[:, columns]
        for head in range(HEADS_HERE):
            span = slice(head * HEAD_DIM, (head + 1) * HEAD_DIM)
            pieces = thirds(-jnp.sum(delta[span], axis=0, keepdims=True))
            marks = pick(row, dict(enumerate(pieces))).astype(LOW)
            change = dot(mem.value_heads[head], jnp.concatenate([grads[span], marks], axis=0))
            mem.probs[head, :, columns] = (mem.probs[head, :, columns].astype(WIDE) * change).astype(LOW)
        return unused

    lax.fori_loop(0, length // pair, score_back, 0)
    back_expand[1].start_near()
    back_expand[1].pass_on()
    mem.bias_sums[...] = jnp.zeros_like(mem.bias_sums)
    scale = HEAD_DIM ** (-0.5)

    def project_grads(block, unused):
        span = block_of(block, pair)
        cosine, sine = mem.cosine[:, span], -mem.sine[:, span]
        queries, keys = [], []
        for head in range(HEADS_HERE):
            features = slice(head * HEAD_DIM, (head + 1) * HEAD_DIM)
            queries.append(dot(mem.key_turned[features, :], mem.probs[head, :, span]) * scale)
            sums = dot(mem.probs[head, span, :], mem.query_heads[head]).T
            keys.append(sums[:HEAD_DIM])
            by_variate = sums[HEAD_DIM : HEAD_DIM + VARIATES]
            same = by_variate * mem.key_marks[:VARIATES, span].astype(WIDE)
            mem.bias_sums[head : head + 1, :] += jnp.sum(same, axis=0, keepdims=True)
            total = sums[HEAD_DIM + VARIATES : HEAD_DIM + VARIATES + 1]
            mem.bias_sums[HEADS_HERE + head : HEADS_HERE + head + 1, :] += total
        mem.grad_project[0, :, span] = turn_rows(jnp.concatenate(queries, axis=0), cosine, sine).astype(LOW)
        mem.grad_project[1, :, span] = turn_rows(jnp.concatenate(keys, axis=0), cosine, sine).astype(LOW)
        return unused

    lax.fori_loop(0, length // pair, project_grads, 0)
    for which in range(2):
        attend_grad(which)
    acts.pass_on(1)
    acts.pass_on(2)
    sums = scatter(heads, 3)

    def project_back(step, unused):
        chip = lax.rem(step + 1, 4)
        span = block_of(chip_of(heads, chip), pair)
        total = jnp.zeros((pair, D), WIDE)
        for which in range(3):
            total = total + dot_turned(mem.grad_project[which, :, span].T, attend_matrix(which))
        sums.put(chip, total)
        at_step(step, 1, lambda: sums.combine(1))
        at_step(step, 2, lambda: sums.combine(2))
        return unused

    lax.fori_loop(0, 4, project_back, 0)
    sums.combine(3)
    acts.pass_on(3)
    for chip in range(4):
        acts.complete(chip)
    acts.finish()
    mem.output_grad[...] = (
        dot(mem.mixed_turned[...], mem.grad_attn[...]).astype(LOW).reshape(mem.output_grad.shape)
    )
    back_output = line_scatter(3, lambda part: mem.output_grad.at[part], mem.output_land)
    back_output.start()
    for which in (2, 0, 1):
        back_attend[which].pass_on()

    column_copies = []
    mem.squares[0:1, :] = jnp.zeros((1, D), WIDE)

    def add_squares(total):
        flat = total.reshape(-1, total.shape[-1])
        width = flat.shape[1]
        mem.squares[0:1, :width] += jnp.sum(flat * flat, axis=0, keepdims=True)

    def store_whole(total, out):
        out[...] = total
        add_squares(total)

    back_reduce.land()
    store_whole(
        mem.reduce_grad[quad].astype(WIDE)
        + mem.reduce_land[0].astype(WIDE)
        + mem.reduce_land[2].astype(WIDE),
        outs.reduce_share,
    )
    grad_act = sums.total()
    unit_one, scale_one = norm_rows(ins.inputs[...].astype(WIDE))
    gain = ins.gains[0:1, :]
    grad_unit = grad_act * gain
    mem.gains[0:1, :] = jnp.sum(grad_act * unit_one, axis=0, keepdims=True)
    grad_input = mem.grad_own[...] + scale_one * (
        grad_unit - unit_one * jnp.mean(grad_unit * unit_one, axis=-1, keepdims=True)
    )
    outs.input_gradient[...] = grad_input * (count_all * D)
    outs.count[...] = jnp.broadcast_to(count_all, (8, LANES))
    back_output.pass_on()

    def expand_shares(which):
        back_expand[which].land()
        own = expand_part_of(mem.expand_grad, which)(quad)

        def one_block(block, unused):
            total = (
                own[block].astype(WIDE)
                + mem.expand_land[which, 0, block].astype(WIDE)
                + mem.expand_land[which, 2, block].astype(WIDE)
            )
            mem.expand_part[which, block] = total.astype(LOW)
            add_squares(total)
            return unused

        lax.fori_loop(0, 4, one_block, 0)
        for mask in masks:
            other = feeds.at(mask)
            copy = push(
                mem.expand_part.at[which, lax.rem(other, 4), lax.div(other, 4)],
                mem.expand_share.at[which, feeds.index],
                mem.share_send.at[which, mask],
                mem.share_recv.at[which, mask],
                feeds.place(mask),
            )
            copy.start()
            column_copies.append(copy)
        mem.expand_share[which, feeds.index] = mem.expand_part[
            which, lax.rem(feeds.index, 4), lax.div(feeds.index, 4)
        ]

    for which in range(2):
        expand_shares(which)
    back_output.land()
    back_output.add(
        lambda: mem.output_grad[group].astype(WIDE),
        lambda slot: mem.output_land[slot].astype(WIDE),
        lambda total: store_whole(total, outs.output_share),
    )

    def attend_shares(which):
        def store(total):
            mem.attend_part[which] = total.astype(LOW)
            add_squares(total)

        back_attend[which].land()
        back_attend[which].add(
            lambda: mem.attend_grad[which, :, group].astype(WIDE),
            lambda slot: mem.attend_land[which, slot].astype(WIDE),
            store,
        )

    for which in (2, 0, 1):
        attend_shares(which)
    for mask in masks:
        copy = push(
            mem.attend_part.at[:, heads.at(mask)],
            outs.attend_share.at[:, :, block_of(me, LANES)],
            mem.share_send.at[2, mask],
            mem.share_recv.at[2, mask],
            heads.place(mask),
        )
        copy.start()
        column_copies.append(copy)
    outs.attend_share[:, :, block_of(me, LANES)] = mem.attend_part[:, me]

    lane = lax.broadcasted_iota(jnp.int32, (1, LANES), 1)
    lines = [
        mem.gains[which : which + 1, start : start + LANES]
        for which in range(2)
        for start in range(0, D, LANES)
    ]
    bias_line = jnp.zeros((1, LANES), WIDE)
    for row in range(2 * HEADS_HERE):
        place = row // HEADS_HERE * HEADS + me * HEADS_HERE + row % HEADS_HERE
        line = mem.bias_sums[row : row + 1, :]
        if row >= HEADS_HERE:
            line = line - mem.bias_sums[row - HEADS_HERE : row - HEADS_HERE + 1, :]
        amount = jnp.sum(line, axis=1, keepdims=True)
        bias_line = bias_line + jnp.where(lane == place, amount, 0.0)
    amounts = jnp.sum(mem.squares[0:2, :], axis=1, keepdims=True)
    amount_line = jnp.where(lane == 0, amounts[0:1], 0.0) + jnp.where(lane == 1, amounts[1:2], 0.0)
    lines += [bias_line, amount_line, jnp.zeros((6, LANES), WIDE)]
    mem.plane_totals[me] = jnp.concatenate(lines, axis=0)
    plane_copies = []
    for mask in masks:
        copy = push(
            mem.plane_totals.at[me],
            mem.plane_totals.at[me],
            mem.total_send.at[0, mask],
            mem.total_recv.at[0, mask],
            (flip(me, mask), group),
        )
        copy.start()
        plane_copies.append(copy)
    for copy in plane_copies:
        copy.wait()
    mem.line_totals[group] = jnp.sum(mem.plane_totals[...], axis=0)
    total_copies = []
    for step in range(1, batch):
        copy = push(
            mem.line_totals.at[group],
            mem.line_totals.at[group],
            mem.total_send.at[1, step],
            mem.total_recv.at[1, step],
            (me, lax.rem(group + step, batch)),
        )
        copy.start()
        total_copies.append(copy)
    for copy in total_copies:
        copy.wait()
    outs.totals[...] = jnp.sum(mem.line_totals[...], axis=0)
    for copy in column_copies:
        copy.wait()
    for which in range(2):
        for block in range(blocks):
            owner, part = feed_block(block)
            outs.expand_share[which, :, block * LANES : (block + 1) * LANES] = mem.expand_share[
                which, owner, :, part * LANES : (part + 1) * LANES
            ]
    for copies in (attend_columns, expand_columns):
        for copy in copies:
            copy.wait_send()
    for line in [line_attend, line_output, line_reduce] + line_expand:
        line.finish()
    for line in [back_output, back_reduce] + back_attend + back_expand:
        line.finish()


def call_layer(seq, batch, inputs, teacher, facts, scored, bias, gains, attend, output, expand, reduce):
    rows, share, hidden = inputs.shape[0], attend.shape[1], expand.shape[2] // seq
    length, pair, chips = rows * seq, 2 * rows, seq // 2
    low = lambda *shape: pltpu.VMEM(shape, LOW)
    wide = lambda *shape: pltpu.VMEM(shape, WIDE)
    sems = lambda *shape: pltpu.SemaphoreType.DMA(shape)
    in_names = ["inputs", "teacher", "facts", "scored", "bias", "gains"]
    in_names += ["attend", "output", "expand", "reduce"]
    outs = dict(
        layer_output=((rows, D), WIDE),
        input_gradient=((rows, D), WIDE),
        totals=((TOTAL_ROWS, LANES), WIDE),
        count=((8, LANES), WIDE),
        attend_share=((3, share, D), LOW),
        output_share=((output.shape[0], D), WIDE),
        expand_share=((2, share, hidden * seq), LOW),
        reduce_share=((reduce.shape[0], D), WIDE),
    )
    scratch = dict(
        gains=wide(2, D),
        squares=wide(8, D),
        plane_totals=wide(seq, TOTAL_ROWS, LANES),
        line_totals=wide(batch, TOTAL_ROWS, LANES),
        attend_low=low(3, share, D),
        expand_low=low(2, seq, share, hidden),
        attend_all=low(3, seq, batch, share, LANES),
        output_full=low(D, D),
        expand_all=low(2, seq, batch, share, hidden),
        reduce_all=low(batch, reduce.shape[0], D),
        own_rows=low(4, rows, D),
        act_one=low(length, D),
        act_two=low(length, D),
        branch=low(length, D),
        grad_attn=low(length, D),
        facts_all=wide(seq * facts.shape[0], LANES),
        cosine=wide(HEAD_DIM // 2, length),
        sine=wide(HEAD_DIM // 2, length),
        labels=wide(8, length),
        key_marks=low(HEAD_DIM, length),
        count=wide(batch, 8, LANES),
        query_turned=low(HEADS_HERE, LANES, length),
        key_turned=low(LANES, length),
        value_turned=low(LANES, length),
        key_heads=low(HEADS_HERE, length, LANES),
        value_heads=low(HEADS_HERE, length, LANES),
        query_heads=low(HEADS_HERE, length, LANES),
        grad_heads=low(HEADS_HERE, length, LANES),
        grad_mixed=low(LANES, length),
        grad_mixed_out=low(seq, LANES, rows),
        probs=low(HEADS_HERE, length, length),
        mixed_out=low(length, LANES),
        mixed_rows=low(rows, D),
        sum_marks=low(HEAD_DIM, length),
        hidden_turned=low(hidden, length),
        act_two_turned=low(D, length),
        exact=wide(LANES, length),
        mixed_wide=wide(LANES, pair),
        mixed_turned=low(LANES, length),
        whole=wide(pair, D),
        keep=wide(chips, rows, D),
        near_from=low(chips, rows, D),
        near=low(chips, rows, D),
        far_from=low(chips, rows, D),
        far=low(chips, rows, D),
        middle=wide(rows, D),
        grad_own=wide(rows, D),
        by_up=wide(length, hidden),
        by_gate=wide(length, hidden),
        hidden=low(length, hidden),
        grad_gate=low(length, hidden),
        grad_up=low(length, hidden),
        bias_sums=wide(8, pair),
        grad_project=low(3, LANES, length),
        reduce_grad=low(batch, reduce.shape[0], D),
        expand_grad=low(2, seq, batch, share, hidden),
        output_grad=low(batch, output.shape[0], D),
        attend_grad=low(3, seq, batch, share, LANES),
        reduce_land=low(3, reduce.shape[0], D),
        expand_land=low(2, 3, 4, 2, share, hidden),
        output_land=low(batch, output.shape[0], D),
        attend_land=low(3, batch, seq, share, LANES),
        expand_part=low(2, 4, 2, share, hidden),
        expand_share=low(2, seq, share, hidden),
        attend_part=low(3, seq, share, LANES),
        stage_sem=sems(5 + 2 * (expand.shape[2] // D)),
        total_send=sems(2, seq),
        total_recv=sems(2, seq),
        column_send=sems(2, seq),
        column_recv=sems(2, seq),
        line_send=sems(5, batch),
        line_recv=sems(5, batch),
        facts_send=sems(seq),
        facts_recv=sems(seq),
        gather_send=sems(4, seq),
        gather_recv=sems(4, seq),
        count_send=sems(batch),
        count_recv=sems(batch),
        near_send=sems(4, chips),
        near_recv=sems(4, chips),
        far_send=sems(4, chips),
        far_recv=sems(4, chips),
        back_send=sems(7, batch),
        back_recv=sems(7, batch),
        output_send=sems(seq),
        output_recv=sems(seq),
        mixed_send=sems(2 * seq),
        mixed_recv=sems(2 * seq),
        share_send=sems(3, seq),
        share_recv=sems(3, seq),
    )

    places = dict.fromkeys(("attend", "output", "expand", "reduce"), pl.BlockSpec(memory_space=pl.ANY))
    places["bias"] = IN_SMEM

    def kernel(*refs):
        groups, start = [], 0
        for names in (in_names, outs, scratch):
            names = list(names)
            groups.append(types.SimpleNamespace(**dict(zip(names, refs[start : start + len(names)]))))
            start += len(names)
        layer_kernel(seq, batch, *groups)

    results = pl.pallas_call(
        kernel,
        out_shape=[jax.ShapeDtypeStruct(*out) for out in outs.values()],
        in_specs=[places.get(name, IN_VMEM) for name in in_names],
        out_specs=[IN_VMEM] * len(outs),
        scratch_shapes=list(scratch.values()),
        compiler_params=pltpu.CompilerParams(
            collective_id=0, has_side_effects=True, vmem_limit_bytes=63 * MIB
        ),
        name="layer",
    )(inputs, teacher, facts, scored, bias, gains, attend, output, expand, reduce)
    return types.SimpleNamespace(**dict(zip(outs, results)))


def update_kernel(
    totals,
    count,
    layer_output,
    input_gradient,
    attend_share,
    output_share,
    expand_share,
    reduce_share,
    gains,
    gains_first,
    gains_second,
    bias,
    bias_first,
    bias_second,
    *refs,
):
    olds, news = refs[:12], refs[12:]
    news[0][...] = layer_output[...]
    news[1][...] = input_gradient[...]
    gains_total = jnp.concatenate(
        [
            jnp.concatenate([totals[row + i : row + i + 1, :] for i in range(D // LANES)], axis=1)
            for row in (0, D // LANES)
        ],
        axis=0,
    )
    row = 2 * D // LANES
    bias_total = jnp.concatenate(
        [totals[row : row + 1, :HEADS], totals[row : row + 1, HEADS : 2 * HEADS]], axis=0
    )
    row += 1

    def sum_all(values):
        return jnp.sum(jnp.sum(values, axis=0, keepdims=True), axis=1, keepdims=True)

    squares = (
        totals[row : row + 1, 0:1] + sum_all(gains_total * gains_total) + sum_all(bias_total * bias_total)
    )
    grad_norm = jnp.sqrt(squares)
    clip = jnp.minimum(1.0, CLIP_NORM / grad_norm)
    news[2][...] = totals[row : row + 1, 1:2] / (count[0:1, 0:1] * D)
    news[3][...] = grad_norm
    shares = (attend_share, output_share, expand_share, reduce_share)
    rates = (RATE_ATTEND, RATE_OUTPUT, RATE_EXPAND, RATE_REDUCE)
    for number, (share, rate) in enumerate(zip(shares, rates)):
        weight, first, second = olds[3 * number : 3 * number + 3]
        new, copy, first_new, second_new = news[4 + 4 * number : 8 + 4 * number]
        scale = clip.reshape((1,) * share.ndim)
        new[...], first_new[...], second_new[...] = adam_step(
            weight[...], first[...], second[...], share[...].astype(WIDE) * scale, rate, WEIGHT_DECAY
        )
        copy[...] = new[...].astype(LOW)
    for number, (old, total, rate) in enumerate(
        (
            ((gains, gains_first, gains_second), gains_total, RATE_GAINS),
            ((bias, bias_first, bias_second), bias_total, RATE_BIAS),
        )
    ):
        new, first_new, second_new = news[20 + 3 * number : 23 + 3 * number]
        new[...], first_new[...], second_new[...] = adam_step(
            old[0][...], old[1][...], old[2][...], total * clip, rate, 0.0
        )


UPDATE_STEPS = 2


def cut_spec(shape):
    rows = shape[-2] // UPDATE_STEPS
    if len(shape) == 3:
        return pl.BlockSpec((shape[0], rows, shape[2]), lambda step: (0, step, 0))
    return pl.BlockSpec((rows, shape[1]), lambda step: (step, 0))


def whole_spec(shape):
    return pl.BlockSpec(shape, lambda step: (0,) * len(shape))


def call_update(done, shares, smalls, olds):
    whole = [done.totals, done.count]
    cut = [done.layer_output, done.input_gradient] + shares
    outs = [(done.layer_output, WIDE, cut_spec), (done.input_gradient, WIDE, cut_spec)]
    one = jax.ShapeDtypeStruct((1, 1), WIDE)
    outs += [(one, WIDE, whole_spec)] * 2
    for weight in olds[::3]:
        outs += [(weight, dtype, cut_spec) for dtype in (WIDE, LOW, WIDE, WIDE)]
    outs += [(small, WIDE, whole_spec) for small in smalls]
    return pl.pallas_call(
        update_kernel,
        grid=(UPDATE_STEPS,),
        out_shape=[jax.ShapeDtypeStruct(array.shape, dtype) for array, dtype, spec in outs],
        in_specs=[whole_spec(array.shape) for array in whole]
        + [cut_spec(array.shape) for array in cut]
        + [whole_spec(array.shape) for array in smalls]
        + [cut_spec(array.shape) for array in olds],
        out_specs=[spec(array.shape) for array, dtype, spec in outs],
        compiler_params=pltpu.CompilerParams(vmem_limit_bytes=63 * MIB),
        name="update",
    )(*whole, *cut, *smalls, *olds)


def fast_body(
    seq,
    batch,
    inputs,
    teacher,
    lengths,
    variate_ids,
    time_ids,
    observed,
    attend_weight,
    output_weight,
    expand_weight,
    reduce_weight,
    norm_gains,
    variate_bias,
    attend_first,
    output_first,
    expand_first,
    reduce_first,
    gains_first,
    bias_first,
    attend_second,
    output_second,
    expand_second,
    reduce_second,
    gains_second,
    bias_second,
):
    me = lax.axis_index("seq")
    rows = inputs.shape[1]
    positions = me * rows + jnp.arange(rows, dtype=jnp.int32)
    inside = positions < lengths[0]
    scored = jnp.logical_and(inside, observed[0] == 1)
    half_dim = HEAD_DIM // 2
    frequency = jnp.exp(-math.log(ROPE_BASE) * jnp.arange(half_dim).astype(WIDE) / half_dim)
    angle = frequency[:, None] * time_ids[0].astype(WIDE)[None, :]
    labels = jnp.stack(
        [
            jnp.where(inside, variate_ids[0], -1).astype(WIDE),
            variate_ids[0].astype(WIDE),
            scored.astype(WIDE),
        ]
    )
    facts = jnp.concatenate([jnp.cos(angle), jnp.sin(angle), jnp.pad(labels, ((0, 5), (0, 0)))])
    done = call_layer(
        seq,
        batch,
        inputs[0],
        teacher[0],
        facts,
        scored.astype(WIDE)[:, None],
        variate_bias,
        norm_gains,
        attend_weight,
        output_weight,
        expand_weight,
        reduce_weight,
    )
    results = call_update(
        done,
        [done.attend_share, done.output_share, done.expand_share, done.reduce_share],
        [norm_gains, gains_first, gains_second, variate_bias, bias_first, bias_second],
        [attend_weight, attend_first, attend_second]
        + [output_weight, output_first, output_second]
        + [expand_weight, expand_first, expand_second]
        + [reduce_weight, reduce_first, reduce_second],
    )
    output, input_gradient, loss, grad_norm = results[:4]
    return (
        output[None],
        loss.reshape(()),
        input_gradient[None],
        grad_norm.reshape(()),
    ) + tuple(results[4:])


def solution(mesh):
    seq, batch = mesh.shape["seq"], mesh.shape["batch"]
    body = functools.partial(fast_body, seq, batch) if fast_fits(seq, batch) else general_body
    in_specs = (
        P("batch", "seq", None),
        P("batch", "seq", None),
        P("batch"),
        P("batch", "seq"),
        P("batch", "seq"),
        P("batch", "seq"),
        P(None, ("seq", "batch"), None),
        P(("seq", "batch"), None),
        P(None, ("seq", "batch"), None),
        P(("seq", "batch"), None),
        P(),
        P(),
        P(None, ("seq", "batch"), None),
        P(("seq", "batch"), None),
        P(None, ("seq", "batch"), None),
        P(("seq", "batch"), None),
        P(),
        P(),
        P(None, ("seq", "batch"), None),
        P(("seq", "batch"), None),
        P(None, ("seq", "batch"), None),
        P(("seq", "batch"), None),
        P(),
        P(),
    )
    out_specs = (
        P("batch", "seq", None),
        P(),
        P("batch", "seq", None),
        P(),
        P(None, ("seq", "batch"), None),
        P(None, ("seq", "batch"), None),
        P(None, ("seq", "batch"), None),
        P(None, ("seq", "batch"), None),
        P(("seq", "batch"), None),
        P(("seq", "batch"), None),
        P(("seq", "batch"), None),
        P(("seq", "batch"), None),
        P(None, ("seq", "batch"), None),
        P(None, ("seq", "batch"), None),
        P(None, ("seq", "batch"), None),
        P(None, ("seq", "batch"), None),
        P(("seq", "batch"), None),
        P(("seq", "batch"), None),
        P(("seq", "batch"), None),
        P(("seq", "batch"), None),
        P(),
        P(),
        P(),
        P(),
        P(),
        P(),
    )
    return jax.shard_map(body, mesh=mesh, in_specs=in_specs, out_specs=out_specs, check_vma=False)
```

```python
import functools
import math
import types

import jax
import jax.numpy as jnp
from jax import lax
from jax.experimental import pallas as pl
from jax.experimental.pallas import tpu as pltpu
from jax.sharding import PartitionSpec as P

D = 1024
HEADS = 16
HEAD_DIM = 64
STEP = 10


NORM_EPS = 1e-05
ROPE_BASE = 10000.0
MASKED = -1e30
CLIP_NORM = 1.0
BETA_ONE = 0.9
BETA_TWO = 0.98
ADAM_EPS = 1e-08
WEIGHT_DECAY = 0.1
RATE_ATTEND = 0.03
RATE_OUTPUT = 0.5
RATE_EXPAND = 0.03
RATE_REDUCE = 0.015
RATE_GAINS = 1.0
RATE_BIAS = 0.5


def angles(times):
    half_dim = HEAD_DIM // 2
    frequency = jnp.exp(-math.log(ROPE_BASE) * jnp.arange(half_dim).astype(jnp.float32) / half_dim)
    angle_table = times.astype(jnp.float32)[..., None] * frequency
    return (jnp.cos(angle_table)[..., None, :], jnp.sin(angle_table)[..., None, :])


def rotate(values, cos_table, sin_table):
    half_dim = values.shape[-1] // 2
    first_half = values[..., :half_dim]
    second_half = values[..., half_dim:]
    return jnp.concatenate(
        [
            first_half * cos_table - second_half * sin_table,
            second_half * cos_table + first_half * sin_table,
        ],
        axis=-1,
    )


def unrotate(values, cos_table, sin_table):
    half_dim = values.shape[-1] // 2
    first_half = values[..., :half_dim]
    second_half = values[..., half_dim:]
    return jnp.concatenate(
        [
            first_half * cos_table + second_half * sin_table,
            second_half * cos_table - first_half * sin_table,
        ],
        axis=-1,
    )


def normalize(values):
    inv_scale = lax.rsqrt(jnp.mean(values * values, axis=-1, keepdims=True) + NORM_EPS)
    return (values * inv_scale, inv_scale)


def norm_back(grad_act, unit_rows, inv_scale, gain_row):
    grad_unit = grad_act * gain_row
    return inv_scale * (
        grad_unit - unit_rows * jnp.mean(grad_unit * unit_rows, axis=-1, keepdims=True)
    )


def score_block(query_rows, query_labels, key_rows, key_labels, bias_table):
    scores = jnp.einsum(
        "ihe,jhe->hij", query_rows, key_rows, preferred_element_type=jnp.float32
    ) * HEAD_DIM ** (-0.5)
    same_var = query_labels[:, None] == key_labels[None, :]
    scores = scores + jnp.where(
        same_var[None], bias_table[0][:, None, None], bias_table[1][:, None, None]
    )
    scores = jnp.where(key_labels[None, None, :] >= 0, scores, MASKED)
    return (scores, same_var)


def block_grads(
    query_rows,
    query_labels,
    grad_rows,
    lse_rows,
    delta_rows,
    key_rows,
    value_rows,
    key_labels,
    bias_table,
    need_query,
    need_keys,
):
    scores, same_var = score_block(query_rows, query_labels, key_rows, key_labels, bias_table)
    weights = jnp.exp(scores - lse_rows.T[:, :, None])
    grad_weights = jnp.einsum(
        "ihe,jhe->hij", grad_rows, value_rows, preferred_element_type=jnp.float32
    )
    grad_scores = (weights * (grad_weights - delta_rows.T[:, :, None])).astype(jnp.bfloat16)
    result = ()
    if need_query:
        grad_query = jnp.einsum(
            "hij,jhe->ihe", grad_scores, key_rows, preferred_element_type=jnp.float32
        ) * HEAD_DIM ** (-0.5)
        widened = grad_scores.astype(jnp.float32)
        bias_same = jnp.sum(jnp.where(same_var[None], widened, 0.0), axis=(1, 2))
        bias_other = jnp.sum(jnp.where(same_var[None], 0.0, widened), axis=(1, 2))
        result = result + (grad_query, jnp.stack([bias_same, bias_other]))
    if need_keys:
        grad_key = jnp.einsum(
            "hij,ihe->jhe", grad_scores, query_rows, preferred_element_type=jnp.float32
        ) * HEAD_DIM ** (-0.5)
        grad_value = jnp.einsum(
            "hij,ihe->jhe",
            weights.astype(jnp.bfloat16),
            grad_rows,
            preferred_element_type=jnp.float32,
        )
        result = result + (grad_key, grad_value)
    return result


def adam_step(weight, first_moment, second_moment, gradient, step_rate, decay_rate):
    first_moment = BETA_ONE * first_moment + (1.0 - BETA_ONE) * gradient
    second_moment = BETA_TWO * second_moment + (1.0 - BETA_TWO) * gradient * gradient
    direction = (
        first_moment
        / (1.0 - BETA_ONE**STEP)
        / (jnp.sqrt(second_moment / (1.0 - BETA_TWO**STEP)) + ADAM_EPS)
    )
    return (weight - step_rate * (direction + decay_rate * weight), first_moment, second_moment)


def general_body(
    inputs,
    teacher,
    lengths,
    variate_ids,
    time_ids,
    observed,
    attend_weight,
    output_weight,
    expand_weight,
    reduce_weight,
    norm_gains,
    variate_bias,
    attend_first,
    output_first,
    expand_first,
    reduce_first,
    gains_first,
    bias_first,
    attend_second,
    output_second,
    expand_second,
    reduce_second,
    gains_second,
    bias_second,
):
    row_count = inputs.shape[1]
    length = row_count * lax.axis_size("seq")
    block_rows = math.gcd(length, 1024)
    blocks = length // block_rows
    states = inputs[0].astype(jnp.float32)
    positions = lax.axis_index("seq") * row_count + jnp.arange(row_count, dtype=jnp.int32)
    inside = positions < lengths[0]
    scored = jnp.logical_and(inside, observed[0] == 1)
    local_count = jnp.sum(scored.astype(jnp.int32))
    count_early = lax.psum(local_count, ("seq", "batch"))
    full_attend, full_output, full_expand, full_reduce = (
        lax.all_gather(attend_weight.astype(jnp.bfloat16), ("seq", "batch"), axis=1, tiled=True),
        lax.all_gather(output_weight.astype(jnp.bfloat16), ("seq", "batch"), axis=0, tiled=True),
        lax.all_gather(expand_weight.astype(jnp.bfloat16), ("seq", "batch"), axis=1, tiled=True),
        lax.all_gather(reduce_weight.astype(jnp.bfloat16), ("seq", "batch"), axis=0, tiled=True),
    )
    unit_one, scale_one = normalize(states)
    act_one = (unit_one * norm_gains[0]).astype(jnp.bfloat16)
    project = jnp.einsum("td,cde->cte", act_one, full_attend, preferred_element_type=jnp.float32)
    cos_table, sin_table = angles(time_ids[0])
    query = rotate(project[0].reshape(row_count, HEADS, HEAD_DIM), cos_table, sin_table).astype(
        jnp.bfloat16
    )
    key_rows = (
        rotate(project[1].reshape(row_count, HEADS, HEAD_DIM), cos_table, sin_table)
        .astype(jnp.bfloat16)
        .reshape(row_count, D)
    )
    value_rows = project[2].astype(jnp.bfloat16)
    own_labels = jnp.where(inside, variate_ids[0], -1).astype(jnp.bfloat16)
    all_keys, all_values, all_labels = (
        lax.all_gather(key_rows, "seq", axis=0, tiled=True),
        lax.all_gather(value_rows, "seq", axis=0, tiled=True),
        lax.all_gather(own_labels, "seq", axis=0, tiled=True),
    )
    key_blocks = all_keys.reshape(blocks, block_rows, HEADS, HEAD_DIM)
    value_blocks = all_values.reshape(blocks, block_rows, HEADS, HEAD_DIM)
    label_blocks = all_labels.astype(jnp.float32).reshape(blocks, block_rows)
    query_labels = variate_ids[0].astype(jnp.float32)

    def sweep_top(carry, pieces):
        running, sum_exp = carry
        scores, same_var = score_block(query, query_labels, pieces[0], pieces[1], variate_bias)
        raised = jnp.maximum(running, jnp.floor(jnp.max(scores, axis=-1)))
        sum_exp = sum_exp * jnp.exp(running - raised) + jnp.sum(
            jnp.exp(scores - raised[..., None]), axis=-1
        )
        return ((raised, sum_exp), None)

    start_top = jnp.full((HEADS, row_count), MASKED, jnp.float32)
    (row_top, sum_exp), unused = lax.scan(
        sweep_top,
        (start_top, jnp.zeros((HEADS, row_count), jnp.float32)),
        (key_blocks, label_blocks),
    )
    log_total = row_top + jnp.log(sum_exp)

    def sweep_out(carry, pieces):
        coarse, finest = carry
        scores, same_var = score_block(query, query_labels, pieces[0], pieces[2], variate_bias)
        weights = jnp.exp(scores - log_total[..., None])
        rounded = weights.astype(jnp.bfloat16)
        residue = (weights - rounded.astype(jnp.float32)).astype(jnp.bfloat16)
        coarse = coarse + jnp.einsum(
            "hij,jhe->ihe", rounded, pieces[1], preferred_element_type=jnp.float32
        )
        finest = finest + jnp.einsum(
            "hij,jhe->ihe", residue, pieces[1], preferred_element_type=jnp.float32
        )
        return ((coarse, finest), None)

    zero_heads = jnp.zeros((row_count, HEADS, HEAD_DIM), jnp.float32)
    (coarse, finest), unused = lax.scan(
        sweep_out, (zero_heads, zero_heads), (key_blocks, value_blocks, label_blocks)
    )
    exact_heads = coarse + finest
    mixed = coarse.reshape(row_count, D).astype(jnp.bfloat16)
    middle = states + jnp.dot(mixed, full_output, preferred_element_type=jnp.float32)
    unit_two, scale_two = normalize(middle)
    act_two = (unit_two * norm_gains[1]).astype(jnp.bfloat16)
    gate_up = jnp.einsum("td,cdf->ctf", act_two, full_expand, preferred_element_type=jnp.float32)
    sigmoid = jax.nn.sigmoid(gate_up[0])
    hidden = (gate_up[0] * sigmoid * gate_up[1]).astype(jnp.bfloat16)
    output = middle + jnp.dot(hidden, full_reduce, preferred_element_type=jnp.float32)
    error = output - teacher[0].astype(jnp.float32)
    local_square = jnp.sum(jnp.where(scored[:, None], error * error, 0.0))
    square_total = lax.psum(local_square, ("seq", "batch"))
    count_all = count_early.astype(jnp.float32)
    loss = square_total / (count_all * D)
    grad_out = jnp.where(scored[:, None], error * (2.0 / (count_all * D)), 0.0)
    back_attend, back_output, back_expand, back_reduce = (
        lax.all_gather(attend_weight.astype(jnp.bfloat16), ("seq", "batch"), axis=1, tiled=True),
        lax.all_gather(output_weight.astype(jnp.bfloat16), ("seq", "batch"), axis=0, tiled=True),
        lax.all_gather(expand_weight.astype(jnp.bfloat16), ("seq", "batch"), axis=1, tiled=True),
        lax.all_gather(reduce_weight.astype(jnp.bfloat16), ("seq", "batch"), axis=0, tiled=True),
    )
    grad_branch = grad_out.astype(jnp.bfloat16)
    reduce_grad = jnp.einsum("tf,td->fd", hidden, grad_branch, preferred_element_type=jnp.float32)
    grad_hidden = jnp.einsum(
        "td,fd->tf", grad_branch, back_reduce, preferred_element_type=jnp.float32
    )
    grad_gate = grad_hidden * gate_up[1] * sigmoid * (1.0 + gate_up[0] * (1.0 - sigmoid))
    grad_up = grad_hidden * gate_up[0] * sigmoid
    grad_expand = jnp.stack([grad_gate, grad_up]).astype(jnp.bfloat16)
    expand_grad = jnp.einsum(
        "td,ctf->cdf", act_two, grad_expand, preferred_element_type=jnp.float32
    )
    grad_act_two = jnp.einsum(
        "ctf,cdf->td", grad_expand, back_expand, preferred_element_type=jnp.float32
    )
    expand_share, reduce_share = (
        lax.psum_scatter(expand_grad, ("seq", "batch"), scatter_dimension=1, tiled=True),
        lax.psum_scatter(reduce_grad, ("seq", "batch"), scatter_dimension=0, tiled=True),
    )
    grad_middle = grad_out + norm_back(grad_act_two, unit_two, scale_two, norm_gains[1])
    grad_attn = grad_middle.astype(jnp.bfloat16)
    output_grad = jnp.einsum("td,te->de", mixed, grad_attn, preferred_element_type=jnp.float32)
    grad_mixed = jnp.einsum(
        "te,de->td", grad_attn, back_output, preferred_element_type=jnp.float32
    ).astype(jnp.bfloat16)
    grad_heads = grad_mixed.reshape(row_count, HEADS, HEAD_DIM)
    row_delta = jnp.sum(grad_heads.astype(jnp.float32) * exact_heads, axis=-1)
    lse_rows = log_total.T
    zero_bias = jnp.zeros((2, HEADS), jnp.float32)

    def sweep_query(carry, pieces):
        part_query, part_bias = block_grads(
            query,
            query_labels,
            grad_heads,
            lse_rows,
            row_delta,
            pieces[0],
            pieces[1],
            pieces[2],
            variate_bias,
            True,
            False,
        )
        return ((carry[0] + part_query, carry[1] + part_bias), None)

    (query_total, bias_grad), unused = lax.scan(
        sweep_query, (zero_heads, zero_bias), (key_blocks, value_blocks, label_blocks)
    )
    all_query, all_grad = (
        lax.all_gather(query.reshape(row_count, D), "seq", axis=0, tiled=True),
        lax.all_gather(grad_mixed, "seq", axis=0, tiled=True),
    )
    all_lse, all_delta = (
        lax.all_gather(lse_rows, "seq", axis=0, tiled=True),
        lax.all_gather(row_delta, "seq", axis=0, tiled=True),
    )
    key_heads = key_rows.reshape(row_count, HEADS, HEAD_DIM)
    value_heads = value_rows.reshape(row_count, HEADS, HEAD_DIM)
    own_float = own_labels.astype(jnp.float32)

    def sweep_keys(carry, pieces):
        part_key, part_value = block_grads(
            pieces[0],
            pieces[1],
            pieces[2],
            pieces[3],
            pieces[4],
            key_heads,
            value_heads,
            own_float,
            variate_bias,
            False,
            True,
        )
        return ((carry[0] + part_key, carry[1] + part_value), None)

    (key_total, value_heads_total), unused = lax.scan(
        sweep_keys,
        (zero_heads, zero_heads),
        (
            all_query.reshape(blocks, block_rows, HEADS, HEAD_DIM),
            label_blocks,
            all_grad.reshape(blocks, block_rows, HEADS, HEAD_DIM),
            all_lse.reshape(blocks, block_rows, HEADS),
            all_delta.reshape(blocks, block_rows, HEADS),
        ),
    )
    value_total = value_heads_total.reshape(row_count, D)
    grad_query = unrotate(query_total, cos_table, sin_table).reshape(row_count, D)
    grad_key = unrotate(key_total, cos_table, sin_table).reshape(row_count, D)
    grad_project = jnp.stack([grad_query, grad_key, value_total]).astype(jnp.bfloat16)
    attend_grad = jnp.einsum(
        "td,cte->cde", act_one, grad_project, preferred_element_type=jnp.float32
    )
    grad_act_one = jnp.einsum(
        "cte,cde->td", grad_project, back_attend, preferred_element_type=jnp.float32
    )
    attend_share, output_share = (
        lax.psum_scatter(attend_grad, ("seq", "batch"), scatter_dimension=1, tiled=True),
        lax.psum_scatter(output_grad, ("seq", "batch"), scatter_dimension=0, tiled=True),
    )
    grad_input = grad_middle + norm_back(grad_act_one, unit_one, scale_one, norm_gains[0])
    gains_grad = jnp.stack(
        [jnp.sum(grad_act_one * unit_one, axis=0), jnp.sum(grad_act_two * unit_two, axis=0)]
    )
    local_squares = (
        jnp.sum(attend_share * attend_share)
        + jnp.sum(output_share * output_share)
        + jnp.sum(expand_share * expand_share)
        + jnp.sum(reduce_share * reduce_share)
    )
    gains_total, bias_total, square_sum = lax.psum(
        (gains_grad, bias_grad, local_squares), ("seq", "batch")
    )
    grad_norm = jnp.sqrt(
        square_sum + jnp.sum(gains_total * gains_total) + jnp.sum(bias_total * bias_total)
    )
    clip_scale = jnp.minimum(1.0, CLIP_NORM / grad_norm)
    attend_new, attend_first_new, attend_second_new = adam_step(
        attend_weight,
        attend_first,
        attend_second,
        attend_share * clip_scale,
        RATE_ATTEND,
        WEIGHT_DECAY,
    )
    output_new, output_first_new, output_second_new = adam_step(
        output_weight,
        output_first,
        output_second,
        output_share * clip_scale,
        RATE_OUTPUT,
        WEIGHT_DECAY,
    )
    expand_new, expand_first_new, expand_second_new = adam_step(
        expand_weight,
        expand_first,
        expand_second,
        expand_share * clip_scale,
        RATE_EXPAND,
        WEIGHT_DECAY,
    )
    reduce_new, reduce_first_new, reduce_second_new = adam_step(
        reduce_weight,
        reduce_first,
        reduce_second,
        reduce_share * clip_scale,
        RATE_REDUCE,
        WEIGHT_DECAY,
    )
    gains_new, gains_first_new, gains_second_new = adam_step(
        norm_gains, gains_first, gains_second, gains_total * clip_scale, RATE_GAINS, 0.0
    )
    bias_new, bias_first_new, bias_second_new = adam_step(
        variate_bias, bias_first, bias_second, bias_total * clip_scale, RATE_BIAS, 0.0
    )
    input_gradient = (grad_input * count_all * D)[None]
    return (
        output[None],
        loss,
        input_gradient,
        grad_norm,
        attend_new,
        attend_new.astype(jnp.bfloat16),
        attend_first_new,
        attend_second_new,
        output_new,
        output_new.astype(jnp.bfloat16),
        output_first_new,
        output_second_new,
        expand_new,
        expand_new.astype(jnp.bfloat16),
        expand_first_new,
        expand_second_new,
        reduce_new,
        reduce_new.astype(jnp.bfloat16),
        reduce_first_new,
        reduce_second_new,
        gains_new,
        gains_first_new,
        gains_second_new,
        bias_new,
        bias_first_new,
        bias_second_new,
    )


MESH = pl.DeviceIdType.MESH
IN_VMEM = pl.BlockSpec(memory_space=pltpu.VMEM)
IN_SMEM = pl.BlockSpec(memory_space=pltpu.SMEM)
LANES = 128
HEADS_HERE = LANES // HEAD_DIM
VARIATES = 16
MIB = 1 << 20
LOW = jnp.bfloat16
WIDE = jnp.float32
TOTAL_ROWS = 24


def fast_fits(seq, batch):
    return seq == 8 and batch == 4 and seq * LANES == D


def flip(index, mask):
    result, bit = index, 1
    while bit <= mask:
        if mask & bit:
            result = result + bit - 2 * bit * lax.rem(lax.div(index, bit), 2)
        bit *= 2
    return result


def push(source, target, send_sem, recv_sem, device):
    return pltpu.make_async_remote_copy(
        src_ref=source,
        dst_ref=target,
        send_sem=send_sem,
        recv_sem=recv_sem,
        device_id=device,
        device_id_type=MESH,
    )


def block_of(index, size):
    return pl.ds(pl.multiple_of(index * size, size), size)


def dot(left, right):
    return jnp.dot(left, right, preferred_element_type=WIDE)


def dot_turned(left, right):
    return lax.dot_general(left, right, (((1,), (1,)), ((), ())), preferred_element_type=WIDE)


def turned_dot(left, right):
    return lax.dot_general(left, right, (((0,), (0,)), ((), ())), preferred_element_type=WIDE)


class Team:
    def __init__(self, index, place):
        self.index, self.place = index, place

    def at(self, mask):
        return flip(self.index, mask)


def head_team(me, group):
    return Team(me, lambda mask: (flip(me, mask), group))


def feed_team(me, group):
    return Team(
        4 * lax.rem(group, 2) + lax.rem(me, 4),
        lambda mask: (flip(me, mask % 4), flip(group, mask // 4)),
    )


class Gather:
    def __init__(self, team, rows, all_rows, sends, recvs):
        self.team, self.all_rows, self.sends, self.recvs = team, all_rows, sends, recvs
        self.size = all_rows.shape[0] // 8
        self.given = rows
        self.rows = all_rows.at[block_of(team.index, self.size)] if rows is None else rows

    def copy(self, mask, passing):
        source = self.all_rows.at[block_of(self.team.at(mask - 1 if passing else 0), self.size)]
        return push(
            source if passing else self.rows,
            source,
            self.sends.at[mask],
            self.recvs.at[mask],
            self.team.place(1 if passing else mask),
        )

    def start(self):
        for mask in (6, 2, 4, 1):
            self.copy(mask, False).start()
        if self.given is not None:
            self.all_rows[block_of(self.team.index, self.size)] = self.given[...]

    def pass_on(self, chip):
        self.copy(2 * chip, False).wait_recv()
        self.copy(2 * chip + 1, True).start()

    def complete(self, chip):
        self.copy(2 * chip + 1, chip > 0).wait_recv()

    def finish(self):
        for mask in (6, 2, 4, 1):
            self.copy(mask, False).wait_send()
        for mask in (3, 5, 7):
            self.copy(mask, True).wait_send()


def at_step(step, number, *works):
    @pl.when(step == number)
    def _():
        for work in works:
            work()


def each_chip(gather, work, after):
    def one_chip(chip, unused):
        @pl.when(chip == 0)
        def _():
            gather.complete(0)

        @pl.when(chip == 1)
        def _():
            gather.pass_on(1)
            gather.pass_on(2)
            gather.complete(1)

        @pl.when(chip == 2)
        def _():
            gather.pass_on(3)
            gather.complete(2)

        @pl.when(chip == 3)
        def _():
            gather.complete(3)

        work(chip)
        for number, works in after.items():
            at_step(chip, number, *works)
        return unused

    lax.fori_loop(0, 4, one_chip, 0)
    gather.finish()


class Scatter:
    def __init__(self, team, buffers, near_sends, near_recvs, far_sends, far_recvs):
        self.whole, self.keep, self.near_from, self.near, self.far_from, self.far = buffers
        self.sems = near_sends, near_recvs, far_sends, far_recvs
        self.team = team
        self.size = self.keep.shape[1]

    def near_copy(self, chip):
        return push(
            self.near_from.at[chip],
            self.near.at[chip],
            self.sems[0].at[chip],
            self.sems[1].at[chip],
            self.team.place(1),
        )

    def far_copy(self, chip):
        return push(
            self.far_from.at[chip],
            self.far.at[chip],
            self.sems[2].at[chip],
            self.sems[3].at[chip],
            self.team.place(2 * chip),
        )

    def put(self, chip, rows):
        core = lax.rem(self.team.index, 2)
        self.whole[...] = rows
        self.near_from[chip] = self.whole[block_of(1 - core, self.size)].astype(LOW)
        self.near_copy(chip).start()
        self.keep[chip] = self.whole[block_of(core, self.size)]

    def combine(self, chip):
        self.near_copy(chip).wait_recv()
        self.far_from[chip] = (self.keep[chip] + self.near[chip].astype(WIDE)).astype(LOW)
        self.far_copy(chip).start()

    def total(self):
        self.near_copy(0).wait_recv()
        total = self.keep[0] + self.near[0].astype(WIDE)
        for chip in (1, 2, 3):
            self.far_copy(chip).wait_recv()
            total = total + self.far[chip].astype(WIDE)
        for chip in (0, 1, 2, 3):
            self.near_copy(chip).wait_send()
            if chip:
                self.far_copy(chip).wait_send()
        return total


class LineGather:
    def __init__(self, part_of, sends, recvs, me, group):
        self.part_of, self.sends, self.recvs, self.me, self.group = part_of, sends, recvs, me, group

    def copy(self, step):
        part = self.part_of(self.group)
        other = lax.rem(self.group + step, 4)
        return push(part, part, self.sends.at[step], self.recvs.at[step], (self.me, other))

    def start(self):
        for step in (2, 1, 3):
            self.copy(step).start()

    def land(self):
        for step in (1, 2, 3):
            self.copy(step).wait_recv()

    def finish(self):
        for step in (1, 2, 3):
            self.copy(step).wait_send()


class LineScatter:
    def __init__(self, part_of, landing, sends, recvs, me, group):
        self.part_of, self.landing, self.sends, self.recvs = part_of, landing, sends, recvs
        self.me, self.group = me, group

    def copy(self, step):
        other = lax.rem(self.group + step, 4)
        return push(
            self.part_of(other),
            self.landing.at[step - 1],
            self.sends.at[step],
            self.recvs.at[step],
            (self.me, other),
        )

    def start(self):
        for step in (2, 1, 3):
            self.copy(step).start()

    def land(self):
        for step in (1, 2, 3):
            self.copy(step).wait_recv()

    def total(self):
        total = self.part_of(self.group)[...].astype(WIDE)
        for slot in range(3):
            total = total + self.landing[slot].astype(WIDE)
        return total

    def finish(self):
        for step in (1, 2, 3):
            self.copy(step).wait_send()


class QuadGather:
    def __init__(self, part_of, sends, recvs, me, group):
        self.part_of, self.sends, self.recvs = part_of, sends, recvs
        self.part = 2 * lax.div(me, 4) + lax.div(group, 2)
        self.along_y, self.along_z = (flip(me, 4), group), (me, flip(group, 2))

    def copy(self, way):
        part = self.part_of(flip(self.part, 1) if way == 3 else self.part)
        device = self.along_z if way == 1 else self.along_y
        return push(part, part, self.sends.at[way], self.recvs.at[way], device)

    def start_y(self):
        self.copy(2).start()

    def start_z(self):
        self.copy(1).start()

    def pass_on(self):
        self.copy(1).wait_recv()
        self.copy(3).start()

    def land(self):
        self.copy(2).wait_recv()
        self.copy(3).wait_recv()

    def finish(self):
        for way in (1, 2, 3):
            self.copy(way).wait_send()


class QuadScatter:
    def __init__(self, part_of, landing, sends, recvs, me, group):
        self.part_of, self.landing, self.sends, self.recvs = part_of, landing, sends, recvs
        self.part = 2 * lax.div(me, 4) + lax.div(group, 2)
        self.along_y, self.along_z = (flip(me, 4), group), (me, flip(group, 2))

    def copy(self, slot):
        return push(
            self.part_of(flip(self.part, (2, 3, 1)[slot])),
            self.landing.at[slot],
            self.sends.at[slot],
            self.recvs.at[slot],
            self.along_z if slot == 2 else self.along_y,
        )

    def start_far(self):
        self.copy(1).start()

    def start_near(self):
        self.copy(0).start()

    def pass_on(self):
        self.copy(1).wait_recv()
        part = self.part_of(flip(self.part, 1))
        part[...] = (part[...].astype(WIDE) + self.landing[1].astype(WIDE)).astype(LOW)
        self.copy(2).start()

    def land(self):
        self.copy(0).wait_recv()
        self.copy(2).wait_recv()

    def finish(self):
        for slot in (0, 1, 2):
            self.copy(slot).wait_send()


def chip_of(team, chip):
    here = lax.div(team.index, 2)
    if isinstance(chip, int):
        return flip(here, chip)
    column = lax.rem(lax.rem(here, 2) + lax.rem(chip, 2), 2)
    row = lax.rem(lax.div(here, 2) + lax.div(chip, 2), 2)
    return 2 * row + column


def turn_rows(values, cosine, sine):
    half = HEAD_DIM // 2
    pieces = []
    for start in range(0, values.shape[0], HEAD_DIM):
        first, second = values[start : start + half], values[start + half : start + HEAD_DIM]
        pieces += [first * cosine - second * sine, second * cosine + first * sine]
    return jnp.concatenate(pieces, axis=0)


def thirds(values):
    first = values.astype(LOW).astype(WIDE)
    second = (values - first).astype(LOW).astype(WIDE)
    return first, second, values - first - second


def pick(row, choices):
    result = jnp.zeros(row.shape, WIDE)
    for number, choice in choices.items():
        result = jnp.where(row == number, choice, result)
    return result


def norm_rows(values):
    scale = lax.rsqrt(jnp.mean(values * values, axis=-1, keepdims=True) + NORM_EPS)
    return values * scale, scale


def feed_block(block):
    y, x, core, far_z, near_z = (block // 16, block // 8 % 2, block // 4 % 2, block // 2 % 2, block % 2)
    return 4 * near_z + 2 * x + core, 2 * y + far_z


def layer_kernel(seq, batch, ins, outs, mem):
    me, group = lax.axis_index("seq"), lax.axis_index("batch")
    rows = ins.inputs.shape[0]
    length = rows * seq
    pair = 2 * rows
    share = ins.attend.shape[1]
    wide_columns = ins.expand.shape[2] // D
    hidden_width = mem.reduce_all.shape[0] * mem.reduce_all.shape[1]
    blocks = ins.expand.shape[2] // LANES
    heads, feeds = head_team(me, group), feed_team(me, group)
    quad = 2 * lax.div(me, 4) + lax.div(group, 2)

    staged = [(ins.attend.at[which], mem.keep.at[0, block_of(which, share)]) for which in range(3)]
    staged.append((ins.output, mem.keep.at[0, block_of(3, share)]))
    staged.append((ins.reduce, mem.keep.at[1]))
    for which in range(2):
        for block in range(wide_columns):
            columns = slice(block * D, (block + 1) * D)
            staged.append(
                (ins.expand.at[which, :, columns], mem.keep.at[2 + which, block_of(block, share)])
            )
    staged = [
        pltpu.make_async_copy(source, target, mem.stage_sem.at[number])
        for number, (source, target) in enumerate(staged)
    ]
    for copy in staged:
        copy.start()
    barrier = pltpu.get_barrier_semaphore()
    for mask in range(1, seq):
        pl.semaphore_signal(barrier, inc=1, device_id=(flip(me, mask), group), device_id_type=MESH)
    for step in range(1, batch):
        pl.semaphore_signal(
            barrier, inc=1, device_id=(me, lax.rem(group + step, batch)), device_id_type=MESH
        )
    for mask in (5, 6, 7):
        pl.semaphore_signal(barrier, inc=1, device_id=feeds.place(mask), device_id_type=MESH)

    position = me * rows + lax.broadcasted_iota(jnp.int32, (1, rows), 1)
    inside = position < ins.lengths[0]
    scored = jnp.logical_and(inside, ins.observed[...] == 1).astype(WIDE)
    variate = ins.variates[...].astype(WIDE)
    turns = ins.turns.shape[0]
    mem.facts_own[:turns] = ins.turns[...]
    mem.facts_own[turns:] = jnp.concatenate(
        [jnp.where(inside, variate, -1.0), variate, scored, jnp.zeros((5, rows), WIDE)], axis=0
    )
    mem.scored[...] = jnp.broadcast_to(scored, (rows, rows)).T
    unit_one, scale_one = norm_rows(ins.inputs[...].astype(WIDE))
    mem.own_rows[0] = (unit_one * ins.gains[0:1, :]).astype(LOW)
    for copy in staged:
        copy.wait()
    for which in range(3):
        mem.attend_low[which] = mem.keep[0, block_of(which, share)].astype(LOW)
    mem.output_full[block_of(batch * me + group, share)] = mem.keep[0, block_of(3, share)].astype(LOW)
    mem.reduce_all[quad] = mem.keep[1].astype(LOW)
    for which in range(2):
        for block in range(blocks):
            owner, part = feed_block(block)
            row, lane = divmod(block * LANES, D)
            mem.expand_low[which, owner, :, part * LANES : (part + 1) * LANES] = mem.keep[
                2 + which, block_of(row, share), lane : lane + LANES
            ].astype(LOW)
    pl.semaphore_wait(barrier, seq + batch + 1)

    masks = (6, 7, 4, 5, 2, 3, 1)

    def start_attend_columns():
        copies = []
        for mask in masks:
            copy = push(
                mem.attend_low.at[:, :, block_of(heads.at(mask), LANES)],
                mem.attend_all.at[:, me, group],
                mem.column_send.at[0, mask],
                mem.column_recv.at[0, mask],
                heads.place(mask),
            )
            copy.start()
            copies.append(copy)
        mem.attend_all[:, me, group] = mem.attend_low[:, :, block_of(me, LANES)]
        return copies

    def start_expand_columns():
        copies = []
        for mask in masks:
            copy = push(
                mem.expand_low.at[:, feeds.at(mask)],
                mem.expand_all.at[:, me, group],
                mem.column_send.at[1, mask],
                mem.column_recv.at[1, mask],
                feeds.place(mask),
            )
            copy.start()
            copies.append(copy)
        mem.expand_all[:, me, group] = mem.expand_low[:, feeds.index]
        return copies

    def expand_part_of(array, which):
        def part_of(part):
            return array.at[which, pl.ds(4 * lax.div(part, 2), 4), pl.ds(2 * lax.rem(part, 2), 2)]

        return part_of

    def line_gather(row, part_of):
        return LineGather(part_of, mem.line_send.at[row], mem.line_recv.at[row], me, group)

    def quad_gather(row, part_of):
        return QuadGather(part_of, mem.line_send.at[row], mem.line_recv.at[row], me, group)

    def gather(team, phase, all_rows):
        return Gather(
            team,
            mem.own_rows.at[phase],
            all_rows,
            mem.gather_send.at[phase],
            mem.gather_recv.at[phase],
        )

    def scatter(team, phase):
        return Scatter(
            team,
            (mem.whole, mem.keep, mem.near_from, mem.near, mem.far_from, mem.far),
            mem.near_send.at[phase],
            mem.near_recv.at[phase],
            mem.far_send.at[phase],
            mem.far_recv.at[phase],
        )

    attend_columns = start_attend_columns()
    line_output = line_gather(1, lambda part: mem.output_full.at[block_of(batch * me + part, share)])
    line_output.start()
    facts = Gather(heads, mem.facts_own, mem.facts_all, mem.facts_send, mem.facts_recv)
    facts.start()
    for copy in attend_columns:
        copy.wait_recv()
    line_attend = line_gather(0, lambda part: mem.attend_all.at[:, :, part])
    line_attend.start()
    acts = gather(heads, 0, mem.act_one)
    acts.start()
    for chip in (1, 2, 3):
        facts.pass_on(chip)
    for chip in (0, 1, 2, 3):
        facts.complete(chip)
    facts.finish()
    step_rows = mem.facts_own.shape[0]
    half = HEAD_DIM // 2
    count = jnp.zeros((8, LANES), WIDE)
    for slot in range(seq):
        columns = slice(slot * rows, (slot + 1) * rows)
        start = slot * step_rows
        mem.cosine[:, columns] = mem.facts_all[start : start + half]
        mem.sine[:, columns] = mem.facts_all[start + half : start + 2 * half]
        labels = mem.facts_all[start + 2 * half : start + 2 * half + 8]
        mem.labels[:, columns] = labels
        count = count + labels
    mem.count[group] = count
    count_copies = []
    for step in range(1, batch):
        copy = push(
            mem.count.at[group],
            mem.count.at[group],
            mem.count_send.at[step],
            mem.count_recv.at[step],
            (me, lax.rem(group + step, batch)),
        )
        copy.start()
        count_copies.append(copy)

    def mark(block, unused):
        span = block_of(block, pair)
        row = lax.broadcasted_iota(jnp.int32, (HEAD_DIM, pair), 0)
        third = lax.div(row, VARIATES)
        variate = lax.rem(row, VARIATES).astype(WIDE)
        key_label, query_label = mem.labels[0:1, span], mem.labels[1:2, span]
        ones = jnp.ones((1, pair), WIDE)
        last = 3 * VARIATES
        hidden_keys = (key_label < 0.0).astype(WIDE)
        mem.key_marks[:, span] = jnp.where(
            third < 3,
            (key_label == variate).astype(WIDE),
            pick(row, {last: ones, last + 1: ones, last + 2: ones, last + 3: hidden_keys}),
        ).astype(LOW)
        query_marks = (query_label == variate).astype(WIDE)
        mem.sum_marks[:, span] = jnp.where(
            row < VARIATES, query_marks, pick(row, {VARIATES: ones})
        ).astype(LOW)
        for head in range(HEADS_HERE):
            number = me * HEADS_HERE + head
            other = jnp.full((HEAD_DIM, pair), ins.bias[1, number], WIDE)
            more = thirds(jnp.full((HEAD_DIM, pair), ins.bias[0, number], WIDE) - other)
            other = thirds(other)
            mem.query_turned[head, HEAD_DIM:, span] = jnp.where(
                third < 3,
                query_marks * jnp.where(third == 0, more[0], jnp.where(third == 1, more[1], more[2])),
                pick(row, {last: other[0], last + 1: other[1], last + 2: other[2], last + 3: MASKED}),
            ).astype(LOW)
        return unused

    lax.fori_loop(0, length // pair, mark, 0)
    acts.pass_on(1)
    acts.pass_on(2)
    line_output.land()
    outputs = Gather(heads, None, mem.output_full, mem.output_send, mem.output_recv)
    outputs.start()
    acts.pass_on(3)
    for chip in range(4):
        acts.complete(chip)
    acts.finish()
    line_attend.land()

    expand_columns = start_expand_columns()
    line_reduce = quad_gather(4, lambda part: mem.reduce_all.at[part])
    line_reduce.start_z()
    line_reduce.start_y()
    line_expand = [
        quad_gather(2 + which, expand_part_of(mem.expand_all, which)) for which in range(2)
    ]

    def attend_matrix(which):
        return mem.attend_all[which].reshape(D, LANES)

    def project(block, unused):
        span = block_of(block, pair)
        act = mem.act_one[span, :]
        cosine, sine = mem.cosine[:, span], mem.sine[:, span]
        query = turn_rows(dot(act, attend_matrix(0)).T, cosine, sine).astype(LOW)
        query = (query.astype(WIDE) * HEAD_DIM ** (-0.5)).astype(LOW)
        key = turn_rows(dot(act, attend_matrix(1)).T, cosine, sine).astype(LOW)
        value = dot(act, attend_matrix(2)).T.astype(LOW)
        mem.key_turned[:, span] = key
        mem.value_turned[:, span] = value

        for head in range(HEADS_HERE):
            features = slice(head * HEAD_DIM, (head + 1) * HEAD_DIM)
            mem.query_turned[head, :HEAD_DIM, span] = query[features]
            whole = jnp.concatenate([key[features], mem.key_marks[:, span]], axis=0)
            mem.key_heads[head, span, :] = whole.T
        return unused

    lax.fori_loop(0, length // pair, project, 0)
    outputs.pass_on(1)
    outputs.pass_on(2)
    for copy in expand_columns:
        copy.wait_recv()
    line_expand[0].start_z()
    line_expand[0].start_y()

    core = lax.rem(me, 2)

    def mixed_copy(chip, which):
        other = 2 * chip_of(heads, chip) + which
        slot = 2 * chip + lax.rem(which + core, 2)
        return push(
            mem.mixed_out.at[block_of(other, rows)],
            mem.mixed_rows.at[:, block_of(me, LANES)],
            mem.mixed_send.at[slot],
            mem.mixed_recv.at[slot],
            (other, group),
        )

    def attend_block(chip):
        columns = block_of(chip_of(heads, chip), pair)
        for head in range(HEADS_HERE):
            span = slice(head * HEAD_DIM, (head + 1) * HEAD_DIM)
            scores = dot(mem.key_heads[head], mem.query_turned[head, :, columns])
            top = jnp.floor(jnp.max(scores, axis=0, keepdims=True))
            powers = jnp.exp(scores - top)
            probs = powers * (1.0 / jnp.sum(powers, axis=0, keepdims=True))
            rounded = probs.astype(LOW)
            mem.probs[head, :, columns] = rounded
            residue = (probs - rounded.astype(WIDE)).astype(LOW)
            coarse = dot(mem.value_turned[span, :], rounded)
            mem.exact[span, columns] = coarse + dot(mem.value_turned[span, :], residue)
            mem.mixed_wide[span, :] = coarse
        mixed = mem.mixed_wide[...].astype(LOW)
        mem.mixed_turned[:, columns] = mixed
        mem.mixed_out[columns, :] = mixed.T

    def attend_step(step, unused):
        chip = lax.rem(step + 1, 4)
        attend_block(chip)
        for which in range(2):

            @pl.when(jnp.logical_or(chip > 0, core != which))
            def _():
                mixed_copy(chip, which).start()

        at_step(step, 1, lambda: outputs.pass_on(3))
        return unused

    lax.fori_loop(0, 4, attend_step, 0)
    line_expand[1].start_z()
    line_expand[1].start_y()
    mem.mixed_rows[:, block_of(me, LANES)] = mem.mixed_out[block_of(me, rows), :]
    for chip in range(4):
        outputs.complete(chip)
    outputs.finish()

    def wait_pieces(copy):
        for mask in range(1, seq):
            copy(mask).wait()

    def mixed_wait(mask):
        other = heads.at(mask)
        return push(
            mem.mixed_out.at[block_of(other, rows)],
            mem.mixed_rows.at[:, block_of(other, LANES)],
            mem.mixed_send.at[mask],
            mem.mixed_recv.at[mask],
            (other, group),
        )

    wait_pieces(mixed_wait)
    middle = ins.inputs[...].astype(WIDE) + dot(mem.mixed_rows[...], mem.output_full[...])
    mem.middle[...] = middle
    unit_two, scale_two = norm_rows(middle)
    mem.own_rows[1] = (unit_two * ins.gains[1:2, :]).astype(LOW)
    acts = gather(feeds, 1, mem.act_two)
    acts.start()
    line_reduce.pass_on()
    line_expand[0].pass_on()

    def split_heads(block, unused):
        span = block_of(block, pair)
        row = lax.broadcasted_iota(jnp.int32, (HEAD_DIM, pair), 0)
        value_marks = jnp.where(row < 3, 1.0, 0.0).astype(LOW)
        for head in range(HEADS_HERE):
            features = slice(head * HEAD_DIM, (head + 1) * HEAD_DIM)
            value = mem.value_turned[features, span]
            mem.value_heads[head, span, :] = jnp.concatenate([value, value_marks], axis=0).T
            query = mem.query_turned[head, :HEAD_DIM, span]
            whole = jnp.concatenate([query, mem.sum_marks[:, span]], axis=0)
            mem.query_heads[head, span, :] = whole.T
        return unused

    lax.fori_loop(0, length // pair, split_heads, 0)
    line_expand[0].land()

    def expand_matrix(which):
        return mem.expand_all[which].reshape(D, hidden_width)

    def reduce_matrix():
        return mem.reduce_all[...].reshape(hidden_width, D)

    def feed_gate(chip):
        span = block_of(chip_of(feeds, chip), pair)
        mem.by_gate[span, :] = dot(mem.act_two[span, :], expand_matrix(0))

    each_chip(acts, feed_gate, {2: [line_expand[1].pass_on]})
    line_expand[1].land()
    line_reduce.land()
    sums = scatter(feeds, 1)

    def feed_down(step, unused):
        chip = lax.rem(step + 1, 4)
        span = block_of(chip_of(feeds, chip), pair)
        gate = mem.by_gate[span, :]
        up = dot(mem.act_two[span, :], expand_matrix(1))
        sigmoid = 1.0 / (1.0 + jnp.exp(-gate))
        swish = gate * sigmoid
        mem.by_up[span, :] = swish
        mem.by_gate[span, :] = up * sigmoid * (1.0 + gate * (1.0 - sigmoid))
        hidden = (swish * up).astype(LOW)
        mem.hidden[span, :] = hidden
        sums.put(chip, dot(hidden, reduce_matrix()))
        at_step(step, 1, lambda: sums.combine(1))
        at_step(step, 2, lambda: sums.combine(2))
        return unused

    lax.fori_loop(0, 4, feed_down, 0)
    sums.combine(3)

    for block in range(length // pair):
        span = block_of(block, pair)
        mem.hidden_turned[:, span] = mem.hidden[span, :].T
        mem.act_two_turned[:, span] = mem.act_two[span, :].T
    output = mem.middle[...] + sums.total()
    outs.layer_output[...] = output
    for copy in count_copies:
        copy.wait()
    count_all = jnp.sum(
        mem.count[0, 2:3] + mem.count[1, 2:3] + mem.count[2, 2:3] + mem.count[3, 2:3],
        axis=1,
        keepdims=True,
    )
    error = jnp.where(mem.scored[:, 0:1] > 0.0, output - ins.teacher[...].astype(WIDE), 0.0)
    mem.squares[1:2, :] = jnp.sum(error * error, axis=0, keepdims=True)
    grad_out = error * (2.0 / (count_all * D))
    mem.grad_own[...] = grad_out
    mem.own_rows[2] = grad_out.astype(LOW)
    acts = gather(feeds, 2, mem.branch)
    acts.start()

    sums = scatter(feeds, 2)

    def feed_back(chip):
        span = block_of(chip_of(feeds, chip), pair)
        grad_hidden = dot_turned(mem.branch[span, :], reduce_matrix())
        grad_gate = (grad_hidden * mem.by_gate[span, :]).astype(LOW)
        grad_up = (grad_hidden * mem.by_up[span, :]).astype(LOW)
        mem.grad_gate[span, :] = grad_gate
        mem.grad_up[span, :] = grad_up
        sums.put(
            chip,
            dot_turned(grad_gate, expand_matrix(0)) + dot_turned(grad_up, expand_matrix(1)),
        )

    each_chip(
        acts, feed_back, {2: [lambda: sums.combine(1)], 3: [lambda: sums.combine(2)]}
    )
    sums.combine(3)

    def line_scatter(row, part_of, landing):
        return LineScatter(
            part_of, landing, mem.back_send.at[row], mem.back_recv.at[row], me, group
        )

    def quad_scatter(row, part_of, landing):
        return QuadScatter(
            part_of, landing, mem.back_send.at[row], mem.back_recv.at[row], me, group
        )

    def reduce_grad(part, unused):
        mem.reduce_grad[part] = dot(
            mem.hidden_turned[block_of(part, rows), :], mem.branch[...]
        ).astype(LOW)
        return unused

    lax.fori_loop(0, batch, reduce_grad, 0)
    back_reduce = quad_scatter(0, lambda part: mem.reduce_grad.at[part], mem.reduce_land)
    back_reduce.start_far()
    back_reduce.start_near()

    def expand_grad(which):
        grads = (mem.grad_gate, mem.grad_up)[which]

        def one_block(block, unused):
            products = dot(mem.act_two_turned[block_of(block, pair), :], grads[...]).astype(LOW)
            mem.expand_grad[which, pl.ds(2 * block, 2)] = products.reshape(
                2, batch, share, hidden_width
            )
            return unused

        lax.fori_loop(0, seq // 2, one_block, 0)
        line = quad_scatter(
            1 + which, expand_part_of(mem.expand_grad, which), mem.expand_land.at[which]
        )
        return line

    back_expand = []
    for which in range(2):
        back_expand.append(expand_grad(which))
        back_expand[which].start_far()
        back_expand[which].start_near()
    grad_act = sums.total()
    unit_two, scale_two = norm_rows(mem.middle[...])
    gain = ins.gains[1:2, :]
    grad_unit = grad_act * gain
    mem.gains[1:2, :] = jnp.sum(grad_act * unit_two, axis=0, keepdims=True)
    grad_middle = mem.grad_own[...] + scale_two * (
        grad_unit - unit_two * jnp.mean(grad_unit * unit_two, axis=-1, keepdims=True)
    )
    mem.grad_own[...] = grad_middle
    mem.own_rows[3] = grad_middle.astype(LOW)
    grad_mixed = dot(mem.output_full[...], grad_middle.T.astype(LOW)).astype(LOW)
    mem.grad_mixed_out[...] = grad_mixed.reshape(seq, LANES, rows)

    def grad_copy(mask, back=False):
        return push(
            mem.grad_mixed_out.at[heads.at(mask)],
            mem.grad_mixed.at[:, block_of(heads.at(mask) if back else me, rows)],
            mem.mixed_send.at[8 + mask],
            mem.mixed_recv.at[8 + mask],
            heads.place(mask),
        )

    for mask in masks:
        grad_copy(mask).start()
    mem.grad_mixed[:, block_of(me, rows)] = mem.grad_mixed_out[me]
    back_reduce.pass_on()

    wait_pieces(lambda mask: grad_copy(mask, True))
    acts = gather(heads, 3, mem.grad_attn)
    acts.start()
    back_attend = [
        line_scatter(
            4 + which,
            lambda part, which=which: mem.attend_grad.at[which, :, part],
            mem.attend_land.at[which],
        )
        for which in range(3)
    ]

    def attend_grad(which):
        grads = dot(mem.grad_project[which], mem.act_one[...])
        mem.attend_grad[which] = grads.T.astype(LOW).reshape(seq, batch, share, LANES)
        back_attend[which].start()

    lane = lax.broadcasted_iota(jnp.int32, (pair, LANES), 1)

    def grad_rows(block, unused):
        span = block_of(block, pair)
        whole = mem.grad_mixed[:, span].astype(WIDE).T
        for head in range(HEADS_HERE):
            mem.grad_heads[head, span, :] = jnp.where(lax.div(lane, HEAD_DIM) == head, whole, 0.0).astype(LOW)
        return unused

    lax.fori_loop(0, length // pair, grad_rows, 0)

    def value_back(block, unused):
        span = block_of(block, pair)
        total = dot(mem.probs[0, span, :], mem.grad_heads[0])
        for head in range(1, HEADS_HERE):
            total = total + dot(mem.probs[head, span, :], mem.grad_heads[head])
        mem.grad_project[2, :, span] = total.T.astype(LOW)
        return unused

    lax.fori_loop(0, length // pair, value_back, 0)
    back_expand[0].pass_on()
    attend_grad(2)

    def score_back(block, unused):
        columns = block_of(block, pair)
        row = lax.broadcasted_iota(jnp.int32, (HEAD_DIM, pair), 0)
        grads = mem.grad_mixed[:, columns]
        delta = grads.astype(WIDE) * mem.exact[:, columns]
        for head in range(HEADS_HERE):
            span = slice(head * HEAD_DIM, (head + 1) * HEAD_DIM)
            pieces = thirds(-jnp.sum(delta[span], axis=0, keepdims=True))
            marks = pick(row, dict(enumerate(pieces))).astype(LOW)
            change = dot(mem.value_heads[head], jnp.concatenate([grads[span], marks], axis=0))
            mem.probs[head, :, columns] = (mem.probs[head, :, columns].astype(WIDE) * change).astype(LOW)
        return unused

    lax.fori_loop(0, length // pair, score_back, 0)
    mem.bias_sums[...] = jnp.zeros_like(mem.bias_sums)
    scale = HEAD_DIM ** (-0.5)

    def project_grads(block, unused):
        span = block_of(block, pair)
        cosine, sine = mem.cosine[:, span], -mem.sine[:, span]
        queries, keys = [], []
        for head in range(HEADS_HERE):
            features = slice(head * HEAD_DIM, (head + 1) * HEAD_DIM)
            queries.append(dot(mem.key_turned[features, :], mem.probs[head, :, span]) * scale)
            sums = dot(mem.probs[head, span, :], mem.query_heads[head]).T
            keys.append(sums[:HEAD_DIM])
            by_variate = sums[HEAD_DIM : HEAD_DIM + VARIATES]
            same = by_variate * mem.key_marks[:VARIATES, span].astype(WIDE)
            mem.bias_sums[head : head + 1, :] += jnp.sum(same, axis=0, keepdims=True)
            total = sums[HEAD_DIM + VARIATES : HEAD_DIM + VARIATES + 1]
            mem.bias_sums[HEADS_HERE + head : HEADS_HERE + head + 1, :] += total
        mem.grad_project[0, :, span] = turn_rows(jnp.concatenate(queries, axis=0), cosine, sine).astype(LOW)
        mem.grad_project[1, :, span] = turn_rows(jnp.concatenate(keys, axis=0), cosine, sine).astype(LOW)
        return unused

    lax.fori_loop(0, length // pair, project_grads, 0)
    back_expand[1].pass_on()
    for which in range(2):
        attend_grad(which)
    acts.pass_on(1)
    acts.pass_on(2)
    sums = scatter(heads, 3)

    def project_back(step, unused):
        chip = lax.rem(step + 1, 4)
        span = block_of(chip_of(heads, chip), pair)
        total = jnp.zeros((pair, D), WIDE)
        for which in range(3):
            total = total + dot_turned(mem.grad_project[which, :, span].T, attend_matrix(which))
        sums.put(chip, total)
        at_step(step, 1, lambda: sums.combine(1))
        at_step(step, 2, lambda: sums.combine(2))
        return unused

    lax.fori_loop(0, 4, project_back, 0)
    sums.combine(3)
    acts.pass_on(3)
    for chip in range(4):
        acts.complete(chip)
    acts.finish()
    mem.output_grad[...] = (
        dot(mem.mixed_turned[...], mem.grad_attn[...]).astype(LOW).reshape(mem.output_grad.shape)
    )
    back_output = line_scatter(3, lambda part: mem.output_grad.at[part], mem.output_land)
    back_output.start()

    column_copies = []
    mem.squares[0:1, :] = jnp.zeros((1, D), WIDE)

    def add_squares(total):
        flat = total.reshape(-1, total.shape[-1])
        width = flat.shape[1]
        mem.squares[0:1, :width] += jnp.sum(flat * flat, axis=0, keepdims=True)

    def store_whole(total, out):
        out[...] = total
        add_squares(total)

    back_reduce.land()
    store_whole(
        mem.reduce_grad[quad].astype(WIDE)
        + mem.reduce_land[0].astype(WIDE)
        + mem.reduce_land[2].astype(WIDE),
        outs.reduce_share,
    )
    def expand_shares(which):
        back_expand[which].land()
        own = expand_part_of(mem.expand_grad, which)(quad)

        def one_block(block, unused):
            total = (
                own[block].astype(WIDE)
                + mem.expand_land[which, 0, block].astype(WIDE)
                + mem.expand_land[which, 2, block].astype(WIDE)
            )
            mem.expand_part[which, block] = total.astype(LOW)
            add_squares(total)
            return unused

        lax.fori_loop(0, 4, one_block, 0)
        for mask in masks:
            other = feeds.at(mask)
            copy = push(
                mem.expand_part.at[which, lax.rem(other, 4), lax.div(other, 4)],
                mem.expand_share.at[which, feeds.index],
                mem.share_send.at[which, mask],
                mem.share_recv.at[which, mask],
                feeds.place(mask),
            )
            copy.start()
            column_copies.append(copy)
        mem.expand_share[which, feeds.index] = mem.expand_part[
            which, lax.rem(feeds.index, 4), lax.div(feeds.index, 4)
        ]

    for which in range(2):
        expand_shares(which)

    def attend_shares(which):
        back_attend[which].land()
        total = back_attend[which].total()
        mem.attend_part[which] = total.astype(LOW)
        add_squares(total)

    attend_shares(2)
    grad_act = sums.total()
    unit_one, scale_one = norm_rows(ins.inputs[...].astype(WIDE))
    gain = ins.gains[0:1, :]
    grad_unit = grad_act * gain
    mem.gains[0:1, :] = jnp.sum(grad_act * unit_one, axis=0, keepdims=True)
    grad_input = mem.grad_own[...] + scale_one * (
        grad_unit - unit_one * jnp.mean(grad_unit * unit_one, axis=-1, keepdims=True)
    )
    outs.input_gradient[...] = grad_input * (count_all * D)
    outs.count[...] = jnp.broadcast_to(count_all, (8, LANES))

    for which in range(2):
        attend_shares(which)
    for mask in masks:
        copy = push(
            mem.attend_part.at[:, heads.at(mask)],
            outs.attend_share.at[:, :, block_of(me, LANES)],
            mem.share_send.at[2, mask],
            mem.share_recv.at[2, mask],
            heads.place(mask),
        )
        copy.start()
        column_copies.append(copy)
    outs.attend_share[:, :, block_of(me, LANES)] = mem.attend_part[:, me]
    back_output.land()
    store_whole(back_output.total(), outs.output_share)

    lane = lax.broadcasted_iota(jnp.int32, (1, LANES), 1)
    lines = [
        mem.gains[which : which + 1, start : start + LANES]
        for which in range(2)
        for start in range(0, D, LANES)
    ]
    bias_line = jnp.zeros((1, LANES), WIDE)
    for row in range(2 * HEADS_HERE):
        place = row // HEADS_HERE * HEADS + me * HEADS_HERE + row % HEADS_HERE
        line = mem.bias_sums[row : row + 1, :]
        if row >= HEADS_HERE:
            line = line - mem.bias_sums[row - HEADS_HERE : row - HEADS_HERE + 1, :]
        amount = jnp.sum(line, axis=1, keepdims=True)
        bias_line = bias_line + jnp.where(lane == place, amount, 0.0)
    amounts = jnp.sum(mem.squares[0:2, :], axis=1, keepdims=True)
    amount_line = jnp.where(lane == 0, amounts[0:1], 0.0) + jnp.where(lane == 1, amounts[1:2], 0.0)
    lines += [bias_line, amount_line, jnp.zeros((6, LANES), WIDE)]
    mem.plane_totals[me] = jnp.concatenate(lines, axis=0)
    plane_copies = []
    for mask in masks:
        copy = push(
            mem.plane_totals.at[me],
            mem.plane_totals.at[me],
            mem.total_send.at[0, mask],
            mem.total_recv.at[0, mask],
            (flip(me, mask), group),
        )
        copy.start()
        plane_copies.append(copy)
    for copy in plane_copies:
        copy.wait()
    mem.line_totals[group] = jnp.sum(mem.plane_totals[...], axis=0)
    total_copies = []
    for step in range(1, batch):
        copy = push(
            mem.line_totals.at[group],
            mem.line_totals.at[group],
            mem.total_send.at[1, step],
            mem.total_recv.at[1, step],
            (me, lax.rem(group + step, batch)),
        )
        copy.start()
        total_copies.append(copy)
    for copy in total_copies:
        copy.wait()
    outs.totals[...] = jnp.sum(mem.line_totals[...], axis=0)
    for copy in column_copies:
        copy.wait()
    for which in range(2):
        for block in range(blocks):
            owner, part = feed_block(block)
            outs.expand_share[which, :, block * LANES : (block + 1) * LANES] = mem.expand_share[
                which, owner, :, part * LANES : (part + 1) * LANES
            ]
    for copies in (attend_columns, expand_columns):
        for copy in copies:
            copy.wait_send()
    for line in [line_attend, line_output, line_reduce] + line_expand:
        line.finish()
    for line in [back_output, back_reduce] + back_attend + back_expand:
        line.finish()


def call_layer(seq, batch, inputs, teacher, lengths, variates, observed, turns, bias, gains, attend, output, expand, reduce):
    rows, share, hidden = inputs.shape[0], attend.shape[1], expand.shape[2] // seq
    length, pair, chips = rows * seq, 2 * rows, seq // 2
    low = lambda *shape: pltpu.VMEM(shape, LOW)
    wide = lambda *shape: pltpu.VMEM(shape, WIDE)
    sems = lambda *shape: pltpu.SemaphoreType.DMA(shape)
    in_names = ["inputs", "teacher", "lengths", "variates", "observed", "turns", "bias", "gains"]
    in_names += ["attend", "output", "expand", "reduce"]
    outs = dict(
        layer_output=((rows, D), WIDE),
        input_gradient=((rows, D), WIDE),
        totals=((TOTAL_ROWS, LANES), WIDE),
        count=((8, LANES), WIDE),
        attend_share=((3, share, D), LOW),
        output_share=((output.shape[0], D), WIDE),
        expand_share=((2, share, hidden * seq), LOW),
        reduce_share=((reduce.shape[0], D), WIDE),
    )
    scratch = dict(
        gains=wide(2, D),
        squares=wide(8, D),
        plane_totals=wide(seq, TOTAL_ROWS, LANES),
        line_totals=wide(batch, TOTAL_ROWS, LANES),
        attend_low=low(3, share, D),
        expand_low=low(2, seq, share, hidden),
        attend_all=low(3, seq, batch, share, LANES),
        output_full=low(D, D),
        expand_all=low(2, seq, batch, share, hidden),
        reduce_all=low(batch, reduce.shape[0], D),
        own_rows=low(4, rows, D),
        act_one=low(length, D),
        act_two=low(length, D),
        branch=low(length, D),
        grad_attn=low(length, D),
        facts_own=wide(turns.shape[0] + 8, LANES),
        facts_all=wide(seq * (turns.shape[0] + 8), LANES),
        scored=wide(rows, LANES),
        cosine=wide(HEAD_DIM // 2, length),
        sine=wide(HEAD_DIM // 2, length),
        labels=wide(8, length),
        key_marks=low(HEAD_DIM, length),
        count=wide(batch, 8, LANES),
        query_turned=low(HEADS_HERE, LANES, length),
        key_turned=low(LANES, length),
        value_turned=low(LANES, length),
        key_heads=low(HEADS_HERE, length, LANES),
        value_heads=low(HEADS_HERE, length, LANES),
        query_heads=low(HEADS_HERE, length, LANES),
        grad_heads=low(HEADS_HERE, length, LANES),
        grad_mixed=low(LANES, length),
        grad_mixed_out=low(seq, LANES, rows),
        probs=low(HEADS_HERE, length, length),
        mixed_out=low(length, LANES),
        mixed_rows=low(rows, D),
        sum_marks=low(HEAD_DIM, length),
        hidden_turned=low(hidden, length),
        act_two_turned=low(D, length),
        exact=wide(LANES, length),
        mixed_wide=wide(LANES, pair),
        mixed_turned=low(LANES, length),
        whole=wide(pair, D),
        keep=wide(chips, rows, D),
        near_from=low(chips, rows, D),
        near=low(chips, rows, D),
        far_from=low(chips, rows, D),
        far=low(chips, rows, D),
        middle=wide(rows, D),
        grad_own=wide(rows, D),
        by_up=wide(length, hidden),
        by_gate=wide(length, hidden),
        hidden=low(length, hidden),
        grad_gate=low(length, hidden),
        grad_up=low(length, hidden),
        bias_sums=wide(8, pair),
        grad_project=low(3, LANES, length),
        reduce_grad=low(batch, reduce.shape[0], D),
        expand_grad=low(2, seq, batch, share, hidden),
        output_grad=low(batch, output.shape[0], D),
        attend_grad=low(3, seq, batch, share, LANES),
        reduce_land=low(3, reduce.shape[0], D),
        expand_land=low(2, 3, 4, 2, share, hidden),
        output_land=low(3, output.shape[0], D),
        attend_land=low(3, 3, seq, share, LANES),
        expand_part=low(2, 4, 2, share, hidden),
        expand_share=low(2, seq, share, hidden),
        attend_part=low(3, seq, share, LANES),
        stage_sem=sems(5 + 2 * (expand.shape[2] // D)),
        total_send=sems(2, seq),
        total_recv=sems(2, seq),
        column_send=sems(2, seq),
        column_recv=sems(2, seq),
        line_send=sems(5, batch),
        line_recv=sems(5, batch),
        facts_send=sems(seq),
        facts_recv=sems(seq),
        gather_send=sems(4, seq),
        gather_recv=sems(4, seq),
        count_send=sems(batch),
        count_recv=sems(batch),
        near_send=sems(4, chips),
        near_recv=sems(4, chips),
        far_send=sems(4, chips),
        far_recv=sems(4, chips),
        back_send=sems(7, batch),
        back_recv=sems(7, batch),
        output_send=sems(seq),
        output_recv=sems(seq),
        mixed_send=sems(2 * seq),
        mixed_recv=sems(2 * seq),
        share_send=sems(3, seq),
        share_recv=sems(3, seq),
    )

    places = dict.fromkeys(("attend", "output", "expand", "reduce"), pl.BlockSpec(memory_space=pl.ANY))
    places["bias"] = places["lengths"] = IN_SMEM

    def kernel(*refs):
        groups, start = [], 0
        for names in (in_names, outs, scratch):
            names = list(names)
            groups.append(types.SimpleNamespace(**dict(zip(names, refs[start : start + len(names)]))))
            start += len(names)
        layer_kernel(seq, batch, *groups)

    results = pl.pallas_call(
        kernel,
        out_shape=[jax.ShapeDtypeStruct(*out) for out in outs.values()],
        in_specs=[places.get(name, IN_VMEM) for name in in_names],
        out_specs=[IN_VMEM] * len(outs),
        scratch_shapes=list(scratch.values()),
        compiler_params=pltpu.CompilerParams(
            collective_id=0, has_side_effects=True, vmem_limit_bytes=63 * MIB
        ),
        name="layer",
    )(inputs, teacher, lengths, variates, observed, turns, bias, gains, attend, output, expand, reduce)
    return types.SimpleNamespace(**dict(zip(outs, results)))


def update_kernel(smalls, ins, small_outs, outs, olds, shares, news, copies, in_sems, out_sems):
    totals, count, gains, gains_first, gains_second, bias, bias_first, bias_second = smalls
    order = (2, 3, 0, 1)
    comes = []
    for place, number in enumerate(order):
        pairs = list(zip(ins[4 + 3 * number : 7 + 3 * number], olds[3 * number : 3 * number + 3]))
        pairs.append((ins[number], shares[number]))
        comes.append(
            [
                pltpu.make_async_copy(source, target, in_sems.at[4 * place + part])
                for part, (source, target) in enumerate(pairs)
            ]
        )
    for copy in sum(comes, []):
        copy.start()
    goes = [
        pltpu.make_async_copy(ins[16 + part], outs[part], out_sems.at[part]) for part in range(2)
    ]
    for copy in goes:
        copy.start()
    gains_total = jnp.concatenate(
        [
            jnp.concatenate([totals[row + i : row + i + 1, :] for i in range(D // LANES)], axis=1)
            for row in (0, D // LANES)
        ],
        axis=0,
    )
    row = 2 * D // LANES
    bias_total = jnp.concatenate(
        [totals[row : row + 1, :HEADS], totals[row : row + 1, HEADS : 2 * HEADS]], axis=0
    )
    row += 1

    def sum_all(values):
        return jnp.sum(jnp.sum(values, axis=0, keepdims=True), axis=1, keepdims=True)

    squares = (
        totals[row : row + 1, 0:1] + sum_all(gains_total * gains_total) + sum_all(bias_total * bias_total)
    )
    grad_norm = jnp.sqrt(squares)
    clip = jnp.minimum(1.0, CLIP_NORM / grad_norm)
    small_outs[0][...] = totals[row : row + 1, 1:2] / (count[0:1, 0:1] * D)
    small_outs[1][...] = grad_norm
    rates = (RATE_ATTEND, RATE_OUTPUT, RATE_EXPAND, RATE_REDUCE)
    for place, number in enumerate(order):
        for copy in comes[place]:
            copy.wait()
        weight, first, second = olds[3 * number : 3 * number + 3]
        new, first_new, second_new = news[3 * number : 3 * number + 3]
        scale = clip.reshape((1,) * weight.ndim)
        new[...], first_new[...], second_new[...] = adam_step(
            weight[...],
            first[...],
            second[...],
            shares[number][...].astype(WIDE) * scale,
            rates[number],
            WEIGHT_DECAY,
        )
        copies[number][...] = new[...].astype(LOW)
        for part, source in enumerate((new, copies[number], first_new, second_new)):
            copy = pltpu.make_async_copy(
                source, outs[2 + 4 * number + part], out_sems.at[2 + 4 * number + part]
            )
            copy.start()
            goes.append(copy)
    for number, (old, total, rate) in enumerate(
        (
            ((gains, gains_first, gains_second), gains_total, RATE_GAINS),
            ((bias, bias_first, bias_second), bias_total, RATE_BIAS),
        )
    ):
        new, first_new, second_new = small_outs[2 + 3 * number : 5 + 3 * number]
        new[...], first_new[...], second_new[...] = adam_step(
            old[0][...], old[1][...], old[2][...], total * clip, rate, 0.0
        )
    for copy in goes:
        copy.wait()


def call_update(done, shares, smalls, olds):
    in_hbm = pl.BlockSpec(memory_space=pl.ANY)
    smalls = [done.totals, done.count] + smalls
    ins = shares + olds + [done.layer_output, done.input_gradient]
    one = jax.ShapeDtypeStruct((1, 1), WIDE)
    small_outs = [one, one] + smalls[2:]
    outs = [(done.layer_output, WIDE), (done.input_gradient, WIDE)]
    for weight in olds[::3]:
        outs += [(weight, dtype) for dtype in (WIDE, LOW, WIDE, WIDE)]
    parts = [smalls, ins, small_outs, outs, olds, shares, olds, olds[::3]]

    def kernel(*refs):
        groups, start = [], 0
        for part in parts:
            groups.append(refs[start : start + len(part)])
            start += len(part)
        update_kernel(*groups, *refs[start:])

    results = pl.pallas_call(
        kernel,
        out_shape=[jax.ShapeDtypeStruct(array.shape, WIDE) for array in small_outs]
        + [jax.ShapeDtypeStruct(array.shape, dtype) for array, dtype in outs],
        in_specs=[IN_VMEM] * len(smalls) + [in_hbm] * len(ins),
        out_specs=[IN_VMEM] * len(small_outs) + [in_hbm] * len(outs),
        scratch_shapes=[pltpu.VMEM(array.shape, WIDE) for array in olds]
        + [pltpu.VMEM(array.shape, array.dtype) for array in shares]
        + [pltpu.VMEM(array.shape, WIDE) for array in olds]
        + [pltpu.VMEM(array.shape, LOW) for array in olds[::3]]
        + [pltpu.SemaphoreType.DMA((16,)), pltpu.SemaphoreType.DMA((18,))],
        compiler_params=pltpu.CompilerParams(vmem_limit_bytes=63 * MIB),
        name="update",
    )(*smalls, *ins)
    return results[: len(small_outs)], results[len(small_outs) :]


def fast_body(
    seq,
    batch,
    inputs,
    teacher,
    lengths,
    variate_ids,
    time_ids,
    observed,
    attend_weight,
    output_weight,
    expand_weight,
    reduce_weight,
    norm_gains,
    variate_bias,
    attend_first,
    output_first,
    expand_first,
    reduce_first,
    gains_first,
    bias_first,
    attend_second,
    output_second,
    expand_second,
    reduce_second,
    gains_second,
    bias_second,
):
    half_dim = HEAD_DIM // 2
    frequency = jnp.exp(-math.log(ROPE_BASE) * jnp.arange(half_dim).astype(WIDE) / half_dim)
    angle = frequency[:, None] * time_ids.astype(WIDE)
    done = call_layer(
        seq,
        batch,
        inputs[0],
        teacher[0],
        lengths,
        variate_ids,
        observed,
        jnp.concatenate([jnp.cos(angle), jnp.sin(angle)]),
        variate_bias,
        norm_gains,
        attend_weight,
        output_weight,
        expand_weight,
        reduce_weight,
    )
    small, large = call_update(
        done,
        [done.attend_share, done.output_share, done.expand_share, done.reduce_share],
        [norm_gains, gains_first, gains_second, variate_bias, bias_first, bias_second],
        [attend_weight, attend_first, attend_second]
        + [output_weight, output_first, output_second]
        + [expand_weight, expand_first, expand_second]
        + [reduce_weight, reduce_first, reduce_second],
    )
    return (
        large[0][None],
        small[0].reshape(()),
        large[1][None],
        small[1].reshape(()),
    ) + tuple(large[2:] + small[2:])


def solution(mesh):
    seq, batch = mesh.shape["seq"], mesh.shape["batch"]
    body = functools.partial(fast_body, seq, batch) if fast_fits(seq, batch) else general_body
    in_specs = (
        P("batch", "seq", None),
        P("batch", "seq", None),
        P("batch"),
        P("batch", "seq"),
        P("batch", "seq"),
        P("batch", "seq"),
        P(None, ("seq", "batch"), None),
        P(("seq", "batch"), None),
        P(None, ("seq", "batch"), None),
        P(("seq", "batch"), None),
        P(),
        P(),
        P(None, ("seq", "batch"), None),
        P(("seq", "batch"), None),
        P(None, ("seq", "batch"), None),
        P(("seq", "batch"), None),
        P(),
        P(),
        P(None, ("seq", "batch"), None),
        P(("seq", "batch"), None),
        P(None, ("seq", "batch"), None),
        P(("seq", "batch"), None),
        P(),
        P(),
    )
    out_specs = (
        P("batch", "seq", None),
        P(),
        P("batch", "seq", None),
        P(),
        P(None, ("seq", "batch"), None),
        P(None, ("seq", "batch"), None),
        P(None, ("seq", "batch"), None),
        P(None, ("seq", "batch"), None),
        P(("seq", "batch"), None),
        P(("seq", "batch"), None),
        P(("seq", "batch"), None),
        P(("seq", "batch"), None),
        P(None, ("seq", "batch"), None),
        P(None, ("seq", "batch"), None),
        P(None, ("seq", "batch"), None),
        P(None, ("seq", "batch"), None),
        P(("seq", "batch"), None),
        P(("seq", "batch"), None),
        P(("seq", "batch"), None),
        P(("seq", "batch"), None),
        P(),
        P(),
        P(),
        P(),
        P(),
        P(),
    )
    return jax.shard_map(body, mesh=mesh, in_specs=in_specs, out_specs=out_specs, check_vma=False)
```

```python
import functools
import math
import types

import jax
import jax.numpy as jnp
from jax import lax
from jax.experimental import pallas as pl
from jax.experimental.pallas import tpu as pltpu
from jax.sharding import PartitionSpec as P

D = 1024
HEADS = 16
HEAD_DIM = 64
STEP = 10


NORM_EPS = 1e-05
ROPE_BASE = 10000.0
MASKED = -1e30
CLIP_NORM = 1.0
BETA_ONE = 0.9
BETA_TWO = 0.98
ADAM_EPS = 1e-08
WEIGHT_DECAY = 0.1
RATE_ATTEND = 0.03
RATE_OUTPUT = 0.5
RATE_EXPAND = 0.03
RATE_REDUCE = 0.015
RATE_GAINS = 1.0
RATE_BIAS = 0.5


def angles(times):
    half_dim = HEAD_DIM // 2
    frequency = jnp.exp(-math.log(ROPE_BASE) * jnp.arange(half_dim).astype(jnp.float32) / half_dim)
    angle_table = times.astype(jnp.float32)[..., None] * frequency
    return (jnp.cos(angle_table)[..., None, :], jnp.sin(angle_table)[..., None, :])


def rotate(values, cos_table, sin_table):
    half_dim = values.shape[-1] // 2
    first_half = values[..., :half_dim]
    second_half = values[..., half_dim:]
    return jnp.concatenate(
        [
            first_half * cos_table - second_half * sin_table,
            second_half * cos_table + first_half * sin_table,
        ],
        axis=-1,
    )


def unrotate(values, cos_table, sin_table):
    half_dim = values.shape[-1] // 2
    first_half = values[..., :half_dim]
    second_half = values[..., half_dim:]
    return jnp.concatenate(
        [
            first_half * cos_table + second_half * sin_table,
            second_half * cos_table - first_half * sin_table,
        ],
        axis=-1,
    )


def normalize(values):
    inv_scale = lax.rsqrt(jnp.mean(values * values, axis=-1, keepdims=True) + NORM_EPS)
    return (values * inv_scale, inv_scale)


def norm_back(grad_act, unit_rows, inv_scale, gain_row):
    grad_unit = grad_act * gain_row
    return inv_scale * (
        grad_unit - unit_rows * jnp.mean(grad_unit * unit_rows, axis=-1, keepdims=True)
    )


def score_block(query_rows, query_labels, key_rows, key_labels, bias_table):
    scores = jnp.einsum(
        "ihe,jhe->hij", query_rows, key_rows, preferred_element_type=jnp.float32
    ) * HEAD_DIM ** (-0.5)
    same_var = query_labels[:, None] == key_labels[None, :]
    scores = scores + jnp.where(
        same_var[None], bias_table[0][:, None, None], bias_table[1][:, None, None]
    )
    scores = jnp.where(key_labels[None, None, :] >= 0, scores, MASKED)
    return (scores, same_var)


def block_grads(
    query_rows,
    query_labels,
    grad_rows,
    lse_rows,
    delta_rows,
    key_rows,
    value_rows,
    key_labels,
    bias_table,
    need_query,
    need_keys,
):
    scores, same_var = score_block(query_rows, query_labels, key_rows, key_labels, bias_table)
    weights = jnp.exp(scores - lse_rows.T[:, :, None])
    grad_weights = jnp.einsum(
        "ihe,jhe->hij", grad_rows, value_rows, preferred_element_type=jnp.float32
    )
    grad_scores = (weights * (grad_weights - delta_rows.T[:, :, None])).astype(jnp.bfloat16)
    result = ()
    if need_query:
        grad_query = jnp.einsum(
            "hij,jhe->ihe", grad_scores, key_rows, preferred_element_type=jnp.float32
        ) * HEAD_DIM ** (-0.5)
        widened = grad_scores.astype(jnp.float32)
        bias_same = jnp.sum(jnp.where(same_var[None], widened, 0.0), axis=(1, 2))
        bias_other = jnp.sum(jnp.where(same_var[None], 0.0, widened), axis=(1, 2))
        result = result + (grad_query, jnp.stack([bias_same, bias_other]))
    if need_keys:
        grad_key = jnp.einsum(
            "hij,ihe->jhe", grad_scores, query_rows, preferred_element_type=jnp.float32
        ) * HEAD_DIM ** (-0.5)
        grad_value = jnp.einsum(
            "hij,ihe->jhe",
            weights.astype(jnp.bfloat16),
            grad_rows,
            preferred_element_type=jnp.float32,
        )
        result = result + (grad_key, grad_value)
    return result


def adam_step(weight, first_moment, second_moment, gradient, step_rate, decay_rate):
    first_moment = BETA_ONE * first_moment + (1.0 - BETA_ONE) * gradient
    second_moment = BETA_TWO * second_moment + (1.0 - BETA_TWO) * gradient * gradient
    direction = (
        first_moment
        / (1.0 - BETA_ONE**STEP)
        / (jnp.sqrt(second_moment / (1.0 - BETA_TWO**STEP)) + ADAM_EPS)
    )
    return (weight - step_rate * (direction + decay_rate * weight), first_moment, second_moment)


def general_body(
    inputs,
    teacher,
    lengths,
    variate_ids,
    time_ids,
    observed,
    attend_weight,
    output_weight,
    expand_weight,
    reduce_weight,
    norm_gains,
    variate_bias,
    attend_first,
    output_first,
    expand_first,
    reduce_first,
    gains_first,
    bias_first,
    attend_second,
    output_second,
    expand_second,
    reduce_second,
    gains_second,
    bias_second,
):
    row_count = inputs.shape[1]
    length = row_count * lax.axis_size("seq")
    block_rows = math.gcd(length, 1024)
    blocks = length // block_rows
    states = inputs[0].astype(jnp.float32)
    positions = lax.axis_index("seq") * row_count + jnp.arange(row_count, dtype=jnp.int32)
    inside = positions < lengths[0]
    scored = jnp.logical_and(inside, observed[0] == 1)
    local_count = jnp.sum(scored.astype(jnp.int32))
    count_early = lax.psum(local_count, ("seq", "batch"))
    full_attend, full_output, full_expand, full_reduce = (
        lax.all_gather(attend_weight.astype(jnp.bfloat16), ("seq", "batch"), axis=1, tiled=True),
        lax.all_gather(output_weight.astype(jnp.bfloat16), ("seq", "batch"), axis=0, tiled=True),
        lax.all_gather(expand_weight.astype(jnp.bfloat16), ("seq", "batch"), axis=1, tiled=True),
        lax.all_gather(reduce_weight.astype(jnp.bfloat16), ("seq", "batch"), axis=0, tiled=True),
    )
    unit_one, scale_one = normalize(states)
    act_one = (unit_one * norm_gains[0]).astype(jnp.bfloat16)
    project = jnp.einsum("td,cde->cte", act_one, full_attend, preferred_element_type=jnp.float32)
    cos_table, sin_table = angles(time_ids[0])
    query = rotate(project[0].reshape(row_count, HEADS, HEAD_DIM), cos_table, sin_table).astype(
        jnp.bfloat16
    )
    key_rows = (
        rotate(project[1].reshape(row_count, HEADS, HEAD_DIM), cos_table, sin_table)
        .astype(jnp.bfloat16)
        .reshape(row_count, D)
    )
    value_rows = project[2].astype(jnp.bfloat16)
    own_labels = jnp.where(inside, variate_ids[0], -1).astype(jnp.bfloat16)
    all_keys, all_values, all_labels = (
        lax.all_gather(key_rows, "seq", axis=0, tiled=True),
        lax.all_gather(value_rows, "seq", axis=0, tiled=True),
        lax.all_gather(own_labels, "seq", axis=0, tiled=True),
    )
    key_blocks = all_keys.reshape(blocks, block_rows, HEADS, HEAD_DIM)
    value_blocks = all_values.reshape(blocks, block_rows, HEADS, HEAD_DIM)
    label_blocks = all_labels.astype(jnp.float32).reshape(blocks, block_rows)
    query_labels = variate_ids[0].astype(jnp.float32)

    def sweep_top(carry, pieces):
        running, sum_exp = carry
        scores, same_var = score_block(query, query_labels, pieces[0], pieces[1], variate_bias)
        raised = jnp.maximum(running, jnp.floor(jnp.max(scores, axis=-1)))
        sum_exp = sum_exp * jnp.exp(running - raised) + jnp.sum(
            jnp.exp(scores - raised[..., None]), axis=-1
        )
        return ((raised, sum_exp), None)

    start_top = jnp.full((HEADS, row_count), MASKED, jnp.float32)
    (row_top, sum_exp), unused = lax.scan(
        sweep_top,
        (start_top, jnp.zeros((HEADS, row_count), jnp.float32)),
        (key_blocks, label_blocks),
    )
    log_total = row_top + jnp.log(sum_exp)

    def sweep_out(carry, pieces):
        coarse, finest = carry
        scores, same_var = score_block(query, query_labels, pieces[0], pieces[2], variate_bias)
        weights = jnp.exp(scores - log_total[..., None])
        rounded = weights.astype(jnp.bfloat16)
        residue = (weights - rounded.astype(jnp.float32)).astype(jnp.bfloat16)
        coarse = coarse + jnp.einsum(
            "hij,jhe->ihe", rounded, pieces[1], preferred_element_type=jnp.float32
        )
        finest = finest + jnp.einsum(
            "hij,jhe->ihe", residue, pieces[1], preferred_element_type=jnp.float32
        )
        return ((coarse, finest), None)

    zero_heads = jnp.zeros((row_count, HEADS, HEAD_DIM), jnp.float32)
    (coarse, finest), unused = lax.scan(
        sweep_out, (zero_heads, zero_heads), (key_blocks, value_blocks, label_blocks)
    )
    exact_heads = coarse + finest
    mixed = coarse.reshape(row_count, D).astype(jnp.bfloat16)
    middle = states + jnp.dot(mixed, full_output, preferred_element_type=jnp.float32)
    unit_two, scale_two = normalize(middle)
    act_two = (unit_two * norm_gains[1]).astype(jnp.bfloat16)
    gate_up = jnp.einsum("td,cdf->ctf", act_two, full_expand, preferred_element_type=jnp.float32)
    sigmoid = jax.nn.sigmoid(gate_up[0])
    hidden = (gate_up[0] * sigmoid * gate_up[1]).astype(jnp.bfloat16)
    output = middle + jnp.dot(hidden, full_reduce, preferred_element_type=jnp.float32)
    error = output - teacher[0].astype(jnp.float32)
    local_square = jnp.sum(jnp.where(scored[:, None], error * error, 0.0))
    square_total = lax.psum(local_square, ("seq", "batch"))
    count_all = count_early.astype(jnp.float32)
    loss = square_total / (count_all * D)
    grad_out = jnp.where(scored[:, None], error * (2.0 / (count_all * D)), 0.0)
    back_attend, back_output, back_expand, back_reduce = (
        lax.all_gather(attend_weight.astype(jnp.bfloat16), ("seq", "batch"), axis=1, tiled=True),
        lax.all_gather(output_weight.astype(jnp.bfloat16), ("seq", "batch"), axis=0, tiled=True),
        lax.all_gather(expand_weight.astype(jnp.bfloat16), ("seq", "batch"), axis=1, tiled=True),
        lax.all_gather(reduce_weight.astype(jnp.bfloat16), ("seq", "batch"), axis=0, tiled=True),
    )
    grad_branch = grad_out.astype(jnp.bfloat16)
    reduce_grad = jnp.einsum("tf,td->fd", hidden, grad_branch, preferred_element_type=jnp.float32)
    grad_hidden = jnp.einsum(
        "td,fd->tf", grad_branch, back_reduce, preferred_element_type=jnp.float32
    )
    grad_gate = grad_hidden * gate_up[1] * sigmoid * (1.0 + gate_up[0] * (1.0 - sigmoid))
    grad_up = grad_hidden * gate_up[0] * sigmoid
    grad_expand = jnp.stack([grad_gate, grad_up]).astype(jnp.bfloat16)
    expand_grad = jnp.einsum(
        "td,ctf->cdf", act_two, grad_expand, preferred_element_type=jnp.float32
    )
    grad_act_two = jnp.einsum(
        "ctf,cdf->td", grad_expand, back_expand, preferred_element_type=jnp.float32
    )
    expand_share, reduce_share = (
        lax.psum_scatter(expand_grad, ("seq", "batch"), scatter_dimension=1, tiled=True),
        lax.psum_scatter(reduce_grad, ("seq", "batch"), scatter_dimension=0, tiled=True),
    )
    grad_middle = grad_out + norm_back(grad_act_two, unit_two, scale_two, norm_gains[1])
    grad_attn = grad_middle.astype(jnp.bfloat16)
    output_grad = jnp.einsum("td,te->de", mixed, grad_attn, preferred_element_type=jnp.float32)
    grad_mixed = jnp.einsum(
        "te,de->td", grad_attn, back_output, preferred_element_type=jnp.float32
    ).astype(jnp.bfloat16)
    grad_heads = grad_mixed.reshape(row_count, HEADS, HEAD_DIM)
    row_delta = jnp.sum(grad_heads.astype(jnp.float32) * exact_heads, axis=-1)
    lse_rows = log_total.T
    zero_bias = jnp.zeros((2, HEADS), jnp.float32)

    def sweep_query(carry, pieces):
        part_query, part_bias = block_grads(
            query,
            query_labels,
            grad_heads,
            lse_rows,
            row_delta,
            pieces[0],
            pieces[1],
            pieces[2],
            variate_bias,
            True,
            False,
        )
        return ((carry[0] + part_query, carry[1] + part_bias), None)

    (query_total, bias_grad), unused = lax.scan(
        sweep_query, (zero_heads, zero_bias), (key_blocks, value_blocks, label_blocks)
    )
    all_query, all_grad = (
        lax.all_gather(query.reshape(row_count, D), "seq", axis=0, tiled=True),
        lax.all_gather(grad_mixed, "seq", axis=0, tiled=True),
    )
    all_lse, all_delta = (
        lax.all_gather(lse_rows, "seq", axis=0, tiled=True),
        lax.all_gather(row_delta, "seq", axis=0, tiled=True),
    )
    key_heads = key_rows.reshape(row_count, HEADS, HEAD_DIM)
    value_heads = value_rows.reshape(row_count, HEADS, HEAD_DIM)
    own_float = own_labels.astype(jnp.float32)

    def sweep_keys(carry, pieces):
        part_key, part_value = block_grads(
            pieces[0],
            pieces[1],
            pieces[2],
            pieces[3],
            pieces[4],
            key_heads,
            value_heads,
            own_float,
            variate_bias,
            False,
            True,
        )
        return ((carry[0] + part_key, carry[1] + part_value), None)

    (key_total, value_heads_total), unused = lax.scan(
        sweep_keys,
        (zero_heads, zero_heads),
        (
            all_query.reshape(blocks, block_rows, HEADS, HEAD_DIM),
            label_blocks,
            all_grad.reshape(blocks, block_rows, HEADS, HEAD_DIM),
            all_lse.reshape(blocks, block_rows, HEADS),
            all_delta.reshape(blocks, block_rows, HEADS),
        ),
    )
    value_total = value_heads_total.reshape(row_count, D)
    grad_query = unrotate(query_total, cos_table, sin_table).reshape(row_count, D)
    grad_key = unrotate(key_total, cos_table, sin_table).reshape(row_count, D)
    grad_project = jnp.stack([grad_query, grad_key, value_total]).astype(jnp.bfloat16)
    attend_grad = jnp.einsum(
        "td,cte->cde", act_one, grad_project, preferred_element_type=jnp.float32
    )
    grad_act_one = jnp.einsum(
        "cte,cde->td", grad_project, back_attend, preferred_element_type=jnp.float32
    )
    attend_share, output_share = (
        lax.psum_scatter(attend_grad, ("seq", "batch"), scatter_dimension=1, tiled=True),
        lax.psum_scatter(output_grad, ("seq", "batch"), scatter_dimension=0, tiled=True),
    )
    grad_input = grad_middle + norm_back(grad_act_one, unit_one, scale_one, norm_gains[0])
    gains_grad = jnp.stack(
        [jnp.sum(grad_act_one * unit_one, axis=0), jnp.sum(grad_act_two * unit_two, axis=0)]
    )
    local_squares = (
        jnp.sum(attend_share * attend_share)
        + jnp.sum(output_share * output_share)
        + jnp.sum(expand_share * expand_share)
        + jnp.sum(reduce_share * reduce_share)
    )
    gains_total, bias_total, square_sum = lax.psum(
        (gains_grad, bias_grad, local_squares), ("seq", "batch")
    )
    grad_norm = jnp.sqrt(
        square_sum + jnp.sum(gains_total * gains_total) + jnp.sum(bias_total * bias_total)
    )
    clip_scale = jnp.minimum(1.0, CLIP_NORM / grad_norm)
    attend_new, attend_first_new, attend_second_new = adam_step(
        attend_weight,
        attend_first,
        attend_second,
        attend_share * clip_scale,
        RATE_ATTEND,
        WEIGHT_DECAY,
    )
    output_new, output_first_new, output_second_new = adam_step(
        output_weight,
        output_first,
        output_second,
        output_share * clip_scale,
        RATE_OUTPUT,
        WEIGHT_DECAY,
    )
    expand_new, expand_first_new, expand_second_new = adam_step(
        expand_weight,
        expand_first,
        expand_second,
        expand_share * clip_scale,
        RATE_EXPAND,
        WEIGHT_DECAY,
    )
    reduce_new, reduce_first_new, reduce_second_new = adam_step(
        reduce_weight,
        reduce_first,
        reduce_second,
        reduce_share * clip_scale,
        RATE_REDUCE,
        WEIGHT_DECAY,
    )
    gains_new, gains_first_new, gains_second_new = adam_step(
        norm_gains, gains_first, gains_second, gains_total * clip_scale, RATE_GAINS, 0.0
    )
    bias_new, bias_first_new, bias_second_new = adam_step(
        variate_bias, bias_first, bias_second, bias_total * clip_scale, RATE_BIAS, 0.0
    )
    input_gradient = (grad_input * count_all * D)[None]
    return (
        output[None],
        loss,
        input_gradient,
        grad_norm,
        attend_new,
        attend_new.astype(jnp.bfloat16),
        attend_first_new,
        attend_second_new,
        output_new,
        output_new.astype(jnp.bfloat16),
        output_first_new,
        output_second_new,
        expand_new,
        expand_new.astype(jnp.bfloat16),
        expand_first_new,
        expand_second_new,
        reduce_new,
        reduce_new.astype(jnp.bfloat16),
        reduce_first_new,
        reduce_second_new,
        gains_new,
        gains_first_new,
        gains_second_new,
        bias_new,
        bias_first_new,
        bias_second_new,
    )


MESH = pl.DeviceIdType.MESH
IN_VMEM = pl.BlockSpec(memory_space=pltpu.VMEM)
IN_SMEM = pl.BlockSpec(memory_space=pltpu.SMEM)
LANES = 128
HEADS_HERE = LANES // HEAD_DIM
VARIATES = 16
MIB = 1 << 20
LOW = jnp.bfloat16
WIDE = jnp.float32
TOTAL_ROWS = 24


def fast_fits(seq, batch):
    return seq == 8 and batch == 4 and seq * LANES == D


def flip(index, mask):
    result, bit = index, 1
    while bit <= mask:
        if mask & bit:
            result = result + bit - 2 * bit * lax.rem(lax.div(index, bit), 2)
        bit *= 2
    return result


def push(source, target, send_sem, recv_sem, device):
    return pltpu.make_async_remote_copy(
        src_ref=source,
        dst_ref=target,
        send_sem=send_sem,
        recv_sem=recv_sem,
        device_id=device,
        device_id_type=MESH,
    )


def block_of(index, size):
    return pl.ds(pl.multiple_of(index * size, size), size)


def dot(left, right):
    return jnp.dot(left, right, preferred_element_type=WIDE)


def dot_turned(left, right):
    return lax.dot_general(left, right, (((1,), (1,)), ((), ())), preferred_element_type=WIDE)


def turned_dot(left, right):
    return lax.dot_general(left, right, (((0,), (0,)), ((), ())), preferred_element_type=WIDE)


class Team:
    def __init__(self, index, place):
        self.index, self.place = index, place

    def at(self, mask):
        return flip(self.index, mask)


def head_team(me, group):
    return Team(me, lambda mask: (flip(me, mask), group))


def feed_team(me, group):
    return Team(
        4 * lax.rem(group, 2) + lax.rem(me, 4),
        lambda mask: (flip(me, mask % 4), flip(group, mask // 4)),
    )


class Gather:
    def __init__(self, team, rows, all_rows, sends, recvs):
        self.team, self.all_rows, self.sends, self.recvs = team, all_rows, sends, recvs
        self.size = all_rows.shape[0] // 8
        self.given = rows
        self.rows = all_rows.at[block_of(team.index, self.size)] if rows is None else rows

    def copy(self, mask, passing):
        source = self.all_rows.at[block_of(self.team.at(mask - 1 if passing else 0), self.size)]
        return push(
            source if passing else self.rows,
            source,
            self.sends.at[mask],
            self.recvs.at[mask],
            self.team.place(1 if passing else mask),
        )

    def start(self):
        for mask in (6, 2, 4, 1):
            self.copy(mask, False).start()
        if self.given is not None:
            self.all_rows[block_of(self.team.index, self.size)] = self.given[...]

    def pass_on(self, chip):
        self.copy(2 * chip, False).wait_recv()
        self.copy(2 * chip + 1, True).start()

    def complete(self, chip):
        self.copy(2 * chip + 1, chip > 0).wait_recv()

    def finish(self):
        for mask in (6, 2, 4, 1):
            self.copy(mask, False).wait_send()
        for mask in (3, 5, 7):
            self.copy(mask, True).wait_send()


def at_step(step, number, *works):
    @pl.when(step == number)
    def _():
        for work in works:
            work()


def each_chip(gather, work, after):
    def one_chip(chip, unused):
        @pl.when(chip == 0)
        def _():
            gather.complete(0)

        @pl.when(chip == 1)
        def _():
            gather.pass_on(1)
            gather.pass_on(2)
            gather.complete(1)

        @pl.when(chip == 2)
        def _():
            gather.pass_on(3)
            gather.complete(2)

        @pl.when(chip == 3)
        def _():
            gather.complete(3)

        work(chip)
        for number, works in after.items():
            at_step(chip, number, *works)
        return unused

    lax.fori_loop(0, 4, one_chip, 0)
    gather.finish()


class Scatter:
    def __init__(self, team, buffers, near_sends, near_recvs, far_sends, far_recvs):
        self.whole, self.keep, self.near_from, self.near, self.far_from, self.far = buffers
        self.sems = near_sends, near_recvs, far_sends, far_recvs
        self.team = team
        self.size = self.keep.shape[1]

    def near_copy(self, chip):
        return push(
            self.near_from.at[chip],
            self.near.at[chip],
            self.sems[0].at[chip],
            self.sems[1].at[chip],
            self.team.place(1),
        )

    def far_copy(self, chip):
        return push(
            self.far_from.at[chip],
            self.far.at[chip],
            self.sems[2].at[chip],
            self.sems[3].at[chip],
            self.team.place(2 * chip),
        )

    def put(self, chip, rows):
        core = lax.rem(self.team.index, 2)
        self.whole[...] = rows
        self.near_from[chip] = self.whole[block_of(1 - core, self.size)].astype(LOW)
        self.near_copy(chip).start()
        self.keep[chip] = self.whole[block_of(core, self.size)]

    def combine(self, chip):
        self.near_copy(chip).wait_recv()
        self.far_from[chip] = (self.keep[chip] + self.near[chip].astype(WIDE)).astype(LOW)
        self.far_copy(chip).start()

    def total(self):
        self.near_copy(0).wait_recv()
        total = self.keep[0] + self.near[0].astype(WIDE)
        for chip in (1, 2, 3):
            self.far_copy(chip).wait_recv()
            total = total + self.far[chip].astype(WIDE)
        for chip in (0, 1, 2, 3):
            self.near_copy(chip).wait_send()
            if chip:
                self.far_copy(chip).wait_send()
        return total


class LineGather:
    def __init__(self, part_of, sends, recvs, me, group):
        self.part_of, self.sends, self.recvs, self.me, self.group = part_of, sends, recvs, me, group
        self.middle = jnp.logical_and(group >= 1, group <= 2)

    def copy(self, part, target, slot):
        return push(
            self.part_of(part),
            self.part_of(part),
            self.sends.at[slot],
            self.recvs.at[part],
            (self.me, target),
        )

    def start(self):
        group = self.group

        @pl.when(self.middle)
        def _():
            self.copy(group, 3 - group, 3 - group).start()
            self.copy(group, 3 * (group - 1), 3 * (group - 1)).start()

        @pl.when(jnp.logical_not(self.middle))
        def _():
            for step in (2, 1, 3):
                other = lax.rem(group + step, 4)
                self.copy(group, other, other).start()

    def pass_on(self):
        group = self.group

        @pl.when(self.middle)
        def _():
            self.copy(3 - group, 3 * (group - 1), group).wait_recv()
            self.copy(3 - group, 3 * (group - 1), group).start()

    def land(self):
        group = self.group

        @pl.when(self.middle)
        def _():
            for part in (0, 3):
                self.copy(part, 3 - group, group).wait_recv()

        @pl.when(jnp.logical_not(self.middle))
        def _():
            for step in (1, 2, 3):
                other = lax.rem(group + step, 4)
                self.copy(other, other, other).wait_recv()

    def finish(self):
        group = self.group

        @pl.when(self.middle)
        def _():
            for other in (3 - group, 3 * (group - 1), group):
                self.copy(group, 3 - group, other).wait_send()

        @pl.when(jnp.logical_not(self.middle))
        def _():
            for step in (1, 2, 3):
                other = lax.rem(group + step, 4)
                self.copy(group, other, other).wait_send()


class LineScatter:
    def __init__(self, part_of, landing, sends, recvs, me, group):
        self.part_of, self.landing, self.sends, self.recvs = part_of, landing, sends, recvs
        self.me, self.group = me, group
        self.middle = jnp.logical_and(group >= 1, group <= 2)
        self.opposite = 3 - 3 * lax.div(group, 2)

    def copy(self, part, slot, target, sem):
        return push(
            self.part_of(part),
            self.landing.at[slot],
            self.sends.at[sem],
            self.recvs.at[slot],
            (self.me, target),
        )

    def start(self):
        group = self.group

        @pl.when(self.middle)
        def _():
            for other in (3 - group, 3 * (group - 1)):
                self.copy(other, group, other, other).start()

        @pl.when(jnp.logical_not(self.middle))
        def _():
            beside = 1 + lax.div(group, 3)
            self.copy(3 - group, beside, beside, 3 - group).start()
            for other in (3 - beside, beside):
                self.copy(other, group, other, other).start()

    def pass_on(self):
        group, opposite = self.group, self.opposite

        @pl.when(self.middle)
        def _():
            self.copy(opposite, group, opposite, group).wait_recv()
            part = self.part_of(opposite)
            part[...] = (part[...].astype(WIDE) + self.landing[group].astype(WIDE)).astype(LOW)
            self.copy(opposite, group, opposite, group).start()

    def land(self):
        group = self.group

        @pl.when(self.middle)
        def _():
            for slot in (0, 3 - group, 3):
                self.copy(group, slot, 3 - group, group).wait_recv()

        @pl.when(jnp.logical_not(self.middle))
        def _():
            for slot in (1, 2):
                self.copy(group, slot, slot, group).wait_recv()

    def add(self, own, landed, store):
        group = self.group

        @pl.when(self.middle)
        def _():
            store(own() + landed(0) + landed(3 - group) + landed(3))

        @pl.when(jnp.logical_not(self.middle))
        def _():
            store(own() + landed(1) + landed(2))

    def finish(self):
        group = self.group

        @pl.when(self.middle)
        def _():
            for sem in (3 - group, 3 * (group - 1), group):
                self.copy(group, group, 3 - group, sem).wait_send()

        @pl.when(jnp.logical_not(self.middle))
        def _():
            for sem in (3 - group, 1, 2):
                self.copy(group, group, 1, sem).wait_send()


class QuadGather:
    def __init__(self, part_of, sends, recvs, me, group):
        self.part_of, self.sends, self.recvs = part_of, sends, recvs
        self.part = 2 * lax.div(me, 4) + lax.div(group, 2)
        self.along_y, self.along_z = (flip(me, 4), group), (me, flip(group, 2))

    def copy(self, way):
        part = self.part_of(flip(self.part, 1) if way == 3 else self.part)
        device = self.along_z if way == 1 else self.along_y
        return push(part, part, self.sends.at[way], self.recvs.at[way], device)

    def start_y(self):
        self.copy(2).start()

    def start_z(self):
        self.copy(1).start()

    def pass_on(self):
        self.copy(1).wait_recv()
        self.copy(3).start()

    def land(self):
        self.copy(2).wait_recv()
        self.copy(3).wait_recv()

    def finish(self):
        for way in (1, 2, 3):
            self.copy(way).wait_send()


class QuadScatter:
    def __init__(self, part_of, landing, sends, recvs, me, group):
        self.part_of, self.landing, self.sends, self.recvs = part_of, landing, sends, recvs
        self.part = 2 * lax.div(me, 4) + lax.div(group, 2)
        self.along_y, self.along_z = (flip(me, 4), group), (me, flip(group, 2))

    def copy(self, slot):
        return push(
            self.part_of(flip(self.part, (2, 3, 1)[slot])),
            self.landing.at[slot],
            self.sends.at[slot],
            self.recvs.at[slot],
            self.along_z if slot == 2 else self.along_y,
        )

    def start_far(self):
        self.copy(1).start()

    def start_near(self):
        self.copy(0).start()

    def pass_on(self):
        self.copy(1).wait_recv()
        part = self.part_of(flip(self.part, 1))
        part[...] = (part[...].astype(WIDE) + self.landing[1].astype(WIDE)).astype(LOW)
        self.copy(2).start()

    def land(self):
        self.copy(0).wait_recv()
        self.copy(2).wait_recv()

    def finish(self):
        for slot in (0, 1, 2):
            self.copy(slot).wait_send()


def chip_of(team, chip):
    here = lax.div(team.index, 2)
    if isinstance(chip, int):
        return flip(here, chip)
    column = lax.rem(lax.rem(here, 2) + lax.rem(chip, 2), 2)
    row = lax.rem(lax.div(here, 2) + lax.div(chip, 2), 2)
    return 2 * row + column


def turn_rows(values, cosine, sine):
    half = HEAD_DIM // 2
    pieces = []
    for start in range(0, values.shape[0], HEAD_DIM):
        first, second = values[start : start + half], values[start + half : start + HEAD_DIM]
        pieces += [first * cosine - second * sine, second * cosine + first * sine]
    return jnp.concatenate(pieces, axis=0)


def thirds(values):
    first = values.astype(LOW).astype(WIDE)
    second = (values - first).astype(LOW).astype(WIDE)
    return first, second, values - first - second


def pick(row, choices):
    result = jnp.zeros(row.shape, WIDE)
    for number, choice in choices.items():
        result = jnp.where(row == number, choice, result)
    return result


def norm_rows(values):
    scale = lax.rsqrt(jnp.mean(values * values, axis=-1, keepdims=True) + NORM_EPS)
    return values * scale, scale


def feed_block(block):
    y, x, core, far_z, near_z = (block // 16, block // 8 % 2, block // 4 % 2, block // 2 % 2, block % 2)
    return 4 * near_z + 2 * x + core, 2 * y + far_z


def layer_kernel(seq, batch, ins, outs, mem):
    me, group = lax.axis_index("seq"), lax.axis_index("batch")
    rows = ins.inputs.shape[0]
    length = rows * seq
    pair = 2 * rows
    share = ins.attend.shape[1]
    wide_columns = ins.expand.shape[2] // D
    hidden_width = mem.reduce_all.shape[0] * mem.reduce_all.shape[1]
    blocks = ins.expand.shape[2] // LANES
    heads, feeds = head_team(me, group), feed_team(me, group)
    quad = 2 * lax.div(me, 4) + lax.div(group, 2)

    staged = [(ins.attend.at[which], mem.keep.at[0, block_of(which, share)]) for which in range(3)]
    staged.append((ins.output, mem.keep.at[0, block_of(3, share)]))
    staged.append((ins.reduce, mem.keep.at[1]))
    for which in range(2):
        for block in range(wide_columns):
            columns = slice(block * D, (block + 1) * D)
            staged.append(
                (ins.expand.at[which, :, columns], mem.keep.at[2 + which, block_of(block, share)])
            )
    staged = [
        pltpu.make_async_copy(source, target, mem.stage_sem.at[number])
        for number, (source, target) in enumerate(staged)
    ]
    for copy in staged:
        copy.start()
    barrier = pltpu.get_barrier_semaphore()
    for mask in range(1, seq):
        pl.semaphore_signal(barrier, inc=1, device_id=(flip(me, mask), group), device_id_type=MESH)
    for step in range(1, batch):
        pl.semaphore_signal(
            barrier, inc=1, device_id=(me, lax.rem(group + step, batch)), device_id_type=MESH
        )
    for mask in (5, 6, 7):
        pl.semaphore_signal(barrier, inc=1, device_id=feeds.place(mask), device_id_type=MESH)

    position = me * rows + lax.broadcasted_iota(jnp.int32, (1, rows), 1)
    inside = position < ins.lengths[0]
    scored = jnp.logical_and(inside, ins.observed[...] == 1).astype(WIDE)
    variate = ins.variates[...].astype(WIDE)
    turns = ins.turns.shape[0]
    mem.facts_own[:turns] = ins.turns[...]
    mem.facts_own[turns:] = jnp.concatenate(
        [jnp.where(inside, variate, -1.0), variate, scored, jnp.zeros((5, rows), WIDE)], axis=0
    )
    mem.scored[...] = jnp.broadcast_to(scored, (rows, rows)).T
    unit_one, scale_one = norm_rows(ins.inputs[...].astype(WIDE))
    mem.own_rows[0] = (unit_one * ins.gains[0:1, :]).astype(LOW)
    for copy in staged:
        copy.wait()
    for which in range(3):
        mem.attend_low[which] = mem.keep[0, block_of(which, share)].astype(LOW)
    mem.output_full[block_of(batch * me + group, share)] = mem.keep[0, block_of(3, share)].astype(LOW)
    mem.reduce_all[quad] = mem.keep[1].astype(LOW)
    for which in range(2):
        for block in range(blocks):
            owner, part = feed_block(block)
            row, lane = divmod(block * LANES, D)
            mem.expand_low[which, owner, :, part * LANES : (part + 1) * LANES] = mem.keep[
                2 + which, block_of(row, share), lane : lane + LANES
            ].astype(LOW)
    pl.semaphore_wait(barrier, seq + batch + 1)

    masks = (6, 7, 4, 5, 2, 3, 1)

    def start_attend_columns():
        copies = []
        for mask in masks:
            copy = push(
                mem.attend_low.at[:, :, block_of(heads.at(mask), LANES)],
                mem.attend_all.at[:, me, group],
                mem.column_send.at[0, mask],
                mem.column_recv.at[0, mask],
                heads.place(mask),
            )
            copy.start()
            copies.append(copy)
        mem.attend_all[:, me, group] = mem.attend_low[:, :, block_of(me, LANES)]
        return copies

    def start_expand_columns():
        copies = []
        for mask in masks:
            copy = push(
                mem.expand_low.at[:, feeds.at(mask)],
                mem.expand_all.at[:, me, group],
                mem.column_send.at[1, mask],
                mem.column_recv.at[1, mask],
                feeds.place(mask),
            )
            copy.start()
            copies.append(copy)
        mem.expand_all[:, me, group] = mem.expand_low[:, feeds.index]
        return copies

    def expand_part_of(array, which):
        def part_of(part):
            return array.at[which, pl.ds(4 * lax.div(part, 2), 4), pl.ds(2 * lax.rem(part, 2), 2)]

        return part_of

    def line_gather(row, part_of):
        return LineGather(part_of, mem.line_send.at[row], mem.line_recv.at[row], me, group)

    def quad_gather(row, part_of):
        return QuadGather(part_of, mem.line_send.at[row], mem.line_recv.at[row], me, group)

    def gather(team, phase, all_rows):
        return Gather(
            team,
            mem.own_rows.at[phase],
            all_rows,
            mem.gather_send.at[phase],
            mem.gather_recv.at[phase],
        )

    def scatter(team, phase):
        return Scatter(
            team,
            (mem.whole, mem.keep, mem.near_from, mem.near, mem.far_from, mem.far),
            mem.near_send.at[phase],
            mem.near_recv.at[phase],
            mem.far_send.at[phase],
            mem.far_recv.at[phase],
        )

    attend_columns = start_attend_columns()
    line_output = line_gather(1, lambda part: mem.output_full.at[block_of(batch * me + part, share)])
    line_output.start()
    facts = Gather(heads, mem.facts_own, mem.facts_all, mem.facts_send, mem.facts_recv)
    facts.start()
    for copy in attend_columns:
        copy.wait_recv()
    line_attend = line_gather(0, lambda part: mem.attend_all.at[:, :, part])
    line_attend.start()
    acts = gather(heads, 0, mem.act_one)
    acts.start()
    for chip in (1, 2, 3):
        facts.pass_on(chip)
    for chip in (0, 1, 2, 3):
        facts.complete(chip)
    facts.finish()
    step_rows = mem.facts_own.shape[0]
    half = HEAD_DIM // 2
    count = jnp.zeros((8, LANES), WIDE)
    for slot in range(seq):
        columns = slice(slot * rows, (slot + 1) * rows)
        start = slot * step_rows
        mem.cosine[:, columns] = mem.facts_all[start : start + half]
        mem.sine[:, columns] = mem.facts_all[start + half : start + 2 * half]
        labels = mem.facts_all[start + 2 * half : start + 2 * half + 8]
        mem.labels[:, columns] = labels
        count = count + labels
    mem.count[group] = count
    count_copies = []
    for step in range(1, batch):
        copy = push(
            mem.count.at[group],
            mem.count.at[group],
            mem.count_send.at[step],
            mem.count_recv.at[step],
            (me, lax.rem(group + step, batch)),
        )
        copy.start()
        count_copies.append(copy)

    def mark(block, unused):
        span = block_of(block, pair)
        row = lax.broadcasted_iota(jnp.int32, (HEAD_DIM, pair), 0)
        third = lax.div(row, VARIATES)
        variate = lax.rem(row, VARIATES).astype(WIDE)
        key_label, query_label = mem.labels[0:1, span], mem.labels[1:2, span]
        ones = jnp.ones((1, pair), WIDE)
        last = 3 * VARIATES
        hidden_keys = (key_label < 0.0).astype(WIDE)
        mem.key_marks[:, span] = jnp.where(
            third < 3,
            (key_label == variate).astype(WIDE),
            pick(row, {last: ones, last + 1: ones, last + 2: ones, last + 3: hidden_keys}),
        ).astype(LOW)
        query_marks = (query_label == variate).astype(WIDE)
        mem.sum_marks[:, span] = jnp.where(
            row < VARIATES, query_marks, pick(row, {VARIATES: ones})
        ).astype(LOW)
        for head in range(HEADS_HERE):
            number = me * HEADS_HERE + head
            other = jnp.full((HEAD_DIM, pair), ins.bias[1, number], WIDE)
            more = thirds(jnp.full((HEAD_DIM, pair), ins.bias[0, number], WIDE) - other)
            other = thirds(other)
            mem.query_turned[head, HEAD_DIM:, span] = jnp.where(
                third < 3,
                query_marks * jnp.where(third == 0, more[0], jnp.where(third == 1, more[1], more[2])),
                pick(row, {last: other[0], last + 1: other[1], last + 2: other[2], last + 3: MASKED}),
            ).astype(LOW)
        return unused

    lax.fori_loop(0, length // pair, mark, 0)
    acts.pass_on(1)
    acts.pass_on(2)
    line_output.pass_on()
    line_output.land()
    outputs = Gather(heads, None, mem.output_full, mem.output_send, mem.output_recv)
    outputs.start()
    acts.pass_on(3)
    line_attend.pass_on()
    for chip in range(4):
        acts.complete(chip)
    acts.finish()

    expand_columns = start_expand_columns()
    line_reduce = quad_gather(4, lambda part: mem.reduce_all.at[part])
    line_reduce.start_z()
    line_expand = [
        quad_gather(2 + which, expand_part_of(mem.expand_all, which)) for which in range(2)
    ]
    line_attend.land()
    line_reduce.start_y()

    def attend_matrix(which):
        return mem.attend_all[which].reshape(D, LANES)

    def project(block, unused):
        span = block_of(block, pair)
        act = mem.act_one[span, :]
        cosine, sine = mem.cosine[:, span], mem.sine[:, span]
        query = turn_rows(dot(act, attend_matrix(0)).T, cosine, sine).astype(LOW)
        query = (query.astype(WIDE) * HEAD_DIM ** (-0.5)).astype(LOW)
        key = turn_rows(dot(act, attend_matrix(1)).T, cosine, sine).astype(LOW)
        value = dot(act, attend_matrix(2)).T.astype(LOW)
        mem.key_turned[:, span] = key
        mem.value_turned[:, span] = value

        for head in range(HEADS_HERE):
            features = slice(head * HEAD_DIM, (head + 1) * HEAD_DIM)
            mem.query_turned[head, :HEAD_DIM, span] = query[features]
            whole = jnp.concatenate([key[features], mem.key_marks[:, span]], axis=0)
            mem.key_heads[head, span, :] = whole.T
        return unused

    for copy in expand_columns:
        copy.wait_recv()
    line_expand[0].start_z()
    line_expand[0].start_y()
    lax.fori_loop(0, length // pair, project, 0)
    line_expand[1].start_z()
    outputs.pass_on(1)
    outputs.pass_on(2)

    core = lax.rem(me, 2)

    def mixed_copy(chip, which):
        other = 2 * chip_of(heads, chip) + which
        slot = 2 * chip + lax.rem(which + core, 2)
        return push(
            mem.mixed_out.at[block_of(other, rows)],
            mem.mixed_rows.at[:, block_of(me, LANES)],
            mem.mixed_send.at[slot],
            mem.mixed_recv.at[slot],
            (other, group),
        )

    def attend_block(chip):
        columns = block_of(chip_of(heads, chip), pair)
        for head in range(HEADS_HERE):
            span = slice(head * HEAD_DIM, (head + 1) * HEAD_DIM)
            scores = dot(mem.key_heads[head], mem.query_turned[head, :, columns])
            top = jnp.floor(jnp.max(scores, axis=0, keepdims=True))
            powers = jnp.exp(scores - top)
            probs = powers * (1.0 / jnp.sum(powers, axis=0, keepdims=True))
            rounded = probs.astype(LOW)
            mem.probs[head, :, columns] = rounded
            residue = (probs - rounded.astype(WIDE)).astype(LOW)
            coarse = dot(mem.value_turned[span, :], rounded)
            mem.exact[span, columns] = coarse + dot(mem.value_turned[span, :], residue)
            mem.mixed_wide[span, :] = coarse
        mixed = mem.mixed_wide[...].astype(LOW)
        mem.mixed_turned[:, columns] = mixed
        mem.mixed_out[columns, :] = mixed.T

    def attend_step(step, unused):
        chip = lax.rem(step + 1, 4)
        attend_block(chip)
        for which in range(2):

            @pl.when(jnp.logical_or(chip > 0, core != which))
            def _():
                mixed_copy(chip, which).start()

        at_step(step, 1, lambda: outputs.pass_on(3))
        return unused

    lax.fori_loop(0, 4, attend_step, 0)
    line_expand[1].start_y()
    mem.mixed_rows[:, block_of(me, LANES)] = mem.mixed_out[block_of(me, rows), :]
    for chip in range(4):
        outputs.complete(chip)
    outputs.finish()

    def wait_pieces(copy):
        for mask in range(1, seq):
            copy(mask).wait()

    def mixed_wait(mask):
        other = heads.at(mask)
        return push(
            mem.mixed_out.at[block_of(other, rows)],
            mem.mixed_rows.at[:, block_of(other, LANES)],
            mem.mixed_send.at[mask],
            mem.mixed_recv.at[mask],
            (other, group),
        )

    wait_pieces(mixed_wait)
    middle = ins.inputs[...].astype(WIDE) + dot(mem.mixed_rows[...], mem.output_full[...])
    mem.middle[...] = middle
    unit_two, scale_two = norm_rows(middle)
    mem.own_rows[1] = (unit_two * ins.gains[1:2, :]).astype(LOW)
    acts = gather(feeds, 1, mem.act_two)
    acts.start()
    line_reduce.pass_on()
    line_expand[0].pass_on()

    def split_heads(block, unused):
        span = block_of(block, pair)
        row = lax.broadcasted_iota(jnp.int32, (HEAD_DIM, pair), 0)
        value_marks = jnp.where(row < 3, 1.0, 0.0).astype(LOW)
        for head in range(HEADS_HERE):
            features = slice(head * HEAD_DIM, (head + 1) * HEAD_DIM)
            value = mem.value_turned[features, span]
            mem.value_heads[head, span, :] = jnp.concatenate([value, value_marks], axis=0).T
            query = mem.query_turned[head, :HEAD_DIM, span]
            whole = jnp.concatenate([query, mem.sum_marks[:, span]], axis=0)
            mem.query_heads[head, span, :] = whole.T
        return unused

    lax.fori_loop(0, length // pair, split_heads, 0)
    line_expand[0].land()

    def expand_matrix(which):
        return mem.expand_all[which].reshape(D, hidden_width)

    def reduce_matrix():
        return mem.reduce_all[...].reshape(hidden_width, D)

    def feed_gate(chip):
        span = block_of(chip_of(feeds, chip), pair)
        mem.by_gate[span, :] = dot(mem.act_two[span, :], expand_matrix(0))

    each_chip(acts, feed_gate, {1: [line_expand[1].pass_on]})
    line_expand[1].land()
    line_reduce.land()
    sums = scatter(feeds, 1)

    def feed_down(step, unused):
        chip = lax.rem(step + 1, 4)
        span = block_of(chip_of(feeds, chip), pair)
        gate = mem.by_gate[span, :]
        up = dot(mem.act_two[span, :], expand_matrix(1))
        sigmoid = 1.0 / (1.0 + jnp.exp(-gate))
        swish = gate * sigmoid
        mem.by_up[span, :] = swish
        mem.by_gate[span, :] = up * sigmoid * (1.0 + gate * (1.0 - sigmoid))
        hidden = (swish * up).astype(LOW)
        mem.hidden[span, :] = hidden
        sums.put(chip, dot(hidden, reduce_matrix()))
        at_step(step, 1, lambda: sums.combine(1))
        at_step(step, 2, lambda: sums.combine(2))
        return unused

    lax.fori_loop(0, 4, feed_down, 0)
    sums.combine(3)

    for block in range(length // pair):
        span = block_of(block, pair)
        mem.hidden_turned[:, span] = mem.hidden[span, :].T
        mem.act_two_turned[:, span] = mem.act_two[span, :].T
    output = mem.middle[...] + sums.total()
    outs.layer_output[...] = output
    for copy in count_copies:
        copy.wait()
    count_all = jnp.sum(
        mem.count[0, 2:3] + mem.count[1, 2:3] + mem.count[2, 2:3] + mem.count[3, 2:3],
        axis=1,
        keepdims=True,
    )
    error = jnp.where(mem.scored[:, 0:1] > 0.0, output - ins.teacher[...].astype(WIDE), 0.0)
    mem.squares[1:2, :] = jnp.sum(error * error, axis=0, keepdims=True)
    grad_out = error * (2.0 / (count_all * D))
    mem.grad_own[...] = grad_out
    mem.own_rows[2] = grad_out.astype(LOW)
    acts = gather(feeds, 2, mem.branch)
    acts.start()

    sums = scatter(feeds, 2)

    def feed_back(chip):
        span = block_of(chip_of(feeds, chip), pair)
        grad_hidden = dot_turned(mem.branch[span, :], reduce_matrix())
        grad_gate = (grad_hidden * mem.by_gate[span, :]).astype(LOW)
        grad_up = (grad_hidden * mem.by_up[span, :]).astype(LOW)
        mem.grad_gate[span, :] = grad_gate
        mem.grad_up[span, :] = grad_up
        sums.put(
            chip,
            dot_turned(grad_gate, expand_matrix(0)) + dot_turned(grad_up, expand_matrix(1)),
        )

    each_chip(
        acts, feed_back, {2: [lambda: sums.combine(1)], 3: [lambda: sums.combine(2)]}
    )
    sums.combine(3)

    def line_scatter(row, part_of, landing):
        return LineScatter(
            part_of, landing, mem.back_send.at[row], mem.back_recv.at[row], me, group
        )

    def quad_scatter(row, part_of, landing):
        return QuadScatter(
            part_of, landing, mem.back_send.at[row], mem.back_recv.at[row], me, group
        )

    def reduce_grad(part, unused):
        mem.reduce_grad[part] = dot(
            mem.hidden_turned[block_of(part, rows), :], mem.branch[...]
        ).astype(LOW)
        return unused

    lax.fori_loop(0, batch, reduce_grad, 0)
    back_reduce = quad_scatter(0, lambda part: mem.reduce_grad.at[part], mem.reduce_land)
    back_reduce.start_far()

    def expand_grad(which):
        grads = (mem.grad_gate, mem.grad_up)[which]

        def one_block(block, unused):
            products = dot(mem.act_two_turned[block_of(block, pair), :], grads[...]).astype(LOW)
            mem.expand_grad[which, pl.ds(2 * block, 2)] = products.reshape(
                2, batch, share, hidden_width
            )
            return unused

        lax.fori_loop(0, seq // 2, one_block, 0)
        line = quad_scatter(
            1 + which, expand_part_of(mem.expand_grad, which), mem.expand_land.at[which]
        )
        return line

    back_expand = []
    for which in range(2):
        back_expand.append(expand_grad(which))
        back_expand[which].start_far()
    grad_act = sums.total()
    unit_two, scale_two = norm_rows(mem.middle[...])
    gain = ins.gains[1:2, :]
    grad_unit = grad_act * gain
    mem.gains[1:2, :] = jnp.sum(grad_act * unit_two, axis=0, keepdims=True)
    grad_middle = mem.grad_own[...] + scale_two * (
        grad_unit - unit_two * jnp.mean(grad_unit * unit_two, axis=-1, keepdims=True)
    )
    mem.grad_own[...] = grad_middle
    mem.own_rows[3] = grad_middle.astype(LOW)
    grad_mixed = dot(mem.output_full[...], grad_middle.T.astype(LOW)).astype(LOW)
    mem.grad_mixed_out[...] = grad_mixed.reshape(seq, LANES, rows)

    def grad_copy(mask, back=False):
        return push(
            mem.grad_mixed_out.at[heads.at(mask)],
            mem.grad_mixed.at[:, block_of(heads.at(mask) if back else me, rows)],
            mem.mixed_send.at[8 + mask],
            mem.mixed_recv.at[8 + mask],
            heads.place(mask),
        )

    for mask in masks:
        grad_copy(mask).start()
    mem.grad_mixed[:, block_of(me, rows)] = mem.grad_mixed_out[me]
    back_reduce.pass_on()

    wait_pieces(lambda mask: grad_copy(mask, True))
    acts = gather(heads, 3, mem.grad_attn)
    acts.start()
    back_reduce.start_near()
    back_expand[0].start_near()
    back_attend = [
        line_scatter(
            4 + which,
            lambda part, which=which: mem.attend_grad.at[which, :, part],
            mem.attend_land.at[which],
        )
        for which in range(3)
    ]

    def attend_grad(which):
        grads = dot(mem.grad_project[which], mem.act_one[...])
        mem.attend_grad[which] = grads.T.astype(LOW).reshape(seq, batch, share, LANES)
        back_attend[which].start()

    lane = lax.broadcasted_iota(jnp.int32, (pair, LANES), 1)

    def grad_rows(block, unused):
        span = block_of(block, pair)
        whole = mem.grad_mixed[:, span].astype(WIDE).T
        for head in range(HEADS_HERE):
            mem.grad_heads[head, span, :] = jnp.where(lax.div(lane, HEAD_DIM) == head, whole, 0.0).astype(LOW)
        return unused

    lax.fori_loop(0, length // pair, grad_rows, 0)

    def value_back(block, unused):
        span = block_of(block, pair)
        total = dot(mem.probs[0, span, :], mem.grad_heads[0])
        for head in range(1, HEADS_HERE):
            total = total + dot(mem.probs[head, span, :], mem.grad_heads[head])
        mem.grad_project[2, :, span] = total.T.astype(LOW)
        return unused

    lax.fori_loop(0, length // pair, value_back, 0)
    back_expand[0].pass_on()
    attend_grad(2)

    def score_back(block, unused):
        columns = block_of(block, pair)
        row = lax.broadcasted_iota(jnp.int32, (HEAD_DIM, pair), 0)
        grads = mem.grad_mixed[:, columns]
        delta = grads.astype(WIDE) * mem.exact[:, columns]
        for head in range(HEADS_HERE):
            span = slice(head * HEAD_DIM, (head + 1) * HEAD_DIM)
            pieces = thirds(-jnp.sum(delta[span], axis=0, keepdims=True))
            marks = pick(row, dict(enumerate(pieces))).astype(LOW)
            change = dot(mem.value_heads[head], jnp.concatenate([grads[span], marks], axis=0))
            mem.probs[head, :, columns] = (mem.probs[head, :, columns].astype(WIDE) * change).astype(LOW)
        return unused

    lax.fori_loop(0, length // pair, score_back, 0)
    back_expand[1].start_near()
    mem.bias_sums[...] = jnp.zeros_like(mem.bias_sums)
    scale = HEAD_DIM ** (-0.5)

    def project_grads(block, unused):
        span = block_of(block, pair)
        cosine, sine = mem.cosine[:, span], -mem.sine[:, span]
        queries, keys = [], []
        for head in range(HEADS_HERE):
            features = slice(head * HEAD_DIM, (head + 1) * HEAD_DIM)
            queries.append(dot(mem.key_turned[features, :], mem.probs[head, :, span]) * scale)
            sums = dot(mem.probs[head, span, :], mem.query_heads[head]).T
            keys.append(sums[:HEAD_DIM])
            by_variate = sums[HEAD_DIM : HEAD_DIM + VARIATES]
            same = by_variate * mem.key_marks[:VARIATES, span].astype(WIDE)
            mem.bias_sums[head : head + 1, :] += jnp.sum(same, axis=0, keepdims=True)
            total = sums[HEAD_DIM + VARIATES : HEAD_DIM + VARIATES + 1]
            mem.bias_sums[HEADS_HERE + head : HEADS_HERE + head + 1, :] += total
        mem.grad_project[0, :, span] = turn_rows(jnp.concatenate(queries, axis=0), cosine, sine).astype(LOW)
        mem.grad_project[1, :, span] = turn_rows(jnp.concatenate(keys, axis=0), cosine, sine).astype(LOW)
        return unused

    lax.fori_loop(0, length // pair, project_grads, 0)
    back_expand[1].pass_on()
    for which in range(2):
        attend_grad(which)
    acts.pass_on(1)
    acts.pass_on(2)
    sums = scatter(heads, 3)

    def project_back(step, unused):
        chip = lax.rem(step + 1, 4)
        span = block_of(chip_of(heads, chip), pair)
        total = jnp.zeros((pair, D), WIDE)
        for which in range(3):
            total = total + dot_turned(mem.grad_project[which, :, span].T, attend_matrix(which))
        sums.put(chip, total)
        at_step(step, 1, lambda: sums.combine(1))
        at_step(step, 2, lambda: sums.combine(2))
        return unused

    lax.fori_loop(0, 4, project_back, 0)
    sums.combine(3)
    acts.pass_on(3)
    for chip in range(4):
        acts.complete(chip)
    acts.finish()
    mem.output_grad[...] = (
        dot(mem.mixed_turned[...], mem.grad_attn[...]).astype(LOW).reshape(mem.output_grad.shape)
    )
    back_output = line_scatter(3, lambda part: mem.output_grad.at[part], mem.output_land)
    back_output.start()
    for which in (2, 0, 1):
        back_attend[which].pass_on()

    column_copies = []
    mem.squares[0:1, :] = jnp.zeros((1, D), WIDE)

    def add_squares(total):
        flat = total.reshape(-1, total.shape[-1])
        width = flat.shape[1]
        mem.squares[0:1, :width] += jnp.sum(flat * flat, axis=0, keepdims=True)

    def store_whole(total, out):
        out[...] = total
        add_squares(total)

    back_reduce.land()
    store_whole(
        mem.reduce_grad[quad].astype(WIDE)
        + mem.reduce_land[0].astype(WIDE)
        + mem.reduce_land[2].astype(WIDE),
        outs.reduce_share,
    )
    def expand_shares(which):
        back_expand[which].land()
        own = expand_part_of(mem.expand_grad, which)(quad)

        def one_block(block, unused):
            total = (
                own[block].astype(WIDE)
                + mem.expand_land[which, 0, block].astype(WIDE)
                + mem.expand_land[which, 2, block].astype(WIDE)
            )
            mem.expand_part[which, block] = total.astype(LOW)
            add_squares(total)
            return unused

        lax.fori_loop(0, 4, one_block, 0)
        for mask in masks:
            other = feeds.at(mask)
            copy = push(
                mem.expand_part.at[which, lax.rem(other, 4), lax.div(other, 4)],
                mem.expand_share.at[which, feeds.index],
                mem.share_send.at[which, mask],
                mem.share_recv.at[which, mask],
                feeds.place(mask),
            )
            copy.start()
            column_copies.append(copy)
        mem.expand_share[which, feeds.index] = mem.expand_part[
            which, lax.rem(feeds.index, 4), lax.div(feeds.index, 4)
        ]

    for which in range(2):
        expand_shares(which)

    def attend_shares(which):
        back_attend[which].land()

        def store(total):
            mem.attend_part[which] = total.astype(LOW)
            add_squares(total)

        back_attend[which].add(
            lambda: mem.attend_grad[which, :, group].astype(WIDE),
            lambda slot: mem.attend_land[which, slot].astype(WIDE),
            store,
        )

    attend_shares(2)
    grad_act = sums.total()
    unit_one, scale_one = norm_rows(ins.inputs[...].astype(WIDE))
    gain = ins.gains[0:1, :]
    grad_unit = grad_act * gain
    mem.gains[0:1, :] = jnp.sum(grad_act * unit_one, axis=0, keepdims=True)
    grad_input = mem.grad_own[...] + scale_one * (
        grad_unit - unit_one * jnp.mean(grad_unit * unit_one, axis=-1, keepdims=True)
    )
    outs.input_gradient[...] = grad_input * (count_all * D)
    outs.count[...] = jnp.broadcast_to(count_all, (8, LANES))

    back_output.pass_on()
    for which in range(2):
        attend_shares(which)
    for mask in masks:
        copy = push(
            mem.attend_part.at[:, heads.at(mask)],
            outs.attend_share.at[:, :, block_of(me, LANES)],
            mem.share_send.at[2, mask],
            mem.share_recv.at[2, mask],
            heads.place(mask),
        )
        copy.start()
        column_copies.append(copy)
    outs.attend_share[:, :, block_of(me, LANES)] = mem.attend_part[:, me]
    back_output.land()
    back_output.add(
        lambda: mem.output_grad[group].astype(WIDE),
        lambda slot: mem.output_land[slot].astype(WIDE),
        lambda total: store_whole(total, outs.output_share),
    )

    lane = lax.broadcasted_iota(jnp.int32, (1, LANES), 1)
    lines = [
        mem.gains[which : which + 1, start : start + LANES]
        for which in range(2)
        for start in range(0, D, LANES)
    ]
    bias_line = jnp.zeros((1, LANES), WIDE)
    for row in range(2 * HEADS_HERE):
        place = row // HEADS_HERE * HEADS + me * HEADS_HERE + row % HEADS_HERE
        line = mem.bias_sums[row : row + 1, :]
        if row >= HEADS_HERE:
            line = line - mem.bias_sums[row - HEADS_HERE : row - HEADS_HERE + 1, :]
        amount = jnp.sum(line, axis=1, keepdims=True)
        bias_line = bias_line + jnp.where(lane == place, amount, 0.0)
    amounts = jnp.sum(mem.squares[0:2, :], axis=1, keepdims=True)
    amount_line = jnp.where(lane == 0, amounts[0:1], 0.0) + jnp.where(lane == 1, amounts[1:2], 0.0)
    lines += [bias_line, amount_line, jnp.zeros((6, LANES), WIDE)]
    mem.plane_totals[me] = jnp.concatenate(lines, axis=0)
    plane_copies = []
    for mask in masks:
        copy = push(
            mem.plane_totals.at[me],
            mem.plane_totals.at[me],
            mem.total_send.at[0, mask],
            mem.total_recv.at[0, mask],
            (flip(me, mask), group),
        )
        copy.start()
        plane_copies.append(copy)
    for copy in plane_copies:
        copy.wait()
    mem.line_totals[group] = jnp.sum(mem.plane_totals[...], axis=0)
    total_copies = []
    for step in range(1, batch):
        copy = push(
            mem.line_totals.at[group],
            mem.line_totals.at[group],
            mem.total_send.at[1, step],
            mem.total_recv.at[1, step],
            (me, lax.rem(group + step, batch)),
        )
        copy.start()
        total_copies.append(copy)
    for copy in total_copies:
        copy.wait()
    outs.totals[...] = jnp.sum(mem.line_totals[...], axis=0)
    for copy in column_copies:
        copy.wait()
    for which in range(2):
        for block in range(blocks):
            owner, part = feed_block(block)
            outs.expand_share[which, :, block * LANES : (block + 1) * LANES] = mem.expand_share[
                which, owner, :, part * LANES : (part + 1) * LANES
            ]
    for copies in (attend_columns, expand_columns):
        for copy in copies:
            copy.wait_send()
    for line in [line_attend, line_output, line_reduce] + line_expand:
        line.finish()
    for line in [back_output, back_reduce] + back_attend + back_expand:
        line.finish()


def call_layer(seq, batch, inputs, teacher, lengths, variates, observed, turns, bias, gains, attend, output, expand, reduce):
    rows, share, hidden = inputs.shape[0], attend.shape[1], expand.shape[2] // seq
    length, pair, chips = rows * seq, 2 * rows, seq // 2
    low = lambda *shape: pltpu.VMEM(shape, LOW)
    wide = lambda *shape: pltpu.VMEM(shape, WIDE)
    sems = lambda *shape: pltpu.SemaphoreType.DMA(shape)
    in_names = ["inputs", "teacher", "lengths", "variates", "observed", "turns", "bias", "gains"]
    in_names += ["attend", "output", "expand", "reduce"]
    outs = dict(
        layer_output=((rows, D), WIDE),
        input_gradient=((rows, D), WIDE),
        totals=((TOTAL_ROWS, LANES), WIDE),
        count=((8, LANES), WIDE),
        attend_share=((3, share, D), LOW),
        output_share=((output.shape[0], D), WIDE),
        expand_share=((2, share, hidden * seq), LOW),
        reduce_share=((reduce.shape[0], D), WIDE),
    )
    scratch = dict(
        gains=wide(2, D),
        squares=wide(8, D),
        plane_totals=wide(seq, TOTAL_ROWS, LANES),
        line_totals=wide(batch, TOTAL_ROWS, LANES),
        attend_low=low(3, share, D),
        expand_low=low(2, seq, share, hidden),
        attend_all=low(3, seq, batch, share, LANES),
        output_full=low(D, D),
        expand_all=low(2, seq, batch, share, hidden),
        reduce_all=low(batch, reduce.shape[0], D),
        own_rows=low(4, rows, D),
        act_one=low(length, D),
        act_two=low(length, D),
        branch=low(length, D),
        grad_attn=low(length, D),
        facts_own=wide(turns.shape[0] + 8, LANES),
        facts_all=wide(seq * (turns.shape[0] + 8), LANES),
        scored=wide(rows, LANES),
        cosine=wide(HEAD_DIM // 2, length),
        sine=wide(HEAD_DIM // 2, length),
        labels=wide(8, length),
        key_marks=low(HEAD_DIM, length),
        count=wide(batch, 8, LANES),
        query_turned=low(HEADS_HERE, LANES, length),
        key_turned=low(LANES, length),
        value_turned=low(LANES, length),
        key_heads=low(HEADS_HERE, length, LANES),
        value_heads=low(HEADS_HERE, length, LANES),
        query_heads=low(HEADS_HERE, length, LANES),
        grad_heads=low(HEADS_HERE, length, LANES),
        grad_mixed=low(LANES, length),
        grad_mixed_out=low(seq, LANES, rows),
        probs=low(HEADS_HERE, length, length),
        mixed_out=low(length, LANES),
        mixed_rows=low(rows, D),
        sum_marks=low(HEAD_DIM, length),
        hidden_turned=low(hidden, length),
        act_two_turned=low(D, length),
        exact=wide(LANES, length),
        mixed_wide=wide(LANES, pair),
        mixed_turned=low(LANES, length),
        whole=wide(pair, D),
        keep=wide(chips, rows, D),
        near_from=low(chips, rows, D),
        near=low(chips, rows, D),
        far_from=low(chips, rows, D),
        far=low(chips, rows, D),
        middle=wide(rows, D),
        grad_own=wide(rows, D),
        by_up=wide(length, hidden),
        by_gate=wide(length, hidden),
        hidden=low(length, hidden),
        grad_gate=low(length, hidden),
        grad_up=low(length, hidden),
        bias_sums=wide(8, pair),
        grad_project=low(3, LANES, length),
        reduce_grad=low(batch, reduce.shape[0], D),
        expand_grad=low(2, seq, batch, share, hidden),
        output_grad=low(batch, output.shape[0], D),
        attend_grad=low(3, seq, batch, share, LANES),
        reduce_land=low(3, reduce.shape[0], D),
        expand_land=low(2, 3, 4, 2, share, hidden),
        output_land=low(batch, output.shape[0], D),
        attend_land=low(3, batch, seq, share, LANES),
        expand_part=low(2, 4, 2, share, hidden),
        expand_share=low(2, seq, share, hidden),
        attend_part=low(3, seq, share, LANES),
        stage_sem=sems(5 + 2 * (expand.shape[2] // D)),
        total_send=sems(2, seq),
        total_recv=sems(2, seq),
        column_send=sems(2, seq),
        column_recv=sems(2, seq),
        line_send=sems(5, batch),
        line_recv=sems(5, batch),
        facts_send=sems(seq),
        facts_recv=sems(seq),
        gather_send=sems(4, seq),
        gather_recv=sems(4, seq),
        count_send=sems(batch),
        count_recv=sems(batch),
        near_send=sems(4, chips),
        near_recv=sems(4, chips),
        far_send=sems(4, chips),
        far_recv=sems(4, chips),
        back_send=sems(7, batch),
        back_recv=sems(7, batch),
        output_send=sems(seq),
        output_recv=sems(seq),
        mixed_send=sems(2 * seq),
        mixed_recv=sems(2 * seq),
        share_send=sems(3, seq),
        share_recv=sems(3, seq),
    )

    places = dict.fromkeys(("attend", "output", "expand", "reduce"), pl.BlockSpec(memory_space=pl.ANY))
    places["bias"] = places["lengths"] = IN_SMEM

    def kernel(*refs):
        groups, start = [], 0
        for names in (in_names, outs, scratch):
            names = list(names)
            groups.append(types.SimpleNamespace(**dict(zip(names, refs[start : start + len(names)]))))
            start += len(names)
        layer_kernel(seq, batch, *groups)

    results = pl.pallas_call(
        kernel,
        out_shape=[jax.ShapeDtypeStruct(*out) for out in outs.values()],
        in_specs=[places.get(name, IN_VMEM) for name in in_names],
        out_specs=[IN_VMEM] * len(outs),
        scratch_shapes=list(scratch.values()),
        compiler_params=pltpu.CompilerParams(
            collective_id=0, has_side_effects=True, vmem_limit_bytes=63 * MIB
        ),
        name="layer",
    )(inputs, teacher, lengths, variates, observed, turns, bias, gains, attend, output, expand, reduce)
    return types.SimpleNamespace(**dict(zip(outs, results)))


def update_kernel(
    smalls, ins, small_outs, outs, olds, shares, news, copies, passed, in_sems, out_sems
):
    totals, count, gains, gains_first, gains_second, bias, bias_first, bias_second = smalls
    order = (2, 3, 0, 1)
    comes = []
    for place, number in enumerate(order):
        pairs = list(zip(ins[4 + 3 * number : 7 + 3 * number], olds[3 * number : 3 * number + 3]))
        pairs.append((ins[number], shares[number]))
        comes.append(
            [
                pltpu.make_async_copy(source, target, in_sems.at[4 * place + part])
                for part, (source, target) in enumerate(pairs)
            ]
        )
    for copy in sum(comes, []):
        copy.start()
    through = [
        pltpu.make_async_copy(ins[16 + part], passed[part], in_sems.at[16 + part]) for part in range(2)
    ]
    for copy in through:
        copy.start()
    goes = []
    gains_total = jnp.concatenate(
        [
            jnp.concatenate([totals[row + i : row + i + 1, :] for i in range(D // LANES)], axis=1)
            for row in (0, D // LANES)
        ],
        axis=0,
    )
    row = 2 * D // LANES
    bias_total = jnp.concatenate(
        [totals[row : row + 1, :HEADS], totals[row : row + 1, HEADS : 2 * HEADS]], axis=0
    )
    row += 1

    def sum_all(values):
        return jnp.sum(jnp.sum(values, axis=0, keepdims=True), axis=1, keepdims=True)

    squares = (
        totals[row : row + 1, 0:1] + sum_all(gains_total * gains_total) + sum_all(bias_total * bias_total)
    )
    grad_norm = jnp.sqrt(squares)
    clip = jnp.minimum(1.0, CLIP_NORM / grad_norm)
    small_outs[0][...] = totals[row : row + 1, 1:2] / (count[0:1, 0:1] * D)
    small_outs[1][...] = grad_norm
    rates = (RATE_ATTEND, RATE_OUTPUT, RATE_EXPAND, RATE_REDUCE)
    for place, number in enumerate(order):
        for copy in comes[place]:
            copy.wait()
        weight, first, second = olds[3 * number : 3 * number + 3]
        new, first_new, second_new = news[3 * number : 3 * number + 3]
        arrays = (new, copies[number], first_new, second_new, weight, first, second, shares[number])
        for lead in range(weight.shape[0] if weight.ndim == 3 else 1):

            def one_block(block, unused, lead=lead, arrays=arrays, rate=rates[number]):
                rows = block_of(block, 16)
                place = (lead, rows) if arrays[0].ndim == 3 else (rows,)
                old, moment, square, share = [array[place] for array in arrays[4:]]
                step = adam_step(old, moment, square, share.astype(WIDE) * clip, rate, WEIGHT_DECAY)
                arrays[0][place], arrays[2][place], arrays[3][place] = step
                arrays[1][place] = step[0].astype(LOW)
                return unused

            lax.fori_loop(0, weight.shape[-2] // 16, one_block, 0)
        for part, source in enumerate((new, copies[number], first_new, second_new)):
            copy = pltpu.make_async_copy(
                source, outs[2 + 4 * number + part], out_sems.at[2 + 4 * number + part]
            )
            copy.start()
            goes.append(copy)
        if place == 0:
            for part in range(2):
                through[part].wait()
                copy = pltpu.make_async_copy(passed[part], outs[part], out_sems.at[part])
                copy.start()
                goes.append(copy)
    for number, (old, total, rate) in enumerate(
        (
            ((gains, gains_first, gains_second), gains_total, RATE_GAINS),
            ((bias, bias_first, bias_second), bias_total, RATE_BIAS),
        )
    ):
        new, first_new, second_new = small_outs[2 + 3 * number : 5 + 3 * number]
        new[...], first_new[...], second_new[...] = adam_step(
            old[0][...], old[1][...], old[2][...], total * clip, rate, 0.0
        )
    for copy in goes:
        copy.wait()


def call_update(done, shares, smalls, olds):
    in_hbm = pl.BlockSpec(memory_space=pl.ANY)
    smalls = [done.totals, done.count] + smalls
    ins = shares + olds + [done.layer_output, done.input_gradient]
    one = jax.ShapeDtypeStruct((1, 1), WIDE)
    small_outs = [one, one] + smalls[2:]
    outs = [(done.layer_output, WIDE), (done.input_gradient, WIDE)]
    for weight in olds[::3]:
        outs += [(weight, dtype) for dtype in (WIDE, LOW, WIDE, WIDE)]
    passed = ins[-2:]
    parts = [smalls, ins, small_outs, outs, olds, shares, olds, olds[::3], passed]

    def kernel(*refs):
        groups, start = [], 0
        for part in parts:
            groups.append(refs[start : start + len(part)])
            start += len(part)
        update_kernel(*groups, *refs[start:])

    results = pl.pallas_call(
        kernel,
        out_shape=[jax.ShapeDtypeStruct(array.shape, WIDE) for array in small_outs]
        + [jax.ShapeDtypeStruct(array.shape, dtype) for array, dtype in outs],
        in_specs=[IN_VMEM] * len(smalls) + [in_hbm] * len(ins),
        out_specs=[IN_VMEM] * len(small_outs) + [in_hbm] * len(outs),
        scratch_shapes=[pltpu.VMEM(array.shape, WIDE) for array in olds]
        + [pltpu.VMEM(array.shape, array.dtype) for array in shares]
        + [pltpu.VMEM(array.shape, WIDE) for array in olds]
        + [pltpu.VMEM(array.shape, LOW) for array in olds[::3]]
        + [pltpu.VMEM(array.shape, WIDE) for array in passed]
        + [pltpu.SemaphoreType.DMA((18,)), pltpu.SemaphoreType.DMA((18,))],
        compiler_params=pltpu.CompilerParams(vmem_limit_bytes=63 * MIB),
        name="update",
    )(*smalls, *ins)
    return results[: len(small_outs)], results[len(small_outs) :]


def fast_body(
    seq,
    batch,
    inputs,
    teacher,
    lengths,
    variate_ids,
    time_ids,
    observed,
    attend_weight,
    output_weight,
    expand_weight,
    reduce_weight,
    norm_gains,
    variate_bias,
    attend_first,
    output_first,
    expand_first,
    reduce_first,
    gains_first,
    bias_first,
    attend_second,
    output_second,
    expand_second,
    reduce_second,
    gains_second,
    bias_second,
):
    half_dim = HEAD_DIM // 2
    frequency = jnp.exp(-math.log(ROPE_BASE) * jnp.arange(half_dim).astype(WIDE) / half_dim)
    angle = frequency[:, None] * time_ids.astype(WIDE)
    done = call_layer(
        seq,
        batch,
        inputs[0],
        teacher[0],
        lengths,
        variate_ids,
        observed,
        jnp.concatenate([jnp.cos(angle), jnp.sin(angle)]),
        variate_bias,
        norm_gains,
        attend_weight,
        output_weight,
        expand_weight,
        reduce_weight,
    )
    small, large = call_update(
        done,
        [done.attend_share, done.output_share, done.expand_share, done.reduce_share],
        [norm_gains, gains_first, gains_second, variate_bias, bias_first, bias_second],
        [attend_weight, attend_first, attend_second]
        + [output_weight, output_first, output_second]
        + [expand_weight, expand_first, expand_second]
        + [reduce_weight, reduce_first, reduce_second],
    )
    return (
        large[0][None],
        small[0].reshape(()),
        large[1][None],
        small[1].reshape(()),
    ) + tuple(large[2:] + small[2:])


def solution(mesh):
    seq, batch = mesh.shape["seq"], mesh.shape["batch"]
    body = functools.partial(fast_body, seq, batch) if fast_fits(seq, batch) else general_body
    in_specs = (
        P("batch", "seq", None),
        P("batch", "seq", None),
        P("batch"),
        P("batch", "seq"),
        P("batch", "seq"),
        P("batch", "seq"),
        P(None, ("seq", "batch"), None),
        P(("seq", "batch"), None),
        P(None, ("seq", "batch"), None),
        P(("seq", "batch"), None),
        P(),
        P(),
        P(None, ("seq", "batch"), None),
        P(("seq", "batch"), None),
        P(None, ("seq", "batch"), None),
        P(("seq", "batch"), None),
        P(),
        P(),
        P(None, ("seq", "batch"), None),
        P(("seq", "batch"), None),
        P(None, ("seq", "batch"), None),
        P(("seq", "batch"), None),
        P(),
        P(),
    )
    out_specs = (
        P("batch", "seq", None),
        P(),
        P("batch", "seq", None),
        P(),
        P(None, ("seq", "batch"), None),
        P(None, ("seq", "batch"), None),
        P(None, ("seq", "batch"), None),
        P(None, ("seq", "batch"), None),
        P(("seq", "batch"), None),
        P(("seq", "batch"), None),
        P(("seq", "batch"), None),
        P(("seq", "batch"), None),
        P(None, ("seq", "batch"), None),
        P(None, ("seq", "batch"), None),
        P(None, ("seq", "batch"), None),
        P(None, ("seq", "batch"), None),
        P(("seq", "batch"), None),
        P(("seq", "batch"), None),
        P(("seq", "batch"), None),
        P(("seq", "batch"), None),
        P(),
        P(),
        P(),
        P(),
        P(),
        P(),
    )
    return jax.shard_map(body, mesh=mesh, in_specs=in_specs, out_specs=out_specs, check_vma=False)
```

```python
import functools
import math
import types

import jax
import jax.numpy as jnp
from jax import lax
from jax.experimental import pallas as pl
from jax.experimental.pallas import tpu as pltpu
from jax.sharding import PartitionSpec as P

D = 1024
HEADS = 16
HEAD_DIM = 64
STEP = 10


NORM_EPS = 1e-05
ROPE_BASE = 10000.0
MASKED = -1e30
CLIP_NORM = 1.0
BETA_ONE = 0.9
BETA_TWO = 0.98
ADAM_EPS = 1e-08
WEIGHT_DECAY = 0.1
RATE_ATTEND = 0.03
RATE_OUTPUT = 0.5
RATE_EXPAND = 0.03
RATE_REDUCE = 0.015
RATE_GAINS = 1.0
RATE_BIAS = 0.5


def angles(times):
    half_dim = HEAD_DIM // 2
    frequency = jnp.exp(-math.log(ROPE_BASE) * jnp.arange(half_dim).astype(jnp.float32) / half_dim)
    angle_table = times.astype(jnp.float32)[..., None] * frequency
    return (jnp.cos(angle_table)[..., None, :], jnp.sin(angle_table)[..., None, :])


def rotate(values, cos_table, sin_table):
    half_dim = values.shape[-1] // 2
    first_half = values[..., :half_dim]
    second_half = values[..., half_dim:]
    return jnp.concatenate(
        [
            first_half * cos_table - second_half * sin_table,
            second_half * cos_table + first_half * sin_table,
        ],
        axis=-1,
    )


def unrotate(values, cos_table, sin_table):
    half_dim = values.shape[-1] // 2
    first_half = values[..., :half_dim]
    second_half = values[..., half_dim:]
    return jnp.concatenate(
        [
            first_half * cos_table + second_half * sin_table,
            second_half * cos_table - first_half * sin_table,
        ],
        axis=-1,
    )


def normalize(values):
    inv_scale = lax.rsqrt(jnp.mean(values * values, axis=-1, keepdims=True) + NORM_EPS)
    return (values * inv_scale, inv_scale)


def norm_back(grad_act, unit_rows, inv_scale, gain_row):
    grad_unit = grad_act * gain_row
    return inv_scale * (
        grad_unit - unit_rows * jnp.mean(grad_unit * unit_rows, axis=-1, keepdims=True)
    )


def score_block(query_rows, query_labels, key_rows, key_labels, bias_table):
    scores = jnp.einsum(
        "ihe,jhe->hij", query_rows, key_rows, preferred_element_type=jnp.float32
    ) * HEAD_DIM ** (-0.5)
    same_var = query_labels[:, None] == key_labels[None, :]
    scores = scores + jnp.where(
        same_var[None], bias_table[0][:, None, None], bias_table[1][:, None, None]
    )
    scores = jnp.where(key_labels[None, None, :] >= 0, scores, MASKED)
    return (scores, same_var)


def block_grads(
    query_rows,
    query_labels,
    grad_rows,
    lse_rows,
    delta_rows,
    key_rows,
    value_rows,
    key_labels,
    bias_table,
    need_query,
    need_keys,
):
    scores, same_var = score_block(query_rows, query_labels, key_rows, key_labels, bias_table)
    weights = jnp.exp(scores - lse_rows.T[:, :, None])
    grad_weights = jnp.einsum(
        "ihe,jhe->hij", grad_rows, value_rows, preferred_element_type=jnp.float32
    )
    grad_scores = (weights * (grad_weights - delta_rows.T[:, :, None])).astype(jnp.bfloat16)
    result = ()
    if need_query:
        grad_query = jnp.einsum(
            "hij,jhe->ihe", grad_scores, key_rows, preferred_element_type=jnp.float32
        ) * HEAD_DIM ** (-0.5)
        widened = grad_scores.astype(jnp.float32)
        bias_same = jnp.sum(jnp.where(same_var[None], widened, 0.0), axis=(1, 2))
        bias_other = jnp.sum(jnp.where(same_var[None], 0.0, widened), axis=(1, 2))
        result = result + (grad_query, jnp.stack([bias_same, bias_other]))
    if need_keys:
        grad_key = jnp.einsum(
            "hij,ihe->jhe", grad_scores, query_rows, preferred_element_type=jnp.float32
        ) * HEAD_DIM ** (-0.5)
        grad_value = jnp.einsum(
            "hij,ihe->jhe",
            weights.astype(jnp.bfloat16),
            grad_rows,
            preferred_element_type=jnp.float32,
        )
        result = result + (grad_key, grad_value)
    return result


def adam_step(weight, first_moment, second_moment, gradient, step_rate, decay_rate):
    first_moment = BETA_ONE * first_moment + (1.0 - BETA_ONE) * gradient
    second_moment = BETA_TWO * second_moment + (1.0 - BETA_TWO) * gradient * gradient
    direction = (
        first_moment
        / (1.0 - BETA_ONE**STEP)
        / (jnp.sqrt(second_moment / (1.0 - BETA_TWO**STEP)) + ADAM_EPS)
    )
    return (weight - step_rate * (direction + decay_rate * weight), first_moment, second_moment)


def general_body(
    inputs,
    teacher,
    lengths,
    variate_ids,
    time_ids,
    observed,
    attend_weight,
    output_weight,
    expand_weight,
    reduce_weight,
    norm_gains,
    variate_bias,
    attend_first,
    output_first,
    expand_first,
    reduce_first,
    gains_first,
    bias_first,
    attend_second,
    output_second,
    expand_second,
    reduce_second,
    gains_second,
    bias_second,
):
    row_count = inputs.shape[1]
    length = row_count * lax.axis_size("seq")
    block_rows = math.gcd(length, 1024)
    blocks = length // block_rows
    states = inputs[0].astype(jnp.float32)
    positions = lax.axis_index("seq") * row_count + jnp.arange(row_count, dtype=jnp.int32)
    inside = positions < lengths[0]
    scored = jnp.logical_and(inside, observed[0] == 1)
    local_count = jnp.sum(scored.astype(jnp.int32))
    count_early = lax.psum(local_count, ("seq", "batch"))
    full_attend, full_output, full_expand, full_reduce = (
        lax.all_gather(attend_weight.astype(jnp.bfloat16), ("seq", "batch"), axis=1, tiled=True),
        lax.all_gather(output_weight.astype(jnp.bfloat16), ("seq", "batch"), axis=0, tiled=True),
        lax.all_gather(expand_weight.astype(jnp.bfloat16), ("seq", "batch"), axis=1, tiled=True),
        lax.all_gather(reduce_weight.astype(jnp.bfloat16), ("seq", "batch"), axis=0, tiled=True),
    )
    unit_one, scale_one = normalize(states)
    act_one = (unit_one * norm_gains[0]).astype(jnp.bfloat16)
    project = jnp.einsum("td,cde->cte", act_one, full_attend, preferred_element_type=jnp.float32)
    cos_table, sin_table = angles(time_ids[0])
    query = rotate(project[0].reshape(row_count, HEADS, HEAD_DIM), cos_table, sin_table).astype(
        jnp.bfloat16
    )
    key_rows = (
        rotate(project[1].reshape(row_count, HEADS, HEAD_DIM), cos_table, sin_table)
        .astype(jnp.bfloat16)
        .reshape(row_count, D)
    )
    value_rows = project[2].astype(jnp.bfloat16)
    own_labels = jnp.where(inside, variate_ids[0], -1).astype(jnp.bfloat16)
    all_keys, all_values, all_labels = (
        lax.all_gather(key_rows, "seq", axis=0, tiled=True),
        lax.all_gather(value_rows, "seq", axis=0, tiled=True),
        lax.all_gather(own_labels, "seq", axis=0, tiled=True),
    )
    key_blocks = all_keys.reshape(blocks, block_rows, HEADS, HEAD_DIM)
    value_blocks = all_values.reshape(blocks, block_rows, HEADS, HEAD_DIM)
    label_blocks = all_labels.astype(jnp.float32).reshape(blocks, block_rows)
    query_labels = variate_ids[0].astype(jnp.float32)

    def sweep_top(carry, pieces):
        running, sum_exp = carry
        scores, same_var = score_block(query, query_labels, pieces[0], pieces[1], variate_bias)
        raised = jnp.maximum(running, jnp.floor(jnp.max(scores, axis=-1)))
        sum_exp = sum_exp * jnp.exp(running - raised) + jnp.sum(
            jnp.exp(scores - raised[..., None]), axis=-1
        )
        return ((raised, sum_exp), None)

    start_top = jnp.full((HEADS, row_count), MASKED, jnp.float32)
    (row_top, sum_exp), unused = lax.scan(
        sweep_top,
        (start_top, jnp.zeros((HEADS, row_count), jnp.float32)),
        (key_blocks, label_blocks),
    )
    log_total = row_top + jnp.log(sum_exp)

    def sweep_out(carry, pieces):
        coarse, finest = carry
        scores, same_var = score_block(query, query_labels, pieces[0], pieces[2], variate_bias)
        weights = jnp.exp(scores - log_total[..., None])
        rounded = weights.astype(jnp.bfloat16)
        residue = (weights - rounded.astype(jnp.float32)).astype(jnp.bfloat16)
        coarse = coarse + jnp.einsum(
            "hij,jhe->ihe", rounded, pieces[1], preferred_element_type=jnp.float32
        )
        finest = finest + jnp.einsum(
            "hij,jhe->ihe", residue, pieces[1], preferred_element_type=jnp.float32
        )
        return ((coarse, finest), None)

    zero_heads = jnp.zeros((row_count, HEADS, HEAD_DIM), jnp.float32)
    (coarse, finest), unused = lax.scan(
        sweep_out, (zero_heads, zero_heads), (key_blocks, value_blocks, label_blocks)
    )
    exact_heads = coarse + finest
    mixed = coarse.reshape(row_count, D).astype(jnp.bfloat16)
    middle = states + jnp.dot(mixed, full_output, preferred_element_type=jnp.float32)
    unit_two, scale_two = normalize(middle)
    act_two = (unit_two * norm_gains[1]).astype(jnp.bfloat16)
    gate_up = jnp.einsum("td,cdf->ctf", act_two, full_expand, preferred_element_type=jnp.float32)
    sigmoid = jax.nn.sigmoid(gate_up[0])
    hidden = (gate_up[0] * sigmoid * gate_up[1]).astype(jnp.bfloat16)
    output = middle + jnp.dot(hidden, full_reduce, preferred_element_type=jnp.float32)
    error = output - teacher[0].astype(jnp.float32)
    local_square = jnp.sum(jnp.where(scored[:, None], error * error, 0.0))
    square_total = lax.psum(local_square, ("seq", "batch"))
    count_all = count_early.astype(jnp.float32)
    loss = square_total / (count_all * D)
    grad_out = jnp.where(scored[:, None], error * (2.0 / (count_all * D)), 0.0)
    back_attend, back_output, back_expand, back_reduce = (
        lax.all_gather(attend_weight.astype(jnp.bfloat16), ("seq", "batch"), axis=1, tiled=True),
        lax.all_gather(output_weight.astype(jnp.bfloat16), ("seq", "batch"), axis=0, tiled=True),
        lax.all_gather(expand_weight.astype(jnp.bfloat16), ("seq", "batch"), axis=1, tiled=True),
        lax.all_gather(reduce_weight.astype(jnp.bfloat16), ("seq", "batch"), axis=0, tiled=True),
    )
    grad_branch = grad_out.astype(jnp.bfloat16)
    reduce_grad = jnp.einsum("tf,td->fd", hidden, grad_branch, preferred_element_type=jnp.float32)
    grad_hidden = jnp.einsum(
        "td,fd->tf", grad_branch, back_reduce, preferred_element_type=jnp.float32
    )
    grad_gate = grad_hidden * gate_up[1] * sigmoid * (1.0 + gate_up[0] * (1.0 - sigmoid))
    grad_up = grad_hidden * gate_up[0] * sigmoid
    grad_expand = jnp.stack([grad_gate, grad_up]).astype(jnp.bfloat16)
    expand_grad = jnp.einsum(
        "td,ctf->cdf", act_two, grad_expand, preferred_element_type=jnp.float32
    )
    grad_act_two = jnp.einsum(
        "ctf,cdf->td", grad_expand, back_expand, preferred_element_type=jnp.float32
    )
    expand_share, reduce_share = (
        lax.psum_scatter(expand_grad, ("seq", "batch"), scatter_dimension=1, tiled=True),
        lax.psum_scatter(reduce_grad, ("seq", "batch"), scatter_dimension=0, tiled=True),
    )
    grad_middle = grad_out + norm_back(grad_act_two, unit_two, scale_two, norm_gains[1])
    grad_attn = grad_middle.astype(jnp.bfloat16)
    output_grad = jnp.einsum("td,te->de", mixed, grad_attn, preferred_element_type=jnp.float32)
    grad_mixed = jnp.einsum(
        "te,de->td", grad_attn, back_output, preferred_element_type=jnp.float32
    ).astype(jnp.bfloat16)
    grad_heads = grad_mixed.reshape(row_count, HEADS, HEAD_DIM)
    row_delta = jnp.sum(grad_heads.astype(jnp.float32) * exact_heads, axis=-1)
    lse_rows = log_total.T
    zero_bias = jnp.zeros((2, HEADS), jnp.float32)

    def sweep_query(carry, pieces):
        part_query, part_bias = block_grads(
            query,
            query_labels,
            grad_heads,
            lse_rows,
            row_delta,
            pieces[0],
            pieces[1],
            pieces[2],
            variate_bias,
            True,
            False,
        )
        return ((carry[0] + part_query, carry[1] + part_bias), None)

    (query_total, bias_grad), unused = lax.scan(
        sweep_query, (zero_heads, zero_bias), (key_blocks, value_blocks, label_blocks)
    )
    all_query, all_grad = (
        lax.all_gather(query.reshape(row_count, D), "seq", axis=0, tiled=True),
        lax.all_gather(grad_mixed, "seq", axis=0, tiled=True),
    )
    all_lse, all_delta = (
        lax.all_gather(lse_rows, "seq", axis=0, tiled=True),
        lax.all_gather(row_delta, "seq", axis=0, tiled=True),
    )
    key_heads = key_rows.reshape(row_count, HEADS, HEAD_DIM)
    value_heads = value_rows.reshape(row_count, HEADS, HEAD_DIM)
    own_float = own_labels.astype(jnp.float32)

    def sweep_keys(carry, pieces):
        part_key, part_value = block_grads(
            pieces[0],
            pieces[1],
            pieces[2],
            pieces[3],
            pieces[4],
            key_heads,
            value_heads,
            own_float,
            variate_bias,
            False,
            True,
        )
        return ((carry[0] + part_key, carry[1] + part_value), None)

    (key_total, value_heads_total), unused = lax.scan(
        sweep_keys,
        (zero_heads, zero_heads),
        (
            all_query.reshape(blocks, block_rows, HEADS, HEAD_DIM),
            label_blocks,
            all_grad.reshape(blocks, block_rows, HEADS, HEAD_DIM),
            all_lse.reshape(blocks, block_rows, HEADS),
            all_delta.reshape(blocks, block_rows, HEADS),
        ),
    )
    value_total = value_heads_total.reshape(row_count, D)
    grad_query = unrotate(query_total, cos_table, sin_table).reshape(row_count, D)
    grad_key = unrotate(key_total, cos_table, sin_table).reshape(row_count, D)
    grad_project = jnp.stack([grad_query, grad_key, value_total]).astype(jnp.bfloat16)
    attend_grad = jnp.einsum(
        "td,cte->cde", act_one, grad_project, preferred_element_type=jnp.float32
    )
    grad_act_one = jnp.einsum(
        "cte,cde->td", grad_project, back_attend, preferred_element_type=jnp.float32
    )
    attend_share, output_share = (
        lax.psum_scatter(attend_grad, ("seq", "batch"), scatter_dimension=1, tiled=True),
        lax.psum_scatter(output_grad, ("seq", "batch"), scatter_dimension=0, tiled=True),
    )
    grad_input = grad_middle + norm_back(grad_act_one, unit_one, scale_one, norm_gains[0])
    gains_grad = jnp.stack(
        [jnp.sum(grad_act_one * unit_one, axis=0), jnp.sum(grad_act_two * unit_two, axis=0)]
    )
    local_squares = (
        jnp.sum(attend_share * attend_share)
        + jnp.sum(output_share * output_share)
        + jnp.sum(expand_share * expand_share)
        + jnp.sum(reduce_share * reduce_share)
    )
    gains_total, bias_total, square_sum = lax.psum(
        (gains_grad, bias_grad, local_squares), ("seq", "batch")
    )
    grad_norm = jnp.sqrt(
        square_sum + jnp.sum(gains_total * gains_total) + jnp.sum(bias_total * bias_total)
    )
    clip_scale = jnp.minimum(1.0, CLIP_NORM / grad_norm)
    attend_new, attend_first_new, attend_second_new = adam_step(
        attend_weight,
        attend_first,
        attend_second,
        attend_share * clip_scale,
        RATE_ATTEND,
        WEIGHT_DECAY,
    )
    output_new, output_first_new, output_second_new = adam_step(
        output_weight,
        output_first,
        output_second,
        output_share * clip_scale,
        RATE_OUTPUT,
        WEIGHT_DECAY,
    )
    expand_new, expand_first_new, expand_second_new = adam_step(
        expand_weight,
        expand_first,
        expand_second,
        expand_share * clip_scale,
        RATE_EXPAND,
        WEIGHT_DECAY,
    )
    reduce_new, reduce_first_new, reduce_second_new = adam_step(
        reduce_weight,
        reduce_first,
        reduce_second,
        reduce_share * clip_scale,
        RATE_REDUCE,
        WEIGHT_DECAY,
    )
    gains_new, gains_first_new, gains_second_new = adam_step(
        norm_gains, gains_first, gains_second, gains_total * clip_scale, RATE_GAINS, 0.0
    )
    bias_new, bias_first_new, bias_second_new = adam_step(
        variate_bias, bias_first, bias_second, bias_total * clip_scale, RATE_BIAS, 0.0
    )
    input_gradient = (grad_input * count_all * D)[None]
    return (
        output[None],
        loss,
        input_gradient,
        grad_norm,
        attend_new,
        attend_new.astype(jnp.bfloat16),
        attend_first_new,
        attend_second_new,
        output_new,
        output_new.astype(jnp.bfloat16),
        output_first_new,
        output_second_new,
        expand_new,
        expand_new.astype(jnp.bfloat16),
        expand_first_new,
        expand_second_new,
        reduce_new,
        reduce_new.astype(jnp.bfloat16),
        reduce_first_new,
        reduce_second_new,
        gains_new,
        gains_first_new,
        gains_second_new,
        bias_new,
        bias_first_new,
        bias_second_new,
    )


MESH = pl.DeviceIdType.MESH
IN_VMEM = pl.BlockSpec(memory_space=pltpu.VMEM)
IN_SMEM = pl.BlockSpec(memory_space=pltpu.SMEM)
LANES = 128
HEADS_HERE = LANES // HEAD_DIM
VARIATES = 16
MIB = 1 << 20
LOW = jnp.bfloat16
WIDE = jnp.float32
TOTAL_ROWS = 24


def fast_fits(seq, batch):
    return seq == 8 and batch == 4 and seq * LANES == D


def flip(index, mask):
    result, bit = index, 1
    while bit <= mask:
        if mask & bit:
            result = result + bit - 2 * bit * lax.rem(lax.div(index, bit), 2)
        bit *= 2
    return result


def push(source, target, send_sem, recv_sem, device):
    return pltpu.make_async_remote_copy(
        src_ref=source,
        dst_ref=target,
        send_sem=send_sem,
        recv_sem=recv_sem,
        device_id=device,
        device_id_type=MESH,
    )


def block_of(index, size):
    return pl.ds(pl.multiple_of(index * size, size), size)


def dot(left, right):
    return jnp.dot(left, right, preferred_element_type=WIDE)


def dot_turned(left, right):
    return lax.dot_general(left, right, (((1,), (1,)), ((), ())), preferred_element_type=WIDE)


def turned_dot(left, right):
    return lax.dot_general(left, right, (((0,), (0,)), ((), ())), preferred_element_type=WIDE)


class Team:
    def __init__(self, index, place):
        self.index, self.place = index, place

    def at(self, mask):
        return flip(self.index, mask)


def head_team(me, group):
    return Team(me, lambda mask: (flip(me, mask), group))


def feed_team(me, group):
    return Team(
        4 * lax.rem(group, 2) + lax.rem(me, 4),
        lambda mask: (flip(me, mask % 4), flip(group, mask // 4)),
    )


class Gather:
    def __init__(self, team, rows, all_rows, sends, recvs):
        self.team, self.all_rows, self.sends, self.recvs = team, all_rows, sends, recvs
        self.size = all_rows.shape[0] // 8
        self.given = rows
        self.rows = all_rows.at[block_of(team.index, self.size)] if rows is None else rows

    def copy(self, mask, passing):
        source = self.all_rows.at[block_of(self.team.at(mask - 1 if passing else 0), self.size)]
        return push(
            source if passing else self.rows,
            source,
            self.sends.at[mask],
            self.recvs.at[mask],
            self.team.place(1 if passing else mask),
        )

    def start(self, masks=(6, 2, 4, 1)):
        for mask in masks:
            self.copy(mask, False).start()
        if self.given is not None:
            self.all_rows[block_of(self.team.index, self.size)] = self.given[...]

    def pass_on(self, chip):
        self.copy(2 * chip, False).wait_recv()
        self.copy(2 * chip + 1, True).start()

    def complete(self, chip):
        self.copy(2 * chip + 1, chip > 0).wait_recv()

    def finish(self):
        for mask in (6, 2, 4, 1):
            self.copy(mask, False).wait_send()
        for mask in (3, 5, 7):
            self.copy(mask, True).wait_send()


def at_step(step, number, *works):
    @pl.when(step == number)
    def _():
        for work in works:
            work()


def each_chip(gather, work, after):
    def one_chip(chip, unused):
        @pl.when(chip == 0)
        def _():
            gather.complete(0)

        @pl.when(chip == 1)
        def _():
            gather.pass_on(1)
            gather.pass_on(2)
            gather.copy(6, False).start()
            gather.complete(1)

        @pl.when(chip == 2)
        def _():
            gather.complete(2)

        @pl.when(chip == 3)
        def _():
            gather.pass_on(3)
            gather.complete(3)

        work(chip)
        for number, works in after.items():
            at_step(chip, number, *works)
        return unused

    lax.fori_loop(0, 4, one_chip, 0)
    gather.finish()


class Scatter:
    def __init__(self, team, buffers, near_sends, near_recvs, far_sends, far_recvs):
        self.whole, self.keep, self.near_from, self.near, self.far_from, self.far = buffers
        self.sems = near_sends, near_recvs, far_sends, far_recvs
        self.team = team
        self.size = self.keep.shape[1]

    def near_copy(self, chip):
        return push(
            self.near_from.at[chip],
            self.near.at[chip],
            self.sems[0].at[chip],
            self.sems[1].at[chip],
            self.team.place(1),
        )

    def far_copy(self, chip):
        return push(
            self.far_from.at[chip],
            self.far.at[chip],
            self.sems[2].at[chip],
            self.sems[3].at[chip],
            self.team.place(2 * chip),
        )

    def put(self, chip, rows):
        core = lax.rem(self.team.index, 2)
        self.whole[...] = rows
        self.near_from[chip] = self.whole[block_of(1 - core, self.size)].astype(LOW)
        self.near_copy(chip).start()
        self.keep[chip] = self.whole[block_of(core, self.size)]

    def combine(self, chip):
        self.near_copy(chip).wait_recv()
        self.far_from[chip] = (self.keep[chip] + self.near[chip].astype(WIDE)).astype(LOW)
        self.far_copy(chip).start()

    def total(self):
        self.near_copy(0).wait_recv()
        total = self.keep[0] + self.near[0].astype(WIDE)
        for chip in (1, 2, 3):
            self.far_copy(chip).wait_recv()
            total = total + self.far[chip].astype(WIDE)
        for chip in (0, 1, 2, 3):
            self.near_copy(chip).wait_send()
            if chip:
                self.far_copy(chip).wait_send()
        return total


class LineGather:
    def __init__(self, part_of, sends, recvs, me, group):
        self.part_of, self.sends, self.recvs, self.me, self.group = part_of, sends, recvs, me, group
        self.middle = jnp.logical_and(group >= 1, group <= 2)

    def copy(self, part, target, slot):
        return push(
            self.part_of(part),
            self.part_of(part),
            self.sends.at[slot],
            self.recvs.at[part],
            (self.me, target),
        )

    def start(self):
        group = self.group

        @pl.when(self.middle)
        def _():
            self.copy(group, 3 - group, 3 - group).start()
            self.copy(group, 3 * (group - 1), 3 * (group - 1)).start()

        @pl.when(jnp.logical_not(self.middle))
        def _():
            for step in (2, 1, 3):
                other = lax.rem(group + step, 4)
                self.copy(group, other, other).start()

    def pass_on(self):
        group = self.group

        @pl.when(self.middle)
        def _():
            self.copy(3 - group, 3 * (group - 1), group).wait_recv()
            self.copy(3 - group, 3 * (group - 1), group).start()

    def land(self):
        group = self.group

        @pl.when(self.middle)
        def _():
            for part in (0, 3):
                self.copy(part, 3 - group, group).wait_recv()

        @pl.when(jnp.logical_not(self.middle))
        def _():
            for step in (1, 2, 3):
                other = lax.rem(group + step, 4)
                self.copy(other, other, other).wait_recv()

    def finish(self):
        group = self.group

        @pl.when(self.middle)
        def _():
            for other in (3 - group, 3 * (group - 1), group):
                self.copy(group, 3 - group, other).wait_send()

        @pl.when(jnp.logical_not(self.middle))
        def _():
            for step in (1, 2, 3):
                other = lax.rem(group + step, 4)
                self.copy(group, other, other).wait_send()


class LineScatter:
    def __init__(self, part_of, landing, sends, recvs, me, group):
        self.part_of, self.landing, self.sends, self.recvs = part_of, landing, sends, recvs
        self.me, self.group = me, group
        self.middle = jnp.logical_and(group >= 1, group <= 2)
        self.opposite = 3 - 3 * lax.div(group, 2)

    def copy(self, part, slot, target, sem):
        return push(
            self.part_of(part),
            self.landing.at[slot],
            self.sends.at[sem],
            self.recvs.at[slot],
            (self.me, target),
        )

    def start(self):
        group = self.group

        @pl.when(self.middle)
        def _():
            for other in (3 - group, 3 * (group - 1)):
                self.copy(other, group, other, other).start()

        @pl.when(jnp.logical_not(self.middle))
        def _():
            beside = 1 + lax.div(group, 3)
            self.copy(3 - group, beside, beside, 3 - group).start()
            for other in (3 - beside, beside):
                self.copy(other, group, other, other).start()

    def pass_on(self):
        group, opposite = self.group, self.opposite

        @pl.when(self.middle)
        def _():
            self.copy(opposite, group, opposite, group).wait_recv()
            part = self.part_of(opposite)
            part[...] = (part[...].astype(WIDE) + self.landing[group].astype(WIDE)).astype(LOW)
            self.copy(opposite, group, opposite, group).start()

    def land(self):
        group = self.group

        @pl.when(self.middle)
        def _():
            for slot in (0, 3 - group, 3):
                self.copy(group, slot, 3 - group, group).wait_recv()

        @pl.when(jnp.logical_not(self.middle))
        def _():
            for slot in (1, 2):
                self.copy(group, slot, slot, group).wait_recv()

    def add(self, own, landed, store):
        group = self.group

        @pl.when(self.middle)
        def _():
            store(own() + landed(0) + landed(3 - group) + landed(3))

        @pl.when(jnp.logical_not(self.middle))
        def _():
            store(own() + landed(1) + landed(2))

    def finish(self):
        group = self.group

        @pl.when(self.middle)
        def _():
            for sem in (3 - group, 3 * (group - 1), group):
                self.copy(group, group, 3 - group, sem).wait_send()

        @pl.when(jnp.logical_not(self.middle))
        def _():
            for sem in (3 - group, 1, 2):
                self.copy(group, group, 1, sem).wait_send()


class QuadGather:
    def __init__(self, part_of, sends, recvs, me, group):
        self.part_of, self.sends, self.recvs = part_of, sends, recvs
        self.part = 2 * lax.div(me, 4) + lax.div(group, 2)
        self.along_y, self.along_z = (flip(me, 4), group), (me, flip(group, 2))

    def copy(self, way):
        part = self.part_of(flip(self.part, 1) if way == 3 else self.part)
        device = self.along_z if way == 1 else self.along_y
        return push(part, part, self.sends.at[way], self.recvs.at[way], device)

    def start_y(self):
        self.copy(2).start()

    def start_z(self):
        self.copy(1).start()

    def pass_on(self):
        self.copy(1).wait_recv()
        self.copy(3).start()

    def land(self):
        self.copy(2).wait_recv()
        self.copy(3).wait_recv()

    def finish(self):
        for way in (1, 2, 3):
            self.copy(way).wait_send()


class QuadScatter:
    def __init__(self, part_of, landing, sends, recvs, me, group):
        self.part_of, self.landing, self.sends, self.recvs = part_of, landing, sends, recvs
        self.part = 2 * lax.div(me, 4) + lax.div(group, 2)
        self.along_y, self.along_z = (flip(me, 4), group), (me, flip(group, 2))

    def copy(self, slot):
        return push(
            self.part_of(flip(self.part, (2, 3, 1)[slot])),
            self.landing.at[slot],
            self.sends.at[slot],
            self.recvs.at[slot],
            self.along_z if slot == 2 else self.along_y,
        )

    def start_far(self):
        self.copy(1).start()

    def start_near(self):
        self.copy(0).start()

    def pass_on(self):
        self.copy(1).wait_recv()
        part = self.part_of(flip(self.part, 1))
        part[...] = (part[...].astype(WIDE) + self.landing[1].astype(WIDE)).astype(LOW)
        self.copy(2).start()

    def land(self):
        self.copy(0).wait_recv()
        self.copy(2).wait_recv()

    def finish(self):
        for slot in (0, 1, 2):
            self.copy(slot).wait_send()


def chip_of(team, chip):
    here = lax.div(team.index, 2)
    if isinstance(chip, int):
        return flip(here, chip)
    column = lax.rem(lax.rem(here, 2) + lax.rem(chip, 2), 2)
    row = lax.rem(lax.div(here, 2) + lax.div(chip, 2), 2)
    return 2 * row + column


def turn_rows(values, cosine, sine):
    half = HEAD_DIM // 2
    pieces = []
    for start in range(0, values.shape[0], HEAD_DIM):
        first, second = values[start : start + half], values[start + half : start + HEAD_DIM]
        pieces += [first * cosine - second * sine, second * cosine + first * sine]
    return jnp.concatenate(pieces, axis=0)


def thirds(values):
    first = values.astype(LOW).astype(WIDE)
    second = (values - first).astype(LOW).astype(WIDE)
    return first, second, values - first - second


def pick(row, choices):
    result = jnp.zeros(row.shape, WIDE)
    for number, choice in choices.items():
        result = jnp.where(row == number, choice, result)
    return result


def norm_rows(values):
    scale = lax.rsqrt(jnp.mean(values * values, axis=-1, keepdims=True) + NORM_EPS)
    return values * scale, scale


def feed_block(block):
    y, x, core, far_z, near_z = (block // 16, block // 8 % 2, block // 4 % 2, block // 2 % 2, block % 2)
    return 4 * near_z + 2 * x + core, 2 * y + far_z


def layer_kernel(seq, batch, ins, outs, mem):
    me, group = lax.axis_index("seq"), lax.axis_index("batch")
    rows = ins.inputs.shape[0]
    length = rows * seq
    pair = 2 * rows
    share = ins.attend.shape[1]
    wide_columns = ins.expand.shape[2] // D
    hidden_width = mem.reduce_all.shape[0] * mem.reduce_all.shape[1]
    blocks = ins.expand.shape[2] // LANES
    heads, feeds = head_team(me, group), feed_team(me, group)
    quad = 2 * lax.div(me, 4) + lax.div(group, 2)

    staged = [(ins.attend.at[which], mem.keep.at[0, block_of(which, share)]) for which in range(3)]
    staged.append((ins.output, mem.keep.at[0, block_of(3, share)]))
    staged.append((ins.reduce, mem.keep.at[1]))
    for which in range(2):
        for block in range(wide_columns):
            columns = slice(block * D, (block + 1) * D)
            staged.append(
                (ins.expand.at[which, :, columns], mem.keep.at[2 + which, block_of(block, share)])
            )
    staged = [
        pltpu.make_async_copy(source, target, mem.stage_sem.at[number])
        for number, (source, target) in enumerate(staged)
    ]
    for copy in staged:
        copy.start()
    barrier = pltpu.get_barrier_semaphore()
    for mask in range(1, seq):
        pl.semaphore_signal(barrier, inc=1, device_id=(flip(me, mask), group), device_id_type=MESH)
    for step in range(1, batch):
        pl.semaphore_signal(
            barrier, inc=1, device_id=(me, lax.rem(group + step, batch)), device_id_type=MESH
        )
    for mask in (5, 6, 7):
        pl.semaphore_signal(barrier, inc=1, device_id=feeds.place(mask), device_id_type=MESH)

    position = me * rows + lax.broadcasted_iota(jnp.int32, (1, rows), 1)
    inside = position < ins.lengths[0]
    scored = jnp.logical_and(inside, ins.observed[...] == 1).astype(WIDE)
    variate = ins.variates[...].astype(WIDE)
    turns = ins.turns.shape[0]
    mem.facts_own[:turns] = ins.turns[...]
    mem.facts_own[turns:] = jnp.concatenate(
        [jnp.where(inside, variate, -1.0), variate, scored, jnp.zeros((5, rows), WIDE)], axis=0
    )
    mem.scored[...] = jnp.broadcast_to(scored, (rows, rows)).T
    unit_one, scale_one = norm_rows(ins.inputs[...].astype(WIDE))
    mem.own_rows[0] = (unit_one * ins.gains[0:1, :]).astype(LOW)
    for copy in staged:
        copy.wait()
    for which in range(3):
        mem.attend_low[which] = mem.keep[0, block_of(which, share)].astype(LOW)
    mem.output_full[block_of(batch * me + group, share)] = mem.keep[0, block_of(3, share)].astype(LOW)
    mem.reduce_all[quad] = mem.keep[1].astype(LOW)
    for which in range(2):
        for block in range(blocks):
            owner, part = feed_block(block)
            row, lane = divmod(block * LANES, D)
            mem.expand_low[which, owner, :, part * LANES : (part + 1) * LANES] = mem.keep[
                2 + which, block_of(row, share), lane : lane + LANES
            ].astype(LOW)
    pl.semaphore_wait(barrier, seq + batch + 1)

    masks = (6, 7, 4, 5, 2, 3, 1)

    def start_attend_columns():
        copies = []
        for mask in masks:
            copy = push(
                mem.attend_low.at[:, :, block_of(heads.at(mask), LANES)],
                mem.attend_all.at[:, me, group],
                mem.column_send.at[0, mask],
                mem.column_recv.at[0, mask],
                heads.place(mask),
            )
            copy.start()
            copies.append(copy)
        mem.attend_all[:, me, group] = mem.attend_low[:, :, block_of(me, LANES)]
        return copies

    def start_expand_columns():
        copies = []
        for mask in masks:
            copy = push(
                mem.expand_low.at[:, feeds.at(mask)],
                mem.expand_all.at[:, me, group],
                mem.column_send.at[1, mask],
                mem.column_recv.at[1, mask],
                feeds.place(mask),
            )
            copy.start()
            copies.append(copy)
        mem.expand_all[:, me, group] = mem.expand_low[:, feeds.index]
        return copies

    def expand_part_of(array, which):
        def part_of(part):
            return array.at[which, pl.ds(4 * lax.div(part, 2), 4), pl.ds(2 * lax.rem(part, 2), 2)]

        return part_of

    def line_gather(row, part_of):
        return LineGather(part_of, mem.line_send.at[row], mem.line_recv.at[row], me, group)

    def quad_gather(row, part_of):
        return QuadGather(part_of, mem.line_send.at[row], mem.line_recv.at[row], me, group)

    def gather(team, phase, all_rows):
        return Gather(
            team,
            mem.own_rows.at[phase],
            all_rows,
            mem.gather_send.at[phase],
            mem.gather_recv.at[phase],
        )

    def scatter(team, phase):
        return Scatter(
            team,
            (mem.whole, mem.keep, mem.near_from, mem.near, mem.far_from, mem.far),
            mem.near_send.at[phase],
            mem.near_recv.at[phase],
            mem.far_send.at[phase],
            mem.far_recv.at[phase],
        )

    attend_columns = start_attend_columns()
    line_output = line_gather(1, lambda part: mem.output_full.at[block_of(batch * me + part, share)])
    line_output.start()
    facts = Gather(heads, mem.facts_own, mem.facts_all, mem.facts_send, mem.facts_recv)
    facts.start()
    for copy in attend_columns:
        copy.wait_recv()
    line_attend = line_gather(0, lambda part: mem.attend_all.at[:, :, part])
    line_attend.start()
    acts = gather(heads, 0, mem.act_one)
    acts.start()
    for chip in (1, 2, 3):
        facts.pass_on(chip)
    for chip in (0, 1, 2, 3):
        facts.complete(chip)
    facts.finish()
    step_rows = mem.facts_own.shape[0]
    half = HEAD_DIM // 2
    count = jnp.zeros((8, LANES), WIDE)
    for slot in range(seq):
        columns = slice(slot * rows, (slot + 1) * rows)
        start = slot * step_rows
        mem.cosine[:, columns] = mem.facts_all[start : start + half]
        mem.sine[:, columns] = mem.facts_all[start + half : start + 2 * half]
        labels = mem.facts_all[start + 2 * half : start + 2 * half + 8]
        mem.labels[:, columns] = labels
        count = count + labels
    mem.count[group] = count
    count_copies = []
    for step in range(1, batch):
        copy = push(
            mem.count.at[group],
            mem.count.at[group],
            mem.count_send.at[step],
            mem.count_recv.at[step],
            (me, lax.rem(group + step, batch)),
        )
        copy.start()
        count_copies.append(copy)

    def mark(block, unused):
        span = block_of(block, pair)
        row = lax.broadcasted_iota(jnp.int32, (HEAD_DIM, pair), 0)
        third = lax.div(row, VARIATES)
        variate = lax.rem(row, VARIATES).astype(WIDE)
        key_label, query_label = mem.labels[0:1, span], mem.labels[1:2, span]
        ones = jnp.ones((1, pair), WIDE)
        last = 3 * VARIATES
        hidden_keys = (key_label < 0.0).astype(WIDE)
        mem.key_marks[:, span] = jnp.where(
            third < 3,
            (key_label == variate).astype(WIDE),
            pick(row, {last: ones, last + 1: ones, last + 2: ones, last + 3: hidden_keys}),
        ).astype(LOW)
        query_marks = (query_label == variate).astype(WIDE)
        mem.sum_marks[:, span] = jnp.where(
            row < VARIATES, query_marks, pick(row, {VARIATES: ones})
        ).astype(LOW)
        for head in range(HEADS_HERE):
            number = me * HEADS_HERE + head
            other = jnp.full((HEAD_DIM, pair), ins.bias[1, number], WIDE)
            more = thirds(jnp.full((HEAD_DIM, pair), ins.bias[0, number], WIDE) - other)
            other = thirds(other)
            mem.query_turned[head, HEAD_DIM:, span] = jnp.where(
                third < 3,
                query_marks * jnp.where(third == 0, more[0], jnp.where(third == 1, more[1], more[2])),
                pick(row, {last: other[0], last + 1: other[1], last + 2: other[2], last + 3: MASKED}),
            ).astype(LOW)
        return unused

    lax.fori_loop(0, length // pair, mark, 0)
    acts.pass_on(1)
    acts.pass_on(2)
    line_output.pass_on()
    line_output.land()
    outputs = Gather(heads, None, mem.output_full, mem.output_send, mem.output_recv)
    outputs.start()
    acts.pass_on(3)
    line_attend.pass_on()
    for chip in range(4):
        acts.complete(chip)
    acts.finish()

    expand_columns = start_expand_columns()
    line_reduce = quad_gather(4, lambda part: mem.reduce_all.at[part])
    line_reduce.start_z()
    line_expand = [
        quad_gather(2 + which, expand_part_of(mem.expand_all, which)) for which in range(2)
    ]
    line_attend.land()
    line_reduce.start_y()

    def attend_matrix(which):
        return mem.attend_all[which].reshape(D, LANES)

    def project(block, unused):
        span = block_of(block, pair)
        act = mem.act_one[span, :]
        cosine, sine = mem.cosine[:, span], mem.sine[:, span]
        query = turn_rows(dot(act, attend_matrix(0)).T, cosine, sine).astype(LOW)
        query = (query.astype(WIDE) * HEAD_DIM ** (-0.5)).astype(LOW)
        key = turn_rows(dot(act, attend_matrix(1)).T, cosine, sine).astype(LOW)
        value = dot(act, attend_matrix(2)).T.astype(LOW)
        mem.key_turned[:, span] = key
        mem.value_turned[:, span] = value

        for head in range(HEADS_HERE):
            features = slice(head * HEAD_DIM, (head + 1) * HEAD_DIM)
            mem.query_turned[head, :HEAD_DIM, span] = query[features]
            whole = jnp.concatenate([key[features], mem.key_marks[:, span]], axis=0)
            mem.key_heads[head, span, :] = whole.T
        return unused

    for copy in expand_columns:
        copy.wait_recv()
    line_expand[0].start_z()
    line_expand[0].start_y()
    lax.fori_loop(0, length // pair, project, 0)
    line_expand[1].start_z()
    outputs.pass_on(1)
    outputs.pass_on(2)

    core = lax.rem(me, 2)

    def mixed_copy(chip, which):
        other = 2 * chip_of(heads, chip) + which
        slot = 2 * chip + lax.rem(which + core, 2)
        return push(
            mem.mixed_out.at[block_of(other, rows)],
            mem.mixed_rows.at[:, block_of(me, LANES)],
            mem.mixed_send.at[slot],
            mem.mixed_recv.at[slot],
            (other, group),
        )

    def attend_block(chip):
        columns = block_of(chip_of(heads, chip), pair)
        for head in range(HEADS_HERE):
            span = slice(head * HEAD_DIM, (head + 1) * HEAD_DIM)
            scores = dot(mem.key_heads[head], mem.query_turned[head, :, columns])
            top = jnp.floor(jnp.max(scores, axis=0, keepdims=True))
            powers = jnp.exp(scores - top)
            probs = powers * (1.0 / jnp.sum(powers, axis=0, keepdims=True))
            rounded = probs.astype(LOW)
            mem.probs[head, :, columns] = rounded
            residue = (probs - rounded.astype(WIDE)).astype(LOW)
            coarse = dot(mem.value_turned[span, :], rounded)
            mem.exact[span, columns] = coarse + dot(mem.value_turned[span, :], residue)
            mem.mixed_wide[span, :] = coarse
        mixed = mem.mixed_wide[...].astype(LOW)
        mem.mixed_turned[:, columns] = mixed
        mem.mixed_out[columns, :] = mixed.T

    def attend_step(step, unused):
        chip = lax.rem(step + 1, 4)
        attend_block(chip)
        for which in range(2):

            @pl.when(jnp.logical_or(chip > 0, core != which))
            def _():
                mixed_copy(chip, which).start()

        at_step(step, 1, lambda: outputs.pass_on(3))
        return unused

    lax.fori_loop(0, 4, attend_step, 0)
    line_expand[1].start_y()
    mem.mixed_rows[:, block_of(me, LANES)] = mem.mixed_out[block_of(me, rows), :]
    for chip in range(4):
        outputs.complete(chip)
    outputs.finish()

    def wait_pieces(copy):
        for mask in range(1, seq):
            copy(mask).wait()

    def mixed_wait(mask):
        other = heads.at(mask)
        return push(
            mem.mixed_out.at[block_of(other, rows)],
            mem.mixed_rows.at[:, block_of(other, LANES)],
            mem.mixed_send.at[mask],
            mem.mixed_recv.at[mask],
            (other, group),
        )

    wait_pieces(mixed_wait)
    middle = ins.inputs[...].astype(WIDE) + dot(mem.mixed_rows[...], mem.output_full[...])
    mem.middle[...] = middle
    unit_two, scale_two = norm_rows(middle)
    mem.own_rows[1] = (unit_two * ins.gains[1:2, :]).astype(LOW)
    acts = gather(feeds, 1, mem.act_two)
    acts.start((2, 4, 1))
    line_reduce.pass_on()
    line_expand[0].pass_on()

    def split_heads(block, unused):
        span = block_of(block, pair)
        row = lax.broadcasted_iota(jnp.int32, (HEAD_DIM, pair), 0)
        value_marks = jnp.where(row < 3, 1.0, 0.0).astype(LOW)
        for head in range(HEADS_HERE):
            features = slice(head * HEAD_DIM, (head + 1) * HEAD_DIM)
            value = mem.value_turned[features, span]
            mem.value_heads[head, span, :] = jnp.concatenate([value, value_marks], axis=0).T
            query = mem.query_turned[head, :HEAD_DIM, span]
            whole = jnp.concatenate([query, mem.sum_marks[:, span]], axis=0)
            mem.query_heads[head, span, :] = whole.T
        return unused

    lax.fori_loop(0, length // pair, split_heads, 0)
    line_expand[0].land()

    def expand_matrix(which):
        return mem.expand_all[which].reshape(D, hidden_width)

    def reduce_matrix():
        return mem.reduce_all[...].reshape(hidden_width, D)

    def feed_gate(chip):
        span = block_of(chip_of(feeds, chip), pair)
        mem.by_gate[span, :] = dot(mem.act_two[span, :], expand_matrix(0))

    def feed_up(chip, unused=0):
        span = block_of(chip_of(feeds, chip), pair)
        gate = mem.by_gate[span, :]
        up = dot(mem.act_two[span, :], expand_matrix(1))
        sigmoid = 1.0 / (1.0 + jnp.exp(-gate))
        swish = gate * sigmoid
        mem.by_up[span, :] = swish
        mem.by_gate[span, :] = up * sigmoid * (1.0 + gate * (1.0 - sigmoid))
        mem.hidden[span, :] = (swish * up).astype(LOW)
        return unused

    each_chip(
        acts,
        feed_gate,
        {
            0: [line_expand[1].pass_on],
            2: [line_expand[1].land, lambda: lax.fori_loop(0, 3, feed_up, 0)],
            3: [lambda: lax.fori_loop(3, 4, feed_up, 0)],
        },
    )
    line_reduce.land()
    sums = scatter(feeds, 1)

    def feed_down(step, unused):
        chip = lax.rem(step + 1, 4)
        span = block_of(chip_of(feeds, chip), pair)
        sums.put(chip, dot(mem.hidden[span, :], reduce_matrix()))
        at_step(step, 1, lambda: sums.combine(1))
        at_step(step, 2, lambda: sums.combine(2))
        return unused

    lax.fori_loop(0, 4, feed_down, 0)
    sums.combine(3)

    for block in range(length // pair):
        span = block_of(block, pair)
        mem.hidden_turned[:, span] = mem.hidden[span, :].T
        mem.act_two_turned[:, span] = mem.act_two[span, :].T
    output = mem.middle[...] + sums.total()
    outs.layer_output[...] = output
    for copy in count_copies:
        copy.wait()
    count_all = jnp.sum(
        mem.count[0, 2:3] + mem.count[1, 2:3] + mem.count[2, 2:3] + mem.count[3, 2:3],
        axis=1,
        keepdims=True,
    )
    error = jnp.where(mem.scored[:, 0:1] > 0.0, output - ins.teacher[...].astype(WIDE), 0.0)
    mem.squares[1:2, :] = jnp.sum(error * error, axis=0, keepdims=True)
    grad_out = error * (2.0 / (count_all * D))
    mem.grad_own[...] = grad_out
    mem.own_rows[2] = grad_out.astype(LOW)
    acts = gather(feeds, 2, mem.branch)
    acts.start((2, 4, 1))

    sums = scatter(feeds, 2)

    def feed_back(chip):
        span = block_of(chip_of(feeds, chip), pair)
        grad_hidden = dot_turned(mem.branch[span, :], reduce_matrix())
        grad_gate = (grad_hidden * mem.by_gate[span, :]).astype(LOW)
        grad_up = (grad_hidden * mem.by_up[span, :]).astype(LOW)
        mem.grad_gate[span, :] = grad_gate
        mem.grad_up[span, :] = grad_up
        sums.put(
            chip,
            dot_turned(grad_gate, expand_matrix(0)) + dot_turned(grad_up, expand_matrix(1)),
        )

    each_chip(acts, feed_back, {2: [lambda: sums.combine(1)], 3: [lambda: sums.combine(2)]})

    def line_scatter(row, part_of, landing):
        return LineScatter(
            part_of, landing, mem.back_send.at[row], mem.back_recv.at[row], me, group
        )

    def quad_scatter(row, part_of, landing):
        return QuadScatter(
            part_of, landing, mem.back_send.at[row], mem.back_recv.at[row], me, group
        )

    def reduce_grad(part, unused):
        mem.reduce_grad[part] = dot(
            mem.hidden_turned[block_of(part, rows), :], mem.branch[...]
        ).astype(LOW)
        at_step(part, 0, lambda: sums.combine(3))
        return unused

    lax.fori_loop(0, batch, reduce_grad, 0)
    back_reduce = quad_scatter(0, lambda part: mem.reduce_grad.at[part], mem.reduce_land)
    back_reduce.start_far()

    def expand_grad(which):
        grads = (mem.grad_gate, mem.grad_up)[which]

        def one_block(block, unused):
            products = dot(mem.act_two_turned[block_of(block, pair), :], grads[...]).astype(LOW)
            mem.expand_grad[which, pl.ds(2 * block, 2)] = products.reshape(
                2, batch, share, hidden_width
            )
            return unused

        lax.fori_loop(0, seq // 2, one_block, 0)
        line = quad_scatter(
            1 + which, expand_part_of(mem.expand_grad, which), mem.expand_land.at[which]
        )
        return line

    back_expand = []
    back_expand.append(expand_grad(0))
    back_expand[0].start_far()
    grad_act = sums.total()
    unit_two, scale_two = norm_rows(mem.middle[...])
    gain = ins.gains[1:2, :]
    grad_unit = grad_act * gain
    mem.gains[1:2, :] = jnp.sum(grad_act * unit_two, axis=0, keepdims=True)
    grad_middle = mem.grad_own[...] + scale_two * (
        grad_unit - unit_two * jnp.mean(grad_unit * unit_two, axis=-1, keepdims=True)
    )
    mem.grad_own[...] = grad_middle
    mem.own_rows[3] = grad_middle.astype(LOW)
    grad_mixed = dot(mem.output_full[...], grad_middle.T.astype(LOW)).astype(LOW)
    mem.grad_mixed_out[...] = grad_mixed.reshape(seq, LANES, rows)

    def grad_copy(mask, back=False):
        return push(
            mem.grad_mixed_out.at[heads.at(mask)],
            mem.grad_mixed.at[:, block_of(heads.at(mask) if back else me, rows)],
            mem.mixed_send.at[8 + mask],
            mem.mixed_recv.at[8 + mask],
            heads.place(mask),
        )

    for mask in masks:
        grad_copy(mask).start()
    mem.grad_mixed[:, block_of(me, rows)] = mem.grad_mixed_out[me]
    back_reduce.pass_on()
    back_expand.append(expand_grad(1))
    back_expand[1].start_far()

    wait_pieces(lambda mask: grad_copy(mask, True))
    acts = gather(heads, 3, mem.grad_attn)
    acts.start()
    back_reduce.start_near()
    back_expand[0].start_near()
    back_attend = [
        line_scatter(
            4 + which,
            lambda part, which=which: mem.attend_grad.at[which, :, part],
            mem.attend_land.at[which],
        )
        for which in range(3)
    ]

    def attend_grad(which):
        grads = dot(mem.grad_project[which], mem.act_one[...])
        mem.attend_grad[which] = grads.T.astype(LOW).reshape(seq, batch, share, LANES)
        back_attend[which].start()

    lane = lax.broadcasted_iota(jnp.int32, (pair, LANES), 1)

    def grad_rows(block, unused):
        span = block_of(block, pair)
        whole = mem.grad_mixed[:, span].astype(WIDE).T
        for head in range(HEADS_HERE):
            mem.grad_heads[head, span, :] = jnp.where(lax.div(lane, HEAD_DIM) == head, whole, 0.0).astype(LOW)
        return unused

    lax.fori_loop(0, length // pair, grad_rows, 0)

    def value_back(block, unused):
        span = block_of(block, pair)
        total = dot(mem.probs[0, span, :], mem.grad_heads[0])
        for head in range(1, HEADS_HERE):
            total = total + dot(mem.probs[head, span, :], mem.grad_heads[head])
        mem.grad_project[2, :, span] = total.T.astype(LOW)
        return unused

    lax.fori_loop(0, length // pair, value_back, 0)
    back_expand[0].pass_on()
    attend_grad(2)

    def score_back(block, unused):
        columns = block_of(block, pair)
        row = lax.broadcasted_iota(jnp.int32, (HEAD_DIM, pair), 0)
        grads = mem.grad_mixed[:, columns]
        delta = grads.astype(WIDE) * mem.exact[:, columns]
        for head in range(HEADS_HERE):
            span = slice(head * HEAD_DIM, (head + 1) * HEAD_DIM)
            pieces = thirds(-jnp.sum(delta[span], axis=0, keepdims=True))
            marks = pick(row, dict(enumerate(pieces))).astype(LOW)
            change = dot(mem.value_heads[head], jnp.concatenate([grads[span], marks], axis=0))
            mem.probs[head, :, columns] = (mem.probs[head, :, columns].astype(WIDE) * change).astype(LOW)
        return unused

    lax.fori_loop(0, length // pair, score_back, 0)
    back_expand[1].start_near()
    mem.bias_sums[...] = jnp.zeros_like(mem.bias_sums)
    scale = HEAD_DIM ** (-0.5)

    def project_grads(block, unused):
        span = block_of(block, pair)
        cosine, sine = mem.cosine[:, span], -mem.sine[:, span]
        queries, keys = [], []
        for head in range(HEADS_HERE):
            features = slice(head * HEAD_DIM, (head + 1) * HEAD_DIM)
            queries.append(dot(mem.key_turned[features, :], mem.probs[head, :, span]) * scale)
            sums = dot(mem.probs[head, span, :], mem.query_heads[head]).T
            keys.append(sums[:HEAD_DIM])
            by_variate = sums[HEAD_DIM : HEAD_DIM + VARIATES]
            same = by_variate * mem.key_marks[:VARIATES, span].astype(WIDE)
            mem.bias_sums[head : head + 1, :] += jnp.sum(same, axis=0, keepdims=True)
            total = sums[HEAD_DIM + VARIATES : HEAD_DIM + VARIATES + 1]
            mem.bias_sums[HEADS_HERE + head : HEADS_HERE + head + 1, :] += total
        mem.grad_project[0, :, span] = turn_rows(jnp.concatenate(queries, axis=0), cosine, sine).astype(LOW)
        mem.grad_project[1, :, span] = turn_rows(jnp.concatenate(keys, axis=0), cosine, sine).astype(LOW)
        return unused

    lax.fori_loop(0, length // pair, project_grads, 0)
    back_expand[1].pass_on()
    attend_grad(0)
    acts.pass_on(1)
    acts.pass_on(2)
    sums = scatter(heads, 3)

    def project_back(step, unused):
        chip = lax.rem(step + 1, 4)
        span = block_of(chip_of(heads, chip), pair)
        total = jnp.zeros((pair, D), WIDE)
        for which in range(3):
            total = total + dot_turned(mem.grad_project[which, :, span].T, attend_matrix(which))
        sums.put(chip, total)
        at_step(step, 1, lambda: sums.combine(1))
        at_step(step, 2, lambda: sums.combine(2))
        return unused

    lax.fori_loop(0, 4, project_back, 0)
    sums.combine(3)
    attend_grad(1)
    acts.pass_on(3)
    for chip in range(4):
        acts.complete(chip)
    acts.finish()
    mem.output_grad[...] = (
        dot(mem.mixed_turned[...], mem.grad_attn[...]).astype(LOW).reshape(mem.output_grad.shape)
    )
    back_output = line_scatter(3, lambda part: mem.output_grad.at[part], mem.output_land)
    back_output.start()
    for which in (2, 0, 1):
        back_attend[which].pass_on()

    column_copies = []
    mem.squares[0:1, :] = jnp.zeros((1, D), WIDE)

    def add_squares(total):
        flat = total.reshape(-1, total.shape[-1])
        width = flat.shape[1]
        mem.squares[0:1, :width] += jnp.sum(flat * flat, axis=0, keepdims=True)

    def store_whole(total, out):
        out[...] = total
        add_squares(total)

    back_reduce.land()
    store_whole(
        mem.reduce_grad[quad].astype(WIDE)
        + mem.reduce_land[0].astype(WIDE)
        + mem.reduce_land[2].astype(WIDE),
        outs.reduce_share,
    )
    def expand_shares(which):
        back_expand[which].land()
        own = expand_part_of(mem.expand_grad, which)(quad)

        def one_block(block, unused):
            total = (
                own[block].astype(WIDE)
                + mem.expand_land[which, 0, block].astype(WIDE)
                + mem.expand_land[which, 2, block].astype(WIDE)
            )
            mem.expand_part[which, block] = total.astype(LOW)
            add_squares(total)
            return unused

        lax.fori_loop(0, 4, one_block, 0)
        for mask in masks:
            other = feeds.at(mask)
            copy = push(
                mem.expand_part.at[which, lax.rem(other, 4), lax.div(other, 4)],
                mem.expand_share.at[which, feeds.index],
                mem.share_send.at[which, mask],
                mem.share_recv.at[which, mask],
                feeds.place(mask),
            )
            copy.start()
            column_copies.append(copy)
        mem.expand_share[which, feeds.index] = mem.expand_part[
            which, lax.rem(feeds.index, 4), lax.div(feeds.index, 4)
        ]

    for which in range(2):
        expand_shares(which)

    def attend_shares(which):
        back_attend[which].land()

        def store(total):
            mem.attend_part[which] = total.astype(LOW)
            add_squares(total)

        back_attend[which].add(
            lambda: mem.attend_grad[which, :, group].astype(WIDE),
            lambda slot: mem.attend_land[which, slot].astype(WIDE),
            store,
        )

    attend_shares(2)
    grad_act = sums.total()
    unit_one, scale_one = norm_rows(ins.inputs[...].astype(WIDE))
    gain = ins.gains[0:1, :]
    grad_unit = grad_act * gain
    mem.gains[0:1, :] = jnp.sum(grad_act * unit_one, axis=0, keepdims=True)
    grad_input = mem.grad_own[...] + scale_one * (
        grad_unit - unit_one * jnp.mean(grad_unit * unit_one, axis=-1, keepdims=True)
    )
    outs.input_gradient[...] = grad_input * (count_all * D)
    outs.count[...] = jnp.broadcast_to(count_all, (8, LANES))

    back_output.pass_on()
    for which in range(2):
        attend_shares(which)
    for mask in masks:
        copy = push(
            mem.attend_part.at[:, heads.at(mask)],
            outs.attend_share.at[:, :, block_of(me, LANES)],
            mem.share_send.at[2, mask],
            mem.share_recv.at[2, mask],
            heads.place(mask),
        )
        copy.start()
        column_copies.append(copy)
    outs.attend_share[:, :, block_of(me, LANES)] = mem.attend_part[:, me]
    back_output.land()
    back_output.add(
        lambda: mem.output_grad[group].astype(WIDE),
        lambda slot: mem.output_land[slot].astype(WIDE),
        lambda total: store_whole(total, outs.output_share),
    )

    lane = lax.broadcasted_iota(jnp.int32, (1, LANES), 1)
    lines = [
        mem.gains[which : which + 1, start : start + LANES]
        for which in range(2)
        for start in range(0, D, LANES)
    ]
    bias_line = jnp.zeros((1, LANES), WIDE)
    for row in range(2 * HEADS_HERE):
        place = row // HEADS_HERE * HEADS + me * HEADS_HERE + row % HEADS_HERE
        line = mem.bias_sums[row : row + 1, :]
        if row >= HEADS_HERE:
            line = line - mem.bias_sums[row - HEADS_HERE : row - HEADS_HERE + 1, :]
        amount = jnp.sum(line, axis=1, keepdims=True)
        bias_line = bias_line + jnp.where(lane == place, amount, 0.0)
    amounts = jnp.sum(mem.squares[0:2, :], axis=1, keepdims=True)
    amount_line = jnp.where(lane == 0, amounts[0:1], 0.0) + jnp.where(lane == 1, amounts[1:2], 0.0)
    lines += [bias_line, amount_line, jnp.zeros((6, LANES), WIDE)]
    mem.plane_totals[me] = jnp.concatenate(lines, axis=0)
    plane_copies = []
    for mask in masks:
        copy = push(
            mem.plane_totals.at[me],
            mem.plane_totals.at[me],
            mem.total_send.at[0, mask],
            mem.total_recv.at[0, mask],
            (flip(me, mask), group),
        )
        copy.start()
        plane_copies.append(copy)
    for copy in column_copies[: 2 * len(masks)]:
        copy.wait()
    for which in range(2):
        for block in range(blocks):
            owner, part = feed_block(block)
            outs.expand_share[which, :, block * LANES : (block + 1) * LANES] = mem.expand_share[
                which, owner, :, part * LANES : (part + 1) * LANES
            ]
    for copy in plane_copies:
        copy.wait()
    mem.line_totals[group] = jnp.sum(mem.plane_totals[...], axis=0)
    total_copies = []
    for step in range(1, batch):
        copy = push(
            mem.line_totals.at[group],
            mem.line_totals.at[group],
            mem.total_send.at[1, step],
            mem.total_recv.at[1, step],
            (me, lax.rem(group + step, batch)),
        )
        copy.start()
        total_copies.append(copy)
    for copy in total_copies:
        copy.wait()
    outs.totals[...] = jnp.sum(mem.line_totals[...], axis=0)
    for copy in column_copies[2 * len(masks) :]:
        copy.wait()
    for copies in (attend_columns, expand_columns):
        for copy in copies:
            copy.wait_send()
    for line in [line_attend, line_output, line_reduce] + line_expand:
        line.finish()
    for line in [back_output, back_reduce] + back_attend + back_expand:
        line.finish()


def call_layer(seq, batch, inputs, teacher, lengths, variates, observed, turns, bias, gains, attend, output, expand, reduce):
    rows, share, hidden = inputs.shape[0], attend.shape[1], expand.shape[2] // seq
    length, pair, chips = rows * seq, 2 * rows, seq // 2
    low = lambda *shape: pltpu.VMEM(shape, LOW)
    wide = lambda *shape: pltpu.VMEM(shape, WIDE)
    sems = lambda *shape: pltpu.SemaphoreType.DMA(shape)
    in_names = ["inputs", "teacher", "lengths", "variates", "observed", "turns", "bias", "gains"]
    in_names += ["attend", "output", "expand", "reduce"]
    outs = dict(
        layer_output=((rows, D), WIDE),
        input_gradient=((rows, D), WIDE),
        totals=((TOTAL_ROWS, LANES), WIDE),
        count=((8, LANES), WIDE),
        attend_share=((3, share, D), LOW),
        output_share=((output.shape[0], D), WIDE),
        expand_share=((2, share, hidden * seq), LOW),
        reduce_share=((reduce.shape[0], D), WIDE),
    )
    scratch = dict(
        gains=wide(2, D),
        squares=wide(8, D),
        plane_totals=wide(seq, TOTAL_ROWS, LANES),
        line_totals=wide(batch, TOTAL_ROWS, LANES),
        attend_low=low(3, share, D),
        expand_low=low(2, seq, share, hidden),
        attend_all=low(3, seq, batch, share, LANES),
        output_full=low(D, D),
        expand_all=low(2, seq, batch, share, hidden),
        reduce_all=low(batch, reduce.shape[0], D),
        own_rows=low(4, rows, D),
        act_one=low(length, D),
        act_two=low(length, D),
        branch=low(length, D),
        grad_attn=low(length, D),
        facts_own=wide(turns.shape[0] + 8, LANES),
        facts_all=wide(seq * (turns.shape[0] + 8), LANES),
        scored=wide(rows, LANES),
        cosine=wide(HEAD_DIM // 2, length),
        sine=wide(HEAD_DIM // 2, length),
        labels=wide(8, length),
        key_marks=low(HEAD_DIM, length),
        count=wide(batch, 8, LANES),
        query_turned=low(HEADS_HERE, LANES, length),
        key_turned=low(LANES, length),
        value_turned=low(LANES, length),
        key_heads=low(HEADS_HERE, length, LANES),
        value_heads=low(HEADS_HERE, length, LANES),
        query_heads=low(HEADS_HERE, length, LANES),
        grad_heads=low(HEADS_HERE, length, LANES),
        grad_mixed=low(LANES, length),
        grad_mixed_out=low(seq, LANES, rows),
        probs=low(HEADS_HERE, length, length),
        mixed_out=low(length, LANES),
        mixed_rows=low(rows, D),
        sum_marks=low(HEAD_DIM, length),
        hidden_turned=low(hidden, length),
        act_two_turned=low(D, length),
        exact=wide(LANES, length),
        mixed_wide=wide(LANES, pair),
        mixed_turned=low(LANES, length),
        whole=wide(pair, D),
        keep=wide(chips, rows, D),
        near_from=low(chips, rows, D),
        near=low(chips, rows, D),
        far_from=low(chips, rows, D),
        far=low(chips, rows, D),
        middle=wide(rows, D),
        grad_own=wide(rows, D),
        by_up=wide(length, hidden),
        by_gate=wide(length, hidden),
        hidden=low(length, hidden),
        grad_gate=low(length, hidden),
        grad_up=low(length, hidden),
        bias_sums=wide(8, pair),
        grad_project=low(3, LANES, length),
        reduce_grad=low(batch, reduce.shape[0], D),
        expand_grad=low(2, seq, batch, share, hidden),
        output_grad=low(batch, output.shape[0], D),
        attend_grad=low(3, seq, batch, share, LANES),
        reduce_land=low(3, reduce.shape[0], D),
        expand_land=low(2, 3, 4, 2, share, hidden),
        output_land=low(batch, output.shape[0], D),
        attend_land=low(3, batch, seq, share, LANES),
        expand_part=low(2, 4, 2, share, hidden),
        expand_share=low(2, seq, share, hidden),
        attend_part=low(3, seq, share, LANES),
        stage_sem=sems(5 + 2 * (expand.shape[2] // D)),
        total_send=sems(2, seq),
        total_recv=sems(2, seq),
        column_send=sems(2, seq),
        column_recv=sems(2, seq),
        line_send=sems(5, batch),
        line_recv=sems(5, batch),
        facts_send=sems(seq),
        facts_recv=sems(seq),
        gather_send=sems(4, seq),
        gather_recv=sems(4, seq),
        count_send=sems(batch),
        count_recv=sems(batch),
        near_send=sems(4, chips),
        near_recv=sems(4, chips),
        far_send=sems(4, chips),
        far_recv=sems(4, chips),
        back_send=sems(7, batch),
        back_recv=sems(7, batch),
        output_send=sems(seq),
        output_recv=sems(seq),
        mixed_send=sems(2 * seq),
        mixed_recv=sems(2 * seq),
        share_send=sems(3, seq),
        share_recv=sems(3, seq),
    )

    places = dict.fromkeys(("attend", "output", "expand", "reduce"), pl.BlockSpec(memory_space=pl.ANY))
    places["bias"] = places["lengths"] = IN_SMEM

    def kernel(*refs):
        groups, start = [], 0
        for names in (in_names, outs, scratch):
            names = list(names)
            groups.append(types.SimpleNamespace(**dict(zip(names, refs[start : start + len(names)]))))
            start += len(names)
        layer_kernel(seq, batch, *groups)

    results = pl.pallas_call(
        kernel,
        out_shape=[jax.ShapeDtypeStruct(*out) for out in outs.values()],
        in_specs=[places.get(name, IN_VMEM) for name in in_names],
        out_specs=[IN_VMEM] * len(outs),
        scratch_shapes=list(scratch.values()),
        compiler_params=pltpu.CompilerParams(
            collective_id=0, has_side_effects=True, vmem_limit_bytes=63 * MIB
        ),
        name="layer",
    )(inputs, teacher, lengths, variates, observed, turns, bias, gains, attend, output, expand, reduce)
    return types.SimpleNamespace(**dict(zip(outs, results)))


def update_kernel(
    smalls, ins, small_outs, outs, olds, shares, news, copies, passed, in_sems, out_sems
):
    totals, count, gains, gains_first, gains_second, bias, bias_first, bias_second = smalls
    order = (2, 3, 0, 1)
    comes = []
    for place, number in enumerate(order):
        pairs = list(zip(ins[4 + 3 * number : 7 + 3 * number], olds[3 * number : 3 * number + 3]))
        pairs.append((ins[number], shares[number]))
        comes.append(
            [
                pltpu.make_async_copy(source, target, in_sems.at[4 * place + part])
                for part, (source, target) in enumerate(pairs)
            ]
        )
    for copy in sum(comes, []):
        copy.start()
    through = [
        pltpu.make_async_copy(ins[16 + part], passed[part], in_sems.at[16 + part]) for part in range(2)
    ]
    for copy in through:
        copy.start()
    goes = []
    gains_total = jnp.concatenate(
        [
            jnp.concatenate([totals[row + i : row + i + 1, :] for i in range(D // LANES)], axis=1)
            for row in (0, D // LANES)
        ],
        axis=0,
    )
    row = 2 * D // LANES
    bias_total = jnp.concatenate(
        [totals[row : row + 1, :HEADS], totals[row : row + 1, HEADS : 2 * HEADS]], axis=0
    )
    row += 1

    def sum_all(values):
        return jnp.sum(jnp.sum(values, axis=0, keepdims=True), axis=1, keepdims=True)

    squares = (
        totals[row : row + 1, 0:1] + sum_all(gains_total * gains_total) + sum_all(bias_total * bias_total)
    )
    grad_norm = jnp.sqrt(squares)
    clip = jnp.minimum(1.0, CLIP_NORM / grad_norm)
    small_outs[0][...] = totals[row : row + 1, 1:2] / (count[0:1, 0:1] * D)
    small_outs[1][...] = grad_norm
    rates = (RATE_ATTEND, RATE_OUTPUT, RATE_EXPAND, RATE_REDUCE)
    for place, number in enumerate(order):
        for copy in comes[place]:
            copy.wait()
        weight, first, second = olds[3 * number : 3 * number + 3]
        new, first_new, second_new = news[3 * number : 3 * number + 3]
        arrays = (new, copies[number], first_new, second_new, weight, first, second, shares[number])
        for lead in range(weight.shape[0] if weight.ndim == 3 else 1):

            def one_block(block, unused, lead=lead, arrays=arrays, rate=rates[number]):
                rows = block_of(block, 16)
                place = (lead, rows) if arrays[0].ndim == 3 else (rows,)
                old, moment, square, share = [array[place] for array in arrays[4:]]
                step = fast_step(old, moment, square, share.astype(WIDE) * clip, rate)
                arrays[0][place], arrays[2][place], arrays[3][place] = step
                arrays[1][place] = step[0].astype(LOW)
                return unused

            lax.fori_loop(0, weight.shape[-2] // 16, one_block, 0)
        for part, source in enumerate((new, copies[number], first_new, second_new)):
            copy = pltpu.make_async_copy(
                source, outs[2 + 4 * number + part], out_sems.at[2 + 4 * number + part]
            )
            copy.start()
            goes.append(copy)
        if place == 0:
            for part in range(2):
                through[part].wait()
                copy = pltpu.make_async_copy(passed[part], outs[part], out_sems.at[part])
                copy.start()
                goes.append(copy)
    for number, (old, total, rate) in enumerate(
        (
            ((gains, gains_first, gains_second), gains_total, RATE_GAINS),
            ((bias, bias_first, bias_second), bias_total, RATE_BIAS),
        )
    ):
        new, first_new, second_new = small_outs[2 + 3 * number : 5 + 3 * number]
        new[...], first_new[...], second_new[...] = adam_step(
            old[0][...], old[1][...], old[2][...], total * clip, rate, 0.0
        )
    for copy in goes:
        copy.wait()


def fast_step(weight, first, second, gradient, rate):
    first = BETA_ONE * first + (1.0 - BETA_ONE) * gradient
    second = BETA_TWO * second + ((1.0 - BETA_TWO) * gradient) * gradient
    low = jnp.sqrt(second * (1.0 / (1.0 - BETA_TWO**STEP))) + ADAM_EPS
    step = first * (rate / (1.0 - BETA_ONE**STEP)) / low
    return weight * (1.0 - rate * WEIGHT_DECAY) - step, first, second


def call_update(done, shares, smalls, olds):
    in_hbm = pl.BlockSpec(memory_space=pl.ANY)
    smalls = [done.totals, done.count] + smalls
    ins = shares + olds + [done.layer_output, done.input_gradient]
    one = jax.ShapeDtypeStruct((1, 1), WIDE)
    small_outs = [one, one] + smalls[2:]
    outs = [(done.layer_output, WIDE), (done.input_gradient, WIDE)]
    for weight in olds[::3]:
        outs += [(weight, dtype) for dtype in (WIDE, LOW, WIDE, WIDE)]
    passed = ins[-2:]
    parts = [smalls, ins, small_outs, outs, olds, shares, olds, olds[::3], passed]

    def kernel(*refs):
        groups, start = [], 0
        for part in parts:
            groups.append(refs[start : start + len(part)])
            start += len(part)
        update_kernel(*groups, *refs[start:])

    results = pl.pallas_call(
        kernel,
        out_shape=[jax.ShapeDtypeStruct(array.shape, WIDE) for array in small_outs]
        + [jax.ShapeDtypeStruct(array.shape, dtype) for array, dtype in outs],
        in_specs=[IN_VMEM] * len(smalls) + [in_hbm] * len(ins),
        out_specs=[IN_VMEM] * len(small_outs) + [in_hbm] * len(outs),
        scratch_shapes=[pltpu.VMEM(array.shape, WIDE) for array in olds]
        + [pltpu.VMEM(array.shape, array.dtype) for array in shares]
        + [pltpu.VMEM(array.shape, WIDE) for array in olds]
        + [pltpu.VMEM(array.shape, LOW) for array in olds[::3]]
        + [pltpu.VMEM(array.shape, WIDE) for array in passed]
        + [pltpu.SemaphoreType.DMA((18,)), pltpu.SemaphoreType.DMA((18,))],
        compiler_params=pltpu.CompilerParams(vmem_limit_bytes=63 * MIB),
        name="update",
    )(*smalls, *ins)
    return results[: len(small_outs)], results[len(small_outs) :]


def fast_body(
    seq,
    batch,
    inputs,
    teacher,
    lengths,
    variate_ids,
    time_ids,
    observed,
    attend_weight,
    output_weight,
    expand_weight,
    reduce_weight,
    norm_gains,
    variate_bias,
    attend_first,
    output_first,
    expand_first,
    reduce_first,
    gains_first,
    bias_first,
    attend_second,
    output_second,
    expand_second,
    reduce_second,
    gains_second,
    bias_second,
):
    half_dim = HEAD_DIM // 2
    frequency = jnp.exp(-math.log(ROPE_BASE) * jnp.arange(half_dim).astype(WIDE) / half_dim)
    angle = frequency[:, None] * time_ids.astype(WIDE)
    done = call_layer(
        seq,
        batch,
        inputs[0],
        teacher[0],
        lengths,
        variate_ids,
        observed,
        jnp.concatenate([jnp.cos(angle), jnp.sin(angle)]),
        variate_bias,
        norm_gains,
        attend_weight,
        output_weight,
        expand_weight,
        reduce_weight,
    )
    small, large = call_update(
        done,
        [done.attend_share, done.output_share, done.expand_share, done.reduce_share],
        [norm_gains, gains_first, gains_second, variate_bias, bias_first, bias_second],
        [attend_weight, attend_first, attend_second]
        + [output_weight, output_first, output_second]
        + [expand_weight, expand_first, expand_second]
        + [reduce_weight, reduce_first, reduce_second],
    )
    return (
        large[0][None],
        small[0].reshape(()),
        large[1][None],
        small[1].reshape(()),
    ) + tuple(large[2:] + small[2:])


def solution(mesh):
    seq, batch = mesh.shape["seq"], mesh.shape["batch"]
    body = functools.partial(fast_body, seq, batch) if fast_fits(seq, batch) else general_body
    in_specs = (
        P("batch", "seq", None),
        P("batch", "seq", None),
        P("batch"),
        P("batch", "seq"),
        P("batch", "seq"),
        P("batch", "seq"),
        P(None, ("seq", "batch"), None),
        P(("seq", "batch"), None),
        P(None, ("seq", "batch"), None),
        P(("seq", "batch"), None),
        P(),
        P(),
        P(None, ("seq", "batch"), None),
        P(("seq", "batch"), None),
        P(None, ("seq", "batch"), None),
        P(("seq", "batch"), None),
        P(),
        P(),
        P(None, ("seq", "batch"), None),
        P(("seq", "batch"), None),
        P(None, ("seq", "batch"), None),
        P(("seq", "batch"), None),
        P(),
        P(),
    )
    out_specs = (
        P("batch", "seq", None),
        P(),
        P("batch", "seq", None),
        P(),
        P(None, ("seq", "batch"), None),
        P(None, ("seq", "batch"), None),
        P(None, ("seq", "batch"), None),
        P(None, ("seq", "batch"), None),
        P(("seq", "batch"), None),
        P(("seq", "batch"), None),
        P(("seq", "batch"), None),
        P(("seq", "batch"), None),
        P(None, ("seq", "batch"), None),
        P(None, ("seq", "batch"), None),
        P(None, ("seq", "batch"), None),
        P(None, ("seq", "batch"), None),
        P(("seq", "batch"), None),
        P(("seq", "batch"), None),
        P(("seq", "batch"), None),
        P(("seq", "batch"), None),
        P(),
        P(),
        P(),
        P(),
        P(),
        P(),
    )
    return jax.shard_map(body, mesh=mesh, in_specs=in_specs, out_specs=out_specs, check_vma=False)
```

```python
import functools
import math
import types

import jax
import jax.numpy as jnp
from jax import lax
from jax.experimental import pallas as pl
from jax.experimental.pallas import tpu as pltpu
from jax.sharding import PartitionSpec as P

D = 1024
HEADS = 16
HEAD_DIM = 64
STEP = 10


NORM_EPS = 1e-05
ROPE_BASE = 10000.0
MASKED = -1e30
CLIP_NORM = 1.0
BETA_ONE = 0.9
BETA_TWO = 0.98
ADAM_EPS = 1e-08
WEIGHT_DECAY = 0.1
RATE_ATTEND = 0.03
RATE_OUTPUT = 0.5
RATE_EXPAND = 0.03
RATE_REDUCE = 0.015
RATE_GAINS = 1.0
RATE_BIAS = 0.5


def angles(times):
    half_dim = HEAD_DIM // 2
    frequency = jnp.exp(-math.log(ROPE_BASE) * jnp.arange(half_dim).astype(jnp.float32) / half_dim)
    angle_table = times.astype(jnp.float32)[..., None] * frequency
    return (jnp.cos(angle_table)[..., None, :], jnp.sin(angle_table)[..., None, :])


def rotate(values, cos_table, sin_table):
    half_dim = values.shape[-1] // 2
    first_half = values[..., :half_dim]
    second_half = values[..., half_dim:]
    return jnp.concatenate(
        [
            first_half * cos_table - second_half * sin_table,
            second_half * cos_table + first_half * sin_table,
        ],
        axis=-1,
    )


def unrotate(values, cos_table, sin_table):
    half_dim = values.shape[-1] // 2
    first_half = values[..., :half_dim]
    second_half = values[..., half_dim:]
    return jnp.concatenate(
        [
            first_half * cos_table + second_half * sin_table,
            second_half * cos_table - first_half * sin_table,
        ],
        axis=-1,
    )


def normalize(values):
    inv_scale = lax.rsqrt(jnp.mean(values * values, axis=-1, keepdims=True) + NORM_EPS)
    return (values * inv_scale, inv_scale)


def norm_back(grad_act, unit_rows, inv_scale, gain_row):
    grad_unit = grad_act * gain_row
    return inv_scale * (
        grad_unit - unit_rows * jnp.mean(grad_unit * unit_rows, axis=-1, keepdims=True)
    )


def score_block(query_rows, query_labels, key_rows, key_labels, bias_table):
    scores = jnp.einsum(
        "ihe,jhe->hij", query_rows, key_rows, preferred_element_type=jnp.float32
    ) * HEAD_DIM ** (-0.5)
    same_var = query_labels[:, None] == key_labels[None, :]
    scores = scores + jnp.where(
        same_var[None], bias_table[0][:, None, None], bias_table[1][:, None, None]
    )
    scores = jnp.where(key_labels[None, None, :] >= 0, scores, MASKED)
    return (scores, same_var)


def block_grads(
    query_rows,
    query_labels,
    grad_rows,
    lse_rows,
    delta_rows,
    key_rows,
    value_rows,
    key_labels,
    bias_table,
    need_query,
    need_keys,
):
    scores, same_var = score_block(query_rows, query_labels, key_rows, key_labels, bias_table)
    weights = jnp.exp(scores - lse_rows.T[:, :, None])
    grad_weights = jnp.einsum(
        "ihe,jhe->hij", grad_rows, value_rows, preferred_element_type=jnp.float32
    )
    grad_scores = (weights * (grad_weights - delta_rows.T[:, :, None])).astype(jnp.bfloat16)
    result = ()
    if need_query:
        grad_query = jnp.einsum(
            "hij,jhe->ihe", grad_scores, key_rows, preferred_element_type=jnp.float32
        ) * HEAD_DIM ** (-0.5)
        widened = grad_scores.astype(jnp.float32)
        bias_same = jnp.sum(jnp.where(same_var[None], widened, 0.0), axis=(1, 2))
        bias_other = jnp.sum(jnp.where(same_var[None], 0.0, widened), axis=(1, 2))
        result = result + (grad_query, jnp.stack([bias_same, bias_other]))
    if need_keys:
        grad_key = jnp.einsum(
            "hij,ihe->jhe", grad_scores, query_rows, preferred_element_type=jnp.float32
        ) * HEAD_DIM ** (-0.5)
        grad_value = jnp.einsum(
            "hij,ihe->jhe",
            weights.astype(jnp.bfloat16),
            grad_rows,
            preferred_element_type=jnp.float32,
        )
        result = result + (grad_key, grad_value)
    return result


def adam_step(weight, first_moment, second_moment, gradient, step_rate, decay_rate):
    first_moment = BETA_ONE * first_moment + (1.0 - BETA_ONE) * gradient
    second_moment = BETA_TWO * second_moment + (1.0 - BETA_TWO) * gradient * gradient
    direction = (
        first_moment
        / (1.0 - BETA_ONE**STEP)
        / (jnp.sqrt(second_moment / (1.0 - BETA_TWO**STEP)) + ADAM_EPS)
    )
    return (weight - step_rate * (direction + decay_rate * weight), first_moment, second_moment)


def general_body(
    inputs,
    teacher,
    lengths,
    variate_ids,
    time_ids,
    observed,
    attend_weight,
    output_weight,
    expand_weight,
    reduce_weight,
    norm_gains,
    variate_bias,
    attend_first,
    output_first,
    expand_first,
    reduce_first,
    gains_first,
    bias_first,
    attend_second,
    output_second,
    expand_second,
    reduce_second,
    gains_second,
    bias_second,
):
    row_count = inputs.shape[1]
    length = row_count * lax.axis_size("seq")
    block_rows = math.gcd(length, 1024)
    blocks = length // block_rows
    states = inputs[0].astype(jnp.float32)
    positions = lax.axis_index("seq") * row_count + jnp.arange(row_count, dtype=jnp.int32)
    inside = positions < lengths[0]
    scored = jnp.logical_and(inside, observed[0] == 1)
    local_count = jnp.sum(scored.astype(jnp.int32))
    count_early = lax.psum(local_count, ("seq", "batch"))
    full_attend, full_output, full_expand, full_reduce = (
        lax.all_gather(attend_weight.astype(jnp.bfloat16), ("seq", "batch"), axis=1, tiled=True),
        lax.all_gather(output_weight.astype(jnp.bfloat16), ("seq", "batch"), axis=0, tiled=True),
        lax.all_gather(expand_weight.astype(jnp.bfloat16), ("seq", "batch"), axis=1, tiled=True),
        lax.all_gather(reduce_weight.astype(jnp.bfloat16), ("seq", "batch"), axis=0, tiled=True),
    )
    unit_one, scale_one = normalize(states)
    act_one = (unit_one * norm_gains[0]).astype(jnp.bfloat16)
    project = jnp.einsum("td,cde->cte", act_one, full_attend, preferred_element_type=jnp.float32)
    cos_table, sin_table = angles(time_ids[0])
    query = rotate(project[0].reshape(row_count, HEADS, HEAD_DIM), cos_table, sin_table).astype(
        jnp.bfloat16
    )
    key_rows = (
        rotate(project[1].reshape(row_count, HEADS, HEAD_DIM), cos_table, sin_table)
        .astype(jnp.bfloat16)
        .reshape(row_count, D)
    )
    value_rows = project[2].astype(jnp.bfloat16)
    own_labels = jnp.where(inside, variate_ids[0], -1).astype(jnp.bfloat16)
    all_keys, all_values, all_labels = (
        lax.all_gather(key_rows, "seq", axis=0, tiled=True),
        lax.all_gather(value_rows, "seq", axis=0, tiled=True),
        lax.all_gather(own_labels, "seq", axis=0, tiled=True),
    )
    key_blocks = all_keys.reshape(blocks, block_rows, HEADS, HEAD_DIM)
    value_blocks = all_values.reshape(blocks, block_rows, HEADS, HEAD_DIM)
    label_blocks = all_labels.astype(jnp.float32).reshape(blocks, block_rows)
    query_labels = variate_ids[0].astype(jnp.float32)

    def sweep_top(carry, pieces):
        running, sum_exp = carry
        scores, same_var = score_block(query, query_labels, pieces[0], pieces[1], variate_bias)
        raised = jnp.maximum(running, jnp.floor(jnp.max(scores, axis=-1)))
        sum_exp = sum_exp * jnp.exp(running - raised) + jnp.sum(
            jnp.exp(scores - raised[..., None]), axis=-1
        )
        return ((raised, sum_exp), None)

    start_top = jnp.full((HEADS, row_count), MASKED, jnp.float32)
    (row_top, sum_exp), unused = lax.scan(
        sweep_top,
        (start_top, jnp.zeros((HEADS, row_count), jnp.float32)),
        (key_blocks, label_blocks),
    )
    log_total = row_top + jnp.log(sum_exp)

    def sweep_out(carry, pieces):
        coarse, finest = carry
        scores, same_var = score_block(query, query_labels, pieces[0], pieces[2], variate_bias)
        weights = jnp.exp(scores - log_total[..., None])
        rounded = weights.astype(jnp.bfloat16)
        residue = (weights - rounded.astype(jnp.float32)).astype(jnp.bfloat16)
        coarse = coarse + jnp.einsum(
            "hij,jhe->ihe", rounded, pieces[1], preferred_element_type=jnp.float32
        )
        finest = finest + jnp.einsum(
            "hij,jhe->ihe", residue, pieces[1], preferred_element_type=jnp.float32
        )
        return ((coarse, finest), None)

    zero_heads = jnp.zeros((row_count, HEADS, HEAD_DIM), jnp.float32)
    (coarse, finest), unused = lax.scan(
        sweep_out, (zero_heads, zero_heads), (key_blocks, value_blocks, label_blocks)
    )
    exact_heads = coarse + finest
    mixed = coarse.reshape(row_count, D).astype(jnp.bfloat16)
    middle = states + jnp.dot(mixed, full_output, preferred_element_type=jnp.float32)
    unit_two, scale_two = normalize(middle)
    act_two = (unit_two * norm_gains[1]).astype(jnp.bfloat16)
    gate_up = jnp.einsum("td,cdf->ctf", act_two, full_expand, preferred_element_type=jnp.float32)
    sigmoid = jax.nn.sigmoid(gate_up[0])
    hidden = (gate_up[0] * sigmoid * gate_up[1]).astype(jnp.bfloat16)
    output = middle + jnp.dot(hidden, full_reduce, preferred_element_type=jnp.float32)
    error = output - teacher[0].astype(jnp.float32)
    local_square = jnp.sum(jnp.where(scored[:, None], error * error, 0.0))
    square_total = lax.psum(local_square, ("seq", "batch"))
    count_all = count_early.astype(jnp.float32)
    loss = square_total / (count_all * D)
    grad_out = jnp.where(scored[:, None], error * (2.0 / (count_all * D)), 0.0)
    back_attend, back_output, back_expand, back_reduce = (
        lax.all_gather(attend_weight.astype(jnp.bfloat16), ("seq", "batch"), axis=1, tiled=True),
        lax.all_gather(output_weight.astype(jnp.bfloat16), ("seq", "batch"), axis=0, tiled=True),
        lax.all_gather(expand_weight.astype(jnp.bfloat16), ("seq", "batch"), axis=1, tiled=True),
        lax.all_gather(reduce_weight.astype(jnp.bfloat16), ("seq", "batch"), axis=0, tiled=True),
    )
    grad_branch = grad_out.astype(jnp.bfloat16)
    reduce_grad = jnp.einsum("tf,td->fd", hidden, grad_branch, preferred_element_type=jnp.float32)
    grad_hidden = jnp.einsum(
        "td,fd->tf", grad_branch, back_reduce, preferred_element_type=jnp.float32
    )
    grad_gate = grad_hidden * gate_up[1] * sigmoid * (1.0 + gate_up[0] * (1.0 - sigmoid))
    grad_up = grad_hidden * gate_up[0] * sigmoid
    grad_expand = jnp.stack([grad_gate, grad_up]).astype(jnp.bfloat16)
    expand_grad = jnp.einsum(
        "td,ctf->cdf", act_two, grad_expand, preferred_element_type=jnp.float32
    )
    grad_act_two = jnp.einsum(
        "ctf,cdf->td", grad_expand, back_expand, preferred_element_type=jnp.float32
    )
    expand_share, reduce_share = (
        lax.psum_scatter(expand_grad, ("seq", "batch"), scatter_dimension=1, tiled=True),
        lax.psum_scatter(reduce_grad, ("seq", "batch"), scatter_dimension=0, tiled=True),
    )
    grad_middle = grad_out + norm_back(grad_act_two, unit_two, scale_two, norm_gains[1])
    grad_attn = grad_middle.astype(jnp.bfloat16)
    output_grad = jnp.einsum("td,te->de", mixed, grad_attn, preferred_element_type=jnp.float32)
    grad_mixed = jnp.einsum(
        "te,de->td", grad_attn, back_output, preferred_element_type=jnp.float32
    ).astype(jnp.bfloat16)
    grad_heads = grad_mixed.reshape(row_count, HEADS, HEAD_DIM)
    row_delta = jnp.sum(grad_heads.astype(jnp.float32) * exact_heads, axis=-1)
    lse_rows = log_total.T
    zero_bias = jnp.zeros((2, HEADS), jnp.float32)

    def sweep_query(carry, pieces):
        part_query, part_bias = block_grads(
            query,
            query_labels,
            grad_heads,
            lse_rows,
            row_delta,
            pieces[0],
            pieces[1],
            pieces[2],
            variate_bias,
            True,
            False,
        )
        return ((carry[0] + part_query, carry[1] + part_bias), None)

    (query_total, bias_grad), unused = lax.scan(
        sweep_query, (zero_heads, zero_bias), (key_blocks, value_blocks, label_blocks)
    )
    all_query, all_grad = (
        lax.all_gather(query.reshape(row_count, D), "seq", axis=0, tiled=True),
        lax.all_gather(grad_mixed, "seq", axis=0, tiled=True),
    )
    all_lse, all_delta = (
        lax.all_gather(lse_rows, "seq", axis=0, tiled=True),
        lax.all_gather(row_delta, "seq", axis=0, tiled=True),
    )
    key_heads = key_rows.reshape(row_count, HEADS, HEAD_DIM)
    value_heads = value_rows.reshape(row_count, HEADS, HEAD_DIM)
    own_float = own_labels.astype(jnp.float32)

    def sweep_keys(carry, pieces):
        part_key, part_value = block_grads(
            pieces[0],
            pieces[1],
            pieces[2],
            pieces[3],
            pieces[4],
            key_heads,
            value_heads,
            own_float,
            variate_bias,
            False,
            True,
        )
        return ((carry[0] + part_key, carry[1] + part_value), None)

    (key_total, value_heads_total), unused = lax.scan(
        sweep_keys,
        (zero_heads, zero_heads),
        (
            all_query.reshape(blocks, block_rows, HEADS, HEAD_DIM),
            label_blocks,
            all_grad.reshape(blocks, block_rows, HEADS, HEAD_DIM),
            all_lse.reshape(blocks, block_rows, HEADS),
            all_delta.reshape(blocks, block_rows, HEADS),
        ),
    )
    value_total = value_heads_total.reshape(row_count, D)
    grad_query = unrotate(query_total, cos_table, sin_table).reshape(row_count, D)
    grad_key = unrotate(key_total, cos_table, sin_table).reshape(row_count, D)
    grad_project = jnp.stack([grad_query, grad_key, value_total]).astype(jnp.bfloat16)
    attend_grad = jnp.einsum(
        "td,cte->cde", act_one, grad_project, preferred_element_type=jnp.float32
    )
    grad_act_one = jnp.einsum(
        "cte,cde->td", grad_project, back_attend, preferred_element_type=jnp.float32
    )
    attend_share, output_share = (
        lax.psum_scatter(attend_grad, ("seq", "batch"), scatter_dimension=1, tiled=True),
        lax.psum_scatter(output_grad, ("seq", "batch"), scatter_dimension=0, tiled=True),
    )
    grad_input = grad_middle + norm_back(grad_act_one, unit_one, scale_one, norm_gains[0])
    gains_grad = jnp.stack(
        [jnp.sum(grad_act_one * unit_one, axis=0), jnp.sum(grad_act_two * unit_two, axis=0)]
    )
    local_squares = (
        jnp.sum(attend_share * attend_share)
        + jnp.sum(output_share * output_share)
        + jnp.sum(expand_share * expand_share)
        + jnp.sum(reduce_share * reduce_share)
    )
    gains_total, bias_total, square_sum = lax.psum(
        (gains_grad, bias_grad, local_squares), ("seq", "batch")
    )
    grad_norm = jnp.sqrt(
        square_sum + jnp.sum(gains_total * gains_total) + jnp.sum(bias_total * bias_total)
    )
    clip_scale = jnp.minimum(1.0, CLIP_NORM / grad_norm)
    attend_new, attend_first_new, attend_second_new = adam_step(
        attend_weight,
        attend_first,
        attend_second,
        attend_share * clip_scale,
        RATE_ATTEND,
        WEIGHT_DECAY,
    )
    output_new, output_first_new, output_second_new = adam_step(
        output_weight,
        output_first,
        output_second,
        output_share * clip_scale,
        RATE_OUTPUT,
        WEIGHT_DECAY,
    )
    expand_new, expand_first_new, expand_second_new = adam_step(
        expand_weight,
        expand_first,
        expand_second,
        expand_share * clip_scale,
        RATE_EXPAND,
        WEIGHT_DECAY,
    )
    reduce_new, reduce_first_new, reduce_second_new = adam_step(
        reduce_weight,
        reduce_first,
        reduce_second,
        reduce_share * clip_scale,
        RATE_REDUCE,
        WEIGHT_DECAY,
    )
    gains_new, gains_first_new, gains_second_new = adam_step(
        norm_gains, gains_first, gains_second, gains_total * clip_scale, RATE_GAINS, 0.0
    )
    bias_new, bias_first_new, bias_second_new = adam_step(
        variate_bias, bias_first, bias_second, bias_total * clip_scale, RATE_BIAS, 0.0
    )
    input_gradient = (grad_input * count_all * D)[None]
    return (
        output[None],
        loss,
        input_gradient,
        grad_norm,
        attend_new,
        attend_new.astype(jnp.bfloat16),
        attend_first_new,
        attend_second_new,
        output_new,
        output_new.astype(jnp.bfloat16),
        output_first_new,
        output_second_new,
        expand_new,
        expand_new.astype(jnp.bfloat16),
        expand_first_new,
        expand_second_new,
        reduce_new,
        reduce_new.astype(jnp.bfloat16),
        reduce_first_new,
        reduce_second_new,
        gains_new,
        gains_first_new,
        gains_second_new,
        bias_new,
        bias_first_new,
        bias_second_new,
    )


MESH = pl.DeviceIdType.MESH
IN_VMEM = pl.BlockSpec(memory_space=pltpu.VMEM)
IN_SMEM = pl.BlockSpec(memory_space=pltpu.SMEM)
LANES = 128
HEADS_HERE = LANES // HEAD_DIM
VARIATES = 16
MIB = 1 << 20
LOW = jnp.bfloat16
WIDE = jnp.float32
TOTAL_ROWS = 24


def fast_fits(seq, batch):
    return seq == 8 and batch == 4 and seq * LANES == D


def flip(index, mask):
    result, bit = index, 1
    while bit <= mask:
        if mask & bit:
            result = result + bit - 2 * bit * lax.rem(lax.div(index, bit), 2)
        bit *= 2
    return result


def push(source, target, send_sem, recv_sem, device):
    return pltpu.make_async_remote_copy(
        src_ref=source,
        dst_ref=target,
        send_sem=send_sem,
        recv_sem=recv_sem,
        device_id=device,
        device_id_type=MESH,
    )


def block_of(index, size):
    return pl.ds(pl.multiple_of(index * size, size), size)


def dot(left, right):
    return jnp.dot(left, right, preferred_element_type=WIDE)


def dot_turned(left, right):
    return lax.dot_general(left, right, (((1,), (1,)), ((), ())), preferred_element_type=WIDE)


def turned_dot(left, right):
    return lax.dot_general(left, right, (((0,), (0,)), ((), ())), preferred_element_type=WIDE)


class Team:
    def __init__(self, index, place):
        self.index, self.place = index, place

    def at(self, mask):
        return flip(self.index, mask)


def head_team(me, group):
    return Team(me, lambda mask: (flip(me, mask), group))


def feed_team(me, group):
    return Team(
        4 * lax.rem(group, 2) + lax.rem(me, 4),
        lambda mask: (flip(me, mask % 4), flip(group, mask // 4)),
    )


class Gather:
    def __init__(self, team, rows, all_rows, sends, recvs):
        self.team, self.all_rows, self.sends, self.recvs = team, all_rows, sends, recvs
        self.size = all_rows.shape[0] // 8
        self.given = rows
        self.rows = all_rows.at[block_of(team.index, self.size)] if rows is None else rows

    def copy(self, mask, passing):
        source = self.all_rows.at[block_of(self.team.at(mask - 1 if passing else 0), self.size)]
        return push(
            source if passing else self.rows,
            source,
            self.sends.at[mask],
            self.recvs.at[mask],
            self.team.place(1 if passing else mask),
        )

    def start(self, masks=(6, 2, 4, 1)):
        for mask in masks:
            self.copy(mask, False).start()
        if self.given is not None:
            self.all_rows[block_of(self.team.index, self.size)] = self.given[...]

    def pass_on(self, chip):
        self.copy(2 * chip, False).wait_recv()
        self.copy(2 * chip + 1, True).start()

    def complete(self, chip):
        self.copy(2 * chip + 1, chip > 0).wait_recv()

    def finish(self):
        for mask in (6, 2, 4, 1):
            self.copy(mask, False).wait_send()
        for mask in (3, 5, 7):
            self.copy(mask, True).wait_send()


def at_step(step, number, *works):
    @pl.when(step == number)
    def _():
        for work in works:
            work()


def each_chip(gather, work, after):
    def one_chip(chip, unused):
        @pl.when(chip == 0)
        def _():
            gather.complete(0)

        @pl.when(chip == 1)
        def _():
            gather.pass_on(1)
            gather.pass_on(2)
            gather.copy(6, False).start()
            gather.complete(1)

        @pl.when(chip == 2)
        def _():
            gather.complete(2)

        @pl.when(chip == 3)
        def _():
            gather.pass_on(3)
            gather.complete(3)

        work(chip)
        for number, works in after.items():
            at_step(chip, number, *works)
        return unused

    lax.fori_loop(0, 4, one_chip, 0)
    gather.finish()


class Scatter:
    def __init__(self, team, buffers, near_sends, near_recvs, far_sends, far_recvs):
        self.whole, self.keep, self.near_from, self.near, self.far_from, self.far = buffers
        self.sems = near_sends, near_recvs, far_sends, far_recvs
        self.team = team
        self.size = self.keep.shape[1]

    def near_copy(self, chip):
        return push(
            self.near_from.at[chip],
            self.near.at[chip],
            self.sems[0].at[chip],
            self.sems[1].at[chip],
            self.team.place(1),
        )

    def far_copy(self, chip):
        return push(
            self.far_from.at[chip],
            self.far.at[chip],
            self.sems[2].at[chip],
            self.sems[3].at[chip],
            self.team.place(2 * chip),
        )

    def put(self, chip, rows):
        core = lax.rem(self.team.index, 2)
        self.whole[...] = rows
        self.near_from[chip] = self.whole[block_of(1 - core, self.size)].astype(LOW)
        self.near_copy(chip).start()
        self.keep[chip] = self.whole[block_of(core, self.size)]

    def combine(self, chip):
        self.near_copy(chip).wait_recv()
        self.far_from[chip] = (self.keep[chip] + self.near[chip].astype(WIDE)).astype(LOW)
        self.far_copy(chip).start()

    def total(self):
        self.near_copy(0).wait_recv()
        total = self.keep[0] + self.near[0].astype(WIDE)
        for chip in (1, 2, 3):
            self.far_copy(chip).wait_recv()
            total = total + self.far[chip].astype(WIDE)
        for chip in (0, 1, 2, 3):
            self.near_copy(chip).wait_send()
            if chip:
                self.far_copy(chip).wait_send()
        return total


class Quad:
    def __init__(self, part, along_near, along_far):
        self.part, self.along_near, self.along_far = part, along_near, along_far


def feed_quad(me, group):
    return Quad(2 * lax.div(me, 4) + lax.div(group, 2), (flip(me, 4), group), (me, flip(group, 2)))


def head_quad(me, group):
    return Quad(
        2 * lax.rem(group, 2) + lax.div(group, 2), (me, flip(group, 1)), (me, flip(group, 2))
    )


def line_place(part):
    return 2 * lax.rem(part, 2) + lax.div(part, 2)


class QuadGather:
    def __init__(self, quad, part_of, sends, recvs):
        self.part_of, self.sends, self.recvs = part_of, sends, recvs
        self.part, self.along_near, self.along_far = quad.part, quad.along_near, quad.along_far

    def copy(self, way):
        part = self.part_of(flip(self.part, 1) if way == 3 else self.part)
        device = self.along_far if way == 1 else self.along_near
        return push(part, part, self.sends.at[way], self.recvs.at[way], device)

    def start_near(self):
        self.copy(2).start()

    def start_far(self):
        self.copy(1).start()

    def start(self):
        self.start_far()
        self.start_near()

    def pass_on(self):
        self.copy(1).wait_recv()
        self.copy(3).start()

    def land(self):
        self.copy(2).wait_recv()
        self.copy(3).wait_recv()

    def finish(self):
        for way in (1, 2, 3):
            self.copy(way).wait_send()


class QuadScatter:
    def __init__(self, quad, part_of, landing, sends, recvs):
        self.part_of, self.landing, self.sends, self.recvs = part_of, landing, sends, recvs
        self.part, self.along_near, self.along_far = quad.part, quad.along_near, quad.along_far

    def copy(self, slot):
        return push(
            self.part_of(flip(self.part, (2, 3, 1)[slot])),
            self.landing.at[slot],
            self.sends.at[slot],
            self.recvs.at[slot],
            self.along_far if slot == 2 else self.along_near,
        )

    def start_far(self):
        self.copy(1).start()

    def start_near(self):
        self.copy(0).start()

    def start(self):
        self.start_far()
        self.start_near()

    def total(self):
        total = self.part_of(self.part)[...].astype(WIDE)
        return total + self.landing[0].astype(WIDE) + self.landing[2].astype(WIDE)

    def pass_on(self):
        self.copy(1).wait_recv()
        part = self.part_of(flip(self.part, 1))
        part[...] = (part[...].astype(WIDE) + self.landing[1].astype(WIDE)).astype(LOW)
        self.copy(2).start()

    def land(self):
        self.copy(0).wait_recv()
        self.copy(2).wait_recv()

    def finish(self):
        for slot in (0, 1, 2):
            self.copy(slot).wait_send()


def chip_of(team, chip):
    here = lax.div(team.index, 2)
    if isinstance(chip, int):
        return flip(here, chip)
    column = lax.rem(lax.rem(here, 2) + lax.rem(chip, 2), 2)
    row = lax.rem(lax.div(here, 2) + lax.div(chip, 2), 2)
    return 2 * row + column


def turn_rows(values, cosine, sine):
    half = HEAD_DIM // 2
    pieces = []
    for start in range(0, values.shape[0], HEAD_DIM):
        first, second = values[start : start + half], values[start + half : start + HEAD_DIM]
        pieces += [first * cosine - second * sine, second * cosine + first * sine]
    return jnp.concatenate(pieces, axis=0)


def thirds(values):
    first = values.astype(LOW).astype(WIDE)
    second = (values - first).astype(LOW).astype(WIDE)
    return first, second, values - first - second


def pick(row, choices):
    result = jnp.zeros(row.shape, WIDE)
    for number, choice in choices.items():
        result = jnp.where(row == number, choice, result)
    return result


def norm_rows(values):
    scale = lax.rsqrt(jnp.mean(values * values, axis=-1, keepdims=True) + NORM_EPS)
    return values * scale, scale


def feed_block(block):
    y, x, core, far_z, near_z = (block // 16, block // 8 % 2, block // 4 % 2, block // 2 % 2, block % 2)
    return 4 * near_z + 2 * x + core, 2 * y + far_z


def layer_kernel(seq, batch, ins, outs, mem):
    me, group = lax.axis_index("seq"), lax.axis_index("batch")
    rows = ins.inputs.shape[0]
    length = rows * seq
    pair = 2 * rows
    share = ins.attend.shape[1]
    wide_columns = ins.expand.shape[2] // D
    hidden_width = mem.reduce_all.shape[0] * mem.reduce_all.shape[1]
    blocks = ins.expand.shape[2] // LANES
    heads, feeds = head_team(me, group), feed_team(me, group)
    head_four, feed_four = head_quad(me, group), feed_quad(me, group)
    quad = feed_four.part

    staged = [(ins.attend.at[which], mem.keep.at[0, block_of(which, share)]) for which in range(3)]
    staged.append((ins.output, mem.keep.at[0, block_of(3, share)]))
    staged.append((ins.reduce, mem.keep.at[1]))
    for which in range(2):
        for block in range(wide_columns):
            columns = slice(block * D, (block + 1) * D)
            staged.append(
                (ins.expand.at[which, :, columns], mem.keep.at[2 + which, block_of(block, share)])
            )
    staged = [
        pltpu.make_async_copy(source, target, mem.stage_sem.at[number])
        for number, (source, target) in enumerate(staged)
    ]
    for copy in staged:
        copy.start()
    barrier = pltpu.get_barrier_semaphore()
    for mask in range(1, seq):
        pl.semaphore_signal(barrier, inc=1, device_id=(flip(me, mask), group), device_id_type=MESH)
    for step in range(1, batch):
        pl.semaphore_signal(
            barrier, inc=1, device_id=(me, lax.rem(group + step, batch)), device_id_type=MESH
        )
    for mask in (5, 6, 7):
        pl.semaphore_signal(barrier, inc=1, device_id=feeds.place(mask), device_id_type=MESH)

    position = me * rows + lax.broadcasted_iota(jnp.int32, (1, rows), 1)
    inside = position < ins.lengths[0]
    scored = jnp.logical_and(inside, ins.observed[...] == 1).astype(WIDE)
    variate = ins.variates[...].astype(WIDE)
    turns = ins.turns.shape[0]
    mem.facts_own[:turns] = ins.turns[...]
    mem.facts_own[turns:] = jnp.concatenate(
        [jnp.where(inside, variate, -1.0), variate, scored, jnp.zeros((5, rows), WIDE)], axis=0
    )
    mem.scored[...] = jnp.broadcast_to(scored, (rows, rows)).T
    unit_one, scale_one = norm_rows(ins.inputs[...].astype(WIDE))
    mem.own_rows[0] = (unit_one * ins.gains[0:1, :]).astype(LOW)
    for copy in staged:
        copy.wait()
    for which in range(3):
        mem.attend_low[which] = mem.keep[0, block_of(which, share)].astype(LOW)
    mem.output_full[block_of(batch * me + group, share)] = mem.keep[0, block_of(3, share)].astype(LOW)
    mem.reduce_all[quad] = mem.keep[1].astype(LOW)
    for which in range(2):
        for block in range(blocks):
            owner, part = feed_block(block)
            row, lane = divmod(block * LANES, D)
            mem.expand_low[which, owner, :, part * LANES : (part + 1) * LANES] = mem.keep[
                2 + which, block_of(row, share), lane : lane + LANES
            ].astype(LOW)
    pl.semaphore_wait(barrier, seq + batch + 1)

    masks = (6, 7, 4, 5, 2, 3, 1)

    def start_attend_columns():
        copies = []
        for mask in masks:
            copy = push(
                mem.attend_low.at[:, :, block_of(heads.at(mask), LANES)],
                mem.attend_all.at[:, me, group],
                mem.column_send.at[0, mask],
                mem.column_recv.at[0, mask],
                heads.place(mask),
            )
            copy.start()
            copies.append(copy)
        mem.attend_all[:, me, group] = mem.attend_low[:, :, block_of(me, LANES)]
        return copies

    def start_expand_columns():
        copies = []
        for mask in masks:
            copy = push(
                mem.expand_low.at[:, feeds.at(mask)],
                mem.expand_all.at[:, me, group],
                mem.column_send.at[1, mask],
                mem.column_recv.at[1, mask],
                feeds.place(mask),
            )
            copy.start()
            copies.append(copy)
        mem.expand_all[:, me, group] = mem.expand_low[:, feeds.index]
        return copies

    def expand_part_of(array, which):
        def part_of(part):
            return array.at[which, pl.ds(4 * lax.div(part, 2), 4), pl.ds(2 * lax.rem(part, 2), 2)]

        return part_of

    def quad_gather(four, row, part_of):
        return QuadGather(four, part_of, mem.line_send.at[row], mem.line_recv.at[row])

    def gather(team, phase, all_rows):
        return Gather(
            team,
            mem.own_rows.at[phase],
            all_rows,
            mem.gather_send.at[phase],
            mem.gather_recv.at[phase],
        )

    def scatter(team, phase):
        return Scatter(
            team,
            (mem.whole, mem.keep, mem.near_from, mem.near, mem.far_from, mem.far),
            mem.near_send.at[phase],
            mem.near_recv.at[phase],
            mem.far_send.at[phase],
            mem.far_recv.at[phase],
        )

    attend_columns = start_attend_columns()
    line_output = quad_gather(
        head_four, 1, lambda part: mem.output_full.at[block_of(batch * me + line_place(part), share)]
    )
    line_output.start()
    facts = Gather(heads, mem.facts_own, mem.facts_all, mem.facts_send, mem.facts_recv)
    facts.start()
    for copy in attend_columns:
        copy.wait_recv()
    line_attend = quad_gather(head_four, 0, lambda part: mem.attend_all.at[:, :, line_place(part)])
    line_attend.start()
    acts = gather(heads, 0, mem.act_one)
    acts.start()
    for chip in (1, 2, 3):
        facts.pass_on(chip)
    for chip in (0, 1, 2, 3):
        facts.complete(chip)
    facts.finish()
    step_rows = mem.facts_own.shape[0]
    half = HEAD_DIM // 2
    count = jnp.zeros((8, LANES), WIDE)
    for slot in range(seq):
        columns = slice(slot * rows, (slot + 1) * rows)
        start = slot * step_rows
        mem.cosine[:, columns] = mem.facts_all[start : start + half]
        mem.sine[:, columns] = mem.facts_all[start + half : start + 2 * half]
        labels = mem.facts_all[start + 2 * half : start + 2 * half + 8]
        mem.labels[:, columns] = labels
        count = count + labels
    mem.count[group] = count
    count_copies = []
    for step in range(1, batch):
        copy = push(
            mem.count.at[group],
            mem.count.at[group],
            mem.count_send.at[step],
            mem.count_recv.at[step],
            (me, lax.rem(group + step, batch)),
        )
        copy.start()
        count_copies.append(copy)

    def mark(block, unused):
        span = block_of(block, pair)
        row = lax.broadcasted_iota(jnp.int32, (HEAD_DIM, pair), 0)
        third = lax.div(row, VARIATES)
        variate = lax.rem(row, VARIATES).astype(WIDE)
        key_label, query_label = mem.labels[0:1, span], mem.labels[1:2, span]
        ones = jnp.ones((1, pair), WIDE)
        last = 3 * VARIATES
        hidden_keys = (key_label < 0.0).astype(WIDE)
        mem.key_marks[:, span] = jnp.where(
            third < 3,
            (key_label == variate).astype(WIDE),
            pick(row, {last: ones, last + 1: ones, last + 2: ones, last + 3: hidden_keys}),
        ).astype(LOW)
        query_marks = (query_label == variate).astype(WIDE)
        mem.sum_marks[:, span] = jnp.where(
            row < VARIATES, query_marks, pick(row, {VARIATES: ones})
        ).astype(LOW)
        for head in range(HEADS_HERE):
            number = me * HEADS_HERE + head
            other = jnp.full((HEAD_DIM, pair), ins.bias[1, number], WIDE)
            more = thirds(jnp.full((HEAD_DIM, pair), ins.bias[0, number], WIDE) - other)
            other = thirds(other)
            mem.query_turned[head, HEAD_DIM:, span] = jnp.where(
                third < 3,
                query_marks * jnp.where(third == 0, more[0], jnp.where(third == 1, more[1], more[2])),
                pick(row, {last: other[0], last + 1: other[1], last + 2: other[2], last + 3: MASKED}),
            ).astype(LOW)
        return unused

    lax.fori_loop(0, length // pair, mark, 0)
    acts.pass_on(1)
    acts.pass_on(2)
    line_output.pass_on()
    line_output.land()
    outputs = Gather(heads, None, mem.output_full, mem.output_send, mem.output_recv)
    outputs.start()
    acts.pass_on(3)
    line_attend.pass_on()
    for chip in range(4):
        acts.complete(chip)
    acts.finish()

    expand_columns = start_expand_columns()
    line_reduce = quad_gather(feed_four, 4, lambda part: mem.reduce_all.at[part])
    line_reduce.start_far()
    line_expand = [
        quad_gather(feed_four, 2 + which, expand_part_of(mem.expand_all, which)) for which in range(2)
    ]
    line_attend.land()
    line_reduce.start_near()

    def attend_matrix(which):
        return mem.attend_all[which].reshape(D, LANES)

    def project(block, unused):
        span = block_of(block, pair)
        weights = jnp.concatenate([attend_matrix(which) for which in range(3)], axis=1)
        products = dot(mem.act_one[span, :], weights)
        cosine, sine = mem.cosine[:, span], mem.sine[:, span]
        query = turn_rows(products[:, :LANES].T, cosine, sine).astype(LOW)
        query = (query.astype(WIDE) * HEAD_DIM ** (-0.5)).astype(LOW)
        key = turn_rows(products[:, LANES : 2 * LANES].T, cosine, sine).astype(LOW)
        value = products[:, 2 * LANES :].T.astype(LOW)
        mem.key_turned[:, span] = key
        mem.value_turned[:, span] = value

        for head in range(HEADS_HERE):
            features = slice(head * HEAD_DIM, (head + 1) * HEAD_DIM)
            mem.query_turned[head, :HEAD_DIM, span] = query[features]
            whole = jnp.concatenate([key[features], mem.key_marks[:, span]], axis=0)
            mem.key_heads[head, span, :] = whole.T
        return unused

    for copy in expand_columns:
        copy.wait_recv()
    line_expand[0].start_far()
    line_expand[0].start_near()
    lax.fori_loop(0, length // pair, project, 0)
    line_expand[1].start_far()
    outputs.pass_on(1)
    outputs.pass_on(2)

    core = lax.rem(me, 2)

    def mixed_copy(chip, which):
        other = 2 * chip_of(heads, chip) + which
        slot = 2 * chip + lax.rem(which + core, 2)
        return push(
            mem.mixed_out.at[block_of(other, rows)],
            mem.mixed_rows.at[:, block_of(me, LANES)],
            mem.mixed_send.at[slot],
            mem.mixed_recv.at[slot],
            (other, group),
        )

    def attend_block(chip):
        columns = block_of(chip_of(heads, chip), pair)
        for head in range(HEADS_HERE):
            span = slice(head * HEAD_DIM, (head + 1) * HEAD_DIM)
            scores = dot(mem.key_heads[head], mem.query_turned[head, :, columns])
            top = jnp.floor(jnp.max(scores, axis=0, keepdims=True))
            powers = jnp.exp(scores - top)
            probs = powers * (1.0 / jnp.sum(powers, axis=0, keepdims=True))
            rounded = probs.astype(LOW)
            mem.probs[head, :, columns] = rounded
            residue = (probs - rounded.astype(WIDE)).astype(LOW)
            coarse = dot(mem.value_turned[span, :], rounded)
            mem.exact[span, columns] = coarse + dot(mem.value_turned[span, :], residue)
            mem.mixed_wide[span, :] = coarse
        mixed = mem.mixed_wide[...].astype(LOW)
        mem.mixed_turned[:, columns] = mixed
        mem.mixed_out[columns, :] = mixed.T

    def attend_step(step, unused):
        chip = lax.rem(step + 1, 4)
        attend_block(chip)
        for which in range(2):

            @pl.when(jnp.logical_or(chip > 0, core != which))
            def _():
                mixed_copy(chip, which).start()

        at_step(step, 1, lambda: outputs.pass_on(3))
        return unused

    lax.fori_loop(0, 4, attend_step, 0)
    line_expand[1].start_near()
    mem.mixed_rows[:, block_of(me, LANES)] = mem.mixed_out[block_of(me, rows), :]
    for chip in range(4):
        outputs.complete(chip)
    outputs.finish()

    def wait_pieces(copy):
        for mask in range(1, seq):
            copy(mask).wait()

    def mixed_wait(mask):
        other = heads.at(mask)
        return push(
            mem.mixed_out.at[block_of(other, rows)],
            mem.mixed_rows.at[:, block_of(other, LANES)],
            mem.mixed_send.at[mask],
            mem.mixed_recv.at[mask],
            (other, group),
        )

    wait_pieces(mixed_wait)
    middle = ins.inputs[...].astype(WIDE) + dot(mem.mixed_rows[...], mem.output_full[...])
    mem.middle[...] = middle
    unit_two, scale_two = norm_rows(middle)
    mem.own_rows[1] = (unit_two * ins.gains[1:2, :]).astype(LOW)
    acts = gather(feeds, 1, mem.act_two)
    acts.start((2, 4, 1))
    line_reduce.pass_on()
    line_expand[0].pass_on()

    def split_heads(block, unused):
        span = block_of(block, pair)
        row = lax.broadcasted_iota(jnp.int32, (HEAD_DIM, pair), 0)
        value_marks = jnp.where(row < 3, 1.0, 0.0).astype(LOW)
        for head in range(HEADS_HERE):
            features = slice(head * HEAD_DIM, (head + 1) * HEAD_DIM)
            value = mem.value_turned[features, span]
            mem.value_heads[head, span, :] = jnp.concatenate([value, value_marks], axis=0).T
            query = mem.query_turned[head, :HEAD_DIM, span]
            whole = jnp.concatenate([query, mem.sum_marks[:, span]], axis=0)
            mem.query_heads[head, span, :] = whole.T
        mem.act_one_turned[:, span] = mem.act_one[span, :].T
        return unused

    lax.fori_loop(0, length // pair, split_heads, 0)
    line_expand[0].land()

    def expand_matrix(which):
        return mem.expand_all[which].reshape(D, hidden_width)

    def reduce_matrix():
        return mem.reduce_all[...].reshape(hidden_width, D)

    def feed_gate(chip):
        span = block_of(chip_of(feeds, chip), pair)
        mem.by_gate[span, :] = dot(mem.act_two[span, :], expand_matrix(0))

    def feed_up(chip, unused=0):
        span = block_of(chip_of(feeds, chip), pair)
        gate = mem.by_gate[span, :]
        up = dot(mem.act_two[span, :], expand_matrix(1))
        sigmoid = 1.0 / (1.0 + jnp.exp(-gate))
        swish = gate * sigmoid
        mem.by_up[span, :] = swish
        mem.by_gate[span, :] = up * sigmoid * (1.0 + gate * (1.0 - sigmoid))
        mem.hidden[span, :] = (swish * up).astype(LOW)
        return unused

    each_chip(
        acts,
        feed_gate,
        {
            0: [line_expand[1].pass_on],
            2: [line_expand[1].land, lambda: lax.fori_loop(0, 3, feed_up, 0)],
            3: [lambda: lax.fori_loop(3, 4, feed_up, 0)],
        },
    )
    line_reduce.land()
    sums = scatter(feeds, 1)

    def feed_down(step, unused):
        chip = lax.rem(step + 1, 4)
        span = block_of(chip_of(feeds, chip), pair)
        sums.put(chip, dot(mem.hidden[span, :], reduce_matrix()))
        at_step(step, 1, lambda: sums.combine(1))
        at_step(step, 2, lambda: sums.combine(2))
        return unused

    lax.fori_loop(0, 4, feed_down, 0)
    sums.combine(3)

    for block in range(length // pair):
        span = block_of(block, pair)
        mem.hidden_turned[:, span] = mem.hidden[span, :].T
        mem.act_two_turned[:, span] = mem.act_two[span, :].T
    output = mem.middle[...] + sums.total()
    outs.layer_output[...] = output
    for copy in count_copies:
        copy.wait()
    count_all = jnp.sum(
        mem.count[0, 2:3] + mem.count[1, 2:3] + mem.count[2, 2:3] + mem.count[3, 2:3],
        axis=1,
        keepdims=True,
    )
    error = jnp.where(mem.scored[:, 0:1] > 0.0, output - ins.teacher[...].astype(WIDE), 0.0)
    mem.squares[1:2, :] = jnp.sum(error * error, axis=0, keepdims=True)
    grad_out = error * (2.0 / (count_all * D))
    mem.grad_own[...] = grad_out
    mem.own_rows[2] = grad_out.astype(LOW)
    acts = gather(feeds, 2, mem.branch)
    acts.start((2, 4, 1))

    sums = scatter(feeds, 2)

    def feed_back(chip):
        span = block_of(chip_of(feeds, chip), pair)
        grad_hidden = dot_turned(mem.branch[span, :], reduce_matrix())
        grad_gate = (grad_hidden * mem.by_gate[span, :]).astype(LOW)
        grad_up = (grad_hidden * mem.by_up[span, :]).astype(LOW)
        mem.grad_gate[span, :] = grad_gate
        mem.grad_up[span, :] = grad_up
        sums.put(
            chip,
            dot_turned(
                jnp.concatenate([grad_gate, grad_up], axis=1),
                jnp.concatenate([expand_matrix(0), expand_matrix(1)], axis=1),
            ),
        )

    each_chip(acts, feed_back, {2: [lambda: sums.combine(1)], 3: [lambda: sums.combine(2)]})

    def quad_scatter(four, row, part_of, landing):
        return QuadScatter(four, part_of, landing, mem.back_send.at[row], mem.back_recv.at[row])

    def reduce_grad(part, unused):
        mem.reduce_grad[part] = dot(
            mem.hidden_turned[block_of(part, rows), :], mem.branch[...]
        ).astype(LOW)
        at_step(part, 0, lambda: sums.combine(3))
        return unused

    lax.fori_loop(0, batch, reduce_grad, 0)
    back_reduce = quad_scatter(
        feed_four, 0, lambda part: mem.reduce_grad.at[part], mem.reduce_land
    )
    back_reduce.start_far()

    def expand_grad(which):
        grads = (mem.grad_gate, mem.grad_up)[which]

        def one_block(block, unused):
            products = dot(mem.act_two_turned[block_of(block, pair), :], grads[...]).astype(LOW)
            mem.expand_grad[which, pl.ds(2 * block, 2)] = products.reshape(
                2, batch, share, hidden_width
            )
            return unused

        lax.fori_loop(0, seq // 2, one_block, 0)
        line = quad_scatter(
            feed_four, 1 + which, expand_part_of(mem.expand_grad, which), mem.expand_land.at[which]
        )
        return line

    back_expand = []
    back_expand.append(expand_grad(0))
    back_expand[0].start_far()
    grad_act = sums.total()
    unit_two, scale_two = norm_rows(mem.middle[...])
    gain = ins.gains[1:2, :]
    grad_unit = grad_act * gain
    mem.gains[1:2, :] = jnp.sum(grad_act * unit_two, axis=0, keepdims=True)
    grad_middle = mem.grad_own[...] + scale_two * (
        grad_unit - unit_two * jnp.mean(grad_unit * unit_two, axis=-1, keepdims=True)
    )
    mem.grad_own[...] = grad_middle
    mem.own_rows[3] = grad_middle.astype(LOW)
    grad_mixed = dot(mem.output_full[...], grad_middle.T.astype(LOW)).astype(LOW)
    mem.grad_mixed_out[...] = grad_mixed.reshape(seq, LANES, rows)

    def grad_copy(mask, back=False):
        return push(
            mem.grad_mixed_out.at[heads.at(mask)],
            mem.grad_mixed.at[:, block_of(heads.at(mask) if back else me, rows)],
            mem.mixed_send.at[8 + mask],
            mem.mixed_recv.at[8 + mask],
            heads.place(mask),
        )

    for mask in masks:
        grad_copy(mask).start()
    mem.grad_mixed[:, block_of(me, rows)] = mem.grad_mixed_out[me]
    back_reduce.pass_on()
    back_expand.append(expand_grad(1))
    back_expand[1].start_far()

    wait_pieces(lambda mask: grad_copy(mask, True))
    acts = gather(heads, 3, mem.grad_attn)
    acts.start()
    back_reduce.start_near()
    back_expand[0].start_near()
    back_attend = [
        quad_scatter(
            head_four,
            4 + which,
            lambda part, which=which: mem.attend_grad.at[which, :, line_place(part)],
            mem.attend_land.at[which],
        )
        for which in range(3)
    ]

    def attend_grad(which):
        def one_block(block, unused):
            products = dot(mem.act_one_turned[block_of(block, pair), :], mem.grad_project[which])
            mem.attend_grad[which, pl.ds(2 * block, 2)] = products.astype(LOW).reshape(
                2, batch, share, LANES
            )
            return unused

        lax.fori_loop(0, length // pair, one_block, 0)
        back_attend[which].start()

    lane = lax.broadcasted_iota(jnp.int32, (pair, LANES), 1)

    def grad_rows(block, unused):
        span = block_of(block, pair)
        whole = mem.grad_mixed[:, span].astype(WIDE).T
        for head in range(HEADS_HERE):
            mem.grad_heads[head, span, :] = jnp.where(lax.div(lane, HEAD_DIM) == head, whole, 0.0).astype(LOW)
        return unused

    lax.fori_loop(0, length // pair, grad_rows, 0)

    def value_back(block, unused):
        span = block_of(block, pair)
        total = dot(mem.probs[0, span, :], mem.grad_heads[0])
        for head in range(1, HEADS_HERE):
            total = total + dot(mem.probs[head, span, :], mem.grad_heads[head])
        mem.grad_project[2, span, :] = total.astype(LOW)
        return unused

    lax.fori_loop(0, length // pair, value_back, 0)
    back_expand[0].pass_on()
    attend_grad(2)

    def score_back(block, unused):
        columns = block_of(block, pair)
        row = lax.broadcasted_iota(jnp.int32, (HEAD_DIM, pair), 0)
        grads = mem.grad_mixed[:, columns]
        delta = grads.astype(WIDE) * mem.exact[:, columns]
        for head in range(HEADS_HERE):
            span = slice(head * HEAD_DIM, (head + 1) * HEAD_DIM)
            pieces = thirds(-jnp.sum(delta[span], axis=0, keepdims=True))
            marks = pick(row, dict(enumerate(pieces))).astype(LOW)
            change = dot(mem.value_heads[head], jnp.concatenate([grads[span], marks], axis=0))
            mem.probs[head, :, columns] = (mem.probs[head, :, columns].astype(WIDE) * change).astype(LOW)
        return unused

    lax.fori_loop(0, length // pair, score_back, 0)
    back_expand[1].start_near()
    mem.bias_sums[...] = jnp.zeros_like(mem.bias_sums)
    scale = HEAD_DIM ** (-0.5)

    def project_grads(block, unused):
        span = block_of(block, pair)
        cosine, sine = mem.cosine[:, span], -mem.sine[:, span]
        queries, keys = [], []
        for head in range(HEADS_HERE):
            features = slice(head * HEAD_DIM, (head + 1) * HEAD_DIM)
            queries.append(dot(mem.key_turned[features, :], mem.probs[head, :, span]) * scale)
            sums = dot(mem.probs[head, span, :], mem.query_heads[head]).T
            keys.append(sums[:HEAD_DIM])
            by_variate = sums[HEAD_DIM : HEAD_DIM + VARIATES]
            same = by_variate * mem.key_marks[:VARIATES, span].astype(WIDE)
            mem.bias_sums[head : head + 1, :] += jnp.sum(same, axis=0, keepdims=True)
            total = sums[HEAD_DIM + VARIATES : HEAD_DIM + VARIATES + 1]
            mem.bias_sums[HEADS_HERE + head : HEADS_HERE + head + 1, :] += total
        queries = turn_rows(jnp.concatenate(queries, axis=0), cosine, sine)
        mem.grad_project[0, span, :] = queries.T.astype(LOW)
        keys = turn_rows(jnp.concatenate(keys, axis=0), cosine, sine)
        mem.grad_project[1, span, :] = keys.T.astype(LOW)
        return unused

    lax.fori_loop(0, length // pair, project_grads, 0)
    back_expand[1].pass_on()
    attend_grad(0)
    acts.pass_on(1)
    acts.pass_on(2)
    sums = scatter(heads, 3)

    def project_back(step, unused):
        chip = lax.rem(step + 1, 4)
        span = block_of(chip_of(heads, chip), pair)
        grads = [mem.grad_project[which, span, :] for which in range(3)]
        weights = [attend_matrix(which) for which in range(3)]
        sums.put(chip, dot_turned(jnp.concatenate(grads, axis=1), jnp.concatenate(weights, axis=1)))
        at_step(step, 1, lambda: sums.combine(1))
        at_step(step, 2, lambda: sums.combine(2))
        return unused

    lax.fori_loop(0, 4, project_back, 0)
    sums.combine(3)
    attend_grad(1)
    acts.pass_on(3)
    for chip in range(4):
        acts.complete(chip)
    acts.finish()
    mem.output_grad[...] = (
        dot(mem.mixed_turned[...], mem.grad_attn[...]).astype(LOW).reshape(mem.output_grad.shape)
    )
    back_output = quad_scatter(
        head_four, 3, lambda part: mem.output_grad.at[line_place(part)], mem.output_land
    )
    back_output.start()
    for which in (2, 0):
        back_attend[which].pass_on()

    column_copies = []
    mem.squares[0:1, :] = jnp.zeros((1, D), WIDE)

    def add_squares(total):
        flat = total.reshape(-1, total.shape[-1])
        width = flat.shape[1]
        mem.squares[0:1, :width] += jnp.sum(flat * flat, axis=0, keepdims=True)

    def store_whole(total, out):
        out[...] = total
        add_squares(total)

    back_reduce.land()
    store_whole(back_reduce.total(), outs.reduce_share)
    def expand_shares(which):
        back_expand[which].land()
        own = expand_part_of(mem.expand_grad, which)(quad)

        def one_block(block, unused):
            total = (
                own[block].astype(WIDE)
                + mem.expand_land[which, 0, block].astype(WIDE)
                + mem.expand_land[which, 2, block].astype(WIDE)
            )
            mem.expand_part[which, block] = total.astype(LOW)
            add_squares(total)
            return unused

        lax.fori_loop(0, 4, one_block, 0)
        for mask in masks:
            other = feeds.at(mask)
            copy = push(
                mem.expand_part.at[which, lax.rem(other, 4), lax.div(other, 4)],
                mem.expand_share.at[which, feeds.index],
                mem.share_send.at[which, mask],
                mem.share_recv.at[which, mask],
                feeds.place(mask),
            )
            copy.start()
            column_copies.append(copy)
        mem.expand_share[which, feeds.index] = mem.expand_part[
            which, lax.rem(feeds.index, 4), lax.div(feeds.index, 4)
        ]

    expand_shares(0)
    back_attend[1].pass_on()
    expand_shares(1)

    def attend_shares(which):
        back_attend[which].land()
        total = back_attend[which].total()
        mem.attend_part[which] = total.astype(LOW)
        add_squares(total)

    attend_shares(2)
    grad_act = sums.total()
    unit_one, scale_one = norm_rows(ins.inputs[...].astype(WIDE))
    gain = ins.gains[0:1, :]
    grad_unit = grad_act * gain
    mem.gains[0:1, :] = jnp.sum(grad_act * unit_one, axis=0, keepdims=True)
    grad_input = mem.grad_own[...] + scale_one * (
        grad_unit - unit_one * jnp.mean(grad_unit * unit_one, axis=-1, keepdims=True)
    )
    outs.input_gradient[...] = grad_input * (count_all * D)
    outs.count[...] = jnp.broadcast_to(count_all, (8, LANES))

    back_output.pass_on()
    for which in range(2):
        attend_shares(which)
    for mask in masks:
        copy = push(
            mem.attend_part.at[:, heads.at(mask)],
            outs.attend_share.at[:, :, block_of(me, LANES)],
            mem.share_send.at[2, mask],
            mem.share_recv.at[2, mask],
            heads.place(mask),
        )
        copy.start()
        column_copies.append(copy)
    outs.attend_share[:, :, block_of(me, LANES)] = mem.attend_part[:, me]
    back_output.land()
    store_whole(back_output.total(), outs.output_share)

    lane = lax.broadcasted_iota(jnp.int32, (1, LANES), 1)
    lines = [
        mem.gains[which : which + 1, start : start + LANES]
        for which in range(2)
        for start in range(0, D, LANES)
    ]
    bias_line = jnp.zeros((1, LANES), WIDE)
    for row in range(2 * HEADS_HERE):
        place = row // HEADS_HERE * HEADS + me * HEADS_HERE + row % HEADS_HERE
        line = mem.bias_sums[row : row + 1, :]
        if row >= HEADS_HERE:
            line = line - mem.bias_sums[row - HEADS_HERE : row - HEADS_HERE + 1, :]
        amount = jnp.sum(line, axis=1, keepdims=True)
        bias_line = bias_line + jnp.where(lane == place, amount, 0.0)
    amounts = jnp.sum(mem.squares[0:2, :], axis=1, keepdims=True)
    amount_line = jnp.where(lane == 0, amounts[0:1], 0.0) + jnp.where(lane == 1, amounts[1:2], 0.0)
    lines += [bias_line, amount_line, jnp.zeros((6, LANES), WIDE)]
    mem.plane_totals[me] = jnp.concatenate(lines, axis=0)
    plane_copies = []
    for mask in masks:
        copy = push(
            mem.plane_totals.at[me],
            mem.plane_totals.at[me],
            mem.total_send.at[0, mask],
            mem.total_recv.at[0, mask],
            (flip(me, mask), group),
        )
        copy.start()
        plane_copies.append(copy)
    for copy in column_copies[: 2 * len(masks)]:
        copy.wait()
    for which in range(2):
        for block in range(blocks):
            owner, part = feed_block(block)
            outs.expand_share[which, :, block * LANES : (block + 1) * LANES] = mem.expand_share[
                which, owner, :, part * LANES : (part + 1) * LANES
            ]
    for copy in plane_copies:
        copy.wait()
    mem.line_totals[group] = jnp.sum(mem.plane_totals[...], axis=0)
    total_copies = []
    for step in range(1, batch):
        copy = push(
            mem.line_totals.at[group],
            mem.line_totals.at[group],
            mem.total_send.at[1, step],
            mem.total_recv.at[1, step],
            (me, lax.rem(group + step, batch)),
        )
        copy.start()
        total_copies.append(copy)
    for copy in total_copies:
        copy.wait()
    outs.totals[...] = jnp.sum(mem.line_totals[...], axis=0)
    for copy in column_copies[2 * len(masks) :]:
        copy.wait()
    for copies in (attend_columns, expand_columns):
        for copy in copies:
            copy.wait_send()
    for line in [line_attend, line_output, line_reduce] + line_expand:
        line.finish()
    for line in [back_output, back_reduce] + back_attend + back_expand:
        line.finish()


def call_layer(seq, batch, inputs, teacher, lengths, variates, observed, turns, bias, gains, attend, output, expand, reduce):
    rows, share, hidden = inputs.shape[0], attend.shape[1], expand.shape[2] // seq
    length, pair, chips = rows * seq, 2 * rows, seq // 2
    low = lambda *shape: pltpu.VMEM(shape, LOW)
    wide = lambda *shape: pltpu.VMEM(shape, WIDE)
    sems = lambda *shape: pltpu.SemaphoreType.DMA(shape)
    in_names = ["inputs", "teacher", "lengths", "variates", "observed", "turns", "bias", "gains"]
    in_names += ["attend", "output", "expand", "reduce"]
    outs = dict(
        layer_output=((rows, D), WIDE),
        input_gradient=((rows, D), WIDE),
        totals=((TOTAL_ROWS, LANES), WIDE),
        count=((8, LANES), WIDE),
        attend_share=((3, share, D), LOW),
        output_share=((output.shape[0], D), WIDE),
        expand_share=((2, share, hidden * seq), LOW),
        reduce_share=((reduce.shape[0], D), WIDE),
    )
    scratch = dict(
        gains=wide(2, D),
        squares=wide(8, D),
        plane_totals=wide(seq, TOTAL_ROWS, LANES),
        line_totals=wide(batch, TOTAL_ROWS, LANES),
        attend_low=low(3, share, D),
        expand_low=low(2, seq, share, hidden),
        attend_all=low(3, seq, batch, share, LANES),
        output_full=low(D, D),
        expand_all=low(2, seq, batch, share, hidden),
        reduce_all=low(batch, reduce.shape[0], D),
        own_rows=low(4, rows, D),
        act_one=low(length, D),
        act_two=low(length, D),
        branch=low(length, D),
        grad_attn=low(length, D),
        facts_own=wide(turns.shape[0] + 8, LANES),
        facts_all=wide(seq * (turns.shape[0] + 8), LANES),
        scored=wide(rows, LANES),
        cosine=wide(HEAD_DIM // 2, length),
        sine=wide(HEAD_DIM // 2, length),
        labels=wide(8, length),
        key_marks=low(HEAD_DIM, length),
        count=wide(batch, 8, LANES),
        query_turned=low(HEADS_HERE, LANES, length),
        key_turned=low(LANES, length),
        value_turned=low(LANES, length),
        key_heads=low(HEADS_HERE, length, LANES),
        value_heads=low(HEADS_HERE, length, LANES),
        query_heads=low(HEADS_HERE, length, LANES),
        grad_heads=low(HEADS_HERE, length, LANES),
        grad_mixed=low(LANES, length),
        grad_mixed_out=low(seq, LANES, rows),
        probs=low(HEADS_HERE, length, length),
        mixed_out=low(length, LANES),
        mixed_rows=low(rows, D),
        sum_marks=low(HEAD_DIM, length),
        hidden_turned=low(hidden, length),
        act_two_turned=low(D, length),
        exact=wide(LANES, length),
        mixed_wide=wide(LANES, pair),
        mixed_turned=low(LANES, length),
        whole=wide(pair, D),
        keep=wide(chips, rows, D),
        near_from=low(chips, rows, D),
        near=low(chips, rows, D),
        far_from=low(chips, rows, D),
        far=low(chips, rows, D),
        middle=wide(rows, D),
        grad_own=wide(rows, D),
        by_up=wide(length, hidden),
        by_gate=wide(length, hidden),
        hidden=low(length, hidden),
        grad_gate=low(length, hidden),
        grad_up=low(length, hidden),
        bias_sums=wide(8, pair),
        grad_project=low(3, length, LANES),
        act_one_turned=low(D, length),
        reduce_grad=low(batch, reduce.shape[0], D),
        expand_grad=low(2, seq, batch, share, hidden),
        output_grad=low(batch, output.shape[0], D),
        attend_grad=low(3, seq, batch, share, LANES),
        reduce_land=low(3, reduce.shape[0], D),
        expand_land=low(2, 3, 4, 2, share, hidden),
        output_land=low(3, output.shape[0], D),
        attend_land=low(3, 3, seq, share, LANES),
        expand_part=low(2, 4, 2, share, hidden),
        expand_share=low(2, seq, share, hidden),
        attend_part=low(3, seq, share, LANES),
        stage_sem=sems(5 + 2 * (expand.shape[2] // D)),
        total_send=sems(2, seq),
        total_recv=sems(2, seq),
        column_send=sems(2, seq),
        column_recv=sems(2, seq),
        line_send=sems(5, batch),
        line_recv=sems(5, batch),
        facts_send=sems(seq),
        facts_recv=sems(seq),
        gather_send=sems(4, seq),
        gather_recv=sems(4, seq),
        count_send=sems(batch),
        count_recv=sems(batch),
        near_send=sems(4, chips),
        near_recv=sems(4, chips),
        far_send=sems(4, chips),
        far_recv=sems(4, chips),
        back_send=sems(7, batch),
        back_recv=sems(7, batch),
        output_send=sems(seq),
        output_recv=sems(seq),
        mixed_send=sems(2 * seq),
        mixed_recv=sems(2 * seq),
        share_send=sems(3, seq),
        share_recv=sems(3, seq),
    )

    places = dict.fromkeys(("attend", "output", "expand", "reduce"), pl.BlockSpec(memory_space=pl.ANY))
    places["bias"] = places["lengths"] = IN_SMEM

    def kernel(*refs):
        groups, start = [], 0
        for names in (in_names, outs, scratch):
            names = list(names)
            groups.append(types.SimpleNamespace(**dict(zip(names, refs[start : start + len(names)]))))
            start += len(names)
        layer_kernel(seq, batch, *groups)

    results = pl.pallas_call(
        kernel,
        out_shape=[jax.ShapeDtypeStruct(*out) for out in outs.values()],
        in_specs=[places.get(name, IN_VMEM) for name in in_names],
        out_specs=[IN_VMEM] * len(outs),
        scratch_shapes=list(scratch.values()),
        compiler_params=pltpu.CompilerParams(
            collective_id=0, has_side_effects=True, vmem_limit_bytes=63 * MIB
        ),
        name="layer",
    )(inputs, teacher, lengths, variates, observed, turns, bias, gains, attend, output, expand, reduce)
    return types.SimpleNamespace(**dict(zip(outs, results)))


def update_kernel(
    smalls, ins, small_outs, outs, olds, shares, news, copies, passed, in_sems, out_sems
):
    totals, count, gains, gains_first, gains_second, bias, bias_first, bias_second = smalls
    order = (2, 3, 0, 1)
    comes = []
    for place, number in enumerate(order):
        pairs = list(zip(ins[4 + 3 * number : 7 + 3 * number], olds[3 * number : 3 * number + 3]))
        pairs.append((ins[number], shares[number]))
        comes.append(
            [
                pltpu.make_async_copy(source, target, in_sems.at[4 * place + part])
                for part, (source, target) in enumerate(pairs)
            ]
        )
    for copy in sum(comes, []):
        copy.start()
    through = [
        pltpu.make_async_copy(ins[16 + part], passed[part], in_sems.at[16 + part]) for part in range(2)
    ]
    for copy in through:
        copy.start()
    goes = []
    gains_total = jnp.concatenate(
        [
            jnp.concatenate([totals[row + i : row + i + 1, :] for i in range(D // LANES)], axis=1)
            for row in (0, D // LANES)
        ],
        axis=0,
    )
    row = 2 * D // LANES
    bias_total = jnp.concatenate(
        [totals[row : row + 1, :HEADS], totals[row : row + 1, HEADS : 2 * HEADS]], axis=0
    )
    row += 1

    def sum_all(values):
        return jnp.sum(jnp.sum(values, axis=0, keepdims=True), axis=1, keepdims=True)

    squares = (
        totals[row : row + 1, 0:1] + sum_all(gains_total * gains_total) + sum_all(bias_total * bias_total)
    )
    grad_norm = jnp.sqrt(squares)
    clip = jnp.minimum(1.0, CLIP_NORM / grad_norm)
    small_outs[0][...] = totals[row : row + 1, 1:2] / (count[0:1, 0:1] * D)
    small_outs[1][...] = grad_norm
    rates = (RATE_ATTEND, RATE_OUTPUT, RATE_EXPAND, RATE_REDUCE)
    for place, number in enumerate(order):
        for copy in comes[place]:
            copy.wait()
        weight, first, second = olds[3 * number : 3 * number + 3]
        new, first_new, second_new = news[3 * number : 3 * number + 3]
        arrays = (new, copies[number], first_new, second_new, weight, first, second, shares[number])
        for lead in range(weight.shape[0] if weight.ndim == 3 else 1):

            def one_block(block, unused, lead=lead, arrays=arrays, rate=rates[number]):
                rows = block_of(block, 16)
                place = (lead, rows) if arrays[0].ndim == 3 else (rows,)
                old, moment, square, share = [array[place] for array in arrays[4:]]
                step = fast_step(old, moment, square, share.astype(WIDE) * clip, rate)
                arrays[0][place], arrays[2][place], arrays[3][place] = step
                arrays[1][place] = step[0].astype(LOW)
                return unused

            lax.fori_loop(0, weight.shape[-2] // 16, one_block, 0)
        for part, source in enumerate((new, copies[number], first_new, second_new)):
            copy = pltpu.make_async_copy(
                source, outs[2 + 4 * number + part], out_sems.at[2 + 4 * number + part]
            )
            copy.start()
            goes.append(copy)
        if place == 0:
            for part in range(2):
                through[part].wait()
                copy = pltpu.make_async_copy(passed[part], outs[part], out_sems.at[part])
                copy.start()
                goes.append(copy)
    for number, (old, total, rate) in enumerate(
        (
            ((gains, gains_first, gains_second), gains_total, RATE_GAINS),
            ((bias, bias_first, bias_second), bias_total, RATE_BIAS),
        )
    ):
        new, first_new, second_new = small_outs[2 + 3 * number : 5 + 3 * number]
        new[...], first_new[...], second_new[...] = adam_step(
            old[0][...], old[1][...], old[2][...], total * clip, rate, 0.0
        )
    for copy in goes:
        copy.wait()


def fast_step(weight, first, second, gradient, rate):
    first = BETA_ONE * first + (1.0 - BETA_ONE) * gradient
    second = BETA_TWO * second + ((1.0 - BETA_TWO) * gradient) * gradient
    low = jnp.sqrt(second * (1.0 / (1.0 - BETA_TWO**STEP))) + ADAM_EPS
    step = first * (rate / (1.0 - BETA_ONE**STEP)) / low
    return weight * (1.0 - rate * WEIGHT_DECAY) - step, first, second


def call_update(done, shares, smalls, olds):
    in_hbm = pl.BlockSpec(memory_space=pl.ANY)
    smalls = [done.totals, done.count] + smalls
    ins = shares + olds + [done.layer_output, done.input_gradient]
    one = jax.ShapeDtypeStruct((1, 1), WIDE)
    small_outs = [one, one] + smalls[2:]
    outs = [(done.layer_output, WIDE), (done.input_gradient, WIDE)]
    for weight in olds[::3]:
        outs += [(weight, dtype) for dtype in (WIDE, LOW, WIDE, WIDE)]
    passed = ins[-2:]
    parts = [smalls, ins, small_outs, outs, olds, shares, olds, olds[::3], passed]

    def kernel(*refs):
        groups, start = [], 0
        for part in parts:
            groups.append(refs[start : start + len(part)])
            start += len(part)
        update_kernel(*groups, *refs[start:])

    results = pl.pallas_call(
        kernel,
        out_shape=[jax.ShapeDtypeStruct(array.shape, WIDE) for array in small_outs]
        + [jax.ShapeDtypeStruct(array.shape, dtype) for array, dtype in outs],
        in_specs=[IN_VMEM] * len(smalls) + [in_hbm] * len(ins),
        out_specs=[IN_VMEM] * len(small_outs) + [in_hbm] * len(outs),
        scratch_shapes=[pltpu.VMEM(array.shape, WIDE) for array in olds]
        + [pltpu.VMEM(array.shape, array.dtype) for array in shares]
        + [pltpu.VMEM(array.shape, WIDE) for array in olds]
        + [pltpu.VMEM(array.shape, LOW) for array in olds[::3]]
        + [pltpu.VMEM(array.shape, WIDE) for array in passed]
        + [pltpu.SemaphoreType.DMA((18,)), pltpu.SemaphoreType.DMA((18,))],
        compiler_params=pltpu.CompilerParams(vmem_limit_bytes=63 * MIB),
        name="update",
    )(*smalls, *ins)
    return results[: len(small_outs)], results[len(small_outs) :]


def fast_body(
    seq,
    batch,
    inputs,
    teacher,
    lengths,
    variate_ids,
    time_ids,
    observed,
    attend_weight,
    output_weight,
    expand_weight,
    reduce_weight,
    norm_gains,
    variate_bias,
    attend_first,
    output_first,
    expand_first,
    reduce_first,
    gains_first,
    bias_first,
    attend_second,
    output_second,
    expand_second,
    reduce_second,
    gains_second,
    bias_second,
):
    half_dim = HEAD_DIM // 2
    frequency = jnp.exp(-math.log(ROPE_BASE) * jnp.arange(half_dim).astype(WIDE) / half_dim)
    angle = frequency[:, None] * time_ids.astype(WIDE)
    done = call_layer(
        seq,
        batch,
        inputs[0],
        teacher[0],
        lengths,
        variate_ids,
        observed,
        jnp.concatenate([jnp.cos(angle), jnp.sin(angle)]),
        variate_bias,
        norm_gains,
        attend_weight,
        output_weight,
        expand_weight,
        reduce_weight,
    )
    small, large = call_update(
        done,
        [done.attend_share, done.output_share, done.expand_share, done.reduce_share],
        [norm_gains, gains_first, gains_second, variate_bias, bias_first, bias_second],
        [attend_weight, attend_first, attend_second]
        + [output_weight, output_first, output_second]
        + [expand_weight, expand_first, expand_second]
        + [reduce_weight, reduce_first, reduce_second],
    )
    return (
        large[0][None],
        small[0].reshape(()),
        large[1][None],
        small[1].reshape(()),
    ) + tuple(large[2:] + small[2:])


def solution(mesh):
    seq, batch = mesh.shape["seq"], mesh.shape["batch"]
    body = functools.partial(fast_body, seq, batch) if fast_fits(seq, batch) else general_body
    in_specs = (
        P("batch", "seq", None),
        P("batch", "seq", None),
        P("batch"),
        P("batch", "seq"),
        P("batch", "seq"),
        P("batch", "seq"),
        P(None, ("seq", "batch"), None),
        P(("seq", "batch"), None),
        P(None, ("seq", "batch"), None),
        P(("seq", "batch"), None),
        P(),
        P(),
        P(None, ("seq", "batch"), None),
        P(("seq", "batch"), None),
        P(None, ("seq", "batch"), None),
        P(("seq", "batch"), None),
        P(),
        P(),
        P(None, ("seq", "batch"), None),
        P(("seq", "batch"), None),
        P(None, ("seq", "batch"), None),
        P(("seq", "batch"), None),
        P(),
        P(),
    )
    out_specs = (
        P("batch", "seq", None),
        P(),
        P("batch", "seq", None),
        P(),
        P(None, ("seq", "batch"), None),
        P(None, ("seq", "batch"), None),
        P(None, ("seq", "batch"), None),
        P(None, ("seq", "batch"), None),
        P(("seq", "batch"), None),
        P(("seq", "batch"), None),
        P(("seq", "batch"), None),
        P(("seq", "batch"), None),
        P(None, ("seq", "batch"), None),
        P(None, ("seq", "batch"), None),
        P(None, ("seq", "batch"), None),
        P(None, ("seq", "batch"), None),
        P(("seq", "batch"), None),
        P(("seq", "batch"), None),
        P(("seq", "batch"), None),
        P(("seq", "batch"), None),
        P(),
        P(),
        P(),
        P(),
        P(),
        P(),
    )
    return jax.shard_map(body, mesh=mesh, in_specs=in_specs, out_specs=out_specs, check_vma=False)
```

```python
import functools
import math
import types

import jax
import jax.numpy as jnp
from jax import lax
from jax.experimental import pallas as pl
from jax.experimental.pallas import tpu as pltpu
from jax.sharding import PartitionSpec as P

D = 1024
HEADS = 16
HEAD_DIM = 64
STEP = 10


NORM_EPS = 1e-05
ROPE_BASE = 10000.0
MASKED = -1e30
CLIP_NORM = 1.0
BETA_ONE = 0.9
BETA_TWO = 0.98
ADAM_EPS = 1e-08
WEIGHT_DECAY = 0.1
RATE_ATTEND = 0.03
RATE_OUTPUT = 0.5
RATE_EXPAND = 0.03
RATE_REDUCE = 0.015
RATE_GAINS = 1.0
RATE_BIAS = 0.5


def angles(times):
    half_dim = HEAD_DIM // 2
    frequency = jnp.exp(-math.log(ROPE_BASE) * jnp.arange(half_dim).astype(jnp.float32) / half_dim)
    angle_table = times.astype(jnp.float32)[..., None] * frequency
    return (jnp.cos(angle_table)[..., None, :], jnp.sin(angle_table)[..., None, :])


def rotate(values, cos_table, sin_table):
    half_dim = values.shape[-1] // 2
    first_half = values[..., :half_dim]
    second_half = values[..., half_dim:]
    return jnp.concatenate(
        [
            first_half * cos_table - second_half * sin_table,
            second_half * cos_table + first_half * sin_table,
        ],
        axis=-1,
    )


def unrotate(values, cos_table, sin_table):
    half_dim = values.shape[-1] // 2
    first_half = values[..., :half_dim]
    second_half = values[..., half_dim:]
    return jnp.concatenate(
        [
            first_half * cos_table + second_half * sin_table,
            second_half * cos_table - first_half * sin_table,
        ],
        axis=-1,
    )


def normalize(values):
    inv_scale = lax.rsqrt(jnp.mean(values * values, axis=-1, keepdims=True) + NORM_EPS)
    return (values * inv_scale, inv_scale)


def norm_back(grad_act, unit_rows, inv_scale, gain_row):
    grad_unit = grad_act * gain_row
    return inv_scale * (
        grad_unit - unit_rows * jnp.mean(grad_unit * unit_rows, axis=-1, keepdims=True)
    )


def score_block(query_rows, query_labels, key_rows, key_labels, bias_table):
    scores = jnp.einsum(
        "ihe,jhe->hij", query_rows, key_rows, preferred_element_type=jnp.float32
    ) * HEAD_DIM ** (-0.5)
    same_var = query_labels[:, None] == key_labels[None, :]
    scores = scores + jnp.where(
        same_var[None], bias_table[0][:, None, None], bias_table[1][:, None, None]
    )
    scores = jnp.where(key_labels[None, None, :] >= 0, scores, MASKED)
    return (scores, same_var)


def block_grads(
    query_rows,
    query_labels,
    grad_rows,
    lse_rows,
    delta_rows,
    key_rows,
    value_rows,
    key_labels,
    bias_table,
    need_query,
    need_keys,
):
    scores, same_var = score_block(query_rows, query_labels, key_rows, key_labels, bias_table)
    weights = jnp.exp(scores - lse_rows.T[:, :, None])
    grad_weights = jnp.einsum(
        "ihe,jhe->hij", grad_rows, value_rows, preferred_element_type=jnp.float32
    )
    grad_scores = (weights * (grad_weights - delta_rows.T[:, :, None])).astype(jnp.bfloat16)
    result = ()
    if need_query:
        grad_query = jnp.einsum(
            "hij,jhe->ihe", grad_scores, key_rows, preferred_element_type=jnp.float32
        ) * HEAD_DIM ** (-0.5)
        widened = grad_scores.astype(jnp.float32)
        bias_same = jnp.sum(jnp.where(same_var[None], widened, 0.0), axis=(1, 2))
        bias_other = jnp.sum(jnp.where(same_var[None], 0.0, widened), axis=(1, 2))
        result = result + (grad_query, jnp.stack([bias_same, bias_other]))
    if need_keys:
        grad_key = jnp.einsum(
            "hij,ihe->jhe", grad_scores, query_rows, preferred_element_type=jnp.float32
        ) * HEAD_DIM ** (-0.5)
        grad_value = jnp.einsum(
            "hij,ihe->jhe",
            weights.astype(jnp.bfloat16),
            grad_rows,
            preferred_element_type=jnp.float32,
        )
        result = result + (grad_key, grad_value)
    return result


def adam_step(weight, first_moment, second_moment, gradient, step_rate, decay_rate):
    first_moment = BETA_ONE * first_moment + (1.0 - BETA_ONE) * gradient
    second_moment = BETA_TWO * second_moment + (1.0 - BETA_TWO) * gradient * gradient
    direction = (
        first_moment
        / (1.0 - BETA_ONE**STEP)
        / (jnp.sqrt(second_moment / (1.0 - BETA_TWO**STEP)) + ADAM_EPS)
    )
    return (weight - step_rate * (direction + decay_rate * weight), first_moment, second_moment)


def general_body(
    inputs,
    teacher,
    lengths,
    variate_ids,
    time_ids,
    observed,
    attend_weight,
    output_weight,
    expand_weight,
    reduce_weight,
    norm_gains,
    variate_bias,
    attend_first,
    output_first,
    expand_first,
    reduce_first,
    gains_first,
    bias_first,
    attend_second,
    output_second,
    expand_second,
    reduce_second,
    gains_second,
    bias_second,
):
    row_count = inputs.shape[1]
    length = row_count * lax.axis_size("seq")
    block_rows = math.gcd(length, 1024)
    blocks = length // block_rows
    states = inputs[0].astype(jnp.float32)
    positions = lax.axis_index("seq") * row_count + jnp.arange(row_count, dtype=jnp.int32)
    inside = positions < lengths[0]
    scored = jnp.logical_and(inside, observed[0] == 1)
    local_count = jnp.sum(scored.astype(jnp.int32))
    count_early = lax.psum(local_count, ("seq", "batch"))
    full_attend, full_output, full_expand, full_reduce = (
        lax.all_gather(attend_weight.astype(jnp.bfloat16), ("seq", "batch"), axis=1, tiled=True),
        lax.all_gather(output_weight.astype(jnp.bfloat16), ("seq", "batch"), axis=0, tiled=True),
        lax.all_gather(expand_weight.astype(jnp.bfloat16), ("seq", "batch"), axis=1, tiled=True),
        lax.all_gather(reduce_weight.astype(jnp.bfloat16), ("seq", "batch"), axis=0, tiled=True),
    )
    unit_one, scale_one = normalize(states)
    act_one = (unit_one * norm_gains[0]).astype(jnp.bfloat16)
    project = jnp.einsum("td,cde->cte", act_one, full_attend, preferred_element_type=jnp.float32)
    cos_table, sin_table = angles(time_ids[0])
    query = rotate(project[0].reshape(row_count, HEADS, HEAD_DIM), cos_table, sin_table).astype(
        jnp.bfloat16
    )
    key_rows = (
        rotate(project[1].reshape(row_count, HEADS, HEAD_DIM), cos_table, sin_table)
        .astype(jnp.bfloat16)
        .reshape(row_count, D)
    )
    value_rows = project[2].astype(jnp.bfloat16)
    own_labels = jnp.where(inside, variate_ids[0], -1).astype(jnp.bfloat16)
    all_keys, all_values, all_labels = (
        lax.all_gather(key_rows, "seq", axis=0, tiled=True),
        lax.all_gather(value_rows, "seq", axis=0, tiled=True),
        lax.all_gather(own_labels, "seq", axis=0, tiled=True),
    )
    key_blocks = all_keys.reshape(blocks, block_rows, HEADS, HEAD_DIM)
    value_blocks = all_values.reshape(blocks, block_rows, HEADS, HEAD_DIM)
    label_blocks = all_labels.astype(jnp.float32).reshape(blocks, block_rows)
    query_labels = variate_ids[0].astype(jnp.float32)

    def sweep_top(carry, pieces):
        running, sum_exp = carry
        scores, same_var = score_block(query, query_labels, pieces[0], pieces[1], variate_bias)
        raised = jnp.maximum(running, jnp.floor(jnp.max(scores, axis=-1)))
        sum_exp = sum_exp * jnp.exp(running - raised) + jnp.sum(
            jnp.exp(scores - raised[..., None]), axis=-1
        )
        return ((raised, sum_exp), None)

    start_top = jnp.full((HEADS, row_count), MASKED, jnp.float32)
    (row_top, sum_exp), unused = lax.scan(
        sweep_top,
        (start_top, jnp.zeros((HEADS, row_count), jnp.float32)),
        (key_blocks, label_blocks),
    )
    log_total = row_top + jnp.log(sum_exp)

    def sweep_out(carry, pieces):
        coarse, finest = carry
        scores, same_var = score_block(query, query_labels, pieces[0], pieces[2], variate_bias)
        weights = jnp.exp(scores - log_total[..., None])
        rounded = weights.astype(jnp.bfloat16)
        residue = (weights - rounded.astype(jnp.float32)).astype(jnp.bfloat16)
        coarse = coarse + jnp.einsum(
            "hij,jhe->ihe", rounded, pieces[1], preferred_element_type=jnp.float32
        )
        finest = finest + jnp.einsum(
            "hij,jhe->ihe", residue, pieces[1], preferred_element_type=jnp.float32
        )
        return ((coarse, finest), None)

    zero_heads = jnp.zeros((row_count, HEADS, HEAD_DIM), jnp.float32)
    (coarse, finest), unused = lax.scan(
        sweep_out, (zero_heads, zero_heads), (key_blocks, value_blocks, label_blocks)
    )
    exact_heads = coarse + finest
    mixed = coarse.reshape(row_count, D).astype(jnp.bfloat16)
    middle = states + jnp.dot(mixed, full_output, preferred_element_type=jnp.float32)
    unit_two, scale_two = normalize(middle)
    act_two = (unit_two * norm_gains[1]).astype(jnp.bfloat16)
    gate_up = jnp.einsum("td,cdf->ctf", act_two, full_expand, preferred_element_type=jnp.float32)
    sigmoid = jax.nn.sigmoid(gate_up[0])
    hidden = (gate_up[0] * sigmoid * gate_up[1]).astype(jnp.bfloat16)
    output = middle + jnp.dot(hidden, full_reduce, preferred_element_type=jnp.float32)
    error = output - teacher[0].astype(jnp.float32)
    local_square = jnp.sum(jnp.where(scored[:, None], error * error, 0.0))
    square_total = lax.psum(local_square, ("seq", "batch"))
    count_all = count_early.astype(jnp.float32)
    loss = square_total / (count_all * D)
    grad_out = jnp.where(scored[:, None], error * (2.0 / (count_all * D)), 0.0)
    back_attend, back_output, back_expand, back_reduce = (
        lax.all_gather(attend_weight.astype(jnp.bfloat16), ("seq", "batch"), axis=1, tiled=True),
        lax.all_gather(output_weight.astype(jnp.bfloat16), ("seq", "batch"), axis=0, tiled=True),
        lax.all_gather(expand_weight.astype(jnp.bfloat16), ("seq", "batch"), axis=1, tiled=True),
        lax.all_gather(reduce_weight.astype(jnp.bfloat16), ("seq", "batch"), axis=0, tiled=True),
    )
    grad_branch = grad_out.astype(jnp.bfloat16)
    reduce_grad = jnp.einsum("tf,td->fd", hidden, grad_branch, preferred_element_type=jnp.float32)
    grad_hidden = jnp.einsum(
        "td,fd->tf", grad_branch, back_reduce, preferred_element_type=jnp.float32
    )
    grad_gate = grad_hidden * gate_up[1] * sigmoid * (1.0 + gate_up[0] * (1.0 - sigmoid))
    grad_up = grad_hidden * gate_up[0] * sigmoid
    grad_expand = jnp.stack([grad_gate, grad_up]).astype(jnp.bfloat16)
    expand_grad = jnp.einsum(
        "td,ctf->cdf", act_two, grad_expand, preferred_element_type=jnp.float32
    )
    grad_act_two = jnp.einsum(
        "ctf,cdf->td", grad_expand, back_expand, preferred_element_type=jnp.float32
    )
    expand_share, reduce_share = (
        lax.psum_scatter(expand_grad, ("seq", "batch"), scatter_dimension=1, tiled=True),
        lax.psum_scatter(reduce_grad, ("seq", "batch"), scatter_dimension=0, tiled=True),
    )
    grad_middle = grad_out + norm_back(grad_act_two, unit_two, scale_two, norm_gains[1])
    grad_attn = grad_middle.astype(jnp.bfloat16)
    output_grad = jnp.einsum("td,te->de", mixed, grad_attn, preferred_element_type=jnp.float32)
    grad_mixed = jnp.einsum(
        "te,de->td", grad_attn, back_output, preferred_element_type=jnp.float32
    ).astype(jnp.bfloat16)
    grad_heads = grad_mixed.reshape(row_count, HEADS, HEAD_DIM)
    row_delta = jnp.sum(grad_heads.astype(jnp.float32) * exact_heads, axis=-1)
    lse_rows = log_total.T
    zero_bias = jnp.zeros((2, HEADS), jnp.float32)

    def sweep_query(carry, pieces):
        part_query, part_bias = block_grads(
            query,
            query_labels,
            grad_heads,
            lse_rows,
            row_delta,
            pieces[0],
            pieces[1],
            pieces[2],
            variate_bias,
            True,
            False,
        )
        return ((carry[0] + part_query, carry[1] + part_bias), None)

    (query_total, bias_grad), unused = lax.scan(
        sweep_query, (zero_heads, zero_bias), (key_blocks, value_blocks, label_blocks)
    )
    all_query, all_grad = (
        lax.all_gather(query.reshape(row_count, D), "seq", axis=0, tiled=True),
        lax.all_gather(grad_mixed, "seq", axis=0, tiled=True),
    )
    all_lse, all_delta = (
        lax.all_gather(lse_rows, "seq", axis=0, tiled=True),
        lax.all_gather(row_delta, "seq", axis=0, tiled=True),
    )
    key_heads = key_rows.reshape(row_count, HEADS, HEAD_DIM)
    value_heads = value_rows.reshape(row_count, HEADS, HEAD_DIM)
    own_float = own_labels.astype(jnp.float32)

    def sweep_keys(carry, pieces):
        part_key, part_value = block_grads(
            pieces[0],
            pieces[1],
            pieces[2],
            pieces[3],
            pieces[4],
            key_heads,
            value_heads,
            own_float,
            variate_bias,
            False,
            True,
        )
        return ((carry[0] + part_key, carry[1] + part_value), None)

    (key_total, value_heads_total), unused = lax.scan(
        sweep_keys,
        (zero_heads, zero_heads),
        (
            all_query.reshape(blocks, block_rows, HEADS, HEAD_DIM),
            label_blocks,
            all_grad.reshape(blocks, block_rows, HEADS, HEAD_DIM),
            all_lse.reshape(blocks, block_rows, HEADS),
            all_delta.reshape(blocks, block_rows, HEADS),
        ),
    )
    value_total = value_heads_total.reshape(row_count, D)
    grad_query = unrotate(query_total, cos_table, sin_table).reshape(row_count, D)
    grad_key = unrotate(key_total, cos_table, sin_table).reshape(row_count, D)
    grad_project = jnp.stack([grad_query, grad_key, value_total]).astype(jnp.bfloat16)
    attend_grad = jnp.einsum(
        "td,cte->cde", act_one, grad_project, preferred_element_type=jnp.float32
    )
    grad_act_one = jnp.einsum(
        "cte,cde->td", grad_project, back_attend, preferred_element_type=jnp.float32
    )
    attend_share, output_share = (
        lax.psum_scatter(attend_grad, ("seq", "batch"), scatter_dimension=1, tiled=True),
        lax.psum_scatter(output_grad, ("seq", "batch"), scatter_dimension=0, tiled=True),
    )
    grad_input = grad_middle + norm_back(grad_act_one, unit_one, scale_one, norm_gains[0])
    gains_grad = jnp.stack(
        [jnp.sum(grad_act_one * unit_one, axis=0), jnp.sum(grad_act_two * unit_two, axis=0)]
    )
    local_squares = (
        jnp.sum(attend_share * attend_share)
        + jnp.sum(output_share * output_share)
        + jnp.sum(expand_share * expand_share)
        + jnp.sum(reduce_share * reduce_share)
    )
    gains_total, bias_total, square_sum = lax.psum(
        (gains_grad, bias_grad, local_squares), ("seq", "batch")
    )
    grad_norm = jnp.sqrt(
        square_sum + jnp.sum(gains_total * gains_total) + jnp.sum(bias_total * bias_total)
    )
    clip_scale = jnp.minimum(1.0, CLIP_NORM / grad_norm)
    attend_new, attend_first_new, attend_second_new = adam_step(
        attend_weight,
        attend_first,
        attend_second,
        attend_share * clip_scale,
        RATE_ATTEND,
        WEIGHT_DECAY,
    )
    output_new, output_first_new, output_second_new = adam_step(
        output_weight,
        output_first,
        output_second,
        output_share * clip_scale,
        RATE_OUTPUT,
        WEIGHT_DECAY,
    )
    expand_new, expand_first_new, expand_second_new = adam_step(
        expand_weight,
        expand_first,
        expand_second,
        expand_share * clip_scale,
        RATE_EXPAND,
        WEIGHT_DECAY,
    )
    reduce_new, reduce_first_new, reduce_second_new = adam_step(
        reduce_weight,
        reduce_first,
        reduce_second,
        reduce_share * clip_scale,
        RATE_REDUCE,
        WEIGHT_DECAY,
    )
    gains_new, gains_first_new, gains_second_new = adam_step(
        norm_gains, gains_first, gains_second, gains_total * clip_scale, RATE_GAINS, 0.0
    )
    bias_new, bias_first_new, bias_second_new = adam_step(
        variate_bias, bias_first, bias_second, bias_total * clip_scale, RATE_BIAS, 0.0
    )
    input_gradient = (grad_input * count_all * D)[None]
    return (
        output[None],
        loss,
        input_gradient,
        grad_norm,
        attend_new,
        attend_new.astype(jnp.bfloat16),
        attend_first_new,
        attend_second_new,
        output_new,
        output_new.astype(jnp.bfloat16),
        output_first_new,
        output_second_new,
        expand_new,
        expand_new.astype(jnp.bfloat16),
        expand_first_new,
        expand_second_new,
        reduce_new,
        reduce_new.astype(jnp.bfloat16),
        reduce_first_new,
        reduce_second_new,
        gains_new,
        gains_first_new,
        gains_second_new,
        bias_new,
        bias_first_new,
        bias_second_new,
    )


MESH = pl.DeviceIdType.MESH
IN_VMEM = pl.BlockSpec(memory_space=pltpu.VMEM)
IN_SMEM = pl.BlockSpec(memory_space=pltpu.SMEM)
LANES = 128
HEADS_HERE = LANES // HEAD_DIM
VARIATES = 16
MIB = 1 << 20
LOW = jnp.bfloat16
WIDE = jnp.float32
TOTAL_ROWS = 24


def fast_fits(seq, batch):
    return seq == 8 and batch == 4 and seq * LANES == D


def flip(index, mask):
    result, bit = index, 1
    while bit <= mask:
        if mask & bit:
            result = result + bit - 2 * bit * lax.rem(lax.div(index, bit), 2)
        bit *= 2
    return result


def push(source, target, send_sem, recv_sem, device):
    return pltpu.make_async_remote_copy(
        src_ref=source,
        dst_ref=target,
        send_sem=send_sem,
        recv_sem=recv_sem,
        device_id=device,
        device_id_type=MESH,
    )


def block_of(index, size):
    return pl.ds(pl.multiple_of(index * size, size), size)


def dot(left, right):
    return jnp.dot(left, right, preferred_element_type=WIDE)


def dot_turned(left, right):
    return lax.dot_general(left, right, (((1,), (1,)), ((), ())), preferred_element_type=WIDE)


def turned_dot(left, right):
    return lax.dot_general(left, right, (((0,), (0,)), ((), ())), preferred_element_type=WIDE)


class Team:
    def __init__(self, index, place):
        self.index, self.place = index, place

    def at(self, mask):
        return flip(self.index, mask)


def head_team(me, group):
    return Team(me, lambda mask: (flip(me, mask), group))


def feed_team(me, group):
    return Team(
        4 * lax.rem(group, 2) + lax.rem(me, 4),
        lambda mask: (flip(me, mask % 4), flip(group, mask // 4)),
    )


class Gather:
    def __init__(self, team, rows, all_rows, sends, recvs):
        self.team, self.all_rows, self.sends, self.recvs = team, all_rows, sends, recvs
        self.size = all_rows.shape[0] // 8
        self.given = rows
        self.rows = all_rows.at[block_of(team.index, self.size)] if rows is None else rows

    def copy(self, mask, passing):
        source = self.all_rows.at[block_of(self.team.at(mask - 1 if passing else 0), self.size)]
        return push(
            source if passing else self.rows,
            source,
            self.sends.at[mask],
            self.recvs.at[mask],
            self.team.place(1 if passing else mask),
        )

    def start(self, masks=(6, 2, 4, 1)):
        for mask in masks:
            self.copy(mask, False).start()
        if self.given is not None:
            self.all_rows[block_of(self.team.index, self.size)] = self.given[...]

    def pass_on(self, chip):
        self.copy(2 * chip, False).wait_recv()
        self.copy(2 * chip + 1, True).start()

    def complete(self, chip):
        self.copy(2 * chip + 1, chip > 0).wait_recv()

    def finish(self):
        for mask in (6, 2, 4, 1):
            self.copy(mask, False).wait_send()
        for mask in (3, 5, 7):
            self.copy(mask, True).wait_send()


def at_step(step, number, *works):
    @pl.when(step == number)
    def _():
        for work in works:
            work()


def each_chip(gather, work, after):
    def one_chip(chip, unused):
        @pl.when(chip == 0)
        def _():
            gather.complete(0)

        @pl.when(chip == 1)
        def _():
            gather.pass_on(1)
            gather.pass_on(2)
            gather.copy(6, False).start()
            gather.complete(1)

        @pl.when(chip == 2)
        def _():
            gather.complete(2)

        @pl.when(chip == 3)
        def _():
            gather.pass_on(3)
            gather.complete(3)

        work(chip)
        for number, works in after.items():
            at_step(chip, number, *works)
        return unused

    lax.fori_loop(0, 4, one_chip, 0)
    gather.finish()


class Scatter:
    def __init__(self, team, buffers, near_sends, near_recvs, far_sends, far_recvs):
        self.whole, self.keep, self.near_from, self.near, self.far_from, self.far = buffers
        self.sems = near_sends, near_recvs, far_sends, far_recvs
        self.team = team
        self.size = self.keep.shape[1]

    def near_copy(self, chip):
        return push(
            self.near_from.at[chip],
            self.near.at[chip],
            self.sems[0].at[chip],
            self.sems[1].at[chip],
            self.team.place(1),
        )

    def far_copy(self, chip):
        return push(
            self.far_from.at[chip],
            self.far.at[chip],
            self.sems[2].at[chip],
            self.sems[3].at[chip],
            self.team.place(2 * chip),
        )

    def put(self, chip, rows):
        core = lax.rem(self.team.index, 2)
        self.whole[...] = rows
        self.near_from[chip] = self.whole[block_of(1 - core, self.size)].astype(LOW)
        self.near_copy(chip).start()
        self.keep[chip] = self.whole[block_of(core, self.size)]

    def combine(self, chip):
        self.near_copy(chip).wait_recv()
        self.far_from[chip] = (self.keep[chip] + self.near[chip].astype(WIDE)).astype(LOW)
        self.far_copy(chip).start()

    def total(self):
        self.near_copy(0).wait_recv()
        total = self.keep[0] + self.near[0].astype(WIDE)
        for chip in (1, 2, 3):
            self.far_copy(chip).wait_recv()
            total = total + self.far[chip].astype(WIDE)
        for chip in (0, 1, 2, 3):
            self.near_copy(chip).wait_send()
            if chip:
                self.far_copy(chip).wait_send()
        return total


class Quad:
    def __init__(self, part, along_near, along_far):
        self.part, self.along_near, self.along_far = part, along_near, along_far


def feed_quad(me, group):
    return Quad(2 * lax.div(me, 4) + lax.div(group, 2), (flip(me, 4), group), (me, flip(group, 2)))


def head_quad(me, group):
    return Quad(
        2 * lax.rem(group, 2) + lax.div(group, 2), (me, flip(group, 1)), (me, flip(group, 2))
    )


def line_place(part):
    return 2 * lax.rem(part, 2) + lax.div(part, 2)


class QuadGather:
    def __init__(self, quad, part_of, sends, recvs):
        self.part_of, self.sends, self.recvs = part_of, sends, recvs
        self.part, self.along_near, self.along_far = quad.part, quad.along_near, quad.along_far

    def copy(self, way):
        part = self.part_of(flip(self.part, 1) if way == 3 else self.part)
        device = self.along_far if way == 1 else self.along_near
        return push(part, part, self.sends.at[way], self.recvs.at[way], device)

    def start_near(self):
        self.copy(2).start()

    def start_far(self):
        self.copy(1).start()

    def start(self):
        self.start_far()
        self.start_near()

    def pass_on(self):
        self.copy(1).wait_recv()
        self.copy(3).start()

    def land(self):
        self.copy(2).wait_recv()
        self.copy(3).wait_recv()

    def finish(self):
        for way in (1, 2, 3):
            self.copy(way).wait_send()


class QuadScatter:
    def __init__(self, quad, part_of, landing, sends, recvs):
        self.part_of, self.landing, self.sends, self.recvs = part_of, landing, sends, recvs
        self.part, self.along_near, self.along_far = quad.part, quad.along_near, quad.along_far

    def copy(self, slot):
        return push(
            self.part_of(flip(self.part, (2, 3, 1)[slot])),
            self.landing.at[slot],
            self.sends.at[slot],
            self.recvs.at[slot],
            self.along_far if slot == 2 else self.along_near,
        )

    def start_far(self):
        self.copy(1).start()

    def start_near(self):
        self.copy(0).start()

    def start(self):
        self.start_far()
        self.start_near()

    def total(self):
        total = self.part_of(self.part)[...].astype(WIDE)
        return total + self.landing[0].astype(WIDE) + self.landing[2].astype(WIDE)

    def pass_on(self):
        self.copy(1).wait_recv()
        part = self.part_of(flip(self.part, 1))
        part[...] = (part[...].astype(WIDE) + self.landing[1].astype(WIDE)).astype(LOW)
        self.copy(2).start()

    def land(self):
        self.copy(0).wait_recv()
        self.copy(2).wait_recv()

    def finish(self):
        for slot in (0, 1, 2):
            self.copy(slot).wait_send()


def chip_of(team, chip):
    here = lax.div(team.index, 2)
    if isinstance(chip, int):
        return flip(here, chip)
    column = lax.rem(lax.rem(here, 2) + lax.rem(chip, 2), 2)
    row = lax.rem(lax.div(here, 2) + lax.div(chip, 2), 2)
    return 2 * row + column


def turn_rows(values, cosine, sine):
    half = HEAD_DIM // 2
    pieces = []
    for start in range(0, values.shape[0], HEAD_DIM):
        first, second = values[start : start + half], values[start + half : start + HEAD_DIM]
        pieces += [first * cosine - second * sine, second * cosine + first * sine]
    return jnp.concatenate(pieces, axis=0)


def thirds(values):
    first = values.astype(LOW).astype(WIDE)
    second = (values - first).astype(LOW).astype(WIDE)
    return first, second, values - first - second


def pick(row, choices):
    result = jnp.zeros(row.shape, WIDE)
    for number, choice in choices.items():
        result = jnp.where(row == number, choice, result)
    return result


def norm_rows(values):
    scale = lax.rsqrt(jnp.mean(values * values, axis=-1, keepdims=True) + NORM_EPS)
    return values * scale, scale


def feed_block(block):
    y, x, core, far_z, near_z = (block // 16, block // 8 % 2, block // 4 % 2, block // 2 % 2, block % 2)
    return 4 * near_z + 2 * x + core, 2 * y + far_z


def layer_kernel(seq, batch, ins, outs, mem):
    me, group = lax.axis_index("seq"), lax.axis_index("batch")
    rows = ins.inputs.shape[0]
    length = rows * seq
    pair = 2 * rows
    share = ins.attend.shape[1]
    wide_columns = ins.expand.shape[2] // D
    hidden_width = mem.reduce_all.shape[0] * mem.reduce_all.shape[1]
    blocks = ins.expand.shape[2] // LANES
    heads, feeds = head_team(me, group), feed_team(me, group)
    head_four, feed_four = head_quad(me, group), feed_quad(me, group)
    quad = feed_four.part

    staged = [(ins.attend.at[which], mem.keep.at[0, block_of(which, share)]) for which in range(3)]
    staged.append((ins.output, mem.keep.at[0, block_of(3, share)]))
    staged.append((ins.reduce, mem.keep.at[1]))
    for which in range(2):
        for block in range(wide_columns):
            columns = slice(block * D, (block + 1) * D)
            staged.append(
                (ins.expand.at[which, :, columns], mem.keep.at[2 + which, block_of(block, share)])
            )
    staged = [
        pltpu.make_async_copy(source, target, mem.stage_sem.at[number])
        for number, (source, target) in enumerate(staged)
    ]
    for copy in staged:
        copy.start()
    barrier = pltpu.get_barrier_semaphore()
    for mask in range(1, seq):
        pl.semaphore_signal(barrier, inc=1, device_id=(flip(me, mask), group), device_id_type=MESH)
    for step in range(1, batch):
        pl.semaphore_signal(
            barrier, inc=1, device_id=(me, lax.rem(group + step, batch)), device_id_type=MESH
        )
    for mask in (5, 6, 7):
        pl.semaphore_signal(barrier, inc=1, device_id=feeds.place(mask), device_id_type=MESH)

    position = me * rows + lax.broadcasted_iota(jnp.int32, (1, rows), 1)
    inside = position < ins.lengths[0]
    scored = jnp.logical_and(inside, ins.observed[...] == 1).astype(WIDE)
    variate = ins.variates[...].astype(WIDE)
    turns = ins.turns.shape[0]
    mem.facts_own[:turns] = ins.turns[...]
    mem.facts_own[turns:] = jnp.concatenate(
        [jnp.where(inside, variate, -1.0), variate, scored, jnp.zeros((5, rows), WIDE)], axis=0
    )
    mem.scored[...] = jnp.broadcast_to(scored, (rows, rows)).T
    for copy in staged:
        copy.wait()
    for which in range(3):
        mem.attend_low[which] = mem.keep[0, block_of(which, share)].astype(LOW)
    pl.semaphore_wait(barrier, seq + batch + 1)

    masks = (6, 7, 4, 5, 2, 3, 1)

    def start_attend_columns():
        copies = []
        for mask in masks:
            copy = push(
                mem.attend_low.at[:, :, block_of(heads.at(mask), LANES)],
                mem.attend_all.at[:, me, group],
                mem.column_send.at[0, mask],
                mem.column_recv.at[0, mask],
                heads.place(mask),
            )
            copy.start()
            copies.append(copy)
        mem.attend_all[:, me, group] = mem.attend_low[:, :, block_of(me, LANES)]
        return copies

    def start_expand_columns():
        copies = []
        for mask in masks:
            copy = push(
                mem.expand_low.at[:, feeds.at(mask)],
                mem.expand_all.at[:, me, group],
                mem.column_send.at[1, mask],
                mem.column_recv.at[1, mask],
                feeds.place(mask),
            )
            copy.start()
            copies.append(copy)
        mem.expand_all[:, me, group] = mem.expand_low[:, feeds.index]
        return copies

    def expand_part_of(array, which):
        def part_of(part):
            return array.at[which, pl.ds(4 * lax.div(part, 2), 4), pl.ds(2 * lax.rem(part, 2), 2)]

        return part_of

    def quad_gather(four, row, part_of):
        return QuadGather(four, part_of, mem.line_send.at[row], mem.line_recv.at[row])

    def gather(team, phase, all_rows):
        return Gather(
            team,
            mem.own_rows.at[phase],
            all_rows,
            mem.gather_send.at[phase],
            mem.gather_recv.at[phase],
        )

    def scatter(team, phase):
        return Scatter(
            team,
            (mem.whole, mem.keep, mem.near_from, mem.near, mem.far_from, mem.far),
            mem.near_send.at[phase],
            mem.near_recv.at[phase],
            mem.far_send.at[phase],
            mem.far_recv.at[phase],
        )

    attend_columns = start_attend_columns()
    mem.output_full[block_of(batch * me + group, share)] = mem.keep[0, block_of(3, share)].astype(LOW)
    mem.reduce_all[quad] = mem.keep[1].astype(LOW)
    for which in range(2):
        for block in range(blocks):
            owner, part = feed_block(block)
            row, lane = divmod(block * LANES, D)
            mem.expand_low[which, owner, :, part * LANES : (part + 1) * LANES] = mem.keep[
                2 + which, block_of(row, share), lane : lane + LANES
            ].astype(LOW)
    line_output = quad_gather(
        head_four, 1, lambda part: mem.output_full.at[block_of(batch * me + line_place(part), share)]
    )
    line_output.start()
    unit_one, scale_one = norm_rows(ins.inputs[...].astype(WIDE))
    mem.own_rows[0] = (unit_one * ins.gains[0:1, :]).astype(LOW)
    facts = Gather(heads, mem.facts_own, mem.facts_all, mem.facts_send, mem.facts_recv)
    facts.start()
    for copy in attend_columns:
        copy.wait_recv()
    line_attend = quad_gather(head_four, 0, lambda part: mem.attend_all.at[:, :, line_place(part)])
    line_attend.start()
    acts = gather(heads, 0, mem.act_one)
    acts.start()
    for chip in (1, 2, 3):
        facts.pass_on(chip)
    for chip in (0, 1, 2, 3):
        facts.complete(chip)
    facts.finish()
    step_rows = mem.facts_own.shape[0]
    half = HEAD_DIM // 2
    count = jnp.zeros((8, LANES), WIDE)
    for slot in range(seq):
        columns = slice(slot * rows, (slot + 1) * rows)
        start = slot * step_rows
        mem.cosine[:, columns] = mem.facts_all[start : start + half]
        mem.sine[:, columns] = mem.facts_all[start + half : start + 2 * half]
        labels = mem.facts_all[start + 2 * half : start + 2 * half + 8]
        mem.labels[:, columns] = labels
        count = count + labels
    mem.count[group] = count
    count_copies = []
    for step in range(1, batch):
        copy = push(
            mem.count.at[group],
            mem.count.at[group],
            mem.count_send.at[step],
            mem.count_recv.at[step],
            (me, lax.rem(group + step, batch)),
        )
        copy.start()
        count_copies.append(copy)

    def mark(block, unused):
        span = block_of(block, pair)
        row = lax.broadcasted_iota(jnp.int32, (HEAD_DIM, pair), 0)
        third = lax.div(row, VARIATES)
        variate = lax.rem(row, VARIATES).astype(WIDE)
        key_label, query_label = mem.labels[0:1, span], mem.labels[1:2, span]
        ones = jnp.ones((1, pair), WIDE)
        last = 3 * VARIATES
        hidden_keys = (key_label < 0.0).astype(WIDE)
        mem.key_marks[:, span] = jnp.where(
            third < 3,
            (key_label == variate).astype(WIDE),
            pick(row, {last: ones, last + 1: ones, last + 2: ones, last + 3: hidden_keys}),
        ).astype(LOW)
        query_marks = (query_label == variate).astype(WIDE)
        mem.sum_marks[:, span] = jnp.where(
            row < VARIATES, query_marks, pick(row, {VARIATES: ones})
        ).astype(LOW)
        for head in range(HEADS_HERE):
            number = me * HEADS_HERE + head
            other = jnp.full((HEAD_DIM, pair), ins.bias[1, number], WIDE)
            more = thirds(jnp.full((HEAD_DIM, pair), ins.bias[0, number], WIDE) - other)
            other = thirds(other)
            mem.query_turned[head, HEAD_DIM:, span] = jnp.where(
                third < 3,
                query_marks * jnp.where(third == 0, more[0], jnp.where(third == 1, more[1], more[2])),
                pick(row, {last: other[0], last + 1: other[1], last + 2: other[2], last + 3: MASKED}),
            ).astype(LOW)
        return unused

    lax.fori_loop(0, length // pair, mark, 0)
    acts.pass_on(1)
    acts.pass_on(2)
    line_output.pass_on()
    line_output.land()
    acts.pass_on(3)
    line_attend.pass_on()
    for chip in range(4):
        acts.complete(chip)
    acts.finish()

    expand_columns = start_expand_columns()
    line_reduce = quad_gather(feed_four, 4, lambda part: mem.reduce_all.at[part])
    line_reduce.start_far()
    line_expand = [
        quad_gather(feed_four, 2 + which, expand_part_of(mem.expand_all, which)) for which in range(2)
    ]
    line_attend.land()
    outputs = Gather(heads, None, mem.output_full, mem.output_send, mem.output_recv)
    outputs.start()
    line_reduce.start_near()

    def attend_matrix(which):
        return mem.attend_all[which].reshape(D, LANES)

    def project(block, unused):
        span = block_of(block, pair)
        weights = jnp.concatenate([attend_matrix(which) for which in range(3)], axis=1)
        products = dot(mem.act_one[span, :], weights)
        cosine, sine = mem.cosine[:, span], mem.sine[:, span]
        query = turn_rows(products[:, :LANES].T, cosine, sine).astype(LOW)
        query = (query.astype(WIDE) * HEAD_DIM ** (-0.5)).astype(LOW)
        key = turn_rows(products[:, LANES : 2 * LANES].T, cosine, sine).astype(LOW)
        value = products[:, 2 * LANES :].T.astype(LOW)
        mem.key_turned[:, span] = key
        mem.value_turned[:, span] = value

        for head in range(HEADS_HERE):
            features = slice(head * HEAD_DIM, (head + 1) * HEAD_DIM)
            mem.query_turned[head, :HEAD_DIM, span] = query[features]
            whole = jnp.concatenate([key[features], mem.key_marks[:, span]], axis=0)
            mem.key_heads[head, span, :] = whole.T
        return unused

    for copy in expand_columns:
        copy.wait_recv()
    line_expand[0].start_far()
    line_expand[0].start_near()
    lax.fori_loop(0, length // pair, project, 0)
    line_expand[1].start_far()

    core = lax.rem(me, 2)

    def mixed_copy(chip, which):
        other = 2 * chip_of(heads, chip) + which
        slot = 2 * chip + lax.rem(which + core, 2)
        return push(
            mem.mixed_out.at[block_of(other, rows)],
            mem.mixed_rows.at[:, block_of(me, LANES)],
            mem.mixed_send.at[slot],
            mem.mixed_recv.at[slot],
            (other, group),
        )

    def attend_block(chip):
        columns = block_of(chip_of(heads, chip), pair)
        for head in range(HEADS_HERE):
            span = slice(head * HEAD_DIM, (head + 1) * HEAD_DIM)
            scores = dot(mem.key_heads[head], mem.query_turned[head, :, columns])
            top = jnp.floor(jnp.max(scores, axis=0, keepdims=True))
            powers = jnp.exp(scores - top)
            probs = powers * (1.0 / jnp.sum(powers, axis=0, keepdims=True))
            rounded = probs.astype(LOW)
            mem.probs[head, :, columns] = rounded
            residue = (probs - rounded.astype(WIDE)).astype(LOW)
            coarse = dot(mem.value_turned[span, :], rounded)
            mem.exact[span, columns] = coarse + dot(mem.value_turned[span, :], residue)
            mem.mixed_wide[span, :] = coarse
        mixed = mem.mixed_wide[...].astype(LOW)
        mem.mixed_turned[:, columns] = mixed
        mem.mixed_out[columns, :] = mixed.T

    def attend_step(step, unused):
        chip = lax.rem(step + 1, 4)
        attend_block(chip)
        for which in range(2):

            @pl.when(jnp.logical_or(chip > 0, core != which))
            def _():
                mixed_copy(chip, which).start()

        at_step(step, 1, lambda: outputs.pass_on(1), lambda: outputs.pass_on(2))
        at_step(step, 3, lambda: outputs.pass_on(3))
        return unused

    lax.fori_loop(0, 4, attend_step, 0)
    line_expand[1].start_near()
    mem.mixed_rows[:, block_of(me, LANES)] = mem.mixed_out[block_of(me, rows), :]
    for chip in range(4):
        outputs.complete(chip)
    outputs.finish()

    def wait_pieces(copy):
        for mask in range(1, seq):
            copy(mask).wait()

    def mixed_wait(mask):
        other = heads.at(mask)
        return push(
            mem.mixed_out.at[block_of(other, rows)],
            mem.mixed_rows.at[:, block_of(other, LANES)],
            mem.mixed_send.at[mask],
            mem.mixed_recv.at[mask],
            (other, group),
        )

    wait_pieces(mixed_wait)
    middle = ins.inputs[...].astype(WIDE) + dot(mem.mixed_rows[...], mem.output_full[...])
    mem.middle[...] = middle
    unit_two, scale_two = norm_rows(middle)
    mem.own_rows[1] = (unit_two * ins.gains[1:2, :]).astype(LOW)
    acts = gather(feeds, 1, mem.act_two)
    acts.start((2, 4, 1))
    line_reduce.pass_on()
    line_expand[0].pass_on()

    def split_heads(block, unused):
        span = block_of(block, pair)
        row = lax.broadcasted_iota(jnp.int32, (HEAD_DIM, pair), 0)
        value_marks = jnp.where(row < 3, 1.0, 0.0).astype(LOW)
        for head in range(HEADS_HERE):
            features = slice(head * HEAD_DIM, (head + 1) * HEAD_DIM)
            value = mem.value_turned[features, span]
            mem.value_heads[head, span, :] = jnp.concatenate([value, value_marks], axis=0).T
            query = mem.query_turned[head, :HEAD_DIM, span]
            whole = jnp.concatenate([query, mem.sum_marks[:, span]], axis=0)
            mem.query_heads[head, span, :] = whole.T
        return unused

    lax.fori_loop(0, length // pair, split_heads, 0)
    line_expand[0].land()

    def expand_matrix(which):
        return mem.expand_all[which].reshape(D, hidden_width)

    def reduce_matrix():
        return mem.reduce_all[...].reshape(hidden_width, D)

    def feed_gate(chip):
        span = block_of(chip_of(feeds, chip), pair)
        mem.by_gate[span, :] = dot(mem.act_two[span, :], expand_matrix(0))

    def feed_up(chip, unused=0):
        span = block_of(chip_of(feeds, chip), pair)
        gate = mem.by_gate[span, :]
        up = dot(mem.act_two[span, :], expand_matrix(1))
        sigmoid = 1.0 / (1.0 + jnp.exp(-gate))
        swish = gate * sigmoid
        mem.by_up[span, :] = swish
        mem.by_gate[span, :] = up * sigmoid * (1.0 + gate * (1.0 - sigmoid))
        mem.hidden[span, :] = (swish * up).astype(LOW)
        return unused

    each_chip(
        acts,
        feed_gate,
        {
            0: [line_expand[1].pass_on],
            2: [line_expand[1].land, lambda: lax.fori_loop(0, 3, feed_up, 0)],
            3: [lambda: lax.fori_loop(3, 4, feed_up, 0)],
        },
    )
    line_reduce.land()
    sums = scatter(feeds, 1)

    def feed_down(step, unused):
        chip = lax.rem(step + 1, 4)
        span = block_of(chip_of(feeds, chip), pair)
        sums.put(chip, dot(mem.hidden[span, :], reduce_matrix()))
        at_step(step, 1, lambda: sums.combine(1))
        at_step(step, 2, lambda: sums.combine(2))
        return unused

    lax.fori_loop(0, 4, feed_down, 0)
    sums.combine(3)

    for block in range(length // pair):
        span = block_of(block, pair)
        mem.hidden_turned[:, span] = mem.hidden[span, :].T
        mem.act_two_turned[:, span] = mem.act_two[span, :].T
    output = mem.middle[...] + sums.total()
    outs.layer_output[...] = output
    for copy in count_copies:
        copy.wait()
    count_all = jnp.sum(
        mem.count[0, 2:3] + mem.count[1, 2:3] + mem.count[2, 2:3] + mem.count[3, 2:3],
        axis=1,
        keepdims=True,
    )
    error = jnp.where(mem.scored[:, 0:1] > 0.0, output - ins.teacher[...].astype(WIDE), 0.0)
    mem.squares[1:2, :] = jnp.sum(error * error, axis=0, keepdims=True)
    grad_out = error * (2.0 / (count_all * D))
    mem.grad_own[...] = grad_out
    mem.own_rows[2] = grad_out.astype(LOW)
    acts = gather(feeds, 2, mem.branch)
    acts.start((2, 4, 1))

    def turn_acts(block, unused):
        span = block_of(block, pair)
        mem.act_one_turned[:, span] = mem.act_one[span, :].T
        return unused

    lax.fori_loop(0, length // pair, turn_acts, 0)

    sums = scatter(feeds, 2)

    def feed_back(chip):
        span = block_of(chip_of(feeds, chip), pair)
        grad_hidden = dot_turned(mem.branch[span, :], reduce_matrix())
        grad_gate = (grad_hidden * mem.by_gate[span, :]).astype(LOW)
        grad_up = (grad_hidden * mem.by_up[span, :]).astype(LOW)
        mem.grad_gate[span, :] = grad_gate
        mem.grad_up[span, :] = grad_up
        sums.put(
            chip,
            dot_turned(
                jnp.concatenate([grad_gate, grad_up], axis=1),
                jnp.concatenate([expand_matrix(0), expand_matrix(1)], axis=1),
            ),
        )

    each_chip(acts, feed_back, {2: [lambda: sums.combine(1)], 3: [lambda: sums.combine(2)]})

    def quad_scatter(four, row, part_of, landing):
        return QuadScatter(four, part_of, landing, mem.back_send.at[row], mem.back_recv.at[row])

    def reduce_grad(part, unused):
        mem.reduce_grad[part] = dot(
            mem.hidden_turned[block_of(part, rows), :], mem.branch[...]
        ).astype(LOW)
        at_step(part, 0, lambda: sums.combine(3))
        return unused

    lax.fori_loop(0, batch, reduce_grad, 0)
    back_reduce = quad_scatter(
        feed_four, 0, lambda part: mem.reduce_grad.at[part], mem.reduce_land
    )
    back_reduce.start_far()

    def expand_grad(which):
        grads = (mem.grad_gate, mem.grad_up)[which]

        def one_block(block, unused):
            products = dot(mem.act_two_turned[block_of(block, pair), :], grads[...]).astype(LOW)
            mem.expand_grad[which, pl.ds(2 * block, 2)] = products.reshape(
                2, batch, share, hidden_width
            )
            return unused

        lax.fori_loop(0, seq // 2, one_block, 0)
        line = quad_scatter(
            feed_four, 1 + which, expand_part_of(mem.expand_grad, which), mem.expand_land.at[which]
        )
        return line

    back_expand = []
    back_expand.append(expand_grad(0))
    back_expand[0].start_far()
    grad_act = sums.total()
    unit_two, scale_two = norm_rows(mem.middle[...])
    gain = ins.gains[1:2, :]
    grad_unit = grad_act * gain
    mem.gains[1:2, :] = jnp.sum(grad_act * unit_two, axis=0, keepdims=True)
    grad_middle = mem.grad_own[...] + scale_two * (
        grad_unit - unit_two * jnp.mean(grad_unit * unit_two, axis=-1, keepdims=True)
    )
    mem.grad_own[...] = grad_middle
    mem.own_rows[3] = grad_middle.astype(LOW)
    grad_mixed = dot(mem.output_full[...], grad_middle.T.astype(LOW)).astype(LOW)
    mem.grad_mixed_out[...] = grad_mixed.reshape(seq, LANES, rows)

    def grad_copy(mask, back=False):
        return push(
            mem.grad_mixed_out.at[heads.at(mask)],
            mem.grad_mixed.at[:, block_of(heads.at(mask) if back else me, rows)],
            mem.mixed_send.at[8 + mask],
            mem.mixed_recv.at[8 + mask],
            heads.place(mask),
        )

    for mask in masks:
        grad_copy(mask).start()
    mem.grad_mixed[:, block_of(me, rows)] = mem.grad_mixed_out[me]
    back_reduce.pass_on()
    back_expand.append(expand_grad(1))
    back_expand[1].start_far()

    wait_pieces(lambda mask: grad_copy(mask, True))
    acts = gather(heads, 3, mem.grad_attn)
    acts.start()
    back_reduce.start_near()
    back_expand[0].start_near()
    back_attend = [
        quad_scatter(
            head_four,
            4 + which,
            lambda part, which=which: mem.attend_grad.at[which, :, line_place(part)],
            mem.attend_land.at[which],
        )
        for which in range(3)
    ]

    def attend_grad(which):
        def one_block(block, unused):
            products = dot(mem.act_one_turned[block_of(block, pair), :], mem.grad_project[which])
            mem.attend_grad[which, pl.ds(2 * block, 2)] = products.astype(LOW).reshape(
                2, batch, share, LANES
            )
            return unused

        lax.fori_loop(0, length // pair, one_block, 0)
        back_attend[which].start()

    lane = lax.broadcasted_iota(jnp.int32, (pair, LANES), 1)

    def grad_rows(block, unused):
        span = block_of(block, pair)
        whole = mem.grad_mixed[:, span].astype(WIDE).T
        for head in range(HEADS_HERE):
            mem.grad_heads[head, span, :] = jnp.where(lax.div(lane, HEAD_DIM) == head, whole, 0.0).astype(LOW)
        return unused

    lax.fori_loop(0, length // pair, grad_rows, 0)

    def value_back(block, unused):
        span = block_of(block, pair)
        total = dot(mem.probs[0, span, :], mem.grad_heads[0])
        for head in range(1, HEADS_HERE):
            total = total + dot(mem.probs[head, span, :], mem.grad_heads[head])
        mem.grad_project[2, span, :] = total.astype(LOW)
        return unused

    lax.fori_loop(0, length // pair, value_back, 0)
    back_expand[0].pass_on()
    attend_grad(2)

    def score_back(block, unused):
        columns = block_of(block, pair)
        row = lax.broadcasted_iota(jnp.int32, (HEAD_DIM, pair), 0)
        grads = mem.grad_mixed[:, columns]
        delta = grads.astype(WIDE) * mem.exact[:, columns]
        for head in range(HEADS_HERE):
            span = slice(head * HEAD_DIM, (head + 1) * HEAD_DIM)
            pieces = thirds(-jnp.sum(delta[span], axis=0, keepdims=True))
            marks = pick(row, dict(enumerate(pieces))).astype(LOW)
            change = dot(mem.value_heads[head], jnp.concatenate([grads[span], marks], axis=0))
            mem.probs[head, :, columns] = (mem.probs[head, :, columns].astype(WIDE) * change).astype(LOW)
        return unused

    lax.fori_loop(0, length // pair, score_back, 0)
    back_expand[1].start_near()
    mem.bias_sums[...] = jnp.zeros_like(mem.bias_sums)
    scale = HEAD_DIM ** (-0.5)

    def project_grads(block, unused):
        span = block_of(block, pair)
        cosine, sine = mem.cosine[:, span], -mem.sine[:, span]
        queries, keys = [], []
        for head in range(HEADS_HERE):
            features = slice(head * HEAD_DIM, (head + 1) * HEAD_DIM)
            queries.append(dot(mem.key_turned[features, :], mem.probs[head, :, span]) * scale)
            sums = dot(mem.probs[head, span, :], mem.query_heads[head]).T
            keys.append(sums[:HEAD_DIM])
            by_variate = sums[HEAD_DIM : HEAD_DIM + VARIATES]
            same = by_variate * mem.key_marks[:VARIATES, span].astype(WIDE)
            mem.bias_sums[head : head + 1, :] += jnp.sum(same, axis=0, keepdims=True)
            total = sums[HEAD_DIM + VARIATES : HEAD_DIM + VARIATES + 1]
            mem.bias_sums[HEADS_HERE + head : HEADS_HERE + head + 1, :] += total
        queries = turn_rows(jnp.concatenate(queries, axis=0), cosine, sine)
        mem.grad_project[0, span, :] = queries.T.astype(LOW)
        keys = turn_rows(jnp.concatenate(keys, axis=0), cosine, sine)
        mem.grad_project[1, span, :] = keys.T.astype(LOW)
        return unused

    lax.fori_loop(0, length // pair, project_grads, 0)
    back_expand[1].pass_on()
    attend_grad(0)
    acts.pass_on(1)
    acts.pass_on(2)
    sums = scatter(heads, 3)

    def project_back(step, unused):
        chip = lax.rem(step + 1, 4)
        span = block_of(chip_of(heads, chip), pair)
        grads = [mem.grad_project[which, span, :] for which in range(3)]
        weights = [attend_matrix(which) for which in range(3)]
        sums.put(chip, dot_turned(jnp.concatenate(grads, axis=1), jnp.concatenate(weights, axis=1)))
        at_step(step, 1, lambda: sums.combine(1))
        at_step(step, 2, lambda: sums.combine(2))
        return unused

    lax.fori_loop(0, 4, project_back, 0)
    sums.combine(3)
    attend_grad(1)
    acts.pass_on(3)
    for chip in range(4):
        acts.complete(chip)
    acts.finish()
    mem.output_grad[...] = (
        dot(mem.mixed_turned[...], mem.grad_attn[...]).astype(LOW).reshape(mem.output_grad.shape)
    )
    back_output = quad_scatter(
        head_four, 3, lambda part: mem.output_grad.at[line_place(part)], mem.output_land
    )
    back_output.start()
    for which in (2, 0):
        back_attend[which].pass_on()

    column_copies = []
    mem.squares[0:1, :] = jnp.zeros((1, D), WIDE)

    def add_squares(total):
        flat = total.reshape(-1, total.shape[-1])
        width = flat.shape[1]
        mem.squares[0:1, :width] += jnp.sum(flat * flat, axis=0, keepdims=True)

    def store_whole(total, out):
        out[...] = total
        add_squares(total)

    back_reduce.land()
    store_whole(back_reduce.total(), outs.reduce_share)
    def expand_shares(which):
        back_expand[which].land()
        own = expand_part_of(mem.expand_grad, which)(quad)

        def one_block(block, unused):
            total = (
                own[block].astype(WIDE)
                + mem.expand_land[which, 0, block].astype(WIDE)
                + mem.expand_land[which, 2, block].astype(WIDE)
            )
            mem.expand_part[which, block] = total.astype(LOW)
            add_squares(total)
            return unused

        lax.fori_loop(0, 4, one_block, 0)
        for mask in masks:
            other = feeds.at(mask)
            copy = push(
                mem.expand_part.at[which, lax.rem(other, 4), lax.div(other, 4)],
                mem.expand_share.at[which, feeds.index],
                mem.share_send.at[which, mask],
                mem.share_recv.at[which, mask],
                feeds.place(mask),
            )
            copy.start()
            column_copies.append(copy)
        mem.expand_share[which, feeds.index] = mem.expand_part[
            which, lax.rem(feeds.index, 4), lax.div(feeds.index, 4)
        ]

    expand_shares(0)
    back_attend[1].pass_on()
    expand_shares(1)

    def attend_shares(which):
        back_attend[which].land()
        total = back_attend[which].total()
        mem.attend_part[which] = total.astype(LOW)
        add_squares(total)

    attend_shares(2)
    grad_act = sums.total()
    unit_one, scale_one = norm_rows(ins.inputs[...].astype(WIDE))
    gain = ins.gains[0:1, :]
    grad_unit = grad_act * gain
    mem.gains[0:1, :] = jnp.sum(grad_act * unit_one, axis=0, keepdims=True)
    grad_input = mem.grad_own[...] + scale_one * (
        grad_unit - unit_one * jnp.mean(grad_unit * unit_one, axis=-1, keepdims=True)
    )
    outs.input_gradient[...] = grad_input * (count_all * D)
    outs.count[...] = jnp.broadcast_to(count_all, (8, LANES))

    back_output.pass_on()
    for which in range(2):
        attend_shares(which)
    for mask in masks:
        copy = push(
            mem.attend_part.at[:, heads.at(mask)],
            outs.attend_share.at[:, :, block_of(me, LANES)],
            mem.share_send.at[2, mask],
            mem.share_recv.at[2, mask],
            heads.place(mask),
        )
        copy.start()
        column_copies.append(copy)
    outs.attend_share[:, :, block_of(me, LANES)] = mem.attend_part[:, me]
    back_output.land()
    store_whole(back_output.total(), outs.output_share)

    lane = lax.broadcasted_iota(jnp.int32, (1, LANES), 1)
    lines = [
        mem.gains[which : which + 1, start : start + LANES]
        for which in range(2)
        for start in range(0, D, LANES)
    ]
    bias_line = jnp.zeros((1, LANES), WIDE)
    for row in range(2 * HEADS_HERE):
        place = row // HEADS_HERE * HEADS + me * HEADS_HERE + row % HEADS_HERE
        line = mem.bias_sums[row : row + 1, :]
        if row >= HEADS_HERE:
            line = line - mem.bias_sums[row - HEADS_HERE : row - HEADS_HERE + 1, :]
        amount = jnp.sum(line, axis=1, keepdims=True)
        bias_line = bias_line + jnp.where(lane == place, amount, 0.0)
    amounts = jnp.sum(mem.squares[0:2, :], axis=1, keepdims=True)
    amount_line = jnp.where(lane == 0, amounts[0:1], 0.0) + jnp.where(lane == 1, amounts[1:2], 0.0)
    lines += [bias_line, amount_line, jnp.zeros((6, LANES), WIDE)]
    mem.plane_totals[me] = jnp.concatenate(lines, axis=0)
    plane_copies = []
    for mask in masks:
        copy = push(
            mem.plane_totals.at[me],
            mem.plane_totals.at[me],
            mem.total_send.at[0, mask],
            mem.total_recv.at[0, mask],
            (flip(me, mask), group),
        )
        copy.start()
        plane_copies.append(copy)
    for copy in column_copies[: 2 * len(masks)]:
        copy.wait()
    for which in range(2):
        for block in range(blocks):
            owner, part = feed_block(block)
            outs.expand_share[which, :, block * LANES : (block + 1) * LANES] = mem.expand_share[
                which, owner, :, part * LANES : (part + 1) * LANES
            ]
    for copy in plane_copies:
        copy.wait()
    mem.line_totals[group] = jnp.sum(mem.plane_totals[...], axis=0)
    total_copies = []
    for step in range(1, batch):
        copy = push(
            mem.line_totals.at[group],
            mem.line_totals.at[group],
            mem.total_send.at[1, step],
            mem.total_recv.at[1, step],
            (me, lax.rem(group + step, batch)),
        )
        copy.start()
        total_copies.append(copy)
    for copy in total_copies:
        copy.wait()
    outs.totals[...] = jnp.sum(mem.line_totals[...], axis=0)
    for copy in column_copies[2 * len(masks) :]:
        copy.wait()
    for copies in (attend_columns, expand_columns):
        for copy in copies:
            copy.wait_send()
    for line in [line_attend, line_output, line_reduce] + line_expand:
        line.finish()
    for line in [back_output, back_reduce] + back_attend + back_expand:
        line.finish()


def call_layer(seq, batch, inputs, teacher, lengths, variates, observed, turns, bias, gains, attend, output, expand, reduce):
    rows, share, hidden = inputs.shape[0], attend.shape[1], expand.shape[2] // seq
    length, pair, chips = rows * seq, 2 * rows, seq // 2
    low = lambda *shape: pltpu.VMEM(shape, LOW)
    wide = lambda *shape: pltpu.VMEM(shape, WIDE)
    sems = lambda *shape: pltpu.SemaphoreType.DMA(shape)
    in_names = ["inputs", "teacher", "lengths", "variates", "observed", "turns", "bias", "gains"]
    in_names += ["attend", "output", "expand", "reduce"]
    outs = dict(
        layer_output=((rows, D), WIDE),
        input_gradient=((rows, D), WIDE),
        totals=((TOTAL_ROWS, LANES), WIDE),
        count=((8, LANES), WIDE),
        attend_share=((3, share, D), LOW),
        output_share=((output.shape[0], D), WIDE),
        expand_share=((2, share, hidden * seq), LOW),
        reduce_share=((reduce.shape[0], D), WIDE),
    )
    scratch = dict(
        gains=wide(2, D),
        squares=wide(8, D),
        plane_totals=wide(seq, TOTAL_ROWS, LANES),
        line_totals=wide(batch, TOTAL_ROWS, LANES),
        attend_low=low(3, share, D),
        expand_low=low(2, seq, share, hidden),
        attend_all=low(3, seq, batch, share, LANES),
        output_full=low(D, D),
        expand_all=low(2, seq, batch, share, hidden),
        reduce_all=low(batch, reduce.shape[0], D),
        own_rows=low(4, rows, D),
        act_one=low(length, D),
        act_two=low(length, D),
        branch=low(length, D),
        grad_attn=low(length, D),
        facts_own=wide(turns.shape[0] + 8, LANES),
        facts_all=wide(seq * (turns.shape[0] + 8), LANES),
        scored=wide(rows, LANES),
        cosine=wide(HEAD_DIM // 2, length),
        sine=wide(HEAD_DIM // 2, length),
        labels=wide(8, length),
        key_marks=low(HEAD_DIM, length),
        count=wide(batch, 8, LANES),
        query_turned=low(HEADS_HERE, LANES, length),
        key_turned=low(LANES, length),
        value_turned=low(LANES, length),
        key_heads=low(HEADS_HERE, length, LANES),
        value_heads=low(HEADS_HERE, length, LANES),
        query_heads=low(HEADS_HERE, length, LANES),
        grad_heads=low(HEADS_HERE, length, LANES),
        grad_mixed=low(LANES, length),
        grad_mixed_out=low(seq, LANES, rows),
        probs=low(HEADS_HERE, length, length),
        mixed_out=low(length, LANES),
        mixed_rows=low(rows, D),
        sum_marks=low(HEAD_DIM, length),
        hidden_turned=low(hidden, length),
        act_two_turned=low(D, length),
        exact=wide(LANES, length),
        mixed_wide=wide(LANES, pair),
        mixed_turned=low(LANES, length),
        whole=wide(pair, D),
        keep=wide(chips, rows, D),
        near_from=low(chips, rows, D),
        near=low(chips, rows, D),
        far_from=low(chips, rows, D),
        far=low(chips, rows, D),
        middle=wide(rows, D),
        grad_own=wide(rows, D),
        by_up=wide(length, hidden),
        by_gate=wide(length, hidden),
        hidden=low(length, hidden),
        grad_gate=low(length, hidden),
        grad_up=low(length, hidden),
        bias_sums=wide(8, pair),
        grad_project=low(3, length, LANES),
        act_one_turned=low(D, length),
        reduce_grad=low(batch, reduce.shape[0], D),
        expand_grad=low(2, seq, batch, share, hidden),
        output_grad=low(batch, output.shape[0], D),
        attend_grad=low(3, seq, batch, share, LANES),
        reduce_land=low(3, reduce.shape[0], D),
        expand_land=low(2, 3, 4, 2, share, hidden),
        output_land=low(3, output.shape[0], D),
        attend_land=low(3, 3, seq, share, LANES),
        expand_part=low(2, 4, 2, share, hidden),
        expand_share=low(2, seq, share, hidden),
        attend_part=low(3, seq, share, LANES),
        stage_sem=sems(5 + 2 * (expand.shape[2] // D)),
        total_send=sems(2, seq),
        total_recv=sems(2, seq),
        column_send=sems(2, seq),
        column_recv=sems(2, seq),
        line_send=sems(5, batch),
        line_recv=sems(5, batch),
        facts_send=sems(seq),
        facts_recv=sems(seq),
        gather_send=sems(4, seq),
        gather_recv=sems(4, seq),
        count_send=sems(batch),
        count_recv=sems(batch),
        near_send=sems(4, chips),
        near_recv=sems(4, chips),
        far_send=sems(4, chips),
        far_recv=sems(4, chips),
        back_send=sems(7, batch),
        back_recv=sems(7, batch),
        output_send=sems(seq),
        output_recv=sems(seq),
        mixed_send=sems(2 * seq),
        mixed_recv=sems(2 * seq),
        share_send=sems(3, seq),
        share_recv=sems(3, seq),
    )

    places = dict.fromkeys(("attend", "output", "expand", "reduce"), pl.BlockSpec(memory_space=pl.ANY))
    places["bias"] = places["lengths"] = IN_SMEM

    def kernel(*refs):
        groups, start = [], 0
        for names in (in_names, outs, scratch):
            names = list(names)
            groups.append(types.SimpleNamespace(**dict(zip(names, refs[start : start + len(names)]))))
            start += len(names)
        layer_kernel(seq, batch, *groups)

    results = pl.pallas_call(
        kernel,
        out_shape=[jax.ShapeDtypeStruct(*out) for out in outs.values()],
        in_specs=[places.get(name, IN_VMEM) for name in in_names],
        out_specs=[IN_VMEM] * len(outs),
        scratch_shapes=list(scratch.values()),
        compiler_params=pltpu.CompilerParams(
            collective_id=0, has_side_effects=True, vmem_limit_bytes=63 * MIB
        ),
        name="layer",
    )(inputs, teacher, lengths, variates, observed, turns, bias, gains, attend, output, expand, reduce)
    return types.SimpleNamespace(**dict(zip(outs, results)))


def update_kernel(
    smalls, ins, small_outs, outs, olds, shares, news, copies, passed, in_sems, out_sems
):
    totals, count, gains, gains_first, gains_second, bias, bias_first, bias_second = smalls
    order = (2, 3, 0, 1)
    comes = []
    for place, number in enumerate(order):
        pairs = list(zip(ins[4 + 3 * number : 7 + 3 * number], olds[3 * number : 3 * number + 3]))
        pairs.append((ins[number], shares[number]))
        comes.append(
            [
                pltpu.make_async_copy(source, target, in_sems.at[4 * place + part])
                for part, (source, target) in enumerate(pairs)
            ]
        )
    for copy in sum(comes, []):
        copy.start()
    through = [
        pltpu.make_async_copy(ins[16 + part], passed[part], in_sems.at[16 + part]) for part in range(2)
    ]
    for copy in through:
        copy.start()
    goes = []
    gains_total = jnp.concatenate(
        [
            jnp.concatenate([totals[row + i : row + i + 1, :] for i in range(D // LANES)], axis=1)
            for row in (0, D // LANES)
        ],
        axis=0,
    )
    row = 2 * D // LANES
    bias_total = jnp.concatenate(
        [totals[row : row + 1, :HEADS], totals[row : row + 1, HEADS : 2 * HEADS]], axis=0
    )
    row += 1

    def sum_all(values):
        return jnp.sum(jnp.sum(values, axis=0, keepdims=True), axis=1, keepdims=True)

    squares = (
        totals[row : row + 1, 0:1] + sum_all(gains_total * gains_total) + sum_all(bias_total * bias_total)
    )
    grad_norm = jnp.sqrt(squares)
    clip = jnp.minimum(1.0, CLIP_NORM / grad_norm)
    small_outs[0][...] = totals[row : row + 1, 1:2] / (count[0:1, 0:1] * D)
    small_outs[1][...] = grad_norm
    rates = (RATE_ATTEND, RATE_OUTPUT, RATE_EXPAND, RATE_REDUCE)
    for place, number in enumerate(order):
        for copy in comes[place]:
            copy.wait()
        weight, first, second = olds[3 * number : 3 * number + 3]
        new, first_new, second_new = news[3 * number : 3 * number + 3]
        arrays = (new, copies[number], first_new, second_new, weight, first, second, shares[number])
        for lead in range(weight.shape[0] if weight.ndim == 3 else 1):

            def one_block(block, unused, lead=lead, arrays=arrays, rate=rates[number]):
                rows = block_of(block, 16)
                place = (lead, rows) if arrays[0].ndim == 3 else (rows,)
                old, moment, square, share = [array[place] for array in arrays[4:]]
                step = fast_step(old, moment, square, share.astype(WIDE) * clip, rate)
                arrays[0][place], arrays[2][place], arrays[3][place] = step
                arrays[1][place] = step[0].astype(LOW)
                return unused

            lax.fori_loop(0, weight.shape[-2] // 16, one_block, 0)
        for part, source in enumerate((new, copies[number], first_new, second_new)):
            copy = pltpu.make_async_copy(
                source, outs[2 + 4 * number + part], out_sems.at[2 + 4 * number + part]
            )
            copy.start()
            goes.append(copy)
        if place == 0:
            for part in range(2):
                through[part].wait()
                copy = pltpu.make_async_copy(passed[part], outs[part], out_sems.at[part])
                copy.start()
                goes.append(copy)
    for number, (old, total, rate) in enumerate(
        (
            ((gains, gains_first, gains_second), gains_total, RATE_GAINS),
            ((bias, bias_first, bias_second), bias_total, RATE_BIAS),
        )
    ):
        new, first_new, second_new = small_outs[2 + 3 * number : 5 + 3 * number]
        new[...], first_new[...], second_new[...] = adam_step(
            old[0][...], old[1][...], old[2][...], total * clip, rate, 0.0
        )
    for copy in goes:
        copy.wait()


def fast_step(weight, first, second, gradient, rate):
    first = BETA_ONE * first + (1.0 - BETA_ONE) * gradient
    second = BETA_TWO * second + ((1.0 - BETA_TWO) * gradient) * gradient
    low = jnp.sqrt(second * (1.0 / (1.0 - BETA_TWO**STEP))) + ADAM_EPS
    step = first * (rate / (1.0 - BETA_ONE**STEP)) / low
    return weight * (1.0 - rate * WEIGHT_DECAY) - step, first, second


def call_update(done, shares, smalls, olds):
    in_hbm = pl.BlockSpec(memory_space=pl.ANY)
    smalls = [done.totals, done.count] + smalls
    ins = shares + olds + [done.layer_output, done.input_gradient]
    one = jax.ShapeDtypeStruct((1, 1), WIDE)
    small_outs = [one, one] + smalls[2:]
    outs = [(done.layer_output, WIDE), (done.input_gradient, WIDE)]
    for weight in olds[::3]:
        outs += [(weight, dtype) for dtype in (WIDE, LOW, WIDE, WIDE)]
    passed = ins[-2:]
    parts = [smalls, ins, small_outs, outs, olds, shares, olds, olds[::3], passed]

    def kernel(*refs):
        groups, start = [], 0
        for part in parts:
            groups.append(refs[start : start + len(part)])
            start += len(part)
        update_kernel(*groups, *refs[start:])

    results = pl.pallas_call(
        kernel,
        out_shape=[jax.ShapeDtypeStruct(array.shape, WIDE) for array in small_outs]
        + [jax.ShapeDtypeStruct(array.shape, dtype) for array, dtype in outs],
        in_specs=[IN_VMEM] * len(smalls) + [in_hbm] * len(ins),
        out_specs=[IN_VMEM] * len(small_outs) + [in_hbm] * len(outs),
        scratch_shapes=[pltpu.VMEM(array.shape, WIDE) for array in olds]
        + [pltpu.VMEM(array.shape, array.dtype) for array in shares]
        + [pltpu.VMEM(array.shape, WIDE) for array in olds]
        + [pltpu.VMEM(array.shape, LOW) for array in olds[::3]]
        + [pltpu.VMEM(array.shape, WIDE) for array in passed]
        + [pltpu.SemaphoreType.DMA((18,)), pltpu.SemaphoreType.DMA((18,))],
        compiler_params=pltpu.CompilerParams(vmem_limit_bytes=63 * MIB),
        name="update",
    )(*smalls, *ins)
    return results[: len(small_outs)], results[len(small_outs) :]


def fast_body(
    seq,
    batch,
    inputs,
    teacher,
    lengths,
    variate_ids,
    time_ids,
    observed,
    attend_weight,
    output_weight,
    expand_weight,
    reduce_weight,
    norm_gains,
    variate_bias,
    attend_first,
    output_first,
    expand_first,
    reduce_first,
    gains_first,
    bias_first,
    attend_second,
    output_second,
    expand_second,
    reduce_second,
    gains_second,
    bias_second,
):
    half_dim = HEAD_DIM // 2
    frequency = jnp.exp(-math.log(ROPE_BASE) * jnp.arange(half_dim).astype(WIDE) / half_dim)
    angle = frequency[:, None] * time_ids.astype(WIDE)
    done = call_layer(
        seq,
        batch,
        inputs[0],
        teacher[0],
        lengths,
        variate_ids,
        observed,
        jnp.concatenate([jnp.cos(angle), jnp.sin(angle)]),
        variate_bias,
        norm_gains,
        attend_weight,
        output_weight,
        expand_weight,
        reduce_weight,
    )
    small, large = call_update(
        done,
        [done.attend_share, done.output_share, done.expand_share, done.reduce_share],
        [norm_gains, gains_first, gains_second, variate_bias, bias_first, bias_second],
        [attend_weight, attend_first, attend_second]
        + [output_weight, output_first, output_second]
        + [expand_weight, expand_first, expand_second]
        + [reduce_weight, reduce_first, reduce_second],
    )
    return (
        large[0][None],
        small[0].reshape(()),
        large[1][None],
        small[1].reshape(()),
    ) + tuple(large[2:] + small[2:])


def solution(mesh):
    seq, batch = mesh.shape["seq"], mesh.shape["batch"]
    body = functools.partial(fast_body, seq, batch) if fast_fits(seq, batch) else general_body
    in_specs = (
        P("batch", "seq", None),
        P("batch", "seq", None),
        P("batch"),
        P("batch", "seq"),
        P("batch", "seq"),
        P("batch", "seq"),
        P(None, ("seq", "batch"), None),
        P(("seq", "batch"), None),
        P(None, ("seq", "batch"), None),
        P(("seq", "batch"), None),
        P(),
        P(),
        P(None, ("seq", "batch"), None),
        P(("seq", "batch"), None),
        P(None, ("seq", "batch"), None),
        P(("seq", "batch"), None),
        P(),
        P(),
        P(None, ("seq", "batch"), None),
        P(("seq", "batch"), None),
        P(None, ("seq", "batch"), None),
        P(("seq", "batch"), None),
        P(),
        P(),
    )
    out_specs = (
        P("batch", "seq", None),
        P(),
        P("batch", "seq", None),
        P(),
        P(None, ("seq", "batch"), None),
        P(None, ("seq", "batch"), None),
        P(None, ("seq", "batch"), None),
        P(None, ("seq", "batch"), None),
        P(("seq", "batch"), None),
        P(("seq", "batch"), None),
        P(("seq", "batch"), None),
        P(("seq", "batch"), None),
        P(None, ("seq", "batch"), None),
        P(None, ("seq", "batch"), None),
        P(None, ("seq", "batch"), None),
        P(None, ("seq", "batch"), None),
        P(("seq", "batch"), None),
        P(("seq", "batch"), None),
        P(("seq", "batch"), None),
        P(("seq", "batch"), None),
        P(),
        P(),
        P(),
        P(),
        P(),
        P(),
    )
    return jax.shard_map(body, mesh=mesh, in_specs=in_specs, out_specs=out_specs, check_vma=False)
```

```python
import functools
import math
import types

import jax
import jax.numpy as jnp
from jax import lax
from jax.experimental import pallas as pl
from jax.experimental.pallas import tpu as pltpu
from jax.sharding import PartitionSpec as P

D = 1024
HEADS = 16
HEAD_DIM = 64
STEP = 10


NORM_EPS = 1e-05
ROPE_BASE = 10000.0
MASKED = -1e30
CLIP_NORM = 1.0
BETA_ONE = 0.9
BETA_TWO = 0.98
ADAM_EPS = 1e-08
WEIGHT_DECAY = 0.1
RATE_ATTEND = 0.03
RATE_OUTPUT = 0.5
RATE_EXPAND = 0.03
RATE_REDUCE = 0.015
RATE_GAINS = 1.0
RATE_BIAS = 0.5


def angles(times):
    half_dim = HEAD_DIM // 2
    frequency = jnp.exp(-math.log(ROPE_BASE) * jnp.arange(half_dim).astype(jnp.float32) / half_dim)
    angle_table = times.astype(jnp.float32)[..., None] * frequency
    return (jnp.cos(angle_table)[..., None, :], jnp.sin(angle_table)[..., None, :])


def rotate(values, cos_table, sin_table):
    half_dim = values.shape[-1] // 2
    first_half = values[..., :half_dim]
    second_half = values[..., half_dim:]
    return jnp.concatenate(
        [
            first_half * cos_table - second_half * sin_table,
            second_half * cos_table + first_half * sin_table,
        ],
        axis=-1,
    )


def unrotate(values, cos_table, sin_table):
    half_dim = values.shape[-1] // 2
    first_half = values[..., :half_dim]
    second_half = values[..., half_dim:]
    return jnp.concatenate(
        [
            first_half * cos_table + second_half * sin_table,
            second_half * cos_table - first_half * sin_table,
        ],
        axis=-1,
    )


def normalize(values):
    inv_scale = lax.rsqrt(jnp.mean(values * values, axis=-1, keepdims=True) + NORM_EPS)
    return (values * inv_scale, inv_scale)


def norm_back(grad_act, unit_rows, inv_scale, gain_row):
    grad_unit = grad_act * gain_row
    return inv_scale * (
        grad_unit - unit_rows * jnp.mean(grad_unit * unit_rows, axis=-1, keepdims=True)
    )


def score_block(query_rows, query_labels, key_rows, key_labels, bias_table):
    scores = jnp.einsum(
        "ihe,jhe->hij", query_rows, key_rows, preferred_element_type=jnp.float32
    ) * HEAD_DIM ** (-0.5)
    same_var = query_labels[:, None] == key_labels[None, :]
    scores = scores + jnp.where(
        same_var[None], bias_table[0][:, None, None], bias_table[1][:, None, None]
    )
    scores = jnp.where(key_labels[None, None, :] >= 0, scores, MASKED)
    return (scores, same_var)


def block_grads(
    query_rows,
    query_labels,
    grad_rows,
    lse_rows,
    delta_rows,
    key_rows,
    value_rows,
    key_labels,
    bias_table,
    need_query,
    need_keys,
):
    scores, same_var = score_block(query_rows, query_labels, key_rows, key_labels, bias_table)
    weights = jnp.exp(scores - lse_rows.T[:, :, None])
    grad_weights = jnp.einsum(
        "ihe,jhe->hij", grad_rows, value_rows, preferred_element_type=jnp.float32
    )
    grad_scores = (weights * (grad_weights - delta_rows.T[:, :, None])).astype(jnp.bfloat16)
    result = ()
    if need_query:
        grad_query = jnp.einsum(
            "hij,jhe->ihe", grad_scores, key_rows, preferred_element_type=jnp.float32
        ) * HEAD_DIM ** (-0.5)
        widened = grad_scores.astype(jnp.float32)
        bias_same = jnp.sum(jnp.where(same_var[None], widened, 0.0), axis=(1, 2))
        bias_other = jnp.sum(jnp.where(same_var[None], 0.0, widened), axis=(1, 2))
        result = result + (grad_query, jnp.stack([bias_same, bias_other]))
    if need_keys:
        grad_key = jnp.einsum(
            "hij,ihe->jhe", grad_scores, query_rows, preferred_element_type=jnp.float32
        ) * HEAD_DIM ** (-0.5)
        grad_value = jnp.einsum(
            "hij,ihe->jhe",
            weights.astype(jnp.bfloat16),
            grad_rows,
            preferred_element_type=jnp.float32,
        )
        result = result + (grad_key, grad_value)
    return result


def adam_step(weight, first_moment, second_moment, gradient, step_rate, decay_rate):
    first_moment = BETA_ONE * first_moment + (1.0 - BETA_ONE) * gradient
    second_moment = BETA_TWO * second_moment + (1.0 - BETA_TWO) * gradient * gradient
    direction = (
        first_moment
        / (1.0 - BETA_ONE**STEP)
        / (jnp.sqrt(second_moment / (1.0 - BETA_TWO**STEP)) + ADAM_EPS)
    )
    return (weight - step_rate * (direction + decay_rate * weight), first_moment, second_moment)


def general_body(
    inputs,
    teacher,
    lengths,
    variate_ids,
    time_ids,
    observed,
    attend_weight,
    output_weight,
    expand_weight,
    reduce_weight,
    norm_gains,
    variate_bias,
    attend_first,
    output_first,
    expand_first,
    reduce_first,
    gains_first,
    bias_first,
    attend_second,
    output_second,
    expand_second,
    reduce_second,
    gains_second,
    bias_second,
):
    row_count = inputs.shape[1]
    length = row_count * lax.axis_size("seq")
    block_rows = math.gcd(length, 1024)
    blocks = length // block_rows
    states = inputs[0].astype(jnp.float32)
    positions = lax.axis_index("seq") * row_count + jnp.arange(row_count, dtype=jnp.int32)
    inside = positions < lengths[0]
    scored = jnp.logical_and(inside, observed[0] == 1)
    local_count = jnp.sum(scored.astype(jnp.int32))
    count_early = lax.psum(local_count, ("seq", "batch"))
    full_attend, full_output, full_expand, full_reduce = (
        lax.all_gather(attend_weight.astype(jnp.bfloat16), ("seq", "batch"), axis=1, tiled=True),
        lax.all_gather(output_weight.astype(jnp.bfloat16), ("seq", "batch"), axis=0, tiled=True),
        lax.all_gather(expand_weight.astype(jnp.bfloat16), ("seq", "batch"), axis=1, tiled=True),
        lax.all_gather(reduce_weight.astype(jnp.bfloat16), ("seq", "batch"), axis=0, tiled=True),
    )
    unit_one, scale_one = normalize(states)
    act_one = (unit_one * norm_gains[0]).astype(jnp.bfloat16)
    project = jnp.einsum("td,cde->cte", act_one, full_attend, preferred_element_type=jnp.float32)
    cos_table, sin_table = angles(time_ids[0])
    query = rotate(project[0].reshape(row_count, HEADS, HEAD_DIM), cos_table, sin_table).astype(
        jnp.bfloat16
    )
    key_rows = (
        rotate(project[1].reshape(row_count, HEADS, HEAD_DIM), cos_table, sin_table)
        .astype(jnp.bfloat16)
        .reshape(row_count, D)
    )
    value_rows = project[2].astype(jnp.bfloat16)
    own_labels = jnp.where(inside, variate_ids[0], -1).astype(jnp.bfloat16)
    all_keys, all_values, all_labels = (
        lax.all_gather(key_rows, "seq", axis=0, tiled=True),
        lax.all_gather(value_rows, "seq", axis=0, tiled=True),
        lax.all_gather(own_labels, "seq", axis=0, tiled=True),
    )
    key_blocks = all_keys.reshape(blocks, block_rows, HEADS, HEAD_DIM)
    value_blocks = all_values.reshape(blocks, block_rows, HEADS, HEAD_DIM)
    label_blocks = all_labels.astype(jnp.float32).reshape(blocks, block_rows)
    query_labels = variate_ids[0].astype(jnp.float32)

    def sweep_top(carry, pieces):
        running, sum_exp = carry
        scores, same_var = score_block(query, query_labels, pieces[0], pieces[1], variate_bias)
        raised = jnp.maximum(running, jnp.floor(jnp.max(scores, axis=-1)))
        sum_exp = sum_exp * jnp.exp(running - raised) + jnp.sum(
            jnp.exp(scores - raised[..., None]), axis=-1
        )
        return ((raised, sum_exp), None)

    start_top = jnp.full((HEADS, row_count), MASKED, jnp.float32)
    (row_top, sum_exp), unused = lax.scan(
        sweep_top,
        (start_top, jnp.zeros((HEADS, row_count), jnp.float32)),
        (key_blocks, label_blocks),
    )
    log_total = row_top + jnp.log(sum_exp)

    def sweep_out(carry, pieces):
        coarse, finest = carry
        scores, same_var = score_block(query, query_labels, pieces[0], pieces[2], variate_bias)
        weights = jnp.exp(scores - log_total[..., None])
        rounded = weights.astype(jnp.bfloat16)
        residue = (weights - rounded.astype(jnp.float32)).astype(jnp.bfloat16)
        coarse = coarse + jnp.einsum(
            "hij,jhe->ihe", rounded, pieces[1], preferred_element_type=jnp.float32
        )
        finest = finest + jnp.einsum(
            "hij,jhe->ihe", residue, pieces[1], preferred_element_type=jnp.float32
        )
        return ((coarse, finest), None)

    zero_heads = jnp.zeros((row_count, HEADS, HEAD_DIM), jnp.float32)
    (coarse, finest), unused = lax.scan(
        sweep_out, (zero_heads, zero_heads), (key_blocks, value_blocks, label_blocks)
    )
    exact_heads = coarse + finest
    mixed = coarse.reshape(row_count, D).astype(jnp.bfloat16)
    middle = states + jnp.dot(mixed, full_output, preferred_element_type=jnp.float32)
    unit_two, scale_two = normalize(middle)
    act_two = (unit_two * norm_gains[1]).astype(jnp.bfloat16)
    gate_up = jnp.einsum("td,cdf->ctf", act_two, full_expand, preferred_element_type=jnp.float32)
    sigmoid = jax.nn.sigmoid(gate_up[0])
    hidden = (gate_up[0] * sigmoid * gate_up[1]).astype(jnp.bfloat16)
    output = middle + jnp.dot(hidden, full_reduce, preferred_element_type=jnp.float32)
    error = output - teacher[0].astype(jnp.float32)
    local_square = jnp.sum(jnp.where(scored[:, None], error * error, 0.0))
    square_total = lax.psum(local_square, ("seq", "batch"))
    count_all = count_early.astype(jnp.float32)
    loss = square_total / (count_all * D)
    grad_out = jnp.where(scored[:, None], error * (2.0 / (count_all * D)), 0.0)
    back_attend, back_output, back_expand, back_reduce = (
        lax.all_gather(attend_weight.astype(jnp.bfloat16), ("seq", "batch"), axis=1, tiled=True),
        lax.all_gather(output_weight.astype(jnp.bfloat16), ("seq", "batch"), axis=0, tiled=True),
        lax.all_gather(expand_weight.astype(jnp.bfloat16), ("seq", "batch"), axis=1, tiled=True),
        lax.all_gather(reduce_weight.astype(jnp.bfloat16), ("seq", "batch"), axis=0, tiled=True),
    )
    grad_branch = grad_out.astype(jnp.bfloat16)
    reduce_grad = jnp.einsum("tf,td->fd", hidden, grad_branch, preferred_element_type=jnp.float32)
    grad_hidden = jnp.einsum(
        "td,fd->tf", grad_branch, back_reduce, preferred_element_type=jnp.float32
    )
    grad_gate = grad_hidden * gate_up[1] * sigmoid * (1.0 + gate_up[0] * (1.0 - sigmoid))
    grad_up = grad_hidden * gate_up[0] * sigmoid
    grad_expand = jnp.stack([grad_gate, grad_up]).astype(jnp.bfloat16)
    expand_grad = jnp.einsum(
        "td,ctf->cdf", act_two, grad_expand, preferred_element_type=jnp.float32
    )
    grad_act_two = jnp.einsum(
        "ctf,cdf->td", grad_expand, back_expand, preferred_element_type=jnp.float32
    )
    expand_share, reduce_share = (
        lax.psum_scatter(expand_grad, ("seq", "batch"), scatter_dimension=1, tiled=True),
        lax.psum_scatter(reduce_grad, ("seq", "batch"), scatter_dimension=0, tiled=True),
    )
    grad_middle = grad_out + norm_back(grad_act_two, unit_two, scale_two, norm_gains[1])
    grad_attn = grad_middle.astype(jnp.bfloat16)
    output_grad = jnp.einsum("td,te->de", mixed, grad_attn, preferred_element_type=jnp.float32)
    grad_mixed = jnp.einsum(
        "te,de->td", grad_attn, back_output, preferred_element_type=jnp.float32
    ).astype(jnp.bfloat16)
    grad_heads = grad_mixed.reshape(row_count, HEADS, HEAD_DIM)
    row_delta = jnp.sum(grad_heads.astype(jnp.float32) * exact_heads, axis=-1)
    lse_rows = log_total.T
    zero_bias = jnp.zeros((2, HEADS), jnp.float32)

    def sweep_query(carry, pieces):
        part_query, part_bias = block_grads(
            query,
            query_labels,
            grad_heads,
            lse_rows,
            row_delta,
            pieces[0],
            pieces[1],
            pieces[2],
            variate_bias,
            True,
            False,
        )
        return ((carry[0] + part_query, carry[1] + part_bias), None)

    (query_total, bias_grad), unused = lax.scan(
        sweep_query, (zero_heads, zero_bias), (key_blocks, value_blocks, label_blocks)
    )
    all_query, all_grad = (
        lax.all_gather(query.reshape(row_count, D), "seq", axis=0, tiled=True),
        lax.all_gather(grad_mixed, "seq", axis=0, tiled=True),
    )
    all_lse, all_delta = (
        lax.all_gather(lse_rows, "seq", axis=0, tiled=True),
        lax.all_gather(row_delta, "seq", axis=0, tiled=True),
    )
    key_heads = key_rows.reshape(row_count, HEADS, HEAD_DIM)
    value_heads = value_rows.reshape(row_count, HEADS, HEAD_DIM)
    own_float = own_labels.astype(jnp.float32)

    def sweep_keys(carry, pieces):
        part_key, part_value = block_grads(
            pieces[0],
            pieces[1],
            pieces[2],
            pieces[3],
            pieces[4],
            key_heads,
            value_heads,
            own_float,
            variate_bias,
            False,
            True,
        )
        return ((carry[0] + part_key, carry[1] + part_value), None)

    (key_total, value_heads_total), unused = lax.scan(
        sweep_keys,
        (zero_heads, zero_heads),
        (
            all_query.reshape(blocks, block_rows, HEADS, HEAD_DIM),
            label_blocks,
            all_grad.reshape(blocks, block_rows, HEADS, HEAD_DIM),
            all_lse.reshape(blocks, block_rows, HEADS),
            all_delta.reshape(blocks, block_rows, HEADS),
        ),
    )
    value_total = value_heads_total.reshape(row_count, D)
    grad_query = unrotate(query_total, cos_table, sin_table).reshape(row_count, D)
    grad_key = unrotate(key_total, cos_table, sin_table).reshape(row_count, D)
    grad_project = jnp.stack([grad_query, grad_key, value_total]).astype(jnp.bfloat16)
    attend_grad = jnp.einsum(
        "td,cte->cde", act_one, grad_project, preferred_element_type=jnp.float32
    )
    grad_act_one = jnp.einsum(
        "cte,cde->td", grad_project, back_attend, preferred_element_type=jnp.float32
    )
    attend_share, output_share = (
        lax.psum_scatter(attend_grad, ("seq", "batch"), scatter_dimension=1, tiled=True),
        lax.psum_scatter(output_grad, ("seq", "batch"), scatter_dimension=0, tiled=True),
    )
    grad_input = grad_middle + norm_back(grad_act_one, unit_one, scale_one, norm_gains[0])
    gains_grad = jnp.stack(
        [jnp.sum(grad_act_one * unit_one, axis=0), jnp.sum(grad_act_two * unit_two, axis=0)]
    )
    local_squares = (
        jnp.sum(attend_share * attend_share)
        + jnp.sum(output_share * output_share)
        + jnp.sum(expand_share * expand_share)
        + jnp.sum(reduce_share * reduce_share)
    )
    gains_total, bias_total, square_sum = lax.psum(
        (gains_grad, bias_grad, local_squares), ("seq", "batch")
    )
    grad_norm = jnp.sqrt(
        square_sum + jnp.sum(gains_total * gains_total) + jnp.sum(bias_total * bias_total)
    )
    clip_scale = jnp.minimum(1.0, CLIP_NORM / grad_norm)
    attend_new, attend_first_new, attend_second_new = adam_step(
        attend_weight,
        attend_first,
        attend_second,
        attend_share * clip_scale,
        RATE_ATTEND,
        WEIGHT_DECAY,
    )
    output_new, output_first_new, output_second_new = adam_step(
        output_weight,
        output_first,
        output_second,
        output_share * clip_scale,
        RATE_OUTPUT,
        WEIGHT_DECAY,
    )
    expand_new, expand_first_new, expand_second_new = adam_step(
        expand_weight,
        expand_first,
        expand_second,
        expand_share * clip_scale,
        RATE_EXPAND,
        WEIGHT_DECAY,
    )
    reduce_new, reduce_first_new, reduce_second_new = adam_step(
        reduce_weight,
        reduce_first,
        reduce_second,
        reduce_share * clip_scale,
        RATE_REDUCE,
        WEIGHT_DECAY,
    )
    gains_new, gains_first_new, gains_second_new = adam_step(
        norm_gains, gains_first, gains_second, gains_total * clip_scale, RATE_GAINS, 0.0
    )
    bias_new, bias_first_new, bias_second_new = adam_step(
        variate_bias, bias_first, bias_second, bias_total * clip_scale, RATE_BIAS, 0.0
    )
    input_gradient = (grad_input * count_all * D)[None]
    return (
        output[None],
        loss,
        input_gradient,
        grad_norm,
        attend_new,
        attend_new.astype(jnp.bfloat16),
        attend_first_new,
        attend_second_new,
        output_new,
        output_new.astype(jnp.bfloat16),
        output_first_new,
        output_second_new,
        expand_new,
        expand_new.astype(jnp.bfloat16),
        expand_first_new,
        expand_second_new,
        reduce_new,
        reduce_new.astype(jnp.bfloat16),
        reduce_first_new,
        reduce_second_new,
        gains_new,
        gains_first_new,
        gains_second_new,
        bias_new,
        bias_first_new,
        bias_second_new,
    )


MESH = pl.DeviceIdType.MESH
IN_VMEM = pl.BlockSpec(memory_space=pltpu.VMEM)
IN_SMEM = pl.BlockSpec(memory_space=pltpu.SMEM)
LANES = 128
HEADS_HERE = LANES // HEAD_DIM
VARIATES = 16
MIB = 1 << 20
LOW = jnp.bfloat16
WIDE = jnp.float32
TOTAL_ROWS = 24


def fast_fits(seq, batch):
    return seq == 8 and batch == 4 and seq * LANES == D


def flip(index, mask):
    result, bit = index, 1
    while bit <= mask:
        if mask & bit:
            result = result + bit - 2 * bit * lax.rem(lax.div(index, bit), 2)
        bit *= 2
    return result


def push(source, target, send_sem, recv_sem, device):
    return pltpu.make_async_remote_copy(
        src_ref=source,
        dst_ref=target,
        send_sem=send_sem,
        recv_sem=recv_sem,
        device_id=device,
        device_id_type=MESH,
    )


def block_of(index, size):
    return pl.ds(pl.multiple_of(index * size, size), size)


def dot(left, right):
    return jnp.dot(left, right, preferred_element_type=WIDE)


def dot_turned(left, right):
    return lax.dot_general(left, right, (((1,), (1,)), ((), ())), preferred_element_type=WIDE)


def turned_dot(left, right):
    return lax.dot_general(left, right, (((0,), (0,)), ((), ())), preferred_element_type=WIDE)


class Team:
    def __init__(self, index, place):
        self.index, self.place = index, place

    def at(self, mask):
        return flip(self.index, mask)


def head_team(me, group):
    return Team(me, lambda mask: (flip(me, mask), group))


def feed_team(me, group):
    return Team(
        4 * lax.rem(group, 2) + lax.rem(me, 4),
        lambda mask: (flip(me, mask % 4), flip(group, mask // 4)),
    )


class Gather:
    def __init__(self, team, rows, all_rows, sends, recvs):
        self.team, self.all_rows, self.sends, self.recvs = team, all_rows, sends, recvs
        self.size = all_rows.shape[0] // 8
        self.given = rows
        self.rows = all_rows.at[block_of(team.index, self.size)] if rows is None else rows

    def copy(self, mask, passing):
        source = self.all_rows.at[block_of(self.team.at(mask - 1 if passing else 0), self.size)]
        return push(
            source if passing else self.rows,
            source,
            self.sends.at[mask],
            self.recvs.at[mask],
            self.team.place(1 if passing else mask),
        )

    def start(self, masks=(6, 2, 4, 1)):
        for mask in masks:
            self.copy(mask, False).start()
        if self.given is not None:
            self.all_rows[block_of(self.team.index, self.size)] = self.given[...]

    def pass_on(self, chip):
        self.copy(2 * chip, False).wait_recv()
        self.copy(2 * chip + 1, True).start()

    def complete(self, chip):
        self.copy(2 * chip + 1, chip > 0).wait_recv()

    def finish(self):
        for mask in (6, 2, 4, 1):
            self.copy(mask, False).wait_send()
        for mask in (3, 5, 7):
            self.copy(mask, True).wait_send()


def at_step(step, number, *works):
    @pl.when(step == number)
    def _():
        for work in works:
            work()


def each_chip(gather, work, after):
    def one_chip(chip, unused):
        @pl.when(chip == 0)
        def _():
            gather.complete(0)

        @pl.when(chip == 1)
        def _():
            gather.pass_on(1)
            gather.pass_on(2)
            gather.copy(6, False).start()
            gather.complete(1)

        @pl.when(chip == 2)
        def _():
            gather.complete(2)

        @pl.when(chip == 3)
        def _():
            gather.pass_on(3)
            gather.complete(3)

        work(chip)
        for number, works in after.items():
            at_step(chip, number, *works)
        return unused

    lax.fori_loop(0, 4, one_chip, 0)
    gather.finish()


class Scatter:
    def __init__(self, team, buffers, near_sends, near_recvs, far_sends, far_recvs):
        self.whole, self.keep, self.near_from, self.near, self.far_from, self.far = buffers
        self.sems = near_sends, near_recvs, far_sends, far_recvs
        self.team = team
        self.size = self.keep.shape[1]

    def near_copy(self, chip):
        return push(
            self.near_from.at[chip],
            self.near.at[chip],
            self.sems[0].at[chip],
            self.sems[1].at[chip],
            self.team.place(1),
        )

    def far_copy(self, chip):
        return push(
            self.far_from.at[chip],
            self.far.at[chip],
            self.sems[2].at[chip],
            self.sems[3].at[chip],
            self.team.place(2 * chip),
        )

    def put(self, chip, rows):
        core = lax.rem(self.team.index, 2)
        self.whole[...] = rows
        self.near_from[chip] = self.whole[block_of(1 - core, self.size)].astype(LOW)
        self.near_copy(chip).start()
        self.keep[chip] = self.whole[block_of(core, self.size)]

    def combine(self, chip):
        self.near_copy(chip).wait_recv()
        self.far_from[chip] = (self.keep[chip] + self.near[chip].astype(WIDE)).astype(LOW)
        self.far_copy(chip).start()

    def total(self):
        self.near_copy(0).wait_recv()
        total = self.keep[0] + self.near[0].astype(WIDE)
        for chip in (1, 2, 3):
            self.far_copy(chip).wait_recv()
            total = total + self.far[chip].astype(WIDE)
        for chip in (0, 1, 2, 3):
            self.near_copy(chip).wait_send()
            if chip:
                self.far_copy(chip).wait_send()
        return total


class Quad:
    def __init__(self, part, along_near, along_far):
        self.part, self.along_near, self.along_far = part, along_near, along_far


def feed_quad(me, group):
    return Quad(2 * lax.div(me, 4) + lax.div(group, 2), (flip(me, 4), group), (me, flip(group, 2)))


def head_quad(me, group):
    return Quad(
        2 * lax.rem(group, 2) + lax.div(group, 2), (me, flip(group, 1)), (me, flip(group, 2))
    )


def line_place(part):
    return 2 * lax.rem(part, 2) + lax.div(part, 2)


class QuadGather:
    def __init__(self, quad, part_of, sends, recvs):
        self.part_of, self.sends, self.recvs = part_of, sends, recvs
        self.part, self.along_near, self.along_far = quad.part, quad.along_near, quad.along_far

    def copy(self, way):
        part = self.part_of(flip(self.part, 1) if way == 3 else self.part)
        device = self.along_far if way == 1 else self.along_near
        return push(part, part, self.sends.at[way], self.recvs.at[way], device)

    def start_near(self):
        self.copy(2).start()

    def start_far(self):
        self.copy(1).start()

    def start(self):
        self.start_far()
        self.start_near()

    def pass_on(self):
        self.copy(1).wait_recv()
        self.copy(3).start()

    def land(self):
        self.copy(2).wait_recv()
        self.copy(3).wait_recv()

    def finish(self):
        for way in (1, 2, 3):
            self.copy(way).wait_send()


class QuadScatter:
    def __init__(self, quad, part_of, landing, sends, recvs):
        self.part_of, self.landing, self.sends, self.recvs = part_of, landing, sends, recvs
        self.part, self.along_near, self.along_far = quad.part, quad.along_near, quad.along_far

    def copy(self, slot):
        return push(
            self.part_of(flip(self.part, (2, 3, 1)[slot])),
            self.landing.at[slot],
            self.sends.at[slot],
            self.recvs.at[slot],
            self.along_far if slot == 2 else self.along_near,
        )

    def start_far(self):
        self.copy(1).start()

    def start_near(self):
        self.copy(0).start()

    def start(self):
        self.start_far()
        self.start_near()

    def total(self):
        total = self.part_of(self.part)[...].astype(WIDE)
        return total + self.landing[0].astype(WIDE) + self.landing[2].astype(WIDE)

    def pass_on(self):
        self.copy(1).wait_recv()
        part = self.part_of(flip(self.part, 1))
        part[...] = (part[...].astype(WIDE) + self.landing[1].astype(WIDE)).astype(LOW)
        self.copy(2).start()

    def land(self):
        self.copy(0).wait_recv()
        self.copy(2).wait_recv()

    def finish(self):
        for slot in (0, 1, 2):
            self.copy(slot).wait_send()


def chip_of(team, chip):
    here = lax.div(team.index, 2)
    if isinstance(chip, int):
        return flip(here, chip)
    column = lax.rem(lax.rem(here, 2) + lax.rem(chip, 2), 2)
    row = lax.rem(lax.div(here, 2) + lax.div(chip, 2), 2)
    return 2 * row + column


def turn_rows(values, cosine, sine):
    half = HEAD_DIM // 2
    pieces = []
    for start in range(0, values.shape[0], HEAD_DIM):
        first, second = values[start : start + half], values[start + half : start + HEAD_DIM]
        pieces += [first * cosine - second * sine, second * cosine + first * sine]
    return jnp.concatenate(pieces, axis=0)


def turned(eye, values):
    size = min(values.shape[1], eye.shape[0])
    rows = [
        dot_turned(eye[:size, :size], values[:, start : start + size]).astype(LOW)
        for start in range(0, values.shape[1], size)
    ]
    return rows[0] if len(rows) == 1 else jnp.concatenate(rows, axis=0)


def thirds(values):
    first = values.astype(LOW).astype(WIDE)
    second = (values - first).astype(LOW).astype(WIDE)
    return first, second, values - first - second


def pick(row, choices):
    result = jnp.zeros(row.shape, WIDE)
    for number, choice in choices.items():
        result = jnp.where(row == number, choice, result)
    return result


def norm_rows(values):
    scale = lax.rsqrt(jnp.mean(values * values, axis=-1, keepdims=True) + NORM_EPS)
    return values * scale, scale


def feed_block(block):
    y, x, core, far_z, near_z = (block // 16, block // 8 % 2, block // 4 % 2, block // 2 % 2, block % 2)
    return 4 * near_z + 2 * x + core, 2 * y + far_z


def layer_kernel(seq, batch, ins, outs, mem):
    me, group = lax.axis_index("seq"), lax.axis_index("batch")
    rows = ins.inputs.shape[0]
    length = rows * seq
    pair = 2 * rows
    share = ins.attend.shape[1]
    wide_columns = ins.expand.shape[2] // D
    hidden_width = mem.reduce_all.shape[0] * mem.reduce_all.shape[1]
    blocks = ins.expand.shape[2] // LANES
    heads, feeds = head_team(me, group), feed_team(me, group)
    head_four, feed_four = head_quad(me, group), feed_quad(me, group)
    quad = feed_four.part

    staged = [(ins.attend.at[which], mem.keep.at[0, block_of(which, share)]) for which in range(3)]
    staged.append((ins.output, mem.keep.at[0, block_of(3, share)]))
    staged.append((ins.reduce, mem.keep.at[1]))
    for which in range(2):
        for block in range(wide_columns):
            columns = slice(block * D, (block + 1) * D)
            staged.append(
                (ins.expand.at[which, :, columns], mem.keep.at[2 + which, block_of(block, share)])
            )
    staged = [
        pltpu.make_async_copy(source, target, mem.stage_sem.at[number])
        for number, (source, target) in enumerate(staged)
    ]
    for copy in staged:
        copy.start()
    barrier = pltpu.get_barrier_semaphore()
    for mask in range(1, seq):
        pl.semaphore_signal(barrier, inc=1, device_id=(flip(me, mask), group), device_id_type=MESH)
    for step in range(1, batch):
        pl.semaphore_signal(
            barrier, inc=1, device_id=(me, lax.rem(group + step, batch)), device_id_type=MESH
        )
    for mask in (5, 6, 7):
        pl.semaphore_signal(barrier, inc=1, device_id=feeds.place(mask), device_id_type=MESH)

    square = (pair, pair)
    mem.eye[...] = jnp.where(
        lax.broadcasted_iota(jnp.int32, square, 0) == lax.broadcasted_iota(jnp.int32, square, 1), 1.0, 0.0
    ).astype(LOW)
    position = me * rows + lax.broadcasted_iota(jnp.int32, (1, rows), 1)
    inside = position < ins.lengths[0]
    scored = jnp.logical_and(inside, ins.observed[...] == 1).astype(WIDE)
    variate = ins.variates[...].astype(WIDE)
    turns = ins.turns.shape[0]
    mem.facts_own[:turns] = ins.turns[...]
    mem.facts_own[turns:] = jnp.concatenate(
        [jnp.where(inside, variate, -1.0), variate, scored, jnp.zeros((5, rows), WIDE)], axis=0
    )
    mem.scored[...] = jnp.broadcast_to(scored, (rows, rows)).T
    for copy in staged:
        copy.wait()
    for which in range(3):
        mem.attend_low[which] = mem.keep[0, block_of(which, share)].astype(LOW)
    pl.semaphore_wait(barrier, seq + batch + 1)

    masks = (6, 7, 4, 5, 2, 3, 1)

    def start_attend_columns():
        copies = []
        for mask in masks:
            copy = push(
                mem.attend_low.at[:, :, block_of(heads.at(mask), LANES)],
                mem.attend_all.at[:, me, group],
                mem.column_send.at[0, mask],
                mem.column_recv.at[0, mask],
                heads.place(mask),
            )
            copy.start()
            copies.append(copy)
        mem.attend_all[:, me, group] = mem.attend_low[:, :, block_of(me, LANES)]
        return copies

    def start_expand_columns():
        copies = []
        for mask in masks:
            copy = push(
                mem.expand_low.at[:, feeds.at(mask)],
                mem.expand_all.at[:, me, group],
                mem.column_send.at[1, mask],
                mem.column_recv.at[1, mask],
                feeds.place(mask),
            )
            copy.start()
            copies.append(copy)
        mem.expand_all[:, me, group] = mem.expand_low[:, feeds.index]
        return copies

    def expand_part_of(array, which):
        def part_of(part):
            return array.at[which, pl.ds(4 * lax.div(part, 2), 4), pl.ds(2 * lax.rem(part, 2), 2)]

        return part_of

    def quad_gather(four, row, part_of):
        return QuadGather(four, part_of, mem.line_send.at[row], mem.line_recv.at[row])

    def gather(team, phase, all_rows):
        return Gather(
            team,
            mem.own_rows.at[phase],
            all_rows,
            mem.gather_send.at[phase],
            mem.gather_recv.at[phase],
        )

    def scatter(team, phase):
        return Scatter(
            team,
            (mem.whole, mem.keep, mem.near_from, mem.near, mem.far_from, mem.far),
            mem.near_send.at[phase],
            mem.near_recv.at[phase],
            mem.far_send.at[phase],
            mem.far_recv.at[phase],
        )

    attend_columns = start_attend_columns()
    mem.output_full[block_of(batch * me + group, share)] = mem.keep[0, block_of(3, share)].astype(LOW)
    mem.reduce_all[quad] = mem.keep[1].astype(LOW)
    for which in range(2):
        for block in range(blocks):
            owner, part = feed_block(block)
            row, lane = divmod(block * LANES, D)
            mem.expand_low[which, owner, :, part * LANES : (part + 1) * LANES] = mem.keep[
                2 + which, block_of(row, share), lane : lane + LANES
            ].astype(LOW)
    line_output = quad_gather(
        head_four, 1, lambda part: mem.output_full.at[block_of(batch * me + line_place(part), share)]
    )
    line_output.start()
    unit_one, scale_one = norm_rows(ins.inputs[...].astype(WIDE))
    mem.own_rows[0] = (unit_one * ins.gains[0:1, :]).astype(LOW)
    facts = Gather(heads, mem.facts_own, mem.facts_all, mem.facts_send, mem.facts_recv)
    facts.start()
    for copy in attend_columns:
        copy.wait_recv()
    line_attend = quad_gather(head_four, 0, lambda part: mem.attend_all.at[:, :, line_place(part)])
    line_attend.start()
    acts = gather(heads, 0, mem.act_one)
    acts.start()
    for chip in (1, 2, 3):
        facts.pass_on(chip)
    for chip in (0, 1, 2, 3):
        facts.complete(chip)
    facts.finish()
    step_rows = mem.facts_own.shape[0]
    half = HEAD_DIM // 2
    count = jnp.zeros((8, LANES), WIDE)
    for slot in range(seq):
        columns = slice(slot * rows, (slot + 1) * rows)
        start = slot * step_rows
        mem.cosine[:, columns] = mem.facts_all[start : start + half]
        mem.sine[:, columns] = mem.facts_all[start + half : start + 2 * half]
        labels = mem.facts_all[start + 2 * half : start + 2 * half + 8]
        mem.labels[:, columns] = labels
        count = count + labels
    mem.count[group] = count
    count_copies = []
    for step in range(1, batch):
        copy = push(
            mem.count.at[group],
            mem.count.at[group],
            mem.count_send.at[step],
            mem.count_recv.at[step],
            (me, lax.rem(group + step, batch)),
        )
        copy.start()
        count_copies.append(copy)

    def mark(block, unused):
        span = block_of(block, pair)
        row = lax.broadcasted_iota(jnp.int32, (HEAD_DIM, pair), 0)
        third = lax.div(row, VARIATES)
        variate = lax.rem(row, VARIATES).astype(WIDE)
        key_label, query_label = mem.labels[0:1, span], mem.labels[1:2, span]
        ones = jnp.ones((1, pair), WIDE)
        last = 3 * VARIATES
        hidden_keys = (key_label < 0.0).astype(WIDE)
        mem.key_marks[:, span] = jnp.where(
            third < 3,
            (key_label == variate).astype(WIDE),
            pick(row, {last: ones, last + 1: ones, last + 2: ones, last + 3: hidden_keys}),
        ).astype(LOW)
        query_marks = (query_label == variate).astype(WIDE)
        sum_marks = jnp.where(row < VARIATES, query_marks, pick(row, {VARIATES: ones})).astype(LOW)
        for head in range(HEADS_HERE):
            mem.query_back[head, HEAD_DIM:, span] = sum_marks
            number = me * HEADS_HERE + head
            other = jnp.full((HEAD_DIM, pair), ins.bias[1, number], WIDE)
            more = thirds(jnp.full((HEAD_DIM, pair), ins.bias[0, number], WIDE) - other)
            other = thirds(other)
            mem.query_turned[head, HEAD_DIM:, span] = jnp.where(
                third < 3,
                query_marks * jnp.where(third == 0, more[0], jnp.where(third == 1, more[1], more[2])),
                pick(row, {last: other[0], last + 1: other[1], last + 2: other[2], last + 3: MASKED}),
            ).astype(LOW)
        return unused

    lax.fori_loop(0, length // pair, mark, 0)
    acts.pass_on(1)
    acts.pass_on(2)
    line_output.pass_on()
    line_output.land()
    outputs = Gather(heads, None, mem.output_full, mem.output_send, mem.output_recv)
    outputs.start()
    acts.pass_on(3)
    line_attend.pass_on()
    for chip in range(4):
        acts.complete(chip)
    acts.finish()

    expand_columns = start_expand_columns()
    line_reduce = quad_gather(feed_four, 4, lambda part: mem.reduce_all.at[part])
    line_reduce.start_far()
    line_expand = [
        quad_gather(feed_four, 2 + which, expand_part_of(mem.expand_all, which)) for which in range(2)
    ]
    line_attend.land()
    line_reduce.start_near()

    def attend_matrix(which):
        return mem.attend_all[which].reshape(D, LANES)

    def project(block, unused):
        span = block_of(block, pair)
        products = dot_turned(mem.attend_turned[...], mem.act_one[span, :])
        cosine, sine = mem.cosine[:, span], mem.sine[:, span]
        query = turn_rows(products[:LANES], cosine, sine).astype(LOW)
        query = (query.astype(WIDE) * HEAD_DIM ** (-0.5)).astype(LOW)
        key = turn_rows(products[LANES : 2 * LANES], cosine, sine).astype(LOW)
        value = products[2 * LANES :].astype(LOW)
        mem.key_turned[:, span] = key
        mem.value_turned[:, span] = value

        for head in range(HEADS_HERE):
            features = slice(head * HEAD_DIM, (head + 1) * HEAD_DIM)
            mem.query_turned[head, :HEAD_DIM, span] = query[features]
            mem.query_back[head, :HEAD_DIM, span] = query[features]
            whole = jnp.concatenate([key[features], mem.key_marks[:, span]], axis=0)
            mem.key_heads[head, span, :] = turned(mem.eye, whole)
        return unused

    for copy in expand_columns:
        copy.wait_recv()
    line_expand[0].start_far()
    line_expand[0].start_near()
    for which in range(3):
        for start in range(0, D, pair):
            piece = attend_matrix(which)[start : start + pair]
            mem.attend_turned[block_of(which, LANES), start : start + pair] = turned(mem.eye, piece)
    lax.fori_loop(0, length // pair, project, 0)
    line_expand[1].start_far()

    core = lax.rem(me, 2)

    def mixed_copy(chip, which):
        other = 2 * chip_of(heads, chip) + which
        slot = 2 * chip + lax.rem(which + core, 2)
        return push(
            mem.mixed_out.at[block_of(other, rows)],
            mem.mixed_rows.at[:, block_of(me, LANES)],
            mem.mixed_send.at[slot],
            mem.mixed_recv.at[slot],
            (other, group),
        )

    def attend_block(chip):
        columns = block_of(chip_of(heads, chip), pair)
        for head in range(HEADS_HERE):
            span = slice(head * HEAD_DIM, (head + 1) * HEAD_DIM)
            scores = dot(mem.key_heads[head], mem.query_turned[head, :, columns])
            top = jnp.floor(jnp.max(scores, axis=0, keepdims=True))
            powers = jnp.exp(scores - top)
            probs = powers * (1.0 / jnp.sum(powers, axis=0, keepdims=True))
            rounded = probs.astype(LOW)
            mem.probs[head, :, columns] = rounded
            residue = (probs - rounded.astype(WIDE)).astype(LOW)
            coarse = dot(mem.value_turned[span, :], rounded)
            mem.exact[span, columns] = coarse + dot(mem.value_turned[span, :], residue)
            mem.mixed_wide[span, :] = coarse
        mixed = mem.mixed_wide[...].astype(LOW)
        mem.mixed_turned[:, columns] = mixed
        mem.mixed_out[columns, :] = turned(mem.eye, mixed)

    def attend_step(step, unused):
        chip = lax.rem(step + 1, 4)
        attend_block(chip)
        for which in range(2):

            @pl.when(jnp.logical_or(chip > 0, core != which))
            def _():
                mixed_copy(chip, which).start()

        at_step(step, 0, lambda: outputs.pass_on(1), lambda: outputs.pass_on(2))
        at_step(step, 1, lambda: outputs.pass_on(3))
        return unused

    lax.fori_loop(0, 4, attend_step, 0)
    line_expand[1].start_near()
    mem.mixed_rows[:, block_of(me, LANES)] = mem.mixed_out[block_of(me, rows), :]
    for chip in range(4):
        outputs.complete(chip)
    outputs.finish()

    def wait_pieces(copy):
        for mask in range(1, seq):
            copy(mask).wait()

    def mixed_wait(mask):
        other = heads.at(mask)
        return push(
            mem.mixed_out.at[block_of(other, rows)],
            mem.mixed_rows.at[:, block_of(other, LANES)],
            mem.mixed_send.at[mask],
            mem.mixed_recv.at[mask],
            (other, group),
        )

    wait_pieces(mixed_wait)
    middle = ins.inputs[...].astype(WIDE) + dot(mem.mixed_rows[...], mem.output_full[...])
    mem.middle[...] = middle
    unit_two, scale_two = norm_rows(middle)
    mem.own_rows[1] = (unit_two * ins.gains[1:2, :]).astype(LOW)
    acts = gather(feeds, 1, mem.act_two)
    acts.start((2, 4, 1))
    line_reduce.pass_on()
    line_expand[0].pass_on()

    def split_heads(block, unused):
        span = block_of(block, pair)
        row = lax.broadcasted_iota(jnp.int32, (HEAD_DIM, pair), 0)
        value_marks = jnp.where(row < 3, 1.0, 0.0).astype(LOW)
        for head in range(HEADS_HERE):
            features = slice(head * HEAD_DIM, (head + 1) * HEAD_DIM)
            value = mem.value_turned[features, span]
            whole = jnp.concatenate([value, value_marks], axis=0)
            mem.value_heads[head, span, :] = turned(mem.eye, whole)
        return unused

    lax.fori_loop(0, length // pair, split_heads, 0)
    line_expand[0].land()

    def expand_matrix(which):
        return mem.expand_all[which].reshape(D, hidden_width)

    def reduce_matrix():
        return mem.reduce_all[...].reshape(hidden_width, D)

    def feed_gate(chip):
        span = block_of(chip_of(feeds, chip), pair)
        mem.by_gate[span, :] = dot(mem.act_two[span, :], expand_matrix(0))

    def feed_up(chip, unused=0):
        span = block_of(chip_of(feeds, chip), pair)
        gate = mem.by_gate[span, :]
        up = dot(mem.act_two[span, :], expand_matrix(1))
        sigmoid = 1.0 / (1.0 + jnp.exp(-gate))
        swish = gate * sigmoid
        mem.by_up[span, :] = swish
        mem.by_gate[span, :] = up * sigmoid * (1.0 + gate * (1.0 - sigmoid))
        mem.hidden[span, :] = (swish * up).astype(LOW)
        return unused

    each_chip(
        acts,
        feed_gate,
        {
            0: [line_expand[1].pass_on],
            2: [line_expand[1].land, lambda: lax.fori_loop(0, 3, feed_up, 0)],
            3: [lambda: lax.fori_loop(3, 4, feed_up, 0)],
        },
    )
    line_reduce.land()
    sums = scatter(feeds, 1)

    def feed_down(step, unused):
        chip = lax.rem(step + 1, 4)
        span = block_of(chip_of(feeds, chip), pair)
        sums.put(chip, dot(mem.hidden[span, :], reduce_matrix()))
        at_step(step, 1, lambda: sums.combine(1))
        at_step(step, 2, lambda: sums.combine(2))
        return unused

    lax.fori_loop(0, 4, feed_down, 0)
    sums.combine(3)

    def turn_feed(block, unused):
        span = block_of(block, pair)
        mem.hidden_turned[:, span] = turned(mem.eye, mem.hidden[span, :])
        mem.act_two_turned[:, span] = turned(mem.eye, mem.act_two[span, :])
        return unused

    lax.fori_loop(0, length // pair, turn_feed, 0)
    output = mem.middle[...] + sums.total()
    outs.layer_output[...] = output
    for copy in count_copies:
        copy.wait()
    count_all = jnp.sum(
        mem.count[0, 2:3] + mem.count[1, 2:3] + mem.count[2, 2:3] + mem.count[3, 2:3],
        axis=1,
        keepdims=True,
    )
    error = jnp.where(mem.scored[:, 0:1] > 0.0, output - ins.teacher[...].astype(WIDE), 0.0)
    mem.squares[1:2, :] = jnp.sum(error * error, axis=0, keepdims=True)
    grad_out = error * (2.0 / (count_all * D))
    mem.grad_own[...] = grad_out
    mem.own_rows[2] = grad_out.astype(LOW)
    acts = gather(feeds, 2, mem.branch)
    acts.start((2, 4, 1))

    def turn_acts(block, unused):
        span = block_of(block, pair)
        mem.act_one_turned[:, span] = turned(mem.eye, mem.act_one[span, :])
        return unused

    lax.fori_loop(0, length // pair, turn_acts, 0)

    sums = scatter(feeds, 2)

    def feed_back(chip):
        span = block_of(chip_of(feeds, chip), pair)
        grad_hidden = dot_turned(mem.branch[span, :], reduce_matrix())
        grad_gate = (grad_hidden * mem.by_gate[span, :]).astype(LOW)
        grad_up = (grad_hidden * mem.by_up[span, :]).astype(LOW)
        mem.grad_gate[span, :] = grad_gate
        mem.grad_up[span, :] = grad_up
        sums.put(
            chip,
            dot_turned(
                jnp.concatenate([grad_gate, grad_up], axis=1),
                jnp.concatenate([expand_matrix(0), expand_matrix(1)], axis=1),
            ),
        )

    each_chip(acts, feed_back, {2: [lambda: sums.combine(1)], 3: [lambda: sums.combine(2)]})

    def quad_scatter(four, row, part_of, landing):
        return QuadScatter(four, part_of, landing, mem.back_send.at[row], mem.back_recv.at[row])

    def reduce_grad(part, unused):
        mem.reduce_grad[part] = dot(
            mem.hidden_turned[block_of(part, rows), :], mem.branch[...]
        ).astype(LOW)
        at_step(part, 0, lambda: sums.combine(3))
        return unused

    lax.fori_loop(0, batch, reduce_grad, 0)
    back_reduce = quad_scatter(
        feed_four, 0, lambda part: mem.reduce_grad.at[part], mem.reduce_land
    )
    back_reduce.start_far()

    def expand_grad(which):
        grads = (mem.grad_gate, mem.grad_up)[which]

        def one_block(block, unused):
            products = dot(mem.act_two_turned[block_of(block, pair), :], grads[...]).astype(LOW)
            mem.expand_grad[which, pl.ds(2 * block, 2)] = products.reshape(
                2, batch, share, hidden_width
            )
            return unused

        lax.fori_loop(0, seq // 2, one_block, 0)
        line = quad_scatter(
            feed_four, 1 + which, expand_part_of(mem.expand_grad, which), mem.expand_land.at[which]
        )
        return line

    back_expand = []
    back_expand.append(expand_grad(0))
    back_expand[0].start_far()
    grad_act = sums.total()
    unit_two, scale_two = norm_rows(mem.middle[...])
    gain = ins.gains[1:2, :]
    grad_unit = grad_act * gain
    mem.gains[1:2, :] = jnp.sum(grad_act * unit_two, axis=0, keepdims=True)
    grad_middle = mem.grad_own[...] + scale_two * (
        grad_unit - unit_two * jnp.mean(grad_unit * unit_two, axis=-1, keepdims=True)
    )
    mem.grad_own[...] = grad_middle
    mem.own_rows[3] = grad_middle.astype(LOW)
    grad_mixed = dot_turned(mem.output_full[...], mem.own_rows[3]).astype(LOW)
    mem.grad_mixed_out[...] = grad_mixed.reshape(seq, LANES, rows)

    def grad_copy(mask, back=False):
        return push(
            mem.grad_mixed_out.at[heads.at(mask)],
            mem.grad_mixed.at[:, block_of(heads.at(mask) if back else me, rows)],
            mem.mixed_send.at[8 + mask],
            mem.mixed_recv.at[8 + mask],
            heads.place(mask),
        )

    for mask in masks:
        grad_copy(mask).start()
    mem.grad_mixed[:, block_of(me, rows)] = mem.grad_mixed_out[me]
    back_reduce.pass_on()
    back_expand.append(expand_grad(1))
    back_expand[1].start_far()

    wait_pieces(lambda mask: grad_copy(mask, True))
    acts = gather(heads, 3, mem.grad_attn)
    acts.start()
    back_reduce.start_near()
    back_expand[0].start_near()
    back_attend = [
        quad_scatter(
            head_four,
            4 + which,
            lambda part, which=which: mem.attend_grad.at[which, :, line_place(part)],
            mem.attend_land.at[which],
        )
        for which in range(3)
    ]

    def attend_grad(which):
        def one_block(block, unused):
            products = dot(mem.act_one_turned[block_of(block, pair), :], mem.grad_project[which])
            mem.attend_grad[which, pl.ds(2 * block, 2)] = products.astype(LOW).reshape(
                2, batch, share, LANES
            )
            return unused

        lax.fori_loop(0, length // pair, one_block, 0)
        back_attend[which].start()

    lane = lax.broadcasted_iota(jnp.int32, (pair, LANES), 1)

    def grad_rows(block, unused):
        span = block_of(block, pair)
        whole = turned(mem.eye, mem.grad_mixed[:, span])
        for head in range(HEADS_HERE):
            mem.grad_heads[head, span, :] = jnp.where(
                lax.div(lane, HEAD_DIM) == head, whole, jnp.zeros_like(whole)
            )
        return unused

    lax.fori_loop(0, length // pair, grad_rows, 0)

    def value_back(block, unused):
        span = block_of(block, pair)
        total = dot(mem.probs[0, span, :], mem.grad_heads[0])
        for head in range(1, HEADS_HERE):
            total = total + dot(mem.probs[head, span, :], mem.grad_heads[head])
        mem.grad_project[2, span, :] = total.astype(LOW)
        return unused

    lax.fori_loop(0, length // pair, value_back, 0)
    back_expand[0].pass_on()
    attend_grad(2)

    def score_back(block, unused):
        columns = block_of(block, pair)
        row = lax.broadcasted_iota(jnp.int32, (HEAD_DIM, pair), 0)
        grads = mem.grad_mixed[:, columns]
        delta = grads.astype(WIDE) * mem.exact[:, columns]
        for head in range(HEADS_HERE):
            span = slice(head * HEAD_DIM, (head + 1) * HEAD_DIM)
            pieces = thirds(-jnp.sum(delta[span], axis=0, keepdims=True))
            marks = pick(row, dict(enumerate(pieces))).astype(LOW)
            change = dot(mem.value_heads[head], jnp.concatenate([grads[span], marks], axis=0))
            mem.probs[head, :, columns] = (mem.probs[head, :, columns].astype(WIDE) * change).astype(LOW)
        return unused

    lax.fori_loop(0, length // pair, score_back, 0)
    back_expand[1].start_near()
    mem.bias_sums[...] = jnp.zeros_like(mem.bias_sums)
    scale = HEAD_DIM ** (-0.5)

    def project_grads(block, unused):
        span = block_of(block, pair)
        cosine, sine = mem.cosine[:, span], -mem.sine[:, span]
        queries, keys = [], []
        for head in range(HEADS_HERE):
            features = slice(head * HEAD_DIM, (head + 1) * HEAD_DIM)
            queries.append(dot(mem.key_turned[features, :], mem.probs[head, :, span]) * scale)
            sums = dot_turned(mem.query_back[head], mem.probs[head, span, :])
            keys.append(sums[:HEAD_DIM])
            by_variate = sums[HEAD_DIM : HEAD_DIM + VARIATES]
            same = by_variate * mem.key_marks[:VARIATES, span].astype(WIDE)
            mem.bias_sums[head : head + 1, :] += jnp.sum(same, axis=0, keepdims=True)
            total = sums[HEAD_DIM + VARIATES : HEAD_DIM + VARIATES + 1]
            mem.bias_sums[HEADS_HERE + head : HEADS_HERE + head + 1, :] += total
        queries = turn_rows(jnp.concatenate(queries, axis=0), cosine, sine)
        mem.grad_project[0, span, :] = turned(mem.eye, queries.astype(LOW))
        keys = turn_rows(jnp.concatenate(keys, axis=0), cosine, sine)
        mem.grad_project[1, span, :] = turned(mem.eye, keys.astype(LOW))
        return unused

    lax.fori_loop(0, length // pair, project_grads, 0)
    back_expand[1].pass_on()
    attend_grad(0)
    acts.pass_on(1)
    acts.pass_on(2)
    sums = scatter(heads, 3)

    def project_back(step, unused):
        chip = lax.rem(step + 1, 4)
        span = block_of(chip_of(heads, chip), pair)
        grads = [mem.grad_project[which, span, :] for which in range(3)]
        weights = [attend_matrix(which) for which in range(3)]
        sums.put(chip, dot_turned(jnp.concatenate(grads, axis=1), jnp.concatenate(weights, axis=1)))
        at_step(step, 1, lambda: sums.combine(1))
        at_step(step, 2, lambda: sums.combine(2))
        return unused

    lax.fori_loop(0, 4, project_back, 0)
    sums.combine(3)
    attend_grad(1)
    acts.pass_on(3)
    for chip in range(4):
        acts.complete(chip)
    acts.finish()
    mem.output_grad[...] = (
        dot(mem.mixed_turned[...], mem.grad_attn[...]).astype(LOW).reshape(mem.output_grad.shape)
    )
    back_output = quad_scatter(
        head_four, 3, lambda part: mem.output_grad.at[line_place(part)], mem.output_land
    )
    back_output.start()
    for which in (2, 0):
        back_attend[which].pass_on()

    column_copies = []
    mem.squares[0:1, :] = jnp.zeros((1, D), WIDE)

    def add_squares(total):
        flat = total.reshape(-1, total.shape[-1])
        width = flat.shape[1]
        mem.squares[0:1, :width] += jnp.sum(flat * flat, axis=0, keepdims=True)

    def store_whole(total, out):
        out[...] = total
        add_squares(total)

    back_reduce.land()
    store_whole(back_reduce.total(), outs.reduce_share)
    def expand_shares(which):
        back_expand[which].land()
        own = expand_part_of(mem.expand_grad, which)(quad)

        def one_block(block, unused):
            total = (
                own[block].astype(WIDE)
                + mem.expand_land[which, 0, block].astype(WIDE)
                + mem.expand_land[which, 2, block].astype(WIDE)
            )
            mem.expand_part[which, block] = total.astype(LOW)
            add_squares(total)
            return unused

        lax.fori_loop(0, 4, one_block, 0)
        for mask in masks:
            other = feeds.at(mask)
            copy = push(
                mem.expand_part.at[which, lax.rem(other, 4), lax.div(other, 4)],
                mem.expand_share.at[which, feeds.index],
                mem.share_send.at[which, mask],
                mem.share_recv.at[which, mask],
                feeds.place(mask),
            )
            copy.start()
            column_copies.append(copy)
        mem.expand_share[which, feeds.index] = mem.expand_part[
            which, lax.rem(feeds.index, 4), lax.div(feeds.index, 4)
        ]

    expand_shares(0)
    back_attend[1].pass_on()
    expand_shares(1)

    def attend_shares(which):
        back_attend[which].land()
        total = back_attend[which].total()
        mem.attend_part[which] = total.astype(LOW)
        add_squares(total)

    attend_shares(2)
    grad_act = sums.total()
    unit_one, scale_one = norm_rows(ins.inputs[...].astype(WIDE))
    gain = ins.gains[0:1, :]
    grad_unit = grad_act * gain
    mem.gains[0:1, :] = jnp.sum(grad_act * unit_one, axis=0, keepdims=True)
    grad_input = mem.grad_own[...] + scale_one * (
        grad_unit - unit_one * jnp.mean(grad_unit * unit_one, axis=-1, keepdims=True)
    )
    outs.input_gradient[...] = grad_input * (count_all * D)
    outs.count[...] = jnp.broadcast_to(count_all, (8, LANES))

    back_output.pass_on()
    for which in range(2):
        attend_shares(which)
    for mask in masks:
        copy = push(
            mem.attend_part.at[:, heads.at(mask)],
            outs.attend_share.at[:, :, block_of(me, LANES)],
            mem.share_send.at[2, mask],
            mem.share_recv.at[2, mask],
            heads.place(mask),
        )
        copy.start()
        column_copies.append(copy)
    outs.attend_share[:, :, block_of(me, LANES)] = mem.attend_part[:, me]
    back_output.land()
    store_whole(back_output.total(), outs.output_share)

    lane = lax.broadcasted_iota(jnp.int32, (1, LANES), 1)
    lines = [
        mem.gains[which : which + 1, start : start + LANES]
        for which in range(2)
        for start in range(0, D, LANES)
    ]
    bias_line = jnp.zeros((1, LANES), WIDE)
    for row in range(2 * HEADS_HERE):
        place = row // HEADS_HERE * HEADS + me * HEADS_HERE + row % HEADS_HERE
        line = mem.bias_sums[row : row + 1, :]
        if row >= HEADS_HERE:
            line = line - mem.bias_sums[row - HEADS_HERE : row - HEADS_HERE + 1, :]
        amount = jnp.sum(line, axis=1, keepdims=True)
        bias_line = bias_line + jnp.where(lane == place, amount, 0.0)
    amounts = jnp.sum(mem.squares[0:2, :], axis=1, keepdims=True)
    amount_line = jnp.where(lane == 0, amounts[0:1], 0.0) + jnp.where(lane == 1, amounts[1:2], 0.0)
    lines += [bias_line, amount_line, jnp.zeros((6, LANES), WIDE)]
    mem.plane_totals[me] = jnp.concatenate(lines, axis=0)
    plane_copies = []
    for mask in masks:
        copy = push(
            mem.plane_totals.at[me],
            mem.plane_totals.at[me],
            mem.total_send.at[0, mask],
            mem.total_recv.at[0, mask],
            (flip(me, mask), group),
        )
        copy.start()
        plane_copies.append(copy)
    for copy in column_copies[: 2 * len(masks)]:
        copy.wait()
    for which in range(2):
        for block in range(blocks):
            owner, part = feed_block(block)
            outs.expand_share[which, :, block * LANES : (block + 1) * LANES] = mem.expand_share[
                which, owner, :, part * LANES : (part + 1) * LANES
            ]
    for copy in plane_copies:
        copy.wait()
    mem.line_totals[group] = jnp.sum(mem.plane_totals[...], axis=0)
    total_copies = []
    for step in range(1, batch):
        copy = push(
            mem.line_totals.at[group],
            mem.line_totals.at[group],
            mem.total_send.at[1, step],
            mem.total_recv.at[1, step],
            (me, lax.rem(group + step, batch)),
        )
        copy.start()
        total_copies.append(copy)
    for copy in total_copies:
        copy.wait()
    outs.totals[...] = jnp.sum(mem.line_totals[...], axis=0)
    for copy in column_copies[2 * len(masks) :]:
        copy.wait()
    for copies in (attend_columns, expand_columns):
        for copy in copies:
            copy.wait_send()
    for line in [line_attend, line_output, line_reduce] + line_expand:
        line.finish()
    for line in [back_output, back_reduce] + back_attend + back_expand:
        line.finish()


def call_layer(seq, batch, inputs, teacher, lengths, variates, observed, turns, bias, gains, attend, output, expand, reduce):
    rows, share, hidden = inputs.shape[0], attend.shape[1], expand.shape[2] // seq
    length, pair, chips = rows * seq, 2 * rows, seq // 2
    low = lambda *shape: pltpu.VMEM(shape, LOW)
    wide = lambda *shape: pltpu.VMEM(shape, WIDE)
    sems = lambda *shape: pltpu.SemaphoreType.DMA(shape)
    in_names = ["inputs", "teacher", "lengths", "variates", "observed", "turns", "bias", "gains"]
    in_names += ["attend", "output", "expand", "reduce"]
    outs = dict(
        layer_output=((rows, D), WIDE),
        input_gradient=((rows, D), WIDE),
        totals=((TOTAL_ROWS, LANES), WIDE),
        count=((8, LANES), WIDE),
        attend_share=((3, share, D), LOW),
        output_share=((output.shape[0], D), WIDE),
        expand_share=((2, share, hidden * seq), LOW),
        reduce_share=((reduce.shape[0], D), WIDE),
    )
    scratch = dict(
        gains=wide(2, D),
        squares=wide(8, D),
        plane_totals=wide(seq, TOTAL_ROWS, LANES),
        line_totals=wide(batch, TOTAL_ROWS, LANES),
        attend_low=low(3, share, D),
        expand_low=low(2, seq, share, hidden),
        attend_all=low(3, seq, batch, share, LANES),
        output_full=low(D, D),
        expand_all=low(2, seq, batch, share, hidden),
        reduce_all=low(batch, reduce.shape[0], D),
        own_rows=low(4, rows, D),
        act_one=low(length, D),
        act_two=low(length, D),
        branch=low(length, D),
        grad_attn=low(length, D),
        facts_own=wide(turns.shape[0] + 8, LANES),
        facts_all=wide(seq * (turns.shape[0] + 8), LANES),
        scored=wide(rows, LANES),
        cosine=wide(HEAD_DIM // 2, length),
        sine=wide(HEAD_DIM // 2, length),
        labels=wide(8, length),
        key_marks=low(HEAD_DIM, length),
        count=wide(batch, 8, LANES),
        query_turned=low(HEADS_HERE, LANES, length),
        key_turned=low(LANES, length),
        value_turned=low(LANES, length),
        key_heads=low(HEADS_HERE, length, LANES),
        value_heads=low(HEADS_HERE, length, LANES),
        query_back=low(HEADS_HERE, LANES, length),
        attend_turned=low(3 * LANES, D),
        eye=low(pair, pair),
        grad_heads=low(HEADS_HERE, length, LANES),
        grad_mixed=low(LANES, length),
        grad_mixed_out=low(seq, LANES, rows),
        probs=low(HEADS_HERE, length, length),
        mixed_out=low(length, LANES),
        mixed_rows=low(rows, D),
        hidden_turned=low(hidden, length),
        act_two_turned=low(D, length),
        exact=wide(LANES, length),
        mixed_wide=wide(LANES, pair),
        mixed_turned=low(LANES, length),
        whole=wide(pair, D),
        keep=wide(chips, rows, D),
        near_from=low(chips, rows, D),
        near=low(chips, rows, D),
        far_from=low(chips, rows, D),
        far=low(chips, rows, D),
        middle=wide(rows, D),
        grad_own=wide(rows, D),
        by_up=wide(length, hidden),
        by_gate=wide(length, hidden),
        hidden=low(length, hidden),
        grad_gate=low(length, hidden),
        grad_up=low(length, hidden),
        bias_sums=wide(8, pair),
        grad_project=low(3, length, LANES),
        act_one_turned=low(D, length),
        reduce_grad=low(batch, reduce.shape[0], D),
        expand_grad=low(2, seq, batch, share, hidden),
        output_grad=low(batch, output.shape[0], D),
        attend_grad=low(3, seq, batch, share, LANES),
        reduce_land=low(3, reduce.shape[0], D),
        expand_land=low(2, 3, 4, 2, share, hidden),
        output_land=low(3, output.shape[0], D),
        attend_land=low(3, 3, seq, share, LANES),
        expand_part=low(2, 4, 2, share, hidden),
        expand_share=low(2, seq, share, hidden),
        attend_part=low(3, seq, share, LANES),
        stage_sem=sems(5 + 2 * (expand.shape[2] // D)),
        total_send=sems(2, seq),
        total_recv=sems(2, seq),
        column_send=sems(2, seq),
        column_recv=sems(2, seq),
        line_send=sems(5, batch),
        line_recv=sems(5, batch),
        facts_send=sems(seq),
        facts_recv=sems(seq),
        gather_send=sems(4, seq),
        gather_recv=sems(4, seq),
        count_send=sems(batch),
        count_recv=sems(batch),
        near_send=sems(4, chips),
        near_recv=sems(4, chips),
        far_send=sems(4, chips),
        far_recv=sems(4, chips),
        back_send=sems(7, batch),
        back_recv=sems(7, batch),
        output_send=sems(seq),
        output_recv=sems(seq),
        mixed_send=sems(2 * seq),
        mixed_recv=sems(2 * seq),
        share_send=sems(3, seq),
        share_recv=sems(3, seq),
    )

    places = dict.fromkeys(("attend", "output", "expand", "reduce"), pl.BlockSpec(memory_space=pl.ANY))
    places["bias"] = places["lengths"] = IN_SMEM

    def kernel(*refs):
        groups, start = [], 0
        for names in (in_names, outs, scratch):
            names = list(names)
            groups.append(types.SimpleNamespace(**dict(zip(names, refs[start : start + len(names)]))))
            start += len(names)
        layer_kernel(seq, batch, *groups)

    results = pl.pallas_call(
        kernel,
        out_shape=[jax.ShapeDtypeStruct(*out) for out in outs.values()],
        in_specs=[places.get(name, IN_VMEM) for name in in_names],
        out_specs=[IN_VMEM] * len(outs),
        scratch_shapes=list(scratch.values()),
        compiler_params=pltpu.CompilerParams(
            collective_id=0, has_side_effects=True, vmem_limit_bytes=63 * MIB
        ),
        name="layer",
    )(inputs, teacher, lengths, variates, observed, turns, bias, gains, attend, output, expand, reduce)
    return types.SimpleNamespace(**dict(zip(outs, results)))


def update_kernel(
    smalls, ins, small_outs, outs, olds, shares, news, copies, passed, in_sems, out_sems
):
    totals, count, gains, gains_first, gains_second, bias, bias_first, bias_second = smalls
    order = (2, 3, 0, 1)
    comes = []
    for place, number in enumerate(order):
        pairs = list(zip(ins[4 + 3 * number : 7 + 3 * number], olds[3 * number : 3 * number + 3]))
        pairs.append((ins[number], shares[number]))
        comes.append(
            [
                pltpu.make_async_copy(source, target, in_sems.at[4 * place + part])
                for part, (source, target) in enumerate(pairs)
            ]
        )
    for copy in sum(comes, []):
        copy.start()
    through = [
        pltpu.make_async_copy(ins[16 + part], passed[part], in_sems.at[16 + part]) for part in range(2)
    ]
    for copy in through:
        copy.start()
    goes = []
    gains_total = jnp.concatenate(
        [
            jnp.concatenate([totals[row + i : row + i + 1, :] for i in range(D // LANES)], axis=1)
            for row in (0, D // LANES)
        ],
        axis=0,
    )
    row = 2 * D // LANES
    bias_total = jnp.concatenate(
        [totals[row : row + 1, :HEADS], totals[row : row + 1, HEADS : 2 * HEADS]], axis=0
    )
    row += 1

    def sum_all(values):
        return jnp.sum(jnp.sum(values, axis=0, keepdims=True), axis=1, keepdims=True)

    squares = (
        totals[row : row + 1, 0:1] + sum_all(gains_total * gains_total) + sum_all(bias_total * bias_total)
    )
    grad_norm = jnp.sqrt(squares)
    clip = jnp.minimum(1.0, CLIP_NORM / grad_norm)
    small_outs[0][...] = totals[row : row + 1, 1:2] / (count[0:1, 0:1] * D)
    small_outs[1][...] = grad_norm
    rates = (RATE_ATTEND, RATE_OUTPUT, RATE_EXPAND, RATE_REDUCE)
    for place, number in enumerate(order):
        for copy in comes[place]:
            copy.wait()
        weight, first, second = olds[3 * number : 3 * number + 3]
        new, first_new, second_new = news[3 * number : 3 * number + 3]
        arrays = (new, copies[number], first_new, second_new, weight, first, second, shares[number])
        for lead in range(weight.shape[0] if weight.ndim == 3 else 1):

            def one_block(block, unused, lead=lead, arrays=arrays, rate=rates[number]):
                rows = block_of(block, 16)
                place = (lead, rows) if arrays[0].ndim == 3 else (rows,)
                old, moment, square, share = [array[place] for array in arrays[4:]]
                step = fast_step(old, moment, square, share.astype(WIDE) * clip, rate)
                arrays[0][place], arrays[2][place], arrays[3][place] = step
                arrays[1][place] = step[0].astype(LOW)
                return unused

            lax.fori_loop(0, weight.shape[-2] // 16, one_block, 0)
        for part, source in enumerate((new, copies[number], first_new, second_new)):
            copy = pltpu.make_async_copy(
                source, outs[2 + 4 * number + part], out_sems.at[2 + 4 * number + part]
            )
            copy.start()
            goes.append(copy)
        if place == 0:
            for part in range(2):
                through[part].wait()
                copy = pltpu.make_async_copy(passed[part], outs[part], out_sems.at[part])
                copy.start()
                goes.append(copy)
    for number, (old, total, rate) in enumerate(
        (
            ((gains, gains_first, gains_second), gains_total, RATE_GAINS),
            ((bias, bias_first, bias_second), bias_total, RATE_BIAS),
        )
    ):
        new, first_new, second_new = small_outs[2 + 3 * number : 5 + 3 * number]
        new[...], first_new[...], second_new[...] = adam_step(
            old[0][...], old[1][...], old[2][...], total * clip, rate, 0.0
        )
    for copy in goes:
        copy.wait()


def fast_step(weight, first, second, gradient, rate):
    first = BETA_ONE * first + (1.0 - BETA_ONE) * gradient
    second = BETA_TWO * second + ((1.0 - BETA_TWO) * gradient) * gradient
    low = jnp.sqrt(second * (1.0 / (1.0 - BETA_TWO**STEP))) + ADAM_EPS
    step = first * (rate / (1.0 - BETA_ONE**STEP)) / low
    return weight * (1.0 - rate * WEIGHT_DECAY) - step, first, second


def call_update(done, shares, smalls, olds):
    in_hbm = pl.BlockSpec(memory_space=pl.ANY)
    smalls = [done.totals, done.count] + smalls
    ins = shares + olds + [done.layer_output, done.input_gradient]
    one = jax.ShapeDtypeStruct((1, 1), WIDE)
    small_outs = [one, one] + smalls[2:]
    outs = [(done.layer_output, WIDE), (done.input_gradient, WIDE)]
    for weight in olds[::3]:
        outs += [(weight, dtype) for dtype in (WIDE, LOW, WIDE, WIDE)]
    passed = ins[-2:]
    parts = [smalls, ins, small_outs, outs, olds, shares, olds, olds[::3], passed]

    def kernel(*refs):
        groups, start = [], 0
        for part in parts:
            groups.append(refs[start : start + len(part)])
            start += len(part)
        update_kernel(*groups, *refs[start:])

    results = pl.pallas_call(
        kernel,
        out_shape=[jax.ShapeDtypeStruct(array.shape, WIDE) for array in small_outs]
        + [jax.ShapeDtypeStruct(array.shape, dtype) for array, dtype in outs],
        in_specs=[IN_VMEM] * len(smalls) + [in_hbm] * len(ins),
        out_specs=[IN_VMEM] * len(small_outs) + [in_hbm] * len(outs),
        scratch_shapes=[pltpu.VMEM(array.shape, WIDE) for array in olds]
        + [pltpu.VMEM(array.shape, array.dtype) for array in shares]
        + [pltpu.VMEM(array.shape, WIDE) for array in olds]
        + [pltpu.VMEM(array.shape, LOW) for array in olds[::3]]
        + [pltpu.VMEM(array.shape, WIDE) for array in passed]
        + [pltpu.SemaphoreType.DMA((18,)), pltpu.SemaphoreType.DMA((18,))],
        compiler_params=pltpu.CompilerParams(vmem_limit_bytes=63 * MIB),
        name="update",
    )(*smalls, *ins)
    return results[: len(small_outs)], results[len(small_outs) :]


def fast_body(
    seq,
    batch,
    inputs,
    teacher,
    lengths,
    variate_ids,
    time_ids,
    observed,
    attend_weight,
    output_weight,
    expand_weight,
    reduce_weight,
    norm_gains,
    variate_bias,
    attend_first,
    output_first,
    expand_first,
    reduce_first,
    gains_first,
    bias_first,
    attend_second,
    output_second,
    expand_second,
    reduce_second,
    gains_second,
    bias_second,
):
    half_dim = HEAD_DIM // 2
    frequency = jnp.exp(-math.log(ROPE_BASE) * jnp.arange(half_dim).astype(WIDE) / half_dim)
    angle = frequency[:, None] * time_ids.astype(WIDE)
    done = call_layer(
        seq,
        batch,
        inputs[0],
        teacher[0],
        lengths,
        variate_ids,
        observed,
        jnp.concatenate([jnp.cos(angle), jnp.sin(angle)]),
        variate_bias,
        norm_gains,
        attend_weight,
        output_weight,
        expand_weight,
        reduce_weight,
    )
    small, large = call_update(
        done,
        [done.attend_share, done.output_share, done.expand_share, done.reduce_share],
        [norm_gains, gains_first, gains_second, variate_bias, bias_first, bias_second],
        [attend_weight, attend_first, attend_second]
        + [output_weight, output_first, output_second]
        + [expand_weight, expand_first, expand_second]
        + [reduce_weight, reduce_first, reduce_second],
    )
    return (
        large[0][None],
        small[0].reshape(()),
        large[1][None],
        small[1].reshape(()),
    ) + tuple(large[2:] + small[2:])


def solution(mesh):
    seq, batch = mesh.shape["seq"], mesh.shape["batch"]
    body = functools.partial(fast_body, seq, batch) if fast_fits(seq, batch) else general_body
    in_specs = (
        P("batch", "seq", None),
        P("batch", "seq", None),
        P("batch"),
        P("batch", "seq"),
        P("batch", "seq"),
        P("batch", "seq"),
        P(None, ("seq", "batch"), None),
        P(("seq", "batch"), None),
        P(None, ("seq", "batch"), None),
        P(("seq", "batch"), None),
        P(),
        P(),
        P(None, ("seq", "batch"), None),
        P(("seq", "batch"), None),
        P(None, ("seq", "batch"), None),
        P(("seq", "batch"), None),
        P(),
        P(),
        P(None, ("seq", "batch"), None),
        P(("seq", "batch"), None),
        P(None, ("seq", "batch"), None),
        P(("seq", "batch"), None),
        P(),
        P(),
    )
    out_specs = (
        P("batch", "seq", None),
        P(),
        P("batch", "seq", None),
        P(),
        P(None, ("seq", "batch"), None),
        P(None, ("seq", "batch"), None),
        P(None, ("seq", "batch"), None),
        P(None, ("seq", "batch"), None),
        P(("seq", "batch"), None),
        P(("seq", "batch"), None),
        P(("seq", "batch"), None),
        P(("seq", "batch"), None),
        P(None, ("seq", "batch"), None),
        P(None, ("seq", "batch"), None),
        P(None, ("seq", "batch"), None),
        P(None, ("seq", "batch"), None),
        P(("seq", "batch"), None),
        P(("seq", "batch"), None),
        P(("seq", "batch"), None),
        P(("seq", "batch"), None),
        P(),
        P(),
        P(),
        P(),
        P(),
        P(),
    )
    return jax.shard_map(body, mesh=mesh, in_specs=in_specs, out_specs=out_specs, check_vma=False)
```

```python
import functools
import math
import types

import jax
import jax.numpy as jnp
import numpy as np
from jax import lax
from jax.experimental import pallas as pl
from jax.experimental.pallas import tpu as pltpu
from jax.sharding import PartitionSpec as P

D = 1024
HEADS = 16
HEAD_DIM = 64
STEP = 10


NORM_EPS = 1e-05
ROPE_BASE = 10000.0
MASKED = -1e30
CLIP_NORM = 1.0
BETA_ONE = 0.9
BETA_TWO = 0.98
ADAM_EPS = 1e-08
WEIGHT_DECAY = 0.1
RATE_ATTEND = 0.03
RATE_OUTPUT = 0.5
RATE_EXPAND = 0.03
RATE_REDUCE = 0.015
RATE_GAINS = 1.0
RATE_BIAS = 0.5


def angles(times):
    half_dim = HEAD_DIM // 2
    frequency = jnp.exp(-math.log(ROPE_BASE) * jnp.arange(half_dim).astype(jnp.float32) / half_dim)
    angle_table = times.astype(jnp.float32)[..., None] * frequency
    return (jnp.cos(angle_table)[..., None, :], jnp.sin(angle_table)[..., None, :])


def rotate(values, cos_table, sin_table):
    half_dim = values.shape[-1] // 2
    first_half = values[..., :half_dim]
    second_half = values[..., half_dim:]
    return jnp.concatenate(
        [
            first_half * cos_table - second_half * sin_table,
            second_half * cos_table + first_half * sin_table,
        ],
        axis=-1,
    )


def unrotate(values, cos_table, sin_table):
    half_dim = values.shape[-1] // 2
    first_half = values[..., :half_dim]
    second_half = values[..., half_dim:]
    return jnp.concatenate(
        [
            first_half * cos_table + second_half * sin_table,
            second_half * cos_table - first_half * sin_table,
        ],
        axis=-1,
    )


def normalize(values):
    inv_scale = lax.rsqrt(jnp.mean(values * values, axis=-1, keepdims=True) + NORM_EPS)
    return (values * inv_scale, inv_scale)


def norm_back(grad_act, unit_rows, inv_scale, gain_row):
    grad_unit = grad_act * gain_row
    return inv_scale * (
        grad_unit - unit_rows * jnp.mean(grad_unit * unit_rows, axis=-1, keepdims=True)
    )


def score_block(query_rows, query_labels, key_rows, key_labels, bias_table):
    scores = jnp.einsum(
        "ihe,jhe->hij", query_rows, key_rows, preferred_element_type=jnp.float32
    ) * HEAD_DIM ** (-0.5)
    same_var = query_labels[:, None] == key_labels[None, :]
    scores = scores + jnp.where(
        same_var[None], bias_table[0][:, None, None], bias_table[1][:, None, None]
    )
    scores = jnp.where(key_labels[None, None, :] >= 0, scores, MASKED)
    return (scores, same_var)


def block_grads(
    query_rows,
    query_labels,
    grad_rows,
    lse_rows,
    delta_rows,
    key_rows,
    value_rows,
    key_labels,
    bias_table,
    need_query,
    need_keys,
):
    scores, same_var = score_block(query_rows, query_labels, key_rows, key_labels, bias_table)
    weights = jnp.exp(scores - lse_rows.T[:, :, None])
    grad_weights = jnp.einsum(
        "ihe,jhe->hij", grad_rows, value_rows, preferred_element_type=jnp.float32
    )
    grad_scores = (weights * (grad_weights - delta_rows.T[:, :, None])).astype(jnp.bfloat16)
    result = ()
    if need_query:
        grad_query = jnp.einsum(
            "hij,jhe->ihe", grad_scores, key_rows, preferred_element_type=jnp.float32
        ) * HEAD_DIM ** (-0.5)
        widened = grad_scores.astype(jnp.float32)
        bias_same = jnp.sum(jnp.where(same_var[None], widened, 0.0), axis=(1, 2))
        bias_other = jnp.sum(jnp.where(same_var[None], 0.0, widened), axis=(1, 2))
        result = result + (grad_query, jnp.stack([bias_same, bias_other]))
    if need_keys:
        grad_key = jnp.einsum(
            "hij,ihe->jhe", grad_scores, query_rows, preferred_element_type=jnp.float32
        ) * HEAD_DIM ** (-0.5)
        grad_value = jnp.einsum(
            "hij,ihe->jhe",
            weights.astype(jnp.bfloat16),
            grad_rows,
            preferred_element_type=jnp.float32,
        )
        result = result + (grad_key, grad_value)
    return result


def adam_step(weight, first_moment, second_moment, gradient, step_rate, decay_rate):
    first_moment = BETA_ONE * first_moment + (1.0 - BETA_ONE) * gradient
    second_moment = BETA_TWO * second_moment + (1.0 - BETA_TWO) * gradient * gradient
    direction = (
        first_moment
        / (1.0 - BETA_ONE**STEP)
        / (jnp.sqrt(second_moment / (1.0 - BETA_TWO**STEP)) + ADAM_EPS)
    )
    return (weight - step_rate * (direction + decay_rate * weight), first_moment, second_moment)


def general_body(
    inputs,
    teacher,
    lengths,
    variate_ids,
    time_ids,
    observed,
    attend_weight,
    output_weight,
    expand_weight,
    reduce_weight,
    norm_gains,
    variate_bias,
    attend_first,
    output_first,
    expand_first,
    reduce_first,
    gains_first,
    bias_first,
    attend_second,
    output_second,
    expand_second,
    reduce_second,
    gains_second,
    bias_second,
):
    row_count = inputs.shape[1]
    length = row_count * lax.axis_size("seq")
    block_rows = math.gcd(length, 1024)
    blocks = length // block_rows
    states = inputs[0].astype(jnp.float32)
    positions = lax.axis_index("seq") * row_count + jnp.arange(row_count, dtype=jnp.int32)
    inside = positions < lengths[0]
    scored = jnp.logical_and(inside, observed[0] == 1)
    local_count = jnp.sum(scored.astype(jnp.int32))
    count_early = lax.psum(local_count, ("seq", "batch"))
    full_attend, full_output, full_expand, full_reduce = (
        lax.all_gather(attend_weight.astype(jnp.bfloat16), ("seq", "batch"), axis=1, tiled=True),
        lax.all_gather(output_weight.astype(jnp.bfloat16), ("seq", "batch"), axis=0, tiled=True),
        lax.all_gather(expand_weight.astype(jnp.bfloat16), ("seq", "batch"), axis=1, tiled=True),
        lax.all_gather(reduce_weight.astype(jnp.bfloat16), ("seq", "batch"), axis=0, tiled=True),
    )
    unit_one, scale_one = normalize(states)
    act_one = (unit_one * norm_gains[0]).astype(jnp.bfloat16)
    project = jnp.einsum("td,cde->cte", act_one, full_attend, preferred_element_type=jnp.float32)
    cos_table, sin_table = angles(time_ids[0])
    query = rotate(project[0].reshape(row_count, HEADS, HEAD_DIM), cos_table, sin_table).astype(
        jnp.bfloat16
    )
    key_rows = (
        rotate(project[1].reshape(row_count, HEADS, HEAD_DIM), cos_table, sin_table)
        .astype(jnp.bfloat16)
        .reshape(row_count, D)
    )
    value_rows = project[2].astype(jnp.bfloat16)
    own_labels = jnp.where(inside, variate_ids[0], -1).astype(jnp.bfloat16)
    all_keys, all_values, all_labels = (
        lax.all_gather(key_rows, "seq", axis=0, tiled=True),
        lax.all_gather(value_rows, "seq", axis=0, tiled=True),
        lax.all_gather(own_labels, "seq", axis=0, tiled=True),
    )
    key_blocks = all_keys.reshape(blocks, block_rows, HEADS, HEAD_DIM)
    value_blocks = all_values.reshape(blocks, block_rows, HEADS, HEAD_DIM)
    label_blocks = all_labels.astype(jnp.float32).reshape(blocks, block_rows)
    query_labels = variate_ids[0].astype(jnp.float32)

    def sweep_top(carry, pieces):
        running, sum_exp = carry
        scores, same_var = score_block(query, query_labels, pieces[0], pieces[1], variate_bias)
        raised = jnp.maximum(running, jnp.floor(jnp.max(scores, axis=-1)))
        sum_exp = sum_exp * jnp.exp(running - raised) + jnp.sum(
            jnp.exp(scores - raised[..., None]), axis=-1
        )
        return ((raised, sum_exp), None)

    start_top = jnp.full((HEADS, row_count), MASKED, jnp.float32)
    (row_top, sum_exp), unused = lax.scan(
        sweep_top,
        (start_top, jnp.zeros((HEADS, row_count), jnp.float32)),
        (key_blocks, label_blocks),
    )
    log_total = row_top + jnp.log(sum_exp)

    def sweep_out(carry, pieces):
        coarse, finest = carry
        scores, same_var = score_block(query, query_labels, pieces[0], pieces[2], variate_bias)
        weights = jnp.exp(scores - log_total[..., None])
        rounded = weights.astype(jnp.bfloat16)
        residue = (weights - rounded.astype(jnp.float32)).astype(jnp.bfloat16)
        coarse = coarse + jnp.einsum(
            "hij,jhe->ihe", rounded, pieces[1], preferred_element_type=jnp.float32
        )
        finest = finest + jnp.einsum(
            "hij,jhe->ihe", residue, pieces[1], preferred_element_type=jnp.float32
        )
        return ((coarse, finest), None)

    zero_heads = jnp.zeros((row_count, HEADS, HEAD_DIM), jnp.float32)
    (coarse, finest), unused = lax.scan(
        sweep_out, (zero_heads, zero_heads), (key_blocks, value_blocks, label_blocks)
    )
    exact_heads = coarse + finest
    mixed = coarse.reshape(row_count, D).astype(jnp.bfloat16)
    middle = states + jnp.dot(mixed, full_output, preferred_element_type=jnp.float32)
    unit_two, scale_two = normalize(middle)
    act_two = (unit_two * norm_gains[1]).astype(jnp.bfloat16)
    gate_up = jnp.einsum("td,cdf->ctf", act_two, full_expand, preferred_element_type=jnp.float32)
    sigmoid = jax.nn.sigmoid(gate_up[0])
    hidden = (gate_up[0] * sigmoid * gate_up[1]).astype(jnp.bfloat16)
    output = middle + jnp.dot(hidden, full_reduce, preferred_element_type=jnp.float32)
    error = output - teacher[0].astype(jnp.float32)
    local_square = jnp.sum(jnp.where(scored[:, None], error * error, 0.0))
    square_total = lax.psum(local_square, ("seq", "batch"))
    count_all = count_early.astype(jnp.float32)
    loss = square_total / (count_all * D)
    grad_out = jnp.where(scored[:, None], error * (2.0 / (count_all * D)), 0.0)
    back_attend, back_output, back_expand, back_reduce = (
        lax.all_gather(attend_weight.astype(jnp.bfloat16), ("seq", "batch"), axis=1, tiled=True),
        lax.all_gather(output_weight.astype(jnp.bfloat16), ("seq", "batch"), axis=0, tiled=True),
        lax.all_gather(expand_weight.astype(jnp.bfloat16), ("seq", "batch"), axis=1, tiled=True),
        lax.all_gather(reduce_weight.astype(jnp.bfloat16), ("seq", "batch"), axis=0, tiled=True),
    )
    grad_branch = grad_out.astype(jnp.bfloat16)
    reduce_grad = jnp.einsum("tf,td->fd", hidden, grad_branch, preferred_element_type=jnp.float32)
    grad_hidden = jnp.einsum(
        "td,fd->tf", grad_branch, back_reduce, preferred_element_type=jnp.float32
    )
    grad_gate = grad_hidden * gate_up[1] * sigmoid * (1.0 + gate_up[0] * (1.0 - sigmoid))
    grad_up = grad_hidden * gate_up[0] * sigmoid
    grad_expand = jnp.stack([grad_gate, grad_up]).astype(jnp.bfloat16)
    expand_grad = jnp.einsum(
        "td,ctf->cdf", act_two, grad_expand, preferred_element_type=jnp.float32
    )
    grad_act_two = jnp.einsum(
        "ctf,cdf->td", grad_expand, back_expand, preferred_element_type=jnp.float32
    )
    expand_share, reduce_share = (
        lax.psum_scatter(expand_grad, ("seq", "batch"), scatter_dimension=1, tiled=True),
        lax.psum_scatter(reduce_grad, ("seq", "batch"), scatter_dimension=0, tiled=True),
    )
    grad_middle = grad_out + norm_back(grad_act_two, unit_two, scale_two, norm_gains[1])
    grad_attn = grad_middle.astype(jnp.bfloat16)
    output_grad = jnp.einsum("td,te->de", mixed, grad_attn, preferred_element_type=jnp.float32)
    grad_mixed = jnp.einsum(
        "te,de->td", grad_attn, back_output, preferred_element_type=jnp.float32
    ).astype(jnp.bfloat16)
    grad_heads = grad_mixed.reshape(row_count, HEADS, HEAD_DIM)
    row_delta = jnp.sum(grad_heads.astype(jnp.float32) * exact_heads, axis=-1)
    lse_rows = log_total.T
    zero_bias = jnp.zeros((2, HEADS), jnp.float32)

    def sweep_query(carry, pieces):
        part_query, part_bias = block_grads(
            query,
            query_labels,
            grad_heads,
            lse_rows,
            row_delta,
            pieces[0],
            pieces[1],
            pieces[2],
            variate_bias,
            True,
            False,
        )
        return ((carry[0] + part_query, carry[1] + part_bias), None)

    (query_total, bias_grad), unused = lax.scan(
        sweep_query, (zero_heads, zero_bias), (key_blocks, value_blocks, label_blocks)
    )
    all_query, all_grad = (
        lax.all_gather(query.reshape(row_count, D), "seq", axis=0, tiled=True),
        lax.all_gather(grad_mixed, "seq", axis=0, tiled=True),
    )
    all_lse, all_delta = (
        lax.all_gather(lse_rows, "seq", axis=0, tiled=True),
        lax.all_gather(row_delta, "seq", axis=0, tiled=True),
    )
    key_heads = key_rows.reshape(row_count, HEADS, HEAD_DIM)
    value_heads = value_rows.reshape(row_count, HEADS, HEAD_DIM)
    own_float = own_labels.astype(jnp.float32)

    def sweep_keys(carry, pieces):
        part_key, part_value = block_grads(
            pieces[0],
            pieces[1],
            pieces[2],
            pieces[3],
            pieces[4],
            key_heads,
            value_heads,
            own_float,
            variate_bias,
            False,
            True,
        )
        return ((carry[0] + part_key, carry[1] + part_value), None)

    (key_total, value_heads_total), unused = lax.scan(
        sweep_keys,
        (zero_heads, zero_heads),
        (
            all_query.reshape(blocks, block_rows, HEADS, HEAD_DIM),
            label_blocks,
            all_grad.reshape(blocks, block_rows, HEADS, HEAD_DIM),
            all_lse.reshape(blocks, block_rows, HEADS),
            all_delta.reshape(blocks, block_rows, HEADS),
        ),
    )
    value_total = value_heads_total.reshape(row_count, D)
    grad_query = unrotate(query_total, cos_table, sin_table).reshape(row_count, D)
    grad_key = unrotate(key_total, cos_table, sin_table).reshape(row_count, D)
    grad_project = jnp.stack([grad_query, grad_key, value_total]).astype(jnp.bfloat16)
    attend_grad = jnp.einsum(
        "td,cte->cde", act_one, grad_project, preferred_element_type=jnp.float32
    )
    grad_act_one = jnp.einsum(
        "cte,cde->td", grad_project, back_attend, preferred_element_type=jnp.float32
    )
    attend_share, output_share = (
        lax.psum_scatter(attend_grad, ("seq", "batch"), scatter_dimension=1, tiled=True),
        lax.psum_scatter(output_grad, ("seq", "batch"), scatter_dimension=0, tiled=True),
    )
    grad_input = grad_middle + norm_back(grad_act_one, unit_one, scale_one, norm_gains[0])
    gains_grad = jnp.stack(
        [jnp.sum(grad_act_one * unit_one, axis=0), jnp.sum(grad_act_two * unit_two, axis=0)]
    )
    local_squares = (
        jnp.sum(attend_share * attend_share)
        + jnp.sum(output_share * output_share)
        + jnp.sum(expand_share * expand_share)
        + jnp.sum(reduce_share * reduce_share)
    )
    gains_total, bias_total, square_sum = lax.psum(
        (gains_grad, bias_grad, local_squares), ("seq", "batch")
    )
    grad_norm = jnp.sqrt(
        square_sum + jnp.sum(gains_total * gains_total) + jnp.sum(bias_total * bias_total)
    )
    clip_scale = jnp.minimum(1.0, CLIP_NORM / grad_norm)
    attend_new, attend_first_new, attend_second_new = adam_step(
        attend_weight,
        attend_first,
        attend_second,
        attend_share * clip_scale,
        RATE_ATTEND,
        WEIGHT_DECAY,
    )
    output_new, output_first_new, output_second_new = adam_step(
        output_weight,
        output_first,
        output_second,
        output_share * clip_scale,
        RATE_OUTPUT,
        WEIGHT_DECAY,
    )
    expand_new, expand_first_new, expand_second_new = adam_step(
        expand_weight,
        expand_first,
        expand_second,
        expand_share * clip_scale,
        RATE_EXPAND,
        WEIGHT_DECAY,
    )
    reduce_new, reduce_first_new, reduce_second_new = adam_step(
        reduce_weight,
        reduce_first,
        reduce_second,
        reduce_share * clip_scale,
        RATE_REDUCE,
        WEIGHT_DECAY,
    )
    gains_new, gains_first_new, gains_second_new = adam_step(
        norm_gains, gains_first, gains_second, gains_total * clip_scale, RATE_GAINS, 0.0
    )
    bias_new, bias_first_new, bias_second_new = adam_step(
        variate_bias, bias_first, bias_second, bias_total * clip_scale, RATE_BIAS, 0.0
    )
    input_gradient = (grad_input * count_all * D)[None]
    return (
        output[None],
        loss,
        input_gradient,
        grad_norm,
        attend_new,
        attend_new.astype(jnp.bfloat16),
        attend_first_new,
        attend_second_new,
        output_new,
        output_new.astype(jnp.bfloat16),
        output_first_new,
        output_second_new,
        expand_new,
        expand_new.astype(jnp.bfloat16),
        expand_first_new,
        expand_second_new,
        reduce_new,
        reduce_new.astype(jnp.bfloat16),
        reduce_first_new,
        reduce_second_new,
        gains_new,
        gains_first_new,
        gains_second_new,
        bias_new,
        bias_first_new,
        bias_second_new,
    )


MESH = pl.DeviceIdType.MESH
IN_VMEM = pl.BlockSpec(memory_space=pltpu.VMEM)
IN_SMEM = pl.BlockSpec(memory_space=pltpu.SMEM)
LANES = 128
HEADS_HERE = LANES // HEAD_DIM
VARIATES = 16
MIB = 1 << 20
LOW = jnp.bfloat16
WIDE = jnp.float32
TOTAL_ROWS = 24


def fast_fits(seq, batch):
    return seq == 8 and batch == 4 and seq * LANES == D


def flip(index, mask):
    result, bit = index, 1
    while bit <= mask:
        if mask & bit:
            result = result + bit - 2 * bit * lax.rem(lax.div(index, bit), 2)
        bit *= 2
    return result


def push(source, target, send_sem, recv_sem, device):
    return pltpu.make_async_remote_copy(
        src_ref=source,
        dst_ref=target,
        send_sem=send_sem,
        recv_sem=recv_sem,
        device_id=device,
        device_id_type=MESH,
    )


def block_of(index, size):
    return pl.ds(pl.multiple_of(index * size, size), size)


def dot(left, right):
    return jnp.dot(left, right, preferred_element_type=WIDE)


def dot_turned(left, right):
    return lax.dot_general(left, right, (((1,), (1,)), ((), ())), preferred_element_type=WIDE)


def turned_dot(left, right):
    return lax.dot_general(left, right, (((0,), (0,)), ((), ())), preferred_element_type=WIDE)


class Team:
    def __init__(self, index, place):
        self.index, self.place = index, place

    def at(self, mask):
        return flip(self.index, mask)


def head_team(me, group):
    return Team(me, lambda mask: (flip(me, mask), group))


def feed_team(me, group):
    return Team(
        4 * lax.rem(group, 2) + lax.rem(me, 4),
        lambda mask: (flip(me, mask % 4), flip(group, mask // 4)),
    )


class Gather:
    def __init__(self, team, rows, all_rows, sends, recvs):
        self.team, self.all_rows, self.sends, self.recvs = team, all_rows, sends, recvs
        self.size = all_rows.shape[0] // 8
        self.given = rows
        self.rows = all_rows.at[block_of(team.index, self.size)] if rows is None else rows

    def copy(self, mask, passing):
        source = self.all_rows.at[block_of(self.team.at(mask - 1 if passing else 0), self.size)]
        return push(
            source if passing else self.rows,
            source,
            self.sends.at[mask],
            self.recvs.at[mask],
            self.team.place(1 if passing else mask),
        )

    def start(self, masks=(6, 2, 4, 1)):
        for mask in masks:
            self.copy(mask, False).start()
        if self.given is not None:
            self.all_rows[block_of(self.team.index, self.size)] = self.given[...]

    def pass_on(self, chip):
        self.copy(2 * chip, False).wait_recv()
        self.copy(2 * chip + 1, True).start()

    def complete(self, chip):
        self.copy(2 * chip + 1, chip > 0).wait_recv()

    def finish(self):
        for mask in (6, 2, 4, 1):
            self.copy(mask, False).wait_send()
        for mask in (3, 5, 7):
            self.copy(mask, True).wait_send()


def at_step(step, number, *works):
    @pl.when(step == number)
    def _():
        for work in works:
            work()


def each_chip(gather, work, after):
    def one_chip(chip, unused):
        @pl.when(chip == 0)
        def _():
            gather.complete(0)

        @pl.when(chip == 1)
        def _():
            gather.pass_on(1)
            gather.pass_on(2)
            gather.copy(6, False).start()
            gather.complete(1)

        @pl.when(chip == 2)
        def _():
            gather.complete(2)

        @pl.when(chip == 3)
        def _():
            gather.pass_on(3)
            gather.complete(3)

        work(chip)
        for number, works in after.items():
            at_step(chip, number, *works)
        return unused

    lax.fori_loop(0, 4, one_chip, 0)
    gather.finish()


class Scatter:
    def __init__(self, team, buffers, near_sends, near_recvs, far_sends, far_recvs):
        self.whole, self.keep, self.near_from, self.near, self.far_from, self.far = buffers
        self.sems = near_sends, near_recvs, far_sends, far_recvs
        self.team = team
        self.size = self.keep.shape[1]

    def near_copy(self, chip):
        return push(
            self.near_from.at[chip],
            self.near.at[chip],
            self.sems[0].at[chip],
            self.sems[1].at[chip],
            self.team.place(1),
        )

    def far_copy(self, chip):
        return push(
            self.far_from.at[chip],
            self.far.at[chip],
            self.sems[2].at[chip],
            self.sems[3].at[chip],
            self.team.place(2 * chip),
        )

    def put(self, chip, rows):
        core = lax.rem(self.team.index, 2)
        self.whole[...] = rows
        self.near_from[chip] = self.whole[block_of(1 - core, self.size)].astype(LOW)
        self.near_copy(chip).start()
        self.keep[chip] = self.whole[block_of(core, self.size)]

    def combine(self, chip):
        self.near_copy(chip).wait_recv()
        self.far_from[chip] = (self.keep[chip] + self.near[chip].astype(WIDE)).astype(LOW)
        self.far_copy(chip).start()

    def total(self):
        self.near_copy(0).wait_recv()
        total = self.keep[0] + self.near[0].astype(WIDE)
        for chip in (1, 2, 3):
            self.far_copy(chip).wait_recv()
            total = total + self.far[chip].astype(WIDE)
        for chip in (0, 1, 2, 3):
            self.near_copy(chip).wait_send()
            if chip:
                self.far_copy(chip).wait_send()
        return total


class Quad:
    def __init__(self, part, along_near, along_far):
        self.part, self.along_near, self.along_far = part, along_near, along_far


def feed_quad(me, group):
    return Quad(2 * lax.div(me, 4) + lax.div(group, 2), (flip(me, 4), group), (me, flip(group, 2)))


def head_quad(me, group):
    return Quad(
        2 * lax.rem(group, 2) + lax.div(group, 2), (me, flip(group, 1)), (me, flip(group, 2))
    )


def line_place(part):
    return 2 * lax.rem(part, 2) + lax.div(part, 2)


class QuadGather:
    def __init__(self, quad, part_of, sends, recvs):
        self.part_of, self.sends, self.recvs = part_of, sends, recvs
        self.part, self.along_near, self.along_far = quad.part, quad.along_near, quad.along_far

    def copy(self, way):
        part = self.part_of(flip(self.part, 1) if way == 3 else self.part)
        device = self.along_far if way == 1 else self.along_near
        return push(part, part, self.sends.at[way], self.recvs.at[way], device)

    def start_near(self):
        self.copy(2).start()

    def start_far(self):
        self.copy(1).start()

    def start(self):
        self.start_far()
        self.start_near()

    def pass_on(self):
        self.copy(1).wait_recv()
        self.copy(3).start()

    def land(self):
        self.copy(2).wait_recv()
        self.copy(3).wait_recv()

    def finish(self):
        for way in (1, 2, 3):
            self.copy(way).wait_send()


class QuadScatter:
    def __init__(self, quad, part_of, landing, sends, recvs):
        self.part_of, self.landing, self.sends, self.recvs = part_of, landing, sends, recvs
        self.part, self.along_near, self.along_far = quad.part, quad.along_near, quad.along_far

    def copy(self, slot):
        return push(
            self.part_of(flip(self.part, (2, 3, 1)[slot])),
            self.landing.at[slot],
            self.sends.at[slot],
            self.recvs.at[slot],
            self.along_far if slot == 2 else self.along_near,
        )

    def start_far(self):
        self.copy(1).start()

    def start_near(self):
        self.copy(0).start()

    def start(self):
        self.start_far()
        self.start_near()

    def total(self):
        total = self.part_of(self.part)[...].astype(WIDE)
        return total + self.landing[0].astype(WIDE) + self.landing[2].astype(WIDE)

    def pass_on(self):
        self.copy(1).wait_recv()
        part = self.part_of(flip(self.part, 1))
        part[...] = (part[...].astype(WIDE) + self.landing[1].astype(WIDE)).astype(LOW)
        self.copy(2).start()

    def land(self):
        self.copy(0).wait_recv()
        self.copy(2).wait_recv()

    def finish(self):
        for slot in (0, 1, 2):
            self.copy(slot).wait_send()


def chip_of(team, chip):
    here = lax.div(team.index, 2)
    if isinstance(chip, int):
        return flip(here, chip)
    column = lax.rem(lax.rem(here, 2) + lax.rem(chip, 2), 2)
    row = lax.rem(lax.div(here, 2) + lax.div(chip, 2), 2)
    return 2 * row + column


def turn_rows(values, cosine, sine):
    half = HEAD_DIM // 2
    pieces = []
    for start in range(0, values.shape[0], HEAD_DIM):
        first, second = values[start : start + half], values[start + half : start + HEAD_DIM]
        pieces += [first * cosine - second * sine, second * cosine + first * sine]
    return jnp.concatenate(pieces, axis=0)


def turned(eye, values):
    size = min(values.shape[1], eye.shape[0])
    rows = [
        dot_turned(eye[:size, :size], values[:, start : start + size]).astype(LOW)
        for start in range(0, values.shape[1], size)
    ]
    return rows[0] if len(rows) == 1 else jnp.concatenate(rows, axis=0)


def thirds(values):
    first = values.astype(LOW).astype(WIDE)
    second = (values - first).astype(LOW).astype(WIDE)
    return first, second, values - first - second


def pick(row, choices):
    result = jnp.zeros(row.shape, WIDE)
    for number, choice in choices.items():
        result = jnp.where(row == number, choice, result)
    return result


def norm_rows(values):
    scale = lax.rsqrt(jnp.mean(values * values, axis=-1, keepdims=True) + NORM_EPS)
    return values * scale, scale


def feed_block(block):
    y, x, core, far_z, near_z = (block // 16, block // 8 % 2, block // 4 % 2, block // 2 % 2, block % 2)
    return 4 * near_z + 2 * x + core, 2 * y + far_z


def layer_kernel(seq, batch, ins, outs, mem):
    me, group = lax.axis_index("seq"), lax.axis_index("batch")
    rows = ins.inputs.shape[0]
    length = rows * seq
    pair = 2 * rows
    share = ins.attend.shape[1]
    wide_columns = ins.expand.shape[2] // D
    hidden_width = mem.reduce_all.shape[0] * mem.reduce_all.shape[1]
    blocks = ins.expand.shape[2] // LANES
    heads, feeds = head_team(me, group), feed_team(me, group)
    head_four, feed_four = head_quad(me, group), feed_quad(me, group)
    quad = feed_four.part

    staged = [(ins.attend.at[which], mem.keep.at[0, block_of(which, share)]) for which in range(3)]
    staged.append((ins.output, mem.keep.at[0, block_of(3, share)]))
    staged.append((ins.reduce, mem.keep.at[1]))
    for which in range(2):
        for block in range(wide_columns):
            columns = slice(block * D, (block + 1) * D)
            staged.append(
                (ins.expand.at[which, :, columns], mem.keep.at[2 + which, block_of(block, share)])
            )
    staged = [
        pltpu.make_async_copy(source, target, mem.stage_sem.at[number])
        for number, (source, target) in enumerate(staged)
    ]
    for copy in staged:
        copy.start()
    barrier = pltpu.get_barrier_semaphore()
    for mask in range(1, seq):
        pl.semaphore_signal(barrier, inc=1, device_id=(flip(me, mask), group), device_id_type=MESH)
    for step in range(1, batch):
        pl.semaphore_signal(
            barrier, inc=1, device_id=(me, lax.rem(group + step, batch)), device_id_type=MESH
        )
    for mask in (5, 6, 7):
        pl.semaphore_signal(barrier, inc=1, device_id=feeds.place(mask), device_id_type=MESH)

    square = (pair, pair)
    mem.eye[...] = jnp.where(
        lax.broadcasted_iota(jnp.int32, square, 0) == lax.broadcasted_iota(jnp.int32, square, 1), 1.0, 0.0
    ).astype(LOW)
    position = me * rows + lax.broadcasted_iota(jnp.int32, (1, rows), 1)
    inside = position < ins.lengths[0]
    scored = jnp.logical_and(inside, ins.observed[...] == 1).astype(WIDE)
    variate = ins.variates[...].astype(WIDE)
    angle = ins.frequency[...] * ins.times[...].astype(WIDE)
    mem.facts_own[: HEAD_DIM // 2] = jnp.cos(angle)
    mem.facts_own[HEAD_DIM // 2 : HEAD_DIM] = jnp.sin(angle)
    mem.facts_own[HEAD_DIM:] = jnp.concatenate(
        [jnp.where(inside, variate, -1.0), variate, scored, jnp.zeros((5, rows), WIDE)], axis=0
    )
    mem.scored[...] = jnp.broadcast_to(scored, (rows, rows)).T
    for copy in staged:
        copy.wait()
    for which in range(3):
        mem.attend_low[which] = mem.keep[0, block_of(which, share)].astype(LOW)
    pl.semaphore_wait(barrier, seq + batch + 1)

    masks = (6, 7, 4, 5, 2, 3, 1)

    def start_attend_columns():
        copies = []
        for mask in masks:
            copy = push(
                mem.attend_low.at[:, :, block_of(heads.at(mask), LANES)],
                mem.attend_all.at[:, me, group],
                mem.column_send.at[0, mask],
                mem.column_recv.at[0, mask],
                heads.place(mask),
            )
            copy.start()
            copies.append(copy)
        mem.attend_all[:, me, group] = mem.attend_low[:, :, block_of(me, LANES)]
        return copies

    def start_expand_columns():
        copies = []
        for mask in masks:
            copy = push(
                mem.expand_low.at[:, feeds.at(mask)],
                mem.expand_all.at[:, me, group],
                mem.column_send.at[1, mask],
                mem.column_recv.at[1, mask],
                feeds.place(mask),
            )
            copy.start()
            copies.append(copy)
        mem.expand_all[:, me, group] = mem.expand_low[:, feeds.index]
        return copies

    def expand_part_of(array, which):
        def part_of(part):
            return array.at[which, pl.ds(4 * lax.div(part, 2), 4), pl.ds(2 * lax.rem(part, 2), 2)]

        return part_of

    def quad_gather(four, row, part_of):
        return QuadGather(four, part_of, mem.line_send.at[row], mem.line_recv.at[row])

    def gather(team, phase, all_rows):
        return Gather(
            team,
            mem.own_rows.at[phase],
            all_rows,
            mem.gather_send.at[phase],
            mem.gather_recv.at[phase],
        )

    def scatter(team, phase):
        return Scatter(
            team,
            (mem.whole, mem.keep, mem.near_from, mem.near, mem.far_from, mem.far),
            mem.near_send.at[phase],
            mem.near_recv.at[phase],
            mem.far_send.at[phase],
            mem.far_recv.at[phase],
        )

    attend_columns = start_attend_columns()
    mem.output_full[block_of(batch * me + group, share)] = mem.keep[0, block_of(3, share)].astype(LOW)
    mem.reduce_all[quad] = mem.keep[1].astype(LOW)
    for which in range(2):
        for block in range(blocks):
            owner, part = feed_block(block)
            row, lane = divmod(block * LANES, D)
            mem.expand_low[which, owner, :, part * LANES : (part + 1) * LANES] = mem.keep[
                2 + which, block_of(row, share), lane : lane + LANES
            ].astype(LOW)
    line_output = quad_gather(
        head_four, 1, lambda part: mem.output_full.at[block_of(batch * me + line_place(part), share)]
    )
    line_output.start()
    unit_one, scale_one = norm_rows(ins.inputs[...].astype(WIDE))
    mem.own_rows[0] = (unit_one * ins.gains[0:1, :]).astype(LOW)
    facts = Gather(heads, mem.facts_own, mem.facts_all, mem.facts_send, mem.facts_recv)
    facts.start()
    for copy in attend_columns:
        copy.wait_recv()
    line_attend = quad_gather(head_four, 0, lambda part: mem.attend_all.at[:, :, line_place(part)])
    line_attend.start()
    acts = gather(heads, 0, mem.act_one)
    acts.start()
    for chip in (1, 2, 3):
        facts.pass_on(chip)
    for chip in (0, 1, 2, 3):
        facts.complete(chip)
    facts.finish()
    step_rows = mem.facts_own.shape[0]
    half = HEAD_DIM // 2
    count = jnp.zeros((8, LANES), WIDE)
    for slot in range(seq):
        columns = slice(slot * rows, (slot + 1) * rows)
        start = slot * step_rows
        mem.cosine[:, columns] = mem.facts_all[start : start + half]
        mem.sine[:, columns] = mem.facts_all[start + half : start + 2 * half]
        labels = mem.facts_all[start + 2 * half : start + 2 * half + 8]
        mem.labels[:, columns] = labels
        count = count + labels
    mem.count[group] = count
    count_copies = []
    for step in range(1, batch):
        copy = push(
            mem.count.at[group],
            mem.count.at[group],
            mem.count_send.at[step],
            mem.count_recv.at[step],
            (me, lax.rem(group + step, batch)),
        )
        copy.start()
        count_copies.append(copy)

    def mark(block, unused):
        span = block_of(block, pair)
        row = lax.broadcasted_iota(jnp.int32, (HEAD_DIM, pair), 0)
        third = lax.div(row, VARIATES)
        variate = lax.rem(row, VARIATES).astype(WIDE)
        key_label, query_label = mem.labels[0:1, span], mem.labels[1:2, span]
        ones = jnp.ones((1, pair), WIDE)
        last = 3 * VARIATES
        hidden_keys = (key_label < 0.0).astype(WIDE)
        mem.key_marks[:, span] = jnp.where(
            third < 3,
            (key_label == variate).astype(WIDE),
            pick(row, {last: ones, last + 1: ones, last + 2: ones, last + 3: hidden_keys}),
        ).astype(LOW)
        query_marks = (query_label == variate).astype(WIDE)
        sum_marks = jnp.where(row < VARIATES, query_marks, pick(row, {VARIATES: ones})).astype(LOW)
        for head in range(HEADS_HERE):
            mem.query_back[head, HEAD_DIM:, span] = sum_marks
            number = me * HEADS_HERE + head
            other = jnp.full((HEAD_DIM, pair), ins.bias[1, number], WIDE)
            more = thirds(jnp.full((HEAD_DIM, pair), ins.bias[0, number], WIDE) - other)
            other = thirds(other)
            mem.query_turned[head, HEAD_DIM:, span] = jnp.where(
                third < 3,
                query_marks * jnp.where(third == 0, more[0], jnp.where(third == 1, more[1], more[2])),
                pick(row, {last: other[0], last + 1: other[1], last + 2: other[2], last + 3: MASKED}),
            ).astype(LOW)
        return unused

    lax.fori_loop(0, length // pair, mark, 0)
    acts.pass_on(1)
    acts.pass_on(2)
    line_output.pass_on()
    line_output.land()
    outputs = Gather(heads, None, mem.output_full, mem.output_send, mem.output_recv)
    outputs.start()
    acts.pass_on(3)
    line_attend.pass_on()
    for chip in range(4):
        acts.complete(chip)
    acts.finish()

    expand_columns = start_expand_columns()
    line_reduce = quad_gather(feed_four, 4, lambda part: mem.reduce_all.at[part])
    line_reduce.start_far()
    line_expand = [
        quad_gather(feed_four, 2 + which, expand_part_of(mem.expand_all, which)) for which in range(2)
    ]
    line_attend.land()
    line_reduce.start_near()

    def attend_matrix(which):
        return mem.attend_all[which].reshape(D, LANES)

    def project(block, unused):
        span = block_of(block, pair)
        products = dot_turned(mem.attend_turned[...], mem.act_one[span, :])
        cosine, sine = mem.cosine[:, span], mem.sine[:, span]
        query = turn_rows(products[:LANES], cosine, sine).astype(LOW)
        query = (query.astype(WIDE) * HEAD_DIM ** (-0.5)).astype(LOW)
        key = turn_rows(products[LANES : 2 * LANES], cosine, sine).astype(LOW)
        value = products[2 * LANES :].astype(LOW)
        mem.key_turned[:, span] = key
        mem.value_turned[:, span] = value

        for head in range(HEADS_HERE):
            features = slice(head * HEAD_DIM, (head + 1) * HEAD_DIM)
            mem.query_turned[head, :HEAD_DIM, span] = query[features]
            mem.query_back[head, :HEAD_DIM, span] = query[features]
            whole = jnp.concatenate([key[features], mem.key_marks[:, span]], axis=0)
            mem.key_heads[head, span, :] = turned(mem.eye, whole)
        return unused

    for copy in expand_columns:
        copy.wait_recv()
    line_expand[0].start_far()
    line_expand[0].start_near()
    for which in range(3):
        for start in range(0, D, pair):
            piece = attend_matrix(which)[start : start + pair]
            mem.attend_turned[block_of(which, LANES), start : start + pair] = turned(mem.eye, piece)
    lax.fori_loop(0, length // pair, project, 0)
    line_expand[1].start_far()

    core = lax.rem(me, 2)

    def mixed_copy(chip, which):
        other = 2 * chip_of(heads, chip) + which
        slot = 2 * chip + lax.rem(which + core, 2)
        return push(
            mem.mixed_out.at[block_of(other, rows)],
            mem.mixed_rows.at[:, block_of(me, LANES)],
            mem.mixed_send.at[slot],
            mem.mixed_recv.at[slot],
            (other, group),
        )

    def attend_block(chip):
        columns = block_of(chip_of(heads, chip), pair)
        for head in range(HEADS_HERE):
            span = slice(head * HEAD_DIM, (head + 1) * HEAD_DIM)
            scores = dot(mem.key_heads[head], mem.query_turned[head, :, columns])
            top = jnp.floor(jnp.max(scores, axis=0, keepdims=True))
            powers = jnp.exp(scores - top)
            probs = powers * (1.0 / jnp.sum(powers, axis=0, keepdims=True))
            rounded = probs.astype(LOW)
            mem.probs[head, :, columns] = rounded
            residue = (probs - rounded.astype(WIDE)).astype(LOW)
            coarse = dot(mem.value_turned[span, :], rounded)
            mem.exact[span, columns] = coarse + dot(mem.value_turned[span, :], residue)
            mem.mixed_wide[span, :] = coarse
        mixed = mem.mixed_wide[...].astype(LOW)
        mem.mixed_turned[:, columns] = mixed
        mem.mixed_out[columns, :] = turned(mem.eye, mixed)

    def attend_step(step, unused):
        chip = lax.rem(step + 1, 4)
        attend_block(chip)
        for which in range(2):

            @pl.when(jnp.logical_or(chip > 0, core != which))
            def _():
                mixed_copy(chip, which).start()

        at_step(step, 0, lambda: outputs.pass_on(1), lambda: outputs.pass_on(2))
        at_step(step, 1, lambda: outputs.pass_on(3))
        return unused

    lax.fori_loop(0, 4, attend_step, 0)
    line_expand[1].start_near()
    mem.mixed_rows[:, block_of(me, LANES)] = mem.mixed_out[block_of(me, rows), :]
    for chip in range(4):
        outputs.complete(chip)
    outputs.finish()

    def wait_pieces(copy):
        for mask in range(1, seq):
            copy(mask).wait()

    def mixed_wait(mask):
        other = heads.at(mask)
        return push(
            mem.mixed_out.at[block_of(other, rows)],
            mem.mixed_rows.at[:, block_of(other, LANES)],
            mem.mixed_send.at[mask],
            mem.mixed_recv.at[mask],
            (other, group),
        )

    wait_pieces(mixed_wait)
    middle = ins.inputs[...].astype(WIDE) + dot(mem.mixed_rows[...], mem.output_full[...])
    mem.middle[...] = middle
    unit_two, scale_two = norm_rows(middle)
    mem.own_rows[1] = (unit_two * ins.gains[1:2, :]).astype(LOW)
    acts = gather(feeds, 1, mem.act_two)
    acts.start((2, 4, 1))
    line_reduce.pass_on()
    line_expand[0].pass_on()

    def split_heads(block, unused):
        span = block_of(block, pair)
        row = lax.broadcasted_iota(jnp.int32, (HEAD_DIM, pair), 0)
        value_marks = jnp.where(row < 3, 1.0, 0.0).astype(LOW)
        for head in range(HEADS_HERE):
            features = slice(head * HEAD_DIM, (head + 1) * HEAD_DIM)
            value = mem.value_turned[features, span]
            whole = jnp.concatenate([value, value_marks], axis=0)
            mem.value_heads[head, span, :] = turned(mem.eye, whole)
        return unused

    lax.fori_loop(0, length // pair, split_heads, 0)
    line_expand[0].land()

    def expand_matrix(which):
        return mem.expand_all[which].reshape(D, hidden_width)

    def reduce_matrix():
        return mem.reduce_all[...].reshape(hidden_width, D)

    def feed_gate(chip):
        span = block_of(chip_of(feeds, chip), pair)
        mem.by_gate[span, :] = dot(mem.act_two[span, :], expand_matrix(0))

    def feed_up(chip, unused=0):
        span = block_of(chip_of(feeds, chip), pair)
        gate = mem.by_gate[span, :]
        up = dot(mem.act_two[span, :], expand_matrix(1))
        sigmoid = 1.0 / (1.0 + jnp.exp(-gate))
        swish = gate * sigmoid
        mem.by_up[span, :] = swish
        mem.by_gate[span, :] = up * sigmoid * (1.0 + gate * (1.0 - sigmoid))
        mem.hidden[span, :] = (swish * up).astype(LOW)
        return unused

    each_chip(
        acts,
        feed_gate,
        {
            0: [line_expand[1].pass_on],
            2: [line_expand[1].land, lambda: lax.fori_loop(0, 3, feed_up, 0)],
            3: [lambda: lax.fori_loop(3, 4, feed_up, 0)],
        },
    )
    line_reduce.land()
    sums = scatter(feeds, 1)

    def feed_down(step, unused):
        chip = lax.rem(step + 1, 4)
        span = block_of(chip_of(feeds, chip), pair)
        sums.put(chip, dot(mem.hidden[span, :], reduce_matrix()))
        at_step(step, 1, lambda: sums.combine(1))
        at_step(step, 2, lambda: sums.combine(2))
        return unused

    lax.fori_loop(0, 4, feed_down, 0)
    sums.combine(3)

    def turn_feed(block, unused):
        span = block_of(block, pair)
        mem.hidden_turned[:, span] = turned(mem.eye, mem.hidden[span, :])
        mem.act_two_turned[:, span] = turned(mem.eye, mem.act_two[span, :])
        return unused

    lax.fori_loop(0, length // pair, turn_feed, 0)
    output = mem.middle[...] + sums.total()
    outs.layer_output[...] = output
    for copy in count_copies:
        copy.wait()
    count_all = jnp.sum(
        mem.count[0, 2:3] + mem.count[1, 2:3] + mem.count[2, 2:3] + mem.count[3, 2:3],
        axis=1,
        keepdims=True,
    )
    error = jnp.where(mem.scored[:, 0:1] > 0.0, output - ins.teacher[...].astype(WIDE), 0.0)
    mem.squares[1:2, :] = jnp.sum(error * error, axis=0, keepdims=True)
    grad_out = error * (2.0 / (count_all * D))
    mem.grad_own[...] = grad_out
    mem.own_rows[2] = grad_out.astype(LOW)
    acts = gather(feeds, 2, mem.branch)
    acts.start((2, 4, 1))

    def turn_acts(block, unused):
        span = block_of(block, pair)
        mem.act_one_turned[:, span] = turned(mem.eye, mem.act_one[span, :])
        return unused

    lax.fori_loop(0, length // pair, turn_acts, 0)

    sums = scatter(feeds, 2)

    def feed_back(chip):
        span = block_of(chip_of(feeds, chip), pair)
        grad_hidden = dot_turned(mem.branch[span, :], reduce_matrix())
        grad_gate = (grad_hidden * mem.by_gate[span, :]).astype(LOW)
        grad_up = (grad_hidden * mem.by_up[span, :]).astype(LOW)
        mem.grad_gate[span, :] = grad_gate
        mem.grad_up[span, :] = grad_up
        sums.put(
            chip,
            dot_turned(grad_gate, expand_matrix(0)) + dot_turned(grad_up, expand_matrix(1)),
        )

    each_chip(acts, feed_back, {2: [lambda: sums.combine(1)], 3: [lambda: sums.combine(2)]})

    def quad_scatter(four, row, part_of, landing):
        return QuadScatter(four, part_of, landing, mem.back_send.at[row], mem.back_recv.at[row])

    def reduce_grad(part, unused):
        mem.reduce_grad[part] = dot(
            mem.hidden_turned[block_of(part, rows), :], mem.branch[...]
        ).astype(LOW)
        at_step(part, 0, lambda: sums.combine(3))
        return unused

    lax.fori_loop(0, batch, reduce_grad, 0)
    back_reduce = quad_scatter(
        feed_four, 0, lambda part: mem.reduce_grad.at[part], mem.reduce_land
    )
    back_reduce.start_far()

    def expand_grad(which):
        grads = (mem.grad_gate, mem.grad_up)[which]

        def one_block(block, unused):
            products = dot(mem.act_two_turned[block_of(block, pair), :], grads[...]).astype(LOW)
            mem.expand_grad[which, pl.ds(2 * block, 2)] = products.reshape(
                2, batch, share, hidden_width
            )
            return unused

        lax.fori_loop(0, seq // 2, one_block, 0)
        line = quad_scatter(
            feed_four, 1 + which, expand_part_of(mem.expand_grad, which), mem.expand_land.at[which]
        )
        return line

    back_expand = []
    back_expand.append(expand_grad(0))
    back_expand[0].start_far()
    grad_act = sums.total()
    unit_two, scale_two = norm_rows(mem.middle[...])
    gain = ins.gains[1:2, :]
    grad_unit = grad_act * gain
    mem.gains[1:2, :] = jnp.sum(grad_act * unit_two, axis=0, keepdims=True)
    grad_middle = mem.grad_own[...] + scale_two * (
        grad_unit - unit_two * jnp.mean(grad_unit * unit_two, axis=-1, keepdims=True)
    )
    mem.grad_own[...] = grad_middle
    mem.own_rows[3] = grad_middle.astype(LOW)
    grad_mixed = dot_turned(mem.output_full[...], mem.own_rows[3]).astype(LOW)
    mem.grad_mixed_out[...] = grad_mixed.reshape(seq, LANES, rows)

    def grad_copy(mask, back=False):
        return push(
            mem.grad_mixed_out.at[heads.at(mask)],
            mem.grad_mixed.at[:, block_of(heads.at(mask) if back else me, rows)],
            mem.mixed_send.at[8 + mask],
            mem.mixed_recv.at[8 + mask],
            heads.place(mask),
        )

    for mask in masks:
        grad_copy(mask).start()
    mem.grad_mixed[:, block_of(me, rows)] = mem.grad_mixed_out[me]
    back_reduce.pass_on()
    back_expand.append(expand_grad(1))
    back_expand[1].start_far()

    wait_pieces(lambda mask: grad_copy(mask, True))
    acts = gather(heads, 3, mem.grad_attn)
    acts.start()
    back_reduce.start_near()
    back_expand[0].start_near()
    back_attend = [
        quad_scatter(
            head_four,
            4 + which,
            lambda part, which=which: mem.attend_grad.at[which, :, line_place(part)],
            mem.attend_land.at[which],
        )
        for which in range(3)
    ]

    def attend_grad(which):
        def one_block(block, unused):
            products = dot(mem.act_one_turned[block_of(block, pair), :], mem.grad_project[which])
            mem.attend_grad[which, pl.ds(2 * block, 2)] = products.astype(LOW).reshape(
                2, batch, share, LANES
            )
            return unused

        lax.fori_loop(0, length // pair, one_block, 0)
        back_attend[which].start()

    lane = lax.broadcasted_iota(jnp.int32, (pair, LANES), 1)

    def grad_rows(block, unused):
        span = block_of(block, pair)
        whole = turned(mem.eye, mem.grad_mixed[:, span])
        for head in range(HEADS_HERE):
            mem.grad_heads[head, span, :] = jnp.where(
                lax.div(lane, HEAD_DIM) == head, whole, jnp.zeros_like(whole)
            )
        return unused

    lax.fori_loop(0, length // pair, grad_rows, 0)

    def value_back(block, unused):
        span = block_of(block, pair)
        total = dot(mem.probs[0, span, :], mem.grad_heads[0])
        for head in range(1, HEADS_HERE):
            total = total + dot(mem.probs[head, span, :], mem.grad_heads[head])
        mem.grad_project[2, span, :] = total.astype(LOW)
        return unused

    lax.fori_loop(0, length // pair, value_back, 0)
    back_expand[0].pass_on()
    attend_grad(2)

    def score_back(block, unused):
        columns = block_of(block, pair)
        row = lax.broadcasted_iota(jnp.int32, (HEAD_DIM, pair), 0)
        grads = mem.grad_mixed[:, columns]
        delta = grads.astype(WIDE) * mem.exact[:, columns]
        for head in range(HEADS_HERE):
            span = slice(head * HEAD_DIM, (head + 1) * HEAD_DIM)
            pieces = thirds(-jnp.sum(delta[span], axis=0, keepdims=True))
            marks = pick(row, dict(enumerate(pieces))).astype(LOW)
            change = dot(mem.value_heads[head], jnp.concatenate([grads[span], marks], axis=0))
            mem.probs[head, :, columns] = (mem.probs[head, :, columns].astype(WIDE) * change).astype(LOW)
        return unused

    lax.fori_loop(0, length // pair, score_back, 0)
    back_expand[1].start_near()
    mem.bias_sums[...] = jnp.zeros_like(mem.bias_sums)
    scale = HEAD_DIM ** (-0.5)

    def project_grads(block, unused):
        span = block_of(block, pair)
        cosine, sine = mem.cosine[:, span], -mem.sine[:, span]
        queries, keys = [], []
        for head in range(HEADS_HERE):
            features = slice(head * HEAD_DIM, (head + 1) * HEAD_DIM)
            queries.append(dot(mem.key_turned[features, :], mem.probs[head, :, span]) * scale)
            sums = dot_turned(mem.query_back[head], mem.probs[head, span, :])
            keys.append(sums[:HEAD_DIM])
            by_variate = sums[HEAD_DIM : HEAD_DIM + VARIATES]
            same = by_variate * mem.key_marks[:VARIATES, span].astype(WIDE)
            mem.bias_sums[head : head + 1, :] += jnp.sum(same, axis=0, keepdims=True)
            total = sums[HEAD_DIM + VARIATES : HEAD_DIM + VARIATES + 1]
            mem.bias_sums[HEADS_HERE + head : HEADS_HERE + head + 1, :] += total
        queries = turn_rows(jnp.concatenate(queries, axis=0), cosine, sine)
        mem.grad_project[0, span, :] = turned(mem.eye, queries.astype(LOW))
        keys = turn_rows(jnp.concatenate(keys, axis=0), cosine, sine)
        mem.grad_project[1, span, :] = turned(mem.eye, keys.astype(LOW))
        return unused

    lax.fori_loop(0, length // pair, project_grads, 0)
    back_expand[1].pass_on()
    attend_grad(0)
    acts.pass_on(1)
    acts.pass_on(2)
    sums = scatter(heads, 3)

    def project_back(step, unused):
        chip = lax.rem(step + 1, 4)
        span = block_of(chip_of(heads, chip), pair)
        grads = [mem.grad_project[which, span, :] for which in range(3)]
        sums.put(chip, dot(jnp.concatenate(grads, axis=1), mem.attend_turned[...]))
        at_step(step, 1, lambda: sums.combine(1))
        at_step(step, 2, lambda: sums.combine(2))
        return unused

    lax.fori_loop(0, 4, project_back, 0)
    sums.combine(3)
    attend_grad(1)
    acts.pass_on(3)
    for chip in range(4):
        acts.complete(chip)
    acts.finish()
    mem.output_grad[...] = (
        dot(mem.mixed_turned[...], mem.grad_attn[...]).astype(LOW).reshape(mem.output_grad.shape)
    )
    back_output = quad_scatter(
        head_four, 3, lambda part: mem.output_grad.at[line_place(part)], mem.output_land
    )
    back_output.start()
    for which in (2, 0):
        back_attend[which].pass_on()

    column_copies = []
    mem.squares[0:1, :] = jnp.zeros((1, D), WIDE)

    def add_squares(total):
        flat = total.reshape(-1, total.shape[-1])
        width = flat.shape[1]
        mem.squares[0:1, :width] += jnp.sum(flat * flat, axis=0, keepdims=True)

    def store_whole(total, out):
        out[...] = total
        add_squares(total)

    back_reduce.land()
    store_whole(back_reduce.total(), outs.reduce_share)
    def expand_shares(which):
        back_expand[which].land()
        own = expand_part_of(mem.expand_grad, which)(quad)

        def one_block(block, unused):
            total = (
                own[block].astype(WIDE)
                + mem.expand_land[which, 0, block].astype(WIDE)
                + mem.expand_land[which, 2, block].astype(WIDE)
            )
            mem.expand_part[which, block] = total.astype(LOW)
            add_squares(total)
            return unused

        lax.fori_loop(0, 4, one_block, 0)
        for mask in masks:
            other = feeds.at(mask)
            copy = push(
                mem.expand_part.at[which, lax.rem(other, 4), lax.div(other, 4)],
                mem.expand_share.at[which, feeds.index],
                mem.share_send.at[which, mask],
                mem.share_recv.at[which, mask],
                feeds.place(mask),
            )
            copy.start()
            column_copies.append(copy)
        mem.expand_share[which, feeds.index] = mem.expand_part[
            which, lax.rem(feeds.index, 4), lax.div(feeds.index, 4)
        ]

    expand_shares(0)
    back_attend[1].pass_on()
    expand_shares(1)

    def attend_shares(which):
        back_attend[which].land()
        total = back_attend[which].total()
        mem.attend_part[which] = total.astype(LOW)
        add_squares(total)

    attend_shares(2)
    grad_act = sums.total()
    unit_one, scale_one = norm_rows(ins.inputs[...].astype(WIDE))
    gain = ins.gains[0:1, :]
    grad_unit = grad_act * gain
    mem.gains[0:1, :] = jnp.sum(grad_act * unit_one, axis=0, keepdims=True)
    grad_input = mem.grad_own[...] + scale_one * (
        grad_unit - unit_one * jnp.mean(grad_unit * unit_one, axis=-1, keepdims=True)
    )
    outs.input_gradient[...] = grad_input * (count_all * D)
    outs.count[...] = jnp.broadcast_to(count_all, (8, LANES))

    back_output.pass_on()
    for which in range(2):
        attend_shares(which)
    for mask in masks:
        copy = push(
            mem.attend_part.at[:, heads.at(mask)],
            outs.attend_share.at[:, :, block_of(me, LANES)],
            mem.share_send.at[2, mask],
            mem.share_recv.at[2, mask],
            heads.place(mask),
        )
        copy.start()
        column_copies.append(copy)
    outs.attend_share[:, :, block_of(me, LANES)] = mem.attend_part[:, me]
    back_output.land()
    store_whole(back_output.total(), outs.output_share)

    lane = lax.broadcasted_iota(jnp.int32, (1, LANES), 1)
    lines = [
        mem.gains[which : which + 1, start : start + LANES]
        for which in range(2)
        for start in range(0, D, LANES)
    ]
    bias_line = jnp.zeros((1, LANES), WIDE)
    for row in range(2 * HEADS_HERE):
        place = row // HEADS_HERE * HEADS + me * HEADS_HERE + row % HEADS_HERE
        line = mem.bias_sums[row : row + 1, :]
        if row >= HEADS_HERE:
            line = line - mem.bias_sums[row - HEADS_HERE : row - HEADS_HERE + 1, :]
        amount = jnp.sum(line, axis=1, keepdims=True)
        bias_line = bias_line + jnp.where(lane == place, amount, 0.0)
    amounts = jnp.sum(mem.squares[0:2, :], axis=1, keepdims=True)
    amount_line = jnp.where(lane == 0, amounts[0:1], 0.0) + jnp.where(lane == 1, amounts[1:2], 0.0)
    lines += [bias_line, amount_line, jnp.zeros((6, LANES), WIDE)]
    mem.plane_totals[me] = jnp.concatenate(lines, axis=0)
    plane_copies = []
    for mask in masks:
        copy = push(
            mem.plane_totals.at[me],
            mem.plane_totals.at[me],
            mem.total_send.at[0, mask],
            mem.total_recv.at[0, mask],
            (flip(me, mask), group),
        )
        copy.start()
        plane_copies.append(copy)
    for copy in column_copies[: 2 * len(masks)]:
        copy.wait()
    for which in range(2):
        for block in range(blocks):
            owner, part = feed_block(block)
            outs.expand_share[which, :, block * LANES : (block + 1) * LANES] = mem.expand_share[
                which, owner, :, part * LANES : (part + 1) * LANES
            ]
    for copy in plane_copies:
        copy.wait()
    mem.line_totals[group] = jnp.sum(mem.plane_totals[...], axis=0)
    total_copies = []
    for step in range(1, batch):
        copy = push(
            mem.line_totals.at[group],
            mem.line_totals.at[group],
            mem.total_send.at[1, step],
            mem.total_recv.at[1, step],
            (me, lax.rem(group + step, batch)),
        )
        copy.start()
        total_copies.append(copy)
    for copy in total_copies:
        copy.wait()
    outs.totals[...] = jnp.sum(mem.line_totals[...], axis=0)
    for copy in column_copies[2 * len(masks) :]:
        copy.wait()
    for copies in (attend_columns, expand_columns):
        for copy in copies:
            copy.wait_send()
    for line in [line_attend, line_output, line_reduce] + line_expand:
        line.finish()
    for line in [back_output, back_reduce] + back_attend + back_expand:
        line.finish()


def call_layer(seq, batch, inputs, teacher, lengths, variates, observed, times, frequency, bias, gains, attend, output, expand, reduce):
    rows, share, hidden = inputs.shape[0], attend.shape[1], expand.shape[2] // seq
    length, pair, chips = rows * seq, 2 * rows, seq // 2
    low = lambda *shape: pltpu.VMEM(shape, LOW)
    wide = lambda *shape: pltpu.VMEM(shape, WIDE)
    sems = lambda *shape: pltpu.SemaphoreType.DMA(shape)
    in_names = ["inputs", "teacher", "lengths", "variates", "observed"]
    in_names += ["times", "frequency", "bias", "gains"]
    in_names += ["attend", "output", "expand", "reduce"]
    outs = dict(
        layer_output=((rows, D), WIDE),
        input_gradient=((rows, D), WIDE),
        totals=((TOTAL_ROWS, LANES), WIDE),
        count=((8, LANES), WIDE),
        attend_share=((3, share, D), LOW),
        output_share=((output.shape[0], D), WIDE),
        expand_share=((2, share, hidden * seq), LOW),
        reduce_share=((reduce.shape[0], D), WIDE),
    )
    scratch = dict(
        gains=wide(2, D),
        squares=wide(8, D),
        plane_totals=wide(seq, TOTAL_ROWS, LANES),
        line_totals=wide(batch, TOTAL_ROWS, LANES),
        attend_low=low(3, share, D),
        expand_low=low(2, seq, share, hidden),
        attend_all=low(3, seq, batch, share, LANES),
        output_full=low(D, D),
        expand_all=low(2, seq, batch, share, hidden),
        reduce_all=low(batch, reduce.shape[0], D),
        own_rows=low(4, rows, D),
        act_one=low(length, D),
        act_two=low(length, D),
        branch=low(length, D),
        grad_attn=low(length, D),
        facts_own=wide(HEAD_DIM + 8, LANES),
        facts_all=wide(seq * (HEAD_DIM + 8), LANES),
        scored=wide(rows, LANES),
        cosine=wide(HEAD_DIM // 2, length),
        sine=wide(HEAD_DIM // 2, length),
        labels=wide(8, length),
        key_marks=low(HEAD_DIM, length),
        count=wide(batch, 8, LANES),
        query_turned=low(HEADS_HERE, LANES, length),
        key_turned=low(LANES, length),
        value_turned=low(LANES, length),
        key_heads=low(HEADS_HERE, length, LANES),
        value_heads=low(HEADS_HERE, length, LANES),
        query_back=low(HEADS_HERE, LANES, length),
        attend_turned=low(3 * LANES, D),
        eye=low(pair, pair),
        grad_heads=low(HEADS_HERE, length, LANES),
        grad_mixed=low(LANES, length),
        grad_mixed_out=low(seq, LANES, rows),
        probs=low(HEADS_HERE, length, length),
        mixed_out=low(length, LANES),
        mixed_rows=low(rows, D),
        hidden_turned=low(hidden, length),
        act_two_turned=low(D, length),
        exact=wide(LANES, length),
        mixed_wide=wide(LANES, pair),
        mixed_turned=low(LANES, length),
        whole=wide(pair, D),
        keep=wide(chips, rows, D),
        near_from=low(chips, rows, D),
        near=low(chips, rows, D),
        far_from=low(chips, rows, D),
        far=low(chips, rows, D),
        middle=wide(rows, D),
        grad_own=wide(rows, D),
        by_up=wide(length, hidden),
        by_gate=wide(length, hidden),
        hidden=low(length, hidden),
        grad_gate=low(length, hidden),
        grad_up=low(length, hidden),
        bias_sums=wide(8, pair),
        grad_project=low(3, length, LANES),
        act_one_turned=low(D, length),
        reduce_grad=low(batch, reduce.shape[0], D),
        expand_grad=low(2, seq, batch, share, hidden),
        output_grad=low(batch, output.shape[0], D),
        attend_grad=low(3, seq, batch, share, LANES),
        reduce_land=low(3, reduce.shape[0], D),
        expand_land=low(2, 3, 4, 2, share, hidden),
        output_land=low(3, output.shape[0], D),
        attend_land=low(3, 3, seq, share, LANES),
        expand_part=low(2, 4, 2, share, hidden),
        expand_share=low(2, seq, share, hidden),
        attend_part=low(3, seq, share, LANES),
        stage_sem=sems(5 + 2 * (expand.shape[2] // D)),
        total_send=sems(2, seq),
        total_recv=sems(2, seq),
        column_send=sems(2, seq),
        column_recv=sems(2, seq),
        line_send=sems(5, batch),
        line_recv=sems(5, batch),
        facts_send=sems(seq),
        facts_recv=sems(seq),
        gather_send=sems(4, seq),
        gather_recv=sems(4, seq),
        count_send=sems(batch),
        count_recv=sems(batch),
        near_send=sems(4, chips),
        near_recv=sems(4, chips),
        far_send=sems(4, chips),
        far_recv=sems(4, chips),
        back_send=sems(7, batch),
        back_recv=sems(7, batch),
        output_send=sems(seq),
        output_recv=sems(seq),
        mixed_send=sems(2 * seq),
        mixed_recv=sems(2 * seq),
        share_send=sems(3, seq),
        share_recv=sems(3, seq),
    )

    places = dict.fromkeys(("attend", "output", "expand", "reduce"), pl.BlockSpec(memory_space=pl.ANY))
    places["bias"] = places["lengths"] = IN_SMEM

    def kernel(*refs):
        groups, start = [], 0
        for names in (in_names, outs, scratch):
            names = list(names)
            groups.append(types.SimpleNamespace(**dict(zip(names, refs[start : start + len(names)]))))
            start += len(names)
        layer_kernel(seq, batch, *groups)

    results = pl.pallas_call(
        kernel,
        out_shape=[jax.ShapeDtypeStruct(*out) for out in outs.values()],
        in_specs=[places.get(name, IN_VMEM) for name in in_names],
        out_specs=[IN_VMEM] * len(outs),
        scratch_shapes=list(scratch.values()),
        compiler_params=pltpu.CompilerParams(
            collective_id=0, has_side_effects=True, vmem_limit_bytes=63 * MIB
        ),
        name="layer",
    )(inputs, teacher, lengths, variates, observed, times, frequency, bias, gains, attend, output, expand, reduce)
    return types.SimpleNamespace(**dict(zip(outs, results)))


def update_kernel(
    smalls, ins, small_outs, outs, olds, shares, news, copies, passed, in_sems, out_sems
):
    totals, count, gains, gains_first, gains_second, bias, bias_first, bias_second = smalls
    order = (2, 3, 0, 1)
    comes = []
    for place, number in enumerate(order):
        pairs = list(zip(ins[4 + 3 * number : 7 + 3 * number], olds[3 * number : 3 * number + 3]))
        pairs.append((ins[number], shares[number]))
        comes.append(
            [
                pltpu.make_async_copy(source, target, in_sems.at[4 * place + part])
                for part, (source, target) in enumerate(pairs)
            ]
        )
    for copy in sum(comes, []):
        copy.start()
    through = [
        pltpu.make_async_copy(ins[16 + part], passed[part], in_sems.at[16 + part]) for part in range(2)
    ]
    for copy in through:
        copy.start()
    goes = []
    gains_total = jnp.concatenate(
        [
            jnp.concatenate([totals[row + i : row + i + 1, :] for i in range(D // LANES)], axis=1)
            for row in (0, D // LANES)
        ],
        axis=0,
    )
    row = 2 * D // LANES
    bias_total = jnp.concatenate(
        [totals[row : row + 1, :HEADS], totals[row : row + 1, HEADS : 2 * HEADS]], axis=0
    )
    row += 1

    def sum_all(values):
        return jnp.sum(jnp.sum(values, axis=0, keepdims=True), axis=1, keepdims=True)

    squares = (
        totals[row : row + 1, 0:1] + sum_all(gains_total * gains_total) + sum_all(bias_total * bias_total)
    )
    grad_norm = jnp.sqrt(squares)
    clip = jnp.minimum(1.0, CLIP_NORM / grad_norm)
    small_outs[0][...] = totals[row : row + 1, 1:2] / (count[0:1, 0:1] * D)
    small_outs[1][...] = grad_norm
    rates = (RATE_ATTEND, RATE_OUTPUT, RATE_EXPAND, RATE_REDUCE)
    for place, number in enumerate(order):
        for copy in comes[place]:
            copy.wait()
        weight, first, second = olds[3 * number : 3 * number + 3]
        new, first_new, second_new = news[3 * number : 3 * number + 3]
        arrays = (new, copies[number], first_new, second_new, weight, first, second, shares[number])
        for lead in range(weight.shape[0] if weight.ndim == 3 else 1):

            def one_block(block, unused, lead=lead, arrays=arrays, rate=rates[number]):
                rows = block_of(block, 16)
                place = (lead, rows) if arrays[0].ndim == 3 else (rows,)
                old, moment, square, share = [array[place] for array in arrays[4:]]
                step = fast_step(old, moment, square, share.astype(WIDE) * clip, rate)
                arrays[0][place], arrays[2][place], arrays[3][place] = step
                arrays[1][place] = step[0].astype(LOW)
                return unused

            lax.fori_loop(0, weight.shape[-2] // 16, one_block, 0)
        for part, source in enumerate((new, copies[number], first_new, second_new)):
            copy = pltpu.make_async_copy(
                source, outs[2 + 4 * number + part], out_sems.at[2 + 4 * number + part]
            )
            copy.start()
            goes.append(copy)
        if place == 0:
            for part in range(2):
                through[part].wait()
                copy = pltpu.make_async_copy(passed[part], outs[part], out_sems.at[part])
                copy.start()
                goes.append(copy)
    for number, (old, total, rate) in enumerate(
        (
            ((gains, gains_first, gains_second), gains_total, RATE_GAINS),
            ((bias, bias_first, bias_second), bias_total, RATE_BIAS),
        )
    ):
        new, first_new, second_new = small_outs[2 + 3 * number : 5 + 3 * number]
        new[...], first_new[...], second_new[...] = adam_step(
            old[0][...], old[1][...], old[2][...], total * clip, rate, 0.0
        )
    for copy in goes:
        copy.wait()


def fast_step(weight, first, second, gradient, rate):
    first = BETA_ONE * first + (1.0 - BETA_ONE) * gradient
    second = BETA_TWO * second + ((1.0 - BETA_TWO) * gradient) * gradient
    low = jnp.sqrt(second * (1.0 / (1.0 - BETA_TWO**STEP))) + ADAM_EPS
    step = first * (rate / (1.0 - BETA_ONE**STEP)) / low
    return weight * (1.0 - rate * WEIGHT_DECAY) - step, first, second


def call_update(done, shares, smalls, olds):
    in_hbm = pl.BlockSpec(memory_space=pl.ANY)
    smalls = [done.totals, done.count] + smalls
    ins = shares + olds + [done.layer_output, done.input_gradient]
    one = jax.ShapeDtypeStruct((1, 1), WIDE)
    small_outs = [one, one] + smalls[2:]
    outs = [(done.layer_output, WIDE), (done.input_gradient, WIDE)]
    for weight in olds[::3]:
        outs += [(weight, dtype) for dtype in (WIDE, LOW, WIDE, WIDE)]
    passed = ins[-2:]
    parts = [smalls, ins, small_outs, outs, olds, shares, olds, olds[::3], passed]

    def kernel(*refs):
        groups, start = [], 0
        for part in parts:
            groups.append(refs[start : start + len(part)])
            start += len(part)
        update_kernel(*groups, *refs[start:])

    results = pl.pallas_call(
        kernel,
        out_shape=[jax.ShapeDtypeStruct(array.shape, WIDE) for array in small_outs]
        + [jax.ShapeDtypeStruct(array.shape, dtype) for array, dtype in outs],
        in_specs=[IN_VMEM] * len(smalls) + [in_hbm] * len(ins),
        out_specs=[IN_VMEM] * len(small_outs) + [in_hbm] * len(outs),
        scratch_shapes=[pltpu.VMEM(array.shape, WIDE) for array in olds]
        + [pltpu.VMEM(array.shape, array.dtype) for array in shares]
        + [pltpu.VMEM(array.shape, WIDE) for array in olds]
        + [pltpu.VMEM(array.shape, LOW) for array in olds[::3]]
        + [pltpu.VMEM(array.shape, WIDE) for array in passed]
        + [pltpu.SemaphoreType.DMA((18,)), pltpu.SemaphoreType.DMA((18,))],
        compiler_params=pltpu.CompilerParams(vmem_limit_bytes=63 * MIB),
        name="update",
    )(*smalls, *ins)
    return results[: len(small_outs)], results[len(small_outs) :]


def fast_body(
    seq,
    batch,
    inputs,
    teacher,
    lengths,
    variate_ids,
    time_ids,
    observed,
    attend_weight,
    output_weight,
    expand_weight,
    reduce_weight,
    norm_gains,
    variate_bias,
    attend_first,
    output_first,
    expand_first,
    reduce_first,
    gains_first,
    bias_first,
    attend_second,
    output_second,
    expand_second,
    reduce_second,
    gains_second,
    bias_second,
):
    half_dim = HEAD_DIM // 2
    frequency = np.exp(-math.log(ROPE_BASE) * np.arange(half_dim) / half_dim).astype(np.float32)
    frequency = np.broadcast_to(frequency[:, None], (half_dim, LANES))
    done = call_layer(
        seq,
        batch,
        inputs[0],
        teacher[0],
        lengths,
        variate_ids,
        observed,
        time_ids,
        jnp.asarray(frequency),
        variate_bias,
        norm_gains,
        attend_weight,
        output_weight,
        expand_weight,
        reduce_weight,
    )
    small, large = call_update(
        done,
        [done.attend_share, done.output_share, done.expand_share, done.reduce_share],
        [norm_gains, gains_first, gains_second, variate_bias, bias_first, bias_second],
        [attend_weight, attend_first, attend_second]
        + [output_weight, output_first, output_second]
        + [expand_weight, expand_first, expand_second]
        + [reduce_weight, reduce_first, reduce_second],
    )
    return (
        large[0][None],
        small[0].reshape(()),
        large[1][None],
        small[1].reshape(()),
    ) + tuple(large[2:] + small[2:])


def solution(mesh):
    seq, batch = mesh.shape["seq"], mesh.shape["batch"]
    body = functools.partial(fast_body, seq, batch) if fast_fits(seq, batch) else general_body
    in_specs = (
        P("batch", "seq", None),
        P("batch", "seq", None),
        P("batch"),
        P("batch", "seq"),
        P("batch", "seq"),
        P("batch", "seq"),
        P(None, ("seq", "batch"), None),
        P(("seq", "batch"), None),
        P(None, ("seq", "batch"), None),
        P(("seq", "batch"), None),
        P(),
        P(),
        P(None, ("seq", "batch"), None),
        P(("seq", "batch"), None),
        P(None, ("seq", "batch"), None),
        P(("seq", "batch"), None),
        P(),
        P(),
        P(None, ("seq", "batch"), None),
        P(("seq", "batch"), None),
        P(None, ("seq", "batch"), None),
        P(("seq", "batch"), None),
        P(),
        P(),
    )
    out_specs = (
        P("batch", "seq", None),
        P(),
        P("batch", "seq", None),
        P(),
        P(None, ("seq", "batch"), None),
        P(None, ("seq", "batch"), None),
        P(None, ("seq", "batch"), None),
        P(None, ("seq", "batch"), None),
        P(("seq", "batch"), None),
        P(("seq", "batch"), None),
        P(("seq", "batch"), None),
        P(("seq", "batch"), None),
        P(None, ("seq", "batch"), None),
        P(None, ("seq", "batch"), None),
        P(None, ("seq", "batch"), None),
        P(None, ("seq", "batch"), None),
        P(("seq", "batch"), None),
        P(("seq", "batch"), None),
        P(("seq", "batch"), None),
        P(("seq", "batch"), None),
        P(),
        P(),
        P(),
        P(),
        P(),
        P(),
    )
    return jax.shard_map(body, mesh=mesh, in_specs=in_specs, out_specs=out_specs, check_vma=False)
```

```python
import functools
import math
import types

import jax
import jax.numpy as jnp
import numpy as np
from jax import lax
from jax.experimental import pallas as pl
from jax.experimental.pallas import tpu as pltpu
from jax.sharding import PartitionSpec as P

D = 1024
HEADS = 16
HEAD_DIM = 64
STEP = 10


NORM_EPS = 1e-05
ROPE_BASE = 10000.0
MASKED = -1e30
CLIP_NORM = 1.0
BETA_ONE = 0.9
BETA_TWO = 0.98
ADAM_EPS = 1e-08
WEIGHT_DECAY = 0.1
RATE_ATTEND = 0.03
RATE_OUTPUT = 0.5
RATE_EXPAND = 0.03
RATE_REDUCE = 0.015
RATE_GAINS = 1.0
RATE_BIAS = 0.5


def angles(times):
    half_dim = HEAD_DIM // 2
    frequency = jnp.exp(-math.log(ROPE_BASE) * jnp.arange(half_dim).astype(jnp.float32) / half_dim)
    angle_table = times.astype(jnp.float32)[..., None] * frequency
    return (jnp.cos(angle_table)[..., None, :], jnp.sin(angle_table)[..., None, :])


def rotate(values, cos_table, sin_table):
    half_dim = values.shape[-1] // 2
    first_half = values[..., :half_dim]
    second_half = values[..., half_dim:]
    return jnp.concatenate(
        [
            first_half * cos_table - second_half * sin_table,
            second_half * cos_table + first_half * sin_table,
        ],
        axis=-1,
    )


def unrotate(values, cos_table, sin_table):
    half_dim = values.shape[-1] // 2
    first_half = values[..., :half_dim]
    second_half = values[..., half_dim:]
    return jnp.concatenate(
        [
            first_half * cos_table + second_half * sin_table,
            second_half * cos_table - first_half * sin_table,
        ],
        axis=-1,
    )


def normalize(values):
    inv_scale = lax.rsqrt(jnp.mean(values * values, axis=-1, keepdims=True) + NORM_EPS)
    return (values * inv_scale, inv_scale)


def norm_back(grad_act, unit_rows, inv_scale, gain_row):
    grad_unit = grad_act * gain_row
    return inv_scale * (
        grad_unit - unit_rows * jnp.mean(grad_unit * unit_rows, axis=-1, keepdims=True)
    )


def score_block(query_rows, query_labels, key_rows, key_labels, bias_table):
    scores = jnp.einsum(
        "ihe,jhe->hij", query_rows, key_rows, preferred_element_type=jnp.float32
    ) * HEAD_DIM ** (-0.5)
    same_var = query_labels[:, None] == key_labels[None, :]
    scores = scores + jnp.where(
        same_var[None], bias_table[0][:, None, None], bias_table[1][:, None, None]
    )
    scores = jnp.where(key_labels[None, None, :] >= 0, scores, MASKED)
    return (scores, same_var)


def block_grads(
    query_rows,
    query_labels,
    grad_rows,
    lse_rows,
    delta_rows,
    key_rows,
    value_rows,
    key_labels,
    bias_table,
    need_query,
    need_keys,
):
    scores, same_var = score_block(query_rows, query_labels, key_rows, key_labels, bias_table)
    weights = jnp.exp(scores - lse_rows.T[:, :, None])
    grad_weights = jnp.einsum(
        "ihe,jhe->hij", grad_rows, value_rows, preferred_element_type=jnp.float32
    )
    grad_scores = (weights * (grad_weights - delta_rows.T[:, :, None])).astype(jnp.bfloat16)
    result = ()
    if need_query:
        grad_query = jnp.einsum(
            "hij,jhe->ihe", grad_scores, key_rows, preferred_element_type=jnp.float32
        ) * HEAD_DIM ** (-0.5)
        widened = grad_scores.astype(jnp.float32)
        bias_same = jnp.sum(jnp.where(same_var[None], widened, 0.0), axis=(1, 2))
        bias_other = jnp.sum(jnp.where(same_var[None], 0.0, widened), axis=(1, 2))
        result = result + (grad_query, jnp.stack([bias_same, bias_other]))
    if need_keys:
        grad_key = jnp.einsum(
            "hij,ihe->jhe", grad_scores, query_rows, preferred_element_type=jnp.float32
        ) * HEAD_DIM ** (-0.5)
        grad_value = jnp.einsum(
            "hij,ihe->jhe",
            weights.astype(jnp.bfloat16),
            grad_rows,
            preferred_element_type=jnp.float32,
        )
        result = result + (grad_key, grad_value)
    return result


def adam_step(weight, first_moment, second_moment, gradient, step_rate, decay_rate):
    first_moment = BETA_ONE * first_moment + (1.0 - BETA_ONE) * gradient
    second_moment = BETA_TWO * second_moment + (1.0 - BETA_TWO) * gradient * gradient
    direction = (
        first_moment
        / (1.0 - BETA_ONE**STEP)
        / (jnp.sqrt(second_moment / (1.0 - BETA_TWO**STEP)) + ADAM_EPS)
    )
    return (weight - step_rate * (direction + decay_rate * weight), first_moment, second_moment)


def general_body(
    inputs,
    teacher,
    lengths,
    variate_ids,
    time_ids,
    observed,
    attend_weight,
    output_weight,
    expand_weight,
    reduce_weight,
    norm_gains,
    variate_bias,
    attend_first,
    output_first,
    expand_first,
    reduce_first,
    gains_first,
    bias_first,
    attend_second,
    output_second,
    expand_second,
    reduce_second,
    gains_second,
    bias_second,
):
    row_count = inputs.shape[1]
    length = row_count * lax.axis_size("seq")
    block_rows = math.gcd(length, 1024)
    blocks = length // block_rows
    states = inputs[0].astype(jnp.float32)
    positions = lax.axis_index("seq") * row_count + jnp.arange(row_count, dtype=jnp.int32)
    inside = positions < lengths[0]
    scored = jnp.logical_and(inside, observed[0] == 1)
    local_count = jnp.sum(scored.astype(jnp.int32))
    count_early = lax.psum(local_count, ("seq", "batch"))
    full_attend, full_output, full_expand, full_reduce = (
        lax.all_gather(attend_weight.astype(jnp.bfloat16), ("seq", "batch"), axis=1, tiled=True),
        lax.all_gather(output_weight.astype(jnp.bfloat16), ("seq", "batch"), axis=0, tiled=True),
        lax.all_gather(expand_weight.astype(jnp.bfloat16), ("seq", "batch"), axis=1, tiled=True),
        lax.all_gather(reduce_weight.astype(jnp.bfloat16), ("seq", "batch"), axis=0, tiled=True),
    )
    unit_one, scale_one = normalize(states)
    act_one = (unit_one * norm_gains[0]).astype(jnp.bfloat16)
    project = jnp.einsum("td,cde->cte", act_one, full_attend, preferred_element_type=jnp.float32)
    cos_table, sin_table = angles(time_ids[0])
    query = rotate(project[0].reshape(row_count, HEADS, HEAD_DIM), cos_table, sin_table).astype(
        jnp.bfloat16
    )
    key_rows = (
        rotate(project[1].reshape(row_count, HEADS, HEAD_DIM), cos_table, sin_table)
        .astype(jnp.bfloat16)
        .reshape(row_count, D)
    )
    value_rows = project[2].astype(jnp.bfloat16)
    own_labels = jnp.where(inside, variate_ids[0], -1).astype(jnp.bfloat16)
    all_keys, all_values, all_labels = (
        lax.all_gather(key_rows, "seq", axis=0, tiled=True),
        lax.all_gather(value_rows, "seq", axis=0, tiled=True),
        lax.all_gather(own_labels, "seq", axis=0, tiled=True),
    )
    key_blocks = all_keys.reshape(blocks, block_rows, HEADS, HEAD_DIM)
    value_blocks = all_values.reshape(blocks, block_rows, HEADS, HEAD_DIM)
    label_blocks = all_labels.astype(jnp.float32).reshape(blocks, block_rows)
    query_labels = variate_ids[0].astype(jnp.float32)

    def sweep_top(carry, pieces):
        running, sum_exp = carry
        scores, same_var = score_block(query, query_labels, pieces[0], pieces[1], variate_bias)
        raised = jnp.maximum(running, jnp.floor(jnp.max(scores, axis=-1)))
        sum_exp = sum_exp * jnp.exp(running - raised) + jnp.sum(
            jnp.exp(scores - raised[..., None]), axis=-1
        )
        return ((raised, sum_exp), None)

    start_top = jnp.full((HEADS, row_count), MASKED, jnp.float32)
    (row_top, sum_exp), unused = lax.scan(
        sweep_top,
        (start_top, jnp.zeros((HEADS, row_count), jnp.float32)),
        (key_blocks, label_blocks),
    )
    log_total = row_top + jnp.log(sum_exp)

    def sweep_out(carry, pieces):
        coarse, finest = carry
        scores, same_var = score_block(query, query_labels, pieces[0], pieces[2], variate_bias)
        weights = jnp.exp(scores - log_total[..., None])
        rounded = weights.astype(jnp.bfloat16)
        residue = (weights - rounded.astype(jnp.float32)).astype(jnp.bfloat16)
        coarse = coarse + jnp.einsum(
            "hij,jhe->ihe", rounded, pieces[1], preferred_element_type=jnp.float32
        )
        finest = finest + jnp.einsum(
            "hij,jhe->ihe", residue, pieces[1], preferred_element_type=jnp.float32
        )
        return ((coarse, finest), None)

    zero_heads = jnp.zeros((row_count, HEADS, HEAD_DIM), jnp.float32)
    (coarse, finest), unused = lax.scan(
        sweep_out, (zero_heads, zero_heads), (key_blocks, value_blocks, label_blocks)
    )
    exact_heads = coarse + finest
    mixed = coarse.reshape(row_count, D).astype(jnp.bfloat16)
    middle = states + jnp.dot(mixed, full_output, preferred_element_type=jnp.float32)
    unit_two, scale_two = normalize(middle)
    act_two = (unit_two * norm_gains[1]).astype(jnp.bfloat16)
    gate_up = jnp.einsum("td,cdf->ctf", act_two, full_expand, preferred_element_type=jnp.float32)
    sigmoid = jax.nn.sigmoid(gate_up[0])
    hidden = (gate_up[0] * sigmoid * gate_up[1]).astype(jnp.bfloat16)
    output = middle + jnp.dot(hidden, full_reduce, preferred_element_type=jnp.float32)
    error = output - teacher[0].astype(jnp.float32)
    local_square = jnp.sum(jnp.where(scored[:, None], error * error, 0.0))
    square_total = lax.psum(local_square, ("seq", "batch"))
    count_all = count_early.astype(jnp.float32)
    loss = square_total / (count_all * D)
    grad_out = jnp.where(scored[:, None], error * (2.0 / (count_all * D)), 0.0)
    back_attend, back_output, back_expand, back_reduce = (
        lax.all_gather(attend_weight.astype(jnp.bfloat16), ("seq", "batch"), axis=1, tiled=True),
        lax.all_gather(output_weight.astype(jnp.bfloat16), ("seq", "batch"), axis=0, tiled=True),
        lax.all_gather(expand_weight.astype(jnp.bfloat16), ("seq", "batch"), axis=1, tiled=True),
        lax.all_gather(reduce_weight.astype(jnp.bfloat16), ("seq", "batch"), axis=0, tiled=True),
    )
    grad_branch = grad_out.astype(jnp.bfloat16)
    reduce_grad = jnp.einsum("tf,td->fd", hidden, grad_branch, preferred_element_type=jnp.float32)
    grad_hidden = jnp.einsum(
        "td,fd->tf", grad_branch, back_reduce, preferred_element_type=jnp.float32
    )
    grad_gate = grad_hidden * gate_up[1] * sigmoid * (1.0 + gate_up[0] * (1.0 - sigmoid))
    grad_up = grad_hidden * gate_up[0] * sigmoid
    grad_expand = jnp.stack([grad_gate, grad_up]).astype(jnp.bfloat16)
    expand_grad = jnp.einsum(
        "td,ctf->cdf", act_two, grad_expand, preferred_element_type=jnp.float32
    )
    grad_act_two = jnp.einsum(
        "ctf,cdf->td", grad_expand, back_expand, preferred_element_type=jnp.float32
    )
    expand_share, reduce_share = (
        lax.psum_scatter(expand_grad, ("seq", "batch"), scatter_dimension=1, tiled=True),
        lax.psum_scatter(reduce_grad, ("seq", "batch"), scatter_dimension=0, tiled=True),
    )
    grad_middle = grad_out + norm_back(grad_act_two, unit_two, scale_two, norm_gains[1])
    grad_attn = grad_middle.astype(jnp.bfloat16)
    output_grad = jnp.einsum("td,te->de", mixed, grad_attn, preferred_element_type=jnp.float32)
    grad_mixed = jnp.einsum(
        "te,de->td", grad_attn, back_output, preferred_element_type=jnp.float32
    ).astype(jnp.bfloat16)
    grad_heads = grad_mixed.reshape(row_count, HEADS, HEAD_DIM)
    row_delta = jnp.sum(grad_heads.astype(jnp.float32) * exact_heads, axis=-1)
    lse_rows = log_total.T
    zero_bias = jnp.zeros((2, HEADS), jnp.float32)

    def sweep_query(carry, pieces):
        part_query, part_bias = block_grads(
            query,
            query_labels,
            grad_heads,
            lse_rows,
            row_delta,
            pieces[0],
            pieces[1],
            pieces[2],
            variate_bias,
            True,
            False,
        )
        return ((carry[0] + part_query, carry[1] + part_bias), None)

    (query_total, bias_grad), unused = lax.scan(
        sweep_query, (zero_heads, zero_bias), (key_blocks, value_blocks, label_blocks)
    )
    all_query, all_grad = (
        lax.all_gather(query.reshape(row_count, D), "seq", axis=0, tiled=True),
        lax.all_gather(grad_mixed, "seq", axis=0, tiled=True),
    )
    all_lse, all_delta = (
        lax.all_gather(lse_rows, "seq", axis=0, tiled=True),
        lax.all_gather(row_delta, "seq", axis=0, tiled=True),
    )
    key_heads = key_rows.reshape(row_count, HEADS, HEAD_DIM)
    value_heads = value_rows.reshape(row_count, HEADS, HEAD_DIM)
    own_float = own_labels.astype(jnp.float32)

    def sweep_keys(carry, pieces):
        part_key, part_value = block_grads(
            pieces[0],
            pieces[1],
            pieces[2],
            pieces[3],
            pieces[4],
            key_heads,
            value_heads,
            own_float,
            variate_bias,
            False,
            True,
        )
        return ((carry[0] + part_key, carry[1] + part_value), None)

    (key_total, value_heads_total), unused = lax.scan(
        sweep_keys,
        (zero_heads, zero_heads),
        (
            all_query.reshape(blocks, block_rows, HEADS, HEAD_DIM),
            label_blocks,
            all_grad.reshape(blocks, block_rows, HEADS, HEAD_DIM),
            all_lse.reshape(blocks, block_rows, HEADS),
            all_delta.reshape(blocks, block_rows, HEADS),
        ),
    )
    value_total = value_heads_total.reshape(row_count, D)
    grad_query = unrotate(query_total, cos_table, sin_table).reshape(row_count, D)
    grad_key = unrotate(key_total, cos_table, sin_table).reshape(row_count, D)
    grad_project = jnp.stack([grad_query, grad_key, value_total]).astype(jnp.bfloat16)
    attend_grad = jnp.einsum(
        "td,cte->cde", act_one, grad_project, preferred_element_type=jnp.float32
    )
    grad_act_one = jnp.einsum(
        "cte,cde->td", grad_project, back_attend, preferred_element_type=jnp.float32
    )
    attend_share, output_share = (
        lax.psum_scatter(attend_grad, ("seq", "batch"), scatter_dimension=1, tiled=True),
        lax.psum_scatter(output_grad, ("seq", "batch"), scatter_dimension=0, tiled=True),
    )
    grad_input = grad_middle + norm_back(grad_act_one, unit_one, scale_one, norm_gains[0])
    gains_grad = jnp.stack(
        [jnp.sum(grad_act_one * unit_one, axis=0), jnp.sum(grad_act_two * unit_two, axis=0)]
    )
    local_squares = (
        jnp.sum(attend_share * attend_share)
        + jnp.sum(output_share * output_share)
        + jnp.sum(expand_share * expand_share)
        + jnp.sum(reduce_share * reduce_share)
    )
    gains_total, bias_total, square_sum = lax.psum(
        (gains_grad, bias_grad, local_squares), ("seq", "batch")
    )
    grad_norm = jnp.sqrt(
        square_sum + jnp.sum(gains_total * gains_total) + jnp.sum(bias_total * bias_total)
    )
    clip_scale = jnp.minimum(1.0, CLIP_NORM / grad_norm)
    attend_new, attend_first_new, attend_second_new = adam_step(
        attend_weight,
        attend_first,
        attend_second,
        attend_share * clip_scale,
        RATE_ATTEND,
        WEIGHT_DECAY,
    )
    output_new, output_first_new, output_second_new = adam_step(
        output_weight,
        output_first,
        output_second,
        output_share * clip_scale,
        RATE_OUTPUT,
        WEIGHT_DECAY,
    )
    expand_new, expand_first_new, expand_second_new = adam_step(
        expand_weight,
        expand_first,
        expand_second,
        expand_share * clip_scale,
        RATE_EXPAND,
        WEIGHT_DECAY,
    )
    reduce_new, reduce_first_new, reduce_second_new = adam_step(
        reduce_weight,
        reduce_first,
        reduce_second,
        reduce_share * clip_scale,
        RATE_REDUCE,
        WEIGHT_DECAY,
    )
    gains_new, gains_first_new, gains_second_new = adam_step(
        norm_gains, gains_first, gains_second, gains_total * clip_scale, RATE_GAINS, 0.0
    )
    bias_new, bias_first_new, bias_second_new = adam_step(
        variate_bias, bias_first, bias_second, bias_total * clip_scale, RATE_BIAS, 0.0
    )
    input_gradient = (grad_input * count_all * D)[None]
    return (
        output[None],
        loss,
        input_gradient,
        grad_norm,
        attend_new,
        attend_new.astype(jnp.bfloat16),
        attend_first_new,
        attend_second_new,
        output_new,
        output_new.astype(jnp.bfloat16),
        output_first_new,
        output_second_new,
        expand_new,
        expand_new.astype(jnp.bfloat16),
        expand_first_new,
        expand_second_new,
        reduce_new,
        reduce_new.astype(jnp.bfloat16),
        reduce_first_new,
        reduce_second_new,
        gains_new,
        gains_first_new,
        gains_second_new,
        bias_new,
        bias_first_new,
        bias_second_new,
    )


MESH = pl.DeviceIdType.MESH
IN_VMEM = pl.BlockSpec(memory_space=pltpu.VMEM)
IN_SMEM = pl.BlockSpec(memory_space=pltpu.SMEM)
LANES = 128
HEADS_HERE = LANES // HEAD_DIM
VARIATES = 16
MIB = 1 << 20
LOW = jnp.bfloat16
WIDE = jnp.float32
TOTAL_ROWS = 24


def fast_fits(seq, batch):
    return seq == 8 and batch == 4 and seq * LANES == D


def flip(index, mask):
    result, bit = index, 1
    while bit <= mask:
        if mask & bit:
            result = result + bit - 2 * bit * lax.rem(lax.div(index, bit), 2)
        bit *= 2
    return result


def push(source, target, send_sem, recv_sem, device):
    return pltpu.make_async_remote_copy(
        src_ref=source,
        dst_ref=target,
        send_sem=send_sem,
        recv_sem=recv_sem,
        device_id=device,
        device_id_type=MESH,
    )


def block_of(index, size):
    return pl.ds(pl.multiple_of(index * size, size), size)


def dot(left, right):
    return jnp.dot(left, right, preferred_element_type=WIDE)


def dot_turned(left, right):
    return lax.dot_general(left, right, (((1,), (1,)), ((), ())), preferred_element_type=WIDE)


def turned_dot(left, right):
    return lax.dot_general(left, right, (((0,), (0,)), ((), ())), preferred_element_type=WIDE)


class Team:
    def __init__(self, index, place):
        self.index, self.place = index, place

    def at(self, mask):
        return flip(self.index, mask)


def head_team(me, group):
    return Team(me, lambda mask: (flip(me, mask), group))


def feed_team(me, group):
    return Team(
        4 * lax.rem(group, 2) + lax.rem(me, 4),
        lambda mask: (flip(me, mask % 4), flip(group, mask // 4)),
    )


class Gather:
    def __init__(self, team, rows, all_rows, sends, recvs):
        self.team, self.all_rows, self.sends, self.recvs = team, all_rows, sends, recvs
        self.size = all_rows.shape[0] // 8
        self.given = rows
        self.rows = all_rows.at[block_of(team.index, self.size)] if rows is None else rows

    def copy(self, mask, passing):
        source = self.all_rows.at[block_of(self.team.at(mask - 1 if passing else 0), self.size)]
        return push(
            source if passing else self.rows,
            source,
            self.sends.at[mask],
            self.recvs.at[mask],
            self.team.place(1 if passing else mask),
        )

    def start(self, masks=(6, 2, 4, 1)):
        for mask in masks:
            self.copy(mask, False).start()
        if self.given is not None:
            self.all_rows[block_of(self.team.index, self.size)] = self.given[...]

    def pass_on(self, chip):
        self.copy(2 * chip, False).wait_recv()
        self.copy(2 * chip + 1, True).start()

    def complete(self, chip):
        self.copy(2 * chip + 1, chip > 0).wait_recv()

    def finish(self):
        for mask in (6, 2, 4, 1):
            self.copy(mask, False).wait_send()
        for mask in (3, 5, 7):
            self.copy(mask, True).wait_send()


def at_step(step, number, *works):
    @pl.when(step == number)
    def _():
        for work in works:
            work()


def each_chip(gather, work, after):
    def one_chip(chip, unused):
        @pl.when(chip == 0)
        def _():
            gather.complete(0)

        @pl.when(chip == 1)
        def _():
            gather.pass_on(1)
            gather.pass_on(2)
            gather.copy(6, False).start()
            gather.complete(1)

        @pl.when(chip == 2)
        def _():
            gather.complete(2)

        @pl.when(chip == 3)
        def _():
            gather.pass_on(3)
            gather.complete(3)

        work(chip)
        for number, works in after.items():
            at_step(chip, number, *works)
        return unused

    lax.fori_loop(0, 4, one_chip, 0)
    gather.finish()


class Scatter:
    def __init__(self, team, buffers, near_sends, near_recvs, far_sends, far_recvs):
        self.whole, self.keep, self.near_from, self.near, self.far_from, self.far = buffers
        self.sems = near_sends, near_recvs, far_sends, far_recvs
        self.team = team
        self.size = self.keep.shape[1]

    def near_copy(self, chip):
        return push(
            self.near_from.at[chip],
            self.near.at[chip],
            self.sems[0].at[chip],
            self.sems[1].at[chip],
            self.team.place(1),
        )

    def far_copy(self, chip):
        return push(
            self.far_from.at[chip],
            self.far.at[chip],
            self.sems[2].at[chip],
            self.sems[3].at[chip],
            self.team.place(2 * chip),
        )

    def put(self, chip, rows):
        core = lax.rem(self.team.index, 2)
        self.whole[...] = rows
        self.near_from[chip] = self.whole[block_of(1 - core, self.size)].astype(LOW)
        self.near_copy(chip).start()
        self.keep[chip] = self.whole[block_of(core, self.size)]

    def combine(self, chip):
        self.near_copy(chip).wait_recv()
        self.far_from[chip] = (self.keep[chip] + self.near[chip].astype(WIDE)).astype(LOW)
        self.far_copy(chip).start()

    def total(self):
        self.near_copy(0).wait_recv()
        total = self.keep[0] + self.near[0].astype(WIDE)
        for chip in (1, 2, 3):
            self.far_copy(chip).wait_recv()
            total = total + self.far[chip].astype(WIDE)
        for chip in (0, 1, 2, 3):
            self.near_copy(chip).wait_send()
            if chip:
                self.far_copy(chip).wait_send()
        return total


class LineGather:
    def __init__(self, part_of, sends, recvs, me, group):
        self.part_of, self.sends, self.recvs, self.me, self.group = part_of, sends, recvs, me, group
        self.middle = jnp.logical_and(group >= 1, group <= 2)

    def copy(self, part, target, slot):
        return push(
            self.part_of(part),
            self.part_of(part),
            self.sends.at[slot],
            self.recvs.at[part],
            (self.me, target),
        )

    def start(self):
        group = self.group

        @pl.when(self.middle)
        def _():
            self.copy(group, 3 - group, 3 - group).start()
            self.copy(group, 3 * (group - 1), 3 * (group - 1)).start()

        @pl.when(jnp.logical_not(self.middle))
        def _():
            for step in (2, 1, 3):
                other = lax.rem(group + step, 4)
                self.copy(group, other, other).start()

    def pass_on(self):
        group = self.group

        @pl.when(self.middle)
        def _():
            self.copy(3 - group, 3 * (group - 1), group).wait_recv()
            self.copy(3 - group, 3 * (group - 1), group).start()

    def land(self):
        group = self.group

        @pl.when(self.middle)
        def _():
            for part in (0, 3):
                self.copy(part, 3 - group, group).wait_recv()

        @pl.when(jnp.logical_not(self.middle))
        def _():
            for step in (1, 2, 3):
                other = lax.rem(group + step, 4)
                self.copy(other, other, other).wait_recv()

    def finish(self):
        group = self.group

        @pl.when(self.middle)
        def _():
            for other in (3 - group, 3 * (group - 1), group):
                self.copy(group, 3 - group, other).wait_send()

        @pl.when(jnp.logical_not(self.middle))
        def _():
            for step in (1, 2, 3):
                other = lax.rem(group + step, 4)
                self.copy(group, other, other).wait_send()


class LineScatter:
    def __init__(self, part_of, landing, sends, recvs, me, group):
        self.part_of, self.landing, self.sends, self.recvs = part_of, landing, sends, recvs
        self.me, self.group = me, group
        self.middle = jnp.logical_and(group >= 1, group <= 2)
        self.opposite = 3 - 3 * lax.div(group, 2)

    def copy(self, part, slot, target, sem):
        return push(
            self.part_of(part),
            self.landing.at[slot],
            self.sends.at[sem],
            self.recvs.at[slot],
            (self.me, target),
        )

    def start(self):
        group = self.group

        @pl.when(self.middle)
        def _():
            for other in (3 - group, 3 * (group - 1)):
                self.copy(other, group, other, other).start()

        @pl.when(jnp.logical_not(self.middle))
        def _():
            beside = 1 + lax.div(group, 3)
            self.copy(3 - group, beside, beside, 3 - group).start()
            for other in (3 - beside, beside):
                self.copy(other, group, other, other).start()

    def pass_on(self):
        group, opposite = self.group, self.opposite

        @pl.when(self.middle)
        def _():
            self.copy(opposite, group, opposite, group).wait_recv()
            part = self.part_of(opposite)
            part[...] = (part[...].astype(WIDE) + self.landing[group].astype(WIDE)).astype(LOW)
            self.copy(opposite, group, opposite, group).start()

    def land(self):
        group = self.group

        @pl.when(self.middle)
        def _():
            for slot in (0, 3 - group, 3):
                self.copy(group, slot, 3 - group, group).wait_recv()

        @pl.when(jnp.logical_not(self.middle))
        def _():
            for slot in (1, 2):
                self.copy(group, slot, slot, group).wait_recv()

    def add(self, own, landed, store):
        group = self.group

        @pl.when(self.middle)
        def _():
            store(own() + landed(0) + landed(3 - group) + landed(3))

        @pl.when(jnp.logical_not(self.middle))
        def _():
            store(own() + landed(1) + landed(2))

    def finish(self):
        group = self.group

        @pl.when(self.middle)
        def _():
            for sem in (3 - group, 3 * (group - 1), group):
                self.copy(group, group, 3 - group, sem).wait_send()

        @pl.when(jnp.logical_not(self.middle))
        def _():
            for sem in (3 - group, 1, 2):
                self.copy(group, group, 1, sem).wait_send()


class QuadGather:
    def __init__(self, part_of, sends, recvs, me, group):
        self.part_of, self.sends, self.recvs = part_of, sends, recvs
        self.part = 2 * lax.div(me, 4) + lax.div(group, 2)
        self.along_y, self.along_z = (flip(me, 4), group), (me, flip(group, 2))

    def copy(self, way):
        part = self.part_of(flip(self.part, 1) if way == 3 else self.part)
        device = self.along_z if way == 1 else self.along_y
        return push(part, part, self.sends.at[way], self.recvs.at[way], device)

    def start_y(self):
        self.copy(2).start()

    def start_z(self):
        self.copy(1).start()

    def pass_on(self):
        self.copy(1).wait_recv()
        self.copy(3).start()

    def land(self):
        self.copy(2).wait_recv()
        self.copy(3).wait_recv()

    def finish(self):
        for way in (1, 2, 3):
            self.copy(way).wait_send()


class QuadScatter:
    def __init__(self, part_of, landing, sends, recvs, me, group):
        self.part_of, self.landing, self.sends, self.recvs = part_of, landing, sends, recvs
        self.part = 2 * lax.div(me, 4) + lax.div(group, 2)
        self.along_y, self.along_z = (flip(me, 4), group), (me, flip(group, 2))

    def copy(self, slot):
        return push(
            self.part_of(flip(self.part, (2, 3, 1)[slot])),
            self.landing.at[slot],
            self.sends.at[slot],
            self.recvs.at[slot],
            self.along_z if slot == 2 else self.along_y,
        )

    def start_far(self):
        self.copy(1).start()

    def start_near(self):
        self.copy(0).start()

    def pass_on(self):
        self.copy(1).wait_recv()
        part = self.part_of(flip(self.part, 1))
        part[...] = (part[...].astype(WIDE) + self.landing[1].astype(WIDE)).astype(LOW)
        self.copy(2).start()

    def land(self):
        self.copy(0).wait_recv()
        self.copy(2).wait_recv()

    def finish(self):
        for slot in (0, 1, 2):
            self.copy(slot).wait_send()


def chip_of(team, chip):
    here = lax.div(team.index, 2)
    if isinstance(chip, int):
        return flip(here, chip)
    column = lax.rem(lax.rem(here, 2) + lax.rem(chip, 2), 2)
    row = lax.rem(lax.div(here, 2) + lax.div(chip, 2), 2)
    return 2 * row + column


def turn_rows(values, cosine, sine):
    half = HEAD_DIM // 2
    pieces = []
    for start in range(0, values.shape[0], HEAD_DIM):
        first, second = values[start : start + half], values[start + half : start + HEAD_DIM]
        pieces += [first * cosine - second * sine, second * cosine + first * sine]
    return jnp.concatenate(pieces, axis=0)


def thirds(values):
    first = values.astype(LOW).astype(WIDE)
    second = (values - first).astype(LOW).astype(WIDE)
    return first, second, values - first - second


def pick(row, choices):
    result = jnp.zeros(row.shape, WIDE)
    for number, choice in choices.items():
        result = jnp.where(row == number, choice, result)
    return result


def norm_rows(values):
    scale = lax.rsqrt(jnp.mean(values * values, axis=-1, keepdims=True) + NORM_EPS)
    return values * scale, scale


def feed_block(block):
    y, x, core, far_z, near_z = (block // 16, block // 8 % 2, block // 4 % 2, block // 2 % 2, block % 2)
    return 4 * near_z + 2 * x + core, 2 * y + far_z


def layer_kernel(seq, batch, ins, outs, mem):
    me, group = lax.axis_index("seq"), lax.axis_index("batch")
    rows = ins.inputs.shape[0]
    length = rows * seq
    pair = 2 * rows
    share = ins.attend.shape[1]
    wide_columns = ins.expand.shape[2] // D
    hidden_width = mem.reduce_all.shape[0] * mem.reduce_all.shape[1]
    blocks = ins.expand.shape[2] // LANES
    heads, feeds = head_team(me, group), feed_team(me, group)
    quad = 2 * lax.div(me, 4) + lax.div(group, 2)

    staged = [(ins.attend.at[which], mem.keep.at[0, block_of(which, share)]) for which in range(3)]
    staged.append((ins.output, mem.keep.at[0, block_of(3, share)]))
    staged.append((ins.reduce, mem.keep.at[1]))
    for which in range(2):
        for block in range(wide_columns):
            columns = slice(block * D, (block + 1) * D)
            staged.append(
                (ins.expand.at[which, :, columns], mem.keep.at[2 + which, block_of(block, share)])
            )
    staged = [
        pltpu.make_async_copy(source, target, mem.stage_sem.at[number])
        for number, (source, target) in enumerate(staged)
    ]
    for copy in staged:
        copy.start()
    barrier = pltpu.get_barrier_semaphore()
    for mask in range(1, seq):
        pl.semaphore_signal(barrier, inc=1, device_id=(flip(me, mask), group), device_id_type=MESH)
    for step in range(1, batch):
        pl.semaphore_signal(
            barrier, inc=1, device_id=(me, lax.rem(group + step, batch)), device_id_type=MESH
        )
    for mask in (5, 6, 7):
        pl.semaphore_signal(barrier, inc=1, device_id=feeds.place(mask), device_id_type=MESH)

    position = me * rows + lax.broadcasted_iota(jnp.int32, (1, rows), 1)
    inside = position < ins.lengths[0]
    scored = jnp.logical_and(inside, ins.observed[...] == 1).astype(WIDE)
    variate = ins.variates[...].astype(WIDE)
    angle = ins.frequency[...] * ins.times[...].astype(WIDE)
    mem.facts_own[: HEAD_DIM // 2] = jnp.cos(angle)
    mem.facts_own[HEAD_DIM // 2 : HEAD_DIM] = jnp.sin(angle)
    mem.facts_own[HEAD_DIM:] = jnp.concatenate(
        [jnp.where(inside, variate, -1.0), variate, scored, jnp.zeros((5, rows), WIDE)], axis=0
    )
    mem.scored[...] = jnp.broadcast_to(scored, (rows, rows)).T
    for copy in staged:
        copy.wait()
    for which in range(3):
        mem.attend_low[which] = mem.keep[0, block_of(which, share)].astype(LOW)
    pl.semaphore_wait(barrier, seq + batch + 1)

    masks = (6, 7, 4, 5, 2, 3, 1)

    def start_attend_columns():
        copies = []
        for mask in masks:
            copy = push(
                mem.attend_low.at[:, :, block_of(heads.at(mask), LANES)],
                mem.attend_all.at[:, me, group],
                mem.column_send.at[0, mask],
                mem.column_recv.at[0, mask],
                heads.place(mask),
            )
            copy.start()
            copies.append(copy)
        mem.attend_all[:, me, group] = mem.attend_low[:, :, block_of(me, LANES)]
        return copies

    def start_expand_columns():
        copies = []
        for mask in masks:
            copy = push(
                mem.expand_low.at[:, feeds.at(mask)],
                mem.expand_all.at[:, me, group],
                mem.column_send.at[1, mask],
                mem.column_recv.at[1, mask],
                feeds.place(mask),
            )
            copy.start()
            copies.append(copy)
        mem.expand_all[:, me, group] = mem.expand_low[:, feeds.index]
        return copies

    def expand_part_of(array, which):
        def part_of(part):
            return array.at[which, pl.ds(4 * lax.div(part, 2), 4), pl.ds(2 * lax.rem(part, 2), 2)]

        return part_of

    def line_gather(row, part_of):
        return LineGather(part_of, mem.line_send.at[row], mem.line_recv.at[row], me, group)

    def quad_gather(row, part_of):
        return QuadGather(part_of, mem.line_send.at[row], mem.line_recv.at[row], me, group)

    def gather(team, phase, all_rows):
        return Gather(
            team,
            mem.own_rows.at[phase],
            all_rows,
            mem.gather_send.at[phase],
            mem.gather_recv.at[phase],
        )

    def scatter(team, phase):
        return Scatter(
            team,
            (mem.whole, mem.keep, mem.near_from, mem.near, mem.far_from, mem.far),
            mem.near_send.at[phase],
            mem.near_recv.at[phase],
            mem.far_send.at[phase],
            mem.far_recv.at[phase],
        )

    attend_columns = start_attend_columns()
    mem.output_full[block_of(batch * me + group, share)] = mem.keep[0, block_of(3, share)].astype(LOW)
    mem.reduce_all[quad] = mem.keep[1].astype(LOW)
    for which in range(2):
        for block in range(blocks):
            owner, part = feed_block(block)
            row, lane = divmod(block * LANES, D)
            mem.expand_low[which, owner, :, part * LANES : (part + 1) * LANES] = mem.keep[
                2 + which, block_of(row, share), lane : lane + LANES
            ].astype(LOW)
    line_output = line_gather(1, lambda part: mem.output_full.at[block_of(batch * me + part, share)])
    line_output.start()
    unit_one, scale_one = norm_rows(ins.inputs[...].astype(WIDE))
    mem.own_rows[0] = (unit_one * ins.gains[0:1, :]).astype(LOW)
    facts = Gather(heads, mem.facts_own, mem.facts_all, mem.facts_send, mem.facts_recv)
    facts.start()
    for copy in attend_columns:
        copy.wait_recv()
    line_attend = line_gather(0, lambda part: mem.attend_all.at[:, :, part])
    line_attend.start()
    acts = gather(heads, 0, mem.act_one)
    acts.start()
    for chip in (1, 2, 3):
        facts.pass_on(chip)
    for chip in (0, 1, 2, 3):
        facts.complete(chip)
    facts.finish()
    step_rows = mem.facts_own.shape[0]
    half = HEAD_DIM // 2
    count = jnp.zeros((8, LANES), WIDE)
    for slot in range(seq):
        columns = slice(slot * rows, (slot + 1) * rows)
        start = slot * step_rows
        mem.cosine[:, columns] = mem.facts_all[start : start + half]
        mem.sine[:, columns] = mem.facts_all[start + half : start + 2 * half]
        labels = mem.facts_all[start + 2 * half : start + 2 * half + 8]
        mem.labels[:, columns] = labels
        count = count + labels
    mem.count[group] = count
    count_copies = []
    for step in range(1, batch):
        copy = push(
            mem.count.at[group],
            mem.count.at[group],
            mem.count_send.at[step],
            mem.count_recv.at[step],
            (me, lax.rem(group + step, batch)),
        )
        copy.start()
        count_copies.append(copy)

    def mark(block, unused):
        span = block_of(block, pair)
        row = lax.broadcasted_iota(jnp.int32, (HEAD_DIM, pair), 0)
        third = lax.div(row, VARIATES)
        variate = lax.rem(row, VARIATES).astype(WIDE)
        key_label, query_label = mem.labels[0:1, span], mem.labels[1:2, span]
        ones = jnp.ones((1, pair), WIDE)
        last = 3 * VARIATES
        hidden_keys = (key_label < 0.0).astype(WIDE)
        mem.key_marks[:, span] = jnp.where(
            third < 3,
            (key_label == variate).astype(WIDE),
            pick(row, {last: ones, last + 1: ones, last + 2: ones, last + 3: hidden_keys}),
        ).astype(LOW)
        query_marks = (query_label == variate).astype(WIDE)
        mem.sum_marks[:, span] = jnp.where(
            row < VARIATES, query_marks, pick(row, {VARIATES: ones})
        ).astype(LOW)
        for head in range(HEADS_HERE):
            number = me * HEADS_HERE + head
            other = jnp.full((HEAD_DIM, pair), ins.bias[1, number], WIDE)
            more = thirds(jnp.full((HEAD_DIM, pair), ins.bias[0, number], WIDE) - other)
            other = thirds(other)
            mem.query_turned[head, HEAD_DIM:, span] = jnp.where(
                third < 3,
                query_marks * jnp.where(third == 0, more[0], jnp.where(third == 1, more[1], more[2])),
                pick(row, {last: other[0], last + 1: other[1], last + 2: other[2], last + 3: MASKED}),
            ).astype(LOW)
        return unused

    lax.fori_loop(0, length // pair, mark, 0)
    acts.pass_on(1)
    acts.pass_on(2)
    line_output.pass_on()
    line_output.land()
    outputs = Gather(heads, None, mem.output_full, mem.output_send, mem.output_recv)
    outputs.start()
    acts.pass_on(3)
    line_attend.pass_on()
    for chip in range(4):
        acts.complete(chip)
    acts.finish()

    expand_columns = start_expand_columns()
    line_reduce = quad_gather(4, lambda part: mem.reduce_all.at[part])
    line_reduce.start_z()
    line_expand = [
        quad_gather(2 + which, expand_part_of(mem.expand_all, which)) for which in range(2)
    ]
    line_attend.land()
    line_reduce.start_y()

    def attend_matrix(which):
        return mem.attend_all[which].reshape(D, LANES)

    def project(block, unused):
        span = block_of(block, pair)
        act = mem.act_one[span, :]
        cosine, sine = mem.cosine[:, span], mem.sine[:, span]
        query = turn_rows(dot(act, attend_matrix(0)).T, cosine, sine).astype(LOW)
        query = (query.astype(WIDE) * HEAD_DIM ** (-0.5)).astype(LOW)
        key = turn_rows(dot(act, attend_matrix(1)).T, cosine, sine).astype(LOW)
        value = dot(act, attend_matrix(2)).T.astype(LOW)
        mem.key_turned[:, span] = key
        mem.value_turned[:, span] = value

        for head in range(HEADS_HERE):
            features = slice(head * HEAD_DIM, (head + 1) * HEAD_DIM)
            mem.query_turned[head, :HEAD_DIM, span] = query[features]
            whole = jnp.concatenate([key[features], mem.key_marks[:, span]], axis=0)
            mem.key_heads[head, span, :] = whole.T
        return unused

    for copy in expand_columns:
        copy.wait_recv()
    line_expand[0].start_z()
    line_expand[0].start_y()
    lax.fori_loop(0, length // pair, project, 0)
    line_expand[1].start_z()
    outputs.pass_on(1)
    outputs.pass_on(2)

    core = lax.rem(me, 2)

    def mixed_copy(chip, which):
        other = 2 * chip_of(heads, chip) + which
        slot = 2 * chip + lax.rem(which + core, 2)
        return push(
            mem.mixed_out.at[block_of(other, rows)],
            mem.mixed_rows.at[:, block_of(me, LANES)],
            mem.mixed_send.at[slot],
            mem.mixed_recv.at[slot],
            (other, group),
        )

    def attend_block(chip):
        columns = block_of(chip_of(heads, chip), pair)
        for head in range(HEADS_HERE):
            span = slice(head * HEAD_DIM, (head + 1) * HEAD_DIM)
            scores = dot(mem.key_heads[head], mem.query_turned[head, :, columns])
            top = jnp.floor(jnp.max(scores, axis=0, keepdims=True))
            powers = jnp.exp(scores - top)
            probs = powers * (1.0 / jnp.sum(powers, axis=0, keepdims=True))
            rounded = probs.astype(LOW)
            mem.probs[head, :, columns] = rounded
            residue = (probs - rounded.astype(WIDE)).astype(LOW)
            coarse = dot(mem.value_turned[span, :], rounded)
            mem.exact[span, columns] = coarse + dot(mem.value_turned[span, :], residue)
            mem.mixed_wide[span, :] = coarse
        mixed = mem.mixed_wide[...].astype(LOW)
        mem.mixed_turned[:, columns] = mixed
        mem.mixed_out[columns, :] = mixed.T

    def attend_step(step, unused):
        chip = lax.rem(step + 1, 4)
        attend_block(chip)
        for which in range(2):

            @pl.when(jnp.logical_or(chip > 0, core != which))
            def _():
                mixed_copy(chip, which).start()

        at_step(step, 1, lambda: outputs.pass_on(3))
        return unused

    lax.fori_loop(0, 4, attend_step, 0)
    line_expand[1].start_y()
    mem.mixed_rows[:, block_of(me, LANES)] = mem.mixed_out[block_of(me, rows), :]
    for chip in range(4):
        outputs.complete(chip)
    outputs.finish()

    def wait_pieces(copy):
        for mask in range(1, seq):
            copy(mask).wait()

    def mixed_wait(mask):
        other = heads.at(mask)
        return push(
            mem.mixed_out.at[block_of(other, rows)],
            mem.mixed_rows.at[:, block_of(other, LANES)],
            mem.mixed_send.at[mask],
            mem.mixed_recv.at[mask],
            (other, group),
        )

    wait_pieces(mixed_wait)
    middle = ins.inputs[...].astype(WIDE) + dot(mem.mixed_rows[...], mem.output_full[...])
    mem.middle[...] = middle
    unit_two, scale_two = norm_rows(middle)
    mem.own_rows[1] = (unit_two * ins.gains[1:2, :]).astype(LOW)
    acts = gather(feeds, 1, mem.act_two)
    acts.start((2, 4, 1))
    line_reduce.pass_on()
    line_expand[0].pass_on()

    def split_heads(block, unused):
        span = block_of(block, pair)
        row = lax.broadcasted_iota(jnp.int32, (HEAD_DIM, pair), 0)
        value_marks = jnp.where(row < 3, 1.0, 0.0).astype(LOW)
        for head in range(HEADS_HERE):
            features = slice(head * HEAD_DIM, (head + 1) * HEAD_DIM)
            value = mem.value_turned[features, span]
            mem.value_heads[head, span, :] = jnp.concatenate([value, value_marks], axis=0).T
            query = mem.query_turned[head, :HEAD_DIM, span]
            whole = jnp.concatenate([query, mem.sum_marks[:, span]], axis=0)
            mem.query_heads[head, span, :] = whole.T
        return unused

    lax.fori_loop(0, length // pair, split_heads, 0)
    line_expand[0].land()

    def expand_matrix(which):
        return mem.expand_all[which].reshape(D, hidden_width)

    def reduce_matrix():
        return mem.reduce_all[...].reshape(hidden_width, D)

    def feed_gate(chip):
        span = block_of(chip_of(feeds, chip), pair)
        mem.by_gate[span, :] = dot(mem.act_two[span, :], expand_matrix(0))

    def feed_up(chip, unused=0):
        span = block_of(chip_of(feeds, chip), pair)
        gate = mem.by_gate[span, :]
        up = dot(mem.act_two[span, :], expand_matrix(1))
        sigmoid = 1.0 / (1.0 + jnp.exp(-gate))
        swish = gate * sigmoid
        mem.by_up[span, :] = swish
        mem.by_gate[span, :] = up * sigmoid * (1.0 + gate * (1.0 - sigmoid))
        mem.hidden[span, :] = (swish * up).astype(LOW)
        return unused

    each_chip(
        acts,
        feed_gate,
        {
            0: [line_expand[1].pass_on],
            2: [line_expand[1].land, lambda: lax.fori_loop(0, 3, feed_up, 0)],
            3: [lambda: lax.fori_loop(3, 4, feed_up, 0)],
        },
    )
    line_reduce.land()
    sums = scatter(feeds, 1)

    def feed_down(step, unused):
        chip = lax.rem(step + 1, 4)
        span = block_of(chip_of(feeds, chip), pair)
        sums.put(chip, dot(mem.hidden[span, :], reduce_matrix()))
        at_step(step, 1, lambda: sums.combine(1))
        at_step(step, 2, lambda: sums.combine(2))
        return unused

    lax.fori_loop(0, 4, feed_down, 0)
    sums.combine(3)

    for block in range(length // pair):
        span = block_of(block, pair)
        mem.hidden_turned[:, span] = mem.hidden[span, :].T
        mem.act_two_turned[:, span] = mem.act_two[span, :].T
    output = mem.middle[...] + sums.total()
    outs.layer_output[...] = output
    for copy in count_copies:
        copy.wait()
    count_all = jnp.sum(
        mem.count[0, 2:3] + mem.count[1, 2:3] + mem.count[2, 2:3] + mem.count[3, 2:3],
        axis=1,
        keepdims=True,
    )
    error = jnp.where(mem.scored[:, 0:1] > 0.0, output - ins.teacher[...].astype(WIDE), 0.0)
    mem.squares[1:2, :] = jnp.sum(error * error, axis=0, keepdims=True)
    grad_out = error * (2.0 / (count_all * D))
    mem.grad_own[...] = grad_out
    mem.own_rows[2] = grad_out.astype(LOW)
    acts = gather(feeds, 2, mem.branch)
    acts.start((2, 4, 1))

    sums = scatter(feeds, 2)

    def feed_back(chip):
        span = block_of(chip_of(feeds, chip), pair)
        grad_hidden = dot_turned(mem.branch[span, :], reduce_matrix())
        grad_gate = (grad_hidden * mem.by_gate[span, :]).astype(LOW)
        grad_up = (grad_hidden * mem.by_up[span, :]).astype(LOW)
        mem.grad_gate[span, :] = grad_gate
        mem.grad_up[span, :] = grad_up
        sums.put(
            chip,
            dot_turned(grad_gate, expand_matrix(0)) + dot_turned(grad_up, expand_matrix(1)),
        )

    each_chip(acts, feed_back, {2: [lambda: sums.combine(1)], 3: [lambda: sums.combine(2)]})

    def line_scatter(row, part_of, landing):
        return LineScatter(
            part_of, landing, mem.back_send.at[row], mem.back_recv.at[row], me, group
        )

    def quad_scatter(row, part_of, landing):
        return QuadScatter(
            part_of, landing, mem.back_send.at[row], mem.back_recv.at[row], me, group
        )

    def reduce_grad(part, unused):
        mem.reduce_grad[part] = dot(
            mem.hidden_turned[block_of(part, rows), :], mem.branch[...]
        ).astype(LOW)
        at_step(part, 0, lambda: sums.combine(3))
        return unused

    lax.fori_loop(0, batch, reduce_grad, 0)
    back_reduce = quad_scatter(0, lambda part: mem.reduce_grad.at[part], mem.reduce_land)
    back_reduce.start_far()

    def expand_grad(which):
        grads = (mem.grad_gate, mem.grad_up)[which]

        def one_block(block, unused):
            products = dot(mem.act_two_turned[block_of(block, pair), :], grads[...]).astype(LOW)
            mem.expand_grad[which, pl.ds(2 * block, 2)] = products.reshape(
                2, batch, share, hidden_width
            )
            return unused

        lax.fori_loop(0, seq // 2, one_block, 0)
        line = quad_scatter(
            1 + which, expand_part_of(mem.expand_grad, which), mem.expand_land.at[which]
        )
        return line

    back_expand = []
    back_expand.append(expand_grad(0))
    back_expand[0].start_far()
    grad_act = sums.total()
    unit_two, scale_two = norm_rows(mem.middle[...])
    gain = ins.gains[1:2, :]
    grad_unit = grad_act * gain
    mem.gains[1:2, :] = jnp.sum(grad_act * unit_two, axis=0, keepdims=True)
    grad_middle = mem.grad_own[...] + scale_two * (
        grad_unit - unit_two * jnp.mean(grad_unit * unit_two, axis=-1, keepdims=True)
    )
    mem.grad_own[...] = grad_middle
    mem.own_rows[3] = grad_middle.astype(LOW)
    grad_mixed = dot(mem.output_full[...], grad_middle.T.astype(LOW)).astype(LOW)
    mem.grad_mixed_out[...] = grad_mixed.reshape(seq, LANES, rows)

    def grad_copy(mask, back=False):
        return push(
            mem.grad_mixed_out.at[heads.at(mask)],
            mem.grad_mixed.at[:, block_of(heads.at(mask) if back else me, rows)],
            mem.mixed_send.at[8 + mask],
            mem.mixed_recv.at[8 + mask],
            heads.place(mask),
        )

    for mask in masks:
        grad_copy(mask).start()
    mem.grad_mixed[:, block_of(me, rows)] = mem.grad_mixed_out[me]
    back_reduce.pass_on()
    back_expand.append(expand_grad(1))
    back_expand[1].start_far()

    wait_pieces(lambda mask: grad_copy(mask, True))
    acts = gather(heads, 3, mem.grad_attn)
    acts.start()
    back_reduce.start_near()
    back_expand[0].start_near()
    back_attend = [
        line_scatter(
            4 + which,
            lambda part, which=which: mem.attend_grad.at[which, :, part],
            mem.attend_land.at[which],
        )
        for which in range(3)
    ]

    def attend_grad(which):
        grads = dot(mem.grad_project[which], mem.act_one[...])
        mem.attend_grad[which] = grads.T.astype(LOW).reshape(seq, batch, share, LANES)
        back_attend[which].start()

    lane = lax.broadcasted_iota(jnp.int32, (pair, LANES), 1)

    def grad_rows(block, unused):
        span = block_of(block, pair)
        whole = mem.grad_mixed[:, span].astype(WIDE).T
        for head in range(HEADS_HERE):
            mem.grad_heads[head, span, :] = jnp.where(lax.div(lane, HEAD_DIM) == head, whole, 0.0).astype(LOW)
        return unused

    lax.fori_loop(0, length // pair, grad_rows, 0)

    def value_back(block, unused):
        span = block_of(block, pair)
        total = dot(mem.probs[0, span, :], mem.grad_heads[0])
        for head in range(1, HEADS_HERE):
            total = total + dot(mem.probs[head, span, :], mem.grad_heads[head])
        mem.grad_project[2, :, span] = total.T.astype(LOW)
        return unused

    lax.fori_loop(0, length // pair, value_back, 0)
    back_expand[0].pass_on()
    attend_grad(2)

    def score_back(block, unused):
        columns = block_of(block, pair)
        row = lax.broadcasted_iota(jnp.int32, (HEAD_DIM, pair), 0)
        grads = mem.grad_mixed[:, columns]
        delta = grads.astype(WIDE) * mem.exact[:, columns]
        for head in range(HEADS_HERE):
            span = slice(head * HEAD_DIM, (head + 1) * HEAD_DIM)
            pieces = thirds(-jnp.sum(delta[span], axis=0, keepdims=True))
            marks = pick(row, dict(enumerate(pieces))).astype(LOW)
            change = dot(mem.value_heads[head], jnp.concatenate([grads[span], marks], axis=0))
            mem.probs[head, :, columns] = (mem.probs[head, :, columns].astype(WIDE) * change).astype(LOW)
        return unused

    lax.fori_loop(0, length // pair, score_back, 0)
    back_expand[1].start_near()
    mem.bias_sums[...] = jnp.zeros_like(mem.bias_sums)
    scale = HEAD_DIM ** (-0.5)

    def project_grads(block, unused):
        span = block_of(block, pair)
        cosine, sine = mem.cosine[:, span], -mem.sine[:, span]
        queries, keys = [], []
        for head in range(HEADS_HERE):
            features = slice(head * HEAD_DIM, (head + 1) * HEAD_DIM)
            queries.append(dot(mem.key_turned[features, :], mem.probs[head, :, span]) * scale)
            sums = dot(mem.probs[head, span, :], mem.query_heads[head]).T
            keys.append(sums[:HEAD_DIM])
            by_variate = sums[HEAD_DIM : HEAD_DIM + VARIATES]
            same = by_variate * mem.key_marks[:VARIATES, span].astype(WIDE)
            mem.bias_sums[head : head + 1, :] += jnp.sum(same, axis=0, keepdims=True)
            total = sums[HEAD_DIM + VARIATES : HEAD_DIM + VARIATES + 1]
            mem.bias_sums[HEADS_HERE + head : HEADS_HERE + head + 1, :] += total
        mem.grad_project[0, :, span] = turn_rows(jnp.concatenate(queries, axis=0), cosine, sine).astype(LOW)
        mem.grad_project[1, :, span] = turn_rows(jnp.concatenate(keys, axis=0), cosine, sine).astype(LOW)
        return unused

    lax.fori_loop(0, length // pair, project_grads, 0)
    back_expand[1].pass_on()
    attend_grad(0)
    acts.pass_on(1)
    acts.pass_on(2)
    sums = scatter(heads, 3)

    def project_back(step, unused):
        chip = lax.rem(step + 1, 4)
        span = block_of(chip_of(heads, chip), pair)
        total = jnp.zeros((pair, D), WIDE)
        for which in range(3):
            total = total + dot_turned(mem.grad_project[which, :, span].T, attend_matrix(which))
        sums.put(chip, total)
        at_step(step, 1, lambda: sums.combine(1))
        at_step(step, 2, lambda: sums.combine(2))
        return unused

    lax.fori_loop(0, 4, project_back, 0)
    sums.combine(3)
    attend_grad(1)
    acts.pass_on(3)
    for chip in range(4):
        acts.complete(chip)
    acts.finish()
    mem.output_grad[...] = (
        dot(mem.mixed_turned[...], mem.grad_attn[...]).astype(LOW).reshape(mem.output_grad.shape)
    )
    back_output = line_scatter(3, lambda part: mem.output_grad.at[part], mem.output_land)
    back_output.start()
    for which in (2, 0, 1):
        back_attend[which].pass_on()

    column_copies = []
    mem.squares[0:1, :] = jnp.zeros((1, D), WIDE)

    def add_squares(total):
        flat = total.reshape(-1, total.shape[-1])
        width = flat.shape[1]
        mem.squares[0:1, :width] += jnp.sum(flat * flat, axis=0, keepdims=True)

    def store_whole(total, out):
        out[...] = total
        add_squares(total)

    back_reduce.land()
    store_whole(
        mem.reduce_grad[quad].astype(WIDE)
        + mem.reduce_land[0].astype(WIDE)
        + mem.reduce_land[2].astype(WIDE),
        outs.reduce_share,
    )
    def expand_shares(which):
        back_expand[which].land()
        own = expand_part_of(mem.expand_grad, which)(quad)

        def one_block(block, unused):
            total = (
                own[block].astype(WIDE)
                + mem.expand_land[which, 0, block].astype(WIDE)
                + mem.expand_land[which, 2, block].astype(WIDE)
            )
            mem.expand_part[which, block] = total.astype(LOW)
            add_squares(total)
            return unused

        lax.fori_loop(0, 4, one_block, 0)
        for mask in masks:
            other = feeds.at(mask)
            copy = push(
                mem.expand_part.at[which, lax.rem(other, 4), lax.div(other, 4)],
                mem.expand_share.at[which, feeds.index],
                mem.share_send.at[which, mask],
                mem.share_recv.at[which, mask],
                feeds.place(mask),
            )
            copy.start()
            column_copies.append(copy)
        mem.expand_share[which, feeds.index] = mem.expand_part[
            which, lax.rem(feeds.index, 4), lax.div(feeds.index, 4)
        ]

    for which in range(2):
        expand_shares(which)

    def attend_shares(which):
        back_attend[which].land()

        def store(total):
            mem.attend_part[which] = total.astype(LOW)
            add_squares(total)

        back_attend[which].add(
            lambda: mem.attend_grad[which, :, group].astype(WIDE),
            lambda slot: mem.attend_land[which, slot].astype(WIDE),
            store,
        )

    attend_shares(2)
    grad_act = sums.total()
    unit_one, scale_one = norm_rows(ins.inputs[...].astype(WIDE))
    gain = ins.gains[0:1, :]
    grad_unit = grad_act * gain
    mem.gains[0:1, :] = jnp.sum(grad_act * unit_one, axis=0, keepdims=True)
    grad_input = mem.grad_own[...] + scale_one * (
        grad_unit - unit_one * jnp.mean(grad_unit * unit_one, axis=-1, keepdims=True)
    )
    outs.input_gradient[...] = grad_input * (count_all * D)
    outs.count[...] = jnp.broadcast_to(count_all, (8, LANES))

    back_output.pass_on()
    for which in range(2):
        attend_shares(which)
    for mask in masks:
        copy = push(
            mem.attend_part.at[:, heads.at(mask)],
            outs.attend_share.at[:, :, block_of(me, LANES)],
            mem.share_send.at[2, mask],
            mem.share_recv.at[2, mask],
            heads.place(mask),
        )
        copy.start()
        column_copies.append(copy)
    outs.attend_share[:, :, block_of(me, LANES)] = mem.attend_part[:, me]
    back_output.land()
    back_output.add(
        lambda: mem.output_grad[group].astype(WIDE),
        lambda slot: mem.output_land[slot].astype(WIDE),
        lambda total: store_whole(total, outs.output_share),
    )

    lane = lax.broadcasted_iota(jnp.int32, (1, LANES), 1)
    lines = [
        mem.gains[which : which + 1, start : start + LANES]
        for which in range(2)
        for start in range(0, D, LANES)
    ]
    bias_line = jnp.zeros((1, LANES), WIDE)
    for row in range(2 * HEADS_HERE):
        place = row // HEADS_HERE * HEADS + me * HEADS_HERE + row % HEADS_HERE
        line = mem.bias_sums[row : row + 1, :]
        if row >= HEADS_HERE:
            line = line - mem.bias_sums[row - HEADS_HERE : row - HEADS_HERE + 1, :]
        amount = jnp.sum(line, axis=1, keepdims=True)
        bias_line = bias_line + jnp.where(lane == place, amount, 0.0)
    amounts = jnp.sum(mem.squares[0:2, :], axis=1, keepdims=True)
    amount_line = jnp.where(lane == 0, amounts[0:1], 0.0) + jnp.where(lane == 1, amounts[1:2], 0.0)
    lines += [bias_line, amount_line, jnp.zeros((6, LANES), WIDE)]
    mem.plane_totals[me] = jnp.concatenate(lines, axis=0)
    plane_copies = []
    for mask in masks:
        copy = push(
            mem.plane_totals.at[me],
            mem.plane_totals.at[me],
            mem.total_send.at[0, mask],
            mem.total_recv.at[0, mask],
            (flip(me, mask), group),
        )
        copy.start()
        plane_copies.append(copy)
    for copy in column_copies[: 2 * len(masks)]:
        copy.wait()
    for which in range(2):
        for block in range(blocks):
            owner, part = feed_block(block)
            outs.expand_share[which, :, block * LANES : (block + 1) * LANES] = mem.expand_share[
                which, owner, :, part * LANES : (part + 1) * LANES
            ]
    for copy in plane_copies:
        copy.wait()
    mem.line_totals[group] = jnp.sum(mem.plane_totals[...], axis=0)
    total_copies = []
    for step in range(1, batch):
        copy = push(
            mem.line_totals.at[group],
            mem.line_totals.at[group],
            mem.total_send.at[1, step],
            mem.total_recv.at[1, step],
            (me, lax.rem(group + step, batch)),
        )
        copy.start()
        total_copies.append(copy)
    for copy in total_copies:
        copy.wait()
    outs.totals[...] = jnp.sum(mem.line_totals[...], axis=0)
    for copy in column_copies[2 * len(masks) :]:
        copy.wait()
    for copies in (attend_columns, expand_columns):
        for copy in copies:
            copy.wait_send()
    for line in [line_attend, line_output, line_reduce] + line_expand:
        line.finish()
    for line in [back_output, back_reduce] + back_attend + back_expand:
        line.finish()


def call_layer(seq, batch, inputs, teacher, lengths, variates, observed, times, frequency, bias, gains, attend, output, expand, reduce):
    rows, share, hidden = inputs.shape[0], attend.shape[1], expand.shape[2] // seq
    length, pair, chips = rows * seq, 2 * rows, seq // 2
    low = lambda *shape: pltpu.VMEM(shape, LOW)
    wide = lambda *shape: pltpu.VMEM(shape, WIDE)
    sems = lambda *shape: pltpu.SemaphoreType.DMA(shape)
    in_names = ["inputs", "teacher", "lengths", "variates", "observed"]
    in_names += ["times", "frequency", "bias", "gains"]
    in_names += ["attend", "output", "expand", "reduce"]
    outs = dict(
        layer_output=((rows, D), WIDE),
        input_gradient=((rows, D), WIDE),
        totals=((TOTAL_ROWS, LANES), WIDE),
        count=((8, LANES), WIDE),
        attend_share=((3, share, D), LOW),
        output_share=((output.shape[0], D), WIDE),
        expand_share=((2, share, hidden * seq), LOW),
        reduce_share=((reduce.shape[0], D), WIDE),
    )
    scratch = dict(
        gains=wide(2, D),
        squares=wide(8, D),
        plane_totals=wide(seq, TOTAL_ROWS, LANES),
        line_totals=wide(batch, TOTAL_ROWS, LANES),
        attend_low=low(3, share, D),
        expand_low=low(2, seq, share, hidden),
        attend_all=low(3, seq, batch, share, LANES),
        output_full=low(D, D),
        expand_all=low(2, seq, batch, share, hidden),
        reduce_all=low(batch, reduce.shape[0], D),
        own_rows=low(4, rows, D),
        act_one=low(length, D),
        act_two=low(length, D),
        branch=low(length, D),
        grad_attn=low(length, D),
        facts_own=wide(HEAD_DIM + 8, LANES),
        facts_all=wide(seq * (HEAD_DIM + 8), LANES),
        scored=wide(rows, LANES),
        cosine=wide(HEAD_DIM // 2, length),
        sine=wide(HEAD_DIM // 2, length),
        labels=wide(8, length),
        key_marks=low(HEAD_DIM, length),
        count=wide(batch, 8, LANES),
        query_turned=low(HEADS_HERE, LANES, length),
        key_turned=low(LANES, length),
        value_turned=low(LANES, length),
        key_heads=low(HEADS_HERE, length, LANES),
        value_heads=low(HEADS_HERE, length, LANES),
        query_heads=low(HEADS_HERE, length, LANES),
        grad_heads=low(HEADS_HERE, length, LANES),
        grad_mixed=low(LANES, length),
        grad_mixed_out=low(seq, LANES, rows),
        probs=low(HEADS_HERE, length, length),
        mixed_out=low(length, LANES),
        mixed_rows=low(rows, D),
        sum_marks=low(HEAD_DIM, length),
        hidden_turned=low(hidden, length),
        act_two_turned=low(D, length),
        exact=wide(LANES, length),
        mixed_wide=wide(LANES, pair),
        mixed_turned=low(LANES, length),
        whole=wide(pair, D),
        keep=wide(chips, rows, D),
        near_from=low(chips, rows, D),
        near=low(chips, rows, D),
        far_from=low(chips, rows, D),
        far=low(chips, rows, D),
        middle=wide(rows, D),
        grad_own=wide(rows, D),
        by_up=wide(length, hidden),
        by_gate=wide(length, hidden),
        hidden=low(length, hidden),
        grad_gate=low(length, hidden),
        grad_up=low(length, hidden),
        bias_sums=wide(8, pair),
        grad_project=low(3, LANES, length),
        reduce_grad=low(batch, reduce.shape[0], D),
        expand_grad=low(2, seq, batch, share, hidden),
        output_grad=low(batch, output.shape[0], D),
        attend_grad=low(3, seq, batch, share, LANES),
        reduce_land=low(3, reduce.shape[0], D),
        expand_land=low(2, 3, 4, 2, share, hidden),
        output_land=low(batch, output.shape[0], D),
        attend_land=low(3, batch, seq, share, LANES),
        expand_part=low(2, 4, 2, share, hidden),
        expand_share=low(2, seq, share, hidden),
        attend_part=low(3, seq, share, LANES),
        stage_sem=sems(5 + 2 * (expand.shape[2] // D)),
        total_send=sems(2, seq),
        total_recv=sems(2, seq),
        column_send=sems(2, seq),
        column_recv=sems(2, seq),
        line_send=sems(5, batch),
        line_recv=sems(5, batch),
        facts_send=sems(seq),
        facts_recv=sems(seq),
        gather_send=sems(4, seq),
        gather_recv=sems(4, seq),
        count_send=sems(batch),
        count_recv=sems(batch),
        near_send=sems(4, chips),
        near_recv=sems(4, chips),
        far_send=sems(4, chips),
        far_recv=sems(4, chips),
        back_send=sems(7, batch),
        back_recv=sems(7, batch),
        output_send=sems(seq),
        output_recv=sems(seq),
        mixed_send=sems(2 * seq),
        mixed_recv=sems(2 * seq),
        share_send=sems(3, seq),
        share_recv=sems(3, seq),
    )

    places = dict.fromkeys(("attend", "output", "expand", "reduce"), pl.BlockSpec(memory_space=pl.ANY))
    places["bias"] = places["lengths"] = IN_SMEM

    def kernel(*refs):
        groups, start = [], 0
        for names in (in_names, outs, scratch):
            names = list(names)
            groups.append(types.SimpleNamespace(**dict(zip(names, refs[start : start + len(names)]))))
            start += len(names)
        layer_kernel(seq, batch, *groups)

    results = pl.pallas_call(
        kernel,
        out_shape=[jax.ShapeDtypeStruct(*out) for out in outs.values()],
        in_specs=[places.get(name, IN_VMEM) for name in in_names],
        out_specs=[IN_VMEM] * len(outs),
        scratch_shapes=list(scratch.values()),
        compiler_params=pltpu.CompilerParams(
            collective_id=0, has_side_effects=True, vmem_limit_bytes=63 * MIB
        ),
        name="layer",
    )(inputs, teacher, lengths, variates, observed, times, frequency, bias, gains, attend, output, expand, reduce)
    return types.SimpleNamespace(**dict(zip(outs, results)))


def update_kernel(
    smalls, ins, small_outs, outs, olds, shares, news, copies, passed, in_sems, out_sems
):
    totals, count, gains, gains_first, gains_second, bias, bias_first, bias_second = smalls
    order = (2, 3, 0, 1)
    comes = []
    for place, number in enumerate(order):
        pairs = list(zip(ins[4 + 3 * number : 7 + 3 * number], olds[3 * number : 3 * number + 3]))
        pairs.append((ins[number], shares[number]))
        comes.append(
            [
                pltpu.make_async_copy(source, target, in_sems.at[4 * place + part])
                for part, (source, target) in enumerate(pairs)
            ]
        )
    for copy in sum(comes, []):
        copy.start()
    through = [
        pltpu.make_async_copy(ins[16 + part], passed[part], in_sems.at[16 + part]) for part in range(2)
    ]
    for copy in through:
        copy.start()
    goes = []
    gains_total = jnp.concatenate(
        [
            jnp.concatenate([totals[row + i : row + i + 1, :] for i in range(D // LANES)], axis=1)
            for row in (0, D // LANES)
        ],
        axis=0,
    )
    row = 2 * D // LANES
    bias_total = jnp.concatenate(
        [totals[row : row + 1, :HEADS], totals[row : row + 1, HEADS : 2 * HEADS]], axis=0
    )
    row += 1

    def sum_all(values):
        return jnp.sum(jnp.sum(values, axis=0, keepdims=True), axis=1, keepdims=True)

    squares = (
        totals[row : row + 1, 0:1] + sum_all(gains_total * gains_total) + sum_all(bias_total * bias_total)
    )
    grad_norm = jnp.sqrt(squares)
    clip = jnp.minimum(1.0, CLIP_NORM / grad_norm)
    small_outs[0][...] = totals[row : row + 1, 1:2] / (count[0:1, 0:1] * D)
    small_outs[1][...] = grad_norm
    rates = (RATE_ATTEND, RATE_OUTPUT, RATE_EXPAND, RATE_REDUCE)
    for place, number in enumerate(order):
        for copy in comes[place]:
            copy.wait()
        weight, first, second = olds[3 * number : 3 * number + 3]
        new, first_new, second_new = news[3 * number : 3 * number + 3]
        arrays = (new, copies[number], first_new, second_new, weight, first, second, shares[number])
        for lead in range(weight.shape[0] if weight.ndim == 3 else 1):

            def one_block(block, unused, lead=lead, arrays=arrays, rate=rates[number]):
                rows = block_of(block, 16)
                place = (lead, rows) if arrays[0].ndim == 3 else (rows,)
                old, moment, square, share = [array[place] for array in arrays[4:]]
                step = fast_step(old, moment, square, share.astype(WIDE) * clip, rate)
                arrays[0][place], arrays[2][place], arrays[3][place] = step
                arrays[1][place] = step[0].astype(LOW)
                return unused

            lax.fori_loop(0, weight.shape[-2] // 16, one_block, 0)
        for part, source in enumerate((new, copies[number], first_new, second_new)):
            copy = pltpu.make_async_copy(
                source, outs[2 + 4 * number + part], out_sems.at[2 + 4 * number + part]
            )
            copy.start()
            goes.append(copy)
        if place == 0:
            for part in range(2):
                through[part].wait()
                copy = pltpu.make_async_copy(passed[part], outs[part], out_sems.at[part])
                copy.start()
                goes.append(copy)
    for number, (old, total, rate) in enumerate(
        (
            ((gains, gains_first, gains_second), gains_total, RATE_GAINS),
            ((bias, bias_first, bias_second), bias_total, RATE_BIAS),
        )
    ):
        new, first_new, second_new = small_outs[2 + 3 * number : 5 + 3 * number]
        new[...], first_new[...], second_new[...] = adam_step(
            old[0][...], old[1][...], old[2][...], total * clip, rate, 0.0
        )
    for copy in goes:
        copy.wait()


def fast_step(weight, first, second, gradient, rate):
    first = BETA_ONE * first + (1.0 - BETA_ONE) * gradient
    second = BETA_TWO * second + ((1.0 - BETA_TWO) * gradient) * gradient
    low = jnp.sqrt(second * (1.0 / (1.0 - BETA_TWO**STEP))) + ADAM_EPS
    step = first * (rate / (1.0 - BETA_ONE**STEP)) / low
    return weight * (1.0 - rate * WEIGHT_DECAY) - step, first, second


def call_update(done, shares, smalls, olds):
    in_hbm = pl.BlockSpec(memory_space=pl.ANY)
    smalls = [done.totals, done.count] + smalls
    ins = shares + olds + [done.layer_output, done.input_gradient]
    one = jax.ShapeDtypeStruct((1, 1), WIDE)
    small_outs = [one, one] + smalls[2:]
    outs = [(done.layer_output, WIDE), (done.input_gradient, WIDE)]
    for weight in olds[::3]:
        outs += [(weight, dtype) for dtype in (WIDE, LOW, WIDE, WIDE)]
    passed = ins[-2:]
    parts = [smalls, ins, small_outs, outs, olds, shares, olds, olds[::3], passed]

    def kernel(*refs):
        groups, start = [], 0
        for part in parts:
            groups.append(refs[start : start + len(part)])
            start += len(part)
        update_kernel(*groups, *refs[start:])

    results = pl.pallas_call(
        kernel,
        out_shape=[jax.ShapeDtypeStruct(array.shape, WIDE) for array in small_outs]
        + [jax.ShapeDtypeStruct(array.shape, dtype) for array, dtype in outs],
        in_specs=[IN_VMEM] * len(smalls) + [in_hbm] * len(ins),
        out_specs=[IN_VMEM] * len(small_outs) + [in_hbm] * len(outs),
        scratch_shapes=[pltpu.VMEM(array.shape, WIDE) for array in olds]
        + [pltpu.VMEM(array.shape, array.dtype) for array in shares]
        + [pltpu.VMEM(array.shape, WIDE) for array in olds]
        + [pltpu.VMEM(array.shape, LOW) for array in olds[::3]]
        + [pltpu.VMEM(array.shape, WIDE) for array in passed]
        + [pltpu.SemaphoreType.DMA((18,)), pltpu.SemaphoreType.DMA((18,))],
        compiler_params=pltpu.CompilerParams(vmem_limit_bytes=63 * MIB),
        name="update",
    )(*smalls, *ins)
    return results[: len(small_outs)], results[len(small_outs) :]


def fast_body(
    seq,
    batch,
    inputs,
    teacher,
    lengths,
    variate_ids,
    time_ids,
    observed,
    attend_weight,
    output_weight,
    expand_weight,
    reduce_weight,
    norm_gains,
    variate_bias,
    attend_first,
    output_first,
    expand_first,
    reduce_first,
    gains_first,
    bias_first,
    attend_second,
    output_second,
    expand_second,
    reduce_second,
    gains_second,
    bias_second,
):
    half_dim = HEAD_DIM // 2
    frequency = np.exp(-math.log(ROPE_BASE) * np.arange(half_dim) / half_dim).astype(np.float32)
    frequency = np.broadcast_to(frequency[:, None], (half_dim, LANES))
    done = call_layer(
        seq,
        batch,
        inputs[0],
        teacher[0],
        lengths,
        variate_ids,
        observed,
        time_ids,
        jnp.asarray(frequency),
        variate_bias,
        norm_gains,
        attend_weight,
        output_weight,
        expand_weight,
        reduce_weight,
    )
    small, large = call_update(
        done,
        [done.attend_share, done.output_share, done.expand_share, done.reduce_share],
        [norm_gains, gains_first, gains_second, variate_bias, bias_first, bias_second],
        [attend_weight, attend_first, attend_second]
        + [output_weight, output_first, output_second]
        + [expand_weight, expand_first, expand_second]
        + [reduce_weight, reduce_first, reduce_second],
    )
    return (
        large[0][None],
        small[0].reshape(()),
        large[1][None],
        small[1].reshape(()),
    ) + tuple(large[2:] + small[2:])


def solution(mesh):
    seq, batch = mesh.shape["seq"], mesh.shape["batch"]
    body = functools.partial(fast_body, seq, batch) if fast_fits(seq, batch) else general_body
    in_specs = (
        P("batch", "seq", None),
        P("batch", "seq", None),
        P("batch"),
        P("batch", "seq"),
        P("batch", "seq"),
        P("batch", "seq"),
        P(None, ("seq", "batch"), None),
        P(("seq", "batch"), None),
        P(None, ("seq", "batch"), None),
        P(("seq", "batch"), None),
        P(),
        P(),
        P(None, ("seq", "batch"), None),
        P(("seq", "batch"), None),
        P(None, ("seq", "batch"), None),
        P(("seq", "batch"), None),
        P(),
        P(),
        P(None, ("seq", "batch"), None),
        P(("seq", "batch"), None),
        P(None, ("seq", "batch"), None),
        P(("seq", "batch"), None),
        P(),
        P(),
    )
    out_specs = (
        P("batch", "seq", None),
        P(),
        P("batch", "seq", None),
        P(),
        P(None, ("seq", "batch"), None),
        P(None, ("seq", "batch"), None),
        P(None, ("seq", "batch"), None),
        P(None, ("seq", "batch"), None),
        P(("seq", "batch"), None),
        P(("seq", "batch"), None),
        P(("seq", "batch"), None),
        P(("seq", "batch"), None),
        P(None, ("seq", "batch"), None),
        P(None, ("seq", "batch"), None),
        P(None, ("seq", "batch"), None),
        P(None, ("seq", "batch"), None),
        P(("seq", "batch"), None),
        P(("seq", "batch"), None),
        P(("seq", "batch"), None),
        P(("seq", "batch"), None),
        P(),
        P(),
        P(),
        P(),
        P(),
        P(),
    )
    return jax.shard_map(body, mesh=mesh, in_specs=in_specs, out_specs=out_specs, check_vma=False)
```

```python
import functools
import math
import types

import jax
import jax.numpy as jnp
import numpy as np
from jax import lax
from jax.experimental import pallas as pl
from jax.experimental.pallas import tpu as pltpu
from jax.sharding import PartitionSpec as P

D = 1024
HEADS = 16
HEAD_DIM = 64
STEP = 10


NORM_EPS = 1e-05
ROPE_BASE = 10000.0
MASKED = -1e30
CLIP_NORM = 1.0
BETA_ONE = 0.9
BETA_TWO = 0.98
ADAM_EPS = 1e-08
WEIGHT_DECAY = 0.1
RATE_ATTEND = 0.03
RATE_OUTPUT = 0.5
RATE_EXPAND = 0.03
RATE_REDUCE = 0.015
RATE_GAINS = 1.0
RATE_BIAS = 0.5


def angles(times):
    half_dim = HEAD_DIM // 2
    frequency = jnp.exp(-math.log(ROPE_BASE) * jnp.arange(half_dim).astype(jnp.float32) / half_dim)
    angle_table = times.astype(jnp.float32)[..., None] * frequency
    return (jnp.cos(angle_table)[..., None, :], jnp.sin(angle_table)[..., None, :])


def rotate(values, cos_table, sin_table):
    half_dim = values.shape[-1] // 2
    first_half = values[..., :half_dim]
    second_half = values[..., half_dim:]
    return jnp.concatenate(
        [
            first_half * cos_table - second_half * sin_table,
            second_half * cos_table + first_half * sin_table,
        ],
        axis=-1,
    )


def unrotate(values, cos_table, sin_table):
    half_dim = values.shape[-1] // 2
    first_half = values[..., :half_dim]
    second_half = values[..., half_dim:]
    return jnp.concatenate(
        [
            first_half * cos_table + second_half * sin_table,
            second_half * cos_table - first_half * sin_table,
        ],
        axis=-1,
    )


def normalize(values):
    inv_scale = lax.rsqrt(jnp.mean(values * values, axis=-1, keepdims=True) + NORM_EPS)
    return (values * inv_scale, inv_scale)


def norm_back(grad_act, unit_rows, inv_scale, gain_row):
    grad_unit = grad_act * gain_row
    return inv_scale * (
        grad_unit - unit_rows * jnp.mean(grad_unit * unit_rows, axis=-1, keepdims=True)
    )


def score_block(query_rows, query_labels, key_rows, key_labels, bias_table):
    scores = jnp.einsum(
        "ihe,jhe->hij", query_rows, key_rows, preferred_element_type=jnp.float32
    ) * HEAD_DIM ** (-0.5)
    same_var = query_labels[:, None] == key_labels[None, :]
    scores = scores + jnp.where(
        same_var[None], bias_table[0][:, None, None], bias_table[1][:, None, None]
    )
    scores = jnp.where(key_labels[None, None, :] >= 0, scores, MASKED)
    return (scores, same_var)


def block_grads(
    query_rows,
    query_labels,
    grad_rows,
    lse_rows,
    delta_rows,
    key_rows,
    value_rows,
    key_labels,
    bias_table,
    need_query,
    need_keys,
):
    scores, same_var = score_block(query_rows, query_labels, key_rows, key_labels, bias_table)
    weights = jnp.exp(scores - lse_rows.T[:, :, None])
    grad_weights = jnp.einsum(
        "ihe,jhe->hij", grad_rows, value_rows, preferred_element_type=jnp.float32
    )
    grad_scores = (weights * (grad_weights - delta_rows.T[:, :, None])).astype(jnp.bfloat16)
    result = ()
    if need_query:
        grad_query = jnp.einsum(
            "hij,jhe->ihe", grad_scores, key_rows, preferred_element_type=jnp.float32
        ) * HEAD_DIM ** (-0.5)
        widened = grad_scores.astype(jnp.float32)
        bias_same = jnp.sum(jnp.where(same_var[None], widened, 0.0), axis=(1, 2))
        bias_other = jnp.sum(jnp.where(same_var[None], 0.0, widened), axis=(1, 2))
        result = result + (grad_query, jnp.stack([bias_same, bias_other]))
    if need_keys:
        grad_key = jnp.einsum(
            "hij,ihe->jhe", grad_scores, query_rows, preferred_element_type=jnp.float32
        ) * HEAD_DIM ** (-0.5)
        grad_value = jnp.einsum(
            "hij,ihe->jhe",
            weights.astype(jnp.bfloat16),
            grad_rows,
            preferred_element_type=jnp.float32,
        )
        result = result + (grad_key, grad_value)
    return result


def adam_step(weight, first_moment, second_moment, gradient, step_rate, decay_rate):
    first_moment = BETA_ONE * first_moment + (1.0 - BETA_ONE) * gradient
    second_moment = BETA_TWO * second_moment + (1.0 - BETA_TWO) * gradient * gradient
    direction = (
        first_moment
        / (1.0 - BETA_ONE**STEP)
        / (jnp.sqrt(second_moment / (1.0 - BETA_TWO**STEP)) + ADAM_EPS)
    )
    return (weight - step_rate * (direction + decay_rate * weight), first_moment, second_moment)


def general_body(
    inputs,
    teacher,
    lengths,
    variate_ids,
    time_ids,
    observed,
    attend_weight,
    output_weight,
    expand_weight,
    reduce_weight,
    norm_gains,
    variate_bias,
    attend_first,
    output_first,
    expand_first,
    reduce_first,
    gains_first,
    bias_first,
    attend_second,
    output_second,
    expand_second,
    reduce_second,
    gains_second,
    bias_second,
):
    row_count = inputs.shape[1]
    length = row_count * lax.axis_size("seq")
    block_rows = math.gcd(length, 1024)
    blocks = length // block_rows
    states = inputs[0].astype(jnp.float32)
    positions = lax.axis_index("seq") * row_count + jnp.arange(row_count, dtype=jnp.int32)
    inside = positions < lengths[0]
    scored = jnp.logical_and(inside, observed[0] == 1)
    local_count = jnp.sum(scored.astype(jnp.int32))
    count_early = lax.psum(local_count, ("seq", "batch"))
    full_attend, full_output, full_expand, full_reduce = (
        lax.all_gather(attend_weight.astype(jnp.bfloat16), ("seq", "batch"), axis=1, tiled=True),
        lax.all_gather(output_weight.astype(jnp.bfloat16), ("seq", "batch"), axis=0, tiled=True),
        lax.all_gather(expand_weight.astype(jnp.bfloat16), ("seq", "batch"), axis=1, tiled=True),
        lax.all_gather(reduce_weight.astype(jnp.bfloat16), ("seq", "batch"), axis=0, tiled=True),
    )
    unit_one, scale_one = normalize(states)
    act_one = (unit_one * norm_gains[0]).astype(jnp.bfloat16)
    project = jnp.einsum("td,cde->cte", act_one, full_attend, preferred_element_type=jnp.float32)
    cos_table, sin_table = angles(time_ids[0])
    query = rotate(project[0].reshape(row_count, HEADS, HEAD_DIM), cos_table, sin_table).astype(
        jnp.bfloat16
    )
    key_rows = (
        rotate(project[1].reshape(row_count, HEADS, HEAD_DIM), cos_table, sin_table)
        .astype(jnp.bfloat16)
        .reshape(row_count, D)
    )
    value_rows = project[2].astype(jnp.bfloat16)
    own_labels = jnp.where(inside, variate_ids[0], -1).astype(jnp.bfloat16)
    all_keys, all_values, all_labels = (
        lax.all_gather(key_rows, "seq", axis=0, tiled=True),
        lax.all_gather(value_rows, "seq", axis=0, tiled=True),
        lax.all_gather(own_labels, "seq", axis=0, tiled=True),
    )
    key_blocks = all_keys.reshape(blocks, block_rows, HEADS, HEAD_DIM)
    value_blocks = all_values.reshape(blocks, block_rows, HEADS, HEAD_DIM)
    label_blocks = all_labels.astype(jnp.float32).reshape(blocks, block_rows)
    query_labels = variate_ids[0].astype(jnp.float32)

    def sweep_top(carry, pieces):
        running, sum_exp = carry
        scores, same_var = score_block(query, query_labels, pieces[0], pieces[1], variate_bias)
        raised = jnp.maximum(running, jnp.floor(jnp.max(scores, axis=-1)))
        sum_exp = sum_exp * jnp.exp(running - raised) + jnp.sum(
            jnp.exp(scores - raised[..., None]), axis=-1
        )
        return ((raised, sum_exp), None)

    start_top = jnp.full((HEADS, row_count), MASKED, jnp.float32)
    (row_top, sum_exp), unused = lax.scan(
        sweep_top,
        (start_top, jnp.zeros((HEADS, row_count), jnp.float32)),
        (key_blocks, label_blocks),
    )
    log_total = row_top + jnp.log(sum_exp)

    def sweep_out(carry, pieces):
        coarse, finest = carry
        scores, same_var = score_block(query, query_labels, pieces[0], pieces[2], variate_bias)
        weights = jnp.exp(scores - log_total[..., None])
        rounded = weights.astype(jnp.bfloat16)
        residue = (weights - rounded.astype(jnp.float32)).astype(jnp.bfloat16)
        coarse = coarse + jnp.einsum(
            "hij,jhe->ihe", rounded, pieces[1], preferred_element_type=jnp.float32
        )
        finest = finest + jnp.einsum(
            "hij,jhe->ihe", residue, pieces[1], preferred_element_type=jnp.float32
        )
        return ((coarse, finest), None)

    zero_heads = jnp.zeros((row_count, HEADS, HEAD_DIM), jnp.float32)
    (coarse, finest), unused = lax.scan(
        sweep_out, (zero_heads, zero_heads), (key_blocks, value_blocks, label_blocks)
    )
    exact_heads = coarse + finest
    mixed = coarse.reshape(row_count, D).astype(jnp.bfloat16)
    middle = states + jnp.dot(mixed, full_output, preferred_element_type=jnp.float32)
    unit_two, scale_two = normalize(middle)
    act_two = (unit_two * norm_gains[1]).astype(jnp.bfloat16)
    gate_up = jnp.einsum("td,cdf->ctf", act_two, full_expand, preferred_element_type=jnp.float32)
    sigmoid = jax.nn.sigmoid(gate_up[0])
    hidden = (gate_up[0] * sigmoid * gate_up[1]).astype(jnp.bfloat16)
    output = middle + jnp.dot(hidden, full_reduce, preferred_element_type=jnp.float32)
    error = output - teacher[0].astype(jnp.float32)
    local_square = jnp.sum(jnp.where(scored[:, None], error * error, 0.0))
    square_total = lax.psum(local_square, ("seq", "batch"))
    count_all = count_early.astype(jnp.float32)
    loss = square_total / (count_all * D)
    grad_out = jnp.where(scored[:, None], error * (2.0 / (count_all * D)), 0.0)
    back_attend, back_output, back_expand, back_reduce = (
        lax.all_gather(attend_weight.astype(jnp.bfloat16), ("seq", "batch"), axis=1, tiled=True),
        lax.all_gather(output_weight.astype(jnp.bfloat16), ("seq", "batch"), axis=0, tiled=True),
        lax.all_gather(expand_weight.astype(jnp.bfloat16), ("seq", "batch"), axis=1, tiled=True),
        lax.all_gather(reduce_weight.astype(jnp.bfloat16), ("seq", "batch"), axis=0, tiled=True),
    )
    grad_branch = grad_out.astype(jnp.bfloat16)
    reduce_grad = jnp.einsum("tf,td->fd", hidden, grad_branch, preferred_element_type=jnp.float32)
    grad_hidden = jnp.einsum(
        "td,fd->tf", grad_branch, back_reduce, preferred_element_type=jnp.float32
    )
    grad_gate = grad_hidden * gate_up[1] * sigmoid * (1.0 + gate_up[0] * (1.0 - sigmoid))
    grad_up = grad_hidden * gate_up[0] * sigmoid
    grad_expand = jnp.stack([grad_gate, grad_up]).astype(jnp.bfloat16)
    expand_grad = jnp.einsum(
        "td,ctf->cdf", act_two, grad_expand, preferred_element_type=jnp.float32
    )
    grad_act_two = jnp.einsum(
        "ctf,cdf->td", grad_expand, back_expand, preferred_element_type=jnp.float32
    )
    expand_share, reduce_share = (
        lax.psum_scatter(expand_grad, ("seq", "batch"), scatter_dimension=1, tiled=True),
        lax.psum_scatter(reduce_grad, ("seq", "batch"), scatter_dimension=0, tiled=True),
    )
    grad_middle = grad_out + norm_back(grad_act_two, unit_two, scale_two, norm_gains[1])
    grad_attn = grad_middle.astype(jnp.bfloat16)
    output_grad = jnp.einsum("td,te->de", mixed, grad_attn, preferred_element_type=jnp.float32)
    grad_mixed = jnp.einsum(
        "te,de->td", grad_attn, back_output, preferred_element_type=jnp.float32
    ).astype(jnp.bfloat16)
    grad_heads = grad_mixed.reshape(row_count, HEADS, HEAD_DIM)
    row_delta = jnp.sum(grad_heads.astype(jnp.float32) * exact_heads, axis=-1)
    lse_rows = log_total.T
    zero_bias = jnp.zeros((2, HEADS), jnp.float32)

    def sweep_query(carry, pieces):
        part_query, part_bias = block_grads(
            query,
            query_labels,
            grad_heads,
            lse_rows,
            row_delta,
            pieces[0],
            pieces[1],
            pieces[2],
            variate_bias,
            True,
            False,
        )
        return ((carry[0] + part_query, carry[1] + part_bias), None)

    (query_total, bias_grad), unused = lax.scan(
        sweep_query, (zero_heads, zero_bias), (key_blocks, value_blocks, label_blocks)
    )
    all_query, all_grad = (
        lax.all_gather(query.reshape(row_count, D), "seq", axis=0, tiled=True),
        lax.all_gather(grad_mixed, "seq", axis=0, tiled=True),
    )
    all_lse, all_delta = (
        lax.all_gather(lse_rows, "seq", axis=0, tiled=True),
        lax.all_gather(row_delta, "seq", axis=0, tiled=True),
    )
    key_heads = key_rows.reshape(row_count, HEADS, HEAD_DIM)
    value_heads = value_rows.reshape(row_count, HEADS, HEAD_DIM)
    own_float = own_labels.astype(jnp.float32)

    def sweep_keys(carry, pieces):
        part_key, part_value = block_grads(
            pieces[0],
            pieces[1],
            pieces[2],
            pieces[3],
            pieces[4],
            key_heads,
            value_heads,
            own_float,
            variate_bias,
            False,
            True,
        )
        return ((carry[0] + part_key, carry[1] + part_value), None)

    (key_total, value_heads_total), unused = lax.scan(
        sweep_keys,
        (zero_heads, zero_heads),
        (
            all_query.reshape(blocks, block_rows, HEADS, HEAD_DIM),
            label_blocks,
            all_grad.reshape(blocks, block_rows, HEADS, HEAD_DIM),
            all_lse.reshape(blocks, block_rows, HEADS),
            all_delta.reshape(blocks, block_rows, HEADS),
        ),
    )
    value_total = value_heads_total.reshape(row_count, D)
    grad_query = unrotate(query_total, cos_table, sin_table).reshape(row_count, D)
    grad_key = unrotate(key_total, cos_table, sin_table).reshape(row_count, D)
    grad_project = jnp.stack([grad_query, grad_key, value_total]).astype(jnp.bfloat16)
    attend_grad = jnp.einsum(
        "td,cte->cde", act_one, grad_project, preferred_element_type=jnp.float32
    )
    grad_act_one = jnp.einsum(
        "cte,cde->td", grad_project, back_attend, preferred_element_type=jnp.float32
    )
    attend_share, output_share = (
        lax.psum_scatter(attend_grad, ("seq", "batch"), scatter_dimension=1, tiled=True),
        lax.psum_scatter(output_grad, ("seq", "batch"), scatter_dimension=0, tiled=True),
    )
    grad_input = grad_middle + norm_back(grad_act_one, unit_one, scale_one, norm_gains[0])
    gains_grad = jnp.stack(
        [jnp.sum(grad_act_one * unit_one, axis=0), jnp.sum(grad_act_two * unit_two, axis=0)]
    )
    local_squares = (
        jnp.sum(attend_share * attend_share)
        + jnp.sum(output_share * output_share)
        + jnp.sum(expand_share * expand_share)
        + jnp.sum(reduce_share * reduce_share)
    )
    gains_total, bias_total, square_sum = lax.psum(
        (gains_grad, bias_grad, local_squares), ("seq", "batch")
    )
    grad_norm = jnp.sqrt(
        square_sum + jnp.sum(gains_total * gains_total) + jnp.sum(bias_total * bias_total)
    )
    clip_scale = jnp.minimum(1.0, CLIP_NORM / grad_norm)
    attend_new, attend_first_new, attend_second_new = adam_step(
        attend_weight,
        attend_first,
        attend_second,
        attend_share * clip_scale,
        RATE_ATTEND,
        WEIGHT_DECAY,
    )
    output_new, output_first_new, output_second_new = adam_step(
        output_weight,
        output_first,
        output_second,
        output_share * clip_scale,
        RATE_OUTPUT,
        WEIGHT_DECAY,
    )
    expand_new, expand_first_new, expand_second_new = adam_step(
        expand_weight,
        expand_first,
        expand_second,
        expand_share * clip_scale,
        RATE_EXPAND,
        WEIGHT_DECAY,
    )
    reduce_new, reduce_first_new, reduce_second_new = adam_step(
        reduce_weight,
        reduce_first,
        reduce_second,
        reduce_share * clip_scale,
        RATE_REDUCE,
        WEIGHT_DECAY,
    )
    gains_new, gains_first_new, gains_second_new = adam_step(
        norm_gains, gains_first, gains_second, gains_total * clip_scale, RATE_GAINS, 0.0
    )
    bias_new, bias_first_new, bias_second_new = adam_step(
        variate_bias, bias_first, bias_second, bias_total * clip_scale, RATE_BIAS, 0.0
    )
    input_gradient = (grad_input * count_all * D)[None]
    return (
        output[None],
        loss,
        input_gradient,
        grad_norm,
        attend_new,
        attend_new.astype(jnp.bfloat16),
        attend_first_new,
        attend_second_new,
        output_new,
        output_new.astype(jnp.bfloat16),
        output_first_new,
        output_second_new,
        expand_new,
        expand_new.astype(jnp.bfloat16),
        expand_first_new,
        expand_second_new,
        reduce_new,
        reduce_new.astype(jnp.bfloat16),
        reduce_first_new,
        reduce_second_new,
        gains_new,
        gains_first_new,
        gains_second_new,
        bias_new,
        bias_first_new,
        bias_second_new,
    )


MESH = pl.DeviceIdType.MESH
IN_VMEM = pl.BlockSpec(memory_space=pltpu.VMEM)
IN_SMEM = pl.BlockSpec(memory_space=pltpu.SMEM)
LANES = 128
HEADS_HERE = LANES // HEAD_DIM
VARIATES = 16
MIB = 1 << 20
LOW = jnp.bfloat16
WIDE = jnp.float32
TOTAL_ROWS = 24


def fast_fits(seq, batch):
    return seq == 8 and batch == 4 and seq * LANES == D


def flip(index, mask):
    result, bit = index, 1
    while bit <= mask:
        if mask & bit:
            result = result + bit - 2 * bit * lax.rem(lax.div(index, bit), 2)
        bit *= 2
    return result


def push(source, target, send_sem, recv_sem, device):
    return pltpu.make_async_remote_copy(
        src_ref=source,
        dst_ref=target,
        send_sem=send_sem,
        recv_sem=recv_sem,
        device_id=device,
        device_id_type=MESH,
    )


def block_of(index, size):
    return pl.ds(pl.multiple_of(index * size, size), size)


def dot(left, right):
    return jnp.dot(left, right, preferred_element_type=WIDE)


def dot_turned(left, right):
    return lax.dot_general(left, right, (((1,), (1,)), ((), ())), preferred_element_type=WIDE)


def turned_dot(left, right):
    return lax.dot_general(left, right, (((0,), (0,)), ((), ())), preferred_element_type=WIDE)


class Team:
    def __init__(self, index, place):
        self.index, self.place = index, place

    def at(self, mask):
        return flip(self.index, mask)


def head_team(me, group):
    return Team(me, lambda mask: (flip(me, mask), group))


def feed_team(me, group):
    return Team(
        4 * lax.rem(group, 2) + lax.rem(me, 4),
        lambda mask: (flip(me, mask % 4), flip(group, mask // 4)),
    )


class Gather:
    def __init__(self, team, rows, all_rows, sends, recvs):
        self.team, self.all_rows, self.sends, self.recvs = team, all_rows, sends, recvs
        self.size = all_rows.shape[0] // 8
        self.given = rows
        self.rows = all_rows.at[block_of(team.index, self.size)] if rows is None else rows

    def copy(self, mask, passing):
        source = self.all_rows.at[block_of(self.team.at(mask - 1 if passing else 0), self.size)]
        return push(
            source if passing else self.rows,
            source,
            self.sends.at[mask],
            self.recvs.at[mask],
            self.team.place(1 if passing else mask),
        )

    def start(self, masks=(6, 2, 4, 1)):
        for mask in masks:
            self.copy(mask, False).start()
        if self.given is not None:
            self.all_rows[block_of(self.team.index, self.size)] = self.given[...]

    def pass_on(self, chip):
        self.copy(2 * chip, False).wait_recv()
        self.copy(2 * chip + 1, True).start()

    def complete(self, chip):
        self.copy(2 * chip + 1, chip > 0).wait_recv()

    def finish(self):
        for mask in (6, 2, 4, 1):
            self.copy(mask, False).wait_send()
        for mask in (3, 5, 7):
            self.copy(mask, True).wait_send()


def at_step(step, number, *works):
    @pl.when(step == number)
    def _():
        for work in works:
            work()


def each_chip(gather, work, after):
    def one_chip(chip, unused):
        @pl.when(chip == 0)
        def _():
            gather.complete(0)

        @pl.when(chip == 1)
        def _():
            gather.pass_on(1)
            gather.pass_on(2)
            gather.copy(6, False).start()
            gather.complete(1)

        @pl.when(chip == 2)
        def _():
            gather.complete(2)

        @pl.when(chip == 3)
        def _():
            gather.pass_on(3)
            gather.complete(3)

        work(chip)
        for number, works in after.items():
            at_step(chip, number, *works)
        return unused

    lax.fori_loop(0, 4, one_chip, 0)
    gather.finish()


class Scatter:
    def __init__(self, team, buffers, near_sends, near_recvs, far_sends, far_recvs):
        self.whole, self.keep, self.near_from, self.near, self.far_from, self.far = buffers
        self.sems = near_sends, near_recvs, far_sends, far_recvs
        self.team = team
        self.size = self.keep.shape[1]

    def near_copy(self, chip):
        return push(
            self.near_from.at[chip],
            self.near.at[chip],
            self.sems[0].at[chip],
            self.sems[1].at[chip],
            self.team.place(1),
        )

    def far_copy(self, chip):
        return push(
            self.far_from.at[chip],
            self.far.at[chip],
            self.sems[2].at[chip],
            self.sems[3].at[chip],
            self.team.place(2 * chip),
        )

    def put(self, chip, rows):
        core = lax.rem(self.team.index, 2)
        self.whole[...] = rows
        self.near_from[chip] = self.whole[block_of(1 - core, self.size)].astype(LOW)
        self.near_copy(chip).start()
        self.keep[chip] = self.whole[block_of(core, self.size)]

    def combine(self, chip):
        self.near_copy(chip).wait_recv()
        self.far_from[chip] = (self.keep[chip] + self.near[chip].astype(WIDE)).astype(LOW)
        self.far_copy(chip).start()

    def total(self):
        self.near_copy(0).wait_recv()
        total = self.keep[0] + self.near[0].astype(WIDE)
        for chip in (1, 2, 3):
            self.far_copy(chip).wait_recv()
            total = total + self.far[chip].astype(WIDE)
        for chip in (0, 1, 2, 3):
            self.near_copy(chip).wait_send()
            if chip:
                self.far_copy(chip).wait_send()
        return total


class LineGather:
    def __init__(self, part_of, sends, recvs, me, group):
        self.part_of, self.sends, self.recvs, self.me, self.group = part_of, sends, recvs, me, group
        self.middle = jnp.logical_and(group >= 1, group <= 2)

    def copy(self, part, target, slot):
        return push(
            self.part_of(part),
            self.part_of(part),
            self.sends.at[slot],
            self.recvs.at[part],
            (self.me, target),
        )

    def start(self):
        group = self.group

        @pl.when(self.middle)
        def _():
            self.copy(group, 3 - group, 3 - group).start()
            self.copy(group, 3 * (group - 1), 3 * (group - 1)).start()

        @pl.when(jnp.logical_not(self.middle))
        def _():
            for step in (2, 1, 3):
                other = lax.rem(group + step, 4)
                self.copy(group, other, other).start()

    def pass_on(self):
        group = self.group

        @pl.when(self.middle)
        def _():
            self.copy(3 - group, 3 * (group - 1), group).wait_recv()
            self.copy(3 - group, 3 * (group - 1), group).start()

    def land(self):
        group = self.group

        @pl.when(self.middle)
        def _():
            for part in (0, 3):
                self.copy(part, 3 - group, group).wait_recv()

        @pl.when(jnp.logical_not(self.middle))
        def _():
            for step in (1, 2, 3):
                other = lax.rem(group + step, 4)
                self.copy(other, other, other).wait_recv()

    def finish(self):
        group = self.group

        @pl.when(self.middle)
        def _():
            for other in (3 - group, 3 * (group - 1), group):
                self.copy(group, 3 - group, other).wait_send()

        @pl.when(jnp.logical_not(self.middle))
        def _():
            for step in (1, 2, 3):
                other = lax.rem(group + step, 4)
                self.copy(group, other, other).wait_send()


class LineScatter:
    def __init__(self, part_of, landing, sends, recvs, me, group):
        self.part_of, self.landing, self.sends, self.recvs = part_of, landing, sends, recvs
        self.me, self.group = me, group
        self.middle = jnp.logical_and(group >= 1, group <= 2)
        self.opposite = 3 - 3 * lax.div(group, 2)

    def copy(self, part, slot, target, sem):
        return push(
            self.part_of(part),
            self.landing.at[slot],
            self.sends.at[sem],
            self.recvs.at[slot],
            (self.me, target),
        )

    def start(self):
        group = self.group

        @pl.when(self.middle)
        def _():
            for other in (3 - group, 3 * (group - 1)):
                self.copy(other, group, other, other).start()

        @pl.when(jnp.logical_not(self.middle))
        def _():
            beside = 1 + lax.div(group, 3)
            self.copy(3 - group, beside, beside, 3 - group).start()
            for other in (3 - beside, beside):
                self.copy(other, group, other, other).start()

    def pass_on(self):
        group, opposite = self.group, self.opposite

        @pl.when(self.middle)
        def _():
            self.copy(opposite, group, opposite, group).wait_recv()
            part = self.part_of(opposite)
            part[...] = (part[...].astype(WIDE) + self.landing[group].astype(WIDE)).astype(LOW)
            self.copy(opposite, group, opposite, group).start()

    def land(self):
        group = self.group

        @pl.when(self.middle)
        def _():
            for slot in (0, 3 - group, 3):
                self.copy(group, slot, 3 - group, group).wait_recv()

        @pl.when(jnp.logical_not(self.middle))
        def _():
            for slot in (1, 2):
                self.copy(group, slot, slot, group).wait_recv()

    def add(self, own, landed, store):
        group = self.group

        @pl.when(self.middle)
        def _():
            store(own() + landed(0) + landed(3 - group) + landed(3))

        @pl.when(jnp.logical_not(self.middle))
        def _():
            store(own() + landed(1) + landed(2))

    def finish(self):
        group = self.group

        @pl.when(self.middle)
        def _():
            for sem in (3 - group, 3 * (group - 1), group):
                self.copy(group, group, 3 - group, sem).wait_send()

        @pl.when(jnp.logical_not(self.middle))
        def _():
            for sem in (3 - group, 1, 2):
                self.copy(group, group, 1, sem).wait_send()


class QuadGather:
    def __init__(self, part_of, sends, recvs, me, group):
        self.part_of, self.sends, self.recvs = part_of, sends, recvs
        self.part = 2 * lax.div(me, 4) + lax.div(group, 2)
        self.along_y, self.along_z = (flip(me, 4), group), (me, flip(group, 2))

    def copy(self, way):
        part = self.part_of(flip(self.part, 1) if way == 3 else self.part)
        device = self.along_z if way == 1 else self.along_y
        return push(part, part, self.sends.at[way], self.recvs.at[way], device)

    def start_y(self):
        self.copy(2).start()

    def start_z(self):
        self.copy(1).start()

    def pass_on(self):
        self.copy(1).wait_recv()
        self.copy(3).start()

    def land(self):
        self.copy(2).wait_recv()
        self.copy(3).wait_recv()

    def finish(self):
        for way in (1, 2, 3):
            self.copy(way).wait_send()


class QuadScatter:
    def __init__(self, part_of, landing, sends, recvs, me, group):
        self.part_of, self.landing, self.sends, self.recvs = part_of, landing, sends, recvs
        self.part = 2 * lax.div(me, 4) + lax.div(group, 2)
        self.along_y, self.along_z = (flip(me, 4), group), (me, flip(group, 2))

    def copy(self, slot):
        return push(
            self.part_of(flip(self.part, (2, 3, 1)[slot])),
            self.landing.at[slot],
            self.sends.at[slot],
            self.recvs.at[slot],
            self.along_z if slot == 2 else self.along_y,
        )

    def start_far(self):
        self.copy(1).start()

    def start_near(self):
        self.copy(0).start()

    def pass_on(self):
        self.copy(1).wait_recv()
        part = self.part_of(flip(self.part, 1))
        part[...] = (part[...].astype(WIDE) + self.landing[1].astype(WIDE)).astype(LOW)
        self.copy(2).start()

    def land(self):
        self.copy(0).wait_recv()
        self.copy(2).wait_recv()

    def finish(self):
        for slot in (0, 1, 2):
            self.copy(slot).wait_send()


def chip_of(team, chip):
    here = lax.div(team.index, 2)
    if isinstance(chip, int):
        return flip(here, chip)
    column = lax.rem(lax.rem(here, 2) + lax.rem(chip, 2), 2)
    row = lax.rem(lax.div(here, 2) + lax.div(chip, 2), 2)
    return 2 * row + column


def turn_rows(values, cosine, sine):
    half = HEAD_DIM // 2
    pieces = []
    for start in range(0, values.shape[0], HEAD_DIM):
        first, second = values[start : start + half], values[start + half : start + HEAD_DIM]
        pieces += [first * cosine - second * sine, second * cosine + first * sine]
    return jnp.concatenate(pieces, axis=0)


def thirds(values):
    first = values.astype(LOW).astype(WIDE)
    second = (values - first).astype(LOW).astype(WIDE)
    return first, second, values - first - second


def pick(row, choices):
    result = jnp.zeros(row.shape, WIDE)
    for number, choice in choices.items():
        result = jnp.where(row == number, choice, result)
    return result


def norm_rows(values):
    scale = lax.rsqrt(jnp.mean(values * values, axis=-1, keepdims=True) + NORM_EPS)
    return values * scale, scale


def feed_block(block):
    y, x, core, far_z, near_z = (block // 16, block // 8 % 2, block // 4 % 2, block // 2 % 2, block % 2)
    return 4 * near_z + 2 * x + core, 2 * y + far_z


def layer_kernel(seq, batch, ins, outs, mem):
    me, group = lax.axis_index("seq"), lax.axis_index("batch")
    rows = ins.inputs.shape[0]
    length = rows * seq
    pair = 2 * rows
    share = ins.attend.shape[1]
    wide_columns = ins.expand.shape[2] // D
    hidden_width = mem.reduce_all.shape[0] * mem.reduce_all.shape[1]
    blocks = ins.expand.shape[2] // LANES
    heads, feeds = head_team(me, group), feed_team(me, group)
    quad = 2 * lax.div(me, 4) + lax.div(group, 2)

    staged = [(ins.attend.at[which], mem.keep.at[0, block_of(which, share)]) for which in range(3)]
    staged.append((ins.output, mem.keep.at[0, block_of(3, share)]))
    staged.append((ins.reduce, mem.keep.at[1]))
    for which in range(2):
        for block in range(wide_columns):
            columns = slice(block * D, (block + 1) * D)
            staged.append(
                (ins.expand.at[which, :, columns], mem.keep.at[2 + which, block_of(block, share)])
            )
    staged = [
        pltpu.make_async_copy(source, target, mem.stage_sem.at[number])
        for number, (source, target) in enumerate(staged)
    ]
    for copy in staged:
        copy.start()
    barrier = pltpu.get_barrier_semaphore()
    for mask in range(1, seq):
        pl.semaphore_signal(barrier, inc=1, device_id=(flip(me, mask), group), device_id_type=MESH)
    for step in range(1, batch):
        pl.semaphore_signal(
            barrier, inc=1, device_id=(me, lax.rem(group + step, batch)), device_id_type=MESH
        )
    for mask in (5, 6, 7):
        pl.semaphore_signal(barrier, inc=1, device_id=feeds.place(mask), device_id_type=MESH)

    position = me * rows + lax.broadcasted_iota(jnp.int32, (1, rows), 1)
    inside = position < ins.lengths[...]
    scored = jnp.logical_and(inside, ins.observed[...] == 1).astype(WIDE)
    variate = ins.variates[...].astype(WIDE)
    half_dim = HEAD_DIM // 2
    number = lax.broadcasted_iota(jnp.int32, (half_dim, rows), 0).astype(WIDE)
    angle = jnp.exp(-math.log(ROPE_BASE) * number / half_dim) * ins.times[...].astype(WIDE)
    mem.facts_own[: HEAD_DIM // 2] = jnp.cos(angle)
    mem.facts_own[HEAD_DIM // 2 : HEAD_DIM] = jnp.sin(angle)
    mem.facts_own[HEAD_DIM:] = jnp.concatenate(
        [jnp.where(inside, variate, -1.0), variate, scored, jnp.zeros((5, rows), WIDE)], axis=0
    )
    mem.scored[...] = jnp.broadcast_to(scored, (rows, rows)).T
    for copy in staged:
        copy.wait()
    for which in range(3):
        mem.attend_low[which] = mem.keep[0, block_of(which, share)].astype(LOW)
    pl.semaphore_wait(barrier, seq + batch + 1)

    masks = (6, 7, 4, 5, 2, 3, 1)

    def start_attend_columns():
        copies = []
        for mask in masks:
            copy = push(
                mem.attend_low.at[:, :, block_of(heads.at(mask), LANES)],
                mem.attend_all.at[:, me, group],
                mem.column_send.at[0, mask],
                mem.column_recv.at[0, mask],
                heads.place(mask),
            )
            copy.start()
            copies.append(copy)
        mem.attend_all[:, me, group] = mem.attend_low[:, :, block_of(me, LANES)]
        return copies

    def start_expand_columns():
        copies = []
        for mask in masks:
            copy = push(
                mem.expand_low.at[:, feeds.at(mask)],
                mem.expand_all.at[:, me, group],
                mem.column_send.at[1, mask],
                mem.column_recv.at[1, mask],
                feeds.place(mask),
            )
            copy.start()
            copies.append(copy)
        mem.expand_all[:, me, group] = mem.expand_low[:, feeds.index]
        return copies

    def expand_part_of(array, which):
        def part_of(part):
            return array.at[which, pl.ds(4 * lax.div(part, 2), 4), pl.ds(2 * lax.rem(part, 2), 2)]

        return part_of

    def line_gather(row, part_of):
        return LineGather(part_of, mem.line_send.at[row], mem.line_recv.at[row], me, group)

    def quad_gather(row, part_of):
        return QuadGather(part_of, mem.line_send.at[row], mem.line_recv.at[row], me, group)

    def gather(team, phase, all_rows):
        return Gather(
            team,
            mem.own_rows.at[phase],
            all_rows,
            mem.gather_send.at[phase],
            mem.gather_recv.at[phase],
        )

    def scatter(team, phase):
        return Scatter(
            team,
            (mem.whole, mem.keep, mem.near_from, mem.near, mem.far_from, mem.far),
            mem.near_send.at[phase],
            mem.near_recv.at[phase],
            mem.far_send.at[phase],
            mem.far_recv.at[phase],
        )

    attend_columns = start_attend_columns()
    mem.output_full[block_of(batch * me + group, share)] = mem.keep[0, block_of(3, share)].astype(LOW)
    mem.reduce_all[quad] = mem.keep[1].astype(LOW)
    for which in range(2):
        for block in range(blocks):
            owner, part = feed_block(block)
            row, lane = divmod(block * LANES, D)
            mem.expand_low[which, owner, :, part * LANES : (part + 1) * LANES] = mem.keep[
                2 + which, block_of(row, share), lane : lane + LANES
            ].astype(LOW)
    line_output = line_gather(1, lambda part: mem.output_full.at[block_of(batch * me + part, share)])
    line_output.start()
    unit_one, scale_one = norm_rows(ins.inputs[...].astype(WIDE))
    mem.own_rows[0] = (unit_one * ins.gains[0:1, :]).astype(LOW)
    facts = Gather(heads, mem.facts_own, mem.facts_all, mem.facts_send, mem.facts_recv)
    facts.start()
    for copy in attend_columns:
        copy.wait_recv()
    line_attend = line_gather(0, lambda part: mem.attend_all.at[:, :, part])
    line_attend.start()
    acts = gather(heads, 0, mem.act_one)
    acts.start()
    for chip in (1, 2, 3):
        facts.pass_on(chip)
    for chip in (0, 1, 2, 3):
        facts.complete(chip)
    facts.finish()
    step_rows = mem.facts_own.shape[0]
    half = HEAD_DIM // 2
    count = jnp.zeros((8, LANES), WIDE)
    for slot in range(seq):
        columns = slice(slot * rows, (slot + 1) * rows)
        start = slot * step_rows
        mem.cosine[:, columns] = mem.facts_all[start : start + half]
        mem.sine[:, columns] = mem.facts_all[start + half : start + 2 * half]
        labels = mem.facts_all[start + 2 * half : start + 2 * half + 8]
        mem.labels[:, columns] = labels
        count = count + labels
    mem.count[group] = count
    count_copies = []
    for step in range(1, batch):
        copy = push(
            mem.count.at[group],
            mem.count.at[group],
            mem.count_send.at[step],
            mem.count_recv.at[step],
            (me, lax.rem(group + step, batch)),
        )
        copy.start()
        count_copies.append(copy)

    def mark(block, unused):
        span = block_of(block, pair)
        row = lax.broadcasted_iota(jnp.int32, (HEAD_DIM, pair), 0)
        third = lax.div(row, VARIATES)
        variate = lax.rem(row, VARIATES).astype(WIDE)
        key_label, query_label = mem.labels[0:1, span], mem.labels[1:2, span]
        ones = jnp.ones((1, pair), WIDE)
        last = 3 * VARIATES
        hidden_keys = (key_label < 0.0).astype(WIDE)
        mem.key_marks[:, span] = jnp.where(
            third < 3,
            (key_label == variate).astype(WIDE),
            pick(row, {last: ones, last + 1: ones, last + 2: ones, last + 3: hidden_keys}),
        ).astype(LOW)
        query_marks = (query_label == variate).astype(WIDE)
        mem.sum_marks[:, span] = jnp.where(
            row < VARIATES, query_marks, pick(row, {VARIATES: ones})
        ).astype(LOW)
        for head in range(HEADS_HERE):
            number = me * HEADS_HERE + head
            other = jnp.full((HEAD_DIM, pair), ins.bias[1, number], WIDE)
            more = thirds(jnp.full((HEAD_DIM, pair), ins.bias[0, number], WIDE) - other)
            other = thirds(other)
            mem.query_turned[head, HEAD_DIM:, span] = jnp.where(
                third < 3,
                query_marks * jnp.where(third == 0, more[0], jnp.where(third == 1, more[1], more[2])),
                pick(row, {last: other[0], last + 1: other[1], last + 2: other[2], last + 3: MASKED}),
            ).astype(LOW)
        return unused

    lax.fori_loop(0, length // pair, mark, 0)
    acts.pass_on(1)
    acts.pass_on(2)
    line_output.pass_on()
    line_output.land()
    outputs = Gather(heads, None, mem.output_full, mem.output_send, mem.output_recv)
    outputs.start()
    acts.pass_on(3)
    line_attend.pass_on()
    for chip in range(4):
        acts.complete(chip)
    acts.finish()

    expand_columns = start_expand_columns()
    line_reduce = quad_gather(4, lambda part: mem.reduce_all.at[part])
    line_reduce.start_z()
    line_expand = [
        quad_gather(2 + which, expand_part_of(mem.expand_all, which)) for which in range(2)
    ]
    line_attend.land()
    line_reduce.start_y()

    def attend_matrix(which):
        return mem.attend_all[which].reshape(D, LANES)

    def project(block, unused):
        span = block_of(block, pair)
        act = mem.act_one[span, :]
        cosine, sine = mem.cosine[:, span], mem.sine[:, span]
        query = turn_rows(dot(act, attend_matrix(0)).T, cosine, sine).astype(LOW)
        query = (query.astype(WIDE) * HEAD_DIM ** (-0.5)).astype(LOW)
        key = turn_rows(dot(act, attend_matrix(1)).T, cosine, sine).astype(LOW)
        value = dot(act, attend_matrix(2)).T.astype(LOW)
        mem.key_turned[:, span] = key
        mem.value_turned[:, span] = value

        for head in range(HEADS_HERE):
            features = slice(head * HEAD_DIM, (head + 1) * HEAD_DIM)
            mem.query_turned[head, :HEAD_DIM, span] = query[features]
            whole = jnp.concatenate([key[features], mem.key_marks[:, span]], axis=0)
            mem.key_heads[head, span, :] = whole.T
        return unused

    for copy in expand_columns:
        copy.wait_recv()
    line_expand[0].start_z()
    line_expand[0].start_y()
    lax.fori_loop(0, length // pair, project, 0)
    line_expand[1].start_z()
    outputs.pass_on(1)
    outputs.pass_on(2)

    core = lax.rem(me, 2)

    def mixed_copy(chip, which):
        other = 2 * chip_of(heads, chip) + which
        slot = 2 * chip + lax.rem(which + core, 2)
        return push(
            mem.mixed_out.at[block_of(other, rows)],
            mem.mixed_rows.at[:, block_of(me, LANES)],
            mem.mixed_send.at[slot],
            mem.mixed_recv.at[slot],
            (other, group),
        )

    def attend_block(chip):
        columns = block_of(chip_of(heads, chip), pair)
        for head in range(HEADS_HERE):
            span = slice(head * HEAD_DIM, (head + 1) * HEAD_DIM)
            scores = dot(mem.key_heads[head], mem.query_turned[head, :, columns])
            top = jnp.floor(jnp.max(scores, axis=0, keepdims=True))
            powers = jnp.exp(scores - top)
            probs = powers * (1.0 / jnp.sum(powers, axis=0, keepdims=True))
            rounded = probs.astype(LOW)
            mem.probs[head, :, columns] = rounded
            residue = (probs - rounded.astype(WIDE)).astype(LOW)
            coarse = dot(mem.value_turned[span, :], rounded)
            mem.exact[span, columns] = coarse + dot(mem.value_turned[span, :], residue)
            mem.mixed_wide[span, :] = coarse
        mixed = mem.mixed_wide[...].astype(LOW)
        mem.mixed_turned[:, columns] = mixed
        mem.mixed_out[columns, :] = mixed.T

    def attend_step(step, unused):
        chip = lax.rem(step + 1, 4)
        attend_block(chip)
        for which in range(2):

            @pl.when(jnp.logical_or(chip > 0, core != which))
            def _():
                mixed_copy(chip, which).start()

        at_step(step, 1, lambda: outputs.pass_on(3))
        return unused

    lax.fori_loop(0, 4, attend_step, 0)
    line_expand[1].start_y()
    mem.mixed_rows[:, block_of(me, LANES)] = mem.mixed_out[block_of(me, rows), :]
    for chip in range(4):
        outputs.complete(chip)
    outputs.finish()

    def wait_pieces(copy):
        for mask in range(1, seq):
            copy(mask).wait()

    def mixed_wait(mask):
        other = heads.at(mask)
        return push(
            mem.mixed_out.at[block_of(other, rows)],
            mem.mixed_rows.at[:, block_of(other, LANES)],
            mem.mixed_send.at[mask],
            mem.mixed_recv.at[mask],
            (other, group),
        )

    wait_pieces(mixed_wait)
    middle = ins.inputs[...].astype(WIDE) + dot(mem.mixed_rows[...], mem.output_full[...])
    mem.middle[...] = middle
    unit_two, scale_two = norm_rows(middle)
    mem.own_rows[1] = (unit_two * ins.gains[1:2, :]).astype(LOW)
    acts = gather(feeds, 1, mem.act_two)
    acts.start((2, 4, 1))
    line_reduce.pass_on()
    line_expand[0].pass_on()

    def split_heads(block, unused):
        span = block_of(block, pair)
        row = lax.broadcasted_iota(jnp.int32, (HEAD_DIM, pair), 0)
        value_marks = jnp.where(row < 3, 1.0, 0.0).astype(LOW)
        for head in range(HEADS_HERE):
            features = slice(head * HEAD_DIM, (head + 1) * HEAD_DIM)
            value = mem.value_turned[features, span]
            mem.value_heads[head, span, :] = jnp.concatenate([value, value_marks], axis=0).T
            query = mem.query_turned[head, :HEAD_DIM, span]
            whole = jnp.concatenate([query, mem.sum_marks[:, span]], axis=0)
            mem.query_heads[head, span, :] = whole.T
        return unused

    lax.fori_loop(0, length // pair, split_heads, 0)
    line_expand[0].land()

    def expand_matrix(which):
        return mem.expand_all[which].reshape(D, hidden_width)

    def reduce_matrix():
        return mem.reduce_all[...].reshape(hidden_width, D)

    def feed_gate(chip):
        span = block_of(chip_of(feeds, chip), pair)
        mem.by_gate[span, :] = dot(mem.act_two[span, :], expand_matrix(0))

    def feed_up(chip, unused=0):
        span = block_of(chip_of(feeds, chip), pair)
        gate = mem.by_gate[span, :]
        up = dot(mem.act_two[span, :], expand_matrix(1))
        sigmoid = 1.0 / (1.0 + jnp.exp(-gate))
        swish = gate * sigmoid
        mem.by_up[span, :] = swish
        mem.by_gate[span, :] = up * sigmoid * (1.0 + gate * (1.0 - sigmoid))
        mem.hidden[span, :] = (swish * up).astype(LOW)
        return unused

    each_chip(
        acts,
        feed_gate,
        {
            0: [line_expand[1].pass_on],
            2: [line_expand[1].land, lambda: lax.fori_loop(0, 3, feed_up, 0)],
            3: [lambda: lax.fori_loop(3, 4, feed_up, 0)],
        },
    )
    line_reduce.land()
    sums = scatter(feeds, 1)

    def feed_down(step, unused):
        chip = lax.rem(step + 1, 4)
        span = block_of(chip_of(feeds, chip), pair)
        sums.put(chip, dot(mem.hidden[span, :], reduce_matrix()))
        at_step(step, 1, lambda: sums.combine(1))
        at_step(step, 2, lambda: sums.combine(2))
        return unused

    lax.fori_loop(0, 4, feed_down, 0)
    sums.combine(3)

    for block in range(length // pair):
        span = block_of(block, pair)
        mem.hidden_turned[:, span] = mem.hidden[span, :].T
        mem.act_two_turned[:, span] = mem.act_two[span, :].T
    output = mem.middle[...] + sums.total()
    outs.layer_output[...] = output
    for copy in count_copies:
        copy.wait()
    count_all = jnp.sum(
        mem.count[0, 2:3] + mem.count[1, 2:3] + mem.count[2, 2:3] + mem.count[3, 2:3],
        axis=1,
        keepdims=True,
    )
    error = jnp.where(mem.scored[:, 0:1] > 0.0, output - ins.teacher[...].astype(WIDE), 0.0)
    mem.squares[1:2, :] = jnp.sum(error * error, axis=0, keepdims=True)
    grad_out = error * (2.0 / (count_all * D))
    mem.grad_own[...] = grad_out
    mem.own_rows[2] = grad_out.astype(LOW)
    acts = gather(feeds, 2, mem.branch)
    acts.start((2, 4, 1))

    sums = scatter(feeds, 2)

    def feed_back(chip):
        span = block_of(chip_of(feeds, chip), pair)
        grad_hidden = dot_turned(mem.branch[span, :], reduce_matrix())
        grad_gate = (grad_hidden * mem.by_gate[span, :]).astype(LOW)
        grad_up = (grad_hidden * mem.by_up[span, :]).astype(LOW)
        mem.grad_gate[span, :] = grad_gate
        mem.grad_up[span, :] = grad_up
        sums.put(
            chip,
            dot_turned(grad_gate, expand_matrix(0)) + dot_turned(grad_up, expand_matrix(1)),
        )

    each_chip(acts, feed_back, {2: [lambda: sums.combine(1)], 3: [lambda: sums.combine(2)]})

    def line_scatter(row, part_of, landing):
        return LineScatter(
            part_of, landing, mem.back_send.at[row], mem.back_recv.at[row], me, group
        )

    def quad_scatter(row, part_of, landing):
        return QuadScatter(
            part_of, landing, mem.back_send.at[row], mem.back_recv.at[row], me, group
        )

    def reduce_grad(part, unused):
        mem.reduce_grad[part] = dot(
            mem.hidden_turned[block_of(part, rows), :], mem.branch[...]
        ).astype(LOW)
        at_step(part, 0, lambda: sums.combine(3))
        return unused

    lax.fori_loop(0, batch, reduce_grad, 0)
    back_reduce = quad_scatter(0, lambda part: mem.reduce_grad.at[part], mem.reduce_land)
    back_reduce.start_far()

    def expand_grad(which):
        grads = (mem.grad_gate, mem.grad_up)[which]

        def one_block(block, unused):
            products = dot(mem.act_two_turned[block_of(block, pair), :], grads[...]).astype(LOW)
            mem.expand_grad[which, pl.ds(2 * block, 2)] = products.reshape(
                2, batch, share, hidden_width
            )
            return unused

        lax.fori_loop(0, seq // 2, one_block, 0)
        line = quad_scatter(
            1 + which, expand_part_of(mem.expand_grad, which), mem.expand_land.at[which]
        )
        return line

    back_expand = []
    back_expand.append(expand_grad(0))
    back_expand[0].start_far()
    grad_act = sums.total()
    unit_two, scale_two = norm_rows(mem.middle[...])
    gain = ins.gains[1:2, :]
    grad_unit = grad_act * gain
    mem.gains[1:2, :] = jnp.sum(grad_act * unit_two, axis=0, keepdims=True)
    grad_middle = mem.grad_own[...] + scale_two * (
        grad_unit - unit_two * jnp.mean(grad_unit * unit_two, axis=-1, keepdims=True)
    )
    mem.grad_own[...] = grad_middle
    mem.own_rows[3] = grad_middle.astype(LOW)
    grad_mixed = dot(mem.output_full[...], grad_middle.T.astype(LOW)).astype(LOW)
    mem.grad_mixed_out[...] = grad_mixed.reshape(seq, LANES, rows)

    def grad_copy(mask, back=False):
        return push(
            mem.grad_mixed_out.at[heads.at(mask)],
            mem.grad_mixed.at[:, block_of(heads.at(mask) if back else me, rows)],
            mem.mixed_send.at[8 + mask],
            mem.mixed_recv.at[8 + mask],
            heads.place(mask),
        )

    for mask in masks:
        grad_copy(mask).start()
    mem.grad_mixed[:, block_of(me, rows)] = mem.grad_mixed_out[me]
    back_reduce.pass_on()
    back_expand.append(expand_grad(1))
    back_expand[1].start_far()

    wait_pieces(lambda mask: grad_copy(mask, True))
    acts = gather(heads, 3, mem.grad_attn)
    acts.start()
    back_reduce.start_near()
    back_expand[0].start_near()
    back_attend = [
        line_scatter(
            4 + which,
            lambda part, which=which: mem.attend_grad.at[which, :, part],
            mem.attend_land.at[which],
        )
        for which in range(3)
    ]

    def attend_grad(which):
        grads = dot(mem.grad_project[which], mem.act_one[...])
        mem.attend_grad[which] = grads.T.astype(LOW).reshape(seq, batch, share, LANES)
        back_attend[which].start()

    lane = lax.broadcasted_iota(jnp.int32, (pair, LANES), 1)

    def grad_rows(block, unused):
        span = block_of(block, pair)
        whole = mem.grad_mixed[:, span].astype(WIDE).T
        for head in range(HEADS_HERE):
            mem.grad_heads[head, span, :] = jnp.where(lax.div(lane, HEAD_DIM) == head, whole, 0.0).astype(LOW)
        return unused

    lax.fori_loop(0, length // pair, grad_rows, 0)

    def value_back(block, unused):
        span = block_of(block, pair)
        total = dot(mem.probs[0, span, :], mem.grad_heads[0])
        for head in range(1, HEADS_HERE):
            total = total + dot(mem.probs[head, span, :], mem.grad_heads[head])
        mem.grad_project[2, :, span] = total.T.astype(LOW)
        return unused

    lax.fori_loop(0, length // pair, value_back, 0)
    back_expand[0].pass_on()
    attend_grad(2)

    def score_back(block, unused):
        columns = block_of(block, pair)
        row = lax.broadcasted_iota(jnp.int32, (HEAD_DIM, pair), 0)
        grads = mem.grad_mixed[:, columns]
        delta = grads.astype(WIDE) * mem.exact[:, columns]
        for head in range(HEADS_HERE):
            span = slice(head * HEAD_DIM, (head + 1) * HEAD_DIM)
            pieces = thirds(-jnp.sum(delta[span], axis=0, keepdims=True))
            marks = pick(row, dict(enumerate(pieces))).astype(LOW)
            change = dot(mem.value_heads[head], jnp.concatenate([grads[span], marks], axis=0))
            mem.probs[head, :, columns] = (mem.probs[head, :, columns].astype(WIDE) * change).astype(LOW)
        return unused

    lax.fori_loop(0, length // pair, score_back, 0)
    back_expand[1].start_near()
    mem.bias_sums[...] = jnp.zeros_like(mem.bias_sums)
    scale = HEAD_DIM ** (-0.5)

    def project_grads(block, unused):
        span = block_of(block, pair)
        cosine, sine = mem.cosine[:, span], -mem.sine[:, span]
        queries, keys = [], []
        for head in range(HEADS_HERE):
            features = slice(head * HEAD_DIM, (head + 1) * HEAD_DIM)
            queries.append(dot(mem.key_turned[features, :], mem.probs[head, :, span]) * scale)
            sums = dot(mem.probs[head, span, :], mem.query_heads[head]).T
            keys.append(sums[:HEAD_DIM])
            by_variate = sums[HEAD_DIM : HEAD_DIM + VARIATES]
            same = by_variate * mem.key_marks[:VARIATES, span].astype(WIDE)
            mem.bias_sums[head : head + 1, :] += jnp.sum(same, axis=0, keepdims=True)
            total = sums[HEAD_DIM + VARIATES : HEAD_DIM + VARIATES + 1]
            mem.bias_sums[HEADS_HERE + head : HEADS_HERE + head + 1, :] += total
        mem.grad_project[0, :, span] = turn_rows(jnp.concatenate(queries, axis=0), cosine, sine).astype(LOW)
        mem.grad_project[1, :, span] = turn_rows(jnp.concatenate(keys, axis=0), cosine, sine).astype(LOW)
        return unused

    lax.fori_loop(0, length // pair, project_grads, 0)
    back_expand[1].pass_on()
    attend_grad(0)
    acts.pass_on(1)
    acts.pass_on(2)
    sums = scatter(heads, 3)

    def project_back(step, unused):
        chip = lax.rem(step + 1, 4)
        span = block_of(chip_of(heads, chip), pair)
        total = jnp.zeros((pair, D), WIDE)
        for which in range(3):
            total = total + dot_turned(mem.grad_project[which, :, span].T, attend_matrix(which))
        sums.put(chip, total)
        at_step(step, 1, lambda: sums.combine(1))
        at_step(step, 2, lambda: sums.combine(2))
        return unused

    lax.fori_loop(0, 4, project_back, 0)
    sums.combine(3)
    attend_grad(1)
    acts.pass_on(3)
    for chip in range(4):
        acts.complete(chip)
    acts.finish()
    mem.output_grad[...] = (
        dot(mem.mixed_turned[...], mem.grad_attn[...]).astype(LOW).reshape(mem.output_grad.shape)
    )
    back_output = line_scatter(3, lambda part: mem.output_grad.at[part], mem.output_land)
    back_output.start()
    for which in (2, 0, 1):
        back_attend[which].pass_on()

    column_copies = []
    mem.squares[0:1, :] = jnp.zeros((1, D), WIDE)

    def add_squares(total):
        flat = total.reshape(-1, total.shape[-1])
        width = flat.shape[1]
        mem.squares[0:1, :width] += jnp.sum(flat * flat, axis=0, keepdims=True)

    def store_whole(total, out):
        out[...] = total
        add_squares(total)

    back_reduce.land()
    store_whole(
        mem.reduce_grad[quad].astype(WIDE)
        + mem.reduce_land[0].astype(WIDE)
        + mem.reduce_land[2].astype(WIDE),
        outs.reduce_share,
    )
    def expand_shares(which):
        back_expand[which].land()
        own = expand_part_of(mem.expand_grad, which)(quad)

        def one_block(block, unused):
            total = (
                own[block].astype(WIDE)
                + mem.expand_land[which, 0, block].astype(WIDE)
                + mem.expand_land[which, 2, block].astype(WIDE)
            )
            mem.expand_part[which, block] = total.astype(LOW)
            add_squares(total)
            return unused

        lax.fori_loop(0, 4, one_block, 0)
        for mask in masks:
            other = feeds.at(mask)
            copy = push(
                mem.expand_part.at[which, lax.rem(other, 4), lax.div(other, 4)],
                mem.expand_share.at[which, feeds.index],
                mem.share_send.at[which, mask],
                mem.share_recv.at[which, mask],
                feeds.place(mask),
            )
            copy.start()
            column_copies.append(copy)
        mem.expand_share[which, feeds.index] = mem.expand_part[
            which, lax.rem(feeds.index, 4), lax.div(feeds.index, 4)
        ]

    for which in range(2):
        expand_shares(which)

    def attend_shares(which):
        back_attend[which].land()

        def store(total):
            mem.attend_part[which] = total.astype(LOW)
            add_squares(total)

        back_attend[which].add(
            lambda: mem.attend_grad[which, :, group].astype(WIDE),
            lambda slot: mem.attend_land[which, slot].astype(WIDE),
            store,
        )

    attend_shares(2)
    grad_act = sums.total()
    unit_one, scale_one = norm_rows(ins.inputs[...].astype(WIDE))
    gain = ins.gains[0:1, :]
    grad_unit = grad_act * gain
    mem.gains[0:1, :] = jnp.sum(grad_act * unit_one, axis=0, keepdims=True)
    grad_input = mem.grad_own[...] + scale_one * (
        grad_unit - unit_one * jnp.mean(grad_unit * unit_one, axis=-1, keepdims=True)
    )
    outs.input_gradient[...] = grad_input * (count_all * D)
    outs.count[...] = jnp.broadcast_to(count_all, (8, LANES))

    back_output.pass_on()
    for which in range(2):
        attend_shares(which)
    for mask in masks:
        copy = push(
            mem.attend_part.at[:, heads.at(mask)],
            outs.attend_share.at[:, :, block_of(me, LANES)],
            mem.share_send.at[2, mask],
            mem.share_recv.at[2, mask],
            heads.place(mask),
        )
        copy.start()
        column_copies.append(copy)
    outs.attend_share[:, :, block_of(me, LANES)] = mem.attend_part[:, me]
    back_output.land()
    back_output.add(
        lambda: mem.output_grad[group].astype(WIDE),
        lambda slot: mem.output_land[slot].astype(WIDE),
        lambda total: store_whole(total, outs.output_share),
    )

    lane = lax.broadcasted_iota(jnp.int32, (1, LANES), 1)
    lines = [
        mem.gains[which : which + 1, start : start + LANES]
        for which in range(2)
        for start in range(0, D, LANES)
    ]
    bias_line = jnp.zeros((1, LANES), WIDE)
    for row in range(2 * HEADS_HERE):
        place = row // HEADS_HERE * HEADS + me * HEADS_HERE + row % HEADS_HERE
        line = mem.bias_sums[row : row + 1, :]
        if row >= HEADS_HERE:
            line = line - mem.bias_sums[row - HEADS_HERE : row - HEADS_HERE + 1, :]
        amount = jnp.sum(line, axis=1, keepdims=True)
        bias_line = bias_line + jnp.where(lane == place, amount, 0.0)
    amounts = jnp.sum(mem.squares[0:2, :], axis=1, keepdims=True)
    amount_line = jnp.where(lane == 0, amounts[0:1], 0.0) + jnp.where(lane == 1, amounts[1:2], 0.0)
    lines += [bias_line, amount_line, jnp.zeros((6, LANES), WIDE)]
    mem.plane_totals[me] = jnp.concatenate(lines, axis=0)
    plane_copies = []
    for mask in masks:
        copy = push(
            mem.plane_totals.at[me],
            mem.plane_totals.at[me],
            mem.total_send.at[0, mask],
            mem.total_recv.at[0, mask],
            (flip(me, mask), group),
        )
        copy.start()
        plane_copies.append(copy)
    for copy in column_copies[: 2 * len(masks)]:
        copy.wait()
    for which in range(2):
        for block in range(blocks):
            owner, part = feed_block(block)
            outs.expand_share[which, :, block * LANES : (block + 1) * LANES] = mem.expand_share[
                which, owner, :, part * LANES : (part + 1) * LANES
            ]
    for copy in plane_copies:
        copy.wait()
    mem.line_totals[group] = jnp.sum(mem.plane_totals[...], axis=0)
    total_copies = []
    for step in range(1, batch):
        copy = push(
            mem.line_totals.at[group],
            mem.line_totals.at[group],
            mem.total_send.at[1, step],
            mem.total_recv.at[1, step],
            (me, lax.rem(group + step, batch)),
        )
        copy.start()
        total_copies.append(copy)
    for copy in total_copies:
        copy.wait()
    outs.totals[...] = jnp.sum(mem.line_totals[...], axis=0)
    for copy in column_copies[2 * len(masks) :]:
        copy.wait()
    for copies in (attend_columns, expand_columns):
        for copy in copies:
            copy.wait_send()
    for line in [line_attend, line_output, line_reduce] + line_expand:
        line.finish()
    for line in [back_output, back_reduce] + back_attend + back_expand:
        line.finish()


def call_layer(seq, batch, inputs, teacher, lengths, variates, observed, times, bias, gains, attend, output, expand, reduce):
    rows, share, hidden = inputs.shape[0], attend.shape[1], expand.shape[2] // seq
    length, pair, chips = rows * seq, 2 * rows, seq // 2
    low = lambda *shape: pltpu.VMEM(shape, LOW)
    wide = lambda *shape: pltpu.VMEM(shape, WIDE)
    sems = lambda *shape: pltpu.SemaphoreType.DMA(shape)
    in_names = ["inputs", "teacher", "lengths", "variates", "observed"]
    in_names += ["times", "bias", "gains"]
    in_names += ["attend", "output", "expand", "reduce"]
    outs = dict(
        layer_output=((rows, D), WIDE),
        input_gradient=((rows, D), WIDE),
        totals=((TOTAL_ROWS, LANES), WIDE),
        count=((8, LANES), WIDE),
        attend_share=((3, share, D), LOW),
        output_share=((output.shape[0], D), WIDE),
        expand_share=((2, share, hidden * seq), LOW),
        reduce_share=((reduce.shape[0], D), WIDE),
    )
    scratch = dict(
        gains=wide(2, D),
        squares=wide(8, D),
        plane_totals=wide(seq, TOTAL_ROWS, LANES),
        line_totals=wide(batch, TOTAL_ROWS, LANES),
        attend_low=low(3, share, D),
        expand_low=low(2, seq, share, hidden),
        attend_all=low(3, seq, batch, share, LANES),
        output_full=low(D, D),
        expand_all=low(2, seq, batch, share, hidden),
        reduce_all=low(batch, reduce.shape[0], D),
        own_rows=low(4, rows, D),
        act_one=low(length, D),
        act_two=low(length, D),
        branch=low(length, D),
        grad_attn=low(length, D),
        facts_own=wide(HEAD_DIM + 8, LANES),
        facts_all=wide(seq * (HEAD_DIM + 8), LANES),
        scored=wide(rows, LANES),
        cosine=wide(HEAD_DIM // 2, length),
        sine=wide(HEAD_DIM // 2, length),
        labels=wide(8, length),
        key_marks=low(HEAD_DIM, length),
        count=wide(batch, 8, LANES),
        query_turned=low(HEADS_HERE, LANES, length),
        key_turned=low(LANES, length),
        value_turned=low(LANES, length),
        key_heads=low(HEADS_HERE, length, LANES),
        value_heads=low(HEADS_HERE, length, LANES),
        query_heads=low(HEADS_HERE, length, LANES),
        grad_heads=low(HEADS_HERE, length, LANES),
        grad_mixed=low(LANES, length),
        grad_mixed_out=low(seq, LANES, rows),
        probs=low(HEADS_HERE, length, length),
        mixed_out=low(length, LANES),
        mixed_rows=low(rows, D),
        sum_marks=low(HEAD_DIM, length),
        hidden_turned=low(hidden, length),
        act_two_turned=low(D, length),
        exact=wide(LANES, length),
        mixed_wide=wide(LANES, pair),
        mixed_turned=low(LANES, length),
        whole=wide(pair, D),
        keep=wide(chips, rows, D),
        near_from=low(chips, rows, D),
        near=low(chips, rows, D),
        far_from=low(chips, rows, D),
        far=low(chips, rows, D),
        middle=wide(rows, D),
        grad_own=wide(rows, D),
        by_up=wide(length, hidden),
        by_gate=wide(length, hidden),
        hidden=low(length, hidden),
        grad_gate=low(length, hidden),
        grad_up=low(length, hidden),
        bias_sums=wide(8, pair),
        grad_project=low(3, LANES, length),
        reduce_grad=low(batch, reduce.shape[0], D),
        expand_grad=low(2, seq, batch, share, hidden),
        output_grad=low(batch, output.shape[0], D),
        attend_grad=low(3, seq, batch, share, LANES),
        reduce_land=low(3, reduce.shape[0], D),
        expand_land=low(2, 3, 4, 2, share, hidden),
        output_land=low(batch, output.shape[0], D),
        attend_land=low(3, batch, seq, share, LANES),
        expand_part=low(2, 4, 2, share, hidden),
        expand_share=low(2, seq, share, hidden),
        attend_part=low(3, seq, share, LANES),
        stage_sem=sems(5 + 2 * (expand.shape[2] // D)),
        total_send=sems(2, seq),
        total_recv=sems(2, seq),
        column_send=sems(2, seq),
        column_recv=sems(2, seq),
        line_send=sems(5, batch),
        line_recv=sems(5, batch),
        facts_send=sems(seq),
        facts_recv=sems(seq),
        gather_send=sems(4, seq),
        gather_recv=sems(4, seq),
        count_send=sems(batch),
        count_recv=sems(batch),
        near_send=sems(4, chips),
        near_recv=sems(4, chips),
        far_send=sems(4, chips),
        far_recv=sems(4, chips),
        back_send=sems(7, batch),
        back_recv=sems(7, batch),
        output_send=sems(seq),
        output_recv=sems(seq),
        mixed_send=sems(2 * seq),
        mixed_recv=sems(2 * seq),
        share_send=sems(3, seq),
        share_recv=sems(3, seq),
    )

    places = dict.fromkeys(("attend", "output", "expand", "reduce"), pl.BlockSpec(memory_space=pl.ANY))
    places["bias"] = IN_SMEM

    def kernel(*refs):
        groups, start = [], 0
        for names in (in_names, outs, scratch):
            names = list(names)
            groups.append(types.SimpleNamespace(**dict(zip(names, refs[start : start + len(names)]))))
            start += len(names)
        layer_kernel(seq, batch, *groups)

    results = pl.pallas_call(
        kernel,
        out_shape=[jax.ShapeDtypeStruct(*out) for out in outs.values()],
        in_specs=[places.get(name, IN_VMEM) for name in in_names],
        out_specs=[IN_VMEM] * len(outs),
        scratch_shapes=list(scratch.values()),
        compiler_params=pltpu.CompilerParams(
            collective_id=0, has_side_effects=True, vmem_limit_bytes=63 * MIB
        ),
        name="layer",
    )(inputs, teacher, lengths, variates, observed, times, bias, gains, attend, output, expand, reduce)
    return types.SimpleNamespace(**dict(zip(outs, results)))


def update_kernel(
    smalls, ins, small_outs, outs, olds, shares, news, copies, passed, in_sems, out_sems
):
    totals, count, gains, gains_first, gains_second, bias, bias_first, bias_second = smalls
    order = (2, 3, 0, 1)
    comes = []
    for place, number in enumerate(order):
        pairs = list(zip(ins[4 + 3 * number : 7 + 3 * number], olds[3 * number : 3 * number + 3]))
        pairs.append((ins[number], shares[number]))
        comes.append(
            [
                pltpu.make_async_copy(source, target, in_sems.at[4 * place + part])
                for part, (source, target) in enumerate(pairs)
            ]
        )
    for copy in sum(comes, []):
        copy.start()
    through = [
        pltpu.make_async_copy(ins[16 + part], passed[part], in_sems.at[16 + part]) for part in range(2)
    ]
    for copy in through:
        copy.start()
    goes = []
    gains_total = jnp.concatenate(
        [
            jnp.concatenate([totals[row + i : row + i + 1, :] for i in range(D // LANES)], axis=1)
            for row in (0, D // LANES)
        ],
        axis=0,
    )
    row = 2 * D // LANES
    bias_total = jnp.concatenate(
        [totals[row : row + 1, :HEADS], totals[row : row + 1, HEADS : 2 * HEADS]], axis=0
    )
    row += 1

    def sum_all(values):
        return jnp.sum(jnp.sum(values, axis=0, keepdims=True), axis=1, keepdims=True)

    squares = (
        totals[row : row + 1, 0:1] + sum_all(gains_total * gains_total) + sum_all(bias_total * bias_total)
    )
    grad_norm = jnp.sqrt(squares)
    clip = jnp.minimum(1.0, CLIP_NORM / grad_norm)
    small_outs[0][...] = totals[row : row + 1, 1:2] / (count[0:1, 0:1] * D)
    small_outs[1][...] = grad_norm
    rates = (RATE_ATTEND, RATE_OUTPUT, RATE_EXPAND, RATE_REDUCE)
    for place, number in enumerate(order):
        for copy in comes[place]:
            copy.wait()
        weight, first, second = olds[3 * number : 3 * number + 3]
        new, first_new, second_new = news[3 * number : 3 * number + 3]
        arrays = (new, copies[number], first_new, second_new, weight, first, second, shares[number])
        for lead in range(weight.shape[0] if weight.ndim == 3 else 1):

            def one_block(block, unused, lead=lead, arrays=arrays, rate=rates[number]):
                across = arrays[0].shape[-1] // D
                rows = block_of(lax.div(block, across), 16)
                columns = block_of(lax.rem(block, across), D)
                place = (lead, rows, columns) if len(arrays[0].shape) == 3 else (rows, columns)
                old, moment, square, share = [array[place] for array in arrays[4:]]
                step = fast_step(old, moment, square, share.astype(WIDE) * clip, rate)
                arrays[0][place], arrays[2][place], arrays[3][place] = step
                arrays[1][place] = step[0].astype(LOW)
                return unused

            lax.fori_loop(0, weight.shape[-2] // 16 * (weight.shape[-1] // D), one_block, 0)
        for part, source in enumerate((new, copies[number], first_new, second_new)):
            copy = pltpu.make_async_copy(
                source, outs[2 + 4 * number + part], out_sems.at[2 + 4 * number + part]
            )
            copy.start()
            goes.append(copy)
        if place == 0:
            for part in range(2):
                through[part].wait()
                copy = pltpu.make_async_copy(passed[part], outs[part], out_sems.at[part])
                copy.start()
                goes.append(copy)
    for number, (old, total, rate) in enumerate(
        (
            ((gains, gains_first, gains_second), gains_total, RATE_GAINS),
            ((bias, bias_first, bias_second), bias_total, RATE_BIAS),
        )
    ):
        new, first_new, second_new = small_outs[2 + 3 * number : 5 + 3 * number]
        new[...], first_new[...], second_new[...] = adam_step(
            old[0][...], old[1][...], old[2][...], total * clip, rate, 0.0
        )
    for copy in goes:
        copy.wait()


def fast_step(weight, first, second, gradient, rate):
    first = BETA_ONE * first + (1.0 - BETA_ONE) * gradient
    second = BETA_TWO * second + ((1.0 - BETA_TWO) * gradient) * gradient
    low = jnp.sqrt(second * (1.0 / (1.0 - BETA_TWO**STEP))) + ADAM_EPS
    step = first * (rate / (1.0 - BETA_ONE**STEP)) / low
    return weight * (1.0 - rate * WEIGHT_DECAY) - step, first, second


def call_update(done, shares, smalls, olds):
    in_hbm = pl.BlockSpec(memory_space=pl.ANY)
    smalls = [done.totals, done.count] + smalls
    ins = shares + olds + [done.layer_output, done.input_gradient]
    one = jax.ShapeDtypeStruct((1, 1), WIDE)
    small_outs = [one, one] + smalls[2:]
    outs = [(done.layer_output, WIDE), (done.input_gradient, WIDE)]
    for weight in olds[::3]:
        outs += [(weight, dtype) for dtype in (WIDE, LOW, WIDE, WIDE)]
    passed = ins[-2:]
    parts = [smalls, ins, small_outs, outs, olds, shares, olds, olds[::3], passed]

    def kernel(*refs):
        groups, start = [], 0
        for part in parts:
            groups.append(refs[start : start + len(part)])
            start += len(part)
        update_kernel(*groups, *refs[start:])

    results = pl.pallas_call(
        kernel,
        out_shape=[jax.ShapeDtypeStruct(array.shape, WIDE) for array in small_outs]
        + [jax.ShapeDtypeStruct(array.shape, dtype) for array, dtype in outs],
        in_specs=[IN_VMEM] * len(smalls) + [in_hbm] * len(ins),
        out_specs=[IN_VMEM] * len(small_outs) + [in_hbm] * len(outs),
        scratch_shapes=[pltpu.VMEM(array.shape, WIDE) for array in olds]
        + [pltpu.VMEM(array.shape, array.dtype) for array in shares]
        + [pltpu.VMEM(array.shape, WIDE) for array in olds]
        + [pltpu.VMEM(array.shape, LOW) for array in olds[::3]]
        + [pltpu.VMEM(array.shape, WIDE) for array in passed]
        + [pltpu.SemaphoreType.DMA((18,)), pltpu.SemaphoreType.DMA((18,))],
        compiler_params=pltpu.CompilerParams(vmem_limit_bytes=63 * MIB),
        name="update",
    )(*smalls, *ins)
    return results[: len(small_outs)], results[len(small_outs) :]


def fast_body(
    seq,
    batch,
    inputs,
    teacher,
    lengths,
    variate_ids,
    time_ids,
    observed,
    attend_weight,
    output_weight,
    expand_weight,
    reduce_weight,
    norm_gains,
    variate_bias,
    attend_first,
    output_first,
    expand_first,
    reduce_first,
    gains_first,
    bias_first,
    attend_second,
    output_second,
    expand_second,
    reduce_second,
    gains_second,
    bias_second,
):
    done = call_layer(
        seq,
        batch,
        inputs[0],
        teacher[0],
        lengths[:, None],
        variate_ids,
        observed,
        time_ids,
        variate_bias,
        norm_gains,
        attend_weight,
        output_weight,
        expand_weight,
        reduce_weight,
    )
    small, large = call_update(
        done,
        [done.attend_share, done.output_share, done.expand_share, done.reduce_share],
        [norm_gains, gains_first, gains_second, variate_bias, bias_first, bias_second],
        [attend_weight, attend_first, attend_second]
        + [output_weight, output_first, output_second]
        + [expand_weight, expand_first, expand_second]
        + [reduce_weight, reduce_first, reduce_second],
    )
    return (
        large[0][None],
        small[0].reshape(()),
        large[1][None],
        small[1].reshape(()),
    ) + tuple(large[2:] + small[2:])


def solution(mesh):
    seq, batch = mesh.shape["seq"], mesh.shape["batch"]
    body = functools.partial(fast_body, seq, batch) if fast_fits(seq, batch) else general_body
    in_specs = (
        P("batch", "seq", None),
        P("batch", "seq", None),
        P("batch"),
        P("batch", "seq"),
        P("batch", "seq"),
        P("batch", "seq"),
        P(None, ("seq", "batch"), None),
        P(("seq", "batch"), None),
        P(None, ("seq", "batch"), None),
        P(("seq", "batch"), None),
        P(),
        P(),
        P(None, ("seq", "batch"), None),
        P(("seq", "batch"), None),
        P(None, ("seq", "batch"), None),
        P(("seq", "batch"), None),
        P(),
        P(),
        P(None, ("seq", "batch"), None),
        P(("seq", "batch"), None),
        P(None, ("seq", "batch"), None),
        P(("seq", "batch"), None),
        P(),
        P(),
    )
    out_specs = (
        P("batch", "seq", None),
        P(),
        P("batch", "seq", None),
        P(),
        P(None, ("seq", "batch"), None),
        P(None, ("seq", "batch"), None),
        P(None, ("seq", "batch"), None),
        P(None, ("seq", "batch"), None),
        P(("seq", "batch"), None),
        P(("seq", "batch"), None),
        P(("seq", "batch"), None),
        P(("seq", "batch"), None),
        P(None, ("seq", "batch"), None),
        P(None, ("seq", "batch"), None),
        P(None, ("seq", "batch"), None),
        P(None, ("seq", "batch"), None),
        P(("seq", "batch"), None),
        P(("seq", "batch"), None),
        P(("seq", "batch"), None),
        P(("seq", "batch"), None),
        P(),
        P(),
        P(),
        P(),
        P(),
        P(),
    )
    return jax.shard_map(body, mesh=mesh, in_specs=in_specs, out_specs=out_specs, check_vma=False)
```

```python
import functools
import math
import types

import jax
import jax.numpy as jnp
import numpy as np
from jax import lax
from jax.experimental import pallas as pl
from jax.experimental.pallas import tpu as pltpu
from jax.sharding import PartitionSpec as P

D = 1024
HEADS = 16
HEAD_DIM = 64
STEP = 10


NORM_EPS = 1e-05
ROPE_BASE = 10000.0
MASKED = -1e30
CLIP_NORM = 1.0
BETA_ONE = 0.9
BETA_TWO = 0.98
ADAM_EPS = 1e-08
WEIGHT_DECAY = 0.1
RATE_ATTEND = 0.03
RATE_OUTPUT = 0.5
RATE_EXPAND = 0.03
RATE_REDUCE = 0.015
RATE_GAINS = 1.0
RATE_BIAS = 0.5


def angles(times):
    half_dim = HEAD_DIM // 2
    frequency = jnp.exp(-math.log(ROPE_BASE) * jnp.arange(half_dim).astype(jnp.float32) / half_dim)
    angle_table = times.astype(jnp.float32)[..., None] * frequency
    return (jnp.cos(angle_table)[..., None, :], jnp.sin(angle_table)[..., None, :])


def rotate(values, cos_table, sin_table):
    half_dim = values.shape[-1] // 2
    first_half = values[..., :half_dim]
    second_half = values[..., half_dim:]
    return jnp.concatenate(
        [
            first_half * cos_table - second_half * sin_table,
            second_half * cos_table + first_half * sin_table,
        ],
        axis=-1,
    )


def unrotate(values, cos_table, sin_table):
    half_dim = values.shape[-1] // 2
    first_half = values[..., :half_dim]
    second_half = values[..., half_dim:]
    return jnp.concatenate(
        [
            first_half * cos_table + second_half * sin_table,
            second_half * cos_table - first_half * sin_table,
        ],
        axis=-1,
    )


def normalize(values):
    inv_scale = lax.rsqrt(jnp.mean(values * values, axis=-1, keepdims=True) + NORM_EPS)
    return (values * inv_scale, inv_scale)


def norm_back(grad_act, unit_rows, inv_scale, gain_row):
    grad_unit = grad_act * gain_row
    return inv_scale * (
        grad_unit - unit_rows * jnp.mean(grad_unit * unit_rows, axis=-1, keepdims=True)
    )


def score_block(query_rows, query_labels, key_rows, key_labels, bias_table):
    scores = jnp.einsum(
        "ihe,jhe->hij", query_rows, key_rows, preferred_element_type=jnp.float32
    ) * HEAD_DIM ** (-0.5)
    same_var = query_labels[:, None] == key_labels[None, :]
    scores = scores + jnp.where(
        same_var[None], bias_table[0][:, None, None], bias_table[1][:, None, None]
    )
    scores = jnp.where(key_labels[None, None, :] >= 0, scores, MASKED)
    return (scores, same_var)


def block_grads(
    query_rows,
    query_labels,
    grad_rows,
    lse_rows,
    delta_rows,
    key_rows,
    value_rows,
    key_labels,
    bias_table,
    need_query,
    need_keys,
):
    scores, same_var = score_block(query_rows, query_labels, key_rows, key_labels, bias_table)
    weights = jnp.exp(scores - lse_rows.T[:, :, None])
    grad_weights = jnp.einsum(
        "ihe,jhe->hij", grad_rows, value_rows, preferred_element_type=jnp.float32
    )
    grad_scores = (weights * (grad_weights - delta_rows.T[:, :, None])).astype(jnp.bfloat16)
    result = ()
    if need_query:
        grad_query = jnp.einsum(
            "hij,jhe->ihe", grad_scores, key_rows, preferred_element_type=jnp.float32
        ) * HEAD_DIM ** (-0.5)
        widened = grad_scores.astype(jnp.float32)
        bias_same = jnp.sum(jnp.where(same_var[None], widened, 0.0), axis=(1, 2))
        bias_other = jnp.sum(jnp.where(same_var[None], 0.0, widened), axis=(1, 2))
        result = result + (grad_query, jnp.stack([bias_same, bias_other]))
    if need_keys:
        grad_key = jnp.einsum(
            "hij,ihe->jhe", grad_scores, query_rows, preferred_element_type=jnp.float32
        ) * HEAD_DIM ** (-0.5)
        grad_value = jnp.einsum(
            "hij,ihe->jhe",
            weights.astype(jnp.bfloat16),
            grad_rows,
            preferred_element_type=jnp.float32,
        )
        result = result + (grad_key, grad_value)
    return result


def adam_step(weight, first_moment, second_moment, gradient, step_rate, decay_rate):
    first_moment = BETA_ONE * first_moment + (1.0 - BETA_ONE) * gradient
    second_moment = BETA_TWO * second_moment + (1.0 - BETA_TWO) * gradient * gradient
    direction = (
        first_moment
        / (1.0 - BETA_ONE**STEP)
        / (jnp.sqrt(second_moment / (1.0 - BETA_TWO**STEP)) + ADAM_EPS)
    )
    return (weight - step_rate * (direction + decay_rate * weight), first_moment, second_moment)


def general_body(
    inputs,
    teacher,
    lengths,
    variate_ids,
    time_ids,
    observed,
    attend_weight,
    output_weight,
    expand_weight,
    reduce_weight,
    norm_gains,
    variate_bias,
    attend_first,
    output_first,
    expand_first,
    reduce_first,
    gains_first,
    bias_first,
    attend_second,
    output_second,
    expand_second,
    reduce_second,
    gains_second,
    bias_second,
):
    row_count = inputs.shape[1]
    length = row_count * lax.axis_size("seq")
    block_rows = math.gcd(length, 1024)
    blocks = length // block_rows
    states = inputs[0].astype(jnp.float32)
    positions = lax.axis_index("seq") * row_count + jnp.arange(row_count, dtype=jnp.int32)
    inside = positions < lengths[0]
    scored = jnp.logical_and(inside, observed[0] == 1)
    local_count = jnp.sum(scored.astype(jnp.int32))
    count_early = lax.psum(local_count, ("seq", "batch"))
    full_attend, full_output, full_expand, full_reduce = (
        lax.all_gather(attend_weight.astype(jnp.bfloat16), ("seq", "batch"), axis=1, tiled=True),
        lax.all_gather(output_weight.astype(jnp.bfloat16), ("seq", "batch"), axis=0, tiled=True),
        lax.all_gather(expand_weight.astype(jnp.bfloat16), ("seq", "batch"), axis=1, tiled=True),
        lax.all_gather(reduce_weight.astype(jnp.bfloat16), ("seq", "batch"), axis=0, tiled=True),
    )
    unit_one, scale_one = normalize(states)
    act_one = (unit_one * norm_gains[0]).astype(jnp.bfloat16)
    project = jnp.einsum("td,cde->cte", act_one, full_attend, preferred_element_type=jnp.float32)
    cos_table, sin_table = angles(time_ids[0])
    query = rotate(project[0].reshape(row_count, HEADS, HEAD_DIM), cos_table, sin_table).astype(
        jnp.bfloat16
    )
    key_rows = (
        rotate(project[1].reshape(row_count, HEADS, HEAD_DIM), cos_table, sin_table)
        .astype(jnp.bfloat16)
        .reshape(row_count, D)
    )
    value_rows = project[2].astype(jnp.bfloat16)
    own_labels = jnp.where(inside, variate_ids[0], -1).astype(jnp.bfloat16)
    all_keys, all_values, all_labels = (
        lax.all_gather(key_rows, "seq", axis=0, tiled=True),
        lax.all_gather(value_rows, "seq", axis=0, tiled=True),
        lax.all_gather(own_labels, "seq", axis=0, tiled=True),
    )
    key_blocks = all_keys.reshape(blocks, block_rows, HEADS, HEAD_DIM)
    value_blocks = all_values.reshape(blocks, block_rows, HEADS, HEAD_DIM)
    label_blocks = all_labels.astype(jnp.float32).reshape(blocks, block_rows)
    query_labels = variate_ids[0].astype(jnp.float32)

    def sweep_top(carry, pieces):
        running, sum_exp = carry
        scores, same_var = score_block(query, query_labels, pieces[0], pieces[1], variate_bias)
        raised = jnp.maximum(running, jnp.floor(jnp.max(scores, axis=-1)))
        sum_exp = sum_exp * jnp.exp(running - raised) + jnp.sum(
            jnp.exp(scores - raised[..., None]), axis=-1
        )
        return ((raised, sum_exp), None)

    start_top = jnp.full((HEADS, row_count), MASKED, jnp.float32)
    (row_top, sum_exp), unused = lax.scan(
        sweep_top,
        (start_top, jnp.zeros((HEADS, row_count), jnp.float32)),
        (key_blocks, label_blocks),
    )
    log_total = row_top + jnp.log(sum_exp)

    def sweep_out(carry, pieces):
        coarse, finest = carry
        scores, same_var = score_block(query, query_labels, pieces[0], pieces[2], variate_bias)
        weights = jnp.exp(scores - log_total[..., None])
        rounded = weights.astype(jnp.bfloat16)
        residue = (weights - rounded.astype(jnp.float32)).astype(jnp.bfloat16)
        coarse = coarse + jnp.einsum(
            "hij,jhe->ihe", rounded, pieces[1], preferred_element_type=jnp.float32
        )
        finest = finest + jnp.einsum(
            "hij,jhe->ihe", residue, pieces[1], preferred_element_type=jnp.float32
        )
        return ((coarse, finest), None)

    zero_heads = jnp.zeros((row_count, HEADS, HEAD_DIM), jnp.float32)
    (coarse, finest), unused = lax.scan(
        sweep_out, (zero_heads, zero_heads), (key_blocks, value_blocks, label_blocks)
    )
    exact_heads = coarse + finest
    mixed = coarse.reshape(row_count, D).astype(jnp.bfloat16)
    middle = states + jnp.dot(mixed, full_output, preferred_element_type=jnp.float32)
    unit_two, scale_two = normalize(middle)
    act_two = (unit_two * norm_gains[1]).astype(jnp.bfloat16)
    gate_up = jnp.einsum("td,cdf->ctf", act_two, full_expand, preferred_element_type=jnp.float32)
    sigmoid = jax.nn.sigmoid(gate_up[0])
    hidden = (gate_up[0] * sigmoid * gate_up[1]).astype(jnp.bfloat16)
    output = middle + jnp.dot(hidden, full_reduce, preferred_element_type=jnp.float32)
    error = output - teacher[0].astype(jnp.float32)
    local_square = jnp.sum(jnp.where(scored[:, None], error * error, 0.0))
    square_total = lax.psum(local_square, ("seq", "batch"))
    count_all = count_early.astype(jnp.float32)
    loss = square_total / (count_all * D)
    grad_out = jnp.where(scored[:, None], error * (2.0 / (count_all * D)), 0.0)
    back_attend, back_output, back_expand, back_reduce = (
        lax.all_gather(attend_weight.astype(jnp.bfloat16), ("seq", "batch"), axis=1, tiled=True),
        lax.all_gather(output_weight.astype(jnp.bfloat16), ("seq", "batch"), axis=0, tiled=True),
        lax.all_gather(expand_weight.astype(jnp.bfloat16), ("seq", "batch"), axis=1, tiled=True),
        lax.all_gather(reduce_weight.astype(jnp.bfloat16), ("seq", "batch"), axis=0, tiled=True),
    )
    grad_branch = grad_out.astype(jnp.bfloat16)
    reduce_grad = jnp.einsum("tf,td->fd", hidden, grad_branch, preferred_element_type=jnp.float32)
    grad_hidden = jnp.einsum(
        "td,fd->tf", grad_branch, back_reduce, preferred_element_type=jnp.float32
    )
    grad_gate = grad_hidden * gate_up[1] * sigmoid * (1.0 + gate_up[0] * (1.0 - sigmoid))
    grad_up = grad_hidden * gate_up[0] * sigmoid
    grad_expand = jnp.stack([grad_gate, grad_up]).astype(jnp.bfloat16)
    expand_grad = jnp.einsum(
        "td,ctf->cdf", act_two, grad_expand, preferred_element_type=jnp.float32
    )
    grad_act_two = jnp.einsum(
        "ctf,cdf->td", grad_expand, back_expand, preferred_element_type=jnp.float32
    )
    expand_share, reduce_share = (
        lax.psum_scatter(expand_grad, ("seq", "batch"), scatter_dimension=1, tiled=True),
        lax.psum_scatter(reduce_grad, ("seq", "batch"), scatter_dimension=0, tiled=True),
    )
    grad_middle = grad_out + norm_back(grad_act_two, unit_two, scale_two, norm_gains[1])
    grad_attn = grad_middle.astype(jnp.bfloat16)
    output_grad = jnp.einsum("td,te->de", mixed, grad_attn, preferred_element_type=jnp.float32)
    grad_mixed = jnp.einsum(
        "te,de->td", grad_attn, back_output, preferred_element_type=jnp.float32
    ).astype(jnp.bfloat16)
    grad_heads = grad_mixed.reshape(row_count, HEADS, HEAD_DIM)
    row_delta = jnp.sum(grad_heads.astype(jnp.float32) * exact_heads, axis=-1)
    lse_rows = log_total.T
    zero_bias = jnp.zeros((2, HEADS), jnp.float32)

    def sweep_query(carry, pieces):
        part_query, part_bias = block_grads(
            query,
            query_labels,
            grad_heads,
            lse_rows,
            row_delta,
            pieces[0],
            pieces[1],
            pieces[2],
            variate_bias,
            True,
            False,
        )
        return ((carry[0] + part_query, carry[1] + part_bias), None)

    (query_total, bias_grad), unused = lax.scan(
        sweep_query, (zero_heads, zero_bias), (key_blocks, value_blocks, label_blocks)
    )
    all_query, all_grad = (
        lax.all_gather(query.reshape(row_count, D), "seq", axis=0, tiled=True),
        lax.all_gather(grad_mixed, "seq", axis=0, tiled=True),
    )
    all_lse, all_delta = (
        lax.all_gather(lse_rows, "seq", axis=0, tiled=True),
        lax.all_gather(row_delta, "seq", axis=0, tiled=True),
    )
    key_heads = key_rows.reshape(row_count, HEADS, HEAD_DIM)
    value_heads = value_rows.reshape(row_count, HEADS, HEAD_DIM)
    own_float = own_labels.astype(jnp.float32)

    def sweep_keys(carry, pieces):
        part_key, part_value = block_grads(
            pieces[0],
            pieces[1],
            pieces[2],
            pieces[3],
            pieces[4],
            key_heads,
            value_heads,
            own_float,
            variate_bias,
            False,
            True,
        )
        return ((carry[0] + part_key, carry[1] + part_value), None)

    (key_total, value_heads_total), unused = lax.scan(
        sweep_keys,
        (zero_heads, zero_heads),
        (
            all_query.reshape(blocks, block_rows, HEADS, HEAD_DIM),
            label_blocks,
            all_grad.reshape(blocks, block_rows, HEADS, HEAD_DIM),
            all_lse.reshape(blocks, block_rows, HEADS),
            all_delta.reshape(blocks, block_rows, HEADS),
        ),
    )
    value_total = value_heads_total.reshape(row_count, D)
    grad_query = unrotate(query_total, cos_table, sin_table).reshape(row_count, D)
    grad_key = unrotate(key_total, cos_table, sin_table).reshape(row_count, D)
    grad_project = jnp.stack([grad_query, grad_key, value_total]).astype(jnp.bfloat16)
    attend_grad = jnp.einsum(
        "td,cte->cde", act_one, grad_project, preferred_element_type=jnp.float32
    )
    grad_act_one = jnp.einsum(
        "cte,cde->td", grad_project, back_attend, preferred_element_type=jnp.float32
    )
    attend_share, output_share = (
        lax.psum_scatter(attend_grad, ("seq", "batch"), scatter_dimension=1, tiled=True),
        lax.psum_scatter(output_grad, ("seq", "batch"), scatter_dimension=0, tiled=True),
    )
    grad_input = grad_middle + norm_back(grad_act_one, unit_one, scale_one, norm_gains[0])
    gains_grad = jnp.stack(
        [jnp.sum(grad_act_one * unit_one, axis=0), jnp.sum(grad_act_two * unit_two, axis=0)]
    )
    local_squares = (
        jnp.sum(attend_share * attend_share)
        + jnp.sum(output_share * output_share)
        + jnp.sum(expand_share * expand_share)
        + jnp.sum(reduce_share * reduce_share)
    )
    gains_total, bias_total, square_sum = lax.psum(
        (gains_grad, bias_grad, local_squares), ("seq", "batch")
    )
    grad_norm = jnp.sqrt(
        square_sum + jnp.sum(gains_total * gains_total) + jnp.sum(bias_total * bias_total)
    )
    clip_scale = jnp.minimum(1.0, CLIP_NORM / grad_norm)
    attend_new, attend_first_new, attend_second_new = adam_step(
        attend_weight,
        attend_first,
        attend_second,
        attend_share * clip_scale,
        RATE_ATTEND,
        WEIGHT_DECAY,
    )
    output_new, output_first_new, output_second_new = adam_step(
        output_weight,
        output_first,
        output_second,
        output_share * clip_scale,
        RATE_OUTPUT,
        WEIGHT_DECAY,
    )
    expand_new, expand_first_new, expand_second_new = adam_step(
        expand_weight,
        expand_first,
        expand_second,
        expand_share * clip_scale,
        RATE_EXPAND,
        WEIGHT_DECAY,
    )
    reduce_new, reduce_first_new, reduce_second_new = adam_step(
        reduce_weight,
        reduce_first,
        reduce_second,
        reduce_share * clip_scale,
        RATE_REDUCE,
        WEIGHT_DECAY,
    )
    gains_new, gains_first_new, gains_second_new = adam_step(
        norm_gains, gains_first, gains_second, gains_total * clip_scale, RATE_GAINS, 0.0
    )
    bias_new, bias_first_new, bias_second_new = adam_step(
        variate_bias, bias_first, bias_second, bias_total * clip_scale, RATE_BIAS, 0.0
    )
    input_gradient = (grad_input * count_all * D)[None]
    return (
        output[None],
        loss,
        input_gradient,
        grad_norm,
        attend_new,
        attend_new.astype(jnp.bfloat16),
        attend_first_new,
        attend_second_new,
        output_new,
        output_new.astype(jnp.bfloat16),
        output_first_new,
        output_second_new,
        expand_new,
        expand_new.astype(jnp.bfloat16),
        expand_first_new,
        expand_second_new,
        reduce_new,
        reduce_new.astype(jnp.bfloat16),
        reduce_first_new,
        reduce_second_new,
        gains_new,
        gains_first_new,
        gains_second_new,
        bias_new,
        bias_first_new,
        bias_second_new,
    )


MESH = pl.DeviceIdType.MESH
IN_VMEM = pl.BlockSpec(memory_space=pltpu.VMEM)
IN_SMEM = pl.BlockSpec(memory_space=pltpu.SMEM)
LANES = 128
HEADS_HERE = LANES // HEAD_DIM
VARIATES = 16
MIB = 1 << 20
LOW = jnp.bfloat16
WIDE = jnp.float32
TOTAL_ROWS = 24


def fast_fits(seq, batch):
    return seq == 8 and batch == 4 and seq * LANES == D


def flip(index, mask):
    result, bit = index, 1
    while bit <= mask:
        if mask & bit:
            result = result + bit - 2 * bit * lax.rem(lax.div(index, bit), 2)
        bit *= 2
    return result


def push(source, target, send_sem, recv_sem, device):
    return pltpu.make_async_remote_copy(
        src_ref=source,
        dst_ref=target,
        send_sem=send_sem,
        recv_sem=recv_sem,
        device_id=device,
        device_id_type=MESH,
    )


def block_of(index, size):
    return pl.ds(pl.multiple_of(index * size, size), size)


def dot(left, right):
    return jnp.dot(left, right, preferred_element_type=WIDE)


def dot_turned(left, right):
    return lax.dot_general(left, right, (((1,), (1,)), ((), ())), preferred_element_type=WIDE)


def turned_dot(left, right):
    return lax.dot_general(left, right, (((0,), (0,)), ((), ())), preferred_element_type=WIDE)


class Team:
    def __init__(self, index, place):
        self.index, self.place = index, place

    def at(self, mask):
        return flip(self.index, mask)


def head_team(me, group):
    return Team(me, lambda mask: (flip(me, mask), group))


def feed_team(me, group):
    return Team(
        4 * lax.rem(group, 2) + lax.rem(me, 4),
        lambda mask: (flip(me, mask % 4), flip(group, mask // 4)),
    )


class Gather:
    def __init__(self, team, rows, all_rows, sends, recvs):
        self.team, self.all_rows, self.sends, self.recvs = team, all_rows, sends, recvs
        self.size = all_rows.shape[0] // 8
        self.given = rows
        self.rows = all_rows.at[block_of(team.index, self.size)] if rows is None else rows

    def copy(self, mask, passing):
        source = self.all_rows.at[block_of(self.team.at(mask - 1 if passing else 0), self.size)]
        return push(
            source if passing else self.rows,
            source,
            self.sends.at[mask],
            self.recvs.at[mask],
            self.team.place(1 if passing else mask),
        )

    def start(self, masks=(6, 2, 4, 1)):
        for mask in masks:
            self.copy(mask, False).start()
        if self.given is not None:
            self.all_rows[block_of(self.team.index, self.size)] = self.given[...]

    def pass_on(self, chip):
        self.copy(2 * chip, False).wait_recv()
        self.copy(2 * chip + 1, True).start()

    def complete(self, chip):
        self.copy(2 * chip + 1, chip > 0).wait_recv()

    def finish(self):
        for mask in (6, 2, 4, 1):
            self.copy(mask, False).wait_send()
        for mask in (3, 5, 7):
            self.copy(mask, True).wait_send()


def at_step(step, number, *works):
    @pl.when(step == number)
    def _():
        for work in works:
            work()


def each_chip(gather, work, after):
    def one_chip(chip, unused):
        @pl.when(chip == 0)
        def _():
            gather.complete(0)

        @pl.when(chip == 1)
        def _():
            gather.pass_on(1)
            gather.pass_on(2)
            gather.copy(6, False).start()
            gather.complete(1)

        @pl.when(chip == 2)
        def _():
            gather.complete(2)

        @pl.when(chip == 3)
        def _():
            gather.pass_on(3)
            gather.complete(3)

        work(chip)
        for number, works in after.items():
            at_step(chip, number, *works)
        return unused

    lax.fori_loop(0, 4, one_chip, 0)
    gather.finish()


class Scatter:
    def __init__(self, team, buffers, near_sends, near_recvs, far_sends, far_recvs):
        self.whole, self.keep, self.near_from, self.near, self.far_from, self.far = buffers
        self.sems = near_sends, near_recvs, far_sends, far_recvs
        self.team = team
        self.size = self.keep.shape[1]

    def near_copy(self, chip):
        return push(
            self.near_from.at[chip],
            self.near.at[chip],
            self.sems[0].at[chip],
            self.sems[1].at[chip],
            self.team.place(1),
        )

    def far_copy(self, chip):
        return push(
            self.far_from.at[chip],
            self.far.at[chip],
            self.sems[2].at[chip],
            self.sems[3].at[chip],
            self.team.place(2 * chip),
        )

    def put(self, chip, rows):
        core = lax.rem(self.team.index, 2)
        self.whole[...] = rows
        self.near_from[chip] = self.whole[block_of(1 - core, self.size)].astype(LOW)
        self.near_copy(chip).start()
        self.keep[chip] = self.whole[block_of(core, self.size)]

    def combine(self, chip):
        self.near_copy(chip).wait_recv()
        self.far_from[chip] = (self.keep[chip] + self.near[chip].astype(WIDE)).astype(LOW)
        self.far_copy(chip).start()

    def total(self):
        self.near_copy(0).wait_recv()
        total = self.keep[0] + self.near[0].astype(WIDE)
        for chip in (1, 2, 3):
            self.far_copy(chip).wait_recv()
            total = total + self.far[chip].astype(WIDE)
        for chip in (0, 1, 2, 3):
            self.near_copy(chip).wait_send()
            if chip:
                self.far_copy(chip).wait_send()
        return total


class LineGather:
    def __init__(self, part_of, sends, recvs, me, group):
        self.part_of, self.sends, self.recvs, self.me, self.group = part_of, sends, recvs, me, group
        self.middle = jnp.logical_and(group >= 1, group <= 2)

    def copy(self, part, target, slot):
        return push(
            self.part_of(part),
            self.part_of(part),
            self.sends.at[slot],
            self.recvs.at[part],
            (self.me, target),
        )

    def start(self):
        group = self.group

        @pl.when(self.middle)
        def _():
            self.copy(group, 3 - group, 3 - group).start()
            self.copy(group, 3 * (group - 1), 3 * (group - 1)).start()

        @pl.when(jnp.logical_not(self.middle))
        def _():
            for step in (2, 1, 3):
                other = lax.rem(group + step, 4)
                self.copy(group, other, other).start()

    def pass_on(self):
        group = self.group

        @pl.when(self.middle)
        def _():
            self.copy(3 - group, 3 * (group - 1), group).wait_recv()
            self.copy(3 - group, 3 * (group - 1), group).start()

    def land(self):
        group = self.group

        @pl.when(self.middle)
        def _():
            for part in (0, 3):
                self.copy(part, 3 - group, group).wait_recv()

        @pl.when(jnp.logical_not(self.middle))
        def _():
            for step in (1, 2, 3):
                other = lax.rem(group + step, 4)
                self.copy(other, other, other).wait_recv()

    def finish(self):
        group = self.group

        @pl.when(self.middle)
        def _():
            for other in (3 - group, 3 * (group - 1), group):
                self.copy(group, 3 - group, other).wait_send()

        @pl.when(jnp.logical_not(self.middle))
        def _():
            for step in (1, 2, 3):
                other = lax.rem(group + step, 4)
                self.copy(group, other, other).wait_send()


class LineScatter:
    def __init__(self, part_of, landing, sends, recvs, me, group):
        self.part_of, self.landing, self.sends, self.recvs = part_of, landing, sends, recvs
        self.me, self.group = me, group
        self.middle = jnp.logical_and(group >= 1, group <= 2)
        self.opposite = 3 - 3 * lax.div(group, 2)

    def copy(self, part, slot, target, sem):
        return push(
            self.part_of(part),
            self.landing.at[slot],
            self.sends.at[sem],
            self.recvs.at[slot],
            (self.me, target),
        )

    def start(self):
        group = self.group

        @pl.when(self.middle)
        def _():
            for other in (3 - group, 3 * (group - 1)):
                self.copy(other, group, other, other).start()

        @pl.when(jnp.logical_not(self.middle))
        def _():
            beside = 1 + lax.div(group, 3)
            self.copy(3 - group, beside, beside, 3 - group).start()
            for other in (3 - beside, beside):
                self.copy(other, group, other, other).start()

    def pass_on(self):
        group, opposite = self.group, self.opposite

        @pl.when(self.middle)
        def _():
            self.copy(opposite, group, opposite, group).wait_recv()
            part = self.part_of(opposite)
            part[...] = (part[...].astype(WIDE) + self.landing[group].astype(WIDE)).astype(LOW)
            self.copy(opposite, group, opposite, group).start()

    def land(self):
        group = self.group

        @pl.when(self.middle)
        def _():
            for slot in (0, 3 - group, 3):
                self.copy(group, slot, 3 - group, group).wait_recv()

        @pl.when(jnp.logical_not(self.middle))
        def _():
            for slot in (1, 2):
                self.copy(group, slot, slot, group).wait_recv()

    def add(self, own, landed, store):
        group = self.group

        @pl.when(self.middle)
        def _():
            store(own() + landed(0) + landed(3 - group) + landed(3))

        @pl.when(jnp.logical_not(self.middle))
        def _():
            store(own() + landed(1) + landed(2))

    def finish(self):
        group = self.group

        @pl.when(self.middle)
        def _():
            for sem in (3 - group, 3 * (group - 1), group):
                self.copy(group, group, 3 - group, sem).wait_send()

        @pl.when(jnp.logical_not(self.middle))
        def _():
            for sem in (3 - group, 1, 2):
                self.copy(group, group, 1, sem).wait_send()


class Quad:
    def __init__(self, part, along_near, along_far):
        self.part, self.along_near, self.along_far = part, along_near, along_far


def feed_quad(me, group):
    return Quad(2 * lax.div(me, 4) + lax.div(group, 2), (flip(me, 4), group), (me, flip(group, 2)))


class QuadGather:
    def __init__(self, quad, part_of, sends, recvs):
        self.part_of, self.sends, self.recvs = part_of, sends, recvs
        self.part, self.along_near, self.along_far = quad.part, quad.along_near, quad.along_far

    def copy(self, way):
        part = self.part_of(flip(self.part, 1) if way == 3 else self.part)
        device = self.along_far if way == 1 else self.along_near
        return push(part, part, self.sends.at[way], self.recvs.at[way], device)

    def start_near(self):
        self.copy(2).start()

    def start_far(self):
        self.copy(1).start()

    def start(self):
        self.start_far()
        self.start_near()

    def pass_on(self):
        self.copy(1).wait_recv()
        self.copy(3).start()

    def land(self):
        self.copy(2).wait_recv()
        self.copy(3).wait_recv()

    def finish(self):
        for way in (1, 2, 3):
            self.copy(way).wait_send()


class QuadScatter:
    def __init__(self, quad, part_of, landing, sends, recvs):
        self.part_of, self.landing, self.sends, self.recvs = part_of, landing, sends, recvs
        self.part, self.along_near, self.along_far = quad.part, quad.along_near, quad.along_far

    def copy(self, slot):
        return push(
            self.part_of(flip(self.part, (2, 3, 1)[slot])),
            self.landing.at[slot],
            self.sends.at[slot],
            self.recvs.at[slot],
            self.along_far if slot == 2 else self.along_near,
        )

    def start_far(self):
        self.copy(1).start()

    def start_near(self):
        self.copy(0).start()

    def start(self):
        self.start_far()
        self.start_near()

    def total(self):
        total = self.part_of(self.part)[...].astype(WIDE)
        return total + self.landing[0].astype(WIDE) + self.landing[2].astype(WIDE)

    def pass_on(self):
        self.copy(1).wait_recv()
        part = self.part_of(flip(self.part, 1))
        part[...] = (part[...].astype(WIDE) + self.landing[1].astype(WIDE)).astype(LOW)
        self.copy(2).start()

    def land(self):
        self.copy(0).wait_recv()
        self.copy(2).wait_recv()

    def finish(self):
        for slot in (0, 1, 2):
            self.copy(slot).wait_send()


def chip_of(team, chip):
    here = lax.div(team.index, 2)
    if isinstance(chip, int):
        return flip(here, chip)
    column = lax.rem(lax.rem(here, 2) + lax.rem(chip, 2), 2)
    row = lax.rem(lax.div(here, 2) + lax.div(chip, 2), 2)
    return 2 * row + column


def turn_rows(values, cosine, sine):
    half = HEAD_DIM // 2
    pieces = []
    for start in range(0, values.shape[0], HEAD_DIM):
        first, second = values[start : start + half], values[start + half : start + HEAD_DIM]
        pieces += [first * cosine - second * sine, second * cosine + first * sine]
    return jnp.concatenate(pieces, axis=0)


def turned(eye, values):
    size = min(values.shape[1], eye.shape[0])
    rows = [
        dot_turned(eye[:size, :size], values[:, start : start + size]).astype(LOW)
        for start in range(0, values.shape[1], size)
    ]
    return rows[0] if len(rows) == 1 else jnp.concatenate(rows, axis=0)


def thirds(values):
    first = values.astype(LOW).astype(WIDE)
    second = (values - first).astype(LOW).astype(WIDE)
    return first, second, values - first - second


def pick(row, choices):
    result = jnp.zeros(row.shape, WIDE)
    for number, choice in choices.items():
        result = jnp.where(row == number, choice, result)
    return result


def norm_rows(values):
    scale = lax.rsqrt(jnp.mean(values * values, axis=-1, keepdims=True) + NORM_EPS)
    return values * scale, scale


def feed_block(block):
    y, x, core, far_z, near_z = (block // 16, block // 8 % 2, block // 4 % 2, block // 2 % 2, block % 2)
    return 4 * near_z + 2 * x + core, 2 * y + far_z


def layer_kernel(seq, batch, ins, outs, mem):
    me, group = lax.axis_index("seq"), lax.axis_index("batch")
    rows = ins.inputs.shape[0]
    length = rows * seq
    pair = 2 * rows
    share = ins.attend.shape[1]
    wide_columns = ins.expand.shape[2] // D
    hidden_width = mem.reduce_all.shape[0] * mem.reduce_all.shape[1]
    blocks = ins.expand.shape[2] // LANES
    heads, feeds = head_team(me, group), feed_team(me, group)
    feed_four = feed_quad(me, group)
    quad = feed_four.part

    staged = [(ins.attend.at[which], mem.keep.at[0, block_of(which, share)]) for which in range(3)]
    staged.append((ins.output, mem.keep.at[0, block_of(3, share)]))
    staged.append((ins.reduce, mem.keep.at[1]))
    for which in range(2):
        for block in range(wide_columns):
            columns = slice(block * D, (block + 1) * D)
            staged.append(
                (ins.expand.at[which, :, columns], mem.keep.at[2 + which, block_of(block, share)])
            )
    staged = [
        pltpu.make_async_copy(source, target, mem.stage_sem.at[number])
        for number, (source, target) in enumerate(staged)
    ]
    for copy in staged:
        copy.start()
    barrier = pltpu.get_barrier_semaphore()
    for mask in range(1, seq):
        pl.semaphore_signal(barrier, inc=1, device_id=(flip(me, mask), group), device_id_type=MESH)
    for step in range(1, batch):
        pl.semaphore_signal(
            barrier, inc=1, device_id=(me, lax.rem(group + step, batch)), device_id_type=MESH
        )
    for mask in (5, 6, 7):
        pl.semaphore_signal(barrier, inc=1, device_id=feeds.place(mask), device_id_type=MESH)

    square = (pair, pair)
    mem.eye[...] = jnp.where(
        lax.broadcasted_iota(jnp.int32, square, 0) == lax.broadcasted_iota(jnp.int32, square, 1), 1.0, 0.0
    ).astype(LOW)
    position = me * rows + lax.broadcasted_iota(jnp.int32, (1, rows), 1)
    inside = position < ins.lengths[...]
    scored = jnp.logical_and(inside, ins.observed[...] == 1).astype(WIDE)
    variate = ins.variates[...].astype(WIDE)
    half_dim = HEAD_DIM // 2
    number = lax.broadcasted_iota(jnp.int32, (half_dim, rows), 0).astype(WIDE)
    angle = jnp.exp(-math.log(ROPE_BASE) * number / half_dim) * ins.times[...].astype(WIDE)
    mem.facts_own[: HEAD_DIM // 2] = jnp.cos(angle)
    mem.facts_own[HEAD_DIM // 2 : HEAD_DIM] = jnp.sin(angle)
    mem.facts_own[HEAD_DIM:] = jnp.concatenate(
        [jnp.where(inside, variate, -1.0), variate, scored, jnp.zeros((5, rows), WIDE)], axis=0
    )
    mem.scored[...] = jnp.broadcast_to(scored, (rows, rows)).T
    for copy in staged:
        copy.wait()
    for which in range(3):
        mem.attend_low[which] = mem.keep[0, block_of(which, share)].astype(LOW)
    pl.semaphore_wait(barrier, seq + batch + 1)

    masks = (6, 7, 4, 5, 2, 3, 1)

    def start_attend_columns():
        copies = []
        for mask in masks:
            copy = push(
                mem.attend_low.at[:, :, block_of(heads.at(mask), LANES)],
                mem.attend_all.at[:, me, group],
                mem.column_send.at[0, mask],
                mem.column_recv.at[0, mask],
                heads.place(mask),
            )
            copy.start()
            copies.append(copy)
        mem.attend_all[:, me, group] = mem.attend_low[:, :, block_of(me, LANES)]
        return copies

    def start_expand_columns():
        copies = []
        for mask in masks:
            copy = push(
                mem.expand_low.at[:, feeds.at(mask)],
                mem.expand_all.at[:, me, group],
                mem.column_send.at[1, mask],
                mem.column_recv.at[1, mask],
                feeds.place(mask),
            )
            copy.start()
            copies.append(copy)
        mem.expand_all[:, me, group] = mem.expand_low[:, feeds.index]
        return copies

    def expand_part_of(array, which):
        def part_of(part):
            return array.at[which, pl.ds(4 * lax.div(part, 2), 4), pl.ds(2 * lax.rem(part, 2), 2)]

        return part_of

    def line_gather(row, part_of):
        return LineGather(part_of, mem.line_send.at[row], mem.line_recv.at[row], me, group)

    def quad_gather(four, row, part_of):
        return QuadGather(four, part_of, mem.line_send.at[row], mem.line_recv.at[row])

    def gather(team, phase, all_rows):
        return Gather(
            team,
            mem.own_rows.at[phase],
            all_rows,
            mem.gather_send.at[phase],
            mem.gather_recv.at[phase],
        )

    def scatter(team, phase):
        return Scatter(
            team,
            (mem.whole, mem.keep, mem.near_from, mem.near, mem.far_from, mem.far),
            mem.near_send.at[phase],
            mem.near_recv.at[phase],
            mem.far_send.at[phase],
            mem.far_recv.at[phase],
        )

    attend_columns = start_attend_columns()
    mem.output_full[block_of(batch * me + group, share)] = mem.keep[0, block_of(3, share)].astype(LOW)
    mem.reduce_all[quad] = mem.keep[1].astype(LOW)
    for which in range(2):
        for block in range(blocks):
            owner, part = feed_block(block)
            row, lane = divmod(block * LANES, D)
            mem.expand_low[which, owner, :, part * LANES : (part + 1) * LANES] = mem.keep[
                2 + which, block_of(row, share), lane : lane + LANES
            ].astype(LOW)
    line_output = line_gather(1, lambda part: mem.output_full.at[block_of(batch * me + part, share)])
    line_output.start()
    unit_one, scale_one = norm_rows(ins.inputs[...].astype(WIDE))
    mem.own_rows[0] = (unit_one * ins.gains[0:1, :]).astype(LOW)
    facts = Gather(heads, mem.facts_own, mem.facts_all, mem.facts_send, mem.facts_recv)
    facts.start()
    for copy in attend_columns:
        copy.wait_recv()
    line_attend = line_gather(0, lambda part: mem.attend_all.at[:, :, part])
    line_attend.start()
    acts = gather(heads, 0, mem.act_one)
    acts.start()
    for chip in (1, 2, 3):
        facts.pass_on(chip)
    for chip in (0, 1, 2, 3):
        facts.complete(chip)
    facts.finish()
    step_rows = mem.facts_own.shape[0]
    half = HEAD_DIM // 2
    count = jnp.zeros((8, LANES), WIDE)
    for slot in range(seq):
        columns = slice(slot * rows, (slot + 1) * rows)
        start = slot * step_rows
        mem.cosine[:, columns] = mem.facts_all[start : start + half]
        mem.sine[:, columns] = mem.facts_all[start + half : start + 2 * half]
        labels = mem.facts_all[start + 2 * half : start + 2 * half + 8]
        mem.labels[:, columns] = labels
        count = count + labels
    mem.count[group] = count
    count_copies = []
    for step in range(1, batch):
        copy = push(
            mem.count.at[group],
            mem.count.at[group],
            mem.count_send.at[step],
            mem.count_recv.at[step],
            (me, lax.rem(group + step, batch)),
        )
        copy.start()
        count_copies.append(copy)

    def mark(block, unused):
        span = block_of(block, pair)
        row = lax.broadcasted_iota(jnp.int32, (HEAD_DIM, pair), 0)
        third = lax.div(row, VARIATES)
        variate = lax.rem(row, VARIATES).astype(WIDE)
        key_label, query_label = mem.labels[0:1, span], mem.labels[1:2, span]
        ones = jnp.ones((1, pair), WIDE)
        last = 3 * VARIATES
        hidden_keys = (key_label < 0.0).astype(WIDE)
        mem.key_marks[:, span] = jnp.where(
            third < 3,
            (key_label == variate).astype(WIDE),
            pick(row, {last: ones, last + 1: ones, last + 2: ones, last + 3: hidden_keys}),
        ).astype(LOW)
        query_marks = (query_label == variate).astype(WIDE)
        sum_marks = jnp.where(row < VARIATES, query_marks, pick(row, {VARIATES: ones})).astype(LOW)
        for head in range(HEADS_HERE):
            mem.query_back[head, HEAD_DIM:, span] = sum_marks
            number = me * HEADS_HERE + head
            other = jnp.full((HEAD_DIM, pair), ins.bias[1, number], WIDE)
            more = thirds(jnp.full((HEAD_DIM, pair), ins.bias[0, number], WIDE) - other)
            other = thirds(other)
            mem.query_turned[head, HEAD_DIM:, span] = jnp.where(
                third < 3,
                query_marks * jnp.where(third == 0, more[0], jnp.where(third == 1, more[1], more[2])),
                pick(row, {last: other[0], last + 1: other[1], last + 2: other[2], last + 3: MASKED}),
            ).astype(LOW)
        return unused

    lax.fori_loop(0, length // pair, mark, 0)
    acts.pass_on(1)
    acts.pass_on(2)
    line_output.pass_on()
    line_output.land()
    outputs = Gather(heads, None, mem.output_full, mem.output_send, mem.output_recv)
    outputs.start()
    acts.pass_on(3)
    line_attend.pass_on()
    for chip in range(4):
        acts.complete(chip)
    acts.finish()

    expand_columns = start_expand_columns()
    line_reduce = quad_gather(feed_four, 4, lambda part: mem.reduce_all.at[part])
    line_reduce.start_far()
    line_expand = [
        quad_gather(feed_four, 2 + which, expand_part_of(mem.expand_all, which)) for which in range(2)
    ]
    line_attend.land()
    line_reduce.start_near()

    def attend_matrix(which):
        return mem.attend_all[which].reshape(D, LANES)

    def project(block, unused):
        span = block_of(block, pair)
        products = dot_turned(mem.attend_turned[...], mem.act_one[span, :])
        cosine, sine = mem.cosine[:, span], mem.sine[:, span]
        query = turn_rows(products[:LANES], cosine, sine).astype(LOW)
        query = (query.astype(WIDE) * HEAD_DIM ** (-0.5)).astype(LOW)
        key = turn_rows(products[LANES : 2 * LANES], cosine, sine).astype(LOW)
        value = products[2 * LANES :].astype(LOW)
        mem.key_turned[:, span] = key
        mem.value_turned[:, span] = value

        for head in range(HEADS_HERE):
            features = slice(head * HEAD_DIM, (head + 1) * HEAD_DIM)
            mem.query_turned[head, :HEAD_DIM, span] = query[features]
            mem.query_back[head, :HEAD_DIM, span] = query[features]
            whole = jnp.concatenate([key[features], mem.key_marks[:, span]], axis=0)
            mem.key_heads[head, span, :] = turned(mem.eye, whole)
        return unused

    for copy in expand_columns:
        copy.wait_recv()
    line_expand[0].start_far()
    line_expand[0].start_near()
    for which in range(3):
        for start in range(0, D, pair):
            piece = attend_matrix(which)[start : start + pair]
            mem.attend_turned[block_of(which, LANES), start : start + pair] = turned(mem.eye, piece)
    lax.fori_loop(0, length // pair, project, 0)
    line_expand[1].start_far()

    core = lax.rem(me, 2)

    def mixed_copy(chip, which):
        other = 2 * chip_of(heads, chip) + which
        slot = 2 * chip + lax.rem(which + core, 2)
        return push(
            mem.mixed_out.at[block_of(other, rows)],
            mem.mixed_rows.at[:, block_of(me, LANES)],
            mem.mixed_send.at[slot],
            mem.mixed_recv.at[slot],
            (other, group),
        )

    def attend_block(chip):
        columns = block_of(chip_of(heads, chip), pair)
        for head in range(HEADS_HERE):
            span = slice(head * HEAD_DIM, (head + 1) * HEAD_DIM)
            scores = dot(mem.key_heads[head], mem.query_turned[head, :, columns])
            top = jnp.floor(jnp.max(scores, axis=0, keepdims=True))
            powers = jnp.exp(scores - top)
            probs = powers * (1.0 / jnp.sum(powers, axis=0, keepdims=True))
            rounded = probs.astype(LOW)
            mem.probs[head, :, columns] = rounded
            residue = (probs - rounded.astype(WIDE)).astype(LOW)
            coarse = dot(mem.value_turned[span, :], rounded)
            mem.exact[span, columns] = coarse + dot(mem.value_turned[span, :], residue)
            mem.mixed_wide[span, :] = coarse
        mixed = mem.mixed_wide[...].astype(LOW)
        mem.mixed_turned[:, columns] = mixed
        mem.mixed_out[columns, :] = turned(mem.eye, mixed)

    def attend_step(step, unused):
        chip = lax.rem(step + 1, 4)
        attend_block(chip)
        for which in range(2):

            @pl.when(jnp.logical_or(chip > 0, core != which))
            def _():
                mixed_copy(chip, which).start()

        at_step(step, 0, lambda: outputs.pass_on(1), lambda: outputs.pass_on(2))
        at_step(step, 1, lambda: outputs.pass_on(3))
        return unused

    lax.fori_loop(0, 4, attend_step, 0)
    line_expand[1].start_near()
    mem.mixed_rows[:, block_of(me, LANES)] = mem.mixed_out[block_of(me, rows), :]
    for chip in range(4):
        outputs.complete(chip)
    outputs.finish()

    def wait_pieces(copy):
        for mask in range(1, seq):
            copy(mask).wait()

    def mixed_wait(mask):
        other = heads.at(mask)
        return push(
            mem.mixed_out.at[block_of(other, rows)],
            mem.mixed_rows.at[:, block_of(other, LANES)],
            mem.mixed_send.at[mask],
            mem.mixed_recv.at[mask],
            (other, group),
        )

    wait_pieces(mixed_wait)
    middle = ins.inputs[...].astype(WIDE) + dot(mem.mixed_rows[...], mem.output_full[...])
    mem.middle[...] = middle
    unit_two, scale_two = norm_rows(middle)
    mem.own_rows[1] = (unit_two * ins.gains[1:2, :]).astype(LOW)
    acts = gather(feeds, 1, mem.act_two)
    acts.start((2, 4, 1))
    line_reduce.pass_on()
    line_expand[0].pass_on()

    def split_heads(block, unused):
        span = block_of(block, pair)
        row = lax.broadcasted_iota(jnp.int32, (HEAD_DIM, pair), 0)
        value_marks = jnp.where(row < 3, 1.0, 0.0).astype(LOW)
        for head in range(HEADS_HERE):
            features = slice(head * HEAD_DIM, (head + 1) * HEAD_DIM)
            value = mem.value_turned[features, span]
            whole = jnp.concatenate([value, value_marks], axis=0)
            mem.value_heads[head, span, :] = turned(mem.eye, whole)
        return unused

    lax.fori_loop(0, length // pair, split_heads, 0)
    line_expand[0].land()

    def expand_matrix(which):
        return mem.expand_all[which].reshape(D, hidden_width)

    def reduce_matrix():
        return mem.reduce_all[...].reshape(hidden_width, D)

    def feed_gate(chip):
        span = block_of(chip_of(feeds, chip), pair)
        mem.by_gate[span, :] = dot(mem.act_two[span, :], expand_matrix(0))

    def feed_up(chip, unused=0):
        span = block_of(chip_of(feeds, chip), pair)
        gate = mem.by_gate[span, :]
        up = dot(mem.act_two[span, :], expand_matrix(1))
        sigmoid = 1.0 / (1.0 + jnp.exp(-gate))
        swish = gate * sigmoid
        mem.by_up[span, :] = swish
        mem.by_gate[span, :] = up * sigmoid * (1.0 + gate * (1.0 - sigmoid))
        mem.hidden[span, :] = (swish * up).astype(LOW)
        return unused

    each_chip(
        acts,
        feed_gate,
        {
            0: [line_expand[1].pass_on],
            2: [line_expand[1].land, lambda: lax.fori_loop(0, 3, feed_up, 0)],
            3: [lambda: lax.fori_loop(3, 4, feed_up, 0)],
        },
    )
    line_reduce.land()
    sums = scatter(feeds, 1)

    def feed_down(step, unused):
        chip = lax.rem(step + 1, 4)
        span = block_of(chip_of(feeds, chip), pair)
        sums.put(chip, dot(mem.hidden[span, :], reduce_matrix()))
        at_step(step, 1, lambda: sums.combine(1))
        at_step(step, 2, lambda: sums.combine(2))
        return unused

    lax.fori_loop(0, 4, feed_down, 0)
    sums.combine(3)

    def turn_feed(block, unused):
        span = block_of(block, pair)
        mem.hidden_turned[:, span] = turned(mem.eye, mem.hidden[span, :])
        mem.act_two_turned[:, span] = turned(mem.eye, mem.act_two[span, :])
        return unused

    lax.fori_loop(0, length // pair, turn_feed, 0)
    output = mem.middle[...] + sums.total()
    outs.layer_output[...] = output
    for copy in count_copies:
        copy.wait()
    count_all = jnp.sum(
        mem.count[0, 2:3] + mem.count[1, 2:3] + mem.count[2, 2:3] + mem.count[3, 2:3],
        axis=1,
        keepdims=True,
    )
    error = jnp.where(mem.scored[:, 0:1] > 0.0, output - ins.teacher[...].astype(WIDE), 0.0)
    mem.squares[1:2, :] = jnp.sum(error * error, axis=0, keepdims=True)
    grad_out = error * (2.0 / (count_all * D))
    mem.grad_own[...] = grad_out
    mem.own_rows[2] = grad_out.astype(LOW)
    acts = gather(feeds, 2, mem.branch)
    acts.start((2, 4, 1))

    def turn_acts(block, unused):
        span = block_of(block, pair)
        mem.act_one_turned[:, span] = turned(mem.eye, mem.act_one[span, :])
        return unused

    lax.fori_loop(0, length // pair, turn_acts, 0)

    sums = scatter(feeds, 2)

    def feed_back(chip):
        span = block_of(chip_of(feeds, chip), pair)
        grad_hidden = dot_turned(mem.branch[span, :], reduce_matrix())
        grad_gate = (grad_hidden * mem.by_gate[span, :]).astype(LOW)
        grad_up = (grad_hidden * mem.by_up[span, :]).astype(LOW)
        mem.grad_gate[span, :] = grad_gate
        mem.grad_up[span, :] = grad_up
        sums.put(
            chip,
            dot_turned(grad_gate, expand_matrix(0)) + dot_turned(grad_up, expand_matrix(1)),
        )

    each_chip(acts, feed_back, {2: [lambda: sums.combine(1)], 3: [lambda: sums.combine(2)]})

    def line_scatter(row, part_of, landing):
        return LineScatter(
            part_of, landing, mem.back_send.at[row], mem.back_recv.at[row], me, group
        )

    def quad_scatter(four, row, part_of, landing):
        return QuadScatter(four, part_of, landing, mem.back_send.at[row], mem.back_recv.at[row])

    def reduce_grad(part, unused):
        mem.reduce_grad[part] = dot(
            mem.hidden_turned[block_of(part, rows), :], mem.branch[...]
        ).astype(LOW)
        at_step(part, 0, lambda: sums.combine(3))
        return unused

    lax.fori_loop(0, batch, reduce_grad, 0)
    back_reduce = quad_scatter(
        feed_four, 0, lambda part: mem.reduce_grad.at[part], mem.reduce_land
    )
    back_reduce.start_far()

    def expand_grad(which):
        grads = (mem.grad_gate, mem.grad_up)[which]

        def one_block(block, unused):
            products = dot(mem.act_two_turned[block_of(block, pair), :], grads[...]).astype(LOW)
            mem.expand_grad[which, pl.ds(2 * block, 2)] = products.reshape(
                2, batch, share, hidden_width
            )
            return unused

        lax.fori_loop(0, seq // 2, one_block, 0)
        line = quad_scatter(
            feed_four, 1 + which, expand_part_of(mem.expand_grad, which), mem.expand_land.at[which]
        )
        return line

    back_expand = []
    back_expand.append(expand_grad(0))
    back_expand[0].start_far()
    grad_act = sums.total()
    unit_two, scale_two = norm_rows(mem.middle[...])
    gain = ins.gains[1:2, :]
    grad_unit = grad_act * gain
    mem.gains[1:2, :] = jnp.sum(grad_act * unit_two, axis=0, keepdims=True)
    grad_middle = mem.grad_own[...] + scale_two * (
        grad_unit - unit_two * jnp.mean(grad_unit * unit_two, axis=-1, keepdims=True)
    )
    mem.grad_own[...] = grad_middle
    mem.own_rows[3] = grad_middle.astype(LOW)
    grad_mixed = dot_turned(mem.output_full[...], mem.own_rows[3]).astype(LOW)
    mem.grad_mixed_out[...] = grad_mixed.reshape(seq, LANES, rows)

    def grad_copy(mask, back=False):
        return push(
            mem.grad_mixed_out.at[heads.at(mask)],
            mem.grad_mixed.at[:, block_of(heads.at(mask) if back else me, rows)],
            mem.mixed_send.at[8 + mask],
            mem.mixed_recv.at[8 + mask],
            heads.place(mask),
        )

    for mask in masks:
        grad_copy(mask).start()
    mem.grad_mixed[:, block_of(me, rows)] = mem.grad_mixed_out[me]
    back_reduce.pass_on()
    back_expand.append(expand_grad(1))
    back_expand[1].start_far()

    wait_pieces(lambda mask: grad_copy(mask, True))
    acts = gather(heads, 3, mem.grad_attn)
    acts.start()
    back_reduce.start_near()
    back_expand[0].start_near()
    back_attend = [
        line_scatter(
            4 + which,
            lambda part, which=which: mem.attend_grad.at[which, :, part],
            mem.attend_land.at[which],
        )
        for which in range(3)
    ]

    def attend_grad(which):
        def one_block(block, unused):
            products = dot(mem.act_one_turned[block_of(block, pair), :], mem.grad_project[which])
            mem.attend_grad[which, pl.ds(2 * block, 2)] = products.astype(LOW).reshape(
                2, batch, share, LANES
            )
            return unused

        lax.fori_loop(0, length // pair, one_block, 0)
        back_attend[which].start()

    lane = lax.broadcasted_iota(jnp.int32, (pair, LANES), 1)

    def grad_rows(block, unused):
        span = block_of(block, pair)
        whole = turned(mem.eye, mem.grad_mixed[:, span])
        for head in range(HEADS_HERE):
            mem.grad_heads[head, span, :] = jnp.where(
                lax.div(lane, HEAD_DIM) == head, whole, jnp.zeros_like(whole)
            )
        return unused

    lax.fori_loop(0, length // pair, grad_rows, 0)

    def value_back(block, unused):
        span = block_of(block, pair)
        total = dot(mem.probs[0, span, :], mem.grad_heads[0])
        for head in range(1, HEADS_HERE):
            total = total + dot(mem.probs[head, span, :], mem.grad_heads[head])
        mem.grad_project[2, span, :] = total.astype(LOW)
        return unused

    lax.fori_loop(0, length // pair, value_back, 0)
    back_expand[0].pass_on()
    attend_grad(2)

    def score_back(block, unused):
        columns = block_of(block, pair)
        row = lax.broadcasted_iota(jnp.int32, (HEAD_DIM, pair), 0)
        grads = mem.grad_mixed[:, columns]
        delta = grads.astype(WIDE) * mem.exact[:, columns]
        for head in range(HEADS_HERE):
            span = slice(head * HEAD_DIM, (head + 1) * HEAD_DIM)
            pieces = thirds(-jnp.sum(delta[span], axis=0, keepdims=True))
            marks = pick(row, dict(enumerate(pieces))).astype(LOW)
            change = dot(mem.value_heads[head], jnp.concatenate([grads[span], marks], axis=0))
            mem.probs[head, :, columns] = (mem.probs[head, :, columns].astype(WIDE) * change).astype(LOW)
        return unused

    lax.fori_loop(0, length // pair, score_back, 0)
    back_expand[1].start_near()
    mem.bias_sums[...] = jnp.zeros_like(mem.bias_sums)
    scale = HEAD_DIM ** (-0.5)

    def project_grads(block, unused):
        span = block_of(block, pair)
        cosine, sine = mem.cosine[:, span], -mem.sine[:, span]
        queries, keys = [], []
        for head in range(HEADS_HERE):
            features = slice(head * HEAD_DIM, (head + 1) * HEAD_DIM)
            queries.append(dot(mem.key_turned[features, :], mem.probs[head, :, span]) * scale)
            sums = dot_turned(mem.query_back[head], mem.probs[head, span, :])
            keys.append(sums[:HEAD_DIM])
            by_variate = sums[HEAD_DIM : HEAD_DIM + VARIATES]
            same = by_variate * mem.key_marks[:VARIATES, span].astype(WIDE)
            mem.bias_sums[head : head + 1, :] += jnp.sum(same, axis=0, keepdims=True)
            total = sums[HEAD_DIM + VARIATES : HEAD_DIM + VARIATES + 1]
            mem.bias_sums[HEADS_HERE + head : HEADS_HERE + head + 1, :] += total
        queries = turn_rows(jnp.concatenate(queries, axis=0), cosine, sine)
        mem.grad_project[0, span, :] = turned(mem.eye, queries.astype(LOW))
        keys = turn_rows(jnp.concatenate(keys, axis=0), cosine, sine)
        mem.grad_project[1, span, :] = turned(mem.eye, keys.astype(LOW))
        return unused

    lax.fori_loop(0, length // pair, project_grads, 0)
    back_expand[1].pass_on()
    attend_grad(0)
    acts.pass_on(1)
    acts.pass_on(2)
    sums = scatter(heads, 3)

    def project_back(step, unused):
        chip = lax.rem(step + 1, 4)
        span = block_of(chip_of(heads, chip), pair)
        grads = [mem.grad_project[which, span, :] for which in range(3)]
        sums.put(chip, dot(jnp.concatenate(grads, axis=1), mem.attend_turned[...]))
        at_step(step, 1, lambda: sums.combine(1))
        at_step(step, 2, lambda: sums.combine(2))
        return unused

    lax.fori_loop(0, 4, project_back, 0)
    sums.combine(3)
    attend_grad(1)
    acts.pass_on(3)
    for chip in range(4):
        acts.complete(chip)
    acts.finish()
    mem.output_grad[...] = (
        dot(mem.mixed_turned[...], mem.grad_attn[...]).astype(LOW).reshape(mem.output_grad.shape)
    )
    back_output = line_scatter(3, lambda part: mem.output_grad.at[part], mem.output_land)
    back_output.start()
    for which in (2, 0):
        back_attend[which].pass_on()

    column_copies = []
    mem.squares[0:1, :] = jnp.zeros((1, D), WIDE)

    def add_squares(total):
        flat = total.reshape(-1, total.shape[-1])
        width = flat.shape[1]
        mem.squares[0:1, :width] += jnp.sum(flat * flat, axis=0, keepdims=True)

    def store_whole(total, out):
        out[...] = total
        add_squares(total)

    back_reduce.land()
    store_whole(back_reduce.total(), outs.reduce_share)
    def expand_shares(which):
        back_expand[which].land()
        own = expand_part_of(mem.expand_grad, which)(quad)

        def one_block(block, unused):
            total = (
                own[block].astype(WIDE)
                + mem.expand_land[which, 0, block].astype(WIDE)
                + mem.expand_land[which, 2, block].astype(WIDE)
            )
            mem.expand_part[which, block] = total.astype(LOW)
            add_squares(total)
            return unused

        lax.fori_loop(0, 4, one_block, 0)
        for mask in masks:
            other = feeds.at(mask)
            copy = push(
                mem.expand_part.at[which, lax.rem(other, 4), lax.div(other, 4)],
                mem.expand_share.at[which, feeds.index],
                mem.share_send.at[which, mask],
                mem.share_recv.at[which, mask],
                feeds.place(mask),
            )
            copy.start()
            column_copies.append(copy)
        mem.expand_share[which, feeds.index] = mem.expand_part[
            which, lax.rem(feeds.index, 4), lax.div(feeds.index, 4)
        ]

    expand_shares(0)
    back_attend[1].pass_on()
    expand_shares(1)

    def attend_shares(which):
        back_attend[which].land()

        def store(total):
            mem.attend_part[which] = total.astype(LOW)
            add_squares(total)

        back_attend[which].add(
            lambda: mem.attend_grad[which, :, group].astype(WIDE),
            lambda slot: mem.attend_land[which, slot].astype(WIDE),
            store,
        )

    attend_shares(2)
    grad_act = sums.total()
    unit_one, scale_one = norm_rows(ins.inputs[...].astype(WIDE))
    gain = ins.gains[0:1, :]
    grad_unit = grad_act * gain
    mem.gains[0:1, :] = jnp.sum(grad_act * unit_one, axis=0, keepdims=True)
    grad_input = mem.grad_own[...] + scale_one * (
        grad_unit - unit_one * jnp.mean(grad_unit * unit_one, axis=-1, keepdims=True)
    )
    outs.input_gradient[...] = grad_input * (count_all * D)
    outs.count[...] = jnp.broadcast_to(count_all, (8, LANES))

    back_output.pass_on()
    for which in range(2):
        attend_shares(which)
    for mask in masks:
        copy = push(
            mem.attend_part.at[:, heads.at(mask)],
            outs.attend_share.at[:, :, block_of(me, LANES)],
            mem.share_send.at[2, mask],
            mem.share_recv.at[2, mask],
            heads.place(mask),
        )
        copy.start()
        column_copies.append(copy)
    outs.attend_share[:, :, block_of(me, LANES)] = mem.attend_part[:, me]
    back_output.land()
    back_output.add(
        lambda: mem.output_grad[group].astype(WIDE),
        lambda slot: mem.output_land[slot].astype(WIDE),
        lambda total: store_whole(total, outs.output_share),
    )

    lane = lax.broadcasted_iota(jnp.int32, (1, LANES), 1)
    lines = [
        mem.gains[which : which + 1, start : start + LANES]
        for which in range(2)
        for start in range(0, D, LANES)
    ]
    bias_line = jnp.zeros((1, LANES), WIDE)
    for row in range(2 * HEADS_HERE):
        place = row // HEADS_HERE * HEADS + me * HEADS_HERE + row % HEADS_HERE
        line = mem.bias_sums[row : row + 1, :]
        if row >= HEADS_HERE:
            line = line - mem.bias_sums[row - HEADS_HERE : row - HEADS_HERE + 1, :]
        amount = jnp.sum(line, axis=1, keepdims=True)
        bias_line = bias_line + jnp.where(lane == place, amount, 0.0)
    amounts = jnp.sum(mem.squares[0:2, :], axis=1, keepdims=True)
    amount_line = jnp.where(lane == 0, amounts[0:1], 0.0) + jnp.where(lane == 1, amounts[1:2], 0.0)
    lines += [bias_line, amount_line, jnp.zeros((6, LANES), WIDE)]
    mem.plane_totals[me] = jnp.concatenate(lines, axis=0)
    plane_copies = []
    for mask in masks:
        copy = push(
            mem.plane_totals.at[me],
            mem.plane_totals.at[me],
            mem.total_send.at[0, mask],
            mem.total_recv.at[0, mask],
            (flip(me, mask), group),
        )
        copy.start()
        plane_copies.append(copy)
    for copy in column_copies[: 2 * len(masks)]:
        copy.wait()
    for which in range(2):
        for block in range(blocks):
            owner, part = feed_block(block)
            outs.expand_share[which, :, block * LANES : (block + 1) * LANES] = mem.expand_share[
                which, owner, :, part * LANES : (part + 1) * LANES
            ]
    for copy in plane_copies:
        copy.wait()
    mem.line_totals[group] = jnp.sum(mem.plane_totals[...], axis=0)
    total_copies = []
    for step in range(1, batch):
        copy = push(
            mem.line_totals.at[group],
            mem.line_totals.at[group],
            mem.total_send.at[1, step],
            mem.total_recv.at[1, step],
            (me, lax.rem(group + step, batch)),
        )
        copy.start()
        total_copies.append(copy)
    for copy in total_copies:
        copy.wait()
    outs.totals[...] = jnp.sum(mem.line_totals[...], axis=0)
    for copy in column_copies[2 * len(masks) :]:
        copy.wait()
    for copies in (attend_columns, expand_columns):
        for copy in copies:
            copy.wait_send()
    for line in [line_attend, line_output, line_reduce] + line_expand:
        line.finish()
    for line in [back_output, back_reduce] + back_attend + back_expand:
        line.finish()


def call_layer(seq, batch, inputs, teacher, lengths, variates, observed, times, bias, gains, attend, output, expand, reduce):
    rows, share, hidden = inputs.shape[0], attend.shape[1], expand.shape[2] // seq
    length, pair, chips = rows * seq, 2 * rows, seq // 2
    low = lambda *shape: pltpu.VMEM(shape, LOW)
    wide = lambda *shape: pltpu.VMEM(shape, WIDE)
    sems = lambda *shape: pltpu.SemaphoreType.DMA(shape)
    in_names = ["inputs", "teacher", "lengths", "variates", "observed"]
    in_names += ["times", "bias", "gains"]
    in_names += ["attend", "output", "expand", "reduce"]
    outs = dict(
        layer_output=((rows, D), WIDE),
        input_gradient=((rows, D), WIDE),
        totals=((TOTAL_ROWS, LANES), WIDE),
        count=((8, LANES), WIDE),
        attend_share=((3, share, D), LOW),
        output_share=((output.shape[0], D), WIDE),
        expand_share=((2, share, hidden * seq), LOW),
        reduce_share=((reduce.shape[0], D), WIDE),
    )
    scratch = dict(
        gains=wide(2, D),
        squares=wide(8, D),
        plane_totals=wide(seq, TOTAL_ROWS, LANES),
        line_totals=wide(batch, TOTAL_ROWS, LANES),
        attend_low=low(3, share, D),
        expand_low=low(2, seq, share, hidden),
        attend_all=low(3, seq, batch, share, LANES),
        output_full=low(D, D),
        expand_all=low(2, seq, batch, share, hidden),
        reduce_all=low(batch, reduce.shape[0], D),
        own_rows=low(4, rows, D),
        act_one=low(length, D),
        act_two=low(length, D),
        branch=low(length, D),
        grad_attn=low(length, D),
        facts_own=wide(HEAD_DIM + 8, LANES),
        facts_all=wide(seq * (HEAD_DIM + 8), LANES),
        scored=wide(rows, LANES),
        cosine=wide(HEAD_DIM // 2, length),
        sine=wide(HEAD_DIM // 2, length),
        labels=wide(8, length),
        key_marks=low(HEAD_DIM, length),
        count=wide(batch, 8, LANES),
        query_turned=low(HEADS_HERE, LANES, length),
        key_turned=low(LANES, length),
        value_turned=low(LANES, length),
        key_heads=low(HEADS_HERE, length, LANES),
        value_heads=low(HEADS_HERE, length, LANES),
        query_back=low(HEADS_HERE, LANES, length),
        attend_turned=low(3 * LANES, D),
        eye=low(pair, pair),
        grad_heads=low(HEADS_HERE, length, LANES),
        grad_mixed=low(LANES, length),
        grad_mixed_out=low(seq, LANES, rows),
        probs=low(HEADS_HERE, length, length),
        mixed_out=low(length, LANES),
        mixed_rows=low(rows, D),
        hidden_turned=low(hidden, length),
        act_two_turned=low(D, length),
        exact=wide(LANES, length),
        mixed_wide=wide(LANES, pair),
        mixed_turned=low(LANES, length),
        whole=wide(pair, D),
        keep=wide(chips, rows, D),
        near_from=low(chips, rows, D),
        near=low(chips, rows, D),
        far_from=low(chips, rows, D),
        far=low(chips, rows, D),
        middle=wide(rows, D),
        grad_own=wide(rows, D),
        by_up=wide(length, hidden),
        by_gate=wide(length, hidden),
        hidden=low(length, hidden),
        grad_gate=low(length, hidden),
        grad_up=low(length, hidden),
        bias_sums=wide(8, pair),
        grad_project=low(3, length, LANES),
        act_one_turned=low(D, length),
        reduce_grad=low(batch, reduce.shape[0], D),
        expand_grad=low(2, seq, batch, share, hidden),
        output_grad=low(batch, output.shape[0], D),
        attend_grad=low(3, seq, batch, share, LANES),
        reduce_land=low(3, reduce.shape[0], D),
        expand_land=low(2, 3, 4, 2, share, hidden),
        output_land=low(batch, output.shape[0], D),
        attend_land=low(3, batch, seq, share, LANES),
        expand_part=low(2, 4, 2, share, hidden),
        expand_share=low(2, seq, share, hidden),
        attend_part=low(3, seq, share, LANES),
        stage_sem=sems(5 + 2 * (expand.shape[2] // D)),
        total_send=sems(2, seq),
        total_recv=sems(2, seq),
        column_send=sems(2, seq),
        column_recv=sems(2, seq),
        line_send=sems(5, batch),
        line_recv=sems(5, batch),
        facts_send=sems(seq),
        facts_recv=sems(seq),
        gather_send=sems(4, seq),
        gather_recv=sems(4, seq),
        count_send=sems(batch),
        count_recv=sems(batch),
        near_send=sems(4, chips),
        near_recv=sems(4, chips),
        far_send=sems(4, chips),
        far_recv=sems(4, chips),
        back_send=sems(7, batch),
        back_recv=sems(7, batch),
        output_send=sems(seq),
        output_recv=sems(seq),
        mixed_send=sems(2 * seq),
        mixed_recv=sems(2 * seq),
        share_send=sems(3, seq),
        share_recv=sems(3, seq),
    )

    places = dict.fromkeys(("attend", "output", "expand", "reduce"), pl.BlockSpec(memory_space=pl.ANY))
    places["bias"] = IN_SMEM

    def kernel(*refs):
        groups, start = [], 0
        for names in (in_names, outs, scratch):
            names = list(names)
            groups.append(types.SimpleNamespace(**dict(zip(names, refs[start : start + len(names)]))))
            start += len(names)
        layer_kernel(seq, batch, *groups)

    results = pl.pallas_call(
        kernel,
        out_shape=[jax.ShapeDtypeStruct(*out) for out in outs.values()],
        in_specs=[places.get(name, IN_VMEM) for name in in_names],
        out_specs=[IN_VMEM] * len(outs),
        scratch_shapes=list(scratch.values()),
        compiler_params=pltpu.CompilerParams(
            collective_id=0, has_side_effects=True, vmem_limit_bytes=63 * MIB
        ),
        name="layer",
    )(inputs, teacher, lengths, variates, observed, times, bias, gains, attend, output, expand, reduce)
    return types.SimpleNamespace(**dict(zip(outs, results)))


def update_kernel(
    smalls, ins, small_outs, outs, olds, shares, news, copies, passed, in_sems, out_sems
):
    totals, count, gains, gains_first, gains_second, bias, bias_first, bias_second = smalls
    order = (2, 3, 0, 1)
    comes = []
    for place, number in enumerate(order):
        pairs = list(zip(ins[4 + 3 * number : 7 + 3 * number], olds[3 * number : 3 * number + 3]))
        pairs.append((ins[number], shares[number]))
        comes.append(
            [
                pltpu.make_async_copy(source, target, in_sems.at[4 * place + part])
                for part, (source, target) in enumerate(pairs)
            ]
        )
    for copy in sum(comes, []):
        copy.start()
    through = [
        pltpu.make_async_copy(ins[16 + part], passed[part], in_sems.at[16 + part]) for part in range(2)
    ]
    for copy in through:
        copy.start()
    goes = []
    gains_total = jnp.concatenate(
        [
            jnp.concatenate([totals[row + i : row + i + 1, :] for i in range(D // LANES)], axis=1)
            for row in (0, D // LANES)
        ],
        axis=0,
    )
    row = 2 * D // LANES
    bias_total = jnp.concatenate(
        [totals[row : row + 1, :HEADS], totals[row : row + 1, HEADS : 2 * HEADS]], axis=0
    )
    row += 1

    def sum_all(values):
        return jnp.sum(jnp.sum(values, axis=0, keepdims=True), axis=1, keepdims=True)

    squares = (
        totals[row : row + 1, 0:1] + sum_all(gains_total * gains_total) + sum_all(bias_total * bias_total)
    )
    grad_norm = jnp.sqrt(squares)
    clip = jnp.minimum(1.0, CLIP_NORM / grad_norm)
    small_outs[0][...] = totals[row : row + 1, 1:2] / (count[0:1, 0:1] * D)
    small_outs[1][...] = grad_norm
    rates = (RATE_ATTEND, RATE_OUTPUT, RATE_EXPAND, RATE_REDUCE)
    for place, number in enumerate(order):
        for copy in comes[place]:
            copy.wait()
        weight, first, second = olds[3 * number : 3 * number + 3]
        new, first_new, second_new = news[3 * number : 3 * number + 3]
        arrays = (new, copies[number], first_new, second_new, weight, first, second, shares[number])
        for lead in range(weight.shape[0] if weight.ndim == 3 else 1):

            def one_block(block, unused, lead=lead, arrays=arrays, rate=rates[number]):
                across = arrays[0].shape[-1] // D
                rows = block_of(lax.div(block, across), 16)
                columns = block_of(lax.rem(block, across), D)
                place = (lead, rows, columns) if len(arrays[0].shape) == 3 else (rows, columns)
                old, moment, square, share = [array[place] for array in arrays[4:]]
                step = fast_step(old, moment, square, share.astype(WIDE) * clip, rate)
                arrays[0][place], arrays[2][place], arrays[3][place] = step
                arrays[1][place] = step[0].astype(LOW)
                return unused

            lax.fori_loop(0, weight.shape[-2] // 16 * (weight.shape[-1] // D), one_block, 0)
        for part, source in enumerate((new, copies[number], first_new, second_new)):
            copy = pltpu.make_async_copy(
                source, outs[2 + 4 * number + part], out_sems.at[2 + 4 * number + part]
            )
            copy.start()
            goes.append(copy)
        if place == 0:
            for part in range(2):
                through[part].wait()
                copy = pltpu.make_async_copy(passed[part], outs[part], out_sems.at[part])
                copy.start()
                goes.append(copy)
    for number, (old, total, rate) in enumerate(
        (
            ((gains, gains_first, gains_second), gains_total, RATE_GAINS),
            ((bias, bias_first, bias_second), bias_total, RATE_BIAS),
        )
    ):
        new, first_new, second_new = small_outs[2 + 3 * number : 5 + 3 * number]
        new[...], first_new[...], second_new[...] = adam_step(
            old[0][...], old[1][...], old[2][...], total * clip, rate, 0.0
        )
    for copy in goes:
        copy.wait()


def fast_step(weight, first, second, gradient, rate):
    first = BETA_ONE * first + (1.0 - BETA_ONE) * gradient
    second = BETA_TWO * second + ((1.0 - BETA_TWO) * gradient) * gradient
    low = jnp.sqrt(second * (1.0 / (1.0 - BETA_TWO**STEP))) + ADAM_EPS
    step = first * (rate / (1.0 - BETA_ONE**STEP)) / low
    return weight * (1.0 - rate * WEIGHT_DECAY) - step, first, second


def call_update(done, shares, smalls, olds):
    in_hbm = pl.BlockSpec(memory_space=pl.ANY)
    smalls = [done.totals, done.count] + smalls
    ins = shares + olds + [done.layer_output, done.input_gradient]
    one = jax.ShapeDtypeStruct((1, 1), WIDE)
    small_outs = [one, one] + smalls[2:]
    outs = [(done.layer_output, WIDE), (done.input_gradient, WIDE)]
    for weight in olds[::3]:
        outs += [(weight, dtype) for dtype in (WIDE, LOW, WIDE, WIDE)]
    passed = ins[-2:]
    parts = [smalls, ins, small_outs, outs, olds, shares, olds, olds[::3], passed]

    def kernel(*refs):
        groups, start = [], 0
        for part in parts:
            groups.append(refs[start : start + len(part)])
            start += len(part)
        update_kernel(*groups, *refs[start:])

    results = pl.pallas_call(
        kernel,
        out_shape=[jax.ShapeDtypeStruct(array.shape, WIDE) for array in small_outs]
        + [jax.ShapeDtypeStruct(array.shape, dtype) for array, dtype in outs],
        in_specs=[IN_VMEM] * len(smalls) + [in_hbm] * len(ins),
        out_specs=[IN_VMEM] * len(small_outs) + [in_hbm] * len(outs),
        scratch_shapes=[pltpu.VMEM(array.shape, WIDE) for array in olds]
        + [pltpu.VMEM(array.shape, array.dtype) for array in shares]
        + [pltpu.VMEM(array.shape, WIDE) for array in olds]
        + [pltpu.VMEM(array.shape, LOW) for array in olds[::3]]
        + [pltpu.VMEM(array.shape, WIDE) for array in passed]
        + [pltpu.SemaphoreType.DMA((18,)), pltpu.SemaphoreType.DMA((18,))],
        compiler_params=pltpu.CompilerParams(vmem_limit_bytes=63 * MIB),
        name="update",
    )(*smalls, *ins)
    return results[: len(small_outs)], results[len(small_outs) :]


def fast_body(
    seq,
    batch,
    inputs,
    teacher,
    lengths,
    variate_ids,
    time_ids,
    observed,
    attend_weight,
    output_weight,
    expand_weight,
    reduce_weight,
    norm_gains,
    variate_bias,
    attend_first,
    output_first,
    expand_first,
    reduce_first,
    gains_first,
    bias_first,
    attend_second,
    output_second,
    expand_second,
    reduce_second,
    gains_second,
    bias_second,
):
    done = call_layer(
        seq,
        batch,
        inputs[0],
        teacher[0],
        lengths[:, None],
        variate_ids,
        observed,
        time_ids,
        variate_bias,
        norm_gains,
        attend_weight,
        output_weight,
        expand_weight,
        reduce_weight,
    )
    small, large = call_update(
        done,
        [done.attend_share, done.output_share, done.expand_share, done.reduce_share],
        [norm_gains, gains_first, gains_second, variate_bias, bias_first, bias_second],
        [attend_weight, attend_first, attend_second]
        + [output_weight, output_first, output_second]
        + [expand_weight, expand_first, expand_second]
        + [reduce_weight, reduce_first, reduce_second],
    )
    return (
        large[0][None],
        small[0].reshape(()),
        large[1][None],
        small[1].reshape(()),
    ) + tuple(large[2:] + small[2:])


def solution(mesh):
    seq, batch = mesh.shape["seq"], mesh.shape["batch"]
    body = functools.partial(fast_body, seq, batch) if fast_fits(seq, batch) else general_body
    in_specs = (
        P("batch", "seq", None),
        P("batch", "seq", None),
        P("batch"),
        P("batch", "seq"),
        P("batch", "seq"),
        P("batch", "seq"),
        P(None, ("seq", "batch"), None),
        P(("seq", "batch"), None),
        P(None, ("seq", "batch"), None),
        P(("seq", "batch"), None),
        P(),
        P(),
        P(None, ("seq", "batch"), None),
        P(("seq", "batch"), None),
        P(None, ("seq", "batch"), None),
        P(("seq", "batch"), None),
        P(),
        P(),
        P(None, ("seq", "batch"), None),
        P(("seq", "batch"), None),
        P(None, ("seq", "batch"), None),
        P(("seq", "batch"), None),
        P(),
        P(),
    )
    out_specs = (
        P("batch", "seq", None),
        P(),
        P("batch", "seq", None),
        P(),
        P(None, ("seq", "batch"), None),
        P(None, ("seq", "batch"), None),
        P(None, ("seq", "batch"), None),
        P(None, ("seq", "batch"), None),
        P(("seq", "batch"), None),
        P(("seq", "batch"), None),
        P(("seq", "batch"), None),
        P(("seq", "batch"), None),
        P(None, ("seq", "batch"), None),
        P(None, ("seq", "batch"), None),
        P(None, ("seq", "batch"), None),
        P(None, ("seq", "batch"), None),
        P(("seq", "batch"), None),
        P(("seq", "batch"), None),
        P(("seq", "batch"), None),
        P(("seq", "batch"), None),
        P(),
        P(),
        P(),
        P(),
        P(),
        P(),
    )
    return jax.shard_map(body, mesh=mesh, in_specs=in_specs, out_specs=out_specs, check_vma=False)
```
